32 devices in a mesh: dp: 8 (over y, x, core), tensor: 4 (over z).
Axes of the slice: x: 2, y: 2, z: 4, core: 2. Of those that a mesh axis runs over, the one named last changes fastest.
Arguments:
- tokens: bfloat16 [16384, 768], P('dp'), may hold values from -6 to 6
- lengths: int32 [32, 8], P('dp'), may hold values from 0 to 256, as said below
- key_mask: int32 [16384], P('dp'), may hold values 0 or 1
- query_weight: bfloat16 [768, 768], P(None, 'tensor'), may hold values from -0.21875 to 0.21875
- query_bias: bfloat16 [768], P('tensor'), may hold values from -3 to 3
- key_weight: bfloat16 [768, 768], P(None, 'tensor'), may hold values from -0.21875 to 0.21875
- value_weight: bfloat16 [768, 768], P(None, 'tensor'), may hold values from -0.21875 to 0.21875
- value_bias: bfloat16 [768], P('tensor'), may hold values from -3 to 3
- output_weight: bfloat16 [768, 768], P('tensor'), may hold values from -0.75 to 0.75
- output_bias: bfloat16 [768], replicated, may hold values from -2 to 2
- first_gain: bfloat16 [768], replicated, may hold values from 0.5 to 1.5
- first_shift: bfloat16 [768], replicated, may hold values from -2 to 2
- inner_weight: bfloat16 [768, 3072], P(None, 'tensor'), may hold values from -0.21875 to 0.21875
- inner_bias: bfloat16 [3072], P('tensor'), may hold values from -3 to 3
- outer_weight: bfloat16 [3072, 768], P('tensor'), may hold values from -0.109375 to 0.109375
- outer_bias: bfloat16 [768], replicated, may hold values from -2 to 2
- second_gain: bfloat16 [768], replicated, may hold values from 0.5 to 1.5
- second_shift: bfloat16 [768], replicated, may hold values from -2 to 2
- cotangent: bfloat16 [16384, 768], P('dp'), may hold values from -6 to 6
Outputs:
- output: bfloat16 [16384, 768], P('dp')
- tokens_grad: bfloat16 [16384, 768], P('dp')
- query_weight_grad: float32 [768, 768], P(None, 'tensor')
- query_bias_grad: float32 [768], P('tensor')
- key_weight_grad: float32 [768, 768], P(None, 'tensor')
- value_weight_grad: float32 [768, 768], P(None, 'tensor')
- value_bias_grad: float32 [768], P('tensor')
- output_weight_grad: float32 [768, 768], P('tensor')
- output_bias_grad: float32 [768], replicated
- first_gain_grad: float32 [768], replicated
- first_shift_grad: float32 [768], replicated
- inner_weight_grad: float32 [768, 3072], P(None, 'tensor')
- inner_bias_grad: float32 [3072], P('tensor')
- outer_weight_grad: float32 [3072, 768], P('tensor')
- outer_bias_grad: float32 [768], replicated
- second_gain_grad: float32 [768], replicated
- second_shift_grad: float32 [768], replicated
The draws below stay inside these ranges and needn't reach their ends.
Inputs may be any that keep to these rules, and one draw needn't show every extreme that they name: Per bucket, the item lengths sum to at most 512; slots past the live items are pad slots; one item of some bucket has exactly 256 tokens.
All inputs are finite; a program needn't handle non-finite values. No bound on the sum of `key_mask` on one device may be relied on, other than what follows from the above.
Results may differ from the reference program's by a relative error of at most 0.015.
Values may be sent and summed in bfloat16 or wider, within the bound.
No kernel may reach another device: no remote copies, remote signals or barrier semaphores. Data moves between devices by JAX's collectives and lax.ppermute only.
A program may use at most 128 MiB of HBM per device.

```python
import jax
import jax.numpy as jnp
from jax import lax

D = 768
HEADS = 12
FF = 3072
HEAD = 64
BUCKET = 512
ITEMS = 8
BUCKETS_DEV = 4
BUCKETS = 32
TOKENS = 16384
N_DP = 8


def draw_lengths(key, part):
    key = jax.random.fold_in(key, 11)
    short_key, long_key, pick_key = jax.random.split(key, 3)
    short_items = jax.random.randint(short_key, (BUCKETS, ITEMS), BUCKET // 32, BUCKET // 9 + 1)
    longest = BUCKET // 2 - jax.random.randint(long_key, (BUCKETS,), 0, BUCKET // 12 + 1)
    numbers = jnp.arange(BUCKETS, dtype=jnp.int32)
    picked = (jax.random.randint(pick_key, (BUCKETS,), 0, 4) == 0) | (numbers == 0)
    longest = jnp.where(numbers == 0, BUCKET // 2, longest)
    slots = jnp.arange(ITEMS, dtype=jnp.int32)
    with_long = jnp.where(slots[None, :] == 0, longest[:, None], jnp.where(slots[None, :] < 4, short_items, 0))
    return jnp.where(picked[:, None], with_long, short_items).astype(jnp.int32)


def place_ends(entries, own_key, smallest, largest):
    longest = entries.shape.index(max(entries.shape))
    spots = []
    for shift in (0, 1):
        where = [jax.random.randint(jax.random.fold_in(own_key, axis), (), 0, length) for axis, length in enumerate(entries.shape)]
        where[longest] = (where[longest] + shift) % entries.shape[longest]
        spots.append(tuple(where))
    return entries.at[spots[0]].set(smallest).at[spots[1]].set(largest)


def levels(rng, dims, shards, smallest, top_value):
    factor_of, own = 1.0, jax.random.fold_in(rng, 6)
    for position, shards_of in shards:
        heights = jnp.exp(jax.random.uniform(jax.random.fold_in(own, position), (shards_of,), jnp.float32, smallest / len(shards), top_value / len(shards)))
        factor_of = factor_of * jnp.repeat(heights, dims[position] // shards_of).reshape([-1 if axis == position else 1 for axis in range(len(dims))])
    return factor_of


def noise(stream_key, shape, width, reach, shards=(), kind=jnp.bfloat16):
    values = jax.random.normal(stream_key, shape, jnp.float32) * width
    if len(shards) > 0:
        values = levels(stream_key, shape, shards, -0.22, 0.18) * values
    return jnp.clip(values, min=-reach, max=reach).astype(kind)


def setup_inputs(seed: int = 0) -> dict:
    key_list = jax.random.split(jax.random.key(seed), 20)
    tokens = noise(key_list[0], (TOKENS, D), 1.0, 6.0, ((0, 8),))
    lengths = draw_lengths(jax.random.fold_in(key_list[19], 71), 0)
    key_mask = place_ends((jax.random.randint(key_list[2], (TOKENS,), 0, 8) < 7).astype(jnp.int32), jax.random.fold_in(key_list[2], 1), 0, 1)
    query_weight = noise(key_list[3], (D, HEADS * HEAD), D ** -0.5, 0.21875, ((1, 4),))
    query_bias = noise(key_list[4], (HEADS * HEAD,), 0.5, 3.0, ((0, 4),))
    key_weight = noise(key_list[5], (D, HEADS * HEAD), D ** -0.5, 0.21875, ((1, 4),))
    value_weight = noise(key_list[6], (D, HEADS * HEAD), D ** -0.5, 0.21875, ((1, 4),))
    value_bias = noise(key_list[7], (HEADS * HEAD,), 0.5, 3.0, ((0, 4),))
    output_weight = noise(key_list[8], (HEADS * HEAD, D), HEAD ** -0.5, 0.75, ((0, 4),))
    output_bias = noise(key_list[9], (D,), 0.3, 2.0)
    first_gain = jnp.clip(1.0 + 0.1 * jax.random.normal(key_list[10], (D,), jnp.float32), 0.5, 1.5).astype(jnp.bfloat16)
    first_shift = noise(key_list[11], (D,), 0.3, 2.0)
    inner_weight = noise(key_list[12], (D, FF), D ** -0.5, 0.21875, ((1, 4),))
    inner_bias = noise(key_list[13], (FF,), 0.5, 3.0, ((0, 4),))
    outer_weight = noise(key_list[14], (FF, D), FF ** -0.5, 0.109375, ((0, 4),))
    outer_bias = noise(key_list[15], (D,), 0.3, 2.0)
    second_gain = jnp.clip(1.0 + 0.1 * jax.random.normal(key_list[16], (D,), jnp.float32), 0.5, 1.5).astype(jnp.bfloat16)
    second_shift = noise(key_list[17], (D,), 0.3, 2.0)
    cotangent = noise(key_list[18], (TOKENS, D), 1.0, 6.0, ((0, 8),))
    return {"tokens": tokens, "lengths": lengths, "key_mask": key_mask, "query_weight": query_weight, "query_bias": query_bias, "key_weight": key_weight, "value_weight": value_weight, "value_bias": value_bias, "output_weight": output_weight, "output_bias": output_bias, "first_gain": first_gain, "first_shift": first_shift, "inner_weight": inner_weight, "inner_bias": inner_bias, "outer_weight": outer_weight, "outer_bias": outer_bias, "second_gain": second_gain, "second_shift": second_shift, "cotangent": cotangent}


@jax.custom_vjp
def low(v):
    return lax.optimization_barrier(v.astype(jnp.bfloat16)).astype(jnp.float32)

@jax.custom_vjp
def low_back(v):
    return v

def low_keep(v):
    return (low(v), None)

def low_pass(kept, grad):
    return (grad,)

def back_keep(v):
    return (v, None)

def back_low(kept, grad):
    return (low(grad),)
low.defvjp(low_keep, low_pass)
low_back.defvjp(back_keep, back_low)
negative_fill = -1e+30
epsilon = 1e-06

def product(left, right):
    return jnp.dot(left, right, precision=lax.Precision.HIGHEST, preferred_element_type=jnp.float32)

def layer_norm(values, norm_gain, norm_shift):
    centred = values - lax.optimization_barrier(jnp.mean(values, axis=1, keepdims=True))
    spread = lax.optimization_barrier(jnp.mean(centred * centred, axis=1, keepdims=True))
    return centred * lax.rsqrt(spread + epsilon) * norm_gain + norm_shift

def bucket_items(lengths):
    ends = jnp.cumsum(lengths, axis=1).astype(jnp.int32)
    places = jnp.arange(BUCKET, dtype=jnp.int32)
    return lax.optimization_barrier(jnp.sum((places[None, :, None] >= ends[:, None, :]).astype(jnp.int32), axis=2))

def attend_bucket(pieces):
    query_rows, key_rows, value_rows, item_row, keys_row = pieces
    query_heads = query_rows.reshape(BUCKET, HEADS, HEAD)
    key_heads = key_rows.reshape(BUCKET, HEADS, HEAD)
    value_heads = value_rows.reshape(BUCKET, HEADS, HEAD)
    scores = jnp.einsum('qhd,khd->hqk', query_heads, key_heads, precision=lax.Precision.HIGHEST)
    scores = low_back(scores * HEAD ** (-0.5))
    places = jnp.arange(BUCKET, dtype=jnp.int32)
    allowed = (item_row[:, None] == item_row[None, :]) & ((keys_row[None, :] == 1) | (places[:, None] == places[None, :]))
    scores = jnp.where(allowed[None], scores, negative_fill)
    row_top = lax.optimization_barrier(jnp.max(scores, axis=2, keepdims=True))
    exponent = jnp.exp(scores - row_top)
    attn_probs = low(exponent / lax.optimization_barrier(jnp.sum(exponent, axis=2, keepdims=True)))
    mixed_heads = jnp.einsum('hqk,khd->qhd', attn_probs, value_heads, precision=lax.Precision.HIGHEST)
    return mixed_heads.reshape(BUCKET, HEADS * HEAD)

def layer_forward(tokens_f, item_ids, keys_rows, live_rows, params):
    query_weight, query_bias, key_weight, value_weight, value_bias, output_weight, output_bias, first_gain, first_shift, inner_weight, inner_bias, outer_weight, outer_bias, second_gain, second_shift = params
    row_count = tokens_f.shape[0]
    blocks = row_count // BUCKET
    queries = low_back(low(product(tokens_f, query_weight) + query_bias))
    key_rows = low_back(low(product(tokens_f, key_weight)))
    values = low_back(low(product(tokens_f, value_weight) + value_bias))
    mixed_rows = lax.map(jax.checkpoint(attend_bucket), (queries.reshape(blocks, BUCKET, HEADS * HEAD), key_rows.reshape(blocks, BUCKET, HEADS * HEAD), values.reshape(blocks, BUCKET, HEADS * HEAD), item_ids, keys_rows))
    mixed_rows = low_back(low(mixed_rows.reshape(row_count, HEADS * HEAD)))
    attended = low_back(product(mixed_rows, output_weight) + output_bias)
    normed_first = layer_norm(tokens_f + attended, first_gain, first_shift)
    inner_pre = low_back(product(low(normed_first), inner_weight) + inner_bias)
    hidden = low(jax.nn.gelu(inner_pre, approximate=False))
    outer_sum = low_back(product(hidden, outer_weight) + outer_bias)
    return layer_norm(normed_first + outer_sum, second_gain, second_shift) * live_rows[:, None]

def reference(tokens, lengths, key_mask, query_weight, query_bias, key_weight, value_weight, value_bias, output_weight, output_bias, first_gain, first_shift, inner_weight, inner_bias, outer_weight, outer_bias, second_gain, second_shift, cotangent):
    weights = tuple((weight.astype(jnp.float32) for weight in (query_weight, query_bias, key_weight, value_weight, value_bias, output_weight, output_bias, first_gain, first_shift, inner_weight, inner_bias, outer_weight, outer_bias, second_gain, second_shift)))
    row_count = BUCKETS_DEV * BUCKET

    def one_group(totals, group_data):
        group_tokens, group_lengths, group_keys, group_cot = group_data
        item_ids = bucket_items(group_lengths)
        live_rows = (item_ids < ITEMS).reshape(row_count).astype(jnp.float32)
        keys_rows = group_keys.reshape(BUCKETS_DEV, BUCKET)

        def forward(tokens_f, params):
            return layer_forward(tokens_f, item_ids, keys_rows, live_rows, params)
        result, pullback = jax.vjp(forward, group_tokens.astype(jnp.float32), weights)
        tokens_back, weight_back = pullback(group_cot.astype(jnp.float32))
        new_totals = tuple((running + gradient for running, gradient in zip(totals, weight_back)))
        return (new_totals, (result.astype(jnp.bfloat16), tokens_back.astype(jnp.bfloat16)))
    zeros = tuple((jnp.zeros(weight.shape, jnp.float32) for weight in weights))
    totals, (outputs, token_grads) = lax.scan(one_group, zeros, (tokens.reshape(N_DP, row_count, D), lengths.reshape(N_DP, BUCKETS_DEV, ITEMS), key_mask.reshape(N_DP, row_count), cotangent.reshape(N_DP, row_count, D)))
    return (outputs.reshape(TOKENS, D), token_grads.reshape(TOKENS, D), totals[0], totals[1], totals[2], totals[3], totals[4], totals[5], totals[6], totals[7], totals[8], totals[9], totals[10], totals[11], totals[12], totals[13], totals[14])
```

```python
import jax
import jax.numpy as jnp
from jax import lax
from jax.sharding import PartitionSpec as P

HEAD = 64
BUCKET = 512
ITEMS = 8


negative_fill = -1e30
epsilon = 1e-06
f32 = jnp.float32
bf16 = jnp.bfloat16


def contract_rows(left, right):
    return lax.dot_general(left, right, (((0,), (0,)), ((), ())), preferred_element_type=f32)


def contract_cols(left, right):
    return lax.dot_general(left, right, (((1,), (1,)), ((), ())), preferred_element_type=f32)


def dot(left, right):
    return jnp.dot(left, right, preferred_element_type=f32)


def norm_rows(values, norm_gain, norm_shift):
    centred = values - jnp.mean(values, axis=1, keepdims=True)
    inv_scale = lax.rsqrt(jnp.mean(centred * centred, axis=1, keepdims=True) + epsilon)
    normed = centred * inv_scale
    return (normed * norm_gain + norm_shift, normed, inv_scale)


def norm_back(grad_rows, norm_gain, normed, inv_scale):
    scaled = grad_rows * norm_gain
    return inv_scale * (
        scaled
        - jnp.mean(scaled, axis=1, keepdims=True)
        - normed * jnp.mean(scaled * normed, axis=1, keepdims=True)
    )


def bucket_items(lengths):
    ends = jnp.cumsum(lengths, axis=1)
    places = jnp.arange(BUCKET, dtype=jnp.int32)
    return jnp.sum((places[None, :, None] >= ends[:, None, :]).astype(jnp.int32), axis=2)


def bucket_scores(query_heads, key_heads, item_row, keys_row):
    places = jnp.arange(BUCKET, dtype=jnp.int32)
    allowed = (item_row[:, None] == item_row[None, :]) & (
        (keys_row[None, :] == 1) | (places[:, None] == places[None, :])
    )
    scores = (
        jnp.einsum("qhd,khd->hqk", query_heads, key_heads, preferred_element_type=f32)
        * HEAD ** (-0.5)
    )
    return jnp.where(allowed[None], scores, negative_fill)


def attend_forward(query_rows, key_rows, value_rows, item_row, keys_row):
    query_heads = query_rows.reshape(BUCKET, -1, HEAD)
    key_heads = key_rows.reshape(BUCKET, -1, HEAD)
    value_heads = value_rows.reshape(BUCKET, -1, HEAD)
    scores = bucket_scores(query_heads, key_heads, item_row, keys_row)
    row_top = jnp.max(scores, axis=2, keepdims=True)
    exponent = jnp.exp(scores - row_top)
    row_total = jnp.sum(exponent, axis=2, keepdims=True)
    attn_probs = (exponent / row_total).astype(bf16)
    mixed_heads = jnp.einsum("hqk,khd->qhd", attn_probs, value_heads, preferred_element_type=f32)
    return (
        mixed_heads.reshape(BUCKET, -1).astype(bf16),
        (row_top + jnp.log(row_total))[..., 0],
    )


def attend_backward(query_rows, key_rows, value_rows, item_row, keys_row, log_total, grad_rows):
    query_heads = query_rows.reshape(BUCKET, -1, HEAD)
    key_heads = key_rows.reshape(BUCKET, -1, HEAD)
    value_heads = value_rows.reshape(BUCKET, -1, HEAD)
    grad_heads = grad_rows.reshape(BUCKET, -1, HEAD)
    scores = bucket_scores(query_heads, key_heads, item_row, keys_row)
    attn_probs = jnp.exp(scores - log_total[..., None])
    grad_probs = jnp.einsum("qhd,khd->hqk", grad_heads, value_heads, preferred_element_type=f32)
    grad_scores = (
        attn_probs * (grad_probs - jnp.sum(attn_probs * grad_probs, axis=2, keepdims=True))
    ).astype(bf16)
    grad_query = jnp.einsum(
        "hqk,khd->qhd", grad_scores, key_heads, preferred_element_type=f32
    ) * HEAD ** (-0.5)
    grad_key = jnp.einsum(
        "hqk,qhd->khd", grad_scores, query_heads, preferred_element_type=f32
    ) * HEAD ** (-0.5)
    grad_value = jnp.einsum(
        "hqk,qhd->khd", attn_probs.astype(bf16), grad_heads, preferred_element_type=f32
    )
    return (
        grad_query.reshape(BUCKET, -1).astype(bf16),
        grad_key.reshape(BUCKET, -1).astype(bf16),
        grad_value.reshape(BUCKET, -1).astype(bf16),
    )


def gelu_slope(values):
    normal_cdf = 0.5 * (1.0 + lax.erf(values * 0.7071067811865476))
    return normal_cdf + values * jnp.exp(-0.5 * values * values) * 0.3989422804014327


def on_device(
    n_dp,
    n_z,
    tokens,
    lengths,
    key_mask,
    query_weight,
    query_bias,
    key_weight,
    value_weight,
    value_bias,
    output_weight,
    output_bias,
    first_gain,
    first_shift,
    inner_weight,
    inner_bias,
    outer_weight,
    outer_bias,
    second_gain,
    second_shift,
    cotangent,
):
    width = tokens.shape[1]
    mine = query_weight.shape[1]
    units = inner_weight.shape[1]
    rows = tokens.shape[0] // n_z
    blocks = rows // BUCKET
    dp = lax.axis_index("dp")
    z = lax.axis_index("tensor")

    def spread(shard):
        piece = shard.shape[0] // n_dp
        part = lax.dynamic_slice_in_dim(shard, dp * piece, piece, 0)
        planes = lax.all_gather(part, "tensor")
        return lax.all_gather(planes, "dp", axis=1, tiled=True)

    def collect(partial):
        plane = lax.psum_scatter(partial.astype(bf16), "dp", scatter_dimension=1, tiled=True)
        part = lax.psum_scatter(plane, "tensor", scatter_dimension=0, tiled=False)
        return lax.all_gather(part, "dp", axis=0, tiled=True).astype(f32)

    attention_all = spread(jnp.concatenate([query_weight, key_weight, value_weight], axis=1))
    mixer_all = spread(output_weight)
    inner_all = spread(inner_weight)
    outer_all = spread(outer_weight)
    biases = lax.all_gather(jnp.concatenate([query_bias, value_bias, inner_bias]), "tensor")
    biases = biases.astype(f32)
    query_bias_all = biases[:, :mine]
    value_bias_all = biases[:, mine : 2 * mine]
    inner_bias_all = biases[:, 2 * mine :]

    my_tokens = lax.dynamic_slice_in_dim(tokens, z * rows, rows, 0)
    my_cotangent = lax.dynamic_slice_in_dim(cotangent, z * rows, rows, 0)
    my_lengths = lax.dynamic_slice_in_dim(lengths, z * blocks, blocks, 0)
    my_keys = lax.dynamic_slice_in_dim(key_mask, z * rows, rows, 0).reshape(blocks, BUCKET)
    item_ids = bucket_items(my_lengths)
    live_rows = (item_ids < ITEMS).reshape(rows, 1).astype(f32)

    projected = [dot(my_tokens, attention_all[j]) for j in range(n_z)]
    queries = jnp.concatenate(
        [(projected[j][:, :mine] + query_bias_all[j]).astype(bf16) for j in range(n_z)], axis=1
    )
    key_rows = jnp.concatenate(
        [projected[j][:, mine : 2 * mine].astype(bf16) for j in range(n_z)], axis=1
    )
    values = jnp.concatenate(
        [(projected[j][:, 2 * mine :] + value_bias_all[j]).astype(bf16) for j in range(n_z)],
        axis=1,
    )

    def bucket(matrix, b):
        return matrix[b * BUCKET : (b + 1) * BUCKET]

    mixed_parts, log_parts = [], []
    for b in range(blocks):
        mixed_b, log_b = attend_forward(
            bucket(queries, b), bucket(key_rows, b), bucket(values, b), item_ids[b], my_keys[b]
        )
        mixed_parts.append(mixed_b)
        log_parts.append(log_b)
    mixed_rows = jnp.concatenate(mixed_parts, axis=0)

    mixer = mixer_all.reshape(-1, width)
    attended = dot(mixed_rows, mixer) + output_bias
    first_sum = my_tokens.astype(f32) + attended
    normed_out, first_normed, first_scale = norm_rows(first_sum, first_gain, first_shift)
    normed_low = normed_out.astype(bf16)
    inner_pre = [dot(normed_low, inner_all[j]) + inner_bias_all[j] for j in range(n_z)]
    hidden = [jax.nn.gelu(pre, approximate=False).astype(bf16) for pre in inner_pre]
    outer_sum = sum(dot(hidden[j], outer_all[j]) for j in range(n_z)) + outer_bias
    final_rows, second_normed, second_scale = norm_rows(
        normed_out + outer_sum, second_gain, second_shift
    )
    my_output = (final_rows * live_rows).astype(bf16)
    output = lax.all_gather(my_output, "tensor", axis=0, tiled=True)

    grad_final = my_cotangent.astype(f32) * live_rows
    second_gain_grad = jnp.sum(grad_final * second_normed, axis=0)
    second_shift_grad = jnp.sum(grad_final, axis=0)
    grad_second = norm_back(grad_final, second_gain, second_normed, second_scale)
    grad_outer = grad_second.astype(bf16)
    outer_bias_grad = jnp.sum(grad_outer, axis=0, dtype=f32)
    grad_inner = [
        (contract_cols(grad_outer, outer_all[j]) * gelu_slope(inner_pre[j])).astype(bf16)
        for j in range(n_z)
    ]
    outer_weight_grad = collect(jnp.stack([contract_rows(h, grad_outer) for h in hidden]))
    inner_bias_grad = jnp.stack([jnp.sum(g, axis=0, dtype=f32) for g in grad_inner])
    inner_weight_grad = collect(jnp.stack([contract_rows(normed_low, g) for g in grad_inner]))
    grad_normed = grad_second + sum(
        contract_cols(grad_inner[j], inner_all[j]) for j in range(n_z)
    )
    first_gain_grad = jnp.sum(grad_normed * first_normed, axis=0)
    first_shift_grad = jnp.sum(grad_normed, axis=0)
    grad_first = norm_back(grad_normed, first_gain, first_normed, first_scale)
    grad_attended = grad_first.astype(bf16)
    output_bias_grad = jnp.sum(grad_attended, axis=0, dtype=f32)
    mixer_grad = contract_rows(mixed_rows, grad_attended)
    output_weight_grad = collect(mixer_grad.reshape(n_z, mine, width))
    grad_mixed = contract_cols(grad_attended, mixer).astype(bf16)

    backs = [
        attend_backward(
            bucket(queries, b),
            bucket(key_rows, b),
            bucket(values, b),
            item_ids[b],
            my_keys[b],
            log_parts[b],
            bucket(grad_mixed, b),
        )
        for b in range(blocks)
    ]
    grad_query = jnp.concatenate([back[0] for back in backs], axis=0)
    grad_key = jnp.concatenate([back[1] for back in backs], axis=0)
    grad_value = jnp.concatenate([back[2] for back in backs], axis=0)
    grad_parts = [
        jnp.concatenate(
            [g[:, j * mine : (j + 1) * mine] for g in (grad_query, grad_key, grad_value)], axis=1
        )
        for j in range(n_z)
    ]
    my_tokens_grad = (
        grad_first + sum(contract_cols(grad_parts[j], attention_all[j]) for j in range(n_z))
    ).astype(bf16)
    tokens_grad = lax.all_gather(my_tokens_grad, "tensor", axis=0, tiled=True)
    attention_grad = collect(jnp.stack([contract_rows(my_tokens, g) for g in grad_parts]))
    query_bias_grad = jnp.sum(grad_query, axis=0, dtype=f32).reshape(n_z, mine)
    value_bias_grad = jnp.sum(grad_value, axis=0, dtype=f32).reshape(n_z, mine)

    small = jnp.concatenate(
        [
            output_bias_grad,
            first_gain_grad,
            first_shift_grad,
            outer_bias_grad,
            second_gain_grad,
            second_shift_grad,
            inner_bias_grad.reshape(-1),
            query_bias_grad.reshape(-1),
            value_bias_grad.reshape(-1),
        ]
    )
    small = lax.psum(small, ("dp", "tensor"))
    shared = small[: 6 * width].reshape(6, width)

    def own(start, count):
        return lax.dynamic_slice_in_dim(small, start + z * count, count, 0)

    inner_start = 6 * width
    query_start = inner_start + n_z * units
    value_start = query_start + n_z * mine
    return (
        output,
        tokens_grad,
        attention_grad[:, :mine],
        own(query_start, mine),
        attention_grad[:, mine : 2 * mine],
        attention_grad[:, 2 * mine :],
        own(value_start, mine),
        output_weight_grad,
        shared[0],
        shared[1],
        shared[2],
        inner_weight_grad,
        own(inner_start, units),
        outer_weight_grad,
        shared[3],
        shared[4],
        shared[5],
    )


def solution(mesh):
    n_dp, n_z = mesh.shape["dp"], mesh.shape["tensor"]
    in_specs = (
        P("dp", None),
        P("dp", None),
        P("dp"),
        P(None, "tensor"),
        P("tensor"),
        P(None, "tensor"),
        P(None, "tensor"),
        P("tensor"),
        P("tensor", None),
        P(),
        P(),
        P(),
        P(None, "tensor"),
        P("tensor"),
        P("tensor", None),
        P(),
        P(),
        P(),
        P("dp", None),
    )
    out_specs = (
        P("dp", None),
        P("dp", None),
        P(None, "tensor"),
        P("tensor"),
        P(None, "tensor"),
        P(None, "tensor"),
        P("tensor"),
        P("tensor", None),
        P(),
        P(),
        P(),
        P(None, "tensor"),
        P("tensor"),
        P("tensor", None),
        P(),
        P(),
        P(),
    )

    def program(*args):
        return on_device(n_dp, n_z, *args)

    return jax.shard_map(
        program, mesh=mesh, in_specs=in_specs, out_specs=out_specs, check_vma=False
    )
```

```python
import jax
import jax.numpy as jnp
from jax import lax
from jax.sharding import PartitionSpec as P

HEAD = 64
BUCKET = 512
ITEMS = 8


negative_fill = -1e30
epsilon = 1e-06
f32 = jnp.float32
bf16 = jnp.bfloat16


def contract_rows(left, right):
    return lax.dot_general(left, right, (((0,), (0,)), ((), ())), preferred_element_type=f32)


def contract_cols(left, right):
    return lax.dot_general(left, right, (((1,), (1,)), ((), ())), preferred_element_type=f32)


def dot(left, right):
    return jnp.dot(left, right, preferred_element_type=f32)


def norm_rows(values, norm_gain, norm_shift):
    centred = values - jnp.mean(values, axis=1, keepdims=True)
    inv_scale = lax.rsqrt(jnp.mean(centred * centred, axis=1, keepdims=True) + epsilon)
    normed = centred * inv_scale
    return (normed * norm_gain + norm_shift, normed, inv_scale)


def norm_back(grad_rows, norm_gain, normed, inv_scale):
    scaled = grad_rows * norm_gain
    return inv_scale * (
        scaled
        - jnp.mean(scaled, axis=1, keepdims=True)
        - normed * jnp.mean(scaled * normed, axis=1, keepdims=True)
    )


def bucket_items(lengths):
    ends = jnp.cumsum(lengths, axis=1)
    places = jnp.arange(BUCKET, dtype=jnp.int32)
    return jnp.sum((places[None, :, None] >= ends[:, None, :]).astype(jnp.int32), axis=2)


def bucket_scores(query_heads, key_heads, item_rows, keys_rows):
    places = jnp.arange(BUCKET, dtype=jnp.int32)
    allowed = (item_rows[:, :, None] == item_rows[:, None, :]) & (
        (keys_rows[:, None, :] == 1) | (places[:, None] == places[None, :])
    )
    scores = (
        jnp.einsum("bqhd,bkhd->bhqk", query_heads, key_heads, preferred_element_type=f32)
        * HEAD ** (-0.5)
    )
    return jnp.where(allowed[:, None], scores, negative_fill)


def split_heads(matrix, blocks):
    return matrix.reshape(blocks, BUCKET, -1, HEAD)


def row_probs(scores):
    exponent = jnp.exp(scores - jnp.max(scores, axis=3, keepdims=True))
    return exponent / jnp.sum(exponent, axis=3, keepdims=True)


def attend_forward(query_rows, key_rows, value_rows, item_rows, keys_rows):
    blocks = item_rows.shape[0]
    scores = bucket_scores(
        split_heads(query_rows, blocks), split_heads(key_rows, blocks), item_rows, keys_rows
    )
    attn_probs = row_probs(scores).astype(bf16)
    mixed_heads = jnp.einsum(
        "bhqk,bkhd->bqhd", attn_probs, split_heads(value_rows, blocks), preferred_element_type=f32
    )
    return mixed_heads.reshape(query_rows.shape).astype(bf16)


def attend_backward(query_rows, key_rows, value_rows, item_rows, keys_rows, grad_rows):
    blocks = item_rows.shape[0]
    query_heads = split_heads(query_rows, blocks)
    key_heads = split_heads(key_rows, blocks)
    value_heads = split_heads(value_rows, blocks)
    grad_heads = split_heads(grad_rows, blocks)
    attn_probs = row_probs(bucket_scores(query_heads, key_heads, item_rows, keys_rows))
    grad_probs = jnp.einsum("bqhd,bkhd->bhqk", grad_heads, value_heads, preferred_element_type=f32)
    grad_scores = (
        attn_probs * (grad_probs - jnp.sum(attn_probs * grad_probs, axis=3, keepdims=True))
    ).astype(bf16)
    grad_query = jnp.einsum(
        "bhqk,bkhd->bqhd", grad_scores, key_heads, preferred_element_type=f32
    ) * HEAD ** (-0.5)
    grad_key = jnp.einsum(
        "bhqk,bqhd->bkhd", grad_scores, query_heads, preferred_element_type=f32
    ) * HEAD ** (-0.5)
    grad_value = jnp.einsum(
        "bhqk,bqhd->bkhd", attn_probs.astype(bf16), grad_heads, preferred_element_type=f32
    )
    return tuple(g.reshape(query_rows.shape).astype(bf16) for g in (grad_query, grad_key, grad_value))


def gelu_slope(values):
    normal_cdf = 0.5 * (1.0 + lax.erf(values * 0.7071067811865476))
    return normal_cdf + values * jnp.exp(-0.5 * values * values) * 0.3989422804014327


class Plane:
    def __init__(self, n_dp, n_z):
        self.n_dp, self.n_z = n_dp, n_z
        self.n_core = 2 if n_dp % 2 == 0 else 1
        self.bits = [1 << i for i in range(1, n_dp.bit_length() - 1)][::-1]
        self.dp = lax.axis_index("dp")
        self.z = lax.axis_index("tensor")
        self.core = self.dp & 1

    def swap(self, array, bit):
        return lax.ppermute(array, "dp", [(i, i ^ bit) for i in range(self.n_dp)])

    def shift(self, array, by):
        n = self.n_z
        return lax.ppermute(array, "tensor", [(i, (i + by) % n) for i in range(n)])

    def has(self, bit):
        return (self.dp & bit) != 0

    def piece_start(self, rows):
        return self.core * (rows // 2) + (self.dp >> 1) * (rows // self.n_dp)

    def join(self, own, other, bit, axis):
        return jnp.where(
            self.has(bit),
            jnp.concatenate([other, own], axis=axis),
            jnp.concatenate([own, other], axis=axis),
        )

    def tracks(self, width):
        half = width // 2
        order = list(range(len(self.bits)))
        return ((slice(0, half), order[::-1]), (slice(half, width), order))

    def grow(self, part):
        grown = []
        for columns, order in self.tracks(part.shape[2]):
            track = part[:, :, columns]
            lead = track.shape[0]
            track = track.reshape((lead,) + (1,) * len(self.bits) + track.shape[1:])
            for index in order:
                other = self.swap(track, self.bits[index])
                track = self.join(track, other, self.bits[index], index + 1)
            grown.append(track.reshape(lead, -1, track.shape[-1]))
        return grown

    def gather(self, shard):
        rows = shard.shape[0]
        piece = lax.dynamic_slice_in_dim(shard, self.piece_start(rows), rows // self.n_dp, 0)
        remote = jnp.stack([self.shift(piece, s) for s in range(1, self.n_z)])
        own = lax.dynamic_slice_in_dim(shard, self.core * (rows // 2), rows // 2, 0)
        grown = self.grow(remote)
        return [
            jnp.concatenate([own[None, :, columns], track], axis=0)
            for track, (columns, _) in zip(grown, self.tracks(shard.shape[1]))
        ]

    def reduce(self, keep, send):
        done = []
        for kept, sent, (_, order) in zip(keep, send, self.tracks(2)):
            track = self.add(kept, self.swap(sent.astype(bf16), 1))
            lead, half, width = track.shape
            track = track.reshape((lead,) + (2,) * len(self.bits) + (-1, width))
            for index in order[::-1]:
                bit = self.bits[index]
                mine = jnp.where(self.has(bit), 1, 0)
                away = lax.dynamic_slice_in_dim(track, 1 - mine, 1, index + 1)
                home = lax.dynamic_slice_in_dim(track, mine, 1, index + 1)
                track = self.add(home, self.swap(away, bit))
            done.append(track.reshape(lead, -1, width))
        whole = jnp.concatenate(done, axis=2)
        total = whole[0].astype(f32)
        for s in range(1, self.n_z):
            total = total + self.shift(whole[s], -s).astype(f32)
        return total.astype(bf16)

    def add(self, left, right):
        return (left.astype(f32) + right.astype(f32)).astype(bf16)

    def regather(self, piece):
        whole = []
        for track in self.grow(piece[None]):
            whole.append(self.join(track, self.swap(track, 1), 1, 1)[0])
        return whole


def on_device(
    n_dp,
    n_z,
    tokens,
    lengths,
    key_mask,
    query_weight,
    query_bias,
    key_weight,
    value_weight,
    value_bias,
    output_weight,
    output_bias,
    first_gain,
    first_shift,
    inner_weight,
    inner_bias,
    outer_weight,
    outer_bias,
    second_gain,
    second_shift,
    cotangent,
):
    width = tokens.shape[1]
    mine = query_weight.shape[1]
    units = inner_weight.shape[1]
    all_rows = tokens.shape[0]
    all_blocks = all_rows // BUCKET
    rows = all_rows // n_z
    blocks = rows // BUCKET
    plane = Plane(n_dp, n_z)
    z, core = plane.z, plane.core

    mixer_left, mixer_right = plane.gather(output_weight)
    inner_keep, outer_keep = plane.gather(jnp.concatenate([inner_weight.T, outer_weight], axis=1))
    bias_row = jnp.concatenate([query_bias, value_bias, inner_bias])
    biases = jnp.stack([bias_row] + [plane.shift(bias_row, s) for s in range(1, n_z)]).astype(f32)
    query_bias_all = biases[:, :mine].reshape(-1)
    value_bias_all = biases[:, mine : 2 * mine].reshape(-1)
    inner_bias_all = biases[:, 2 * mine :].reshape(n_z, 2, units // 2)
    bias_keep = lax.dynamic_slice_in_dim(inner_bias_all, core, 1, 1).reshape(-1)
    bias_send = lax.dynamic_slice_in_dim(inner_bias_all, 1 - core, 1, 1).reshape(-1)

    item_ids = bucket_items(lengths)
    keys_rows = key_mask.reshape(all_blocks, BUCKET)

    queries = (dot(tokens, query_weight) + query_bias).astype(bf16)
    key_rows = dot(tokens, key_weight).astype(bf16)
    values = (dot(tokens, value_weight) + value_bias).astype(bf16)
    mixed_all = attend_forward(queries, key_rows, values, item_ids, keys_rows)

    def own_rows(matrix, count, place):
        return lax.dynamic_slice_in_dim(matrix, place * count, count, 0)

    mixed_rows = jnp.concatenate(
        [own_rows(mixed_all, rows, z)]
        + [
            plane.shift(own_rows(mixed_all, rows, lax.rem(z + s, n_z)), s) for s in range(1, n_z)
        ],
        axis=1,
    )

    def whole_rows(track):
        return plane.join(track, plane.swap(track, 1), 1, 1).reshape(n_z * mine, -1)

    mixer = jnp.concatenate([whole_rows(mixer_left), whole_rows(mixer_right)], axis=1)
    inner_send = plane.swap(inner_keep, 1)
    outer_send = plane.swap(outer_keep, 1)
    inner_parts = [w.reshape(-1, width) for w in (inner_keep, inner_send)]
    outer_parts = [w.reshape(-1, width) for w in (outer_keep, outer_send)]
    bias_parts = [bias_keep, bias_send]

    my_tokens = own_rows(tokens, rows, z)
    my_cotangent = own_rows(cotangent, rows, z)
    my_items = own_rows(item_ids, blocks, z)
    my_keys = own_rows(keys_rows, blocks, z)
    live_rows = (my_items < ITEMS).reshape(rows, 1).astype(f32)

    attended = dot(mixed_rows, mixer) + output_bias
    first_sum = my_tokens.astype(f32) + attended
    normed_out, first_normed, first_scale = norm_rows(first_sum, first_gain, first_shift)
    normed_low = normed_out.astype(bf16)
    inner_pre = [contract_cols(normed_low, w) + b for w, b in zip(inner_parts, bias_parts)]
    hidden = [jax.nn.gelu(pre, approximate=False).astype(bf16) for pre in inner_pre]
    outer_sum = sum(dot(h, w) for h, w in zip(hidden, outer_parts)) + outer_bias
    final_rows, second_normed, second_scale = norm_rows(
        normed_out + outer_sum, second_gain, second_shift
    )
    my_output = (final_rows * live_rows).astype(bf16)
    output = lax.all_gather(my_output, "tensor", axis=0, tiled=True)

    left, right = plane.gather(
        jnp.concatenate([query_weight.T, key_weight.T, value_weight.T], axis=1)
    )
    attention_all = jnp.concatenate([whole_rows(left), whole_rows(right)], axis=1)
    query_all, key_all, value_all = (
        attention_all[:, i * width : (i + 1) * width] for i in range(3)
    )
    my_queries = (contract_cols(my_tokens, query_all) + query_bias_all).astype(bf16)
    my_key_rows = contract_cols(my_tokens, key_all).astype(bf16)
    my_values = (contract_cols(my_tokens, value_all) + value_bias_all).astype(bf16)

    grad_final = my_cotangent.astype(f32) * live_rows
    second_gain_grad = jnp.sum(grad_final * second_normed, axis=0)
    second_shift_grad = jnp.sum(grad_final, axis=0)
    grad_second = norm_back(grad_final, second_gain, second_normed, second_scale)
    grad_outer = grad_second.astype(bf16)
    outer_bias_grad = jnp.sum(grad_outer, axis=0, dtype=f32)
    grad_inner = [
        (contract_cols(grad_outer, w) * gelu_slope(pre)).astype(bf16)
        for w, pre in zip(outer_parts, inner_pre)
    ]
    outer_grads = [
        contract_rows(h, grad_outer).astype(bf16).reshape(n_z, -1, width) for h in hidden
    ]
    inner_grads = [
        contract_rows(g, normed_low).astype(bf16).reshape(n_z, -1, width) for g in grad_inner
    ]
    inner_bias_grads = [
        jnp.sum(g, axis=0, dtype=f32).reshape(n_z, 1, units // 2) for g in grad_inner
    ]
    inner_bias_grad = plane.join(*inner_bias_grads, 1, 1).reshape(n_z, units)
    feed_piece = plane.reduce(
        (inner_grads[0], outer_grads[0]), (inner_grads[1], outer_grads[1])
    )
    inner_grad, outer_grad = plane.regather(feed_piece)

    grad_normed = grad_second + sum(dot(g, w) for g, w in zip(grad_inner, inner_parts))
    first_gain_grad = jnp.sum(grad_normed * first_normed, axis=0)
    first_shift_grad = jnp.sum(grad_normed, axis=0)
    grad_first = norm_back(grad_normed, first_gain, first_normed, first_scale)
    grad_attended = grad_first.astype(bf16)
    output_bias_grad = jnp.sum(grad_attended, axis=0, dtype=f32)
    mixer_grad = contract_rows(mixed_rows, grad_attended).astype(bf16)
    grad_mixed = contract_cols(grad_attended, mixer).astype(bf16)
    grad_query, grad_key, grad_value = attend_backward(
        my_queries, my_key_rows, my_values, my_items, my_keys, grad_mixed
    )
    my_tokens_grad = (
        grad_first + dot(grad_query, query_all) + dot(grad_key, key_all) + dot(grad_value, value_all)
    ).astype(bf16)
    tokens_grad = lax.all_gather(my_tokens_grad, "tensor", axis=0, tiled=True)

    query_grad, key_grad, value_grad = (
        contract_rows(g, my_tokens).astype(bf16) for g in (grad_query, grad_key, grad_value)
    )
    bundle = jnp.concatenate([query_grad, key_grad, value_grad, mixer_grad], axis=1)
    bundle = bundle.reshape(n_z, 2, mine // 2, 4 * width)
    bundle_keep = lax.dynamic_slice_in_dim(bundle, core, 1, 1)[:, 0]
    bundle_send = lax.dynamic_slice_in_dim(bundle, 1 - core, 1, 1)[:, 0]
    sides = [columns for columns, _ in plane.tracks(4 * width)]
    attention_piece = plane.reduce(
        [bundle_keep[:, :, side] for side in sides], [bundle_send[:, :, side] for side in sides]
    )
    query_key_grad, value_output_grad = plane.regather(attention_piece)
    query_bias_grad = jnp.sum(grad_query, axis=0, dtype=f32).reshape(n_z, mine)
    value_bias_grad = jnp.sum(grad_value, axis=0, dtype=f32).reshape(n_z, mine)

    shared = jnp.concatenate(
        [
            output_bias_grad,
            first_gain_grad,
            first_shift_grad,
            outer_bias_grad,
            second_gain_grad,
            second_shift_grad,
        ]
    )
    split = jnp.concatenate([inner_bias_grad, query_bias_grad, value_bias_grad], axis=1)
    small = jnp.concatenate([shared, split.reshape(-1)])
    for bit in [1] + plane.bits:
        small = small + plane.swap(small, bit)
    n_shared, n_split = 6 * width, split.shape[1]
    shared = small[:n_shared]
    split = small[n_shared : n_shared + n_split]
    for s in range(1, n_z):
        there = plane.shift(small, -s)
        shared = shared + there[:n_shared]
        split = split + there[n_shared + s * n_split : n_shared + (s + 1) * n_split]
    shared = shared.reshape(6, width)

    return (
        output,
        tokens_grad,
        query_key_grad[:, :width].T.astype(f32),
        split[units : units + mine],
        query_key_grad[:, width:].T.astype(f32),
        value_output_grad[:, :width].T.astype(f32),
        split[units + mine :],
        value_output_grad[:, width:].astype(f32),
        shared[0],
        shared[1],
        shared[2],
        inner_grad.T.astype(f32),
        split[:units],
        outer_grad.astype(f32),
        shared[3],
        shared[4],
        shared[5],
    )


def solution(mesh):
    n_dp, n_z = mesh.shape["dp"], mesh.shape["tensor"]
    in_specs = (
        P("dp", None),
        P("dp", None),
        P("dp"),
        P(None, "tensor"),
        P("tensor"),
        P(None, "tensor"),
        P(None, "tensor"),
        P("tensor"),
        P("tensor", None),
        P(),
        P(),
        P(),
        P(None, "tensor"),
        P("tensor"),
        P("tensor", None),
        P(),
        P(),
        P(),
        P("dp", None),
    )
    out_specs = (
        P("dp", None),
        P("dp", None),
        P(None, "tensor"),
        P("tensor"),
        P(None, "tensor"),
        P(None, "tensor"),
        P("tensor"),
        P("tensor", None),
        P(),
        P(),
        P(),
        P(None, "tensor"),
        P("tensor"),
        P("tensor", None),
        P(),
        P(),
        P(),
    )

    def program(*args):
        return on_device(n_dp, n_z, *args)

    return jax.shard_map(
        program, mesh=mesh, in_specs=in_specs, out_specs=out_specs, check_vma=False
    )
```

```python
import functools

import jax
import jax.numpy as jnp
from jax import lax
from jax.experimental import pallas as pl
from jax.experimental.pallas import tpu as pltpu
from jax.sharding import PartitionSpec as P

HEAD = 64
BUCKET = 512
ITEMS = 8


negative_fill = -1e30
epsilon = 1e-06
f32 = jnp.float32
bf16 = jnp.bfloat16
VMEM_BYTES = 56 * 1024 * 1024


def dot(left, right):
    return jnp.dot(left, right, preferred_element_type=f32)


def contract_rows(left, right):
    return lax.dot_general(left, right, (((0,), (0,)), ((), ())), preferred_element_type=f32)


def contract_cols(left, right):
    return lax.dot_general(left, right, (((1,), (1,)), ((), ())), preferred_element_type=f32)


def norm_rows(values):
    centred = values - jnp.mean(values, axis=1, keepdims=True)
    inv_scale = lax.rsqrt(jnp.mean(centred * centred, axis=1, keepdims=True) + epsilon)
    return centred * inv_scale, inv_scale


def norm_back(grad_rows, norm_gain, normed, inv_scale):
    scaled = grad_rows * norm_gain
    return inv_scale * (
        scaled
        - jnp.mean(scaled, axis=1, keepdims=True)
        - normed * jnp.mean(scaled * normed, axis=1, keepdims=True)
    )


def column_sum(matrix):
    return jnp.sum(matrix.astype(f32), axis=0, keepdims=True)


def fixed(shape):
    return pl.BlockSpec(shape, lambda *_: (0,) * len(shape))


def params(axes):
    return pltpu.CompilerParams(
        dimension_semantics=("arbitrary",) * axes, vmem_limit_bytes=VMEM_BYTES
    )


def mask_bias(code_column, item_row):
    shape = (BUCKET, BUCKET)
    diagonal = lax.broadcasted_iota(jnp.int32, shape, 0) == lax.broadcasted_iota(
        jnp.int32, shape, 1
    )
    return jnp.where((code_column == item_row) | diagonal, 0.0, negative_fill).astype(f32)


def attend_forward_kernel(
    tokens_ref, query_ref, key_ref, value_ref, query_bias_ref, value_bias_ref, code_ref, item_ref,
    mixed_ref,
):
    rows = tokens_ref[...]
    queries = contract_cols(query_ref[...], rows) + query_bias_ref[...]
    queries = (queries.astype(bf16) * HEAD ** (-0.5)).astype(bf16)
    keys = dot(rows, key_ref[...]).astype(bf16)
    values = (contract_cols(value_ref[...], rows) + value_bias_ref[...]).astype(bf16)
    bias = mask_bias(code_ref[0], item_ref[0])
    parts = []
    for head in range(queries.shape[0] // HEAD):
        at = slice(head * HEAD, (head + 1) * HEAD)
        scores = dot(keys[:, at], queries[at]) + bias
        exponent = jnp.exp(scores - jnp.max(scores, axis=0, keepdims=True))
        total = jnp.sum(exponent, axis=0, keepdims=True)
        parts.append(dot(values[at], exponent.astype(bf16)) / total)
    mixed_ref[...] = jnp.concatenate(parts, axis=0).T.astype(bf16)


def attend_forward(tokens, query_t, key_weight, value_t, query_bias, value_bias, codes, items):
    blocks = codes.shape[0]
    width, mine = key_weight.shape
    return pl.pallas_call(
        attend_forward_kernel,
        grid=(blocks,),
        in_specs=[
            pl.BlockSpec((BUCKET, width), lambda b: (b, 0)),
            fixed((mine, width)),
            fixed((width, mine)),
            fixed((mine, width)),
            fixed((mine, 1)),
            fixed((mine, 1)),
            pl.BlockSpec((1, BUCKET, 1), lambda b: (b, 0, 0)),
            pl.BlockSpec((1, 1, BUCKET), lambda b: (b, 0, 0)),
        ],
        out_specs=pl.BlockSpec((BUCKET, mine), lambda b: (b, 0)),
        out_shape=jax.ShapeDtypeStruct((blocks * BUCKET, mine), bf16),
        compiler_params=params(1),
        name="attend_forward",
    )(tokens, query_t, key_weight, value_t, query_bias, value_bias, codes, items)


def feed_forward_kernel(
    parts,
    mixed_ref, mixer_ref, tokens_ref, cotangent_ref, live_ref, vectors_ref,
    inner_keep_ref, outer_keep_ref, bias_keep_ref, inner_send_ref, outer_send_ref, bias_send_ref,
    output_ref, hidden_keep_ref, slope_keep_ref, hidden_send_ref, slope_send_ref,
    normed_low_ref, first_normed_ref, first_scale_ref, grad_second_ref, grad_outer_ref, sums_ref,
    normed_out, outer_sum,
):
    step = pl.program_id(0)
    output_bias, first_gain, first_shift, outer_bias, second_gain, second_shift = (
        vectors_ref[i : i + 1, :] for i in range(6)
    )

    @pl.when(step == 0)
    def _():
        attended = dot(mixed_ref[...], mixer_ref[...]) + output_bias
        normed, inv_scale = norm_rows(tokens_ref[...].astype(f32) + attended)
        whole = normed * first_gain + first_shift
        first_normed_ref[...] = normed
        first_scale_ref[...] = inv_scale
        normed_out[...] = whole
        normed_low_ref[...] = whole.astype(bf16)
        outer_sum[...] = jnp.zeros_like(outer_sum)

    def chunk(inner_ref, outer_ref, bias_ref, hidden_ref, slope_ref):
        inner_pre = contract_cols(normed_low_ref[...], inner_ref[0]) + bias_ref[0]
        normal_cdf = 0.5 + 0.5 * lax.erf(inner_pre * 0.7071067811865476)
        density = jnp.exp(-0.5 * inner_pre * inner_pre) * 0.3989422804014327
        hidden = (inner_pre * normal_cdf).astype(bf16)
        hidden_ref[...] = hidden
        slope_ref[...] = (normal_cdf + inner_pre * density).astype(bf16)
        outer_sum[...] += dot(hidden, outer_ref[0])

    @pl.when(step < parts)
    def _():
        chunk(inner_keep_ref, outer_keep_ref, bias_keep_ref, hidden_keep_ref, slope_keep_ref)

    @pl.when(step >= parts)
    def _():
        chunk(inner_send_ref, outer_send_ref, bias_send_ref, hidden_send_ref, slope_send_ref)

    @pl.when(step == 2 * parts - 1)
    def _():
        second_sum = normed_out[...] + (outer_sum[...] + outer_bias)
        normed, inv_scale = norm_rows(second_sum)
        live = live_ref[...]
        output_ref[...] = ((normed * second_gain + second_shift) * live).astype(bf16)
        grad_final = cotangent_ref[...].astype(f32) * live
        grad_second = norm_back(grad_final, second_gain, normed, inv_scale)
        grad_outer = grad_second.astype(bf16)
        grad_second_ref[...] = grad_second
        grad_outer_ref[...] = grad_outer
        sums_ref[0:1, :] = column_sum(grad_outer)
        sums_ref[1:2, :] = column_sum(grad_final * normed)
        sums_ref[2:3, :] = column_sum(grad_final)


def feed_forward(
    mixed, mixer, tokens, cotangent, live, vectors, inner_keep, outer_keep, bias_keep,
    inner_send, outer_send, bias_send,
):
    rows, width = tokens.shape
    parts, half = inner_keep.shape[:2]
    first = lambda j: (jnp.minimum(j, parts - 1), 0, 0)
    second = lambda j: (jnp.maximum(j - parts, 0), 0, 0)
    first_columns = lambda j: (0, jnp.minimum(j, parts - 1))
    second_columns = lambda j: (0, jnp.maximum(j - parts, 0))
    weights = [
        pl.BlockSpec((1, half, width), first),
        pl.BlockSpec((1, half, width), first),
        pl.BlockSpec((1, 1, half), first),
        pl.BlockSpec((1, half, width), second),
        pl.BlockSpec((1, half, width), second),
        pl.BlockSpec((1, 1, half), second),
    ]
    units = parts * half
    return pl.pallas_call(
        functools.partial(feed_forward_kernel, parts),
        grid=(2 * parts,),
        in_specs=[
            fixed((rows, width)),
            fixed((width, width)),
            fixed((rows, width)),
            fixed((rows, width)),
            fixed((rows, 1)),
            fixed((8, width)),
        ]
        + weights,
        out_specs=[
            fixed((rows, width)),
            pl.BlockSpec((rows, half), first_columns),
            pl.BlockSpec((rows, half), first_columns),
            pl.BlockSpec((rows, half), second_columns),
            pl.BlockSpec((rows, half), second_columns),
            fixed((rows, width)),
            fixed((rows, width)),
            fixed((rows, 1)),
            fixed((rows, width)),
            fixed((rows, width)),
            fixed((8, width)),
        ],
        out_shape=[
            jax.ShapeDtypeStruct((rows, width), bf16),
            jax.ShapeDtypeStruct((rows, units), bf16),
            jax.ShapeDtypeStruct((rows, units), bf16),
            jax.ShapeDtypeStruct((rows, units), bf16),
            jax.ShapeDtypeStruct((rows, units), bf16),
            jax.ShapeDtypeStruct((rows, width), bf16),
            jax.ShapeDtypeStruct((rows, width), f32),
            jax.ShapeDtypeStruct((rows, 1), f32),
            jax.ShapeDtypeStruct((rows, width), f32),
            jax.ShapeDtypeStruct((rows, width), bf16),
            jax.ShapeDtypeStruct((8, width), f32),
        ],
        scratch_shapes=[pltpu.VMEM((rows, width), f32), pltpu.VMEM((rows, width), f32)],
        compiler_params=params(1),
        name="feed_forward",
    )(
        mixed, mixer, tokens, cotangent, live, vectors, inner_keep, outer_keep, bias_keep,
        inner_send, outer_send, bias_send,
    )


def feed_chunk(grad_outer_ref, normed_low_ref, hidden_ref, slope_ref, inner_ref, outer_ref,
               inner_grad_ref, outer_grad_ref, bias_grad_ref):
    grad_outer = grad_outer_ref[...]
    grad_hidden = contract_cols(grad_outer, outer_ref[0])
    grad_inner = (grad_hidden * slope_ref[...].astype(f32)).astype(bf16)
    outer_grad_ref[0] = contract_rows(hidden_ref[...], grad_outer).astype(bf16)
    inner_grad_ref[0] = contract_rows(grad_inner, normed_low_ref[...]).astype(bf16)
    bias_grad_ref[0] = column_sum(grad_inner)
    return dot(grad_inner, inner_ref[0])


def feed_back_kernel(
    grad_outer_ref, normed_low_ref, hidden_ref, slope_ref, inner_ref, outer_ref, start_ref,
    inner_grad_ref, outer_grad_ref, bias_grad_ref, grad_normed_ref,
):
    @pl.when(pl.program_id(0) == 0)
    def _():
        grad_normed_ref[...] = start_ref[...]

    grad_normed_ref[...] += feed_chunk(
        grad_outer_ref, normed_low_ref, hidden_ref, slope_ref, inner_ref, outer_ref,
        inner_grad_ref, outer_grad_ref, bias_grad_ref,
    )


def feed_back_norm_kernel(
    grad_outer_ref, normed_low_ref, hidden_ref, slope_ref, inner_ref, outer_ref, start_ref,
    first_normed_ref, first_scale_ref, vectors_ref,
    inner_grad_ref, outer_grad_ref, bias_grad_ref, grad_first_ref, grad_attended_ref, sums_ref,
    grad_normed,
):
    @pl.when(pl.program_id(0) == 0)
    def _():
        grad_normed[...] = start_ref[...]

    grad_normed[...] += feed_chunk(
        grad_outer_ref, normed_low_ref, hidden_ref, slope_ref, inner_ref, outer_ref,
        inner_grad_ref, outer_grad_ref, bias_grad_ref,
    )

    @pl.when(pl.program_id(0) == pl.num_programs(0) - 1)
    def _():
        grad_rows, normed = grad_normed[...], first_normed_ref[...]
        grad_first = norm_back(grad_rows, vectors_ref[1:2, :], normed, first_scale_ref[...])
        grad_attended = grad_first.astype(bf16)
        grad_first_ref[...] = grad_first
        grad_attended_ref[...] = grad_attended
        sums_ref[0:1, :] = column_sum(grad_attended)
        sums_ref[1:2, :] = column_sum(grad_rows * normed)
        sums_ref[2:3, :] = column_sum(grad_rows)


def feed_back(grad_outer, normed_low, hidden, slope, inner, outer, start, norm=None):
    rows, width = grad_outer.shape
    parts, half = inner.shape[:2]
    by_part = lambda j: (j, 0, 0)
    columns = lambda j: (0, j)
    whole = fixed((rows, width))
    in_specs = [
        whole,
        whole,
        pl.BlockSpec((rows, half), columns),
        pl.BlockSpec((rows, half), columns),
        pl.BlockSpec((1, half, width), by_part),
        pl.BlockSpec((1, half, width), by_part),
        whole,
    ]
    out_specs = [
        pl.BlockSpec((1, half, width), by_part),
        pl.BlockSpec((1, half, width), by_part),
        pl.BlockSpec((1, 1, half), by_part),
        whole,
    ]
    out_shape = [
        jax.ShapeDtypeStruct((parts, half, width), bf16),
        jax.ShapeDtypeStruct((parts, half, width), bf16),
        jax.ShapeDtypeStruct((parts, 1, half), f32),
        jax.ShapeDtypeStruct((rows, width), f32),
    ]
    args = [grad_outer, normed_low, hidden, slope, inner, outer, start]
    scratch = []
    if norm is not None:
        in_specs += [whole, fixed((rows, 1)), fixed((8, width))]
        out_specs += [whole, fixed((8, width))]
        out_shape += [
            jax.ShapeDtypeStruct((rows, width), bf16),
            jax.ShapeDtypeStruct((8, width), f32),
        ]
        args += list(norm)
        scratch = [pltpu.VMEM((rows, width), f32)]
    return pl.pallas_call(
        feed_back_kernel if norm is None else feed_back_norm_kernel,
        grid=(parts,),
        in_specs=in_specs,
        out_specs=out_specs,
        out_shape=out_shape,
        scratch_shapes=scratch,
        compiler_params=params(1),
        name="feed_back" if norm is None else "feed_back_norm",
    )(*args)


def attend_back_kernel(
    tokens_ref, grad_attended_ref, grad_first_ref, left_ref, right_ref, mixer_ref,
    query_bias_ref, value_bias_ref, code_ref, item_ref,
    grads_ref, tokens_grad_ref, sums_ref,
    bias, total_grad,
):
    pair = pl.program_id(1)

    @pl.when(pair == 0)
    def _():
        bias[...] = mask_bias(code_ref[0], item_ref[0])
        total_grad[...] = grad_first_ref[...]

    rows, grad_attended = tokens_ref[...], grad_attended_ref[...]
    width = rows.shape[1]
    left, right = left_ref[...], right_ref[...]
    query_w = left[:, :width]
    key_w = jnp.concatenate([left[:, width:], right[:, : width // 2]], axis=1)
    value_w = right[:, width // 2 :]
    queries = contract_cols(query_w, rows) + query_bias_ref[...]
    queries = (queries.astype(bf16) * HEAD ** (-0.5)).astype(bf16)
    keys = contract_cols(rows, key_w).astype(bf16)
    values = (contract_cols(rows, value_w) + value_bias_ref[...]).astype(bf16)
    grad_mixed = contract_cols(mixer_ref[...], grad_attended).astype(bf16)
    keys_t = keys.T
    grad_queries, grad_keys, grad_values = [], [], []
    for head in range(keys.shape[1] // HEAD):
        at = slice(head * HEAD, (head + 1) * HEAD)
        scores = dot(keys[:, at], queries[at]) + bias[...]
        exponent = jnp.exp(scores - jnp.max(scores, axis=0, keepdims=True))
        probs = exponent * (1.0 / jnp.sum(exponent, axis=0, keepdims=True))
        grad_probs = dot(values[:, at], grad_mixed[at])
        shift = jnp.sum(probs * grad_probs, axis=0, keepdims=True)
        grad_scores = (probs * (grad_probs - shift)).astype(bf16)
        grad_values.append(contract_cols(probs.astype(bf16), grad_mixed[at]))
        grad_keys.append(contract_cols(grad_scores, queries[at]))
        grad_queries.append(dot(keys_t[at], grad_scores) * HEAD ** (-0.5))
    grad_query = jnp.concatenate(grad_queries, axis=0).T.astype(bf16)
    grad_key = jnp.concatenate(grad_keys, axis=1).astype(bf16)
    grad_value = jnp.concatenate(grad_values, axis=1).astype(bf16)
    grads_ref[0] = grad_query
    grads_ref[1] = grad_key
    grads_ref[2] = grad_value
    sums_ref[0, 0:1, :] = column_sum(grad_query)
    sums_ref[0, 1:2, :] = column_sum(grad_value)
    total_grad[...] += dot(grad_query, query_w) + dot(grad_key, key_w) + dot(grad_value, value_w)

    @pl.when(pair == pl.num_programs(1) - 1)
    def _():
        tokens_grad_ref[...] = total_grad[...].astype(bf16)


def attend_back(
    tokens, grad_attended, grad_first, left, right, mixer, query_bias, value_bias, codes, items
):
    blocks = codes.shape[0]
    rows, width = tokens.shape
    pair = 2 * HEAD
    by_bucket = pl.BlockSpec((BUCKET, width), lambda b, h: (b, 0))
    by_pair = lambda b, h: (h, 0)
    return pl.pallas_call(
        attend_back_kernel,
        grid=(blocks, width // pair),
        in_specs=[
            by_bucket,
            by_bucket,
            by_bucket,
            pl.BlockSpec((pair, left.shape[1]), by_pair),
            pl.BlockSpec((pair, right.shape[1]), by_pair),
            pl.BlockSpec((pair, width), by_pair),
            pl.BlockSpec((pair, 1), by_pair),
            pl.BlockSpec((1, pair), lambda b, h: (0, h)),
            pl.BlockSpec((1, BUCKET, 1), lambda b, h: (b, 0, 0)),
            pl.BlockSpec((1, 1, BUCKET), lambda b, h: (b, 0, 0)),
        ],
        out_specs=[
            pl.BlockSpec((3, BUCKET, pair), lambda b, h: (0, b, h)),
            by_bucket,
            pl.BlockSpec((1, 8, pair), lambda b, h: (b, 0, h)),
        ],
        out_shape=[
            jax.ShapeDtypeStruct((3, rows, width), bf16),
            jax.ShapeDtypeStruct((rows, width), bf16),
            jax.ShapeDtypeStruct((blocks, 8, width), f32),
        ],
        scratch_shapes=[pltpu.VMEM((BUCKET, BUCKET), f32), pltpu.VMEM((BUCKET, width), f32)],
        compiler_params=params(2),
        name="attend_back",
    )(
        tokens, grad_attended, grad_first, left, right, mixer, query_bias, value_bias, codes, items
    )


def attention_grads_kernel(
    order_ref, grads_ref, mixed_ref, tokens_ref, grad_attended_ref, weight_grad_ref
):
    which = order_ref[pl.program_id(0)]

    @pl.when(which < 3)
    def _():
        weight_grad_ref[0] = contract_rows(grads_ref[0], tokens_ref[...]).astype(bf16)

    @pl.when(which == 3)
    def _():
        weight_grad_ref[0] = contract_rows(mixed_ref[...], grad_attended_ref[...]).astype(bf16)


def attention_grads(order, grads, mixed, tokens, grad_attended):
    rows, width = tokens.shape
    cut = 2
    columns = pl.BlockSpec((rows, width // cut), lambda i, j, order: (0, j))
    whole = pl.BlockSpec((rows, width), lambda i, j, order: (0, 0))
    return pl.pallas_call(
        attention_grads_kernel,
        grid_spec=pltpu.PrefetchScalarGridSpec(
            num_scalar_prefetch=1,
            grid=(2, cut),
            in_specs=[
                pl.BlockSpec(
                    (1, rows, width // cut),
                    lambda i, j, order: (jnp.minimum(order[i], 2), 0, j),
                ),
                columns,
                whole,
                whole,
            ],
            out_specs=pl.BlockSpec((1, width // cut, width), lambda i, j, order: (i, j, 0)),
        ),
        out_shape=jax.ShapeDtypeStruct((2, width, width), bf16),
        compiler_params=params(2),
        name="attention_grads",
    )(order, grads, mixed, tokens, grad_attended)


def bucket_items(lengths):
    ends = jnp.cumsum(lengths, axis=1)
    places = jnp.arange(BUCKET, dtype=jnp.int32)
    return jnp.sum((places[None, :, None] >= ends[:, None, :]).astype(jnp.int32), axis=2)


class Plane:
    def __init__(self, n_dp, n_z):
        self.n_dp, self.n_z = n_dp, n_z
        self.n_core = 2 if n_dp % 2 == 0 else 1
        self.bits = [1 << i for i in range(1, n_dp.bit_length() - 1)][::-1]
        self.dp = lax.axis_index("dp")
        self.z = lax.axis_index("tensor")
        self.core = self.dp & 1

    def swap(self, array, bit):
        return lax.ppermute(array, "dp", [(i, i ^ bit) for i in range(self.n_dp)])

    def shift(self, array, by):
        n = self.n_z
        return lax.ppermute(array, "tensor", [(i, (i + by) % n) for i in range(n)])

    def has(self, bit):
        return (self.dp & bit) != 0

    def piece_start(self, rows):
        return self.core * (rows // 2) + (self.dp >> 1) * (rows // self.n_dp)

    def join(self, own, other, bit, axis):
        return jnp.where(
            self.has(bit),
            jnp.concatenate([other, own], axis=axis),
            jnp.concatenate([own, other], axis=axis),
        )

    def tracks(self, width):
        half = width // 2
        order = list(range(len(self.bits)))
        return ((slice(0, half), order[::-1]), (slice(half, width), order))

    def grow(self, part):
        grown = []
        for columns, order in self.tracks(part.shape[2]):
            track = part[:, :, columns]
            lead = track.shape[0]
            track = track.reshape((lead,) + (1,) * len(self.bits) + track.shape[1:])
            for index in order:
                other = self.swap(track, self.bits[index])
                track = self.join(track, other, self.bits[index], index + 1)
            grown.append(track.reshape(lead, -1, track.shape[-1]))
        return grown

    def gather(self, shard):
        rows = shard.shape[0]
        piece = lax.dynamic_slice_in_dim(shard, self.piece_start(rows), rows // self.n_dp, 0)
        remote = jnp.stack([self.shift(piece, s) for s in range(1, self.n_z)])
        own = lax.dynamic_slice_in_dim(shard, self.core * (rows // 2), rows // 2, 0)
        grown = self.grow(remote)
        return [
            jnp.concatenate([own[None, :, columns], track], axis=0)
            for track, (columns, _) in zip(grown, self.tracks(shard.shape[1]))
        ]

    def reduce(self, keep, send):
        done = []
        for kept, sent, (_, order) in zip(keep, send, self.tracks(2)):
            track = self.add(kept, self.swap(sent.astype(bf16), 1))
            lead, half, width = track.shape
            track = track.reshape((lead,) + (2,) * len(self.bits) + (-1, width))
            for index in order[::-1]:
                bit = self.bits[index]
                mine = jnp.where(self.has(bit), 1, 0)
                away = lax.dynamic_slice_in_dim(track, 1 - mine, 1, index + 1)
                home = lax.dynamic_slice_in_dim(track, mine, 1, index + 1)
                track = self.add(home, self.swap(away, bit))
            done.append(track.reshape(lead, -1, width))
        whole = jnp.concatenate(done, axis=2)
        total = whole[0].astype(f32)
        for s in range(1, self.n_z):
            total = total + self.shift(whole[s], -s).astype(f32)
        return total.astype(bf16)

    def add(self, left, right):
        return (left.astype(f32) + right.astype(f32)).astype(bf16)

    def regather(self, piece):
        return [track[0] for track in self.grow(piece[None])]

    def both(self, track):
        return self.join(track, self.swap(track, 1), 1, 0)


def on_device(
    n_dp,
    n_z,
    tokens,
    lengths,
    key_mask,
    query_weight,
    query_bias,
    key_weight,
    value_weight,
    value_bias,
    output_weight,
    output_bias,
    first_gain,
    first_shift,
    inner_weight,
    inner_bias,
    outer_weight,
    outer_bias,
    second_gain,
    second_shift,
    cotangent,
):
    width = tokens.shape[1]
    mine = query_weight.shape[1]
    units = inner_weight.shape[1]
    all_rows = tokens.shape[0]
    all_blocks = all_rows // BUCKET
    rows = all_rows // n_z
    blocks = rows // BUCKET
    plane = Plane(n_dp, n_z)
    z, core = plane.z, plane.core
    query_t, value_t = query_weight.T, value_weight.T

    mixer_left, mixer_right = plane.gather(output_weight)
    inner_keep, outer_keep = plane.gather(jnp.concatenate([inner_weight.T, outer_weight], axis=1))
    bias_row = jnp.concatenate([query_bias, value_bias, inner_bias])
    biases = jnp.stack([bias_row] + [plane.shift(bias_row, s) for s in range(1, n_z)]).astype(f32)
    query_bias_all = biases[:, :mine].reshape(-1)
    value_bias_all = biases[:, mine : 2 * mine].reshape(-1)
    inner_bias_all = biases[:, 2 * mine :].reshape(n_z, 2, units // 2)
    bias_keep = lax.dynamic_slice_in_dim(inner_bias_all, core, 1, 1)
    bias_send = lax.dynamic_slice_in_dim(inner_bias_all, 1 - core, 1, 1)

    item_ids = bucket_items(lengths)
    keys_rows = key_mask.reshape(all_blocks, BUCKET)
    codes = jnp.where(keys_rows == 1, item_ids, -1).reshape(all_blocks, BUCKET, 1)
    items = item_ids.reshape(all_blocks, 1, BUCKET)

    mixed_all = attend_forward(
        tokens,
        query_t,
        key_weight,
        value_t,
        query_bias.astype(f32).reshape(mine, 1),
        value_bias.astype(f32).reshape(mine, 1),
        codes,
        items,
    )

    def own_rows(matrix, count, place):
        return lax.dynamic_slice_in_dim(matrix, place * count, count, 0)

    mixed_rows = jnp.concatenate(
        [own_rows(mixed_all, rows, z)]
        + [
            plane.shift(own_rows(mixed_all, rows, lax.rem(z + s, n_z)), s) for s in range(1, n_z)
        ],
        axis=1,
    )

    def whole_rows(track):
        return plane.join(track, plane.swap(track, 1), 1, 1).reshape(n_z * mine, -1)

    mixer = jnp.concatenate([whole_rows(mixer_left), whole_rows(mixer_right)], axis=1)
    inner_send = plane.swap(inner_keep, 1)
    outer_send = plane.swap(outer_keep, 1)

    my_tokens = own_rows(tokens, rows, z)
    my_cotangent = own_rows(cotangent, rows, z)
    my_items = own_rows(items, blocks, z)
    my_codes = own_rows(codes, blocks, z)
    live_rows = (own_rows(item_ids, blocks, z) < ITEMS).reshape(rows, 1).astype(f32)
    vectors = jnp.stack(
        [output_bias, first_gain, first_shift, outer_bias, second_gain, second_shift]
        + [jnp.zeros_like(output_bias)] * 2
    ).astype(f32)

    (
        my_output, hidden_keep, slope_keep, hidden_send, slope_send,
        normed_low, first_normed, first_scale, grad_second, grad_outer, second_sums,
    ) = feed_forward(
        mixed_rows, mixer, my_tokens, my_cotangent, live_rows, vectors,
        inner_keep, outer_keep, bias_keep, inner_send, outer_send, bias_send,
    )
    output = lax.all_gather(my_output, "tensor", axis=0, tiled=True)

    left, right = (
        whole_rows(track)
        for track in plane.gather(jnp.concatenate([query_t, key_weight.T, value_t], axis=1))
    )

    inner_grad_send, outer_grad_send, bias_grad_send, grad_normed = feed_back(
        grad_outer, normed_low, hidden_send, slope_send, inner_send, outer_send, grad_second
    )
    inner_grad_keep, outer_grad_keep, bias_grad_keep, grad_first, grad_attended, first_sums = (
        feed_back(
            grad_outer, normed_low, hidden_keep, slope_keep, inner_keep, outer_keep, grad_normed,
            (first_normed, first_scale, vectors),
        )
    )
    feed_piece = plane.reduce(
        (inner_grad_keep, outer_grad_keep), (inner_grad_send, outer_grad_send)
    )
    inner_grad, outer_grad = (plane.both(track) for track in plane.regather(feed_piece))
    inner_bias_grad = plane.join(bias_grad_keep, bias_grad_send, 1, 1).reshape(n_z, units)

    attention_back, my_tokens_grad, back_sums = attend_back(
        my_tokens, grad_attended, grad_first, left, right, mixer,
        query_bias_all.reshape(width, 1), value_bias_all.reshape(1, width), my_codes, my_items,
    )
    tokens_grad = lax.all_gather(my_tokens_grad, "tensor", axis=0, tiled=True)

    pair = jnp.arange(2, dtype=jnp.int32)
    grads_send, grads_keep = (
        attention_grads(
            pair + 2 * side, attention_back, mixed_rows, my_tokens, grad_attended
        ).reshape(2, n_z, mine, width)
        for side in (1 - core, core)
    )
    attention_piece = plane.reduce(
        (grads_keep[0], grads_keep[1]), (grads_send[0], grads_send[1])
    )
    kept = jnp.concatenate(plane.regather(attention_piece), axis=0).reshape(2, mine, width)
    grad_list = plane.join(kept, plane.swap(kept, 1), 1, 0)
    back_sums = jnp.sum(back_sums, axis=0)
    query_bias_grad = back_sums[0].reshape(n_z, mine)
    value_bias_grad = back_sums[1].reshape(n_z, mine)

    shared = jnp.concatenate([first_sums[:3], second_sums[:3]], axis=0).reshape(-1)
    split = jnp.concatenate([inner_bias_grad, query_bias_grad, value_bias_grad], axis=1)
    small = jnp.concatenate([shared, split.reshape(-1)])
    for bit in [1] + plane.bits:
        small = small + plane.swap(small, bit)
    n_shared, n_split = 6 * width, split.shape[1]
    shared = small[:n_shared]
    split = small[n_shared : n_shared + n_split]
    for s in range(1, n_z):
        there = plane.shift(small, -s)
        shared = shared + there[:n_shared]
        split = split + there[n_shared + s * n_split : n_shared + (s + 1) * n_split]
    shared = shared.reshape(6, width)

    return (
        output,
        tokens_grad,
        grad_list[0].T.astype(f32),
        split[units : units + mine],
        grad_list[1].T.astype(f32),
        grad_list[2].T.astype(f32),
        split[units + mine :],
        grad_list[3].astype(f32),
        shared[0],
        shared[1],
        shared[2],
        inner_grad.T.astype(f32),
        split[:units],
        outer_grad.astype(f32),
        shared[3],
        shared[4],
        shared[5],
    )


def solution(mesh):
    n_dp, n_z = mesh.shape["dp"], mesh.shape["tensor"]
    in_specs = (
        P("dp", None),
        P("dp", None),
        P("dp"),
        P(None, "tensor"),
        P("tensor"),
        P(None, "tensor"),
        P(None, "tensor"),
        P("tensor"),
        P("tensor", None),
        P(),
        P(),
        P(),
        P(None, "tensor"),
        P("tensor"),
        P("tensor", None),
        P(),
        P(),
        P(),
        P("dp", None),
    )
    out_specs = (
        P("dp", None),
        P("dp", None),
        P(None, "tensor"),
        P("tensor"),
        P(None, "tensor"),
        P(None, "tensor"),
        P("tensor"),
        P("tensor", None),
        P(),
        P(),
        P(),
        P(None, "tensor"),
        P("tensor"),
        P("tensor", None),
        P(),
        P(),
        P(),
    )

    def program(*args):
        return on_device(n_dp, n_z, *args)

    return jax.shard_map(
        program, mesh=mesh, in_specs=in_specs, out_specs=out_specs, check_vma=False
    )
```

```python
import functools

import jax
import jax.numpy as jnp
from jax import lax
from jax.experimental import pallas as pl
from jax.experimental.pallas import tpu as pltpu
from jax.sharding import PartitionSpec as P

HEAD = 64
BUCKET = 512
ITEMS = 8


negative_fill = -1e30
epsilon = 1e-06
f32 = jnp.float32
bf16 = jnp.bfloat16
VMEM_BYTES = 56 * 1024 * 1024


def dot(left, right):
    return jnp.dot(left, right, preferred_element_type=f32)


def contract_rows(left, right):
    return lax.dot_general(left, right, (((0,), (0,)), ((), ())), preferred_element_type=f32)


def contract_cols(left, right):
    return lax.dot_general(left, right, (((1,), (1,)), ((), ())), preferred_element_type=f32)


def norm_rows(values):
    centred = values - jnp.mean(values, axis=1, keepdims=True)
    inv_scale = lax.rsqrt(jnp.mean(centred * centred, axis=1, keepdims=True) + epsilon)
    return centred * inv_scale, inv_scale


def norm_back(grad_rows, norm_gain, normed, inv_scale):
    scaled = grad_rows * norm_gain
    return inv_scale * (
        scaled
        - jnp.mean(scaled, axis=1, keepdims=True)
        - normed * jnp.mean(scaled * normed, axis=1, keepdims=True)
    )


def column_sum(matrix):
    return jnp.sum(matrix.astype(f32), axis=0, keepdims=True)


def fixed(shape):
    return pl.BlockSpec(shape, lambda *_: (0,) * len(shape))


def params(axes):
    return pltpu.CompilerParams(
        dimension_semantics=("arbitrary",) * axes, vmem_limit_bytes=VMEM_BYTES
    )


def item_places(lengths_ref, row, shape, axis):
    places = lax.broadcasted_iota(jnp.int32, shape, axis)
    end = jnp.int32(0)
    items = jnp.zeros(shape, jnp.int32)
    for slot in range(ITEMS):
        end = end + lengths_ref[row, slot]
        items = items + (places >= end).astype(jnp.int32)
    return items


def as_column(row):
    return jnp.broadcast_to(row.astype(f32), (8, row.shape[1])).T[:, :1]


def mask_bias(lengths_ref, row, key_mask):
    shape = (BUCKET, BUCKET)
    diagonal = lax.broadcasted_iota(jnp.int32, shape, 0) == lax.broadcasted_iota(
        jnp.int32, shape, 1
    )
    item_row = item_places(lengths_ref, row, (1, BUCKET), 1)
    item_column = item_places(lengths_ref, row, (BUCKET, 1), 0)
    code_column = jnp.where(as_column(key_mask) == 1.0, item_column, -1)
    return jnp.where((code_column == item_row) | diagonal, 0.0, negative_fill).astype(f32)


def attend_forward_kernel(
    lengths_ref, tokens_ref, query_ref, key_ref, value_ref, query_bias_ref, value_bias_ref,
    key_mask_ref, mixed_ref, query_t, value_t,
):
    @pl.when(pl.program_id(0) == 0)
    def _():
        query_t[...] = query_ref[...].T
        value_t[...] = value_ref[...].T

    rows = tokens_ref[...]
    queries = contract_cols(query_t[...], rows) + as_column(query_bias_ref[...])
    queries = (queries.astype(bf16) * HEAD ** (-0.5)).astype(bf16)
    keys = dot(rows, key_ref[...]).astype(bf16)
    values = (contract_cols(value_t[...], rows) + as_column(value_bias_ref[...])).astype(bf16)
    bias = mask_bias(lengths_ref, pl.program_id(0), key_mask_ref[0])
    parts = []
    for head in range(queries.shape[0] // HEAD):
        at = slice(head * HEAD, (head + 1) * HEAD)
        scores = dot(keys[:, at], queries[at]) + bias
        exponent = jnp.exp(scores - jnp.max(scores, axis=0, keepdims=True))
        total = jnp.sum(exponent, axis=0, keepdims=True)
        parts.append(dot(values[at], exponent.astype(bf16)) / total)
    mixed_ref[...] = jnp.concatenate(parts, axis=0).T.astype(bf16)


def attend_forward(lengths, tokens, query, key, value, query_bias, value_bias, key_mask):
    blocks = lengths.shape[0]
    width, mine = key.shape
    return pl.pallas_call(
        attend_forward_kernel,
        grid=(blocks,),
        in_specs=[
            pl.BlockSpec(memory_space=pltpu.SMEM),
            pl.BlockSpec((BUCKET, width), lambda b: (b, 0)),
            fixed((width, mine)),
            fixed((width, mine)),
            fixed((width, mine)),
            fixed((1, mine)),
            fixed((1, mine)),
            pl.BlockSpec((1, 1, BUCKET), lambda b: (b, 0, 0)),
        ],
        out_specs=pl.BlockSpec((BUCKET, mine), lambda b: (b, 0)),
        out_shape=jax.ShapeDtypeStruct((blocks * BUCKET, mine), bf16),
        scratch_shapes=[pltpu.VMEM((mine, width), bf16), pltpu.VMEM((mine, width), bf16)],
        compiler_params=params(1),
        name="attend_forward",
    )(lengths, tokens, query, key, value, query_bias, value_bias, key_mask)


def feed_forward_kernel(
    parts, place_ref, lengths_ref,
    mixed_ref, mixer_ref, tokens_ref, cotangent_ref, vectors_ref,
    keep_ref, bias_keep_ref, send_ref, bias_send_ref,
    output_ref, hidden_keep_ref, slope_keep_ref, hidden_send_ref, slope_send_ref,
    normed_low_ref, first_normed_ref, first_scale_ref, grad_second_ref, grad_outer_ref, sums_ref,
    normed_out, outer_sum,
):
    step = pl.program_id(0)
    output_bias, first_gain, first_shift, outer_bias, second_gain, second_shift = (
        vectors_ref[i : i + 1, :] for i in range(6)
    )

    @pl.when(step == 0)
    def _():
        attended = dot(mixed_ref[...], mixer_ref[...]) + output_bias
        normed, inv_scale = norm_rows(tokens_ref[...].astype(f32) + attended)
        whole = normed * first_gain + first_shift
        first_normed_ref[...] = normed
        first_scale_ref[...] = inv_scale
        normed_out[...] = whole
        normed_low_ref[...] = whole.astype(bf16)
        outer_sum[...] = jnp.zeros_like(outer_sum)

    def chunk(weights_ref, bias_ref, hidden_ref, slope_ref):
        inner_pre = contract_cols(normed_low_ref[...], weights_ref[0, 0]) + bias_ref[0]
        normal_cdf = 0.5 + 0.5 * lax.erf(inner_pre * 0.7071067811865476)
        density = jnp.exp(-0.5 * inner_pre * inner_pre) * 0.3989422804014327
        hidden = (inner_pre * normal_cdf).astype(bf16)
        hidden_ref[...] = hidden
        slope_ref[...] = (normal_cdf + inner_pre * density).astype(bf16)
        outer_sum[...] += dot(hidden, weights_ref[1, 0])

    @pl.when(step < parts)
    def _():
        chunk(keep_ref, bias_keep_ref, hidden_keep_ref, slope_keep_ref)

    @pl.when(step >= parts)
    def _():
        chunk(send_ref, bias_send_ref, hidden_send_ref, slope_send_ref)

    @pl.when(step == 2 * parts - 1)
    def _():
        second_sum = normed_out[...] + (outer_sum[...] + outer_bias)
        normed, inv_scale = norm_rows(second_sum)
        blocks = normed.shape[0] // BUCKET
        live = jnp.concatenate(
            [
                (item_places(lengths_ref, place_ref[0] * blocks + b, (BUCKET, 1), 0) < ITEMS)
                for b in range(blocks)
            ],
            axis=0,
        ).astype(f32)
        output_ref[...] = ((normed * second_gain + second_shift) * live).astype(bf16)
        grad_final = cotangent_ref[...].astype(f32) * live
        grad_second = norm_back(grad_final, second_gain, normed, inv_scale)
        grad_outer = grad_second.astype(bf16)
        grad_second_ref[...] = grad_second
        grad_outer_ref[...] = grad_outer
        sums_ref[0:1, :] = column_sum(grad_outer)
        sums_ref[1:2, :] = column_sum(grad_final * normed)
        sums_ref[2:3, :] = column_sum(grad_final)


def feed_forward(
    place, lengths, mixed, mixer, tokens, cotangent, vectors, keep, bias_keep, send, bias_send
):
    rows, width = mixed.shape
    parts, half = keep.shape[1:3]
    first = lambda j: jnp.minimum(j, parts - 1)
    second = lambda j: jnp.maximum(j - parts, 0)
    weights = []
    for at in (first, second):
        weights += [
            pl.BlockSpec((2, 1, half, width), lambda j, place, at=at: (0, at(j), 0, 0)),
            pl.BlockSpec((1, 1, half), lambda j, place, at=at: (at(j), 0, 0)),
        ]
    units = [
        pl.BlockSpec((rows, half), lambda j, place, at=at: (0, at(j)))
        for at in (first, first, second, second)
    ]
    own = pl.BlockSpec((rows, width), lambda j, place: (place[0], 0))
    return pl.pallas_call(
        functools.partial(feed_forward_kernel, parts),
        grid_spec=pltpu.PrefetchScalarGridSpec(
            num_scalar_prefetch=1,
            grid=(2 * parts,),
            in_specs=[
                pl.BlockSpec(memory_space=pltpu.SMEM),
                fixed((rows, width)),
                fixed((width, width)),
                own,
                own,
                fixed((8, width)),
            ]
            + weights,
            out_specs=[fixed((rows, width))]
            + units
            + [
                fixed((rows, width)),
                fixed((rows, width)),
                fixed((rows, 1)),
                fixed((rows, width)),
                fixed((rows, width)),
                fixed((8, width)),
            ],
            scratch_shapes=[pltpu.VMEM((rows, width), f32), pltpu.VMEM((rows, width), f32)],
        ),
        out_shape=[
            jax.ShapeDtypeStruct((rows, width), bf16),
            jax.ShapeDtypeStruct((rows, parts * half), bf16),
            jax.ShapeDtypeStruct((rows, parts * half), bf16),
            jax.ShapeDtypeStruct((rows, parts * half), bf16),
            jax.ShapeDtypeStruct((rows, parts * half), bf16),
            jax.ShapeDtypeStruct((rows, width), bf16),
            jax.ShapeDtypeStruct((rows, width), f32),
            jax.ShapeDtypeStruct((rows, 1), f32),
            jax.ShapeDtypeStruct((rows, width), f32),
            jax.ShapeDtypeStruct((rows, width), bf16),
            jax.ShapeDtypeStruct((8, width), f32),
        ],
        compiler_params=params(1),
        name="feed_forward",
    )(place, lengths, mixed, mixer, tokens, cotangent, vectors, keep, bias_keep, send, bias_send)


def feed_chunk(grad_outer_ref, normed_low_ref, hidden_ref, slope_ref, weights_ref,
               weights_grad_ref, bias_grad_ref):
    grad_outer = grad_outer_ref[...]
    grad_hidden = contract_cols(grad_outer, weights_ref[1, 0])
    grad_inner = (grad_hidden * slope_ref[...].astype(f32)).astype(bf16)
    weights_grad_ref[1, 0] = contract_rows(hidden_ref[...], grad_outer).astype(bf16)
    weights_grad_ref[0, 0] = contract_rows(grad_inner, normed_low_ref[...]).astype(bf16)
    bias_grad_ref[0] = column_sum(grad_inner)
    return dot(grad_inner, weights_ref[0, 0])


def feed_back_kernel(
    grad_outer_ref, normed_low_ref, hidden_ref, slope_ref, weights_ref, start_ref,
    weights_grad_ref, bias_grad_ref, grad_normed_ref,
):
    @pl.when(pl.program_id(0) == 0)
    def _():
        grad_normed_ref[...] = start_ref[...]

    grad_normed_ref[...] += feed_chunk(
        grad_outer_ref, normed_low_ref, hidden_ref, slope_ref, weights_ref,
        weights_grad_ref, bias_grad_ref,
    )


def feed_back_norm_kernel(
    grad_outer_ref, normed_low_ref, hidden_ref, slope_ref, weights_ref, start_ref,
    first_normed_ref, first_scale_ref, vectors_ref,
    weights_grad_ref, bias_grad_ref, grad_first_ref, grad_attended_ref, sums_ref,
    grad_normed,
):
    @pl.when(pl.program_id(0) == 0)
    def _():
        grad_normed[...] = start_ref[...]

    grad_normed[...] += feed_chunk(
        grad_outer_ref, normed_low_ref, hidden_ref, slope_ref, weights_ref,
        weights_grad_ref, bias_grad_ref,
    )

    @pl.when(pl.program_id(0) == pl.num_programs(0) - 1)
    def _():
        grad_rows, normed = grad_normed[...], first_normed_ref[...]
        grad_first = norm_back(grad_rows, vectors_ref[1:2, :], normed, first_scale_ref[...])
        grad_attended = grad_first.astype(bf16)
        grad_first_ref[...] = grad_first
        grad_attended_ref[...] = grad_attended
        sums_ref[0:1, :] = column_sum(grad_attended)
        sums_ref[1:2, :] = column_sum(grad_rows * normed)
        sums_ref[2:3, :] = column_sum(grad_rows)


def feed_back(grad_outer, normed_low, hidden, slope, weights, start, norm=None):
    rows, width = grad_outer.shape
    parts, half = weights.shape[1:3]
    columns = pl.BlockSpec((rows, half), lambda j: (0, j))
    by_part = pl.BlockSpec((2, 1, half, width), lambda j: (0, j, 0, 0))
    whole = fixed((rows, width))
    in_specs = [whole, whole, columns, columns, by_part, whole]
    out_specs = [by_part, pl.BlockSpec((1, 1, half), lambda j: (j, 0, 0)), whole]
    out_shape = [
        jax.ShapeDtypeStruct((2, parts, half, width), bf16),
        jax.ShapeDtypeStruct((parts, 1, half), f32),
        jax.ShapeDtypeStruct((rows, width), f32),
    ]
    args = [grad_outer, normed_low, hidden, slope, weights, start]
    scratch = []
    if norm is not None:
        in_specs += [whole, fixed((rows, 1)), fixed((8, width))]
        out_specs += [whole, fixed((8, width))]
        out_shape += [
            jax.ShapeDtypeStruct((rows, width), bf16),
            jax.ShapeDtypeStruct((8, width), f32),
        ]
        args += list(norm)
        scratch = [pltpu.VMEM((rows, width), f32)]
    return pl.pallas_call(
        feed_back_kernel if norm is None else feed_back_norm_kernel,
        grid=(parts,),
        in_specs=in_specs,
        out_specs=out_specs,
        out_shape=out_shape,
        scratch_shapes=scratch,
        compiler_params=params(1),
        name="feed_back" if norm is None else "feed_back_norm",
    )(*args)


def attend_back_kernel(
    place_ref, lengths_ref, tokens_ref, grad_attended_ref, grad_first_ref, weights_ref, mixer_ref,
    query_bias_ref, value_bias_ref, key_mask_ref,
    grads_ref, tokens_grad_ref, sums_ref,
    bias, total_grad,
):
    pair = pl.program_id(1)

    @pl.when(pair == 0)
    def _():
        row = place_ref[0] * pl.num_programs(0) + pl.program_id(0)
        bias[...] = mask_bias(lengths_ref, row, key_mask_ref[0])
        total_grad[...] = grad_first_ref[...]

    rows, grad_attended = tokens_ref[...], grad_attended_ref[...]
    width = rows.shape[1]
    query_w, key_w, value_w = (
        weights_ref[:, i * width : (i + 1) * width] for i in range(3)
    )
    queries = contract_cols(query_w, rows) + as_column(query_bias_ref[...])
    queries = (queries.astype(bf16) * HEAD ** (-0.5)).astype(bf16)
    keys = contract_cols(rows, key_w).astype(bf16)
    values = (contract_cols(rows, value_w) + value_bias_ref[...]).astype(bf16)
    grad_mixed = contract_cols(mixer_ref[...], grad_attended).astype(bf16)
    keys_t = keys.T
    grad_queries, grad_keys, grad_values = [], [], []
    for head in range(keys.shape[1] // HEAD):
        at = slice(head * HEAD, (head + 1) * HEAD)
        scores = dot(keys[:, at], queries[at]) + bias[...]
        exponent = jnp.exp(scores - jnp.max(scores, axis=0, keepdims=True))
        probs = exponent * (1.0 / jnp.sum(exponent, axis=0, keepdims=True))
        grad_probs = dot(values[:, at], grad_mixed[at])
        shift = jnp.sum(probs * grad_probs, axis=0, keepdims=True)
        grad_scores = (probs * (grad_probs - shift)).astype(bf16)
        grad_values.append(contract_cols(probs.astype(bf16), grad_mixed[at]))
        grad_keys.append(contract_cols(grad_scores, queries[at]))
        grad_queries.append(dot(keys_t[at], grad_scores) * HEAD ** (-0.5))
    grad_query = jnp.concatenate(grad_queries, axis=0).T.astype(bf16)
    grad_key = jnp.concatenate(grad_keys, axis=1).astype(bf16)
    grad_value = jnp.concatenate(grad_values, axis=1).astype(bf16)
    grads_ref[0] = grad_query
    grads_ref[1] = grad_key
    grads_ref[2] = grad_value
    sums_ref[0, 0:1, :] = column_sum(grad_query)
    sums_ref[0, 1:2, :] = column_sum(grad_value)
    total_grad[...] += dot(grad_query, query_w) + dot(grad_key, key_w) + dot(grad_value, value_w)

    @pl.when(pair == pl.num_programs(1) - 1)
    def _():
        tokens_grad_ref[...] = total_grad[...].astype(bf16)


def attend_back(
    place, lengths, tokens, grad_attended, grad_first, weights, mixer, query_bias, value_bias,
    key_mask,
):
    rows, width = grad_attended.shape
    blocks = rows // BUCKET
    pair = 2 * HEAD
    own = lambda b, h, place: (place[0] * blocks + b, 0)
    by_bucket = pl.BlockSpec((BUCKET, width), lambda b, h, place: (b, 0))
    by_pair = lambda b, h, place: (h, 0)
    row_pair = pl.BlockSpec((1, pair), lambda b, h, place: (0, h))
    return pl.pallas_call(
        attend_back_kernel,
        grid_spec=pltpu.PrefetchScalarGridSpec(
            num_scalar_prefetch=1,
            grid=(blocks, width // pair),
            in_specs=[
                pl.BlockSpec(memory_space=pltpu.SMEM),
                pl.BlockSpec((BUCKET, width), own),
                by_bucket,
                by_bucket,
                pl.BlockSpec((pair, 3 * width), by_pair),
                pl.BlockSpec((pair, width), by_pair),
                row_pair,
                row_pair,
                pl.BlockSpec((1, 1, BUCKET), lambda b, h, place: (place[0] * blocks + b, 0, 0)),
            ],
            out_specs=[
                pl.BlockSpec((3, BUCKET, pair), lambda b, h, place: (0, b, h)),
                by_bucket,
                pl.BlockSpec((1, 8, pair), lambda b, h, place: (b, 0, h)),
            ],
            scratch_shapes=[pltpu.VMEM((BUCKET, BUCKET), f32), pltpu.VMEM((BUCKET, width), f32)],
        ),
        out_shape=[
            jax.ShapeDtypeStruct((3, rows, width), bf16),
            jax.ShapeDtypeStruct((rows, width), bf16),
            jax.ShapeDtypeStruct((blocks, 8, width), f32),
        ],
        compiler_params=params(2),
        name="attend_back",
    )(
        place, lengths, tokens, grad_attended, grad_first, weights, mixer, query_bias, value_bias,
        key_mask,
    )


def attention_grads_kernel(
    order_ref, grads_ref, mixed_ref, tokens_ref, grad_attended_ref, weight_grad_ref
):
    which = order_ref[pl.program_id(0)]

    @pl.when(which < 3)
    def _():
        weight_grad_ref[0] = contract_rows(grads_ref[0], tokens_ref[...]).astype(bf16)

    @pl.when(which == 3)
    def _():
        weight_grad_ref[0] = contract_rows(mixed_ref[...], grad_attended_ref[...]).astype(bf16)


def attention_grads(order, grads, mixed, tokens, grad_attended):
    rows, width = grad_attended.shape
    cut = 2
    columns = pl.BlockSpec((rows, width // cut), lambda i, j, order: (0, j))
    return pl.pallas_call(
        attention_grads_kernel,
        grid_spec=pltpu.PrefetchScalarGridSpec(
            num_scalar_prefetch=1,
            grid=(2, cut),
            in_specs=[
                pl.BlockSpec(
                    (1, rows, width // cut),
                    lambda i, j, order: (jnp.minimum(order[i], 2), 0, j),
                ),
                columns,
                pl.BlockSpec((rows, width), lambda i, j, order: (order[2], 0)),
                pl.BlockSpec((rows, width), lambda i, j, order: (0, 0)),
            ],
            out_specs=pl.BlockSpec((1, width // cut, width), lambda i, j, order: (i, j, 0)),
        ),
        out_shape=jax.ShapeDtypeStruct((2, width, width), bf16),
        compiler_params=params(2),
        name="attention_grads",
    )(order, grads, mixed, tokens, grad_attended)


def together(*values):
    return lax.optimization_barrier(values)


def add(first, *others):
    total = first.astype(f32)
    for other in others:
        total = total + other.astype(f32)
    return total.astype(bf16)


class Plane:
    def __init__(self, n_dp, n_z):
        self.n_dp, self.n_z = n_dp, n_z
        self.bits = [1 << i for i in range(1, n_dp.bit_length() - 1)][::-1]
        self.dp = lax.axis_index("dp")
        self.z = lax.axis_index("tensor")
        self.core = self.dp & 1
        numbers = list(range(len(self.bits)))
        self.orders = (numbers, numbers[::-1])
        self.groups = [numbers[i : i + 2] for i in range(0, len(numbers), 2)]

    def swap(self, array, bit):
        return lax.ppermute(array, "dp", [(i, i ^ bit) for i in range(self.n_dp)])

    def shift(self, array, by):
        n = self.n_z
        return lax.ppermute(array, "tensor", [(i, (i + by) % n) for i in range(n)])

    def has(self, bit):
        return (self.dp & bit) != 0

    def join(self, own, other, bit, axis):
        return jnp.where(
            self.has(bit),
            jnp.concatenate([other, own], axis=axis),
            jnp.concatenate([own, other], axis=axis),
        )

    def by_bits(self, track):
        lead, _, width = track.shape
        return track.reshape((lead,) + (2,) * len(self.bits) + (-1, width))

    def one(self, track, flips):
        for index, flip in flips.items():
            mine = jnp.where(self.has(self.bits[index]), 1, 0)
            track = lax.dynamic_slice_in_dim(track, 1 - mine if flip else mine, 1, index + 1)
        return track

    def grow(self, track, order):
        lead, _, width = track.shape
        track = track.reshape((lead,) + (1,) * len(self.bits) + track.shape[1:])
        for index in order:
            other = self.swap(track, self.bits[index])
            track = self.join(track, other, self.bits[index], index + 1)
        return track.reshape(lead, -1, width)

    def flips(self, group):
        for number in range(1, 1 << len(group)):
            chosen = {index: bool(number >> i & 1) for i, index in enumerate(group)}
            yield chosen, sum(self.bits[index] for index in group if chosen[index])

    def grow_direct(self, track):
        lead, _, width = track.shape
        track = track.reshape((lead,) + (1,) * len(self.bits) + track.shape[1:])
        for group in self.groups:
            found = [track] + [self.swap(track, mask) for _, mask in self.flips(group)]
            for index in group:
                found = [
                    self.join(own, other, self.bits[index], index + 1)
                    for own, other in zip(found[::2], found[1::2])
                ]
            track = found[0]
        return track.reshape(lead, -1, width)

    def fold(self, track, index):
        away, home = self.one(track, {index: True}), self.one(track, {index: False})
        return home, self.swap(away, self.bits[index])

    def fold_direct(self, track, group):
        home = self.one(track, {index: False for index in group})
        return home, [self.swap(self.one(track, chosen), mask) for chosen, mask in self.flips(group)]

    def sum_line(self, parts):
        return [self.shift(parts[s], -s) for s in range(1, self.n_z)]

    def spread_line(self, rows):
        n = self.n_z
        right = left = rows
        steps = []
        for _ in range(n - 1):
            right = lax.ppermute(right, "tensor", [(i, i + 1) for i in range(n - 1)])
            left = lax.ppermute(left, "tensor", [(i + 1, i) for i in range(n - 1)])
            steps.append((right, left))
        return steps


def on_device(
    n_dp,
    n_z,
    tokens,
    lengths,
    key_mask,
    query_weight,
    query_bias,
    key_weight,
    value_weight,
    value_bias,
    output_weight,
    output_bias,
    first_gain,
    first_shift,
    inner_weight,
    inner_bias,
    outer_weight,
    outer_bias,
    second_gain,
    second_shift,
    cotangent,
):
    width = tokens.shape[1]
    mine = query_weight.shape[1]
    units = inner_weight.shape[1]
    all_rows = tokens.shape[0]
    all_blocks = all_rows // BUCKET
    rows = all_rows // n_z
    plane = Plane(n_dp, n_z)
    dp, z, core = plane.dp, plane.z, plane.core
    others = range(1, n_z)
    place = z.reshape(1)

    feed_piece_rows = units // n_dp
    feed_start = core * (units // 2) + (dp >> 1) * feed_piece_rows
    feed_piece = jnp.concatenate(
        [
            lax.dynamic_slice_in_dim(inner_weight, feed_start, feed_piece_rows, 1).T,
            lax.dynamic_slice_in_dim(outer_weight, feed_start, feed_piece_rows, 0),
        ],
        axis=1,
    )
    feed_line = [plane.shift(feed_piece, s) for s in others]

    head_rows = mine // n_dp
    bias_row = jnp.concatenate([query_bias, value_bias, inner_bias])
    bias_rows = -(-bias_row.shape[0] // width)
    bias_row = jnp.pad(bias_row, (0, bias_rows * width - bias_row.shape[0]))
    mixer_piece = jnp.concatenate(
        [
            lax.dynamic_slice_in_dim(output_weight, dp * head_rows, head_rows, 0),
            bias_row.reshape(bias_rows, width),
        ],
        axis=0,
    )
    mixer_line = [plane.shift(mixer_piece, s) for s in others]

    key_mask_rows = key_mask.reshape(all_blocks, 1, BUCKET)
    mixed_all = attend_forward(
        lengths, tokens, query_weight, key_weight, value_weight,
        query_bias.reshape(1, mine), value_bias.reshape(1, mine), key_mask_rows,
    )
    mixed_all, feed_line, mixer_line = together(mixed_all, feed_line, mixer_line)

    def block(matrix, number):
        return lax.dynamic_slice_in_dim(matrix, number * rows, rows, 0)

    mixed_line = [
        plane.shift(block(mixed_all, lax.rem(z + s, n_z)), s) for s in others
    ]
    mixed_rows = jnp.concatenate([block(mixed_all, z)] + mixed_line, axis=1)

    feed_remote = jnp.stack(feed_line)
    own_half = [
        lax.dynamic_slice_in_dim(inner_weight, core * (units // 2), units // 2, 1).T,
        lax.dynamic_slice_in_dim(outer_weight, core * (units // 2), units // 2, 0),
    ]
    feed_keep = jnp.stack(
        [
            jnp.concatenate(
                [own[None], plane.grow(feed_remote[:, :, i * width : (i + 1) * width], order)],
                axis=0,
            )
            for i, (own, order) in enumerate(zip(own_half, plane.orders))
        ]
    )
    feed_send = plane.swap(feed_keep, 1)

    mixer_remote = jnp.stack([piece[:head_rows] for piece in mixer_line])
    mixer_remote = lax.all_gather(mixer_remote, "dp", axis=1, tiled=True)
    mixer = jnp.concatenate([output_weight[None], mixer_remote], axis=0).reshape(-1, width)
    biases = jnp.stack(
        [bias_row] + [piece[head_rows:].reshape(-1) for piece in mixer_line]
    ).astype(f32)
    query_bias_all = biases[:, :mine].reshape(1, -1)
    value_bias_all = biases[:, mine : 2 * mine].reshape(1, -1)
    inner_bias_all = biases[:, 2 * mine : 2 * mine + units].reshape(n_z, 2, units // 2)
    bias_keep = lax.dynamic_slice_in_dim(inner_bias_all, core, 1, 1)
    bias_send = lax.dynamic_slice_in_dim(inner_bias_all, 1 - core, 1, 1)

    attention_own = jnp.concatenate([query_weight.T, key_weight.T, value_weight.T], axis=1)
    attention_piece = lax.dynamic_slice_in_dim(attention_own, dp * head_rows, head_rows, 0)
    attention_line = jnp.stack([plane.shift(attention_piece, s) for s in others])
    attention_remote = lax.all_gather(attention_line, "dp", axis=1, tiled=True)
    attention_weights = jnp.concatenate([attention_own[None], attention_remote], axis=0)
    attention_weights = attention_weights.reshape(-1, 3 * width)

    vectors = jnp.stack(
        [output_bias, first_gain, first_shift, outer_bias, second_gain, second_shift]
        + [jnp.zeros_like(output_bias)] * 2
    ).astype(f32)

    (
        my_output, hidden_keep, slope_keep, hidden_send, slope_send,
        normed_low, first_normed, first_scale, grad_second, grad_outer, second_sums,
    ) = feed_forward(
        place, lengths, mixed_rows, mixer, tokens, cotangent, vectors,
        feed_keep, bias_keep, feed_send, bias_send,
    )
    output = lax.all_gather(my_output, "tensor", axis=0, tiled=True)

    feed_grad_send, bias_grad_send, grad_normed = feed_back(
        grad_outer, normed_low, hidden_send, slope_send, feed_send, grad_second
    )
    feed_grad_other = plane.swap(feed_grad_send, 1)
    feed_grad_keep, bias_grad_keep, grad_first, grad_attended, first_sums = feed_back(
        grad_outer, normed_low, hidden_keep, slope_keep, feed_keep, grad_normed,
        (first_normed, first_scale, vectors),
    )
    grad_first, grad_attended, feed_grad_other = together(
        grad_first, grad_attended, feed_grad_other
    )
    inner_bias_grad = plane.join(bias_grad_keep, bias_grad_send, 1, 1).reshape(n_z, units)
    feed_sum = add(feed_grad_keep, feed_grad_other)
    tracks = [plane.by_bits(feed_sum[i]) for i in range(2)]

    def step(number):
        return [
            plane.fold(track, order[number]) for track, order in zip(tracks, plane.orders)
        ]

    folded = step(0)
    attention_back, my_tokens_grad, back_sums = attend_back(
        place, lengths, tokens, grad_attended, grad_first, attention_weights, mixer,
        query_bias_all, value_bias_all, key_mask_rows,
    )
    line_steps = plane.spread_line(my_tokens_grad)
    attention_back, folded = together(attention_back, folded)
    tracks = [add(*pair) for pair in folded]
    for number in range(1, len(plane.bits)):
        folded = step(number)
        if number < len(plane.bits) - 1:
            tracks = [add(*pair) for pair in folded]

    pair = jnp.arange(2, dtype=jnp.int32)

    def weight_grads(side):
        order = jnp.concatenate([pair + 2 * side, place])
        return attention_grads(order, attention_back, mixed_rows, tokens, grad_attended)

    grads_send = weight_grads(1 - core)
    grads_send, folded = together(grads_send, folded)
    grads_other = plane.swap(grads_send, 1)
    tracks = [add(*pair) for pair in folded]
    feed_parts = jnp.concatenate([t.reshape(n_z, -1, width) for t in tracks], axis=2)
    feed_line = plane.sum_line(feed_parts)
    grads_keep = weight_grads(core)
    grads_keep, grads_other, line_steps[0], output = together(
        grads_keep, grads_other, line_steps[0], output
    )
    grads_sum = add(grads_keep, grads_other).reshape(2 * n_z, mine, width)
    grads_sum = plane.by_bits(grads_sum)
    for group in plane.groups:
        home, arrived = plane.fold_direct(grads_sum, group)
        grads_sum = add(home, *arrived)
    attention_parts = grads_sum.reshape(2, n_z, -1, width)
    attention_parts, feed_line, line_steps[1:2] = together(
        attention_parts, feed_line, line_steps[1:2]
    )
    attention_line = plane.sum_line([attention_parts[:, s] for s in range(n_z)])
    feed_total = add(feed_parts[0], *feed_line)
    feed_half = plane.grow_direct(feed_total[None])
    feed_grad = plane.join(feed_half, plane.swap(feed_half, 1), 1, 1)[0]
    attention_half = plane.grow_direct(add(attention_parts[:, 0], *attention_line))
    grad_list = plane.join(attention_half, plane.swap(attention_half, 1), 1, 0)

    tokens_grad = jnp.zeros((all_rows, width), bf16)
    tokens_grad = lax.dynamic_update_slice_in_dim(tokens_grad, my_tokens_grad, z * rows, 0)
    for s in others:
        came = jnp.where(z >= s, line_steps[s - 1][0], line_steps[n_z - 1 - s][1])
        there = lax.rem(z + n_z - s, n_z) * rows
        tokens_grad = lax.dynamic_update_slice_in_dim(tokens_grad, came, there, 0)

    back_sums = jnp.sum(back_sums, axis=0)
    query_bias_grad = back_sums[0].reshape(n_z, mine)
    value_bias_grad = back_sums[1].reshape(n_z, mine)

    shared = jnp.concatenate([first_sums[:3], second_sums[:3]], axis=0).reshape(-1)
    split = jnp.concatenate([inner_bias_grad, query_bias_grad, value_bias_grad], axis=1)
    small = jnp.concatenate([shared, split.reshape(-1)])
    for bit in [1] + plane.bits:
        small = small + plane.swap(small, bit)
    n_shared, n_split = 6 * width, split.shape[1]
    shared = small[:n_shared]
    split = small[n_shared : n_shared + n_split]
    for s in others:
        there = plane.shift(small, -s)
        shared = shared + there[:n_shared]
        split = split + there[n_shared + s * n_split : n_shared + (s + 1) * n_split]
    shared = shared.reshape(6, width)

    return (
        output,
        tokens_grad,
        grad_list[0].T.astype(f32),
        split[units : units + mine],
        grad_list[1].T.astype(f32),
        grad_list[2].T.astype(f32),
        split[units + mine :],
        grad_list[3].astype(f32),
        shared[0],
        shared[1],
        shared[2],
        feed_grad[:, :width].T.astype(f32),
        split[:units],
        feed_grad[:, width:].astype(f32),
        shared[3],
        shared[4],
        shared[5],
    )


def solution(mesh):
    n_dp, n_z = mesh.shape["dp"], mesh.shape["tensor"]
    in_specs = (
        P("dp", None),
        P("dp", None),
        P("dp"),
        P(None, "tensor"),
        P("tensor"),
        P(None, "tensor"),
        P(None, "tensor"),
        P("tensor"),
        P("tensor", None),
        P(),
        P(),
        P(),
        P(None, "tensor"),
        P("tensor"),
        P("tensor", None),
        P(),
        P(),
        P(),
        P("dp", None),
    )
    out_specs = (
        P("dp", None),
        P("dp", None),
        P(None, "tensor"),
        P("tensor"),
        P(None, "tensor"),
        P(None, "tensor"),
        P("tensor"),
        P("tensor", None),
        P(),
        P(),
        P(),
        P(None, "tensor"),
        P("tensor"),
        P("tensor", None),
        P(),
        P(),
        P(),
    )

    def program(*args):
        return on_device(n_dp, n_z, *args)

    return jax.shard_map(
        program, mesh=mesh, in_specs=in_specs, out_specs=out_specs, check_vma=False
    )
```

```python
import functools

import jax
import jax.numpy as jnp
from jax import lax
from jax.experimental import pallas as pl
from jax.experimental.pallas import tpu as pltpu
from jax.sharding import PartitionSpec as P

HEAD = 64
BUCKET = 512
ITEMS = 8


negative_fill = -1e30
epsilon = 1e-06
f32 = jnp.float32
bf16 = jnp.bfloat16
VMEM_BYTES = 56 * 1024 * 1024


def dot(left, right):
    return jnp.dot(left, right, preferred_element_type=f32)


def contract_rows(left, right):
    return lax.dot_general(left, right, (((0,), (0,)), ((), ())), preferred_element_type=f32)


def contract_cols(left, right):
    return lax.dot_general(left, right, (((1,), (1,)), ((), ())), preferred_element_type=f32)


def norm_rows(values):
    centred = values - jnp.mean(values, axis=1, keepdims=True)
    inv_scale = lax.rsqrt(jnp.mean(centred * centred, axis=1, keepdims=True) + epsilon)
    return centred * inv_scale, inv_scale


def norm_back(grad_rows, norm_gain, normed, inv_scale):
    scaled = grad_rows * norm_gain
    return inv_scale * (
        scaled
        - jnp.mean(scaled, axis=1, keepdims=True)
        - normed * jnp.mean(scaled * normed, axis=1, keepdims=True)
    )


def column_sum(matrix):
    return jnp.sum(matrix.astype(f32), axis=0, keepdims=True)


def fixed(shape):
    return pl.BlockSpec(shape, lambda *_: (0,) * len(shape))


def cost(microseconds):
    return pl.CostEstimate(
        flops=int(microseconds * 1.0e9), bytes_accessed=int(microseconds * 1.0e6), transcendentals=0
    )


def params(axes):
    return pltpu.CompilerParams(
        dimension_semantics=("arbitrary",) * axes, vmem_limit_bytes=VMEM_BYTES
    )


def item_places(lengths_ref, row, shape, axis):
    places = lax.broadcasted_iota(jnp.int32, shape, axis)
    end = jnp.int32(0)
    items = jnp.zeros(shape, jnp.int32)
    for slot in range(ITEMS):
        end = end + lengths_ref[row, slot]
        items = items + (places >= end).astype(jnp.int32)
    return items


def as_column(row):
    return jnp.broadcast_to(row.astype(f32), (8, row.shape[1])).T[:, :1]


def mask_bias(lengths_ref, row, key_mask):
    shape = (BUCKET, BUCKET)
    diagonal = lax.broadcasted_iota(jnp.int32, shape, 0) == lax.broadcasted_iota(
        jnp.int32, shape, 1
    )
    item_row = item_places(lengths_ref, row, (1, BUCKET), 1)
    item_column = item_places(lengths_ref, row, (BUCKET, 1), 0)
    code_column = jnp.where(as_column(key_mask) == 1.0, item_column, -1)
    return jnp.where((code_column == item_row) | diagonal, 0.0, negative_fill).astype(f32)


def attend_forward_kernel(
    lengths_ref, tokens_ref, query_ref, key_ref, value_ref, biases_ref, key_mask_ref, mixed_ref,
):
    rows = tokens_ref[...]
    queries = contract_cols(query_ref[...], rows) + as_column(biases_ref[0:1, :])
    queries = (queries.astype(bf16) * HEAD ** (-0.5)).astype(bf16)
    keys = contract_cols(rows, key_ref[...]).astype(bf16)
    values = (contract_cols(value_ref[...], rows) + as_column(biases_ref[1:2, :])).astype(bf16)
    bias = mask_bias(lengths_ref, pl.program_id(0), key_mask_ref[0])
    parts = []
    for head in range(queries.shape[0] // HEAD):
        at = slice(head * HEAD, (head + 1) * HEAD)
        scores = dot(keys[:, at], queries[at]) + bias
        exponent = jnp.exp(scores - jnp.max(scores, axis=0, keepdims=True))
        total = jnp.sum(exponent, axis=0, keepdims=True)
        parts.append(dot(values[at], exponent.astype(bf16)) / total)
    mixed_ref[...] = jnp.concatenate(parts, axis=0).T.astype(bf16)


def attend_forward(lengths, tokens, query, key, value, biases, key_mask):
    blocks = lengths.shape[0]
    mine, width = key.shape
    return pl.pallas_call(
        attend_forward_kernel,
        grid=(blocks,),
        in_specs=[
            pl.BlockSpec(memory_space=pltpu.SMEM),
            pl.BlockSpec((BUCKET, width), lambda b: (b, 0)),
            fixed((mine, width)),
            fixed((mine, width)),
            fixed((mine, width)),
            fixed((2, mine)),
            pl.BlockSpec((1, 1, BUCKET), lambda b: (b, 0, 0)),
        ],
        out_specs=pl.BlockSpec((BUCKET, mine), lambda b: (b, 0)),
        out_shape=jax.ShapeDtypeStruct((blocks * BUCKET, mine), bf16),
        compiler_params=params(1),
        name="attend_forward",
        cost_estimate=cost(12),
    )(lengths, tokens, query, key, value, biases, key_mask)


def feed_units(normed_low_ref, weights_ref, bias_ref, hidden_ref, slope_ref):
    inner_pre = contract_cols(normed_low_ref[...], weights_ref[0, 0]) + bias_ref[0]
    normal_cdf = 0.5 + 0.5 * lax.erf(inner_pre * 0.7071067811865476)
    density = jnp.exp(-0.5 * inner_pre * inner_pre) * 0.3989422804014327
    hidden = (inner_pre * normal_cdf).astype(bf16)
    hidden_ref[...] = hidden
    slope_ref[...] = (normal_cdf + inner_pre * density).astype(bf16)
    return dot(hidden, weights_ref[1, 0])


def feed_first_kernel(
    place_ref, mixed_ref, mixer_ref, tokens_ref, vectors_ref, weights_ref, bias_ref,
    hidden_ref, slope_ref, normed_low_ref, first_normed_ref, first_scale_ref, sum_ref,
):
    @pl.when(pl.program_id(0) == 0)
    def _():
        output_bias, first_gain, first_shift, outer_bias = (
            vectors_ref[i : i + 1, :] for i in range(4)
        )
        attended = dot(mixed_ref[...], mixer_ref[...]) + output_bias
        normed, inv_scale = norm_rows(tokens_ref[...].astype(f32) + attended)
        whole = normed * first_gain + first_shift
        first_normed_ref[...] = normed
        first_scale_ref[...] = inv_scale
        normed_low_ref[...] = whole.astype(bf16)
        sum_ref[...] = whole + outer_bias

    sum_ref[...] += feed_units(normed_low_ref, weights_ref, bias_ref, hidden_ref, slope_ref)


def feed_second_kernel(
    place_ref, lengths_ref, normed_low_ref, start_ref, cotangent_ref, vectors_ref, weights_ref,
    bias_ref, hidden_ref, slope_ref, output_ref, grad_second_ref, grad_outer_ref, sums_ref,
    second_sum,
):
    @pl.when(pl.program_id(0) == 0)
    def _():
        second_sum[...] = start_ref[...]

    second_sum[...] += feed_units(normed_low_ref, weights_ref, bias_ref, hidden_ref, slope_ref)

    @pl.when(pl.program_id(0) == pl.num_programs(0) - 1)
    def _():
        second_gain, second_shift = vectors_ref[4:5, :], vectors_ref[5:6, :]
        normed, inv_scale = norm_rows(second_sum[...])
        blocks = normed.shape[0] // BUCKET
        live = jnp.concatenate(
            [
                (item_places(lengths_ref, place_ref[0] * blocks + b, (BUCKET, 1), 0) < ITEMS)
                for b in range(blocks)
            ],
            axis=0,
        ).astype(f32)
        output_ref[...] = ((normed * second_gain + second_shift) * live).astype(bf16)
        grad_final = cotangent_ref[...].astype(f32) * live
        grad_second = norm_back(grad_final, second_gain, normed, inv_scale)
        grad_outer = grad_second.astype(bf16)
        grad_second_ref[...] = grad_second
        grad_outer_ref[...] = grad_outer
        sums_ref[0:1, :] = column_sum(grad_outer)
        sums_ref[1:2, :] = column_sum(grad_final * normed)
        sums_ref[2:3, :] = column_sum(grad_final)


def feed_specs(weights, rows):
    parts, half, width = weights.shape[1:]
    whole = fixed((rows, width))
    own = pl.BlockSpec((rows, width), lambda j, place: (place[0], 0))
    by_part = [
        pl.BlockSpec((2, 1, half, width), lambda j, place: (0, j, 0, 0)),
        pl.BlockSpec((1, 1, half), lambda j, place: (j, 0, 0)),
    ]
    columns = [pl.BlockSpec((rows, half), lambda j, place: (0, j))] * 2
    unit_shapes = [jax.ShapeDtypeStruct((rows, parts * half), bf16)] * 2
    return parts, width, whole, own, by_part, columns, unit_shapes


def feed_first(place, mixed, mixer, tokens, vectors, weights, bias):
    rows = mixed.shape[0]
    parts, width, whole, own, by_part, columns, unit_shapes = feed_specs(weights, rows)
    return pl.pallas_call(
        feed_first_kernel,
        grid_spec=pltpu.PrefetchScalarGridSpec(
            num_scalar_prefetch=1,
            grid=(parts,),
            in_specs=[whole, fixed((width, width)), own, fixed((8, width))] + by_part,
            out_specs=columns + [whole, whole, fixed((rows, 1)), whole],
        ),
        out_shape=unit_shapes
        + [
            jax.ShapeDtypeStruct((rows, width), bf16),
            jax.ShapeDtypeStruct((rows, width), f32),
            jax.ShapeDtypeStruct((rows, 1), f32),
            jax.ShapeDtypeStruct((rows, width), f32),
        ],
        compiler_params=params(1),
        name="feed_first",
        cost_estimate=cost(11),
    )(place, mixed, mixer, tokens, vectors, weights, bias)


def feed_second(place, lengths, normed_low, start, cotangent, vectors, weights, bias):
    rows = normed_low.shape[0]
    parts, width, whole, own, by_part, columns, unit_shapes = feed_specs(weights, rows)
    return pl.pallas_call(
        feed_second_kernel,
        grid_spec=pltpu.PrefetchScalarGridSpec(
            num_scalar_prefetch=1,
            grid=(parts,),
            in_specs=[pl.BlockSpec(memory_space=pltpu.SMEM), whole, whole, own, fixed((8, width))]
            + by_part,
            out_specs=columns + [whole, whole, whole, fixed((8, width))],
            scratch_shapes=[pltpu.VMEM((rows, width), f32)],
        ),
        out_shape=unit_shapes
        + [
            jax.ShapeDtypeStruct((rows, width), bf16),
            jax.ShapeDtypeStruct((rows, width), f32),
            jax.ShapeDtypeStruct((rows, width), bf16),
            jax.ShapeDtypeStruct((8, width), f32),
        ],
        compiler_params=params(1),
        name="feed_second",
        cost_estimate=cost(11),
    )(place, lengths, normed_low, start, cotangent, vectors, weights, bias)


def feed_chunk(grad_outer_ref, normed_low_ref, hidden_ref, slope_ref, weights_ref,
               weights_grad_ref, bias_grad_ref):
    grad_outer = grad_outer_ref[...]
    grad_hidden = contract_cols(grad_outer, weights_ref[1, 0])
    grad_inner = (grad_hidden * slope_ref[...].astype(f32)).astype(bf16)
    weights_grad_ref[1, 0] = contract_rows(hidden_ref[...], grad_outer).astype(bf16)
    weights_grad_ref[0, 0] = contract_rows(grad_inner, normed_low_ref[...]).astype(bf16)
    bias_grad_ref[0] = column_sum(grad_inner)
    return dot(grad_inner, weights_ref[0, 0])


def feed_back_kernel(
    grad_outer_ref, normed_low_ref, hidden_ref, slope_ref, weights_ref, start_ref,
    weights_grad_ref, bias_grad_ref, grad_normed_ref,
):
    @pl.when(pl.program_id(0) == 0)
    def _():
        grad_normed_ref[...] = start_ref[...]

    grad_normed_ref[...] += feed_chunk(
        grad_outer_ref, normed_low_ref, hidden_ref, slope_ref, weights_ref,
        weights_grad_ref, bias_grad_ref,
    )


def feed_back_norm_kernel(
    grad_outer_ref, normed_low_ref, hidden_ref, slope_ref, weights_ref, start_ref,
    first_normed_ref, first_scale_ref, vectors_ref,
    weights_grad_ref, bias_grad_ref, grad_first_ref, grad_attended_ref, sums_ref,
    grad_normed,
):
    @pl.when(pl.program_id(0) == 0)
    def _():
        grad_normed[...] = start_ref[...]

    grad_normed[...] += feed_chunk(
        grad_outer_ref, normed_low_ref, hidden_ref, slope_ref, weights_ref,
        weights_grad_ref, bias_grad_ref,
    )

    @pl.when(pl.program_id(0) == pl.num_programs(0) - 1)
    def _():
        grad_rows, normed = grad_normed[...], first_normed_ref[...]
        grad_first = norm_back(grad_rows, vectors_ref[1:2, :], normed, first_scale_ref[...])
        grad_attended = grad_first.astype(bf16)
        grad_first_ref[...] = grad_first
        grad_attended_ref[...] = grad_attended
        sums_ref[0:1, :] = column_sum(grad_attended)
        sums_ref[1:2, :] = column_sum(grad_rows * normed)
        sums_ref[2:3, :] = column_sum(grad_rows)


def feed_back(grad_outer, normed_low, hidden, slope, weights, start, norm=None):
    rows, width = grad_outer.shape
    parts, half = weights.shape[1:3]
    columns = pl.BlockSpec((rows, half), lambda j: (0, j))
    by_part = pl.BlockSpec((2, 1, half, width), lambda j: (0, j, 0, 0))
    whole = fixed((rows, width))
    in_specs = [whole, whole, columns, columns, by_part, whole]
    out_specs = [by_part, pl.BlockSpec((1, 1, half), lambda j: (j, 0, 0)), whole]
    out_shape = [
        jax.ShapeDtypeStruct((2, parts, half, width), bf16),
        jax.ShapeDtypeStruct((parts, 1, half), f32),
        jax.ShapeDtypeStruct((rows, width), f32),
    ]
    args = [grad_outer, normed_low, hidden, slope, weights, start]
    scratch = []
    if norm is not None:
        in_specs += [whole, fixed((rows, 1)), fixed((8, width))]
        out_specs += [whole, fixed((8, width))]
        out_shape += [
            jax.ShapeDtypeStruct((rows, width), bf16),
            jax.ShapeDtypeStruct((8, width), f32),
        ]
        args += list(norm)
        scratch = [pltpu.VMEM((rows, width), f32)]
    return pl.pallas_call(
        feed_back_kernel if norm is None else feed_back_norm_kernel,
        grid=(parts,),
        in_specs=in_specs,
        out_specs=out_specs,
        out_shape=out_shape,
        scratch_shapes=scratch,
        compiler_params=params(1),
        name="feed_back" if norm is None else "feed_back_norm",
        cost_estimate=cost(11 if norm is None else 13),
    )(*args)


def attend_back_kernel(
    place_ref, lengths_ref, tokens_ref, grad_attended_ref, grad_first_ref, weights_ref, mixer_ref,
    query_bias_ref, value_bias_ref, key_mask_ref,
    grads_ref, tokens_grad_ref, sums_ref,
    bias, total_grad,
):
    pair = pl.program_id(1)

    @pl.when(pair == 0)
    def _():
        row = place_ref[0] * pl.num_programs(0) + pl.program_id(0)
        bias[...] = mask_bias(lengths_ref, row, key_mask_ref[0])
        total_grad[...] = grad_first_ref[...]

    rows, grad_attended = tokens_ref[...], grad_attended_ref[...]
    width = rows.shape[1]
    query_w, key_w, value_w = (
        weights_ref[:, i * width : (i + 1) * width] for i in range(3)
    )
    queries = contract_cols(query_w, rows) + as_column(query_bias_ref[...])
    queries = (queries.astype(bf16) * HEAD ** (-0.5)).astype(bf16)
    keys = contract_cols(rows, key_w).astype(bf16)
    values = (contract_cols(rows, value_w) + value_bias_ref[...]).astype(bf16)
    grad_mixed = contract_cols(mixer_ref[...], grad_attended).astype(bf16)
    keys_t = keys.T
    grad_queries, grad_keys, grad_values = [], [], []
    for head in range(keys.shape[1] // HEAD):
        at = slice(head * HEAD, (head + 1) * HEAD)
        scores = dot(keys[:, at], queries[at]) + bias[...]
        exponent = jnp.exp(scores - jnp.max(scores, axis=0, keepdims=True))
        probs = exponent * (1.0 / jnp.sum(exponent, axis=0, keepdims=True))
        grad_probs = dot(values[:, at], grad_mixed[at])
        shift = jnp.sum(probs * grad_probs, axis=0, keepdims=True)
        grad_scores = (probs * (grad_probs - shift)).astype(bf16)
        grad_values.append(contract_cols(probs.astype(bf16), grad_mixed[at]))
        grad_keys.append(contract_cols(grad_scores, queries[at]))
        grad_queries.append(dot(keys_t[at], grad_scores) * HEAD ** (-0.5))
    grad_query = jnp.concatenate(grad_queries, axis=0).T.astype(bf16)
    grad_key = jnp.concatenate(grad_keys, axis=1).astype(bf16)
    grad_value = jnp.concatenate(grad_values, axis=1).astype(bf16)
    grads_ref[0] = grad_query
    grads_ref[1] = grad_key
    grads_ref[2] = grad_value
    sums_ref[0, 0:1, :] = column_sum(grad_query)
    sums_ref[0, 1:2, :] = column_sum(grad_value)
    total_grad[...] += dot(grad_query, query_w) + dot(grad_key, key_w) + dot(grad_value, value_w)

    @pl.when(pair == pl.num_programs(1) - 1)
    def _():
        tokens_grad_ref[...] = total_grad[...].astype(bf16)


def attend_back(
    place, lengths, tokens, grad_attended, grad_first, weights, mixer, query_bias, value_bias,
    key_mask,
):
    rows, width = grad_attended.shape
    blocks = rows // BUCKET
    pair = 2 * HEAD
    own = lambda b, h, place: (place[0] * blocks + b, 0)
    by_bucket = pl.BlockSpec((BUCKET, width), lambda b, h, place: (b, 0))
    by_pair = lambda b, h, place: (h, 0)
    row_pair = pl.BlockSpec((1, pair), lambda b, h, place: (0, h))
    return pl.pallas_call(
        attend_back_kernel,
        grid_spec=pltpu.PrefetchScalarGridSpec(
            num_scalar_prefetch=1,
            grid=(blocks, width // pair),
            in_specs=[
                pl.BlockSpec(memory_space=pltpu.SMEM),
                pl.BlockSpec((BUCKET, width), own),
                by_bucket,
                by_bucket,
                pl.BlockSpec((pair, 3 * width), by_pair),
                pl.BlockSpec((pair, width), by_pair),
                row_pair,
                row_pair,
                pl.BlockSpec((1, 1, BUCKET), lambda b, h, place: (place[0] * blocks + b, 0, 0)),
            ],
            out_specs=[
                pl.BlockSpec((3, BUCKET, pair), lambda b, h, place: (0, b, h)),
                by_bucket,
                pl.BlockSpec((1, 8, pair), lambda b, h, place: (b, 0, h)),
            ],
            scratch_shapes=[pltpu.VMEM((BUCKET, BUCKET), f32), pltpu.VMEM((BUCKET, width), f32)],
        ),
        out_shape=[
            jax.ShapeDtypeStruct((3, rows, width), bf16),
            jax.ShapeDtypeStruct((rows, width), bf16),
            jax.ShapeDtypeStruct((blocks, 8, width), f32),
        ],
        compiler_params=params(2),
        name="attend_back",
        cost_estimate=cost(26),
    )(
        place, lengths, tokens, grad_attended, grad_first, weights, mixer, query_bias, value_bias,
        key_mask,
    )


def attention_grads_kernel(
    order_ref, grads_ref, mixed_ref, tokens_ref, grad_attended_ref, weight_grad_ref
):
    which = order_ref[pl.program_id(0)]

    @pl.when(which < 3)
    def _():
        weight_grad_ref[0] = contract_rows(grads_ref[0], tokens_ref[...]).astype(bf16)

    @pl.when(which == 3)
    def _():
        weight_grad_ref[0] = contract_rows(mixed_ref[...], grad_attended_ref[...]).astype(bf16)


def attention_grads(order, grads, mixed, tokens, grad_attended):
    rows, width = grad_attended.shape
    cut = 2
    columns = pl.BlockSpec((rows, width // cut), lambda i, j, order: (0, j))
    return pl.pallas_call(
        attention_grads_kernel,
        grid_spec=pltpu.PrefetchScalarGridSpec(
            num_scalar_prefetch=1,
            grid=(2, cut),
            in_specs=[
                pl.BlockSpec(
                    (1, rows, width // cut),
                    lambda i, j, order: (jnp.minimum(order[i], 2), 0, j),
                ),
                columns,
                pl.BlockSpec((rows, width), lambda i, j, order: (order[2], 0)),
                pl.BlockSpec((rows, width), lambda i, j, order: (0, 0)),
            ],
            out_specs=pl.BlockSpec((1, width // cut, width), lambda i, j, order: (i, j, 0)),
        ),
        out_shape=jax.ShapeDtypeStruct((2, width, width), bf16),
        compiler_params=params(2),
        name="attention_grads",
        cost_estimate=cost(6),
    )(order, grads, mixed, tokens, grad_attended)


def together(*values):
    return lax.optimization_barrier(values)


def add(first, *others):
    total = first.astype(f32)
    for other in others:
        total = total + other.astype(f32)
    return total.astype(bf16)


class Plane:
    def __init__(self, n_dp, n_z):
        self.n_dp, self.n_z = n_dp, n_z
        self.bits = [1 << i for i in range(1, n_dp.bit_length() - 1)][::-1]
        self.dp = lax.axis_index("dp")
        self.z = lax.axis_index("tensor")
        self.core = self.dp & 1
        numbers = list(range(len(self.bits)))
        self.orders = (numbers, numbers[::-1])
        self.groups = [numbers[i : i + 2] for i in range(0, len(numbers), 2)]

    def swap(self, array, bit):
        return lax.ppermute(array, "dp", [(i, i ^ bit) for i in range(self.n_dp)])

    def shift(self, array, by):
        n = self.n_z
        return lax.ppermute(array, "tensor", [(i, (i + by) % n) for i in range(n)])

    def has(self, bit):
        return (self.dp & bit) != 0

    def join(self, own, other, bit, axis):
        return jnp.where(
            self.has(bit),
            jnp.concatenate([other, own], axis=axis),
            jnp.concatenate([own, other], axis=axis),
        )

    def by_bits(self, track):
        lead, _, width = track.shape
        return track.reshape((lead,) + (2,) * len(self.bits) + (-1, width))

    def one(self, track, flips):
        for index, flip in flips.items():
            mine = jnp.where(self.has(self.bits[index]), 1, 0)
            track = lax.dynamic_slice_in_dim(track, 1 - mine if flip else mine, 1, index + 1)
        return track

    def open_bits(self, track):
        return track.reshape((track.shape[0],) + (1,) * len(self.bits) + track.shape[1:])

    def grow_swaps(self, tracks, number):
        return [
            self.swap(track, self.bits[order[number]]) for track, order in zip(tracks, self.orders)
        ]

    def grow_joins(self, tracks, swaps, number):
        return [
            self.join(track, other, self.bits[order[number]], order[number] + 1)
            for track, other, order in zip(tracks, swaps, self.orders)
        ]

    def flips(self, group):
        for number in range(1, 1 << len(group)):
            chosen = {index: bool(number >> i & 1) for i, index in enumerate(group)}
            yield chosen, sum(self.bits[index] for index in group if chosen[index])

    def direct_swaps(self, track, group):
        return [self.swap(track, mask) for _, mask in self.flips(group)]

    def direct_joins(self, track, swaps, group):
        found = [track] + swaps
        for index in group:
            found = [
                self.join(own, other, self.bits[index], index + 1)
                for own, other in zip(found[::2], found[1::2])
            ]
        return found[0]

    def grow_direct(self, track):
        lead, _, width = track.shape
        track = self.open_bits(track)
        for group in self.groups:
            track = self.direct_joins(track, self.direct_swaps(track, group), group)
        return track.reshape(lead, -1, width)

    def fold(self, track, index):
        away, home = self.one(track, {index: True}), self.one(track, {index: False})
        return home, self.swap(away, self.bits[index])

    def fold_direct(self, track, group):
        home = self.one(track, {index: False for index in group})
        return home, [self.swap(self.one(track, chosen), mask) for chosen, mask in self.flips(group)]

    def sum_line(self, parts):
        return [self.shift(parts[s], -s) for s in range(1, self.n_z)]

    def spread_line(self, rows):
        n = self.n_z
        right = left = rows
        steps = []
        for _ in range(n - 1):
            right = lax.ppermute(right, "tensor", [(i, i + 1) for i in range(n - 1)])
            left = lax.ppermute(left, "tensor", [(i + 1, i) for i in range(n - 1)])
            steps.append((right, left))
        return steps


def on_device(
    n_dp,
    n_z,
    tokens,
    lengths,
    key_mask,
    query_weight,
    query_bias,
    key_weight,
    value_weight,
    value_bias,
    output_weight,
    output_bias,
    first_gain,
    first_shift,
    inner_weight,
    inner_bias,
    outer_weight,
    outer_bias,
    second_gain,
    second_shift,
    cotangent,
):
    width = tokens.shape[1]
    mine = query_weight.shape[1]
    units = inner_weight.shape[1]
    all_rows = tokens.shape[0]
    all_blocks = all_rows // BUCKET
    rows = all_rows // n_z
    plane = Plane(n_dp, n_z)
    dp, z, core = plane.dp, plane.z, plane.core
    others = range(1, n_z)
    place = z.reshape(1)

    feed_rows = units // n_dp
    mixer_rows = mine // n_dp
    spot = core * (n_dp // 2) + (dp >> 1)
    outer_start = spot * feed_rows
    bias_row = jnp.concatenate([query_bias, value_bias, inner_bias])
    piece = jnp.concatenate(
        [
            lax.dynamic_slice_in_dim(inner_weight, outer_start, feed_rows, 1).T,
            lax.dynamic_slice_in_dim(outer_weight, outer_start, feed_rows, 0),
        ],
        axis=1,
    )
    extra = lax.dynamic_slice_in_dim(output_weight, spot * mixer_rows, mixer_rows, 0)
    extra = jnp.pad(extra, ((0, mixer_rows % 2), (0, 0))).reshape(-1, 2 * width)
    mixer_pairs = extra.shape[0]
    bias_line = jnp.pad(bias_row, (0, 2 * width - bias_row.shape[0]))[None]
    piece = jnp.concatenate([piece, extra, bias_line], axis=0)
    piece = jnp.pad(piece, ((0, -piece.shape[0] % 16), (0, 0)))
    line = [plane.shift(piece, s) for s in others]

    query_t, key_t, value_t = query_weight.T, key_weight.T, value_weight.T
    key_mask_rows = key_mask.reshape(all_blocks, 1, BUCKET)
    mixed_all = attend_forward(
        lengths, tokens, query_t, key_t, value_t, jnp.stack([query_bias, value_bias]),
        key_mask_rows,
    )
    mixed_all, line = together(mixed_all, line)

    def block(matrix, number):
        return lax.dynamic_slice_in_dim(matrix, number * rows, rows, 0)

    remote = jnp.stack(line)
    biases = jnp.concatenate(
        [bias_row[None], remote[:, feed_rows + mixer_pairs, : bias_row.shape[0]]], axis=0
    ).astype(f32)
    count = feed_rows + mixer_pairs
    tracks = [
        plane.open_bits(remote[:, :count, i * width : (i + 1) * width]) for i in range(2)
    ]
    swaps = plane.grow_swaps(tracks, 0)
    mixed_line = [plane.shift(block(mixed_all, lax.rem(z + s, n_z)), s) for s in others]
    attention_own = jnp.concatenate([query_t, key_t, value_t], axis=1)
    attention_piece = lax.dynamic_slice_in_dim(attention_own, dp * mixer_rows, mixer_rows, 0)
    attention_line = [plane.shift(attention_piece, s) for s in others]
    for number in range(len(plane.bits)):
        if number > 0:
            swaps = plane.grow_swaps(tracks, number)
        if number == len(plane.bits) - 1:
            swaps, attention_line = together(swaps, attention_line)
        tracks = plane.grow_joins(tracks, swaps, number)
    tracks = [track.reshape(n_z - 1, -1, count, width) for track in tracks]

    mixer_half = jnp.stack([track[:, :, feed_rows:] for track in tracks], axis=3)
    mixer_half = mixer_half.reshape(n_z - 1, n_dp // 2, 2 * mixer_pairs, width)[:, :, :mixer_rows]
    mixer_half = mixer_half.reshape(n_z - 1, 1, -1, width)
    mixer_remote = plane.join(mixer_half, plane.swap(mixer_half, 1), 1, 1)
    mixer = jnp.concatenate(
        [output_weight, mixer_remote.reshape(-1, width)], axis=0
    )
    own_half = [
        lax.dynamic_slice_in_dim(inner_weight, core * (units // 2), units // 2, 1).T,
        lax.dynamic_slice_in_dim(outer_weight, core * (units // 2), units // 2, 0),
    ]
    feed_keep = jnp.stack(
        [
            jnp.concatenate(
                [own[None], track[:, :, :feed_rows].reshape(n_z - 1, -1, width)], axis=0
            )
            for own, track in zip(own_half, tracks)
        ]
    )
    feed_send = plane.swap(feed_keep, 1)
    mixed_rows = jnp.concatenate([block(mixed_all, z)] + mixed_line, axis=1)

    query_bias_all = biases[:, :mine].reshape(1, -1)
    value_bias_all = biases[:, mine : 2 * mine].reshape(1, -1)
    inner_bias_all = biases[:, 2 * mine : 2 * mine + units].reshape(n_z, 2, units // 2)
    bias_keep = lax.dynamic_slice_in_dim(inner_bias_all, core, 1, 1)
    bias_send = lax.dynamic_slice_in_dim(inner_bias_all, 1 - core, 1, 1)
    vectors = jnp.stack(
        [output_bias, first_gain, first_shift, outer_bias, second_gain, second_shift]
        + [jnp.zeros_like(output_bias)] * 2
    ).astype(f32)

    attention_grown = plane.open_bits(jnp.stack(attention_line))
    for group in plane.groups[:-1]:
        attention_grown = plane.direct_joins(
            attention_grown, plane.direct_swaps(attention_grown, group), group
        )
    attention_swaps = plane.direct_swaps(attention_grown, plane.groups[-1])

    hidden_keep, slope_keep, normed_low, first_normed, first_scale, second_start = feed_first(
        place, mixed_rows, mixer, tokens, vectors, feed_keep, bias_keep
    )
    second_start, feed_send, attention_swaps = together(
        second_start, feed_send, attention_swaps
    )
    attention_half = plane.direct_joins(attention_grown, attention_swaps, plane.groups[-1])
    attention_half = attention_half.reshape(n_z - 1, -1, 1, mixer_rows, 3 * width)
    attention_other = plane.swap(attention_half, 1)
    hidden_send, slope_send, my_output, grad_second, grad_outer, second_sums = feed_second(
        place, lengths, normed_low, second_start, cotangent, vectors, feed_send, bias_send
    )
    output = lax.all_gather(my_output, "tensor", axis=0, tiled=True)
    grad_outer, attention_other = together(grad_outer, attention_other)
    attention_remote = plane.join(attention_half, attention_other, 1, 2)
    attention_weights = jnp.concatenate(
        [attention_own, attention_remote.reshape(-1, 3 * width)], axis=0
    )

    feed_grad_send, bias_grad_send, grad_normed = feed_back(
        grad_outer, normed_low, hidden_send, slope_send, feed_send, grad_second
    )
    feed_grad_other = plane.swap(feed_grad_send, 1)
    feed_grad_keep, bias_grad_keep, grad_first, grad_attended, first_sums = feed_back(
        grad_outer, normed_low, hidden_keep, slope_keep, feed_keep, grad_normed,
        (first_normed, first_scale, vectors),
    )
    grad_first, grad_attended, feed_grad_other = together(
        grad_first, grad_attended, feed_grad_other
    )
    inner_bias_grad = plane.join(bias_grad_keep, bias_grad_send, 1, 1).reshape(n_z, units)
    feed_sum = add(feed_grad_keep, feed_grad_other)
    tracks = [plane.by_bits(feed_sum[i]) for i in range(2)]

    def step(number):
        return [
            plane.fold(track, order[number]) for track, order in zip(tracks, plane.orders)
        ]

    folded = step(0)
    attention_back, my_tokens_grad, back_sums = attend_back(
        place, lengths, tokens, grad_attended, grad_first, attention_weights, mixer,
        query_bias_all, value_bias_all, key_mask_rows,
    )
    line_steps = plane.spread_line(my_tokens_grad)
    attention_back, folded = together(attention_back, folded)
    tracks = [add(*pair) for pair in folded]
    for number in range(1, len(plane.bits)):
        folded = step(number)
        if number < len(plane.bits) - 1:
            tracks = [add(*pair) for pair in folded]

    pair = jnp.arange(2, dtype=jnp.int32)

    def weight_grads(side):
        order = jnp.concatenate([pair + 2 * side, place])
        return attention_grads(order, attention_back, mixed_rows, tokens, grad_attended)

    grads_send = weight_grads(1 - core)
    grads_send, folded = together(grads_send, folded)
    grads_other = plane.swap(grads_send, 1)
    tracks = [add(*pair) for pair in folded]
    feed_parts = jnp.concatenate([t.reshape(n_z, -1, width) for t in tracks], axis=2)
    feed_line = plane.sum_line(feed_parts)
    grads_keep = weight_grads(core)
    grads_keep, grads_other, line_steps[0], output = together(
        grads_keep, grads_other, line_steps[0], output
    )
    grads_sum = add(grads_keep, grads_other).reshape(2 * n_z, mine, width)
    grads_sum = plane.by_bits(grads_sum)
    for group in plane.groups:
        home, arrived = plane.fold_direct(grads_sum, group)
        grads_sum = add(home, *arrived)
    attention_parts = grads_sum.reshape(2, n_z, -1, width)
    attention_parts, feed_line, line_steps[1:2] = together(
        attention_parts, feed_line, line_steps[1:2]
    )
    attention_line = plane.sum_line([attention_parts[:, s] for s in range(n_z)])
    feed_total = add(feed_parts[0], *feed_line)
    feed_half = plane.grow_direct(feed_total[None])
    feed_grad = plane.join(feed_half, plane.swap(feed_half, 1), 1, 1)[0]
    attention_half = plane.grow_direct(add(attention_parts[:, 0], *attention_line))
    grad_list = plane.join(attention_half, plane.swap(attention_half, 1), 1, 0)

    tokens_grad = jnp.zeros((all_rows, width), bf16)
    tokens_grad = lax.dynamic_update_slice_in_dim(tokens_grad, my_tokens_grad, z * rows, 0)
    for s in others:
        came = jnp.where(z >= s, line_steps[s - 1][0], line_steps[n_z - 1 - s][1])
        there = lax.rem(z + n_z - s, n_z) * rows
        tokens_grad = lax.dynamic_update_slice_in_dim(tokens_grad, came, there, 0)

    back_sums = jnp.sum(back_sums, axis=0)
    query_bias_grad = back_sums[0].reshape(n_z, mine)
    value_bias_grad = back_sums[1].reshape(n_z, mine)

    shared = jnp.concatenate([first_sums[:3], second_sums[:3]], axis=0).reshape(-1)
    split = jnp.concatenate([inner_bias_grad, query_bias_grad, value_bias_grad], axis=1)
    small = jnp.concatenate([shared, split.reshape(-1)])
    for bit in [1] + plane.bits:
        small = small + plane.swap(small, bit)
    n_shared, n_split = 6 * width, split.shape[1]
    shared = small[:n_shared]
    split = small[n_shared : n_shared + n_split]
    for s in others:
        there = plane.shift(small, -s)
        shared = shared + there[:n_shared]
        split = split + there[n_shared + s * n_split : n_shared + (s + 1) * n_split]
    shared = shared.reshape(6, width)

    return (
        output,
        tokens_grad,
        grad_list[0].T.astype(f32),
        split[units : units + mine],
        grad_list[1].T.astype(f32),
        grad_list[2].T.astype(f32),
        split[units + mine :],
        grad_list[3].astype(f32),
        shared[0],
        shared[1],
        shared[2],
        feed_grad[:, :width].T.astype(f32),
        split[:units],
        feed_grad[:, width:].astype(f32),
        shared[3],
        shared[4],
        shared[5],
    )


def solution(mesh):
    n_dp, n_z = mesh.shape["dp"], mesh.shape["tensor"]
    in_specs = (
        P("dp", None),
        P("dp", None),
        P("dp"),
        P(None, "tensor"),
        P("tensor"),
        P(None, "tensor"),
        P(None, "tensor"),
        P("tensor"),
        P("tensor", None),
        P(),
        P(),
        P(),
        P(None, "tensor"),
        P("tensor"),
        P("tensor", None),
        P(),
        P(),
        P(),
        P("dp", None),
    )
    out_specs = (
        P("dp", None),
        P("dp", None),
        P(None, "tensor"),
        P("tensor"),
        P(None, "tensor"),
        P(None, "tensor"),
        P("tensor"),
        P("tensor", None),
        P(),
        P(),
        P(),
        P(None, "tensor"),
        P("tensor"),
        P("tensor", None),
        P(),
        P(),
        P(),
    )

    def program(*args):
        return on_device(n_dp, n_z, *args)

    return jax.shard_map(
        program, mesh=mesh, in_specs=in_specs, out_specs=out_specs, check_vma=False
    )
```

```python
import functools

import jax
import jax.numpy as jnp
from jax import lax
from jax.experimental import pallas as pl
from jax.experimental.pallas import tpu as pltpu
from jax.sharding import PartitionSpec as P

HEAD = 64
BUCKET = 512
ITEMS = 8


negative_fill = -1e30
epsilon = 1e-06
f32 = jnp.float32
bf16 = jnp.bfloat16
VMEM_BYTES = 56 * 1024 * 1024


def dot(left, right):
    return jnp.dot(left, right, preferred_element_type=f32)


def contract_rows(left, right):
    return lax.dot_general(left, right, (((0,), (0,)), ((), ())), preferred_element_type=f32)


def contract_cols(left, right):
    return lax.dot_general(left, right, (((1,), (1,)), ((), ())), preferred_element_type=f32)


def norm_rows(values):
    centred = values - jnp.mean(values, axis=1, keepdims=True)
    inv_scale = lax.rsqrt(jnp.mean(centred * centred, axis=1, keepdims=True) + epsilon)
    return centred * inv_scale, inv_scale


def norm_back(grad_rows, norm_gain, normed, inv_scale):
    scaled = grad_rows * norm_gain
    return inv_scale * (
        scaled
        - jnp.mean(scaled, axis=1, keepdims=True)
        - normed * jnp.mean(scaled * normed, axis=1, keepdims=True)
    )


def column_sum(matrix):
    return jnp.sum(matrix.astype(f32), axis=0, keepdims=True)


def fixed(shape):
    return pl.BlockSpec(shape, lambda *_: (0,) * len(shape))


def cost(microseconds):
    return pl.CostEstimate(
        flops=int(microseconds * 1.0e9), bytes_accessed=int(microseconds * 1.0e6), transcendentals=0
    )


def params(axes):
    return pltpu.CompilerParams(
        dimension_semantics=("arbitrary",) * axes, vmem_limit_bytes=VMEM_BYTES
    )


def item_places(lengths_ref, row, shape, axis):
    places = lax.broadcasted_iota(jnp.int32, shape, axis)
    end = jnp.int32(0)
    items = jnp.zeros(shape, jnp.int32)
    for slot in range(ITEMS):
        end = end + lengths_ref[row, slot]
        items = items + (places >= end).astype(jnp.int32)
    return items


def as_column(row):
    return jnp.broadcast_to(row.astype(f32), (8, row.shape[1])).T[:, :1]


def mask_bias(lengths_ref, row, key_mask):
    shape = (BUCKET, BUCKET)
    diagonal = lax.broadcasted_iota(jnp.int32, shape, 0) == lax.broadcasted_iota(
        jnp.int32, shape, 1
    )
    item_row = item_places(lengths_ref, row, (1, BUCKET), 1)
    item_column = item_places(lengths_ref, row, (BUCKET, 1), 0)
    code_column = jnp.where(as_column(key_mask) == 1.0, item_column, -1)
    return jnp.where((code_column == item_row) | diagonal, 0.0, negative_fill).astype(f32)


def attend_forward_kernel(
    lengths_ref, tokens_ref, query_ref, key_ref, value_ref, biases_ref, key_mask_ref, mixed_ref,
):
    rows = tokens_ref[...]
    queries = contract_cols(query_ref[...], rows) + as_column(biases_ref[0:1, :])
    queries = (queries.astype(bf16) * HEAD ** (-0.5)).astype(bf16)
    keys = contract_cols(rows, key_ref[...]).astype(bf16)
    values = (contract_cols(value_ref[...], rows) + as_column(biases_ref[1:2, :])).astype(bf16)
    bias = mask_bias(lengths_ref, pl.program_id(0), key_mask_ref[0])
    parts = []
    for head in range(queries.shape[0] // HEAD):
        at = slice(head * HEAD, (head + 1) * HEAD)
        scores = dot(keys[:, at], queries[at]) + bias
        exponent = jnp.exp(scores - jnp.max(scores, axis=0, keepdims=True))
        total = jnp.sum(exponent, axis=0, keepdims=True)
        parts.append(dot(values[at], exponent.astype(bf16)) / total)
    mixed_ref[...] = jnp.concatenate(parts, axis=0).T.astype(bf16)


def attend_forward(lengths, tokens, query, key, value, biases, key_mask):
    blocks = lengths.shape[0]
    mine, width = key.shape
    return pl.pallas_call(
        attend_forward_kernel,
        grid=(blocks,),
        in_specs=[
            pl.BlockSpec(memory_space=pltpu.SMEM),
            pl.BlockSpec((BUCKET, width), lambda b: (b, 0)),
            fixed((mine, width)),
            fixed((mine, width)),
            fixed((mine, width)),
            fixed((2, mine)),
            pl.BlockSpec((1, 1, BUCKET), lambda b: (b, 0, 0)),
        ],
        out_specs=pl.BlockSpec((BUCKET, mine), lambda b: (b, 0)),
        out_shape=jax.ShapeDtypeStruct((blocks * BUCKET, mine), bf16),
        compiler_params=params(1),
        name="attend_forward",
        cost_estimate=cost(12),
    )(lengths, tokens, query, key, value, biases, key_mask)


def feed_units(normed_low_ref, weights_ref, bias_ref, hidden_ref, slope_ref):
    inner_pre = contract_cols(normed_low_ref[...], weights_ref[0, 0]) + bias_ref[0]
    normal_cdf = 0.5 + 0.5 * lax.erf(inner_pre * 0.7071067811865476)
    density = jnp.exp(-0.5 * inner_pre * inner_pre) * 0.3989422804014327
    hidden = (inner_pre * normal_cdf).astype(bf16)
    hidden_ref[...] = hidden
    slope_ref[...] = (normal_cdf + inner_pre * density).astype(bf16)
    return dot(hidden, weights_ref[1, 0])


def feed_first_kernel(
    place_ref, mixed_ref, mixer_ref, tokens_ref, vectors_ref, weights_ref, bias_ref,
    hidden_ref, slope_ref, normed_low_ref, first_normed_ref, first_scale_ref, sum_ref,
):
    @pl.when(pl.program_id(0) == 0)
    def _():
        output_bias, first_gain, first_shift, outer_bias = (
            vectors_ref[i : i + 1, :] for i in range(4)
        )
        attended = dot(mixed_ref[...], mixer_ref[...]) + output_bias
        normed, inv_scale = norm_rows(tokens_ref[...].astype(f32) + attended)
        whole = normed * first_gain + first_shift
        first_normed_ref[...] = normed
        first_scale_ref[...] = inv_scale
        normed_low_ref[...] = whole.astype(bf16)
        sum_ref[...] = whole + outer_bias

    sum_ref[...] += feed_units(normed_low_ref, weights_ref, bias_ref, hidden_ref, slope_ref)


def feed_second_kernel(
    place_ref, lengths_ref, normed_low_ref, start_ref, cotangent_ref, vectors_ref, weights_ref,
    bias_ref, hidden_ref, slope_ref, output_ref, grad_second_ref, grad_outer_ref, sums_ref,
    second_sum,
):
    @pl.when(pl.program_id(0) == 0)
    def _():
        second_sum[...] = start_ref[...]

    second_sum[...] += feed_units(normed_low_ref, weights_ref, bias_ref, hidden_ref, slope_ref)

    @pl.when(pl.program_id(0) == pl.num_programs(0) - 1)
    def _():
        second_gain, second_shift = vectors_ref[4:5, :], vectors_ref[5:6, :]
        normed, inv_scale = norm_rows(second_sum[...])
        blocks = normed.shape[0] // BUCKET
        live = jnp.concatenate(
            [
                (item_places(lengths_ref, place_ref[0] * blocks + b, (BUCKET, 1), 0) < ITEMS)
                for b in range(blocks)
            ],
            axis=0,
        ).astype(f32)
        output_ref[...] = ((normed * second_gain + second_shift) * live).astype(bf16)
        grad_final = cotangent_ref[...].astype(f32) * live
        grad_second = norm_back(grad_final, second_gain, normed, inv_scale)
        grad_outer = grad_second.astype(bf16)
        grad_second_ref[...] = grad_second
        grad_outer_ref[...] = grad_outer
        sums_ref[0:1, :] = column_sum(grad_outer)
        sums_ref[1:2, :] = column_sum(grad_final * normed)
        sums_ref[2:3, :] = column_sum(grad_final)


def feed_specs(weights, rows):
    parts, half, width = weights.shape[1:]
    whole = fixed((rows, width))
    own = pl.BlockSpec((rows, width), lambda j, place: (place[0], 0))
    by_part = [
        pl.BlockSpec((2, 1, half, width), lambda j, place: (0, j, 0, 0)),
        pl.BlockSpec((1, 1, half), lambda j, place: (j, 0, 0)),
    ]
    columns = [pl.BlockSpec((rows, half), lambda j, place: (0, j))] * 2
    unit_shapes = [jax.ShapeDtypeStruct((rows, parts * half), bf16)] * 2
    return parts, width, whole, own, by_part, columns, unit_shapes


def feed_first(place, mixed, mixer, tokens, vectors, weights, bias):
    rows = mixed.shape[0]
    parts, width, whole, own, by_part, columns, unit_shapes = feed_specs(weights, rows)
    return pl.pallas_call(
        feed_first_kernel,
        grid_spec=pltpu.PrefetchScalarGridSpec(
            num_scalar_prefetch=1,
            grid=(parts,),
            in_specs=[whole, fixed((width, width)), own, fixed((8, width))] + by_part,
            out_specs=columns + [whole, whole, fixed((rows, 1)), whole],
        ),
        out_shape=unit_shapes
        + [
            jax.ShapeDtypeStruct((rows, width), bf16),
            jax.ShapeDtypeStruct((rows, width), f32),
            jax.ShapeDtypeStruct((rows, 1), f32),
            jax.ShapeDtypeStruct((rows, width), f32),
        ],
        compiler_params=params(1),
        name="feed_first",
        cost_estimate=cost(11),
    )(place, mixed, mixer, tokens, vectors, weights, bias)


def feed_second(place, lengths, normed_low, start, cotangent, vectors, weights, bias):
    rows = normed_low.shape[0]
    parts, width, whole, own, by_part, columns, unit_shapes = feed_specs(weights, rows)
    return pl.pallas_call(
        feed_second_kernel,
        grid_spec=pltpu.PrefetchScalarGridSpec(
            num_scalar_prefetch=1,
            grid=(parts,),
            in_specs=[pl.BlockSpec(memory_space=pltpu.SMEM), whole, whole, own, fixed((8, width))]
            + by_part,
            out_specs=columns + [whole, whole, whole, fixed((8, width))],
            scratch_shapes=[pltpu.VMEM((rows, width), f32)],
        ),
        out_shape=unit_shapes
        + [
            jax.ShapeDtypeStruct((rows, width), bf16),
            jax.ShapeDtypeStruct((rows, width), f32),
            jax.ShapeDtypeStruct((rows, width), bf16),
            jax.ShapeDtypeStruct((8, width), f32),
        ],
        compiler_params=params(1),
        name="feed_second",
        cost_estimate=cost(11),
    )(place, lengths, normed_low, start, cotangent, vectors, weights, bias)


def feed_chunk(grad_outer_ref, normed_low_ref, hidden_ref, slope_ref, weights_ref,
               weights_grad_ref, bias_grad_ref):
    grad_outer = grad_outer_ref[...]
    grad_hidden = contract_cols(grad_outer, weights_ref[1, 0])
    grad_inner = (grad_hidden * slope_ref[...].astype(f32)).astype(bf16)
    weights_grad_ref[1, 0] = contract_rows(hidden_ref[...], grad_outer).astype(bf16)
    weights_grad_ref[0, 0] = contract_rows(grad_inner, normed_low_ref[...]).astype(bf16)
    bias_grad_ref[0] = column_sum(grad_inner)
    return dot(grad_inner, weights_ref[0, 0])


def feed_back_kernel(
    grad_outer_ref, normed_low_ref, hidden_ref, slope_ref, weights_ref, start_ref,
    weights_grad_ref, bias_grad_ref, grad_normed_ref,
):
    @pl.when(pl.program_id(0) == 0)
    def _():
        grad_normed_ref[...] = start_ref[...]

    grad_normed_ref[...] += feed_chunk(
        grad_outer_ref, normed_low_ref, hidden_ref, slope_ref, weights_ref,
        weights_grad_ref, bias_grad_ref,
    )


def feed_back_norm_kernel(
    grad_outer_ref, normed_low_ref, hidden_ref, slope_ref, weights_ref, start_ref,
    first_normed_ref, first_scale_ref, vectors_ref,
    weights_grad_ref, bias_grad_ref, grad_first_ref, grad_attended_ref, sums_ref,
    grad_normed,
):
    @pl.when(pl.program_id(0) == 0)
    def _():
        grad_normed[...] = start_ref[...]

    grad_normed[...] += feed_chunk(
        grad_outer_ref, normed_low_ref, hidden_ref, slope_ref, weights_ref,
        weights_grad_ref, bias_grad_ref,
    )

    @pl.when(pl.program_id(0) == pl.num_programs(0) - 1)
    def _():
        grad_rows, normed = grad_normed[...], first_normed_ref[...]
        grad_first = norm_back(grad_rows, vectors_ref[1:2, :], normed, first_scale_ref[...])
        grad_attended = grad_first.astype(bf16)
        grad_first_ref[...] = grad_first
        grad_attended_ref[...] = grad_attended
        sums_ref[0:1, :] = column_sum(grad_attended)
        sums_ref[1:2, :] = column_sum(grad_rows * normed)
        sums_ref[2:3, :] = column_sum(grad_rows)


def feed_back(grad_outer, normed_low, hidden, slope, weights, start, norm=None):
    rows, width = grad_outer.shape
    parts, half = weights.shape[1:3]
    columns = pl.BlockSpec((rows, half), lambda j: (0, j))
    by_part = pl.BlockSpec((2, 1, half, width), lambda j: (0, j, 0, 0))
    whole = fixed((rows, width))
    in_specs = [whole, whole, columns, columns, by_part, whole]
    out_specs = [by_part, pl.BlockSpec((1, 1, half), lambda j: (j, 0, 0)), whole]
    out_shape = [
        jax.ShapeDtypeStruct((2, parts, half, width), bf16),
        jax.ShapeDtypeStruct((parts, 1, half), f32),
        jax.ShapeDtypeStruct((rows, width), f32),
    ]
    args = [grad_outer, normed_low, hidden, slope, weights, start]
    scratch = []
    if norm is not None:
        in_specs += [whole, fixed((rows, 1)), fixed((8, width))]
        out_specs += [whole, fixed((8, width))]
        out_shape += [
            jax.ShapeDtypeStruct((rows, width), bf16),
            jax.ShapeDtypeStruct((8, width), f32),
        ]
        args += list(norm)
        scratch = [pltpu.VMEM((rows, width), f32)]
    return pl.pallas_call(
        feed_back_kernel if norm is None else feed_back_norm_kernel,
        grid=(parts,),
        in_specs=in_specs,
        out_specs=out_specs,
        out_shape=out_shape,
        scratch_shapes=scratch,
        compiler_params=params(1),
        name="feed_back" if norm is None else "feed_back_norm",
        cost_estimate=cost(11 if norm is None else 13),
    )(*args)


def attend_back_kernel(
    own_heads, place_ref, lengths_ref, tokens_ref, grad_attended_ref, grad_first_ref,
    own_even_ref, own_odd_ref, remote_even_ref, remote_odd_ref, mixer_ref, biases_ref, key_mask_ref,
    grads_ref, tokens_grad_ref, sums_ref,
    bias, total_grad,
):
    pair = pl.program_id(1)

    @pl.when(pair == 0)
    def _():
        row = place_ref[0] * pl.num_programs(0) + pl.program_id(0)
        bias[...] = mask_bias(lengths_ref, row, key_mask_ref[0])
        total_grad[...] = grad_first_ref[...]

    rows, grad_attended = tokens_ref[...], grad_attended_ref[...]
    width = rows.shape[1]
    weights = jnp.concatenate(
        [
            jnp.where(2 * pair < own_heads, own_even_ref[...], remote_even_ref[...]),
            jnp.where(2 * pair + 1 < own_heads, own_odd_ref[...], remote_odd_ref[...]),
        ],
        axis=0,
    )
    query_w, key_w, value_w = (weights[:, i * width : (i + 1) * width] for i in range(3))
    queries = contract_cols(query_w, rows) + as_column(biases_ref[0:1, :])
    queries = (queries.astype(bf16) * HEAD ** (-0.5)).astype(bf16)
    keys = contract_cols(rows, key_w).astype(bf16)
    values = (contract_cols(rows, value_w) + biases_ref[1:2, :]).astype(bf16)
    grad_mixed = contract_cols(mixer_ref[...], grad_attended).astype(bf16)
    keys_t = keys.T
    grad_queries, grad_keys, grad_values = [], [], []
    for head in range(keys.shape[1] // HEAD):
        at = slice(head * HEAD, (head + 1) * HEAD)
        scores = dot(keys[:, at], queries[at]) + bias[...]
        exponent = jnp.exp(scores - jnp.max(scores, axis=0, keepdims=True))
        probs = exponent * (1.0 / jnp.sum(exponent, axis=0, keepdims=True))
        grad_probs = dot(values[:, at], grad_mixed[at])
        shift = jnp.sum(probs * grad_probs, axis=0, keepdims=True)
        grad_scores = (probs * (grad_probs - shift)).astype(bf16)
        grad_values.append(contract_cols(probs.astype(bf16), grad_mixed[at]))
        grad_keys.append(contract_cols(grad_scores, queries[at]))
        grad_queries.append(dot(keys_t[at], grad_scores) * HEAD ** (-0.5))
    grad_query = jnp.concatenate(grad_queries, axis=0).T.astype(bf16)
    grad_key = jnp.concatenate(grad_keys, axis=1).astype(bf16)
    grad_value = jnp.concatenate(grad_values, axis=1).astype(bf16)
    grads_ref[0] = grad_query
    grads_ref[1] = grad_key
    grads_ref[2] = grad_value
    sums_ref[0, 0:1, :] = column_sum(grad_query)
    sums_ref[0, 1:2, :] = column_sum(grad_value)
    total_grad[...] += dot(grad_query, query_w) + dot(grad_key, key_w) + dot(grad_value, value_w)

    @pl.when(pair == pl.num_programs(1) - 1)
    def _():
        tokens_grad_ref[...] = total_grad[...].astype(bf16)


def attend_back(
    place, lengths, tokens, grad_attended, grad_first, own_weights, remote_weights, mixer, biases,
    key_mask,
):
    rows, width = grad_attended.shape
    blocks = rows // BUCKET
    pair = 2 * HEAD
    own = lambda b, h, place: (place[0] * blocks + b, 0)
    by_bucket = pl.BlockSpec((BUCKET, width), lambda b, h, place: (b, 0))
    by_pair = lambda b, h, place: (h, 0)
    own_heads, remote_heads = own_weights.shape[0] // HEAD, remote_weights.shape[0] // HEAD

    def own_head(odd):
        return pl.BlockSpec(
            (HEAD, 3 * width), lambda b, h, place: (jnp.minimum(2 * h + odd, own_heads - 1), 0)
        )

    def remote_head(odd):
        return pl.BlockSpec(
            (HEAD, 3 * width),
            lambda b, h, place: (
                jnp.clip(2 * h + odd - own_heads, 0, remote_heads - 1),
                0,
            ),
        )

    return pl.pallas_call(
        functools.partial(attend_back_kernel, own_heads),
        grid_spec=pltpu.PrefetchScalarGridSpec(
            num_scalar_prefetch=1,
            grid=(blocks, width // pair),
            in_specs=[
                pl.BlockSpec(memory_space=pltpu.SMEM),
                pl.BlockSpec((BUCKET, width), own),
                by_bucket,
                by_bucket,
                own_head(0),
                own_head(1),
                remote_head(0),
                remote_head(1),
                pl.BlockSpec((pair, width), by_pair),
                pl.BlockSpec((8, pair), lambda b, h, place: (0, h)),
                pl.BlockSpec((1, 1, BUCKET), lambda b, h, place: (place[0] * blocks + b, 0, 0)),
            ],
            out_specs=[
                pl.BlockSpec((3, BUCKET, pair), lambda b, h, place: (0, b, h)),
                by_bucket,
                pl.BlockSpec((1, 8, pair), lambda b, h, place: (b, 0, h)),
            ],
            scratch_shapes=[pltpu.VMEM((BUCKET, BUCKET), f32), pltpu.VMEM((BUCKET, width), f32)],
        ),
        out_shape=[
            jax.ShapeDtypeStruct((3, rows, width), bf16),
            jax.ShapeDtypeStruct((rows, width), bf16),
            jax.ShapeDtypeStruct((blocks, 8, width), f32),
        ],
        compiler_params=params(2),
        name="attend_back",
        cost_estimate=cost(26),
    )(
        place, lengths, tokens, grad_attended, grad_first, own_weights, own_weights,
        remote_weights, remote_weights, mixer, biases, key_mask,
    )


def attention_grads_kernel(
    order_ref, grads_ref, mixed_ref, tokens_ref, grad_attended_ref, weight_grad_ref
):
    which = order_ref[pl.program_id(0)]

    @pl.when(which < 3)
    def _():
        weight_grad_ref[0] = contract_rows(grads_ref[0], tokens_ref[...]).astype(bf16)

    @pl.when(which == 3)
    def _():
        weight_grad_ref[0] = contract_rows(mixed_ref[...], grad_attended_ref[...]).astype(bf16)


def attention_grads(order, grads, mixed, tokens, grad_attended):
    rows, width = grad_attended.shape
    cut = 2
    columns = pl.BlockSpec((rows, width // cut), lambda i, j, order: (0, j))
    return pl.pallas_call(
        attention_grads_kernel,
        grid_spec=pltpu.PrefetchScalarGridSpec(
            num_scalar_prefetch=1,
            grid=(2, cut),
            in_specs=[
                pl.BlockSpec(
                    (1, rows, width // cut),
                    lambda i, j, order: (jnp.minimum(order[i], 2), 0, j),
                ),
                columns,
                pl.BlockSpec((rows, width), lambda i, j, order: (order[2], 0)),
                pl.BlockSpec((rows, width), lambda i, j, order: (0, 0)),
            ],
            out_specs=pl.BlockSpec((1, width // cut, width), lambda i, j, order: (i, j, 0)),
        ),
        out_shape=jax.ShapeDtypeStruct((2, width, width), bf16),
        compiler_params=params(2),
        name="attention_grads",
        cost_estimate=cost(6),
    )(order, grads, mixed, tokens, grad_attended)


def together(*values):
    return lax.optimization_barrier(values)


def add(first, *others):
    total = first.astype(f32)
    for other in others:
        total = total + other.astype(f32)
    return total.astype(bf16)


class Plane:
    def __init__(self, n_dp, n_z):
        self.n_dp, self.n_z = n_dp, n_z
        self.bits = [1 << i for i in range(1, n_dp.bit_length() - 1)][::-1]
        self.dp = lax.axis_index("dp")
        self.z = lax.axis_index("tensor")
        self.core = self.dp & 1
        numbers = list(range(len(self.bits)))
        self.orders = (numbers, numbers[::-1])
        self.groups = [numbers[i : i + 2] for i in range(0, len(numbers), 2)]

    def swap(self, array, bit):
        return lax.ppermute(array, "dp", [(i, i ^ bit) for i in range(self.n_dp)])

    def shift(self, array, by):
        n = self.n_z
        return lax.ppermute(array, "tensor", [(i, (i + by) % n) for i in range(n)])

    def has(self, bit):
        return (self.dp & bit) != 0

    def join(self, own, other, bit, axis):
        return jnp.where(
            self.has(bit),
            jnp.concatenate([other, own], axis=axis),
            jnp.concatenate([own, other], axis=axis),
        )

    def by_bits(self, track):
        lead, _, width = track.shape
        return track.reshape((lead,) + (2,) * len(self.bits) + (-1, width))

    def one(self, track, flips):
        for index, flip in flips.items():
            mine = jnp.where(self.has(self.bits[index]), 1, 0)
            track = lax.dynamic_slice_in_dim(track, 1 - mine if flip else mine, 1, index + 1)
        return track

    def open_bits(self, track):
        return track.reshape((track.shape[0],) + (1,) * len(self.bits) + track.shape[1:])

    def grow_swaps(self, tracks, number):
        return [
            self.swap(track, self.bits[order[number]]) for track, order in zip(tracks, self.orders)
        ]

    def grow_joins(self, tracks, swaps, number):
        return [
            self.join(track, other, self.bits[order[number]], order[number] + 1)
            for track, other, order in zip(tracks, swaps, self.orders)
        ]

    def flips(self, group):
        for number in range(1, 1 << len(group)):
            chosen = {index: bool(number >> i & 1) for i, index in enumerate(group)}
            yield chosen, sum(self.bits[index] for index in group if chosen[index])

    def direct_swaps(self, track, group):
        return [self.swap(track, mask) for _, mask in self.flips(group)]

    def direct_joins(self, track, swaps, group):
        found = [track] + swaps
        for index in group:
            found = [
                self.join(own, other, self.bits[index], index + 1)
                for own, other in zip(found[::2], found[1::2])
            ]
        return found[0]

    def grow_direct(self, track):
        lead, _, width = track.shape
        track = self.open_bits(track)
        for group in self.groups:
            track = self.direct_joins(track, self.direct_swaps(track, group), group)
        return track.reshape(lead, -1, width)

    def fold(self, track, index):
        away, home = self.one(track, {index: True}), self.one(track, {index: False})
        return home, self.swap(away, self.bits[index])

    def sum_line(self, parts):
        return [self.shift(parts[s], -s) for s in range(1, self.n_z)]

    def step_line(self, right, left):
        n = self.n_z
        return (
            lax.ppermute(right, "tensor", [(i, i + 1) for i in range(n - 1)]),
            lax.ppermute(left, "tensor", [(i + 1, i) for i in range(n - 1)]),
        )


def on_device(
    n_dp,
    n_z,
    tokens,
    lengths,
    key_mask,
    query_weight,
    query_bias,
    key_weight,
    value_weight,
    value_bias,
    output_weight,
    output_bias,
    first_gain,
    first_shift,
    inner_weight,
    inner_bias,
    outer_weight,
    outer_bias,
    second_gain,
    second_shift,
    cotangent,
):
    width = tokens.shape[1]
    mine = query_weight.shape[1]
    units = inner_weight.shape[1]
    all_rows = tokens.shape[0]
    all_blocks = all_rows // BUCKET
    rows = all_rows // n_z
    plane = Plane(n_dp, n_z)
    dp, z, core = plane.dp, plane.z, plane.core
    others = range(1, n_z)
    place = z.reshape(1)

    feed_rows = units // n_dp
    mixer_rows = mine // n_dp
    spot = core * (n_dp // 2) + (dp >> 1)
    outer_start = spot * feed_rows
    bias_row = jnp.concatenate([query_bias, value_bias, inner_bias])
    piece = jnp.concatenate(
        [
            lax.dynamic_slice_in_dim(inner_weight, outer_start, feed_rows, 1).T,
            lax.dynamic_slice_in_dim(outer_weight, outer_start, feed_rows, 0),
        ],
        axis=1,
    )
    extra = lax.dynamic_slice_in_dim(output_weight, spot * mixer_rows, mixer_rows, 0)
    extra = jnp.pad(extra, ((0, mixer_rows % 2), (0, 0))).reshape(-1, 2 * width)
    mixer_pairs = extra.shape[0]
    bias_line = jnp.pad(bias_row, (0, 2 * width - bias_row.shape[0]))[None]
    piece = jnp.concatenate([piece, extra, bias_line], axis=0)
    piece = jnp.pad(piece, ((0, -piece.shape[0] % 16), (0, 0)))
    line = [plane.shift(piece, s) for s in others]

    query_t, key_t, value_t = query_weight.T, key_weight.T, value_weight.T
    key_mask_rows = key_mask.reshape(all_blocks, 1, BUCKET)
    mixed_all = attend_forward(
        lengths, tokens, query_t, key_t, value_t, jnp.stack([query_bias, value_bias]),
        key_mask_rows,
    )
    mixed_all, line = together(mixed_all, line)

    def block(matrix, number):
        return lax.dynamic_slice_in_dim(matrix, number * rows, rows, 0)

    remote = jnp.stack(line)
    biases = jnp.concatenate(
        [bias_row[None], remote[:, feed_rows + mixer_pairs, : bias_row.shape[0]]], axis=0
    ).astype(f32)
    count = piece.shape[0]
    tracks = [plane.open_bits(remote[:, :, i * width : (i + 1) * width]) for i in range(2)]
    mixed_line = [plane.shift(block(mixed_all, lax.rem(z + s, n_z)), s) for s in others]
    for number in range(len(plane.bits)):
        swaps = plane.grow_swaps(tracks, number)
        if number == len(plane.bits) - 1:
            swaps, mixed_line = together(swaps, mixed_line)
        tracks = plane.grow_joins(tracks, swaps, number)
    tracks = [track.reshape(n_z - 1, -1, count, width) for track in tracks]

    mixer_half = jnp.stack(
        [track[:, :, feed_rows : feed_rows + mixer_pairs] for track in tracks], axis=3
    )
    mixer_half = mixer_half.reshape(n_z - 1, n_dp // 2, 2 * mixer_pairs, width)[:, :, :mixer_rows]
    mixer_half = mixer_half.reshape(n_z - 1, 1, -1, width)
    mixer_remote = plane.join(mixer_half, plane.swap(mixer_half, 1), 1, 1)
    mixer = jnp.concatenate(
        [output_weight, mixer_remote.reshape(-1, width)], axis=0
    )
    own_half = [
        lax.dynamic_slice_in_dim(inner_weight, core * (units // 2), units // 2, 1).T,
        lax.dynamic_slice_in_dim(outer_weight, core * (units // 2), units // 2, 0),
    ]
    feed_keep = jnp.stack(
        [
            jnp.concatenate(
                [own[None], track[:, :, :feed_rows].reshape(n_z - 1, -1, width)], axis=0
            )
            for own, track in zip(own_half, tracks)
        ]
    )
    feed_send = plane.swap(feed_keep, 1)
    mixed_rows = jnp.concatenate([block(mixed_all, z)] + mixed_line, axis=1)

    head_biases = jnp.stack(
        [biases[:, :mine].reshape(-1), biases[:, mine : 2 * mine].reshape(-1)]
        + [jnp.zeros((width,), f32)] * 6
    )
    inner_bias_all = biases[:, 2 * mine : 2 * mine + units].reshape(n_z, 2, units // 2)
    bias_keep = lax.dynamic_slice_in_dim(inner_bias_all, core, 1, 1)
    bias_send = lax.dynamic_slice_in_dim(inner_bias_all, 1 - core, 1, 1)
    vectors = jnp.stack(
        [output_bias, first_gain, first_shift, outer_bias, second_gain, second_shift]
        + [jnp.zeros_like(output_bias)] * 2
    ).astype(f32)

    attention_own = jnp.concatenate([query_t, key_t, value_t], axis=1)
    attention_piece = lax.dynamic_slice_in_dim(attention_own, spot * mixer_rows, mixer_rows, 0)
    mixed_rows, attention_piece = together(mixed_rows, attention_piece)
    attention_line = [plane.shift(attention_piece, s) for s in others]

    hidden_keep, slope_keep, normed_low, first_normed, first_scale, second_start = feed_first(
        place, mixed_rows, mixer, tokens, vectors, feed_keep, bias_keep
    )
    second_start, feed_send, attention_line = together(second_start, feed_send, attention_line)
    attention_half = plane.open_bits(jnp.stack(attention_line))
    for group in plane.groups[:-1]:
        attention_half = plane.direct_joins(
            attention_half, plane.direct_swaps(attention_half, group), group
        )
    attention_swaps = plane.direct_swaps(attention_half, plane.groups[-1])

    hidden_send, slope_send, my_output, grad_second, grad_outer, second_sums = feed_second(
        place, lengths, normed_low, second_start, cotangent, vectors, feed_send, bias_send
    )
    output = lax.all_gather(my_output, "tensor", axis=0, tiled=True)
    grad_outer, attention_swaps = together(grad_outer, attention_swaps)
    attention_half = plane.direct_joins(attention_half, attention_swaps, plane.groups[-1])
    attention_half = attention_half.reshape(n_z - 1, 1, -1, 3 * width)
    attention_other = plane.swap(attention_half, 1)

    feed_grad_send, bias_grad_send, grad_normed = feed_back(
        grad_outer, normed_low, hidden_send, slope_send, feed_send, grad_second
    )
    grad_normed, attention_other = together(grad_normed, attention_other)
    attention_remote = plane.join(attention_half, attention_other, 1, 1).reshape(-1, 3 * width)
    feed_grad_other = plane.swap(feed_grad_send, 1)
    feed_grad_keep, bias_grad_keep, grad_first, grad_attended, first_sums = feed_back(
        grad_outer, normed_low, hidden_keep, slope_keep, feed_keep, grad_normed,
        (first_normed, first_scale, vectors),
    )
    grad_first, grad_attended, feed_grad_other, attention_remote = together(
        grad_first, grad_attended, feed_grad_other, attention_remote
    )
    inner_bias_grad = plane.join(bias_grad_keep, bias_grad_send, 1, 1).reshape(n_z, units)
    feed_sum = add(feed_grad_keep, feed_grad_other)
    tracks = [plane.by_bits(feed_sum[i]) for i in range(2)]

    def step(number):
        return [
            plane.fold(track, order[number]) for track, order in zip(tracks, plane.orders)
        ]

    folded = step(0)
    attention_back, my_tokens_grad, back_sums = attend_back(
        place, lengths, tokens, grad_attended, grad_first, attention_own, attention_remote, mixer,
        head_biases, key_mask_rows,
    )
    attention_back, folded = together(attention_back, folded)
    tracks = [add(*pair) for pair in folded]
    for number in range(1, len(plane.bits)):
        folded = step(number)
        if number < len(plane.bits) - 1:
            tracks = [add(*pair) for pair in folded]

    pair = jnp.arange(2, dtype=jnp.int32)

    def weight_grads(side):
        order = jnp.concatenate([pair + 2 * side, place])
        return attention_grads(order, attention_back, mixed_rows, tokens, grad_attended)

    right, left = plane.step_line(my_tokens_grad, my_tokens_grad)
    grads_send = weight_grads(1 - core)

    back_sums = jnp.sum(back_sums, axis=0)
    split = jnp.concatenate(
        [inner_bias_grad, back_sums[0].reshape(n_z, mine), back_sums[1].reshape(n_z, mine)], axis=1
    )
    small = jnp.concatenate([first_sums[:3], second_sums[:3], split.reshape(-1, width)], axis=0)
    small = jnp.pad(small, ((0, -small.shape[0] % 16), (0, 0))).astype(bf16)
    small_rows = small.shape[0]

    grads_send, folded, small, output = together(grads_send, folded, small, output)
    grads_other = plane.swap(grads_send, 1)
    small_other = plane.swap(small, 1)
    tracks = [add(*pair) for pair in folded]
    feed_parts = jnp.concatenate([t.reshape(n_z, -1, width) for t in tracks], axis=2)
    feed_line = plane.sum_line(feed_parts)
    grads_keep = weight_grads(core)
    grads_keep, grads_other, small_other, right, left = together(
        grads_keep, grads_other, small_other, right, left
    )
    line_steps = [(right, left)]
    grads_sum = add(grads_keep, grads_other).reshape(2 * n_z, mine, width)
    grads_sum = plane.by_bits(grads_sum)
    small = add(small, small_other)
    for group in plane.groups:
        home = plane.one(grads_sum, {index: False for index in group})
        arrived = []
        for chosen, mask in plane.flips(group):
            away = plane.one(grads_sum, chosen).reshape(-1, width)
            arrived.append(plane.swap(jnp.concatenate([away, small], axis=0), mask))
        if group is plane.groups[-1]:
            arrived, feed_line = together(arrived, feed_line)
        grads_sum = add(home, *[a[:-small_rows].reshape(home.shape) for a in arrived])
        small = add(small, *[a[-small_rows:] for a in arrived])
    attention_parts = grads_sum.reshape(2, n_z, -1, width)

    def for_line(s):
        return jnp.concatenate([attention_parts[:, s].reshape(-1, width), small], axis=0)

    attention_line = plane.sum_line([for_line(s) for s in range(n_z)])
    right, left = plane.step_line(right, left)
    line_steps.append((right, left))
    feed_total = add(feed_parts[0], *feed_line)
    feed_half = plane.grow_direct(feed_total[None])
    attention_line, feed_half = together(attention_line, feed_half)
    attention_total = add(
        attention_parts[:, 0],
        *[a[:-small_rows].reshape(attention_parts[:, 0].shape) for a in attention_line],
    )
    attention_half = plane.grow_direct(attention_total)
    feed_other = plane.swap(feed_half, 1)
    attention_half, feed_other, right, left = together(attention_half, feed_other, right, left)
    for _ in range(n_z - 3):
        right, left = plane.step_line(right, left)
        line_steps.append((right, left))
    feed_grad = plane.join(feed_half, feed_other, 1, 1)[0]
    grad_list = plane.join(attention_half, plane.swap(attention_half, 1), 1, 0)

    smalls = [small.astype(f32)] + [a[-small_rows:].astype(f32) for a in attention_line]
    shared = sum(a[:6] for a in smalls)
    n_split = split.shape[1]
    split = sum(
        a[6:].reshape(-1)[s * n_split : (s + 1) * n_split] for s, a in enumerate(smalls)
    )

    tokens_grad = jnp.zeros((all_rows, width), bf16)
    tokens_grad = lax.dynamic_update_slice_in_dim(tokens_grad, my_tokens_grad, z * rows, 0)
    for s in others:
        came = jnp.where(z >= s, line_steps[s - 1][0], line_steps[n_z - 1 - s][1])
        there = lax.rem(z + n_z - s, n_z) * rows
        tokens_grad = lax.dynamic_update_slice_in_dim(tokens_grad, came, there, 0)

    return (
        output,
        tokens_grad,
        grad_list[0].T.astype(f32),
        split[units : units + mine],
        grad_list[1].T.astype(f32),
        grad_list[2].T.astype(f32),
        split[units + mine :],
        grad_list[3].astype(f32),
        shared[0],
        shared[1],
        shared[2],
        feed_grad[:, :width].T.astype(f32),
        split[:units],
        feed_grad[:, width:].astype(f32),
        shared[3],
        shared[4],
        shared[5],
    )


def solution(mesh):
    n_dp, n_z = mesh.shape["dp"], mesh.shape["tensor"]
    in_specs = (
        P("dp", None),
        P("dp", None),
        P("dp"),
        P(None, "tensor"),
        P("tensor"),
        P(None, "tensor"),
        P(None, "tensor"),
        P("tensor"),
        P("tensor", None),
        P(),
        P(),
        P(),
        P(None, "tensor"),
        P("tensor"),
        P("tensor", None),
        P(),
        P(),
        P(),
        P("dp", None),
    )
    out_specs = (
        P("dp", None),
        P("dp", None),
        P(None, "tensor"),
        P("tensor"),
        P(None, "tensor"),
        P(None, "tensor"),
        P("tensor"),
        P("tensor", None),
        P(),
        P(),
        P(),
        P(None, "tensor"),
        P("tensor"),
        P("tensor", None),
        P(),
        P(),
        P(),
    )

    def program(*args):
        return on_device(n_dp, n_z, *args)

    return jax.shard_map(
        program, mesh=mesh, in_specs=in_specs, out_specs=out_specs, check_vma=False
    )
```

```python
import functools

import jax
import jax.numpy as jnp
from jax import lax
from jax.experimental import pallas as pl
from jax.experimental.pallas import tpu as pltpu
from jax.sharding import PartitionSpec as P

HEAD = 64
BUCKET = 512
ITEMS = 8


negative_fill = -1e30
epsilon = 1e-06
f32 = jnp.float32
bf16 = jnp.bfloat16
VMEM_BYTES = 56 * 1024 * 1024


def dot(left, right):
    return jnp.dot(left, right, preferred_element_type=f32)


def contract_rows(left, right):
    return lax.dot_general(left, right, (((0,), (0,)), ((), ())), preferred_element_type=f32)


def contract_cols(left, right):
    return lax.dot_general(left, right, (((1,), (1,)), ((), ())), preferred_element_type=f32)


def norm_rows(values):
    centred = values - jnp.mean(values, axis=1, keepdims=True)
    inv_scale = lax.rsqrt(jnp.mean(centred * centred, axis=1, keepdims=True) + epsilon)
    return centred * inv_scale, inv_scale


def norm_back(grad_rows, norm_gain, normed, inv_scale):
    scaled = grad_rows * norm_gain
    return inv_scale * (
        scaled
        - jnp.mean(scaled, axis=1, keepdims=True)
        - normed * jnp.mean(scaled * normed, axis=1, keepdims=True)
    )


def column_sum(matrix):
    return jnp.sum(matrix.astype(f32), axis=0, keepdims=True)


def fixed(shape):
    return pl.BlockSpec(shape, lambda *_: (0,) * len(shape))


def cost(microseconds):
    return pl.CostEstimate(
        flops=int(microseconds * 1.0e9), bytes_accessed=int(microseconds * 1.0e6), transcendentals=0
    )


def params(axes):
    return pltpu.CompilerParams(
        dimension_semantics=("arbitrary",) * axes, vmem_limit_bytes=VMEM_BYTES
    )


def item_places(lengths_ref, row, shape, axis):
    places = lax.broadcasted_iota(jnp.int32, shape, axis)
    end = jnp.int32(0)
    items = jnp.zeros(shape, jnp.int32)
    for slot in range(ITEMS):
        end = end + lengths_ref[row, slot]
        items = items + (places >= end).astype(jnp.int32)
    return items


def as_column(row):
    return jnp.broadcast_to(row.astype(f32), (8, row.shape[1])).T[:, :1]


def mask_bias(lengths_ref, row, key_mask):
    shape = (BUCKET, BUCKET)
    diagonal = lax.broadcasted_iota(jnp.int32, shape, 0) == lax.broadcasted_iota(
        jnp.int32, shape, 1
    )
    item_row = item_places(lengths_ref, row, (1, BUCKET), 1)
    item_column = item_places(lengths_ref, row, (BUCKET, 1), 0)
    code_column = jnp.where(as_column(key_mask) == 1.0, item_column, -1)
    return jnp.where((code_column == item_row) | diagonal, 0.0, negative_fill).astype(f32)


def attend_forward_kernel(
    lengths_ref, tokens_ref, query_ref, key_ref, value_ref, biases_ref, key_mask_ref, mixed_ref,
):
    rows = tokens_ref[...]
    queries = contract_cols(query_ref[...], rows) + as_column(biases_ref[0:1, :])
    queries = (queries.astype(bf16) * HEAD ** (-0.5)).astype(bf16)
    keys = contract_cols(rows, key_ref[...]).astype(bf16)
    values = (contract_cols(value_ref[...], rows) + as_column(biases_ref[1:2, :])).astype(bf16)
    bias = mask_bias(lengths_ref, pl.program_id(0), key_mask_ref[0])
    parts = []
    for head in range(queries.shape[0] // HEAD):
        at = slice(head * HEAD, (head + 1) * HEAD)
        scores = dot(keys[:, at], queries[at]) + bias
        exponent = jnp.exp(scores - jnp.max(scores, axis=0, keepdims=True))
        total = jnp.sum(exponent, axis=0, keepdims=True)
        parts.append(dot(values[at], exponent.astype(bf16)) / total)
    mixed_ref[...] = jnp.concatenate(parts, axis=0).T.astype(bf16)


def attend_forward(lengths, tokens, query, key, value, biases, key_mask):
    blocks = lengths.shape[0]
    mine, width = key.shape
    return pl.pallas_call(
        attend_forward_kernel,
        grid=(blocks,),
        in_specs=[
            pl.BlockSpec(memory_space=pltpu.SMEM),
            pl.BlockSpec((BUCKET, width), lambda b: (b, 0)),
            fixed((mine, width)),
            fixed((mine, width)),
            fixed((mine, width)),
            fixed((2, mine)),
            pl.BlockSpec((1, 1, BUCKET), lambda b: (b, 0, 0)),
        ],
        out_specs=pl.BlockSpec((BUCKET, mine), lambda b: (b, 0)),
        out_shape=jax.ShapeDtypeStruct((blocks * BUCKET, mine), bf16),
        compiler_params=params(1),
        name="attend_forward",
        cost_estimate=cost(12),
    )(lengths, tokens, query, key, value, biases, key_mask)


def feed_weights(weights_ref, feed_rows):
    block = weights_ref[:, 0, :feed_rows, :]
    block = block.reshape(block.shape[0] * feed_rows, block.shape[2])
    width = block.shape[1] // 2
    return block[:, :width], block[:, width:]


def feed_forward_kernel(
    feed_rows, info_ref, lengths_ref, mixed_ref, mixer_ref, tokens_ref, cotangent_ref, vectors_ref,
    weights_ref, bias_ref,
    hidden_ref, slope_ref, output_ref, normed_low_ref, first_normed_ref, first_scale_ref,
    grad_second_ref, grad_outer_ref, sums_ref,
    second_sum,
):
    output_bias, first_gain, first_shift, outer_bias, second_gain, second_shift = (
        vectors_ref[i : i + 1, :] for i in range(6)
    )

    @pl.when(pl.program_id(0) == 0)
    def _():
        attended = output_bias + sum(
            dot(mixed_ref[t], mixer_ref[t]) for t in range(mixed_ref.shape[0])
        )
        normed, inv_scale = norm_rows(tokens_ref[...].astype(f32) + attended)
        whole = normed * first_gain + first_shift
        first_normed_ref[...] = normed
        first_scale_ref[...] = inv_scale
        normed_low_ref[...] = whole.astype(bf16)
        second_sum[...] = whole + outer_bias

    inner, outer = feed_weights(weights_ref, feed_rows)
    inner_pre = contract_cols(normed_low_ref[...], inner) + bias_ref[0]
    normal_cdf = 0.5 + 0.5 * lax.erf(inner_pre * 0.7071067811865476)
    density = jnp.exp(-0.5 * inner_pre * inner_pre) * 0.3989422804014327
    hidden = (inner_pre * normal_cdf).astype(bf16)
    hidden_ref[...] = hidden
    slope_ref[...] = (normal_cdf + inner_pre * density).astype(bf16)
    second_sum[...] += dot(hidden, outer)

    @pl.when(pl.program_id(0) == pl.num_programs(0) - 1)
    def _():
        normed, inv_scale = norm_rows(second_sum[...])
        blocks = normed.shape[0] // BUCKET
        live = jnp.concatenate(
            [
                (item_places(lengths_ref, info_ref[0] * blocks + b, (BUCKET, 1), 0) < ITEMS)
                for b in range(blocks)
            ],
            axis=0,
        ).astype(f32)
        output_ref[...] = ((normed * second_gain + second_shift) * live).astype(bf16)
        grad_final = cotangent_ref[...].astype(f32) * live
        grad_second = norm_back(grad_final, second_gain, normed, inv_scale)
        grad_outer = grad_second.astype(bf16)
        grad_second_ref[...] = grad_second
        grad_outer_ref[...] = grad_outer
        sums_ref[0:1, :] = column_sum(grad_outer)
        sums_ref[1:2, :] = column_sum(grad_final * normed)
        sums_ref[2:3, :] = column_sum(grad_final)


def feed_forward(
    feed_rows, info, lengths, mixed, mixer, tokens, cotangent, vectors, weights, biases
):
    n_z, rows, mine = mixed.shape
    n_z, chunks, piece, twice = weights.shape
    width = twice // 2
    chunk = n_z * feed_rows
    whole = fixed((rows, width))
    own = pl.BlockSpec((rows, width), lambda j, info: (info[0], 0))
    columns = pl.BlockSpec((rows, chunk), lambda j, info: (0, j))
    shapes = [
        ((rows, chunks * chunk), bf16, columns),
        ((rows, chunks * chunk), bf16, columns),
        ((rows, width), bf16, whole),
        ((rows, width), bf16, whole),
        ((rows, width), f32, whole),
        ((rows, 1), f32, fixed((rows, 1))),
        ((rows, width), f32, whole),
        ((rows, width), bf16, whole),
        ((8, width), f32, fixed((8, width))),
    ]
    return pl.pallas_call(
        functools.partial(feed_forward_kernel, feed_rows),
        grid_spec=pltpu.PrefetchScalarGridSpec(
            num_scalar_prefetch=1,
            grid=(chunks,),
            in_specs=[
                pl.BlockSpec(memory_space=pltpu.SMEM),
                fixed((n_z, rows, mine)),
                fixed((n_z, mine, width)),
                own,
                own,
                fixed((8, width)),
                pl.BlockSpec((n_z, 1, piece, twice), lambda j, info: (0, j, 0, 0)),
                pl.BlockSpec((1, 1, chunk), lambda j, info: (j, 0, 0)),
            ],
            out_specs=[spec for _, _, spec in shapes],
            scratch_shapes=[pltpu.VMEM((rows, width), f32)],
        ),
        out_shape=[jax.ShapeDtypeStruct(shape, kind) for shape, kind, _ in shapes],
        compiler_params=params(1),
        name="feed_forward",
        cost_estimate=cost(21),
    )(info, lengths, mixed, mixer, tokens, cotangent, vectors, weights, biases)


def feed_back_kernel(
    feed_rows, count, adds, last, info_ref, grad_outer_ref, normed_low_ref, hidden_ref, slope_ref,
    weights_ref, start_ref, *rest,
):
    other_ref, rest = (rest[0], rest[1:]) if adds else (None, rest)
    norm_refs, rest = (rest[:3], rest[3:]) if last else (None, rest)
    grad_refs, rest = (rest[:count], rest[count:]) if adds else (rest[:1], rest[1:])
    bias_grad_ref, rest = rest[0], rest[1:]
    if last:
        grad_first_ref, grad_attended_ref, sums_ref, grad_normed_ref = rest
    else:
        (grad_normed_ref,) = rest
    step = pl.program_id(0)

    @pl.when(step == 0)
    def _():
        grad_normed_ref[...] = start_ref[...]

    inner, outer = feed_weights(weights_ref, feed_rows)
    n_z = weights_ref.shape[0]
    width = inner.shape[1]
    grad_outer = grad_outer_ref[...]
    grad_hidden = contract_cols(grad_outer, outer)
    grad_inner = (grad_hidden * slope_ref[...].astype(f32)).astype(bf16)
    outer_grad = contract_rows(hidden_ref[...], grad_outer)
    inner_grad = contract_rows(grad_inner, normed_low_ref[...])
    bias_grad_ref[0] = column_sum(grad_inner)
    grad_normed_ref[...] += dot(grad_inner, inner)

    def store(ref, lead):
        for t in range(n_z):
            s = lax.rem(t - info_ref[0] + n_z, n_z)
            at = slice(t * feed_rows, (t + 1) * feed_rows)
            both = ((inner_grad[at], slice(0, width)), (outer_grad[at], slice(width, 2 * width)))
            for value, columns in both:
                if adds:
                    value = value + other_ref[0, s, :, columns].astype(f32)
                ref[lead + (s, slice(None), columns)] = value.astype(bf16)

    if adds:
        for number in range(count):

            @pl.when(step == number)
            def _(number=number):
                store(grad_refs[number], ())

    else:
        store(grad_refs[0], (0,))

    if last:

        @pl.when(step == pl.num_programs(0) - 1)
        def _():
            first_normed_ref, first_scale_ref, vectors_ref = norm_refs
            grad_rows, normed = grad_normed_ref[...], first_normed_ref[...]
            grad_first = norm_back(grad_rows, vectors_ref[1:2, :], normed, first_scale_ref[...])
            grad_attended = grad_first.astype(bf16)
            grad_first_ref[...] = grad_first
            grad_attended_ref[...] = grad_attended
            sums_ref[0:1, :] = column_sum(grad_attended)
            sums_ref[1:2, :] = column_sum(grad_rows * normed)
            sums_ref[2:3, :] = column_sum(grad_rows)


def feed_back(
    feed_rows, count, info, grad_outer, normed_low, hidden, slope, weights, start,
    other=None, norm=None,
):
    rows, width = grad_outer.shape
    n_z, _, piece, twice = weights.shape
    chunk = n_z * feed_rows
    device = lambda i, info: (info[1] ^ (info[2] + i)) * 2 + info[3]
    columns = pl.BlockSpec((rows, chunk), lambda i, info: (0, device(i, info)))
    whole = fixed((rows, width))
    part = (n_z, feed_rows, twice)
    one = pl.BlockSpec((1,) + part, lambda i, info: (i, 0, 0, 0))
    in_specs = [
        whole,
        whole,
        columns,
        columns,
        pl.BlockSpec((n_z, 1, piece, twice), lambda i, info: (0, device(i, info), 0, 0)),
        whole,
    ]
    args = [grad_outer, normed_low, hidden, slope, weights, start]
    scratch = []
    if other is None:
        shapes = [((count,) + part, bf16, one)]
    else:
        in_specs.append(one)
        args.append(other)
        shapes = [(part, bf16, fixed(part))] * count
    shapes.append(((count, 1, chunk), f32, pl.BlockSpec((1, 1, chunk), lambda i, info: (i, 0, 0))))
    if norm is None:
        shapes.append(((rows, width), f32, whole))
    else:
        in_specs += [whole, fixed((rows, 1)), fixed((8, width))]
        args += list(norm)
        shapes += [
            ((rows, width), f32, whole),
            ((rows, width), bf16, whole),
            ((8, width), f32, fixed((8, width))),
        ]
        scratch = [pltpu.VMEM((rows, width), f32)]
    return pl.pallas_call(
        functools.partial(
            feed_back_kernel, feed_rows, count, other is not None, norm is not None
        ),
        grid_spec=pltpu.PrefetchScalarGridSpec(
            num_scalar_prefetch=1,
            grid=(count,),
            in_specs=in_specs,
            out_specs=[spec for _, _, spec in shapes],
            scratch_shapes=scratch,
        ),
        out_shape=[jax.ShapeDtypeStruct(shape, kind) for shape, kind, _ in shapes],
        compiler_params=params(1),
        name="feed_back" if norm is None else "feed_back_norm",
        cost_estimate=cost(6),
    )(info, *args)


def attend_back_kernel(
    place_ref, lengths_ref, tokens_ref, grad_attended_ref, grad_first_ref, weights_ref, mixer_ref,
    biases_ref, key_mask_ref,
    grads_ref, tokens_grad_ref, sums_ref,
    bias, total_grad,
):
    pair = pl.program_id(1)

    @pl.when(pair == 0)
    def _():
        row = place_ref[0] * pl.num_programs(0) + pl.program_id(0)
        bias[...] = mask_bias(lengths_ref, row, key_mask_ref[0])
        total_grad[...] = grad_first_ref[...]

    rows, grad_attended = tokens_ref[...], grad_attended_ref[...]
    width = rows.shape[1]
    query_w, key_w, value_w = (
        weights_ref[:, i * width : (i + 1) * width] for i in range(3)
    )
    queries = contract_cols(query_w, rows) + as_column(biases_ref[0:1, :])
    queries = (queries.astype(bf16) * HEAD ** (-0.5)).astype(bf16)
    keys = contract_cols(rows, key_w).astype(bf16)
    values = (contract_cols(rows, value_w) + biases_ref[1:2, :]).astype(bf16)
    grad_mixed = contract_cols(mixer_ref[...], grad_attended).astype(bf16)
    keys_t = keys.T
    grad_queries, grad_keys, grad_values = [], [], []
    for head in range(keys.shape[1] // HEAD):
        at = slice(head * HEAD, (head + 1) * HEAD)
        scores = dot(keys[:, at], queries[at]) + bias[...]
        exponent = jnp.exp(scores - jnp.max(scores, axis=0, keepdims=True))
        probs = exponent * (1.0 / jnp.sum(exponent, axis=0, keepdims=True))
        grad_probs = dot(values[:, at], grad_mixed[at])
        shift = jnp.sum(probs * grad_probs, axis=0, keepdims=True)
        grad_scores = (probs * (grad_probs - shift)).astype(bf16)
        grad_values.append(contract_cols(probs.astype(bf16), grad_mixed[at]))
        grad_keys.append(contract_cols(grad_scores, queries[at]))
        grad_queries.append(dot(keys_t[at], grad_scores) * HEAD ** (-0.5))
    grad_query = jnp.concatenate(grad_queries, axis=0).T.astype(bf16)
    grad_key = jnp.concatenate(grad_keys, axis=1).astype(bf16)
    grad_value = jnp.concatenate(grad_values, axis=1).astype(bf16)
    grads_ref[0] = grad_query
    grads_ref[1] = grad_key
    grads_ref[2] = grad_value
    sums_ref[0, 0:1, :] = column_sum(grad_query)
    sums_ref[0, 1:2, :] = column_sum(grad_value)
    total_grad[...] += dot(grad_query, query_w) + dot(grad_key, key_w) + dot(grad_value, value_w)

    @pl.when(pair == pl.num_programs(1) - 1)
    def _():
        tokens_grad_ref[...] = total_grad[...].astype(bf16)


def attend_back(
    place, lengths, tokens, grad_attended, grad_first, weights, mixer, biases, key_mask
):
    rows, width = grad_attended.shape
    blocks = rows // BUCKET
    pair = 2 * HEAD
    own = lambda b, h, place: (place[0] * blocks + b, 0)
    by_bucket = pl.BlockSpec((BUCKET, width), lambda b, h, place: (b, 0))
    by_pair = lambda b, h, place: (h, 0)
    return pl.pallas_call(
        attend_back_kernel,
        grid_spec=pltpu.PrefetchScalarGridSpec(
            num_scalar_prefetch=1,
            grid=(blocks, width // pair),
            in_specs=[
                pl.BlockSpec(memory_space=pltpu.SMEM),
                pl.BlockSpec((BUCKET, width), own),
                by_bucket,
                by_bucket,
                pl.BlockSpec((pair, 3 * width), by_pair),
                pl.BlockSpec((pair, width), by_pair),
                pl.BlockSpec((8, pair), lambda b, h, place: (0, h)),
                pl.BlockSpec((1, 1, BUCKET), lambda b, h, place: (place[0] * blocks + b, 0, 0)),
            ],
            out_specs=[
                pl.BlockSpec((3, BUCKET, pair), lambda b, h, place: (0, b, h)),
                by_bucket,
                pl.BlockSpec((1, 8, pair), lambda b, h, place: (b, 0, h)),
            ],
            scratch_shapes=[pltpu.VMEM((BUCKET, BUCKET), f32), pltpu.VMEM((BUCKET, width), f32)],
        ),
        out_shape=[
            jax.ShapeDtypeStruct((3, rows, width), bf16),
            jax.ShapeDtypeStruct((rows, width), bf16),
            jax.ShapeDtypeStruct((blocks, 8, width), f32),
        ],
        compiler_params=params(2),
        name="attend_back",
        cost_estimate=cost(26),
    )(
        place, lengths, tokens, grad_attended, grad_first, weights, mixer, biases, key_mask
    )


def attention_grads_kernel(
    n_places, adds, info_ref, grads_ref, mixed_ref, tokens_ref, grad_attended_ref, *rest
):
    if adds:
        other_ref, small_ref = rest[:2]
        out_refs, whole = rest[2:-1], rest[-1]
    else:
        (out_ref, whole) = rest
    step = pl.program_id(0)
    which = info_ref[step]
    n_z, _, mine = mixed_ref.shape
    count = mine // n_places

    @pl.when(which < 3)
    def _():
        whole[...] = contract_rows(grads_ref[0], tokens_ref[...]).astype(bf16)

    @pl.when(which == 3)
    def _():
        for t in range(n_z):
            whole[t * mine : (t + 1) * mine, :] = contract_rows(
                mixed_ref[t], grad_attended_ref[...]
            ).astype(bf16)

    for number in range(n_places):
        for s in range(n_z):
            start = lax.rem(info_ref[2] + s, n_z) * mine + (info_ref[3] ^ number) * count
            value = whole[pl.ds(pl.multiple_of(start, 16), count), :]
            if adds:
                value = value.astype(f32) + other_ref[number, s, 0].astype(f32)
                row = (2 * s + step) * count
                out_refs[number][pl.ds(pl.multiple_of(row, 16), count), :] = value.astype(bf16)
            else:
                out_ref[number, s, 0] = value

    if adds:
        for number in range(n_places):
            out_refs[number][2 * n_z * count :, :] = small_ref[...]


def attention_grads(n_places, info, grads, mixed, tokens, grad_attended, other=None, small=None):
    rows, width = grad_attended.shape
    n_z, _, mine = mixed.shape
    count = mine // n_places
    parts = (n_places, n_z, 1, count, width)
    by_step = pl.BlockSpec(parts, lambda i, info: (0, 0, i, 0, 0))
    in_specs = [
        pl.BlockSpec((1, rows, width), lambda i, info: (jnp.minimum(info[i], 2), 0, 0)),
        fixed((n_z, rows, mine)),
        pl.BlockSpec((rows, width), lambda i, info: (info[2], 0)),
        fixed((rows, width)),
    ]
    args = [grads, mixed, tokens, grad_attended]
    if other is None:
        shapes = [((n_places, n_z, 2, count, width), by_step)]
    else:
        in_specs += [by_step, fixed(small.shape)]
        args += [other, small]
        flat = (2 * n_z * count + small.shape[0], width)
        shapes = [(flat, fixed(flat))] * n_places
    return pl.pallas_call(
        functools.partial(attention_grads_kernel, n_places, other is not None),
        grid_spec=pltpu.PrefetchScalarGridSpec(
            num_scalar_prefetch=1,
            grid=(2,),
            in_specs=in_specs,
            out_specs=[spec for _, spec in shapes],
            scratch_shapes=[pltpu.VMEM((width, width), bf16)],
        ),
        out_shape=[jax.ShapeDtypeStruct(shape, bf16) for shape, _ in shapes],
        compiler_params=params(1),
        name="attention_grads",
        cost_estimate=cost(6),
    )(info, *args)


def together(*values):
    return lax.optimization_barrier(values)


def add(first, *others):
    total = first.astype(f32)
    for other in others:
        total = total + other.astype(f32)
    return total.astype(bf16)


class Plane:
    def __init__(self, n_dp, n_z):
        self.n_dp, self.n_z = n_dp, n_z
        self.n_group = min(n_dp, 8)
        self.n_places = self.n_group // 2
        self.dp = lax.axis_index("dp")
        self.z = lax.axis_index("tensor")
        self.index = lax.rem(self.dp, self.n_group)
        self.core = self.index & 1
        self.place = self.index >> 1

    def swap(self, array, bits):
        return lax.ppermute(array, "dp", [(i, i ^ bits) for i in range(self.n_dp)])

    def shift(self, array, by):
        n = self.n_z
        return lax.ppermute(array, "tensor", [(i, (i + by) % n) for i in range(n)])

    def gather(self, piece):
        if self.n_dp == self.n_group:
            whole = lax.all_gather(piece, ("tensor", "dp"))
            return whole.reshape((self.n_z, self.n_group) + piece.shape)
        groups = [
            list(range(i, i + self.n_group)) for i in range(0, self.n_dp, self.n_group)
        ]
        line = lax.all_gather(piece, "tensor")
        return lax.all_gather(line, "dp", axis=1, axis_index_groups=groups)

    def to_places(self, parts):
        return [self.swap(parts[number], 2 * number) for number in range(1, self.n_places)]

    def from_places(self, own, arrived):
        found = jnp.stack([own] + arrived)
        bit = 1
        while bit < self.n_places:
            lead = found.reshape((-1, 2, bit) + own.shape)
            flipped = lead[:, ::-1]
            found = jnp.where((self.place & bit) != 0, flipped, lead).reshape(found.shape)
            bit *= 2
        return found

    def by_core(self, own, other):
        return jnp.where(
            self.core == 1, jnp.stack([other, own]), jnp.stack([own, other])
        )

    def over_groups(self, array):
        bit = self.n_group
        while bit < self.n_dp:
            array = add(array, self.swap(array, bit))
            bit *= 2
        return array


def on_device(
    n_dp,
    n_z,
    tokens,
    lengths,
    key_mask,
    query_weight,
    query_bias,
    key_weight,
    value_weight,
    value_bias,
    output_weight,
    output_bias,
    first_gain,
    first_shift,
    inner_weight,
    inner_bias,
    outer_weight,
    outer_bias,
    second_gain,
    second_shift,
    cotangent,
):
    width = tokens.shape[1]
    mine = query_weight.shape[1]
    units = inner_weight.shape[1]
    all_rows = tokens.shape[0]
    all_blocks = all_rows // BUCKET
    rows = all_rows // n_z
    plane = Plane(n_dp, n_z)
    z, core, place, index = plane.z, plane.core, plane.place, plane.index
    n_places = plane.n_places
    others = range(1, n_z)

    feed_rows = units // plane.n_group
    head_rows = mine // plane.n_group
    piece = jnp.concatenate(
        [
            lax.dynamic_slice_in_dim(inner_weight, index * feed_rows, feed_rows, 1).T,
            lax.dynamic_slice_in_dim(outer_weight, index * feed_rows, feed_rows, 0),
        ],
        axis=1,
    )
    extra = lax.dynamic_slice_in_dim(output_weight, index * head_rows, head_rows, 0)
    extra = extra.reshape(head_rows // 2, 2 * width)
    piece = jnp.concatenate([piece, extra], axis=0)
    piece = jnp.pad(piece, ((0, -piece.shape[0] % 16), (0, 0)))
    weights = plane.gather(piece)

    bias_row = jnp.concatenate([query_bias, value_bias, inner_bias]).reshape(1, -1)
    bias_line = [bias_row] + [plane.shift(bias_row, s) for s in others]
    biases = jnp.concatenate(
        [
            sum(
                jnp.where(lax.rem(z - t + n_z, n_z) == s, bias_line[s], 0).astype(f32)
                for s in range(n_z)
            )
            for t in range(n_z)
        ],
        axis=0,
    )
    head_biases = jnp.pad(
        jnp.stack([biases[:, :mine].reshape(-1), biases[:, mine : 2 * mine].reshape(-1)]),
        ((0, 6), (0, 0)),
    )
    inner_biases = biases[:, 2 * mine :].reshape(n_z, plane.n_group, feed_rows)
    inner_biases = inner_biases.transpose(1, 0, 2).reshape(plane.n_group, 1, n_z * feed_rows)
    vectors = jnp.stack(
        [output_bias, first_gain, first_shift, outer_bias, second_gain, second_shift]
        + [jnp.zeros_like(output_bias)] * 2
    ).astype(f32)

    query_t, key_t, value_t = query_weight.T, key_weight.T, value_weight.T
    key_mask_rows = key_mask.reshape(all_blocks, 1, BUCKET)
    mixed = attend_forward(
        lengths, tokens, query_t, key_t, value_t, jnp.stack([query_bias, value_bias]),
        key_mask_rows,
    )
    mixed = lax.all_to_all(mixed.reshape(n_z, rows, mine), "tensor", 0, 0)

    attention_piece = lax.dynamic_slice_in_dim(
        jnp.concatenate([query_t, key_t, value_t], axis=1), index * head_rows, head_rows, 0
    )
    weights, attention_piece = together(weights, attention_piece)
    attention_weights = plane.gather(attention_piece).reshape(width, 3 * width)
    mixer = weights[:, :, feed_rows : feed_rows + head_rows // 2].reshape(n_z, mine, width)

    place_z = z.reshape(1)
    hidden, slope, my_output, normed_low, first_normed, first_scale, grad_second, grad_outer, second_sums = (
        feed_forward(
            feed_rows, place_z, lengths, mixed, mixer, tokens, cotangent, vectors, weights,
            inner_biases,
        )
    )
    output = lax.all_gather(my_output, "tensor", axis=0, tiled=True)

    def back(first, count, side, start, other=None, norm=None):
        info = jnp.stack([z, place, jnp.int32(first), side])
        return feed_back(
            feed_rows, count, info, grad_outer, normed_low, hidden, slope, weights, start, other,
            norm,
        )

    half = n_places // 2
    sent_a, bias_sent_a, grad_normed = back(0, half, 1 - core, grad_second)
    other_a = plane.swap(sent_a, 1)
    sent_b, bias_sent_b, grad_normed = back(half, half, 1 - core, grad_normed)
    grad_normed, other_a = together(grad_normed, other_a)
    other_b = plane.swap(sent_b, 1)
    *kept_a, bias_kept_a, grad_normed = back(0, half, core, grad_normed, other_a)
    grad_normed, other_b = together(grad_normed, other_b)
    *kept_b, bias_kept_b, grad_first, grad_attended, first_sums = back(
        half, half, core, grad_normed, other_b, (first_normed, first_scale, vectors)
    )
    feed_kept = kept_a + kept_b
    feed_arrived = plane.to_places(feed_kept)
    bias_grads = jnp.stack(
        [
            jnp.concatenate([bias_kept_a, bias_kept_b])[:, 0],
            jnp.concatenate([bias_sent_a, bias_sent_b])[:, 0],
        ],
        axis=1,
    )
    bit = 1
    flat = bias_grads.reshape(plane.n_group, -1)
    while bit < plane.n_group:
        lead = flat.reshape(-1, 2, bit, flat.shape[1])
        flat = jnp.where((index & bit) != 0, lead[:, ::-1], lead).reshape(flat.shape)
        bit *= 2
    inner_bias_grad = (
        flat.reshape(plane.n_group, n_z, feed_rows).transpose(1, 0, 2).reshape(n_z, units)
    )

    grads, my_tokens_grad, back_sums = attend_back(
        place_z, lengths, tokens, grad_attended, grad_first, attention_weights,
        mixer.reshape(width, width), head_biases, key_mask_rows,
    )
    tokens_grad = lax.all_gather(my_tokens_grad, "tensor", axis=0, tiled=True)

    back_sums = jnp.sum(back_sums, axis=0)
    split = jnp.concatenate(
        [inner_bias_grad, back_sums[0].reshape(n_z, mine), back_sums[1].reshape(n_z, mine)], axis=1
    )
    small = jnp.concatenate([first_sums[:3], second_sums[:3], split.reshape(-1, width)], axis=0)
    small = jnp.pad(small, ((0, -small.shape[0] % 16), (0, 0))).astype(bf16)
    small_rows = small.shape[0]

    def weight_grads(side, other=None, small=None):
        info = jnp.stack([2 * side, 2 * side + 1, z, place])
        return attention_grads(
            n_places, info, grads, mixed, tokens, grad_attended, other, small
        )

    (sent,) = weight_grads(1 - core)
    sent, small, feed_arrived, output = together(sent, small, feed_arrived, output)
    other = plane.swap(sent, 1)
    small = add(small, plane.swap(small, 1))
    feed_parts = [
        add(feed_kept[0][s], *[arrived[s] for arrived in feed_arrived]) for s in range(n_z)
    ]
    feed_line = [plane.shift(feed_parts[s], s) for s in others]
    kept = weight_grads(core, other, small)
    arrived = plane.to_places(kept)
    arrived, feed_line = together(arrived, feed_line)
    small = add(small, *[a[-small_rows:] for a in arrived])
    count = 2 * mine // n_places
    attention_parts = [
        add(*[a[s * count : (s + 1) * count] for a in [kept[0]] + arrived]) for s in range(n_z)
    ]
    attention_line = [
        plane.shift(jnp.concatenate([attention_parts[s], small], axis=0), s) for s in others
    ]
    feed_total = plane.over_groups(add(feed_parts[0], *feed_line))
    feed_arrived = plane.to_places([feed_total] * n_places)
    attention_line, feed_arrived, tokens_grad = together(
        attention_line, feed_arrived, tokens_grad
    )
    attention_total = plane.over_groups(
        add(attention_parts[0], *[a[:count] for a in attention_line])
    )
    small = plane.over_groups(add(small, *[a[count:] for a in attention_line])).astype(f32)
    arrived = plane.to_places([attention_total] * n_places)
    feed_half = plane.from_places(feed_total, feed_arrived)
    feed_other = plane.swap(feed_half, 1)
    arrived, feed_other = together(arrived, feed_other)
    attention_half = plane.from_places(attention_total, arrived)
    attention_other = plane.swap(attention_half, 1)
    feed_grad = plane.by_core(feed_half, feed_other).transpose(1, 0, 2, 3).reshape(units, -1)
    grad_list = plane.by_core(attention_half, attention_other)
    grad_list = grad_list.reshape(2, n_places, 2, mine // n_places, width)
    grad_list = grad_list.transpose(0, 2, 1, 3, 4).reshape(4, mine, width)

    shared = small[:6]
    split_rows = n_z * split.shape[1] // width
    split = lax.dynamic_slice_in_dim(
        small[6 : 6 + split_rows].reshape(n_z, -1), z, 1, 0
    )[0]

    return (
        output,
        tokens_grad,
        grad_list[0].T.astype(f32),
        split[units : units + mine],
        grad_list[1].T.astype(f32),
        grad_list[2].T.astype(f32),
        split[units + mine :],
        grad_list[3].astype(f32),
        shared[0],
        shared[1],
        shared[2],
        feed_grad[:, :width].T.astype(f32),
        split[:units],
        feed_grad[:, width:].astype(f32),
        shared[3],
        shared[4],
        shared[5],
    )


def solution(mesh):
    n_dp, n_z = mesh.shape["dp"], mesh.shape["tensor"]
    in_specs = (
        P("dp", None),
        P("dp", None),
        P("dp"),
        P(None, "tensor"),
        P("tensor"),
        P(None, "tensor"),
        P(None, "tensor"),
        P("tensor"),
        P("tensor", None),
        P(),
        P(),
        P(),
        P(None, "tensor"),
        P("tensor"),
        P("tensor", None),
        P(),
        P(),
        P(),
        P("dp", None),
    )
    out_specs = (
        P("dp", None),
        P("dp", None),
        P(None, "tensor"),
        P("tensor"),
        P(None, "tensor"),
        P(None, "tensor"),
        P("tensor"),
        P("tensor", None),
        P(),
        P(),
        P(),
        P(None, "tensor"),
        P("tensor"),
        P("tensor", None),
        P(),
        P(),
        P(),
    )

    def program(*args):
        return on_device(n_dp, n_z, *args)

    return jax.shard_map(
        program, mesh=mesh, in_specs=in_specs, out_specs=out_specs, check_vma=False
    )
```

```python
import functools

import jax
import jax.numpy as jnp
from jax import lax
from jax.experimental import pallas as pl
from jax.experimental.pallas import tpu as pltpu
from jax.sharding import PartitionSpec as P

HEAD = 64
BUCKET = 512
ITEMS = 8


negative_fill = -1e30
epsilon = 1e-06
f32 = jnp.float32
bf16 = jnp.bfloat16
VMEM_BYTES = 56 * 1024 * 1024


def dot(left, right):
    return jnp.dot(left, right, preferred_element_type=f32)


def contract_rows(left, right):
    return lax.dot_general(left, right, (((0,), (0,)), ((), ())), preferred_element_type=f32)


def contract_cols(left, right):
    return lax.dot_general(left, right, (((1,), (1,)), ((), ())), preferred_element_type=f32)


def norm_rows(values):
    centred = values - jnp.mean(values, axis=1, keepdims=True)
    inv_scale = lax.rsqrt(jnp.mean(centred * centred, axis=1, keepdims=True) + epsilon)
    return centred * inv_scale, inv_scale


def norm_back(grad_rows, norm_gain, normed, inv_scale):
    scaled = grad_rows * norm_gain
    return inv_scale * (
        scaled
        - jnp.mean(scaled, axis=1, keepdims=True)
        - normed * jnp.mean(scaled * normed, axis=1, keepdims=True)
    )


def column_sum(matrix):
    return jnp.sum(matrix.astype(f32), axis=0, keepdims=True)


def fixed(shape):
    return pl.BlockSpec(shape, lambda *_: (0,) * len(shape))


def cost(microseconds):
    return pl.CostEstimate(
        flops=int(microseconds * 1.0e9), bytes_accessed=int(microseconds * 1.0e6), transcendentals=0
    )


def params(axes):
    return pltpu.CompilerParams(
        dimension_semantics=("arbitrary",) * axes, vmem_limit_bytes=VMEM_BYTES
    )


def item_places(lengths_ref, row, shape, axis):
    places = lax.broadcasted_iota(jnp.int32, shape, axis)
    end = jnp.int32(0)
    items = jnp.zeros(shape, jnp.int32)
    for slot in range(ITEMS):
        end = end + lengths_ref[row, slot]
        items = items + (places >= end).astype(jnp.int32)
    return items


def as_column(row):
    return jnp.broadcast_to(row.astype(f32), (8, row.shape[1])).T[:, :1]


def mask_bias(lengths_ref, row, key_mask):
    shape = (BUCKET, BUCKET)
    diagonal = lax.broadcasted_iota(jnp.int32, shape, 0) == lax.broadcasted_iota(
        jnp.int32, shape, 1
    )
    item_row = item_places(lengths_ref, row, (1, BUCKET), 1)
    item_column = item_places(lengths_ref, row, (BUCKET, 1), 0)
    code_column = jnp.where(as_column(key_mask) == 1.0, item_column, -1)
    return jnp.where((code_column == item_row) | diagonal, 0.0, negative_fill).astype(f32)


def attend_forward_kernel(
    lengths_ref, tokens_ref, query_ref, key_ref, value_ref, biases_ref, key_mask_ref, mixed_ref,
):
    rows = tokens_ref[...]
    queries = contract_cols(query_ref[...], rows) + as_column(biases_ref[0:1, :])
    queries = (queries.astype(bf16) * HEAD ** (-0.5)).astype(bf16)
    keys = contract_cols(rows, key_ref[...]).astype(bf16)
    values = (contract_cols(value_ref[...], rows) + as_column(biases_ref[1:2, :])).astype(bf16)
    bias = mask_bias(lengths_ref, pl.program_id(0), key_mask_ref[0])
    parts = []
    for head in range(queries.shape[0] // HEAD):
        at = slice(head * HEAD, (head + 1) * HEAD)
        scores = dot(keys[:, at], queries[at]) + bias
        exponent = jnp.exp(scores - jnp.max(scores, axis=0, keepdims=True))
        total = jnp.sum(exponent, axis=0, keepdims=True)
        parts.append(dot(values[at], exponent.astype(bf16)) / total)
    mixed_ref[0] = jnp.concatenate(parts, axis=0).T.astype(bf16)


def attend_forward(n_z, lengths, tokens, query, key, value, biases, key_mask):
    blocks = lengths.shape[0]
    own = blocks // n_z
    mine, width = key.shape
    return pl.pallas_call(
        attend_forward_kernel,
        grid=(blocks,),
        in_specs=[
            pl.BlockSpec(memory_space=pltpu.SMEM),
            pl.BlockSpec((BUCKET, width), lambda b: (b, 0)),
            fixed((mine, width)),
            fixed((mine, width)),
            fixed((mine, width)),
            fixed((2, mine)),
            pl.BlockSpec((1, 1, BUCKET), lambda b: (b, 0, 0)),
        ],
        out_specs=pl.BlockSpec((1, BUCKET, mine), lambda b: (b // own, b % own, 0)),
        out_shape=jax.ShapeDtypeStruct((n_z, own * BUCKET, mine), bf16),
        compiler_params=params(1),
        name="attend_forward",
        cost_estimate=cost(12),
    )(lengths, tokens, query, key, value, biases, key_mask)


def load_units(number, own_ref, side_refs, units):
    units[0] = own_ref[...]

    for index in range(3):

        @pl.when(number == index)
        def _(index=index):
            units[1:] = side_refs[index][...]

    @pl.when(number == 3)
    def _():
        cut = side_refs[3].shape[1]
        units[1:, :cut] = side_refs[3][...]
        units[1:, cut:] = side_refs[4][...]


def feed_forward_kernel(
    info_ref, lengths_ref, mixed_ref, mixer_ref, tokens_ref, cotangent_ref, vectors_ref,
    bias_ref, own_ref, *rest,
):
    keep_refs, send_refs = rest[:5], rest[5:10]
    (
        hidden_ref, slope_ref, output_ref, normed_low_ref, first_normed_ref, first_scale_ref,
        grad_second_ref, grad_outer_ref, sums_ref, second_sum, units,
    ) = rest[10:]
    step = pl.program_id(0)
    places = pl.num_programs(0) // 2
    output_bias, first_gain, first_shift, outer_bias, second_gain, second_shift = (
        vectors_ref[i : i + 1, :] for i in range(6)
    )

    @pl.when(step == 0)
    def _():
        attended = output_bias + sum(
            dot(mixed_ref[t], mixer_ref[t]) for t in range(mixed_ref.shape[0])
        )
        normed, inv_scale = norm_rows(tokens_ref[...].astype(f32) + attended)
        whole = normed * first_gain + first_shift
        first_normed_ref[...] = normed
        first_scale_ref[...] = inv_scale
        normed_low_ref[...] = whole.astype(bf16)
        second_sum[...] = whole + outer_bias

    @pl.when(step < places)
    def _():
        load_units(step, own_ref, keep_refs, units)

    @pl.when(step >= places)
    def _():
        load_units(step - places, own_ref, send_refs, units)

    width = units.shape[2] // 2
    inner = units[:, :, :width].reshape(-1, width)
    outer = units[:, :, width:].reshape(-1, width)
    inner_pre = contract_cols(normed_low_ref[...], inner) + bias_ref[0]
    normal_cdf = 0.5 + 0.5 * lax.erf(inner_pre * 0.7071067811865476)
    density = jnp.exp(-0.5 * inner_pre * inner_pre) * 0.3989422804014327
    hidden = (inner_pre * normal_cdf).astype(bf16)
    hidden_ref[...] = hidden
    slope_ref[...] = (normal_cdf + inner_pre * density).astype(bf16)
    second_sum[...] += dot(hidden, outer)

    @pl.when(step == pl.num_programs(0) - 1)
    def _():
        normed, inv_scale = norm_rows(second_sum[...])
        blocks = normed.shape[0] // BUCKET
        live = jnp.concatenate(
            [
                (item_places(lengths_ref, info_ref[0] * blocks + b, (BUCKET, 1), 0) < ITEMS)
                for b in range(blocks)
            ],
            axis=0,
        ).astype(f32)
        output_ref[...] = ((normed * second_gain + second_shift) * live).astype(bf16)
        grad_final = cotangent_ref[...].astype(f32) * live
        grad_second = norm_back(grad_final, second_gain, normed, inv_scale)
        grad_outer = grad_second.astype(bf16)
        grad_second_ref[...] = grad_second
        grad_outer_ref[...] = grad_outer
        sums_ref[0:1, :] = column_sum(grad_outer)
        sums_ref[1:2, :] = column_sum(grad_final * normed)
        sums_ref[2:3, :] = column_sum(grad_final)


def feed_forward(info, lengths, mixed, mixer, tokens, cotangent, vectors, biases, own, keep, send):
    n_z, rows, mine = mixed.shape
    places = 4
    feed_rows, twice = keep[0].shape[1:]
    width = twice // 2
    chunk = n_z * feed_rows
    whole = fixed((rows, width))
    my_rows = pl.BlockSpec((rows, width), lambda j, info: (info[0], 0))
    columns = pl.BlockSpec((rows, chunk), lambda j, info: (0, j))
    shapes = [
        ((rows, 2 * places * chunk), bf16, columns),
        ((rows, 2 * places * chunk), bf16, columns),
        ((rows, width), bf16, whole),
        ((rows, width), bf16, whole),
        ((rows, width), f32, whole),
        ((rows, 1), f32, fixed((rows, 1))),
        ((rows, width), f32, whole),
        ((rows, width), bf16, whole),
        ((8, width), f32, fixed((8, width))),
    ]
    return pl.pallas_call(
        feed_forward_kernel,
        grid_spec=pltpu.PrefetchScalarGridSpec(
            num_scalar_prefetch=1,
            grid=(2 * places,),
            in_specs=[
                pl.BlockSpec(memory_space=pltpu.SMEM),
                fixed((n_z, rows, mine)),
                fixed((n_z, mine, width)),
                my_rows,
                my_rows,
                fixed((8, width)),
                pl.BlockSpec((1, 1, chunk), lambda j, info: (j, 0, 0)),
                pl.BlockSpec(
                    (feed_rows, twice),
                    lambda j, info: ((info[1] ^ (j % places)) * 2 + (info[2] ^ (j // places)), 0),
                ),
            ]
            + [fixed(array.shape) for array in keep + send],
            out_specs=[spec for _, _, spec in shapes],
            scratch_shapes=[
                pltpu.VMEM((rows, width), f32),
                pltpu.VMEM((n_z, feed_rows, twice), bf16),
            ],
        ),
        out_shape=[jax.ShapeDtypeStruct(shape, kind) for shape, kind, _ in shapes],
        compiler_params=params(1),
        name="feed_forward",
        cost_estimate=cost(21),
    )(info, lengths, mixed, mixer, tokens, cotangent, vectors, biases, own, *keep, *send)


STAY = ((0, 1), (0, 2))
GO = ((2, 3), (1, 3))


def feed_back_kernel(
    first, keeps, n_side, info_ref, grad_outer_ref, normed_low_ref, hidden_ref, slope_ref,
    own_ref, start_ref, *rest,
):
    side_refs, rest = rest[:n_side], rest[n_side:]
    if keeps:
        other_refs, norm_refs, rest = rest[:2], rest[2:5], rest[5:]
        stay_refs, go_refs, rest = rest[0:2], rest[2:4], rest[4:]
        bias_grad_ref, grad_first_ref, grad_attended_ref, sums_ref, units, grad_normed_ref = rest
    else:
        grad_ref, bias_grad_ref, grad_normed_ref, units = rest
    step = pl.program_id(0)

    @pl.when(step == 0)
    def _():
        grad_normed_ref[...] = start_ref[...]

    if n_side == 5:
        load_units(step, own_ref, side_refs, units)
    elif first == 0:
        units[0] = own_ref[...]
        for index in range(2):

            @pl.when(step == index)
            def _(index=index):
                units[1:] = side_refs[index][...]

    else:
        units[0] = own_ref[...]

        @pl.when(step == 0)
        def _():
            units[1:] = side_refs[0][...]

        @pl.when(step == 1)
        def _():
            cut = side_refs[1].shape[1]
            units[1:, :cut] = side_refs[1][...]
            units[1:, cut:] = side_refs[2][...]

    n_z, feed_rows, twice = units.shape
    width = twice // 2
    inner = units[:, :, :width].reshape(-1, width)
    outer = units[:, :, width:].reshape(-1, width)
    grad_outer = grad_outer_ref[...]
    grad_hidden = contract_cols(grad_outer, outer)
    grad_inner = (grad_hidden * slope_ref[...].astype(f32)).astype(bf16)
    outer_grad = contract_rows(hidden_ref[...], grad_outer).reshape(n_z, feed_rows, width)
    inner_grad = contract_rows(grad_inner, normed_low_ref[...]).reshape(n_z, feed_rows, width)
    bias_grad_ref[0] = column_sum(grad_inner)
    grad_normed_ref[...] += dot(grad_inner, inner)

    if keeps:
        for number in range(4):

            @pl.when(step == number)
            def _(number=number):
                other_ref = other_refs[number // 2]
                for track, value in enumerate((inner_grad, outer_grad)):
                    at = slice(track * width, (track + 1) * width)
                    value = (value + other_ref[number % 2, :, :, at].astype(f32)).astype(bf16)
                    if number in STAY[track]:
                        stay_refs[track][STAY[track].index(number)] = value
                    else:
                        go_refs[track][GO[track].index(number)] = value

        @pl.when(step == pl.num_programs(0) - 1)
        def _():
            first_normed_ref, first_scale_ref, vectors_ref = norm_refs
            grad_rows, normed = grad_normed_ref[...], first_normed_ref[...]
            grad_first = norm_back(grad_rows, vectors_ref[1:2, :], normed, first_scale_ref[...])
            grad_attended = grad_first.astype(bf16)
            grad_first_ref[...] = grad_first
            grad_attended_ref[...] = grad_attended
            sums_ref[0:1, :] = column_sum(grad_attended)
            sums_ref[1:2, :] = column_sum(grad_rows * normed)
            sums_ref[2:3, :] = column_sum(grad_rows)

    else:
        grad_ref[0, :, :, :width] = inner_grad.astype(bf16)
        grad_ref[0, :, :, width:] = outer_grad.astype(bf16)


def feed_back(
    first, count, info, grad_outer, normed_low, hidden, slope, own, start, side,
    others=None, norm=None,
):
    rows, width = grad_outer.shape
    keeps = others is not None
    feed_rows, twice = side[0].shape[1:]
    n_z = side[0].shape[0] + 1
    chunk = n_z * feed_rows
    flip = 0 if keeps else 1
    columns = pl.BlockSpec((rows, chunk), lambda i, info: (0, 4 * flip + first + i))
    whole = fixed((rows, width))
    part = (n_z, feed_rows, twice)
    track = (2, n_z, feed_rows, width)
    in_specs = [
        whole,
        whole,
        columns,
        columns,
        pl.BlockSpec(
            (feed_rows, twice),
            lambda i, info: ((info[1] ^ (first + i)) * 2 + (info[2] ^ flip), 0),
        ),
        whole,
    ] + [fixed(array.shape) for array in side]
    args = [grad_outer, normed_low, hidden, slope, own, start] + side
    bias_shape = (
        (count, 1, chunk),
        f32,
        pl.BlockSpec((1, 1, chunk), lambda i, info: (i, 0, 0)),
    )
    scratch = [pltpu.VMEM(part, bf16)]
    if keeps:
        in_specs += [fixed(array.shape) for array in others]
        in_specs += [whole, fixed((rows, 1)), fixed((8, width))]
        args += others + list(norm)
        shapes = [(track, bf16, fixed(track))] * 4 + [
            bias_shape,
            ((rows, width), f32, whole),
            ((rows, width), bf16, whole),
            ((8, width), f32, fixed((8, width))),
        ]
        scratch.append(pltpu.VMEM((rows, width), f32))
    else:
        shapes = [
            ((count,) + part, bf16, pl.BlockSpec((1,) + part, lambda i, info: (i, 0, 0, 0))),
            bias_shape,
            ((rows, width), f32, whole),
        ]
    return pl.pallas_call(
        functools.partial(feed_back_kernel, first, keeps, len(side)),
        grid_spec=pltpu.PrefetchScalarGridSpec(
            num_scalar_prefetch=1,
            grid=(count,),
            in_specs=in_specs,
            out_specs=[spec for _, _, spec in shapes],
            scratch_shapes=scratch,
        ),
        out_shape=[jax.ShapeDtypeStruct(shape, kind) for shape, kind, _ in shapes],
        compiler_params=params(1),
        name="feed_back_own" if keeps else "feed_back",
        cost_estimate=cost(3 * count),
    )(info, *args)


def attend_back_kernel(
    place_ref, lengths_ref, tokens_ref, grad_attended_ref, grad_first_ref, weights_ref, mixer_ref,
    biases_ref, key_mask_ref,
    grads_ref, tokens_grad_ref, sums_ref,
    bias, total_grad,
):
    pair = pl.program_id(1)

    @pl.when(pair == 0)
    def _():
        row = place_ref[0] * pl.num_programs(0) + pl.program_id(0)
        bias[...] = mask_bias(lengths_ref, row, key_mask_ref[0])
        total_grad[...] = grad_first_ref[...]

    rows, grad_attended = tokens_ref[...], grad_attended_ref[...]
    width = rows.shape[1]
    query_w, key_w, value_w = (
        weights_ref[:, i * width : (i + 1) * width] for i in range(3)
    )
    queries = contract_cols(query_w, rows) + as_column(biases_ref[0:1, :])
    queries = (queries.astype(bf16) * HEAD ** (-0.5)).astype(bf16)
    keys = contract_cols(rows, key_w).astype(bf16)
    values = (contract_cols(rows, value_w) + biases_ref[1:2, :]).astype(bf16)
    grad_mixed = contract_cols(mixer_ref[...], grad_attended).astype(bf16)
    keys_t = keys.T
    grad_queries, grad_keys, grad_values = [], [], []
    for head in range(keys.shape[1] // HEAD):
        at = slice(head * HEAD, (head + 1) * HEAD)
        scores = dot(keys[:, at], queries[at]) + bias[...]
        exponent = jnp.exp(scores - jnp.max(scores, axis=0, keepdims=True))
        probs = exponent * (1.0 / jnp.sum(exponent, axis=0, keepdims=True))
        grad_probs = dot(values[:, at], grad_mixed[at])
        shift = jnp.sum(probs * grad_probs, axis=0, keepdims=True)
        grad_scores = (probs * (grad_probs - shift)).astype(bf16)
        grad_values.append(contract_cols(probs.astype(bf16), grad_mixed[at]))
        grad_keys.append(contract_cols(grad_scores, queries[at]))
        grad_queries.append(dot(keys_t[at], grad_scores) * HEAD ** (-0.5))
    grad_query = jnp.concatenate(grad_queries, axis=0).T.astype(bf16)
    grad_key = jnp.concatenate(grad_keys, axis=1).astype(bf16)
    grad_value = jnp.concatenate(grad_values, axis=1).astype(bf16)
    grads_ref[0] = grad_query
    grads_ref[1] = grad_key
    grads_ref[2] = grad_value
    sums_ref[0, 0:1, :] = column_sum(grad_query)
    sums_ref[0, 1:2, :] = column_sum(grad_value)
    total_grad[...] += dot(grad_query, query_w) + dot(grad_key, key_w) + dot(grad_value, value_w)

    @pl.when(pair == pl.num_programs(1) - 1)
    def _():
        tokens_grad_ref[...] = total_grad[...].astype(bf16)


def attend_back(
    place, lengths, tokens, grad_attended, grad_first, weights, mixer, biases, key_mask
):
    rows, width = grad_attended.shape
    blocks = rows // BUCKET
    pair = 2 * HEAD
    own = lambda b, h, place: (place[0] * blocks + b, 0)
    by_bucket = pl.BlockSpec((BUCKET, width), lambda b, h, place: (b, 0))
    by_pair = lambda b, h, place: (h, 0)
    return pl.pallas_call(
        attend_back_kernel,
        grid_spec=pltpu.PrefetchScalarGridSpec(
            num_scalar_prefetch=1,
            grid=(blocks, width // pair),
            in_specs=[
                pl.BlockSpec(memory_space=pltpu.SMEM),
                pl.BlockSpec((BUCKET, width), own),
                by_bucket,
                by_bucket,
                pl.BlockSpec((pair, 3 * width), by_pair),
                pl.BlockSpec((pair, width), by_pair),
                pl.BlockSpec((8, pair), lambda b, h, place: (0, h)),
                pl.BlockSpec((1, 1, BUCKET), lambda b, h, place: (place[0] * blocks + b, 0, 0)),
            ],
            out_specs=[
                pl.BlockSpec((3, BUCKET, pair), lambda b, h, place: (0, b, h)),
                by_bucket,
                pl.BlockSpec((1, 8, pair), lambda b, h, place: (b, 0, h)),
            ],
            scratch_shapes=[pltpu.VMEM((BUCKET, BUCKET), f32), pltpu.VMEM((BUCKET, width), f32)],
        ),
        out_shape=[
            jax.ShapeDtypeStruct((3, rows, width), bf16),
            jax.ShapeDtypeStruct((rows, width), bf16),
            jax.ShapeDtypeStruct((blocks, 8, width), f32),
        ],
        compiler_params=params(2),
        name="attend_back",
        cost_estimate=cost(26),
    )(
        place, lengths, tokens, grad_attended, grad_first, weights, mixer, biases, key_mask
    )


def attention_grads_kernel(
    n_places, adds, info_ref, grads_ref, mixed_ref, tokens_ref, grad_attended_ref, *rest
):
    if adds:
        other_ref, small_ref = rest[:2]
        out_refs, whole = rest[2:-1], rest[-1]
    else:
        (out_ref, whole) = rest
    step = pl.program_id(0)
    which = info_ref[step]
    n_z, _, mine = mixed_ref.shape
    count = mine // n_places

    @pl.when(which < 3)
    def _():
        whole[...] = contract_rows(grads_ref[0], tokens_ref[...]).astype(bf16)

    @pl.when(which == 3)
    def _():
        for t in range(n_z):
            whole[t * mine : (t + 1) * mine, :] = contract_rows(
                mixed_ref[t], grad_attended_ref[...]
            ).astype(bf16)

    for number in range(n_places):
        for s in range(n_z):
            start = lax.rem(info_ref[2] + s, n_z) * mine + (info_ref[3] ^ number) * count
            value = whole[pl.ds(pl.multiple_of(start, 16), count), :]
            if adds:
                value = value.astype(f32) + other_ref[number, s, 0].astype(f32)
                row = (2 * s + step) * count
                out_refs[number][pl.ds(pl.multiple_of(row, 16), count), :] = value.astype(bf16)
            else:
                out_ref[number, s, 0] = value

    if adds:
        for number in range(n_places):
            out_refs[number][2 * n_z * count :, :] = small_ref[...]


def attention_grads(n_places, info, grads, mixed, tokens, grad_attended, other=None, small=None):
    rows, width = grad_attended.shape
    n_z, _, mine = mixed.shape
    count = mine // n_places
    parts = (n_places, n_z, 1, count, width)
    by_step = pl.BlockSpec(parts, lambda i, info: (0, 0, i, 0, 0))
    in_specs = [
        pl.BlockSpec((1, rows, width), lambda i, info: (jnp.minimum(info[i], 2), 0, 0)),
        fixed((n_z, rows, mine)),
        pl.BlockSpec((rows, width), lambda i, info: (info[2], 0)),
        fixed((rows, width)),
    ]
    args = [grads, mixed, tokens, grad_attended]
    if other is None:
        shapes = [((n_places, n_z, 2, count, width), by_step)]
    else:
        in_specs += [by_step, fixed(small.shape)]
        args += [other, small]
        flat = (2 * n_z * count + small.shape[0], width)
        shapes = [(flat, fixed(flat))] * n_places
    return pl.pallas_call(
        functools.partial(attention_grads_kernel, n_places, other is not None),
        grid_spec=pltpu.PrefetchScalarGridSpec(
            num_scalar_prefetch=1,
            grid=(2,),
            in_specs=in_specs,
            out_specs=[spec for _, spec in shapes],
            scratch_shapes=[pltpu.VMEM((width, width), bf16)],
        ),
        out_shape=[jax.ShapeDtypeStruct(shape, bf16) for shape, _ in shapes],
        compiler_params=params(1),
        name="attention_grads",
        cost_estimate=cost(6),
    )(info, *args)


def together(*values):
    return lax.optimization_barrier(values)


def add(first, *others):
    total = first.astype(f32)
    for other in others:
        total = total + other.astype(f32)
    return total.astype(bf16)


class Plane:
    def __init__(self, n_dp, n_z):
        self.n_dp, self.n_z = n_dp, n_z
        self.n_group = min(n_dp, 8)
        self.n_places = self.n_group // 2
        self.dp = lax.axis_index("dp")
        self.z = lax.axis_index("tensor")
        self.index = lax.rem(self.dp, self.n_group)
        self.core = self.index & 1
        self.place = self.index >> 1

    def swap(self, array, bits):
        return lax.ppermute(array, "dp", [(i, i ^ bits) for i in range(self.n_dp)])

    def shift(self, array, by):
        n = self.n_z
        return lax.ppermute(array, "tensor", [(i, (i + by) % n) for i in range(n)])

    def gather(self, piece):
        if self.n_dp == self.n_group:
            whole = lax.all_gather(piece, ("tensor", "dp"))
            return whole.reshape((self.n_z, self.n_group) + piece.shape)
        groups = [
            list(range(i, i + self.n_group)) for i in range(0, self.n_dp, self.n_group)
        ]
        line = lax.all_gather(piece, "tensor")
        return lax.all_gather(line, "dp", axis=1, axis_index_groups=groups)

    def turned(self, array):
        bit = 1
        while bit < self.n_group:
            lead = array.reshape((-1, 2, bit) + array.shape[1:])
            array = jnp.where((self.index & bit) != 0, lead[:, ::-1], lead).reshape(array.shape)
            bit *= 2
        return array

    def to_places(self, parts):
        return [self.swap(parts[number], 2 * number) for number in range(1, self.n_places)]

    def from_places(self, own, arrived):
        found = jnp.stack([own] + arrived)
        bit = 1
        while bit < self.n_places:
            lead = found.reshape((-1, 2, bit) + own.shape)
            flipped = lead[:, ::-1]
            found = jnp.where((self.place & bit) != 0, flipped, lead).reshape(found.shape)
            bit *= 2
        return found

    def by_core(self, own, other):
        return jnp.where(
            self.core == 1, jnp.stack([other, own]), jnp.stack([own, other])
        )

    def over_groups(self, array):
        bit = self.n_group
        while bit < self.n_dp:
            array = add(array, self.swap(array, bit))
            bit *= 2
        return array


def on_device(
    n_dp,
    n_z,
    tokens,
    lengths,
    key_mask,
    query_weight,
    query_bias,
    key_weight,
    value_weight,
    value_bias,
    output_weight,
    output_bias,
    first_gain,
    first_shift,
    inner_weight,
    inner_bias,
    outer_weight,
    outer_bias,
    second_gain,
    second_shift,
    cotangent,
):
    width = tokens.shape[1]
    mine = query_weight.shape[1]
    units = inner_weight.shape[1]
    all_rows = tokens.shape[0]
    all_blocks = all_rows // BUCKET
    rows = all_rows // n_z
    plane = Plane(n_dp, n_z)
    z, core, place, index = plane.z, plane.core, plane.place, plane.index
    n_places = plane.n_places
    others = range(1, n_z)

    feed_rows = units // plane.n_group
    head_rows = mine // plane.n_group
    piece = jnp.concatenate(
        [
            lax.dynamic_slice_in_dim(inner_weight, index * feed_rows, feed_rows, 1).T,
            lax.dynamic_slice_in_dim(outer_weight, index * feed_rows, feed_rows, 0),
        ],
        axis=1,
    )
    line = [plane.shift(piece, s) for s in others]

    mixer = plane.gather(
        lax.dynamic_slice_in_dim(output_weight, index * head_rows, head_rows, 0)
    ).reshape(n_z, mine, width)
    query_t, key_t, value_t = query_weight.T, key_weight.T, value_weight.T
    attention_weights = plane.gather(
        lax.dynamic_slice_in_dim(
            jnp.concatenate([query_t, key_t, value_t], axis=1), index * head_rows, head_rows, 0
        )
    ).reshape(width, 3 * width)

    key_mask_rows = key_mask.reshape(all_blocks, 1, BUCKET)
    mixed = attend_forward(
        n_z, lengths, tokens, query_t, key_t, value_t, jnp.stack([query_bias, value_bias]),
        key_mask_rows,
    )
    mixed, line = together(mixed, line)
    mixed = lax.all_to_all(mixed, "tensor", 0, 0)

    near = jnp.stack(line)
    by_x, by_y = plane.swap(near, 2), plane.swap(near, 4)
    bias_row = jnp.concatenate([query_bias, value_bias, inner_bias]).reshape(1, -1)
    bias_line = [bias_row] + [plane.shift(bias_row, s) for s in others]
    by_x, by_y, bias_line = together(by_x, by_y, bias_line)
    cut = feed_rows // 2
    far_x, far_y = plane.swap(by_x[:, :cut], 4), plane.swap(by_y[:, cut:], 2)
    there = [plane.swap(array, 1) for array in (near, by_x, by_y)]
    far_x, far_y, there, mixed = together(far_x, far_y, there, mixed)
    keep = [near, by_x, by_y, far_x, far_y]
    send = there + [plane.swap(array, 1) for array in (far_x, far_y)]
    own_units = jnp.concatenate([inner_weight.T, outer_weight], axis=1)

    biases = jnp.concatenate(
        [
            sum(
                jnp.where(lax.rem(z - t + n_z, n_z) == s, bias_line[s], 0).astype(f32)
                for s in range(n_z)
            )
            for t in range(n_z)
        ],
        axis=0,
    )
    head_biases = jnp.pad(
        jnp.stack([biases[:, :mine].reshape(-1), biases[:, mine : 2 * mine].reshape(-1)]),
        ((0, 6), (0, 0)),
    )
    inner_biases = jnp.concatenate(bias_line, axis=0)[:, 2 * mine :].astype(f32)
    inner_biases = inner_biases.reshape(n_z, plane.n_group, feed_rows).transpose(1, 0, 2)
    inner_biases = plane.turned(inner_biases).reshape(n_places, 2, 1, n_z * feed_rows)
    inner_biases = inner_biases.transpose(1, 0, 2, 3).reshape(plane.n_group, 1, -1)
    vectors = jnp.stack(
        [output_bias, first_gain, first_shift, outer_bias, second_gain, second_shift]
        + [jnp.zeros_like(output_bias)] * 2
    ).astype(f32)

    place_z = z.reshape(1)
    info = jnp.stack([z, place, core])
    (
        hidden, slope, my_output, normed_low, first_normed, first_scale, grad_second, grad_outer,
        second_sums,
    ) = feed_forward(
        info, lengths, mixed, mixer, tokens, cotangent, vectors, inner_biases, own_units, keep, send
    )
    output = lax.all_gather(my_output, "tensor", axis=0, tiled=True)

    shared_args = (info, grad_outer, normed_low, hidden, slope, own_units)
    sent_a, bias_sent_a, grad_normed = feed_back(0, 2, *shared_args, grad_second, send[:2])
    other_a = plane.swap(sent_a, 1)
    sent_b, bias_sent_b, grad_normed = feed_back(2, 2, *shared_args, grad_normed, send[2:])
    grad_normed, other_a, attention_weights = together(grad_normed, other_a, attention_weights)
    other_b = plane.swap(sent_b, 1)
    (
        inner_stay, outer_stay, inner_go, outer_go, bias_kept, grad_first, grad_attended, first_sums
    ) = feed_back(
        0, 4, *shared_args, grad_normed, keep, [other_a, other_b],
        (first_normed, first_scale, vectors),
    )
    inner_came, outer_came = plane.swap(inner_go, 4), plane.swap(outer_go, 2)
    bias_grads = jnp.stack(
        [bias_kept[:, 0], jnp.concatenate([bias_sent_a, bias_sent_b])[:, 0]], axis=1
    )
    inner_bias_grad = plane.turned(bias_grads.reshape(plane.n_group, n_z, feed_rows))
    inner_bias_grad = inner_bias_grad.transpose(1, 0, 2)
    inner_bias_grad = jnp.concatenate(
        [
            sum(
                jnp.where(lax.rem(z - t + n_z, n_z) == s, inner_bias_grad[s : s + 1], 0.0)
                for s in range(n_z)
            )
            for t in range(n_z)
        ],
        axis=0,
    ).reshape(n_z, units)

    grads, my_tokens_grad, back_sums = attend_back(
        place_z, lengths, tokens, grad_attended, grad_first, attention_weights,
        mixer.reshape(width, width), head_biases, key_mask_rows,
    )
    grads, inner_came, outer_came, output = together(grads, inner_came, outer_came, output)
    inner_on, outer_on = (
        plane.swap(add(inner_stay[1], inner_came[1]), 2),
        plane.swap(add(outer_stay[1], outer_came[1]), 4),
    )
    tokens_grad = lax.all_gather(my_tokens_grad, "tensor", axis=0, tiled=True)

    back_sums = jnp.sum(back_sums, axis=0)
    split = jnp.concatenate(
        [inner_bias_grad, back_sums[0].reshape(n_z, mine), back_sums[1].reshape(n_z, mine)], axis=1
    )
    small = jnp.concatenate([first_sums[:3], second_sums[:3], split.reshape(-1, width)], axis=0)
    small = jnp.pad(small, ((0, -small.shape[0] % 16), (0, 0))).astype(bf16)
    small_rows = small.shape[0]

    def weight_grads(side, other=None, small=None):
        info = jnp.stack([2 * side, 2 * side + 1, z, place])
        return attention_grads(
            n_places, info, grads, mixed, tokens, grad_attended, other, small
        )

    (sent,) = weight_grads(1 - core)
    sent, small, inner_on, outer_on = together(sent, small, inner_on, outer_on)
    other = plane.swap(sent, 1)
    small = add(small, plane.swap(small, 1))
    feed_parts = [
        jnp.concatenate(
            [
                add(inner_stay[0, s], inner_came[0, s], inner_on[s]),
                add(outer_stay[0, s], outer_came[0, s], outer_on[s]),
            ],
            axis=1,
        )
        for s in range(n_z)
    ]
    feed_line = [plane.shift(feed_parts[s], -s) for s in others]
    kept = weight_grads(core, other, small)
    arrived = plane.to_places(kept)
    arrived, feed_line = together(arrived, feed_line)
    small = add(small, *[a[-small_rows:] for a in arrived])
    count = 2 * mine // n_places
    attention_parts = [
        add(*[a[s * count : (s + 1) * count] for a in [kept[0]] + arrived]) for s in range(n_z)
    ]
    attention_line = [
        plane.shift(jnp.concatenate([attention_parts[s], small], axis=0), s) for s in others
    ]
    feed_total = plane.over_groups(add(feed_parts[0], *feed_line))
    feed_arrived = plane.to_places([feed_total] * n_places)
    attention_line, feed_arrived, tokens_grad = together(
        attention_line, feed_arrived, tokens_grad
    )
    attention_total = plane.over_groups(
        add(attention_parts[0], *[a[:count] for a in attention_line])
    )
    small = plane.over_groups(add(small, *[a[count:] for a in attention_line])).astype(f32)
    arrived = plane.to_places([attention_total] * n_places)
    feed_half = plane.from_places(feed_total, feed_arrived)
    feed_other = plane.swap(feed_half, 1)
    arrived, feed_other = together(arrived, feed_other)
    attention_half = plane.from_places(attention_total, arrived)
    attention_other = plane.swap(attention_half, 1)
    feed_grad = plane.by_core(feed_half, feed_other).transpose(1, 0, 2, 3).reshape(units, -1)
    grad_list = plane.by_core(attention_half, attention_other)
    grad_list = grad_list.reshape(2, n_places, 2, mine // n_places, width)
    grad_list = grad_list.transpose(0, 2, 1, 3, 4).reshape(4, mine, width)

    shared = small[:6]
    split_rows = n_z * split.shape[1] // width
    split = lax.dynamic_slice_in_dim(
        small[6 : 6 + split_rows].reshape(n_z, -1), z, 1, 0
    )[0]

    return (
        output,
        tokens_grad,
        grad_list[0].T.astype(f32),
        split[units : units + mine],
        grad_list[1].T.astype(f32),
        grad_list[2].T.astype(f32),
        split[units + mine :],
        grad_list[3].astype(f32),
        shared[0],
        shared[1],
        shared[2],
        feed_grad[:, :width].T.astype(f32),
        split[:units],
        feed_grad[:, width:].astype(f32),
        shared[3],
        shared[4],
        shared[5],
    )


def solution(mesh):
    n_dp, n_z = mesh.shape["dp"], mesh.shape["tensor"]
    in_specs = (
        P("dp", None),
        P("dp", None),
        P("dp"),
        P(None, "tensor"),
        P("tensor"),
        P(None, "tensor"),
        P(None, "tensor"),
        P("tensor"),
        P("tensor", None),
        P(),
        P(),
        P(),
        P(None, "tensor"),
        P("tensor"),
        P("tensor", None),
        P(),
        P(),
        P(),
        P("dp", None),
    )
    out_specs = (
        P("dp", None),
        P("dp", None),
        P(None, "tensor"),
        P("tensor"),
        P(None, "tensor"),
        P(None, "tensor"),
        P("tensor"),
        P("tensor", None),
        P(),
        P(),
        P(),
        P(None, "tensor"),
        P("tensor"),
        P("tensor", None),
        P(),
        P(),
        P(),
    )

    def program(*args):
        return on_device(n_dp, n_z, *args)

    return jax.shard_map(
        program, mesh=mesh, in_specs=in_specs, out_specs=out_specs, check_vma=False
    )
```

```python
import functools

import jax
import jax.numpy as jnp
from jax import lax
from jax.experimental import pallas as pl
from jax.experimental.pallas import tpu as pltpu
from jax.sharding import PartitionSpec as P

HEAD = 64
BUCKET = 512
ITEMS = 8


negative_fill = -1e30
epsilon = 1e-06
f32 = jnp.float32
bf16 = jnp.bfloat16
VMEM_BYTES = 56 * 1024 * 1024


def dot(left, right):
    return jnp.dot(left, right, preferred_element_type=f32)


def contract_rows(left, right):
    return lax.dot_general(left, right, (((0,), (0,)), ((), ())), preferred_element_type=f32)


def contract_cols(left, right):
    return lax.dot_general(left, right, (((1,), (1,)), ((), ())), preferred_element_type=f32)


def norm_rows(values):
    centred = values - jnp.mean(values, axis=1, keepdims=True)
    inv_scale = lax.rsqrt(jnp.mean(centred * centred, axis=1, keepdims=True) + epsilon)
    return centred * inv_scale, inv_scale


def norm_back(grad_rows, norm_gain, normed, inv_scale):
    scaled = grad_rows * norm_gain
    return inv_scale * (
        scaled
        - jnp.mean(scaled, axis=1, keepdims=True)
        - normed * jnp.mean(scaled * normed, axis=1, keepdims=True)
    )


def column_sum(matrix):
    return jnp.sum(matrix.astype(f32), axis=0, keepdims=True)


def fixed(shape):
    return pl.BlockSpec(shape, lambda *_: (0,) * len(shape))


def cost(microseconds):
    return pl.CostEstimate(
        flops=int(microseconds * 2.5e8),
        bytes_accessed=int(microseconds * 2.5e5),
        transcendentals=0,
    )


def params(axes):
    return pltpu.CompilerParams(
        dimension_semantics=("arbitrary",) * axes, vmem_limit_bytes=VMEM_BYTES
    )


def item_places(lengths_ref, row, shape, axis):
    places = lax.broadcasted_iota(jnp.int32, shape, axis)
    end = jnp.int32(0)
    items = jnp.zeros(shape, jnp.int32)
    for slot in range(ITEMS):
        end = end + lengths_ref[row, slot]
        items = items + (places >= end).astype(jnp.int32)
    return items


def as_column(row):
    return jnp.broadcast_to(row.astype(f32), (8, row.shape[1])).T[:, :1]


def mask_bias(lengths_ref, row, key_mask):
    shape = (BUCKET, BUCKET)
    diagonal = lax.broadcasted_iota(jnp.int32, shape, 0) == lax.broadcasted_iota(
        jnp.int32, shape, 1
    )
    item_row = item_places(lengths_ref, row, (1, BUCKET), 1)
    item_column = item_places(lengths_ref, row, (BUCKET, 1), 0)
    code_column = jnp.where(as_column(key_mask) == 1.0, item_column, -1)
    return jnp.where((code_column == item_row) | diagonal, 0.0, negative_fill).astype(f32)


def attend_forward_kernel(
    lengths_ref, tokens_ref, query_ref, key_ref, value_ref, biases_ref, key_mask_ref, mixed_ref,
):
    mine = query_ref.shape[0]
    rows = tokens_ref[...]
    queries = contract_cols(query_ref[...], rows) + as_column(biases_ref[0:1, :mine])
    queries = (queries.astype(bf16) * HEAD ** (-0.5)).astype(bf16)
    keys = contract_cols(rows, key_ref[...]).astype(bf16)
    values = contract_cols(value_ref[...], rows) + as_column(biases_ref[0:1, mine : 2 * mine])
    values = values.astype(bf16)
    bias = mask_bias(lengths_ref, pl.program_id(0), key_mask_ref[0])
    for head in range(mine // HEAD):
        at = slice(head * HEAD, (head + 1) * HEAD)
        scores = dot(keys[:, at], queries[at]) + bias
        exponent = jnp.exp(scores - jnp.max(scores, axis=0, keepdims=True))
        total = jnp.sum(exponent, axis=0, keepdims=True)
        mixed_ref[0, 0, at] = (dot(values[at], exponent.astype(bf16)) / total).astype(bf16)
    mixed_ref[0, 0, mine:] = biases_ref[...]


def attend_forward(n_z, lengths, tokens, query, key, value, biases, key_mask):
    blocks = lengths.shape[0]
    own = blocks // n_z
    mine, width = key.shape
    whole = (n_z, own, mine + biases.shape[0], BUCKET)
    return pl.pallas_call(
        attend_forward_kernel,
        grid=(blocks,),
        in_specs=[
            pl.BlockSpec(memory_space=pltpu.SMEM),
            pl.BlockSpec((BUCKET, width), lambda b: (b, 0)),
            fixed((mine, width)),
            fixed((mine, width)),
            fixed((mine, width)),
            fixed(biases.shape),
            pl.BlockSpec((1, 1, BUCKET), lambda b: (b, 0, 0)),
        ],
        out_specs=pl.BlockSpec((1, 1) + whole[2:], lambda b: (b // own, b % own, 0, 0)),
        out_shape=jax.ShapeDtypeStruct(whole, bf16),
        compiler_params=params(1),
        name="attend_forward",
        cost_estimate=cost(12),
    )(lengths, tokens, query, key, value, biases, key_mask)


def fetch_units(step, picks, own_ref, halves, units, sems):
    feed_rows = units.shape[2]
    cut = feed_rows // 2

    def copies(number):
        slot = number % 2
        row = pl.multiple_of(picks[number] * feed_rows, 16)
        ends = [
            (own_ref.at[pl.ds(row, feed_rows)], units.at[slot, 0]),
            (halves[number][0], units.at[slot, 1:, :cut]),
            (halves[number][1], units.at[slot, 1:, cut:]),
        ]
        return [
            pltpu.make_async_copy(source, target, sems.at[slot, i])
            for i, (source, target) in enumerate(ends)
        ]

    for number in range(len(halves)):

        @pl.when(step == number)
        def _(number=number):
            if number == 0:
                for copy in copies(0):
                    copy.start()
            if number + 1 < len(halves):
                for copy in copies(number + 1):
                    copy.start()
            for copy in copies(number):
                copy.wait()

    return units.at[lax.rem(step, 2)]


def split_units(units):
    width = units.shape[2] // 2
    return units[:, :, :width].reshape(-1, width), units[:, :, width:].reshape(-1, width)


ANYWHERE = pl.BlockSpec(memory_space=pl.ANY)


def feed_forward_kernel(
    info_ref, lengths_ref, mixed_ref, mixer_ref, tokens_ref, cotangent_ref, vectors_ref,
    bias_ref, own_ref, *rest,
):
    halves, rest = list(zip(rest[:16:2], rest[1:16:2])), rest[16:]
    (
        hidden_ref, slope_ref, output_ref, normed_low_ref, first_normed_ref, first_scale_ref,
        grad_second_ref, grad_outer_ref, sums_ref, second_sum, units, sems,
    ) = rest
    step = pl.program_id(0)
    picks = [(info_ref[1] ^ (k % 4)) * 2 + (info_ref[2] ^ (k // 4)) for k in range(8)]
    weights = fetch_units(step, picks, own_ref, halves, units, sems)
    output_bias, first_gain, first_shift, outer_bias, second_gain, second_shift = (
        vectors_ref[i : i + 1, :] for i in range(6)
    )

    @pl.when(step == 0)
    def _():
        n_z, own, mine, _ = mixed_ref.shape
        attended = output_bias + jnp.concatenate(
            [
                sum(
                    contract_rows(mixed_ref[t, b], mixer_ref[t * mine : (t + 1) * mine, :])
                    for t in range(n_z)
                )
                for b in range(own)
            ],
            axis=0,
        )
        normed, inv_scale = norm_rows(tokens_ref[...].astype(f32) + attended)
        whole = normed * first_gain + first_shift
        first_normed_ref[...] = normed
        first_scale_ref[...] = inv_scale
        normed_low_ref[...] = whole.astype(bf16)
        second_sum[...] = whole + outer_bias

    inner, outer = split_units(weights)
    inner_pre = contract_cols(normed_low_ref[...], inner) + bias_ref[0]
    normal_cdf = 0.5 + 0.5 * lax.erf(inner_pre * 0.7071067811865476)
    density = jnp.exp(-0.5 * inner_pre * inner_pre) * 0.3989422804014327
    hidden = (inner_pre * normal_cdf).astype(bf16)
    hidden_ref[...] = hidden
    slope_ref[...] = (normal_cdf + inner_pre * density).astype(bf16)
    second_sum[...] += dot(hidden, outer)

    @pl.when(step == pl.num_programs(0) - 1)
    def _():
        normed, inv_scale = norm_rows(second_sum[...])
        blocks = normed.shape[0] // BUCKET
        live = jnp.concatenate(
            [
                (item_places(lengths_ref, info_ref[0] * blocks + b, (BUCKET, 1), 0) < ITEMS)
                for b in range(blocks)
            ],
            axis=0,
        ).astype(f32)
        output_ref[...] = ((normed * second_gain + second_shift) * live).astype(bf16)
        grad_final = cotangent_ref[...].astype(f32) * live
        grad_second = norm_back(grad_final, second_gain, normed, inv_scale)
        grad_outer = grad_second.astype(bf16)
        grad_second_ref[...] = grad_second
        grad_outer_ref[...] = grad_outer
        sums_ref[0:1, :] = column_sum(grad_outer)
        sums_ref[1:2, :] = column_sum(grad_final * normed)
        sums_ref[2:3, :] = column_sum(grad_final)


def feed_forward(info, lengths, mixed, attention, tokens, cotangent, vectors, biases, own, halves):
    n_z, buckets = mixed.shape[:2]
    rows = buckets * BUCKET
    width = own.shape[1] // 2
    mine = width // n_z
    feed_rows, twice = own.shape[0] // 8, 2 * width
    chunk = n_z * feed_rows
    whole = fixed((rows, width))
    my_rows = pl.BlockSpec((rows, width), lambda j, info: (info[0], 0))
    columns = pl.BlockSpec((rows, chunk), lambda j, info: (0, j))
    shapes = [
        ((rows, 8 * chunk), bf16, columns),
        ((rows, 8 * chunk), bf16, columns),
        ((rows, width), bf16, whole),
        ((rows, width), bf16, whole),
        ((rows, width), f32, whole),
        ((rows, 1), f32, fixed((rows, 1))),
        ((rows, width), f32, whole),
        ((rows, width), bf16, whole),
        ((8, width), f32, fixed((8, width))),
    ]
    return pl.pallas_call(
        feed_forward_kernel,
        grid_spec=pltpu.PrefetchScalarGridSpec(
            num_scalar_prefetch=1,
            grid=(8,),
            in_specs=[
                pl.BlockSpec(memory_space=pltpu.SMEM),
                fixed((n_z, buckets, mine, BUCKET)),
                pl.BlockSpec((width, width), lambda j, info: (0, 3)),
                my_rows,
                my_rows,
                fixed((8, width)),
                pl.BlockSpec((1, 1, chunk), lambda j, info: (j, 0, 0)),
                ANYWHERE,
            ]
            + [ANYWHERE] * 16,
            out_specs=[spec for _, _, spec in shapes],
            scratch_shapes=[
                pltpu.VMEM((rows, width), f32),
                pltpu.VMEM((2, n_z, feed_rows, twice), bf16),
                pltpu.SemaphoreType.DMA((2, 3)),
            ],
        ),
        out_shape=[jax.ShapeDtypeStruct(shape, kind) for shape, kind, _ in shapes],
        compiler_params=params(1),
        name="feed_forward",
        cost_estimate=cost(21),
    )(info, lengths, mixed, attention, tokens, cotangent, vectors, biases, own, *halves)


STAY = ((0, 1), (0, 2))
GO = ((2, 3), (1, 3))


def feed_back_kernel(
    first, count, keeps, info_ref, grad_outer_ref, normed_low_ref, hidden_ref, slope_ref,
    own_ref, start_ref, *rest,
):
    halves = list(zip(rest[: 2 * count : 2], rest[1 : 2 * count : 2]))
    rest = rest[2 * count :]
    if keeps:
        other_refs, norm_refs, rest = rest[:2], rest[2:5], rest[5:]
        stay_refs, go_refs, rest = rest[0:2], rest[2:4], rest[4:]
        bias_grad_ref, grad_first_ref, grad_attended_ref, sums_ref, units, sems = rest[:6]
        grad_normed_ref = rest[6]
    else:
        grad_ref, bias_grad_ref, grad_normed_ref, units, sems = rest
    step = pl.program_id(0)
    side = info_ref[2] if keeps else 1 - info_ref[2]
    picks = [(info_ref[1] ^ (first + k)) * 2 + side for k in range(count)]
    weights = fetch_units(step, picks, own_ref, halves, units, sems)

    @pl.when(step == 0)
    def _():
        grad_normed_ref[...] = start_ref[...]

    n_z, feed_rows, twice = weights.shape
    width = twice // 2
    inner, outer = split_units(weights)
    grad_outer = grad_outer_ref[...]
    grad_hidden = contract_cols(grad_outer, outer)
    grad_inner = (grad_hidden * slope_ref[...].astype(f32)).astype(bf16)
    outer_grad = contract_rows(hidden_ref[...], grad_outer).reshape(n_z, feed_rows, width)
    inner_grad = contract_rows(grad_inner, normed_low_ref[...]).reshape(n_z, feed_rows, width)
    bias_grad_ref[0] = column_sum(grad_inner)
    grad_normed_ref[...] += dot(grad_inner, inner)

    if keeps:
        for number in range(4):

            @pl.when(step == number)
            def _(number=number):
                other_ref = other_refs[number // 2]
                for track, value in enumerate((inner_grad, outer_grad)):
                    at = slice(track * width, (track + 1) * width)
                    value = (value + other_ref[0, :, :, at].astype(f32)).astype(bf16)
                    ref = stay_refs[track] if number in STAY[track] else go_refs[track]
                    ref[0] = value

        @pl.when(step == pl.num_programs(0) - 1)
        def _():
            first_normed_ref, first_scale_ref, vectors_ref = norm_refs
            grad_rows, normed = grad_normed_ref[...], first_normed_ref[...]
            grad_first = norm_back(grad_rows, vectors_ref[1:2, :], normed, first_scale_ref[...])
            grad_attended = grad_first.astype(bf16)
            grad_first_ref[...] = grad_first
            grad_attended_ref[...] = grad_attended
            sums_ref[0:1, :] = column_sum(grad_attended)
            sums_ref[1:2, :] = column_sum(grad_rows * normed)
            sums_ref[2:3, :] = column_sum(grad_rows)

    else:
        grad_ref[0, :, :, :width] = inner_grad.astype(bf16)
        grad_ref[0, :, :, width:] = outer_grad.astype(bf16)


def feed_back(
    first, count, info, grad_outer, normed_low, hidden, slope, own, start, halves,
    others=None, norm=None,
):
    rows, width = grad_outer.shape
    keeps = others is not None
    feed_rows, twice = own.shape[0] // 8, 2 * width
    n_z = halves[0].shape[0] + 1
    chunk = n_z * feed_rows
    flip = 0 if keeps else 1
    columns = pl.BlockSpec((rows, chunk), lambda i, info: (0, 4 * flip + first + i))
    whole = fixed((rows, width))
    part = (n_z, feed_rows, twice)
    track = (2, n_z, feed_rows, width)
    in_specs = [whole, whole, columns, columns, ANYWHERE, whole] + [ANYWHERE] * (2 * count)
    args = [grad_outer, normed_low, hidden, slope, own, start] + halves
    bias_shape = (
        (count, 1, chunk),
        f32,
        pl.BlockSpec((1, 1, chunk), lambda i, info: (i, 0, 0)),
    )
    scratch = [pltpu.VMEM((2,) + part, bf16), pltpu.SemaphoreType.DMA((2, 3))]

    def one(shape, at):
        return pl.BlockSpec((1,) + shape[1:], lambda i, info: (at(i), 0, 0, 0))

    if keeps:
        early, late = (lambda i: jnp.minimum(i, 1)), (lambda i: jnp.maximum(i - 2, 0))
        in_specs += [one((2,) + part, early), one((2,) + part, late)]
        in_specs += [whole, fixed((rows, 1)), fixed((8, width))]
        args += others + list(norm)
        slow, slower = (lambda i: i // 2), (lambda i: jnp.maximum(i - 1, 0) // 2)
        shapes = [(track, bf16, one(track, at)) for at in (early, slow, late, slower)] + [
            bias_shape,
            ((rows, width), f32, whole),
            ((rows, width), bf16, whole),
            ((8, width), f32, fixed((8, width))),
        ]
        scratch.append(pltpu.VMEM((rows, width), f32))
    else:
        shapes = [
            ((count,) + part, bf16, one((count,) + part, lambda i: i)),
            bias_shape,
            ((rows, width), f32, whole),
        ]
    return pl.pallas_call(
        functools.partial(feed_back_kernel, first, count, keeps),
        grid_spec=pltpu.PrefetchScalarGridSpec(
            num_scalar_prefetch=1,
            grid=(count,),
            in_specs=in_specs,
            out_specs=[spec for _, _, spec in shapes],
            scratch_shapes=scratch,
        ),
        out_shape=[jax.ShapeDtypeStruct(shape, kind) for shape, kind, _ in shapes],
        compiler_params=params(1),
        name="feed_back_own" if keeps else "feed_back",
        cost_estimate=cost(3 * count),
    )(info, *args)


def copy_kernel(from_ref, to_ref, sem):
    copy = pltpu.make_async_copy(from_ref, to_ref, sem)
    copy.start()
    copy.wait()


def copied(array):
    return pl.pallas_call(
        copy_kernel,
        in_specs=[ANYWHERE],
        out_specs=ANYWHERE,
        out_shape=jax.ShapeDtypeStruct(array.shape, array.dtype),
        scratch_shapes=[pltpu.SemaphoreType.DMA(())],
        name="copied",
        cost_estimate=cost(2),
    )(array)


def attend_back_kernel(
    place_ref, lengths_ref, tokens_ref, grad_attended_ref, grad_first_ref, weights_ref, biases_ref,
    key_mask_ref,
    grads_ref, tokens_grad_ref, sums_ref,
    bias, total_grad,
):
    pair = pl.program_id(1)

    @pl.when(pair == 0)
    def _():
        row = place_ref[0] * pl.num_programs(0) + pl.program_id(0)
        bias[...] = mask_bias(lengths_ref, row, key_mask_ref[0])
        total_grad[...] = grad_first_ref[...]

    rows, grad_attended = tokens_ref[...], grad_attended_ref[...]
    width = rows.shape[1]
    query_w, key_w, value_w, output_w = (
        weights_ref[:, i * width : (i + 1) * width] for i in range(4)
    )
    queries = contract_cols(query_w, rows) + as_column(biases_ref[0:1, :])
    queries = (queries.astype(bf16) * HEAD ** (-0.5)).astype(bf16)
    keys = contract_cols(rows, key_w).astype(bf16)
    values = (contract_cols(rows, value_w) + biases_ref[1:2, :]).astype(bf16)
    grad_mixed = contract_cols(output_w, grad_attended).astype(bf16)
    keys_t = keys.T
    grad_queries, grad_keys, grad_values = [], [], []
    for head in range(keys.shape[1] // HEAD):
        at = slice(head * HEAD, (head + 1) * HEAD)
        scores = dot(keys[:, at], queries[at]) + bias[...]
        exponent = jnp.exp(scores - jnp.max(scores, axis=0, keepdims=True))
        probs = exponent * (1.0 / jnp.sum(exponent, axis=0, keepdims=True))
        grad_probs = dot(values[:, at], grad_mixed[at])
        shift = jnp.sum(probs * grad_probs, axis=0, keepdims=True)
        grad_scores = (probs * (grad_probs - shift)).astype(bf16)
        grad_values.append(contract_cols(probs.astype(bf16), grad_mixed[at]))
        grad_keys.append(contract_cols(grad_scores, queries[at]))
        grad_queries.append(dot(keys_t[at], grad_scores) * HEAD ** (-0.5))
    grad_query = jnp.concatenate(grad_queries, axis=0).T.astype(bf16)
    grad_key = jnp.concatenate(grad_keys, axis=1).astype(bf16)
    grad_value = jnp.concatenate(grad_values, axis=1).astype(bf16)
    grads_ref[0] = grad_query
    grads_ref[1] = grad_key
    grads_ref[2] = grad_value
    sums_ref[0, 0:1, :] = column_sum(grad_query)
    sums_ref[0, 1:2, :] = column_sum(grad_value)
    total_grad[...] += dot(grad_query, query_w) + dot(grad_key, key_w) + dot(grad_value, value_w)

    @pl.when(pair == pl.num_programs(1) - 1)
    def _():
        tokens_grad_ref[...] = total_grad[...].astype(bf16)


def attend_back(
    place, lengths, tokens, grad_attended, grad_first, weights, biases, key_mask
):
    rows, width = grad_attended.shape
    blocks = rows // BUCKET
    pair = 2 * HEAD
    own = lambda b, h, place: (place[0] * blocks + b, 0)
    by_bucket = pl.BlockSpec((BUCKET, width), lambda b, h, place: (b, 0))
    by_pair = lambda b, h, place: (h, 0)
    return pl.pallas_call(
        attend_back_kernel,
        grid_spec=pltpu.PrefetchScalarGridSpec(
            num_scalar_prefetch=1,
            grid=(blocks, width // pair),
            in_specs=[
                pl.BlockSpec(memory_space=pltpu.SMEM),
                pl.BlockSpec((BUCKET, width), own),
                by_bucket,
                by_bucket,
                pl.BlockSpec((pair, 4 * width), by_pair),
                pl.BlockSpec((8, pair), lambda b, h, place: (0, h)),
                pl.BlockSpec((1, 1, BUCKET), lambda b, h, place: (place[0] * blocks + b, 0, 0)),
            ],
            out_specs=[
                pl.BlockSpec((3, BUCKET, pair), lambda b, h, place: (0, b, h)),
                by_bucket,
                pl.BlockSpec((1, 8, pair), lambda b, h, place: (b, 0, h)),
            ],
            scratch_shapes=[pltpu.VMEM((BUCKET, BUCKET), f32), pltpu.VMEM((BUCKET, width), f32)],
        ),
        out_shape=[
            jax.ShapeDtypeStruct((3, rows, width), bf16),
            jax.ShapeDtypeStruct((rows, width), bf16),
            jax.ShapeDtypeStruct((blocks, 8, width), f32),
        ],
        compiler_params=params(2),
        name="attend_back",
        cost_estimate=cost(26),
    )(
        place, lengths, tokens, grad_attended, grad_first, weights, biases, key_mask
    )


def attention_grads_kernel(
    n_places, adds, info_ref, grads_ref, mixed_ref, tokens_ref, grad_attended_ref, *rest
):
    if adds:
        other_ref, small_ref = rest[:2]
        out_refs, whole = rest[2:-1], rest[-1]
    else:
        (out_ref, whole) = rest
    step = pl.program_id(0)
    which = info_ref[step]
    n_z, buckets, mine, _ = mixed_ref.shape
    count = mine // n_places

    @pl.when(which < 3)
    def _():
        whole[...] = contract_rows(grads_ref[0], tokens_ref[...]).astype(bf16)

    @pl.when(which == 3)
    def _():
        for t in range(n_z):
            whole[t * mine : (t + 1) * mine, :] = sum(
                dot(mixed_ref[t, b], grad_attended_ref[b * BUCKET : (b + 1) * BUCKET, :])
                for b in range(buckets)
            ).astype(bf16)

    for number in range(n_places):
        for s in range(n_z):
            start = lax.rem(info_ref[2] + s, n_z) * mine + (info_ref[3] ^ number) * count
            value = whole[pl.ds(pl.multiple_of(start, 16), count), :]
            if adds:
                value = value.astype(f32) + other_ref[number, s, 0].astype(f32)
                row = (2 * s + step) * count
                out_refs[number][pl.ds(pl.multiple_of(row, 16), count), :] = value.astype(bf16)
            else:
                out_ref[number, s, 0] = value

    if adds:
        for number in range(n_places):
            out_refs[number][2 * n_z * count :, :] = small_ref[...]


def attention_grads(n_places, info, grads, mixed, tokens, grad_attended, other=None, small=None):
    rows, width = grad_attended.shape
    n_z, buckets = mixed.shape[:2]
    mine = width // n_z
    count = mine // n_places
    parts = (n_places, n_z, 1, count, width)
    by_step = pl.BlockSpec(parts, lambda i, info: (0, 0, i, 0, 0))
    in_specs = [
        pl.BlockSpec((1, rows, width), lambda i, info: (jnp.minimum(info[i], 2), 0, 0)),
        fixed((n_z, buckets, mine, BUCKET)),
        pl.BlockSpec((rows, width), lambda i, info: (info[2], 0)),
        fixed((rows, width)),
    ]
    args = [grads, mixed, tokens, grad_attended]
    if other is None:
        shapes = [((n_places, n_z, 2, count, width), by_step)]
    else:
        in_specs += [by_step, fixed(small.shape)]
        args += [other, small]
        flat = (2 * n_z * count + small.shape[0], width)
        shapes = [(flat, fixed(flat))] * n_places
    return pl.pallas_call(
        functools.partial(attention_grads_kernel, n_places, other is not None),
        grid_spec=pltpu.PrefetchScalarGridSpec(
            num_scalar_prefetch=1,
            grid=(2,),
            in_specs=in_specs,
            out_specs=[spec for _, spec in shapes],
            scratch_shapes=[pltpu.VMEM((width, width), bf16)],
        ),
        out_shape=[jax.ShapeDtypeStruct(shape, bf16) for shape, _ in shapes],
        compiler_params=params(1),
        name="attention_grads",
        cost_estimate=cost(6),
    )(info, *args)


def together(*values):
    return lax.optimization_barrier(values)


def add(first, *others):
    total = first.astype(f32)
    for other in others:
        total = total + other.astype(f32)
    return total.astype(bf16)


class Plane:
    def __init__(self, n_dp, n_z):
        self.n_dp, self.n_z = n_dp, n_z
        self.n_group = min(n_dp, 8)
        self.n_places = self.n_group // 2
        self.dp = lax.axis_index("dp")
        self.z = lax.axis_index("tensor")
        self.index = lax.rem(self.dp, self.n_group)
        self.core = self.index & 1
        self.place = self.index >> 1

    def swap(self, array, bits):
        return lax.ppermute(array, "dp", [(i, i ^ bits) for i in range(self.n_dp)])

    def shift(self, array, by):
        n = self.n_z
        return lax.ppermute(array, "tensor", [(i, (i + by) % n) for i in range(n)])

    def gather(self, piece):
        if self.n_dp == self.n_group:
            whole = lax.all_gather(piece, ("tensor", "dp"))
            return whole.reshape((self.n_z, self.n_group) + piece.shape)
        groups = [
            list(range(i, i + self.n_group)) for i in range(0, self.n_dp, self.n_group)
        ]
        line = lax.all_gather(piece, "tensor")
        return lax.all_gather(line, "dp", axis=1, axis_index_groups=groups)

    def turned(self, array):
        bit = 1
        while bit < self.n_group:
            lead = array.reshape((-1, 2, bit) + array.shape[1:])
            array = jnp.where((self.index & bit) != 0, lead[:, ::-1], lead).reshape(array.shape)
            bit *= 2
        return array

    def to_places(self, parts):
        return [self.swap(parts[number], 2 * number) for number in range(1, self.n_places)]

    def from_places(self, own, arrived):
        found = jnp.stack([own] + arrived)
        bit = 1
        while bit < self.n_places:
            lead = found.reshape((-1, 2, bit) + own.shape)
            flipped = lead[:, ::-1]
            found = jnp.where((self.place & bit) != 0, flipped, lead).reshape(found.shape)
            bit *= 2
        return found

    def by_core(self, own, other):
        return jnp.where(
            self.core == 1, jnp.stack([other, own]), jnp.stack([own, other])
        )

    def over_groups(self, array):
        bit = self.n_group
        while bit < self.n_dp:
            array = add(array, self.swap(array, bit))
            bit *= 2
        return array


def on_device(
    n_dp,
    n_z,
    tokens,
    lengths,
    key_mask,
    query_weight,
    query_bias,
    key_weight,
    value_weight,
    value_bias,
    output_weight,
    output_bias,
    first_gain,
    first_shift,
    inner_weight,
    inner_bias,
    outer_weight,
    outer_bias,
    second_gain,
    second_shift,
    cotangent,
):
    width = tokens.shape[1]
    mine = query_weight.shape[1]
    units = inner_weight.shape[1]
    all_rows = tokens.shape[0]
    all_blocks = all_rows // BUCKET
    rows = all_rows // n_z
    plane = Plane(n_dp, n_z)
    z, core, place, index = plane.z, plane.core, plane.place, plane.index
    n_places = plane.n_places
    others = range(1, n_z)

    feed_rows = units // plane.n_group
    head_rows = mine // plane.n_group
    piece = jnp.concatenate(
        [
            lax.dynamic_slice_in_dim(inner_weight, index * feed_rows, feed_rows, 1).T,
            lax.dynamic_slice_in_dim(outer_weight, index * feed_rows, feed_rows, 0),
        ],
        axis=1,
    )
    line = [plane.shift(piece, s) for s in others]

    query_t, key_t, value_t = query_weight.T, key_weight.T, value_weight.T
    attention_own = jnp.concatenate([query_t, key_t, value_t, output_weight], axis=1)
    attention_weights = plane.gather(
        lax.dynamic_slice_in_dim(attention_own, index * head_rows, head_rows, 0)
    ).reshape(width, 4 * width)

    key_mask_rows = key_mask.reshape(all_blocks, 1, BUCKET)
    bias_row = jnp.concatenate([query_bias, value_bias, inner_bias])
    bias_rows = jnp.pad(bias_row, (0, 16 * BUCKET - bias_row.shape[0])).reshape(16, BUCKET)
    mixed = attend_forward(
        n_z, lengths, tokens, query_t, key_t, value_t, bias_rows, key_mask_rows
    )
    mixed, line = together(mixed, line)
    mixed = lax.all_to_all(mixed, "tensor", 0, 0)

    cut = feed_rows // 2
    near = [jnp.stack([part[:cut] for part in line]), jnp.stack([part[cut:] for part in line])]
    by_x, by_y = [plane.swap(half, 2) for half in near], [plane.swap(half, 4) for half in near]
    far = [plane.swap(by_x[0], 4), plane.swap(by_y[1], 2)]
    keep = near + by_x + by_y + far
    send = [plane.swap(half, 1) for half in near + by_x + by_y]
    far, send, mixed = together(far, send, mixed)
    keep = keep[:6] + far
    send = send + [plane.swap(half, 1) for half in far]
    own_units = jnp.concatenate([inner_weight.T, outer_weight], axis=1)

    biases = mixed[:, 0, mine:].reshape(n_z, -1)[:, : bias_row.shape[0]].astype(f32)
    head_biases = jnp.pad(
        jnp.stack([biases[:, :mine].reshape(-1), biases[:, mine : 2 * mine].reshape(-1)]),
        ((0, 6), (0, 0)),
    )
    inner_biases = biases[:, 2 * mine :]
    inner_biases = jnp.concatenate(
        [
            lax.dynamic_slice_in_dim(inner_biases, lax.rem(z + n_z - s, n_z), 1, 0)
            for s in range(n_z)
        ],
        axis=0,
    )
    inner_biases = inner_biases.reshape(n_z, plane.n_group, feed_rows).transpose(1, 0, 2)
    inner_biases = plane.turned(inner_biases).reshape(n_places, 2, 1, n_z * feed_rows)
    inner_biases = inner_biases.transpose(1, 0, 2, 3).reshape(plane.n_group, 1, -1)
    vectors = jnp.stack(
        [output_bias, first_gain, first_shift, outer_bias, second_gain, second_shift]
        + [jnp.zeros_like(output_bias)] * 2
    ).astype(f32)

    place_z = z.reshape(1)
    info = jnp.stack([z, place, core])
    (
        hidden, slope, my_output, normed_low, first_normed, first_scale, grad_second, grad_outer,
        second_sums,
    ) = feed_forward(
        info, lengths, mixed, attention_weights, tokens, cotangent, vectors, inner_biases,
        own_units, keep + send,
    )
    output = lax.all_gather(my_output, "tensor", axis=0, tiled=True)

    shared_args = (info, grad_outer, normed_low, hidden, slope, own_units)
    sent_a, bias_sent_a, grad_normed = feed_back(0, 2, *shared_args, grad_second, send[:4])
    other_a = plane.swap(sent_a, 1)
    sent_b, bias_sent_b, grad_normed = feed_back(2, 2, *shared_args, grad_normed, send[4:])
    grad_normed, other_a = together(grad_normed, other_a)
    other_b = plane.swap(sent_b, 1)
    (
        inner_stay, outer_stay, inner_go, outer_go, bias_kept, grad_first, grad_attended, first_sums
    ) = feed_back(
        0, 4, *shared_args, grad_normed, keep, [other_a, other_b],
        (first_normed, first_scale, vectors),
    )
    inner_came, outer_came = plane.swap(inner_go, 4), plane.swap(outer_go, 2)
    bias_grads = jnp.stack(
        [bias_kept[:, 0], jnp.concatenate([bias_sent_a, bias_sent_b])[:, 0]], axis=1
    )
    inner_bias_grad = plane.turned(bias_grads.reshape(plane.n_group, n_z, feed_rows))
    inner_bias_grad = inner_bias_grad.transpose(1, 0, 2)
    inner_bias_grad = jnp.concatenate(
        [
            sum(
                jnp.where(lax.rem(z - t + n_z, n_z) == s, inner_bias_grad[s : s + 1], 0.0)
                for s in range(n_z)
            )
            for t in range(n_z)
        ],
        axis=0,
    ).reshape(n_z, units)

    grads, my_tokens_grad, back_sums = attend_back(
        place_z, lengths, tokens, grad_attended, grad_first, attention_weights, head_biases,
        key_mask_rows,
    )
    grads, inner_came, outer_came, output = together(grads, inner_came, outer_came, output)
    inner_on, outer_on = (
        plane.swap(add(inner_stay[1], inner_came[1]), 2),
        plane.swap(add(outer_stay[1], outer_came[1]), 4),
    )
    tokens_grad = lax.all_gather(my_tokens_grad, "tensor", axis=0, tiled=True)

    def weight_grads(side, other=None, small=None):
        info = jnp.stack([2 * side, 2 * side + 1, z, place])
        return attention_grads(
            n_places, info, grads, mixed, tokens, grad_attended, other, small
        )

    (sent,) = weight_grads(1 - core)
    sent, inner_on, outer_on, back_sums, first_sums, second_sums, inner_bias_grad = together(
        sent, inner_on, outer_on, back_sums, first_sums, second_sums, inner_bias_grad
    )
    other = plane.swap(sent, 1)

    back_sums = jnp.sum(back_sums, axis=0)
    split = jnp.concatenate(
        [inner_bias_grad, back_sums[0].reshape(n_z, mine), back_sums[1].reshape(n_z, mine)], axis=1
    )
    small = jnp.concatenate([first_sums[:3], second_sums[:3], split.reshape(-1, width)], axis=0)
    small = jnp.pad(small, ((0, -small.shape[0] % 16), (0, 0))).astype(bf16)
    small_rows = small.shape[0]

    small = add(small, plane.swap(small, 1))
    feed_parts = [
        jnp.concatenate(
            [
                add(inner_stay[0, s], inner_came[0, s], inner_on[s]),
                add(outer_stay[0, s], outer_came[0, s], outer_on[s]),
            ],
            axis=1,
        )
        for s in range(n_z)
    ]
    feed_line = [plane.shift(feed_parts[s], -s) for s in others]
    kept = weight_grads(core, other, small)
    arrived = plane.to_places(kept)
    output = copied(output)
    arrived, feed_line, output = together(arrived, feed_line, output)
    small = add(small, *[a[-small_rows:] for a in arrived])
    count = 2 * mine // n_places
    attention_parts = [
        add(*[a[s * count : (s + 1) * count] for a in [kept[0]] + arrived]) for s in range(n_z)
    ]
    attention_line = [
        plane.shift(jnp.concatenate([attention_parts[s], small], axis=0), s) for s in others
    ]
    feed_total = plane.over_groups(add(feed_parts[0], *feed_line))
    feed_arrived = plane.to_places([feed_total] * n_places)
    attention_line, feed_arrived, tokens_grad = together(
        attention_line, feed_arrived, tokens_grad
    )
    attention_total = plane.over_groups(
        add(attention_parts[0], *[a[:count] for a in attention_line])
    )
    small = plane.over_groups(add(small, *[a[count:] for a in attention_line])).astype(f32)
    arrived = plane.to_places([attention_total] * n_places)
    feed_half = plane.from_places(feed_total, feed_arrived)
    feed_other = plane.swap(feed_half, 1)
    feed_grad = plane.by_core(feed_half, feed_other).transpose(1, 0, 2, 3).reshape(units, -1)
    inner_grad = feed_grad[:, :width].T.astype(f32)
    outer_grad = feed_grad[:, width:].astype(f32)
    arrived, inner_grad, outer_grad = together(arrived, inner_grad, outer_grad)
    attention_half = plane.from_places(attention_total, arrived)
    attention_other = plane.swap(attention_half, 1)
    grad_list = plane.by_core(attention_half, attention_other)
    grad_list = grad_list.reshape(2, n_places, 2, mine // n_places, width)
    grad_list = grad_list.transpose(0, 2, 1, 3, 4).reshape(4, mine, width)

    shared = small[:6]
    split_rows = n_z * split.shape[1] // width
    split = lax.dynamic_slice_in_dim(
        small[6 : 6 + split_rows].reshape(n_z, -1), z, 1, 0
    )[0]

    return (
        output,
        tokens_grad,
        grad_list[0].T.astype(f32),
        split[units : units + mine],
        grad_list[1].T.astype(f32),
        grad_list[2].T.astype(f32),
        split[units + mine :],
        grad_list[3].astype(f32),
        shared[0],
        shared[1],
        shared[2],
        inner_grad,
        split[:units],
        outer_grad,
        shared[3],
        shared[4],
        shared[5],
    )


def solution(mesh):
    n_dp, n_z = mesh.shape["dp"], mesh.shape["tensor"]
    in_specs = (
        P("dp", None),
        P("dp", None),
        P("dp"),
        P(None, "tensor"),
        P("tensor"),
        P(None, "tensor"),
        P(None, "tensor"),
        P("tensor"),
        P("tensor", None),
        P(),
        P(),
        P(),
        P(None, "tensor"),
        P("tensor"),
        P("tensor", None),
        P(),
        P(),
        P(),
        P("dp", None),
    )
    out_specs = (
        P("dp", None),
        P("dp", None),
        P(None, "tensor"),
        P("tensor"),
        P(None, "tensor"),
        P(None, "tensor"),
        P("tensor"),
        P("tensor", None),
        P(),
        P(),
        P(),
        P(None, "tensor"),
        P("tensor"),
        P("tensor", None),
        P(),
        P(),
        P(),
    )

    def program(*args):
        return on_device(n_dp, n_z, *args)

    return jax.shard_map(
        program, mesh=mesh, in_specs=in_specs, out_specs=out_specs, check_vma=False
    )
```

```python
import functools

import jax
import jax.numpy as jnp
from jax import lax
from jax.experimental import pallas as pl
from jax.experimental.pallas import tpu as pltpu
from jax.sharding import PartitionSpec as P

HEAD = 64
BUCKET = 512
ITEMS = 8


negative_fill = -1e30
epsilon = 1e-06
f32 = jnp.float32
bf16 = jnp.bfloat16
VMEM_BYTES = 56 * 1024 * 1024


def dot(left, right):
    return jnp.dot(left, right, preferred_element_type=f32)


def contract_rows(left, right):
    return lax.dot_general(left, right, (((0,), (0,)), ((), ())), preferred_element_type=f32)


def contract_cols(left, right):
    return lax.dot_general(left, right, (((1,), (1,)), ((), ())), preferred_element_type=f32)


def norm_rows(values):
    centred = values - jnp.mean(values, axis=1, keepdims=True)
    inv_scale = lax.rsqrt(jnp.mean(centred * centred, axis=1, keepdims=True) + epsilon)
    return centred * inv_scale, inv_scale


def norm_back(grad_rows, norm_gain, normed, inv_scale):
    scaled = grad_rows * norm_gain
    return inv_scale * (
        scaled
        - jnp.mean(scaled, axis=1, keepdims=True)
        - normed * jnp.mean(scaled * normed, axis=1, keepdims=True)
    )


def column_sum(matrix):
    return jnp.sum(matrix.astype(f32), axis=0, keepdims=True)


def fixed(shape):
    return pl.BlockSpec(shape, lambda *_: (0,) * len(shape))


def cost(microseconds):
    return pl.CostEstimate(
        flops=int(microseconds * 2.5e8),
        bytes_accessed=int(microseconds * 2.5e5),
        transcendentals=0,
    )


def params(axes):
    return pltpu.CompilerParams(
        dimension_semantics=("arbitrary",) * axes, vmem_limit_bytes=VMEM_BYTES
    )


def item_places(lengths_ref, row, shape, axis):
    places = lax.broadcasted_iota(jnp.int32, shape, axis)
    end = jnp.int32(0)
    items = jnp.zeros(shape, jnp.int32)
    for slot in range(ITEMS):
        end = end + lengths_ref[row, slot]
        items = items + (places >= end).astype(jnp.int32)
    return items


def as_column(row):
    return jnp.broadcast_to(row.astype(f32), (8, row.shape[1])).T[:, :1]


def mask_bias(lengths_ref, row, key_mask):
    shape = (BUCKET, BUCKET)
    diagonal = lax.broadcasted_iota(jnp.int32, shape, 0) == lax.broadcasted_iota(
        jnp.int32, shape, 1
    )
    item_row = item_places(lengths_ref, row, (1, BUCKET), 1)
    item_column = item_places(lengths_ref, row, (BUCKET, 1), 0)
    code_column = jnp.where(as_column(key_mask) == 1.0, item_column, -1)
    return jnp.where((code_column == item_row) | diagonal, 0.0, negative_fill).astype(f32)


def attend_forward_kernel(
    lengths_ref, tokens_ref, query_ref, key_ref, value_ref, biases_ref, key_mask_ref, mixed_ref,
):
    mine = query_ref.shape[0]
    rows = tokens_ref[...]
    queries = contract_cols(query_ref[...], rows) + as_column(biases_ref[0:1, :mine])
    queries = (queries.astype(bf16) * HEAD ** (-0.5)).astype(bf16)
    keys = contract_cols(rows, key_ref[...]).astype(bf16)
    values = contract_cols(value_ref[...], rows) + as_column(biases_ref[0:1, mine : 2 * mine])
    values = values.astype(bf16)
    bias = mask_bias(lengths_ref, pl.program_id(0), key_mask_ref[0])
    for head in range(mine // HEAD):
        at = slice(head * HEAD, (head + 1) * HEAD)
        scores = dot(keys[:, at], queries[at]) + bias
        exponent = jnp.exp(scores - jnp.max(scores, axis=0, keepdims=True))
        total = jnp.sum(exponent, axis=0, keepdims=True)
        mixed_ref[0, 0, at] = (dot(values[at], exponent.astype(bf16)) / total).astype(bf16)
    mixed_ref[0, 0, mine:] = biases_ref[...]


def attend_forward(n_z, lengths, tokens, query, key, value, biases, key_mask):
    blocks = lengths.shape[0]
    own = blocks // n_z
    mine, width = key.shape
    whole = (n_z, own, mine + biases.shape[0], BUCKET)
    return pl.pallas_call(
        attend_forward_kernel,
        grid=(blocks,),
        in_specs=[
            pl.BlockSpec(memory_space=pltpu.SMEM),
            pl.BlockSpec((BUCKET, width), lambda b: (b, 0)),
            fixed((mine, width)),
            fixed((mine, width)),
            fixed((mine, width)),
            fixed(biases.shape),
            pl.BlockSpec((1, 1, BUCKET), lambda b: (b, 0, 0)),
        ],
        out_specs=pl.BlockSpec((1, 1) + whole[2:], lambda b: (b // own, b % own, 0, 0)),
        out_shape=jax.ShapeDtypeStruct(whole, bf16),
        compiler_params=params(1),
        name="attend_forward",
        cost_estimate=cost(12),
    )(lengths, tokens, query, key, value, biases, key_mask)


def fetch_units(step, picks, own_ref, halves, units, sems):
    feed_rows, twice = units.shape[2:]
    cut = feed_rows // 2

    def copies(number):
        slot = number % 2
        row = pl.multiple_of(picks[number] * feed_rows, 16)
        ends = [
            (own_ref.at[pl.ds(row, feed_rows), :twice], units.at[slot, 0]),
            (halves[number][0].at[:, :, :twice], units.at[slot, 1:, :cut]),
            (halves[number][1].at[:, :, :twice], units.at[slot, 1:, cut:]),
        ]
        return [
            pltpu.make_async_copy(source, target, sems.at[slot, i])
            for i, (source, target) in enumerate(ends)
        ]

    for number in range(len(halves)):

        @pl.when(step == number)
        def _(number=number):
            if number == 0:
                for copy in copies(0):
                    copy.start()
            if number + 1 < len(halves):
                for copy in copies(number + 1):
                    copy.start()
            for copy in copies(number):
                copy.wait()

    return units.at[lax.rem(step, 2)]


def fetch_mixer(picks, own_ref, halves, mixer, sems):
    feed_rows = mixer.shape[1] // 8
    cut = feed_rows // 2
    start = own_ref.shape[1] - mixer.shape[2]
    ends = [(own_ref.at[:, start:], mixer.at[0])]
    for number, pair in enumerate(halves):
        for half in range(2):
            row = pl.multiple_of(picks[number] * feed_rows + half * cut, 16)
            ends.append((pair[half].at[:, :, start:], mixer.at[1:, pl.ds(row, cut)]))
    copies = [
        pltpu.make_async_copy(source, target, sems.at[i])
        for i, (source, target) in enumerate(ends)
    ]
    for copy in copies:
        copy.start()
    for copy in copies:
        copy.wait()


def split_units(units):
    width = units.shape[2] // 2
    return units[:, :, :width].reshape(-1, width), units[:, :, width:].reshape(-1, width)


ANYWHERE = pl.BlockSpec(memory_space=pl.ANY)


def feed_forward_kernel(
    info_ref, lengths_ref, mixed_ref, tokens_ref, cotangent_ref, vectors_ref, bias_ref, own_ref,
    *rest,
):
    halves, rest = list(zip(rest[:16:2], rest[1:16:2])), rest[16:]
    (
        hidden_ref, slope_ref, output_ref, normed_low_ref, first_normed_ref, first_scale_ref,
        grad_second_ref, grad_outer_ref, sums_ref, second_sum, units, sems,
        mixer, mixer_sems,
    ) = rest
    step = pl.program_id(0)
    picks = [(info_ref[1] ^ (k % 4)) * 2 + (info_ref[2] ^ (k // 4)) for k in range(8)]
    weights = fetch_units(step, picks, own_ref, halves, units, sems)
    output_bias, first_gain, first_shift, outer_bias, second_gain, second_shift = (
        vectors_ref[i : i + 1, :] for i in range(6)
    )

    @pl.when(step == 0)
    def _():
        fetch_mixer(picks, own_ref, halves, mixer, mixer_sems)
        n_z, own, mine, _ = mixed_ref.shape
        attended = output_bias + jnp.concatenate(
            [
                sum(
                    dot(mixer[s, :, :mine], mixed_ref[lax.rem(info_ref[0] + n_z - s, n_z), b])
                    for s in range(n_z)
                ).T
                for b in range(own)
            ],
            axis=0,
        )
        normed, inv_scale = norm_rows(tokens_ref[...].astype(f32) + attended)
        whole = normed * first_gain + first_shift
        first_normed_ref[...] = normed
        first_scale_ref[...] = inv_scale
        normed_low_ref[...] = whole.astype(bf16)
        second_sum[...] = whole + outer_bias

    inner, outer = split_units(weights)
    inner_pre = contract_cols(normed_low_ref[...], inner) + bias_ref[0]
    normal_cdf = 0.5 + 0.5 * lax.erf(inner_pre * 0.7071067811865476)
    density = jnp.exp(-0.5 * inner_pre * inner_pre) * 0.3989422804014327
    hidden = (inner_pre * normal_cdf).astype(bf16)
    hidden_ref[...] = hidden
    slope_ref[...] = (normal_cdf + inner_pre * density).astype(bf16)
    second_sum[...] += dot(hidden, outer)

    @pl.when(step == pl.num_programs(0) - 1)
    def _():
        normed, inv_scale = norm_rows(second_sum[...])
        blocks = normed.shape[0] // BUCKET
        live = jnp.concatenate(
            [
                (item_places(lengths_ref, info_ref[0] * blocks + b, (BUCKET, 1), 0) < ITEMS)
                for b in range(blocks)
            ],
            axis=0,
        ).astype(f32)
        output_ref[...] = ((normed * second_gain + second_shift) * live).astype(bf16)
        grad_final = cotangent_ref[...].astype(f32) * live
        grad_second = norm_back(grad_final, second_gain, normed, inv_scale)
        grad_outer = grad_second.astype(bf16)
        grad_second_ref[...] = grad_second
        grad_outer_ref[...] = grad_outer
        sums_ref[0:1, :] = column_sum(grad_outer)
        sums_ref[1:2, :] = column_sum(grad_final * normed)
        sums_ref[2:3, :] = column_sum(grad_final)


def feed_forward(info, lengths, mixed, tokens, cotangent, vectors, biases, own, halves):
    n_z, buckets = mixed.shape[:2]
    rows = buckets * BUCKET
    width = tokens.shape[1]
    mine = width // n_z
    feed_rows, twice = own.shape[0] // 8, 2 * width
    chunk = n_z * feed_rows
    whole = fixed((rows, width))
    my_rows = pl.BlockSpec((rows, width), lambda j, info: (info[0], 0))
    columns = pl.BlockSpec((rows, chunk), lambda j, info: (0, j))
    shapes = [
        ((rows, 8 * chunk), bf16, columns),
        ((rows, 8 * chunk), bf16, columns),
        ((rows, width), bf16, whole),
        ((rows, width), bf16, whole),
        ((rows, width), f32, whole),
        ((rows, 1), f32, fixed((rows, 1))),
        ((rows, width), f32, whole),
        ((rows, width), bf16, whole),
        ((8, width), f32, fixed((8, width))),
    ]
    return pl.pallas_call(
        feed_forward_kernel,
        grid_spec=pltpu.PrefetchScalarGridSpec(
            num_scalar_prefetch=1,
            grid=(8,),
            in_specs=[
                pl.BlockSpec(memory_space=pltpu.SMEM),
                fixed((n_z, buckets, mine, BUCKET)),
                my_rows,
                my_rows,
                fixed((8, width)),
                pl.BlockSpec((1, 1, chunk), lambda j, info: (j, 0, 0)),
                ANYWHERE,
            ]
            + [ANYWHERE] * 16,
            out_specs=[spec for _, _, spec in shapes],
            scratch_shapes=[
                pltpu.VMEM((rows, width), f32),
                pltpu.VMEM((2, n_z, feed_rows, twice), bf16),
                pltpu.SemaphoreType.DMA((2, 3)),
                pltpu.VMEM((n_z, width, own.shape[1] - twice), bf16),
                pltpu.SemaphoreType.DMA((17,)),
            ],
        ),
        out_shape=[jax.ShapeDtypeStruct(shape, kind) for shape, kind, _ in shapes],
        compiler_params=params(1),
        name="feed_forward",
        cost_estimate=cost(21),
    )(info, lengths, mixed, tokens, cotangent, vectors, biases, own, *halves)


STAY = ((0, 1), (0, 2))
GO = ((2, 3), (1, 3))


def feed_back_kernel(
    first, count, keeps, info_ref, grad_outer_ref, normed_low_ref, hidden_ref, slope_ref,
    own_ref, start_ref, *rest,
):
    halves = list(zip(rest[: 2 * count : 2], rest[1 : 2 * count : 2]))
    rest = rest[2 * count :]
    if keeps:
        other_refs, norm_refs, rest = rest[:2], rest[2:5], rest[5:]
        stay_refs, go_refs, rest = rest[0:2], rest[2:4], rest[4:]
        bias_grad_ref, grad_first_ref, grad_attended_ref, sums_ref, units, sems = rest[:6]
        grad_normed_ref = rest[6]
    else:
        grad_ref, bias_grad_ref, grad_normed_ref, units, sems = rest
    step = pl.program_id(0)
    side = info_ref[2] if keeps else 1 - info_ref[2]
    picks = [(info_ref[1] ^ (first + k)) * 2 + side for k in range(count)]
    weights = fetch_units(step, picks, own_ref, halves, units, sems)

    @pl.when(step == 0)
    def _():
        grad_normed_ref[...] = start_ref[...]

    n_z, feed_rows, twice = weights.shape
    width = twice // 2
    inner, outer = split_units(weights)
    grad_outer = grad_outer_ref[...]
    grad_hidden = contract_cols(grad_outer, outer)
    grad_inner = (grad_hidden * slope_ref[...].astype(f32)).astype(bf16)
    outer_grad = contract_rows(hidden_ref[...], grad_outer).reshape(n_z, feed_rows, width)
    inner_grad = contract_rows(grad_inner, normed_low_ref[...]).reshape(n_z, feed_rows, width)
    bias_grad_ref[0] = column_sum(grad_inner)
    grad_normed_ref[...] += dot(grad_inner, inner)

    if keeps:
        for number in range(4):

            @pl.when(step == number)
            def _(number=number):
                other_ref = other_refs[number // 2]
                for track, value in enumerate((inner_grad, outer_grad)):
                    at = slice(track * width, (track + 1) * width)
                    value = (value + other_ref[0, :, :, at].astype(f32)).astype(bf16)
                    ref = stay_refs[track] if number in STAY[track] else go_refs[track]
                    ref[0] = value

        @pl.when(step == pl.num_programs(0) - 1)
        def _():
            first_normed_ref, first_scale_ref, vectors_ref = norm_refs
            grad_rows, normed = grad_normed_ref[...], first_normed_ref[...]
            grad_first = norm_back(grad_rows, vectors_ref[1:2, :], normed, first_scale_ref[...])
            grad_attended = grad_first.astype(bf16)
            grad_first_ref[...] = grad_first
            grad_attended_ref[...] = grad_attended
            sums_ref[0:1, :] = column_sum(grad_attended)
            sums_ref[1:2, :] = column_sum(grad_rows * normed)
            sums_ref[2:3, :] = column_sum(grad_rows)

    else:
        grad_ref[0, :, :, :width] = inner_grad.astype(bf16)
        grad_ref[0, :, :, width:] = outer_grad.astype(bf16)


def feed_back(
    first, count, info, grad_outer, normed_low, hidden, slope, own, start, halves,
    others=None, norm=None,
):
    rows, width = grad_outer.shape
    keeps = others is not None
    feed_rows, twice = own.shape[0] // 8, 2 * width
    n_z = halves[0].shape[0] + 1
    chunk = n_z * feed_rows
    flip = 0 if keeps else 1
    columns = pl.BlockSpec((rows, chunk), lambda i, info: (0, 4 * flip + first + i))
    whole = fixed((rows, width))
    part = (n_z, feed_rows, twice)
    track = (2, n_z, feed_rows, width)
    in_specs = [whole, whole, columns, columns, ANYWHERE, whole] + [ANYWHERE] * (2 * count)
    args = [grad_outer, normed_low, hidden, slope, own, start] + halves
    bias_shape = (
        (count, 1, chunk),
        f32,
        pl.BlockSpec((1, 1, chunk), lambda i, info: (i, 0, 0)),
    )
    scratch = [pltpu.VMEM((2,) + part, bf16), pltpu.SemaphoreType.DMA((2, 3))]

    def one(shape, at):
        return pl.BlockSpec((1,) + shape[1:], lambda i, info: (at(i), 0, 0, 0))

    if keeps:
        early, late = (lambda i: jnp.minimum(i, 1)), (lambda i: jnp.maximum(i - 2, 0))
        in_specs += [one((2,) + part, early), one((2,) + part, late)]
        in_specs += [whole, fixed((rows, 1)), fixed((8, width))]
        args += others + list(norm)
        slow, slower = (lambda i: i // 2), (lambda i: jnp.maximum(i - 1, 0) // 2)
        shapes = [(track, bf16, one(track, at)) for at in (early, slow, late, slower)] + [
            bias_shape,
            ((rows, width), f32, whole),
            ((rows, width), bf16, whole),
            ((8, width), f32, fixed((8, width))),
        ]
        scratch.append(pltpu.VMEM((rows, width), f32))
    else:
        shapes = [
            ((count,) + part, bf16, one((count,) + part, lambda i: i)),
            bias_shape,
            ((rows, width), f32, whole),
        ]
    return pl.pallas_call(
        functools.partial(feed_back_kernel, first, count, keeps),
        grid_spec=pltpu.PrefetchScalarGridSpec(
            num_scalar_prefetch=1,
            grid=(count,),
            in_specs=in_specs,
            out_specs=[spec for _, _, spec in shapes],
            scratch_shapes=scratch,
        ),
        out_shape=[jax.ShapeDtypeStruct(shape, kind) for shape, kind, _ in shapes],
        compiler_params=params(1),
        name="feed_back_own" if keeps else "feed_back",
        cost_estimate=cost(3 * count),
    )(info, *args)


def copy_kernel(from_ref, to_ref):
    to_ref[...] = from_ref[...]


def copied(array):
    block = pl.BlockSpec((BUCKET, array.shape[1]), lambda i: (i, 0))
    return pl.pallas_call(
        copy_kernel,
        grid=(array.shape[0] // BUCKET,),
        in_specs=[block],
        out_specs=block,
        out_shape=jax.ShapeDtypeStruct(array.shape, array.dtype),
        compiler_params=params(1),
        name="copied",
        cost_estimate=cost(2),
    )(array)


def attend_back_kernel(
    place_ref, lengths_ref, tokens_ref, grad_attended_ref, grad_first_ref, weights_ref, biases_ref,
    key_mask_ref,
    grads_ref, tokens_grad_ref, sums_ref,
    bias, total_grad,
):
    pair = pl.program_id(1)

    @pl.when(pair == 0)
    def _():
        row = place_ref[0] * pl.num_programs(0) + pl.program_id(0)
        bias[...] = mask_bias(lengths_ref, row, key_mask_ref[0])
        total_grad[...] = grad_first_ref[...]

    rows, grad_attended = tokens_ref[...], grad_attended_ref[...]
    width = rows.shape[1]
    query_w, key_w, value_w, output_w = (
        weights_ref[:, i * width : (i + 1) * width] for i in range(4)
    )
    queries = contract_cols(query_w, rows) + as_column(biases_ref[0:1, :])
    queries = (queries.astype(bf16) * HEAD ** (-0.5)).astype(bf16)
    keys = contract_cols(rows, key_w).astype(bf16)
    values = (contract_cols(rows, value_w) + biases_ref[1:2, :]).astype(bf16)
    grad_mixed = contract_cols(output_w, grad_attended).astype(bf16)
    keys_t = keys.T
    grad_queries, grad_keys, grad_values = [], [], []
    for head in range(keys.shape[1] // HEAD):
        at = slice(head * HEAD, (head + 1) * HEAD)
        scores = dot(keys[:, at], queries[at]) + bias[...]
        exponent = jnp.exp(scores - jnp.max(scores, axis=0, keepdims=True))
        probs = exponent * (1.0 / jnp.sum(exponent, axis=0, keepdims=True))
        grad_probs = dot(values[:, at], grad_mixed[at])
        shift = jnp.sum(probs * grad_probs, axis=0, keepdims=True)
        grad_scores = (probs * (grad_probs - shift)).astype(bf16)
        grad_values.append(contract_cols(probs.astype(bf16), grad_mixed[at]))
        grad_keys.append(contract_cols(grad_scores, queries[at]))
        grad_queries.append(dot(keys_t[at], grad_scores) * HEAD ** (-0.5))
    grad_query = jnp.concatenate(grad_queries, axis=0).T.astype(bf16)
    grad_key = jnp.concatenate(grad_keys, axis=1).astype(bf16)
    grad_value = jnp.concatenate(grad_values, axis=1).astype(bf16)
    grads_ref[0] = grad_query
    grads_ref[1] = grad_key
    grads_ref[2] = grad_value
    sums_ref[0, 0:1, :] = column_sum(grad_query)
    sums_ref[0, 1:2, :] = column_sum(grad_value)
    total_grad[...] += dot(grad_query, query_w) + dot(grad_key, key_w) + dot(grad_value, value_w)

    @pl.when(pair == pl.num_programs(1) - 1)
    def _():
        tokens_grad_ref[...] = total_grad[...].astype(bf16)


def attend_back(
    place, lengths, tokens, grad_attended, grad_first, weights, biases, key_mask
):
    rows, width = grad_attended.shape
    blocks = rows // BUCKET
    pair = 2 * HEAD
    own = lambda b, h, place: (place[0] * blocks + b, 0)
    by_bucket = pl.BlockSpec((BUCKET, width), lambda b, h, place: (b, 0))
    by_pair = lambda b, h, place: (h, 0)
    return pl.pallas_call(
        attend_back_kernel,
        grid_spec=pltpu.PrefetchScalarGridSpec(
            num_scalar_prefetch=1,
            grid=(blocks, width // pair),
            in_specs=[
                pl.BlockSpec(memory_space=pltpu.SMEM),
                pl.BlockSpec((BUCKET, width), own),
                by_bucket,
                by_bucket,
                pl.BlockSpec((pair, 4 * width), by_pair),
                pl.BlockSpec((8, pair), lambda b, h, place: (0, h)),
                pl.BlockSpec((1, 1, BUCKET), lambda b, h, place: (place[0] * blocks + b, 0, 0)),
            ],
            out_specs=[
                pl.BlockSpec((3, BUCKET, pair), lambda b, h, place: (0, b, h)),
                by_bucket,
                pl.BlockSpec((1, 8, pair), lambda b, h, place: (b, 0, h)),
            ],
            scratch_shapes=[pltpu.VMEM((BUCKET, BUCKET), f32), pltpu.VMEM((BUCKET, width), f32)],
        ),
        out_shape=[
            jax.ShapeDtypeStruct((3, rows, width), bf16),
            jax.ShapeDtypeStruct((rows, width), bf16),
            jax.ShapeDtypeStruct((blocks, 8, width), f32),
        ],
        compiler_params=params(2),
        name="attend_back",
        cost_estimate=cost(26),
    )(
        place, lengths, tokens, grad_attended, grad_first, weights, biases, key_mask
    )


def attention_grads_kernel(
    n_places, adds, info_ref, grads_ref, mixed_ref, tokens_ref, grad_attended_ref, *rest
):
    if adds:
        other_ref, small_ref = rest[:2]
        out_refs, whole = rest[2:-1], rest[-1]
    else:
        (out_ref, whole) = rest
    step = pl.program_id(0)
    which = info_ref[step]
    n_z, buckets, mine, _ = mixed_ref.shape
    count = mine // n_places

    @pl.when(which < 3)
    def _():
        whole[...] = contract_rows(grads_ref[0], tokens_ref[...]).astype(bf16)

    @pl.when(which == 3)
    def _():
        for t in range(n_z):
            whole[t * mine : (t + 1) * mine, :] = sum(
                dot(mixed_ref[t, b], grad_attended_ref[b * BUCKET : (b + 1) * BUCKET, :])
                for b in range(buckets)
            ).astype(bf16)

    for number in range(n_places):
        for s in range(n_z):
            start = lax.rem(info_ref[2] + s, n_z) * mine + (info_ref[3] ^ number) * count
            value = whole[pl.ds(pl.multiple_of(start, 16), count), :]
            if adds:
                value = value.astype(f32) + other_ref[number, s, 0].astype(f32)
                row = (2 * s + step) * count
                out_refs[number][pl.ds(pl.multiple_of(row, 16), count), :] = value.astype(bf16)
            else:
                out_ref[number, s, 0] = value

    if adds:
        for number in range(n_places):
            out_refs[number][2 * n_z * count :, :] = small_ref[...]


def attention_grads(n_places, info, grads, mixed, tokens, grad_attended, other=None, small=None):
    rows, width = grad_attended.shape
    n_z, buckets = mixed.shape[:2]
    mine = width // n_z
    count = mine // n_places
    parts = (n_places, n_z, 1, count, width)
    by_step = pl.BlockSpec(parts, lambda i, info: (0, 0, i, 0, 0))
    in_specs = [
        pl.BlockSpec((1, rows, width), lambda i, info: (jnp.minimum(info[i], 2), 0, 0)),
        fixed((n_z, buckets, mine, BUCKET)),
        pl.BlockSpec((rows, width), lambda i, info: (info[2], 0)),
        fixed((rows, width)),
    ]
    args = [grads, mixed, tokens, grad_attended]
    if other is None:
        shapes = [((n_places, n_z, 2, count, width), by_step)]
    else:
        in_specs += [by_step, fixed(small.shape)]
        args += [other, small]
        flat = (2 * n_z * count + small.shape[0], width)
        shapes = [(flat, fixed(flat))] * n_places
    return pl.pallas_call(
        functools.partial(attention_grads_kernel, n_places, other is not None),
        grid_spec=pltpu.PrefetchScalarGridSpec(
            num_scalar_prefetch=1,
            grid=(2,),
            in_specs=in_specs,
            out_specs=[spec for _, spec in shapes],
            scratch_shapes=[pltpu.VMEM((width, width), bf16)],
        ),
        out_shape=[jax.ShapeDtypeStruct(shape, bf16) for shape, _ in shapes],
        compiler_params=params(1),
        name="attention_grads",
        cost_estimate=cost(6),
    )(info, *args)


def together(*values):
    return lax.optimization_barrier(values)


def add(first, *others):
    total = first.astype(f32)
    for other in others:
        total = total + other.astype(f32)
    return total.astype(bf16)


class Plane:
    def __init__(self, n_dp, n_z):
        self.n_dp, self.n_z = n_dp, n_z
        self.n_group = min(n_dp, 8)
        self.n_places = self.n_group // 2
        self.dp = lax.axis_index("dp")
        self.z = lax.axis_index("tensor")
        self.index = lax.rem(self.dp, self.n_group)
        self.core = self.index & 1
        self.place = self.index >> 1

    def swap(self, array, bits):
        return lax.ppermute(array, "dp", [(i, i ^ bits) for i in range(self.n_dp)])

    def shift(self, array, by):
        n = self.n_z
        return lax.ppermute(array, "tensor", [(i, (i + by) % n) for i in range(n)])

    def gather(self, piece):
        if self.n_dp == self.n_group:
            whole = lax.all_gather(piece, ("tensor", "dp"))
            return whole.reshape((self.n_z, self.n_group) + piece.shape)
        groups = [
            list(range(i, i + self.n_group)) for i in range(0, self.n_dp, self.n_group)
        ]
        line = lax.all_gather(piece, "tensor")
        return lax.all_gather(line, "dp", axis=1, axis_index_groups=groups)

    def turned(self, array):
        bit = 1
        while bit < self.n_group:
            lead = array.reshape((-1, 2, bit) + array.shape[1:])
            array = jnp.where((self.index & bit) != 0, lead[:, ::-1], lead).reshape(array.shape)
            bit *= 2
        return array

    def to_places(self, parts):
        return [self.swap(parts[number], 2 * number) for number in range(1, self.n_places)]

    def from_places(self, own, arrived):
        found = jnp.stack([own] + arrived)
        bit = 1
        while bit < self.n_places:
            lead = found.reshape((-1, 2, bit) + own.shape)
            flipped = lead[:, ::-1]
            found = jnp.where((self.place & bit) != 0, flipped, lead).reshape(found.shape)
            bit *= 2
        return found

    def by_core(self, own, other):
        return jnp.where(
            self.core == 1, jnp.stack([other, own]), jnp.stack([own, other])
        )

    def over_groups(self, array):
        bit = self.n_group
        while bit < self.n_dp:
            array = add(array, self.swap(array, bit))
            bit *= 2
        return array


def on_device(
    n_dp,
    n_z,
    tokens,
    lengths,
    key_mask,
    query_weight,
    query_bias,
    key_weight,
    value_weight,
    value_bias,
    output_weight,
    output_bias,
    first_gain,
    first_shift,
    inner_weight,
    inner_bias,
    outer_weight,
    outer_bias,
    second_gain,
    second_shift,
    cotangent,
):
    width = tokens.shape[1]
    mine = query_weight.shape[1]
    units = inner_weight.shape[1]
    all_rows = tokens.shape[0]
    all_blocks = all_rows // BUCKET
    rows = all_rows // n_z
    plane = Plane(n_dp, n_z)
    z, core, place, index = plane.z, plane.core, plane.place, plane.index
    n_places = plane.n_places
    others = range(1, n_z)

    mixer_t = jnp.pad(output_weight.T, ((0, 0), (0, -mine % 128)))
    feed_rows = units // plane.n_group
    head_rows = mine // plane.n_group
    piece = jnp.concatenate(
        [
            lax.dynamic_slice_in_dim(inner_weight, index * feed_rows, feed_rows, 1).T,
            lax.dynamic_slice_in_dim(outer_weight, index * feed_rows, feed_rows, 0),
            lax.dynamic_slice_in_dim(mixer_t, index * feed_rows, feed_rows, 0),
        ],
        axis=1,
    )
    line = [plane.shift(piece, s) for s in others]

    query_t, key_t, value_t = query_weight.T, key_weight.T, value_weight.T
    attention_own = jnp.concatenate([query_t, key_t, value_t, output_weight], axis=1)
    attention_weights = plane.gather(
        lax.dynamic_slice_in_dim(attention_own, index * head_rows, head_rows, 0)
    ).reshape(width, 4 * width)

    key_mask_rows = key_mask.reshape(all_blocks, 1, BUCKET)
    bias_row = jnp.concatenate([query_bias, value_bias, inner_bias])
    bias_rows = jnp.pad(bias_row, (0, 16 * BUCKET - bias_row.shape[0])).reshape(16, BUCKET)
    mixed = attend_forward(
        n_z, lengths, tokens, query_t, key_t, value_t, bias_rows, key_mask_rows
    )
    mixed, line = together(mixed, line)

    cut = feed_rows // 2
    near = [jnp.stack([part[:cut] for part in line]), jnp.stack([part[cut:] for part in line])]
    by_x, by_y = [plane.swap(half, 2) for half in near], [plane.swap(half, 4) for half in near]
    by_x[0], by_y[1], mixed = together(by_x[0], by_y[1], mixed)
    far = [plane.swap(by_x[0], 4), plane.swap(by_y[1], 2)]
    by_x[1], by_y[0], mixed = together(by_x[1], by_y[0], mixed)
    mixed = lax.all_to_all(mixed, "tensor", 0, 0)
    keep = near + by_x + by_y + far
    send = [plane.swap(half, 1) for half in near + by_x + by_y]
    far, send, mixed = together(far, send, mixed)
    keep = keep[:6] + far
    send = send + [plane.swap(half, 1) for half in far]
    own_units = jnp.concatenate([inner_weight.T, outer_weight, mixer_t], axis=1)

    biases = mixed[:, 0, mine:].reshape(n_z, -1)[:, : bias_row.shape[0]].astype(f32)
    head_biases = jnp.pad(
        jnp.stack([biases[:, :mine].reshape(-1), biases[:, mine : 2 * mine].reshape(-1)]),
        ((0, 6), (0, 0)),
    )
    inner_biases = biases[:, 2 * mine :]
    inner_biases = jnp.concatenate(
        [
            lax.dynamic_slice_in_dim(inner_biases, lax.rem(z + n_z - s, n_z), 1, 0)
            for s in range(n_z)
        ],
        axis=0,
    )
    inner_biases = inner_biases.reshape(n_z, plane.n_group, feed_rows).transpose(1, 0, 2)
    inner_biases = plane.turned(inner_biases).reshape(n_places, 2, 1, n_z * feed_rows)
    inner_biases = inner_biases.transpose(1, 0, 2, 3).reshape(plane.n_group, 1, -1)
    vectors = jnp.stack(
        [output_bias, first_gain, first_shift, outer_bias, second_gain, second_shift]
        + [jnp.zeros_like(output_bias)] * 2
    ).astype(f32)

    place_z = z.reshape(1)
    info = jnp.stack([z, place, core])
    (
        hidden, slope, my_output, normed_low, first_normed, first_scale, grad_second, grad_outer,
        second_sums,
    ) = feed_forward(
        info, lengths, mixed, tokens, cotangent, vectors, inner_biases, own_units, keep + send
    )
    output = lax.all_gather(my_output, "tensor", axis=0, tiled=True)

    shared_args = (info, grad_outer, normed_low, hidden, slope, own_units)
    sent_a, bias_sent_a, grad_normed = feed_back(0, 2, *shared_args, grad_second, send[:4])
    other_a = plane.swap(sent_a, 1)
    sent_b, bias_sent_b, grad_normed = feed_back(2, 2, *shared_args, grad_normed, send[4:])
    grad_normed, other_a = together(grad_normed, other_a)
    other_b = plane.swap(sent_b, 1)
    (
        inner_stay, outer_stay, inner_go, outer_go, bias_kept, grad_first, grad_attended, first_sums
    ) = feed_back(
        0, 4, *shared_args, grad_normed, keep, [other_a, other_b],
        (first_normed, first_scale, vectors),
    )
    inner_came, outer_came = plane.swap(inner_go, 4), plane.swap(outer_go, 2)
    bias_grads = jnp.stack(
        [bias_kept[:, 0], jnp.concatenate([bias_sent_a, bias_sent_b])[:, 0]], axis=1
    )
    inner_bias_grad = plane.turned(bias_grads.reshape(plane.n_group, n_z, feed_rows))
    inner_bias_grad = inner_bias_grad.transpose(1, 0, 2)
    inner_bias_grad = jnp.concatenate(
        [
            sum(
                jnp.where(lax.rem(z - t + n_z, n_z) == s, inner_bias_grad[s : s + 1], 0.0)
                for s in range(n_z)
            )
            for t in range(n_z)
        ],
        axis=0,
    ).reshape(n_z, units)

    grads, my_tokens_grad, back_sums = attend_back(
        place_z, lengths, tokens, grad_attended, grad_first, attention_weights, head_biases,
        key_mask_rows,
    )
    grads, inner_came, outer_came, output = together(grads, inner_came, outer_came, output)
    inner_on, outer_on = (
        plane.swap(add(inner_stay[1], inner_came[1]), 2),
        plane.swap(add(outer_stay[1], outer_came[1]), 4),
    )
    tokens_grad = lax.all_gather(my_tokens_grad, "tensor", axis=0, tiled=True)

    def weight_grads(side, other=None, small=None):
        info = jnp.stack([2 * side, 2 * side + 1, z, place])
        return attention_grads(
            n_places, info, grads, mixed, tokens, grad_attended, other, small
        )

    (sent,) = weight_grads(1 - core)
    sent, back_sums, first_sums, second_sums, inner_bias_grad = together(
        sent, back_sums, first_sums, second_sums, inner_bias_grad
    )
    other = plane.swap(sent, 1)

    back_sums = jnp.sum(back_sums, axis=0)
    split = jnp.concatenate(
        [inner_bias_grad, back_sums[0].reshape(n_z, mine), back_sums[1].reshape(n_z, mine)], axis=1
    )
    small = jnp.concatenate([first_sums[:3], second_sums[:3], split.reshape(-1, width)], axis=0)
    small = jnp.pad(small, ((0, -small.shape[0] % 16), (0, 0))).astype(bf16)
    small_rows = small.shape[0]

    small = add(small, plane.swap(small, 1))
    kept = list(weight_grads(core, other, small))
    arrived = plane.to_places(kept)
    kept[0], inner_on, outer_on = together(kept[0], inner_on, outer_on)
    feed_parts = [
        jnp.concatenate(
            [
                add(inner_stay[0, s], inner_came[0, s], inner_on[s]),
                add(outer_stay[0, s], outer_came[0, s], outer_on[s]),
            ],
            axis=1,
        )
        for s in range(n_z)
    ]
    feed_line = [plane.shift(feed_parts[s], -s) for s in others]
    output = copied(output)
    arrived, feed_line, output = together(arrived, feed_line, output)
    small = add(small, *[a[-small_rows:] for a in arrived])
    count = 2 * mine // n_places
    attention_parts = [
        add(*[a[s * count : (s + 1) * count] for a in [kept[0]] + arrived]) for s in range(n_z)
    ]
    attention_line = [
        plane.shift(jnp.concatenate([attention_parts[s], small], axis=0), s) for s in others
    ]
    feed_total = plane.over_groups(add(feed_parts[0], *feed_line))
    feed_arrived = plane.to_places([feed_total] * n_places)
    attention_line, feed_arrived, tokens_grad = together(
        attention_line, feed_arrived, tokens_grad
    )
    attention_total = plane.over_groups(
        add(attention_parts[0], *[a[:count] for a in attention_line])
    )
    small = plane.over_groups(add(small, *[a[count:] for a in attention_line])).astype(f32)
    arrived = plane.to_places([attention_total] * n_places)
    feed_half = plane.from_places(feed_total, feed_arrived)
    feed_other = plane.swap(feed_half, 1)
    feed_grad = plane.by_core(feed_half, feed_other).transpose(1, 0, 2, 3).reshape(units, -1)
    inner_grad = feed_grad[:, :width].T.astype(f32)
    outer_grad = feed_grad[:, width:].astype(f32)
    arrived, inner_grad, outer_grad = together(arrived, inner_grad, outer_grad)
    attention_half = plane.from_places(attention_total, arrived)
    tokens_grad = copied(tokens_grad)
    attention_half, tokens_grad = together(attention_half, tokens_grad)
    attention_other = plane.swap(attention_half, 1)
    grad_list = plane.by_core(attention_half, attention_other)
    grad_list = grad_list.reshape(2, n_places, 2, mine // n_places, width)
    grad_list = grad_list.transpose(0, 2, 1, 3, 4).reshape(4, mine, width)

    shared = small[:6]
    split_rows = n_z * split.shape[1] // width
    split = lax.dynamic_slice_in_dim(
        small[6 : 6 + split_rows].reshape(n_z, -1), z, 1, 0
    )[0]

    return (
        output,
        tokens_grad,
        grad_list[0].T.astype(f32),
        split[units : units + mine],
        grad_list[1].T.astype(f32),
        grad_list[2].T.astype(f32),
        split[units + mine :],
        grad_list[3].astype(f32),
        shared[0],
        shared[1],
        shared[2],
        inner_grad,
        split[:units],
        outer_grad,
        shared[3],
        shared[4],
        shared[5],
    )


def solution(mesh):
    n_dp, n_z = mesh.shape["dp"], mesh.shape["tensor"]
    in_specs = (
        P("dp", None),
        P("dp", None),
        P("dp"),
        P(None, "tensor"),
        P("tensor"),
        P(None, "tensor"),
        P(None, "tensor"),
        P("tensor"),
        P("tensor", None),
        P(),
        P(),
        P(),
        P(None, "tensor"),
        P("tensor"),
        P("tensor", None),
        P(),
        P(),
        P(),
        P("dp", None),
    )
    out_specs = (
        P("dp", None),
        P("dp", None),
        P(None, "tensor"),
        P("tensor"),
        P(None, "tensor"),
        P(None, "tensor"),
        P("tensor"),
        P("tensor", None),
        P(),
        P(),
        P(),
        P(None, "tensor"),
        P("tensor"),
        P("tensor", None),
        P(),
        P(),
        P(),
    )

    def program(*args):
        return on_device(n_dp, n_z, *args)

    return jax.shard_map(
        program, mesh=mesh, in_specs=in_specs, out_specs=out_specs, check_vma=False
    )
```

```python
import functools

import jax
import jax.numpy as jnp
from jax import lax
from jax.experimental import pallas as pl
from jax.experimental.pallas import tpu as pltpu
from jax.sharding import PartitionSpec as P

HEAD = 64
BUCKET = 512
ITEMS = 8


negative_fill = -1e30
epsilon = 1e-06
f32 = jnp.float32
bf16 = jnp.bfloat16
VMEM_BYTES = 56 * 1024 * 1024


def dot(left, right):
    return jnp.dot(left, right, preferred_element_type=f32)


def contract_rows(left, right):
    return lax.dot_general(left, right, (((0,), (0,)), ((), ())), preferred_element_type=f32)


def contract_cols(left, right):
    return lax.dot_general(left, right, (((1,), (1,)), ((), ())), preferred_element_type=f32)


def norm_rows(values):
    centred = values - jnp.mean(values, axis=1, keepdims=True)
    inv_scale = lax.rsqrt(jnp.mean(centred * centred, axis=1, keepdims=True) + epsilon)
    return centred * inv_scale, inv_scale


def norm_back(grad_rows, norm_gain, normed, inv_scale):
    scaled = grad_rows * norm_gain
    return inv_scale * (
        scaled
        - jnp.mean(scaled, axis=1, keepdims=True)
        - normed * jnp.mean(scaled * normed, axis=1, keepdims=True)
    )


def column_sum(matrix):
    return jnp.sum(matrix.astype(f32), axis=0, keepdims=True)


def fixed(shape):
    return pl.BlockSpec(shape, lambda *_: (0,) * len(shape))


def cost(microseconds):
    return pl.CostEstimate(
        flops=int(microseconds * 6e7),
        bytes_accessed=int(microseconds * 6e4),
        transcendentals=0,
    )


def params(axes):
    return pltpu.CompilerParams(
        dimension_semantics=("arbitrary",) * axes, vmem_limit_bytes=VMEM_BYTES
    )


def item_places(lengths_ref, row, shape, axis):
    places = lax.broadcasted_iota(jnp.int32, shape, axis)
    end = jnp.int32(0)
    items = jnp.zeros(shape, jnp.int32)
    for slot in range(ITEMS):
        end = end + lengths_ref[row, slot]
        items = items + (places >= end).astype(jnp.int32)
    return items


def as_column(row):
    return jnp.broadcast_to(row.astype(f32), (8, row.shape[1])).T[:, :1]


def mask_bias(lengths_ref, row, key_mask):
    shape = (BUCKET, BUCKET)
    diagonal = lax.broadcasted_iota(jnp.int32, shape, 0) == lax.broadcasted_iota(
        jnp.int32, shape, 1
    )
    item_row = item_places(lengths_ref, row, (1, BUCKET), 1)
    item_column = item_places(lengths_ref, row, (BUCKET, 1), 0)
    code_column = jnp.where(as_column(key_mask) == 1.0, item_column, -1)
    return jnp.where((code_column == item_row) | diagonal, 0.0, negative_fill).astype(f32)


def attend_forward_kernel(
    lengths_ref, tokens_ref, query_ref, key_ref, value_ref, biases_ref, key_mask_ref, mixed_ref,
):
    mine = query_ref.shape[0]
    rows = tokens_ref[...]
    queries = contract_cols(query_ref[...], rows) + as_column(biases_ref[0:1, :mine])
    queries = (queries.astype(bf16) * HEAD ** (-0.5)).astype(bf16)
    keys = contract_cols(rows, key_ref[...]).astype(bf16)
    values = contract_cols(value_ref[...], rows) + as_column(biases_ref[0:1, mine : 2 * mine])
    values = values.astype(bf16)
    bias = mask_bias(lengths_ref, pl.program_id(0), key_mask_ref[0])
    for head in range(mine // HEAD):
        at = slice(head * HEAD, (head + 1) * HEAD)
        scores = dot(keys[:, at], queries[at]) + bias
        exponent = jnp.exp(scores - jnp.max(scores, axis=0, keepdims=True))
        total = jnp.sum(exponent, axis=0, keepdims=True)
        mixed_ref[0, 0, at] = (dot(values[at], exponent.astype(bf16)) / total).astype(bf16)
    mixed_ref[0, 0, mine:] = biases_ref[...]


def attend_forward(n_z, lengths, tokens, query, key, value, biases, key_mask):
    blocks = lengths.shape[0]
    own = blocks // n_z
    mine, width = key.shape
    whole = (n_z, own, mine + biases.shape[0], BUCKET)
    return pl.pallas_call(
        attend_forward_kernel,
        grid=(blocks,),
        in_specs=[
            pl.BlockSpec(memory_space=pltpu.SMEM),
            pl.BlockSpec((BUCKET, width), lambda b: (b, 0)),
            fixed((mine, width)),
            fixed((mine, width)),
            fixed((mine, width)),
            fixed(biases.shape),
            pl.BlockSpec((1, 1, BUCKET), lambda b: (b, 0, 0)),
        ],
        out_specs=pl.BlockSpec((1, 1) + whole[2:], lambda b: (b // own, b % own, 0, 0)),
        out_shape=jax.ShapeDtypeStruct(whole, bf16),
        compiler_params=params(1),
        name="attend_forward",
        cost_estimate=cost(12),
    )(lengths, tokens, query, key, value, biases, key_mask)


def fetch_units(step, picks, own_ref, halves, units, sems):
    feed_rows, twice = units.shape[2:]
    cut = feed_rows // 2

    def copies(number):
        slot = number % 2
        row = pl.multiple_of(picks[number] * feed_rows, 16)
        ends = [
            (own_ref.at[pl.ds(row, feed_rows), :twice], units.at[slot, 0]),
            (halves[number][0].at[:, :, :twice], units.at[slot, 1:, :cut]),
            (halves[number][1].at[:, :, :twice], units.at[slot, 1:, cut:]),
        ]
        return [
            pltpu.make_async_copy(source, target, sems.at[slot, i])
            for i, (source, target) in enumerate(ends)
        ]

    for number in range(len(halves)):

        @pl.when(step == number)
        def _(number=number):
            if number == 0:
                for copy in copies(0):
                    copy.start()
            if number + 1 < len(halves):
                for copy in copies(number + 1):
                    copy.start()
            for copy in copies(number):
                copy.wait()

    return units.at[lax.rem(step, 2)]


def fetch_mixer(picks, own_ref, halves, mixer, sems):
    feed_rows = mixer.shape[1] // 8
    cut = feed_rows // 2
    start = own_ref.shape[1] - mixer.shape[2]
    ends = [(own_ref.at[:, start:], mixer.at[0])]
    for number, pair in enumerate(halves):
        for half in range(2):
            row = pl.multiple_of(picks[number] * feed_rows + half * cut, 16)
            ends.append((pair[half].at[:, :, start:], mixer.at[1:, pl.ds(row, cut)]))
    copies = [
        pltpu.make_async_copy(source, target, sems.at[i])
        for i, (source, target) in enumerate(ends)
    ]
    for copy in copies:
        copy.start()
    for copy in copies:
        copy.wait()


def split_units(units):
    width = units.shape[2] // 2
    return units[:, :, :width].reshape(-1, width), units[:, :, width:].reshape(-1, width)


ANYWHERE = pl.BlockSpec(memory_space=pl.ANY)


def feed_forward_kernel(
    info_ref, lengths_ref, mixed_ref, tokens_ref, cotangent_ref, vectors_ref, bias_ref, own_ref,
    *rest,
):
    halves, rest = list(zip(rest[:16:2], rest[1:16:2])), rest[16:]
    (
        hidden_ref, slope_ref, output_ref, normed_low_ref, first_normed_ref, first_scale_ref,
        grad_second_ref, grad_outer_ref, sums_ref, second_sum, units, sems,
        mixer, mixer_sems,
    ) = rest
    step = pl.program_id(0)
    picks = [(info_ref[1] ^ (k % 4)) * 2 + (info_ref[2] ^ (k // 4)) for k in range(8)]
    weights = fetch_units(step, picks, own_ref, halves, units, sems)
    output_bias, first_gain, first_shift, outer_bias, second_gain, second_shift = (
        vectors_ref[i : i + 1, :] for i in range(6)
    )

    @pl.when(step == 0)
    def _():
        fetch_mixer(picks, own_ref, halves, mixer, mixer_sems)
        n_z, own, mine, _ = mixed_ref.shape
        attended = output_bias + jnp.concatenate(
            [
                sum(
                    dot(mixer[s, :, :mine], mixed_ref[lax.rem(info_ref[0] + n_z - s, n_z), b])
                    for s in range(n_z)
                ).T
                for b in range(own)
            ],
            axis=0,
        )
        normed, inv_scale = norm_rows(tokens_ref[...].astype(f32) + attended)
        whole = normed * first_gain + first_shift
        first_normed_ref[...] = normed
        first_scale_ref[...] = inv_scale
        normed_low_ref[...] = whole.astype(bf16)
        second_sum[...] = whole + outer_bias

    inner, outer = split_units(weights)
    inner_pre = contract_cols(normed_low_ref[...], inner) + bias_ref[0]
    normal_cdf = 0.5 + 0.5 * lax.erf(inner_pre * 0.7071067811865476)
    density = jnp.exp(-0.5 * inner_pre * inner_pre) * 0.3989422804014327
    hidden = (inner_pre * normal_cdf).astype(bf16)
    hidden_ref[...] = hidden.T
    slope_ref[...] = (normal_cdf + inner_pre * density).astype(bf16)
    second_sum[...] += dot(hidden, outer)

    @pl.when(step == pl.num_programs(0) - 1)
    def _():
        normed, inv_scale = norm_rows(second_sum[...])
        blocks = normed.shape[0] // BUCKET
        live = jnp.concatenate(
            [
                (item_places(lengths_ref, info_ref[0] * blocks + b, (BUCKET, 1), 0) < ITEMS)
                for b in range(blocks)
            ],
            axis=0,
        ).astype(f32)
        output_ref[...] = ((normed * second_gain + second_shift) * live).astype(bf16)
        grad_final = cotangent_ref[...].astype(f32) * live
        grad_second = norm_back(grad_final, second_gain, normed, inv_scale)
        grad_outer = grad_second.astype(bf16)
        grad_second_ref[...] = grad_second
        grad_outer_ref[...] = grad_outer
        sums_ref[0:1, :] = column_sum(grad_outer)
        sums_ref[1:2, :] = column_sum(grad_final * normed)
        sums_ref[2:3, :] = column_sum(grad_final)


def feed_forward(info, lengths, mixed, tokens, cotangent, vectors, biases, own, halves):
    n_z, buckets = mixed.shape[:2]
    rows = buckets * BUCKET
    width = tokens.shape[1]
    mine = width // n_z
    feed_rows, twice = own.shape[0] // 8, 2 * width
    chunk = n_z * feed_rows
    whole = fixed((rows, width))
    my_rows = pl.BlockSpec((rows, width), lambda j, info: (info[0], 0))
    columns = pl.BlockSpec((rows, chunk), lambda j, info: (0, j))
    shapes = [
        ((8 * chunk, rows), bf16, pl.BlockSpec((chunk, rows), lambda j, info: (j, 0))),
        ((rows, 8 * chunk), bf16, columns),
        ((rows, width), bf16, whole),
        ((rows, width), bf16, whole),
        ((rows, width), f32, whole),
        ((rows, 1), f32, fixed((rows, 1))),
        ((rows, width), f32, whole),
        ((rows, width), bf16, whole),
        ((8, width), f32, fixed((8, width))),
    ]
    return pl.pallas_call(
        feed_forward_kernel,
        grid_spec=pltpu.PrefetchScalarGridSpec(
            num_scalar_prefetch=1,
            grid=(8,),
            in_specs=[
                pl.BlockSpec(memory_space=pltpu.SMEM),
                fixed((n_z, buckets, mine, BUCKET)),
                my_rows,
                my_rows,
                fixed((8, width)),
                pl.BlockSpec((1, 1, chunk), lambda j, info: (j, 0, 0)),
                ANYWHERE,
            ]
            + [ANYWHERE] * 16,
            out_specs=[spec for _, _, spec in shapes],
            scratch_shapes=[
                pltpu.VMEM((rows, width), f32),
                pltpu.VMEM((2, n_z, feed_rows, twice), bf16),
                pltpu.SemaphoreType.DMA((2, 3)),
                pltpu.VMEM((n_z, width, own.shape[1] - twice), bf16),
                pltpu.SemaphoreType.DMA((17,)),
            ],
        ),
        out_shape=[jax.ShapeDtypeStruct(shape, kind) for shape, kind, _ in shapes],
        compiler_params=params(1),
        name="feed_forward",
        cost_estimate=cost(21),
    )(info, lengths, mixed, tokens, cotangent, vectors, biases, own, *halves)


STAY = ((0, 1), (0, 2))
GO = ((2, 3), (1, 3))


def feed_back_kernel(
    first, count, keeps, info_ref, grad_outer_ref, normed_low_ref, hidden_ref, slope_ref,
    own_ref, start_ref, *rest,
):
    halves = list(zip(rest[: 2 * count : 2], rest[1 : 2 * count : 2]))
    rest = rest[2 * count :]
    if keeps:
        other_ref, norm_refs, rest = rest[0], rest[1:4], rest[4:]
        stay_refs, go_refs, rest = rest[0:2], rest[2:4], rest[4:]
        bias_grad_ref, grad_first_ref, grad_attended_ref, sums_ref, units, sems = rest[:6]
        grad_normed_ref = rest[6]
    else:
        grad_ref, bias_grad_ref, grad_normed_ref, units, sems = rest
    step = pl.program_id(0)
    side = info_ref[2] if keeps else 1 - info_ref[2]
    picks = [(info_ref[1] ^ (first + k)) * 2 + side for k in range(count)]
    weights = fetch_units(step, picks, own_ref, halves, units, sems)

    @pl.when(step == 0)
    def _():
        grad_normed_ref[...] = start_ref[...]

    n_z, feed_rows, twice = weights.shape
    width = twice // 2
    inner, outer = split_units(weights)
    grad_outer = grad_outer_ref[...]
    grad_hidden = contract_cols(grad_outer, outer)
    grad_inner = (grad_hidden * slope_ref[...].astype(f32)).astype(bf16)
    outer_grad = dot(hidden_ref[...], grad_outer).reshape(n_z, feed_rows, width)
    inner_grad = contract_rows(grad_inner, normed_low_ref[...]).reshape(n_z, feed_rows, width)
    bias_grad_ref[0] = column_sum(grad_inner)
    grad_normed_ref[...] += dot(grad_inner, inner)

    if keeps:
        for number in range(4):

            @pl.when(step == number)
            def _(number=number):
                for track, value in enumerate((inner_grad, outer_grad)):
                    at = slice(track * width, (track + 1) * width)
                    value = (value + other_ref[0, :, :, at].astype(f32)).astype(bf16)
                    ref = stay_refs[track] if number in STAY[track] else go_refs[track]
                    ref[0] = value

        @pl.when(step == pl.num_programs(0) - 1)
        def _():
            first_normed_ref, first_scale_ref, vectors_ref = norm_refs
            grad_rows, normed = grad_normed_ref[...], first_normed_ref[...]
            grad_first = norm_back(grad_rows, vectors_ref[1:2, :], normed, first_scale_ref[...])
            grad_attended = grad_first.astype(bf16)
            grad_first_ref[...] = grad_first
            grad_attended_ref[...] = grad_attended
            sums_ref[0:1, :] = column_sum(grad_attended)
            sums_ref[1:2, :] = column_sum(grad_rows * normed)
            sums_ref[2:3, :] = column_sum(grad_rows)

    else:
        grad_ref[0, :, :, :width] = inner_grad.astype(bf16)
        grad_ref[0, :, :, width:] = outer_grad.astype(bf16)


def feed_back(
    first, count, info, grad_outer, normed_low, hidden, slope, own, start, halves,
    other=None, norm=None,
):
    rows, width = grad_outer.shape
    keeps = other is not None
    feed_rows, twice = own.shape[0] // 8, 2 * width
    n_z = halves[0].shape[0] + 1
    chunk = n_z * feed_rows
    flip = 0 if keeps else 1
    columns = pl.BlockSpec((rows, chunk), lambda i, info: (0, 4 * flip + first + i))
    whole = fixed((rows, width))
    part = (n_z, feed_rows, twice)
    track = (2, n_z, feed_rows, width)
    unit_rows = pl.BlockSpec((chunk, rows), lambda i, info: (4 * flip + first + i, 0))
    in_specs = [whole, whole, unit_rows, columns, ANYWHERE, whole] + [ANYWHERE] * (2 * count)
    args = [grad_outer, normed_low, hidden, slope, own, start] + halves
    bias_shape = (
        (count, 1, chunk),
        f32,
        pl.BlockSpec((1, 1, chunk), lambda i, info: (i, 0, 0)),
    )
    scratch = [pltpu.VMEM((2,) + part, bf16), pltpu.SemaphoreType.DMA((2, 3))]

    def one(shape, at):
        return pl.BlockSpec((1,) + shape[1:], lambda i, info: (at(i), 0, 0, 0))

    if keeps:
        early, late = (lambda i: jnp.minimum(i, 1)), (lambda i: jnp.maximum(i - 2, 0))
        in_specs.append(one((4,) + part, lambda i: i))
        in_specs += [whole, fixed((rows, 1)), fixed((8, width))]
        args += [other] + list(norm)
        slow, slower = (lambda i: i // 2), (lambda i: jnp.maximum(i - 1, 0) // 2)
        shapes = [(track, bf16, one(track, at)) for at in (early, slow, late, slower)] + [
            bias_shape,
            ((rows, width), f32, whole),
            ((rows, width), bf16, whole),
            ((8, width), f32, fixed((8, width))),
        ]
        scratch.append(pltpu.VMEM((rows, width), f32))
    else:
        shapes = [
            ((count,) + part, bf16, one((count,) + part, lambda i: i)),
            bias_shape,
            ((rows, width), f32, whole),
        ]
    return pl.pallas_call(
        functools.partial(feed_back_kernel, first, count, keeps),
        grid_spec=pltpu.PrefetchScalarGridSpec(
            num_scalar_prefetch=1,
            grid=(count,),
            in_specs=in_specs,
            out_specs=[spec for _, _, spec in shapes],
            scratch_shapes=scratch,
        ),
        out_shape=[jax.ShapeDtypeStruct(shape, kind) for shape, kind, _ in shapes],
        compiler_params=params(1),
        name="feed_back_own" if keeps else "feed_back",
        cost_estimate=cost(3 * count),
    )(info, *args)


def copy_kernel(from_ref, to_ref):
    to_ref[...] = from_ref[...]


def copied(array):
    block = pl.BlockSpec((BUCKET, array.shape[1]), lambda i: (i, 0))
    return pl.pallas_call(
        copy_kernel,
        grid=(array.shape[0] // BUCKET,),
        in_specs=[block],
        out_specs=block,
        out_shape=jax.ShapeDtypeStruct(array.shape, array.dtype),
        compiler_params=params(1),
        name="copied",
        cost_estimate=cost(2),
    )(array)


def project_kernel(place_ref, tokens_ref, weights_ref, biases_ref, query_ref, key_ref, value_ref):
    rows = tokens_ref[...]
    width = rows.shape[1]
    queries = contract_cols(weights_ref[:, :width], rows) + as_column(biases_ref[0:1, :])
    query_ref[...] = (queries.astype(bf16) * HEAD ** (-0.5)).astype(bf16)
    key_ref[...] = contract_cols(rows, weights_ref[:, width : 2 * width]).astype(bf16)
    values = contract_cols(rows, weights_ref[:, 2 * width :]) + biases_ref[1:2, :]
    value_ref[...] = values.astype(bf16)


def project(place, tokens, weights, biases, buckets):
    width = tokens.shape[1]
    part = width // 3
    shapes = [
        ((buckets, width, BUCKET), pl.BlockSpec((None, part, BUCKET), lambda b, j, _: (b, j, 0))),
        ((buckets * BUCKET, width), pl.BlockSpec((BUCKET, part), lambda b, j, _: (b, j))),
        ((buckets * BUCKET, width), pl.BlockSpec((BUCKET, part), lambda b, j, _: (b, j))),
    ]
    return pl.pallas_call(
        project_kernel,
        grid_spec=pltpu.PrefetchScalarGridSpec(
            num_scalar_prefetch=1,
            grid=(buckets, 3),
            in_specs=[
                pl.BlockSpec((BUCKET, width), lambda b, j, place: (place[0] * buckets + b, 0)),
                pl.BlockSpec((part, 3 * width), lambda b, j, place: (j, 0)),
                pl.BlockSpec((8, part), lambda b, j, place: (0, j)),
            ],
            out_specs=[spec for _, spec in shapes],
        ),
        out_shape=[jax.ShapeDtypeStruct(shape, bf16) for shape, _ in shapes],
        compiler_params=params(2),
        name="project",
        cost_estimate=cost(5),
    )(place, tokens, weights, biases)


def attend_back_kernel(
    place_ref, lengths_ref, grad_attended_ref, grad_first_ref, weights_ref, query_ref, key_ref,
    value_ref, key_mask_ref,
    grads_ref, tokens_grad_ref, sums_ref,
    bias, grad_mixed_t, whole, weights, sem,
):
    pair = pl.program_id(1)
    pairs, width = whole.shape[1], weights.shape[0]
    fetch = pltpu.make_async_copy(weights_ref, weights, sem)

    @pl.when(pair == 0)
    def _():
        fetch.start()
        row = place_ref[0] * pl.num_programs(0) + pl.program_id(0)
        bias[...] = mask_bias(lengths_ref, row, key_mask_ref[0])
        fetch.wait()
        grad_mixed_t[...] = contract_cols(
            weights[:, 3 * width :], grad_attended_ref[...]
        ).astype(bf16)

    queries, keys, values = query_ref[...], key_ref[...], value_ref[...]
    start = pl.multiple_of(pair * keys.shape[1], 128)
    grad_mixed = grad_mixed_t[pl.ds(start, keys.shape[1]), :]
    keys_t = keys.T
    grad_queries, grad_keys, grad_values = [], [], []
    for head in range(keys.shape[1] // HEAD):
        at = slice(head * HEAD, (head + 1) * HEAD)
        scores = dot(keys[:, at], queries[at]) + bias[...]
        exponent = jnp.exp(scores - jnp.max(scores, axis=0, keepdims=True))
        probs = exponent * (1.0 / jnp.sum(exponent, axis=0, keepdims=True))
        grad_probs = dot(values[:, at], grad_mixed[at])
        shift = jnp.sum(probs * grad_probs, axis=0, keepdims=True)
        grad_scores = (probs * (grad_probs - shift)).astype(bf16)
        grad_values.append(contract_cols(probs.astype(bf16), grad_mixed[at]))
        grad_keys.append(contract_cols(grad_scores, queries[at]))
        grad_queries.append(dot(keys_t[at], grad_scores) * HEAD ** (-0.5))
    found = (
        jnp.concatenate(grad_queries, axis=0).T.astype(bf16),
        jnp.concatenate(grad_keys, axis=1).astype(bf16),
        jnp.concatenate(grad_values, axis=1).astype(bf16),
    )
    for number, grad in enumerate(found):
        grads_ref[number] = grad
        whole[number, pair] = grad
    sums_ref[0, 0:1, :] = column_sum(found[0])
    sums_ref[0, 1:2, :] = column_sum(found[2])

    @pl.when(pair == pl.num_programs(1) - 1)
    def _():
        total = grad_first_ref[...]
        for number in range(3):
            grad = jnp.concatenate([whole[number, i] for i in range(pairs)], axis=1)
            total += dot(grad, weights[:, number * width : (number + 1) * width])
        tokens_grad_ref[...] = total.astype(bf16)


def attend_back(place, lengths, grad_attended, grad_first, weights, queries, keys, values, key_mask):
    rows, width = grad_attended.shape
    blocks = rows // BUCKET
    pair = 2 * HEAD
    by_bucket = pl.BlockSpec((BUCKET, width), lambda b, h, place: (b, 0))
    by_pair = pl.BlockSpec((BUCKET, pair), lambda b, h, place: (b, h))
    return pl.pallas_call(
        attend_back_kernel,
        grid_spec=pltpu.PrefetchScalarGridSpec(
            num_scalar_prefetch=1,
            grid=(blocks, width // pair),
            in_specs=[
                pl.BlockSpec(memory_space=pltpu.SMEM),
                by_bucket,
                by_bucket,
                ANYWHERE,
                pl.BlockSpec((None, pair, BUCKET), lambda b, h, place: (b, h, 0)),
                by_pair,
                by_pair,
                pl.BlockSpec((1, 1, BUCKET), lambda b, h, place: (place[0] * blocks + b, 0, 0)),
            ],
            out_specs=[
                pl.BlockSpec((3, BUCKET, pair), lambda b, h, place: (0, b, h)),
                by_bucket,
                pl.BlockSpec((1, 8, pair), lambda b, h, place: (b, 0, h)),
            ],
            scratch_shapes=[
                pltpu.VMEM((BUCKET, BUCKET), f32),
                pltpu.VMEM((width, BUCKET), bf16),
                pltpu.VMEM((3, width // pair, BUCKET, pair), bf16),
                pltpu.VMEM(weights.shape, bf16),
                pltpu.SemaphoreType.DMA(()),
            ],
        ),
        out_shape=[
            jax.ShapeDtypeStruct((3, rows, width), bf16),
            jax.ShapeDtypeStruct((rows, width), bf16),
            jax.ShapeDtypeStruct((blocks, 8, width), f32),
        ],
        compiler_params=params(2),
        name="attend_back",
        cost_estimate=cost(20),
    )(place, lengths, grad_attended, grad_first, weights, queries, keys, values, key_mask)


def attention_grads_kernel(
    n_places, adds, info_ref, grads_ref, mixed_ref, tokens_ref, grad_attended_ref, *rest
):
    if adds:
        other_ref, small_ref = rest[:2]
        out_refs, whole = rest[2:-1], rest[-1]
    else:
        (out_ref, whole) = rest
    step = pl.program_id(0)
    which = info_ref[step]
    n_z, buckets, mine, _ = mixed_ref.shape
    count = mine // n_places

    @pl.when(which < 3)
    def _():
        whole[...] = contract_rows(grads_ref[0], tokens_ref[...]).astype(bf16)

    @pl.when(which == 3)
    def _():
        for t in range(n_z):
            whole[t * mine : (t + 1) * mine, :] = sum(
                dot(mixed_ref[t, b], grad_attended_ref[b * BUCKET : (b + 1) * BUCKET, :])
                for b in range(buckets)
            ).astype(bf16)

    for number in range(n_places):
        for s in range(n_z):
            start = lax.rem(info_ref[2] + s, n_z) * mine + (info_ref[3] ^ number) * count
            value = whole[pl.ds(pl.multiple_of(start, 16), count), :]
            if adds:
                value = value.astype(f32) + other_ref[number, s, 0].astype(f32)
                row = (2 * s + step) * count
                out_refs[number][pl.ds(pl.multiple_of(row, 16), count), :] = value.astype(bf16)
            else:
                out_ref[number, s, 0] = value

    if adds:
        for number in range(n_places):
            out_refs[number][2 * n_z * count :, :] = small_ref[...]


def attention_grads(n_places, info, grads, mixed, tokens, grad_attended, other=None, small=None):
    rows, width = grad_attended.shape
    n_z, buckets = mixed.shape[:2]
    mine = width // n_z
    count = mine // n_places
    parts = (n_places, n_z, 1, count, width)
    by_step = pl.BlockSpec(parts, lambda i, info: (0, 0, i, 0, 0))
    in_specs = [
        pl.BlockSpec((1, rows, width), lambda i, info: (jnp.minimum(info[i], 2), 0, 0)),
        fixed((n_z, buckets, mine, BUCKET)),
        pl.BlockSpec((rows, width), lambda i, info: (info[2], 0)),
        fixed((rows, width)),
    ]
    args = [grads, mixed, tokens, grad_attended]
    if other is None:
        shapes = [((n_places, n_z, 2, count, width), by_step)]
    else:
        in_specs += [by_step, fixed(small.shape)]
        args += [other, small]
        flat = (2 * n_z * count + small.shape[0], width)
        shapes = [(flat, fixed(flat))] * n_places
    return pl.pallas_call(
        functools.partial(attention_grads_kernel, n_places, other is not None),
        grid_spec=pltpu.PrefetchScalarGridSpec(
            num_scalar_prefetch=1,
            grid=(2,),
            in_specs=in_specs,
            out_specs=[spec for _, spec in shapes],
            scratch_shapes=[pltpu.VMEM((width, width), bf16)],
        ),
        out_shape=[jax.ShapeDtypeStruct(shape, bf16) for shape, _ in shapes],
        compiler_params=params(1),
        name="attention_grads",
        cost_estimate=cost(6),
    )(info, *args)


def together(*values):
    return lax.optimization_barrier(values)


def add(first, *others):
    total = first.astype(f32)
    for other in others:
        total = total + other.astype(f32)
    return total.astype(bf16)


class Plane:
    def __init__(self, n_dp, n_z):
        self.n_dp, self.n_z = n_dp, n_z
        self.n_group = min(n_dp, 8)
        self.n_places = self.n_group // 2
        self.dp = lax.axis_index("dp")
        self.z = lax.axis_index("tensor")
        self.index = lax.rem(self.dp, self.n_group)
        self.core = self.index & 1
        self.place = self.index >> 1

    def swap(self, array, bits):
        return lax.ppermute(array, "dp", [(i, i ^ bits) for i in range(self.n_dp)])

    def shift(self, array, by):
        n = self.n_z
        return lax.ppermute(array, "tensor", [(i, (i + by) % n) for i in range(n)])

    def gather(self, piece):
        if self.n_dp == self.n_group:
            whole = lax.all_gather(piece, ("tensor", "dp"))
            return whole.reshape((self.n_z, self.n_group) + piece.shape)
        groups = [
            list(range(i, i + self.n_group)) for i in range(0, self.n_dp, self.n_group)
        ]
        line = lax.all_gather(piece, "tensor")
        return lax.all_gather(line, "dp", axis=1, axis_index_groups=groups)

    def turned(self, array):
        bit = 1
        while bit < self.n_group:
            lead = array.reshape((-1, 2, bit) + array.shape[1:])
            array = jnp.where((self.index & bit) != 0, lead[:, ::-1], lead).reshape(array.shape)
            bit *= 2
        return array

    def to_places(self, parts):
        return [self.swap(parts[number], 2 * number) for number in range(1, self.n_places)]

    def from_places(self, own, arrived):
        found = jnp.stack([own] + arrived)
        bit = 1
        while bit < self.n_places:
            lead = found.reshape((-1, 2, bit) + own.shape)
            flipped = lead[:, ::-1]
            found = jnp.where((self.place & bit) != 0, flipped, lead).reshape(found.shape)
            bit *= 2
        return found

    def by_core(self, own, other):
        return jnp.where(
            self.core == 1, jnp.stack([other, own]), jnp.stack([own, other])
        )

    def over_groups(self, array):
        bit = self.n_group
        while bit < self.n_dp:
            array = add(array, self.swap(array, bit))
            bit *= 2
        return array


def on_device(
    n_dp,
    n_z,
    tokens,
    lengths,
    key_mask,
    query_weight,
    query_bias,
    key_weight,
    value_weight,
    value_bias,
    output_weight,
    output_bias,
    first_gain,
    first_shift,
    inner_weight,
    inner_bias,
    outer_weight,
    outer_bias,
    second_gain,
    second_shift,
    cotangent,
):
    width = tokens.shape[1]
    mine = query_weight.shape[1]
    units = inner_weight.shape[1]
    all_rows = tokens.shape[0]
    all_blocks = all_rows // BUCKET
    rows = all_rows // n_z
    plane = Plane(n_dp, n_z)
    z, core, place, index = plane.z, plane.core, plane.place, plane.index
    n_places = plane.n_places
    others = range(1, n_z)

    mixer_t = jnp.pad(output_weight.T, ((0, 0), (0, -mine % 128)))
    feed_rows = units // plane.n_group
    head_rows = mine // plane.n_group
    piece = jnp.concatenate(
        [
            lax.dynamic_slice_in_dim(inner_weight, index * feed_rows, feed_rows, 1).T,
            lax.dynamic_slice_in_dim(outer_weight, index * feed_rows, feed_rows, 0),
            lax.dynamic_slice_in_dim(mixer_t, index * feed_rows, feed_rows, 0),
        ],
        axis=1,
    )
    line = [plane.shift(piece, s) for s in others]

    query_t, key_t, value_t = query_weight.T, key_weight.T, value_weight.T
    attention_own = jnp.concatenate([query_t, key_t, value_t, output_weight], axis=1)
    attention_weights = plane.gather(
        lax.dynamic_slice_in_dim(attention_own, index * head_rows, head_rows, 0)
    ).reshape(width, 4 * width)

    key_mask_rows = key_mask.reshape(all_blocks, 1, BUCKET)
    bias_row = jnp.concatenate([query_bias, value_bias, inner_bias])
    bias_rows = jnp.pad(bias_row, (0, 16 * BUCKET - bias_row.shape[0])).reshape(16, BUCKET)
    mixed = attend_forward(
        n_z, lengths, tokens, query_t, key_t, value_t, bias_rows, key_mask_rows
    )
    _, line = together(mixed, line)
    mixed = lax.all_to_all(mixed, "tensor", 0, 0)

    cut = feed_rows // 2
    near = [jnp.stack([part[:cut] for part in line]), jnp.stack([part[cut:] for part in line])]
    by_x, by_y = [plane.swap(half, 2) for half in near], [plane.swap(half, 4) for half in near]
    by_x[0], by_y[1], mixed = together(by_x[0], by_y[1], mixed)
    far = [plane.swap(by_x[0], 4), plane.swap(by_y[1], 2)]
    keep = near + by_x + by_y + far
    send = [plane.swap(half, 1) for half in near + by_x + by_y]
    far, send = together(far, send)
    keep = keep[:6] + far
    send = send + [plane.swap(half, 1) for half in far]
    own_units = jnp.concatenate([inner_weight.T, outer_weight, mixer_t], axis=1)

    biases = mixed[:, 0, mine:].reshape(n_z, -1)[:, : bias_row.shape[0]].astype(f32)
    head_biases = jnp.pad(
        jnp.stack([biases[:, :mine].reshape(-1), biases[:, mine : 2 * mine].reshape(-1)]),
        ((0, 6), (0, 0)),
    )
    inner_biases = biases[:, 2 * mine :]
    inner_biases = jnp.concatenate(
        [
            lax.dynamic_slice_in_dim(inner_biases, lax.rem(z + n_z - s, n_z), 1, 0)
            for s in range(n_z)
        ],
        axis=0,
    )
    inner_biases = inner_biases.reshape(n_z, plane.n_group, feed_rows).transpose(1, 0, 2)
    inner_biases = plane.turned(inner_biases).reshape(n_places, 2, 1, n_z * feed_rows)
    inner_biases = inner_biases.transpose(1, 0, 2, 3).reshape(plane.n_group, 1, -1)
    vectors = jnp.stack(
        [output_bias, first_gain, first_shift, outer_bias, second_gain, second_shift]
        + [jnp.zeros_like(output_bias)] * 2
    ).astype(f32)

    place_z = z.reshape(1)
    info = jnp.stack([z, place, core])
    (
        hidden, slope, my_output, normed_low, first_normed, first_scale, grad_second, grad_outer,
        second_sums,
    ) = feed_forward(
        info, lengths, mixed, tokens, cotangent, vectors, inner_biases, own_units, keep + send
    )
    output = lax.all_gather(my_output, "tensor", axis=0, tiled=True)

    shared_args = (info, grad_outer, normed_low, hidden, slope, own_units)
    sent, bias_sent, grad_normed = feed_back(0, 4, *shared_args, grad_second, send)
    other = plane.swap(sent, 1)
    grad_normed, head_biases, tokens = together(grad_normed, head_biases, tokens)
    projected = project(place_z, tokens, attention_weights, head_biases, mixed.shape[1])
    projected, other = together(projected, other)
    (
        inner_stay, outer_stay, inner_go, outer_go, bias_kept, grad_first, grad_attended, first_sums
    ) = feed_back(
        0, 4, *shared_args, grad_normed, keep, other,
        (first_normed, first_scale, vectors),
    )
    inner_came, outer_came = plane.swap(inner_go, 4), plane.swap(outer_go, 2)
    bias_grads = jnp.stack(
        [bias_kept[:, 0], bias_sent[:, 0]], axis=1
    )
    inner_bias_grad = plane.turned(bias_grads.reshape(plane.n_group, n_z, feed_rows))
    inner_bias_grad = inner_bias_grad.transpose(1, 0, 2)
    inner_bias_grad = jnp.concatenate(
        [
            sum(
                jnp.where(lax.rem(z - t + n_z, n_z) == s, inner_bias_grad[s : s + 1], 0.0)
                for s in range(n_z)
            )
            for t in range(n_z)
        ],
        axis=0,
    ).reshape(n_z, units)

    grads, my_tokens_grad, back_sums = attend_back(
        place_z, lengths, grad_attended, grad_first, attention_weights, *projected, key_mask_rows
    )
    grads, inner_came, outer_came, output = together(grads, inner_came, outer_came, output)
    inner_on, outer_on = (
        plane.swap(add(inner_stay[1], inner_came[1]), 2),
        plane.swap(add(outer_stay[1], outer_came[1]), 4),
    )
    tokens_grad = lax.all_gather(my_tokens_grad, "tensor", axis=0, tiled=True)

    def weight_grads(side, other=None, small=None):
        info = jnp.stack([2 * side, 2 * side + 1, z, place])
        return attention_grads(
            n_places, info, grads, mixed, tokens, grad_attended, other, small
        )

    (sent,) = weight_grads(1 - core)
    sent, back_sums, first_sums, second_sums, inner_bias_grad = together(
        sent, back_sums, first_sums, second_sums, inner_bias_grad
    )
    other = plane.swap(sent, 1)

    back_sums = jnp.sum(back_sums, axis=0)
    split = jnp.concatenate(
        [inner_bias_grad, back_sums[0].reshape(n_z, mine), back_sums[1].reshape(n_z, mine)], axis=1
    )
    small = jnp.concatenate([first_sums[:3], second_sums[:3], split.reshape(-1, width)], axis=0)
    small = jnp.pad(small, ((0, -small.shape[0] % 16), (0, 0))).astype(bf16)
    small_rows = small.shape[0]

    small = add(small, plane.swap(small, 1))
    kept = list(weight_grads(core, other, small))
    arrived = plane.to_places(kept)
    kept[0], inner_on, outer_on = together(kept[0], inner_on, outer_on)
    feed_parts = [
        jnp.concatenate(
            [
                add(inner_stay[0, s], inner_came[0, s], inner_on[s]),
                add(outer_stay[0, s], outer_came[0, s], outer_on[s]),
            ],
            axis=1,
        )
        for s in range(n_z)
    ]
    feed_line = [plane.shift(feed_parts[s], -s) for s in others]
    output = copied(output)
    arrived, feed_line, output = together(arrived, feed_line, output)
    small = add(small, *[a[-small_rows:] for a in arrived])
    count = 2 * mine // n_places
    attention_parts = [
        add(*[a[s * count : (s + 1) * count] for a in [kept[0]] + arrived]) for s in range(n_z)
    ]
    attention_line = [
        plane.shift(jnp.concatenate([attention_parts[s], small], axis=0), s) for s in others
    ]
    feed_total = plane.over_groups(add(feed_parts[0], *feed_line))
    feed_arrived = plane.to_places([feed_total] * n_places)
    attention_line, feed_arrived, tokens_grad = together(
        attention_line, feed_arrived, tokens_grad
    )
    attention_total = plane.over_groups(
        add(attention_parts[0], *[a[:count] for a in attention_line])
    )
    small = plane.over_groups(add(small, *[a[count:] for a in attention_line])).astype(f32)
    arrived = plane.to_places([attention_total] * n_places)
    feed_half = plane.from_places(feed_total, feed_arrived)
    feed_other = plane.swap(feed_half, 1)
    feed_grad = plane.by_core(feed_half, feed_other).transpose(1, 0, 2, 3).reshape(units, -1)
    inner_grad = feed_grad[:, :width].T.astype(f32)
    outer_grad = feed_grad[:, width:].astype(f32)
    arrived, inner_grad, outer_grad = together(arrived, inner_grad, outer_grad)
    attention_half = plane.from_places(attention_total, arrived)
    attention_other = plane.swap(attention_half, 1)
    grad_list = plane.by_core(attention_half, attention_other)
    grad_list = grad_list.reshape(2, n_places, 2, mine // n_places, width)
    grad_list = grad_list.transpose(0, 2, 1, 3, 4).reshape(4, mine, width)

    shared = small[:6]
    split_rows = n_z * split.shape[1] // width
    split = lax.dynamic_slice_in_dim(
        small[6 : 6 + split_rows].reshape(n_z, -1), z, 1, 0
    )[0]

    return (
        output,
        tokens_grad,
        grad_list[0].T.astype(f32),
        split[units : units + mine],
        grad_list[1].T.astype(f32),
        grad_list[2].T.astype(f32),
        split[units + mine :],
        grad_list[3].astype(f32),
        shared[0],
        shared[1],
        shared[2],
        inner_grad,
        split[:units],
        outer_grad,
        shared[3],
        shared[4],
        shared[5],
    )


def solution(mesh):
    n_dp, n_z = mesh.shape["dp"], mesh.shape["tensor"]
    in_specs = (
        P("dp", None),
        P("dp", None),
        P("dp"),
        P(None, "tensor"),
        P("tensor"),
        P(None, "tensor"),
        P(None, "tensor"),
        P("tensor"),
        P("tensor", None),
        P(),
        P(),
        P(),
        P(None, "tensor"),
        P("tensor"),
        P("tensor", None),
        P(),
        P(),
        P(),
        P("dp", None),
    )
    out_specs = (
        P("dp", None),
        P("dp", None),
        P(None, "tensor"),
        P("tensor"),
        P(None, "tensor"),
        P(None, "tensor"),
        P("tensor"),
        P("tensor", None),
        P(),
        P(),
        P(),
        P(None, "tensor"),
        P("tensor"),
        P("tensor", None),
        P(),
        P(),
        P(),
    )

    def program(*args):
        return on_device(n_dp, n_z, *args)

    return jax.shard_map(
        program, mesh=mesh, in_specs=in_specs, out_specs=out_specs, check_vma=False
    )
```

```python
import functools

import jax
import jax.numpy as jnp
from jax import lax
from jax.experimental import pallas as pl
from jax.experimental.pallas import tpu as pltpu
from jax.sharding import PartitionSpec as P

HEAD = 64
BUCKET = 512
ITEMS = 8


negative_fill = -1e30
epsilon = 1e-06
f32 = jnp.float32
bf16 = jnp.bfloat16
VMEM_BYTES = 56 * 1024 * 1024


def dot(left, right):
    return jnp.dot(left, right, preferred_element_type=f32)


def contract_rows(left, right):
    return lax.dot_general(left, right, (((0,), (0,)), ((), ())), preferred_element_type=f32)


def contract_cols(left, right):
    return lax.dot_general(left, right, (((1,), (1,)), ((), ())), preferred_element_type=f32)


def norm_rows(values):
    centred = values - jnp.mean(values, axis=1, keepdims=True)
    inv_scale = lax.rsqrt(jnp.mean(centred * centred, axis=1, keepdims=True) + epsilon)
    return centred * inv_scale, inv_scale


def norm_back(grad_rows, norm_gain, normed, inv_scale):
    scaled = grad_rows * norm_gain
    return inv_scale * (
        scaled
        - jnp.mean(scaled, axis=1, keepdims=True)
        - normed * jnp.mean(scaled * normed, axis=1, keepdims=True)
    )


def column_sum(matrix):
    return jnp.sum(matrix.astype(f32), axis=0, keepdims=True)


def fixed(shape):
    return pl.BlockSpec(shape, lambda *_: (0,) * len(shape))


def cost(microseconds):
    return pl.CostEstimate(
        flops=int(microseconds * 6e7),
        bytes_accessed=int(microseconds * 6e4),
        transcendentals=0,
    )


def params(axes):
    return pltpu.CompilerParams(
        dimension_semantics=("arbitrary",) * axes, vmem_limit_bytes=VMEM_BYTES
    )


def item_places(lengths_ref, row, shape, axis):
    places = lax.broadcasted_iota(jnp.int32, shape, axis)
    end = jnp.int32(0)
    items = jnp.zeros(shape, jnp.int32)
    for slot in range(ITEMS):
        end = end + lengths_ref[row, slot]
        items = items + (places >= end).astype(jnp.int32)
    return items


def as_column(row):
    return jnp.broadcast_to(row.astype(f32), (8, row.shape[1])).T[:, :1]


def mask_bias(lengths_ref, row, key_mask):
    shape = (BUCKET, BUCKET)
    diagonal = lax.broadcasted_iota(jnp.int32, shape, 0) == lax.broadcasted_iota(
        jnp.int32, shape, 1
    )
    item_row = item_places(lengths_ref, row, (1, BUCKET), 1)
    item_column = item_places(lengths_ref, row, (BUCKET, 1), 0)
    code_column = jnp.where(as_column(key_mask) == 1.0, item_column, -1)
    return jnp.where((code_column == item_row) | diagonal, 0.0, negative_fill).astype(f32)


def attend_forward_kernel(
    lengths_ref, tokens_ref, query_ref, key_ref, value_ref, biases_ref, key_mask_ref, mixed_ref,
):
    mine = query_ref.shape[0]
    rows = tokens_ref[...]
    queries = contract_cols(query_ref[...], rows) + as_column(biases_ref[0:1, :mine])
    queries = (queries.astype(bf16) * HEAD ** (-0.5)).astype(bf16)
    keys = contract_cols(rows, key_ref[...]).astype(bf16)
    values = contract_cols(value_ref[...], rows) + as_column(biases_ref[0:1, mine : 2 * mine])
    values = values.astype(bf16)
    bias = mask_bias(lengths_ref, pl.program_id(0), key_mask_ref[0])
    for head in range(mine // HEAD):
        at = slice(head * HEAD, (head + 1) * HEAD)
        scores = dot(keys[:, at], queries[at]) + bias
        exponent = jnp.exp(scores - jnp.max(scores, axis=0, keepdims=True))
        total = jnp.sum(exponent, axis=0, keepdims=True)
        mixed_ref[0, 0, at] = (dot(values[at], exponent.astype(bf16)) / total).astype(bf16)
    mixed_ref[0, 0, mine:] = biases_ref[...]


def attend_forward(n_z, lengths, tokens, query, key, value, biases, key_mask):
    blocks = lengths.shape[0]
    own = blocks // n_z
    mine, width = key.shape
    whole = (n_z, own, mine + biases.shape[0], BUCKET)
    return pl.pallas_call(
        attend_forward_kernel,
        grid=(blocks,),
        in_specs=[
            pl.BlockSpec(memory_space=pltpu.SMEM),
            pl.BlockSpec((BUCKET, width), lambda b: (b, 0)),
            fixed((mine, width)),
            fixed((mine, width)),
            fixed((mine, width)),
            fixed(biases.shape),
            pl.BlockSpec((1, 1, BUCKET), lambda b: (b, 0, 0)),
        ],
        out_specs=pl.BlockSpec((1, 1) + whole[2:], lambda b: (b // own, b % own, 0, 0)),
        out_shape=jax.ShapeDtypeStruct(whole, bf16),
        compiler_params=params(1),
        name="attend_forward",
        cost_estimate=cost(12),
    )(lengths, tokens, query, key, value, biases, key_mask)


def fetch_units(step, picks, own_ref, halves, units, sems):
    feed_rows, twice = units.shape[2:]
    cut = feed_rows // 2

    def copies(number):
        slot = number % 2
        row = pl.multiple_of(picks[number] * feed_rows, 16)
        ends = [
            (own_ref.at[pl.ds(row, feed_rows), :twice], units.at[slot, 0]),
            (halves[number][0].at[:, :, :twice], units.at[slot, 1:, :cut]),
            (halves[number][1].at[:, :, :twice], units.at[slot, 1:, cut:]),
        ]
        return [
            pltpu.make_async_copy(source, target, sems.at[slot, i])
            for i, (source, target) in enumerate(ends)
        ]

    for number in range(len(halves)):

        @pl.when(step == number)
        def _(number=number):
            if number == 0:
                for copy in copies(0):
                    copy.start()
            if number + 1 < len(halves):
                for copy in copies(number + 1):
                    copy.start()
            for copy in copies(number):
                copy.wait()

    return units.at[lax.rem(step, 2)]


def fetch_mixer(picks, own_ref, halves, mixer, sems):
    feed_rows = mixer.shape[1] // 8
    cut = feed_rows // 2
    start = own_ref.shape[1] - mixer.shape[2]
    ends = [(own_ref.at[:, start:], mixer.at[0])]
    for number, pair in enumerate(halves):
        for half in range(2):
            row = pl.multiple_of(picks[number] * feed_rows + half * cut, 16)
            ends.append((pair[half].at[:, :, start:], mixer.at[1:, pl.ds(row, cut)]))
    copies = [
        pltpu.make_async_copy(source, target, sems.at[i])
        for i, (source, target) in enumerate(ends)
    ]
    for copy in copies:
        copy.start()
    for copy in copies:
        copy.wait()


def split_units(units):
    width = units.shape[2] // 2
    return units[:, :, :width].reshape(-1, width), units[:, :, width:].reshape(-1, width)


ANYWHERE = pl.BlockSpec(memory_space=pl.ANY)


def normal_parts(values):
    bell = jnp.exp(-0.5 * values * values)
    t = 1.0 / (1.0 + 0.23164189 * jnp.abs(values))
    series = 0.530702715
    for factor in (-0.7265760135, 0.7107068705, -0.142248368, 0.127414796):
        series = series * t + factor
    above = series * t * bell
    return jnp.where(values >= 0.0, 1.0 - above, above), bell


def feed_forward_kernel(
    info_ref, lengths_ref, mixed_ref, tokens_ref, cotangent_ref, vectors_ref, bias_ref, own_ref,
    *rest,
):
    halves, rest = list(zip(rest[:16:2], rest[1:16:2])), rest[16:]
    (
        hidden_ref, slope_ref, output_ref, normed_low_ref, first_normed_ref, first_scale_ref,
        grad_second_ref, grad_outer_ref, sums_ref, second_sum, units, sems,
        mixer, mixer_sems,
    ) = rest
    step = pl.program_id(0)
    picks = [(info_ref[1] ^ (k % 4)) * 2 + (info_ref[2] ^ (k // 4)) for k in range(8)]
    weights = fetch_units(step, picks, own_ref, halves, units, sems)
    output_bias, first_gain, first_shift, outer_bias, second_gain, second_shift = (
        vectors_ref[i : i + 1, :] for i in range(6)
    )

    @pl.when(step == 0)
    def _():
        fetch_mixer(picks, own_ref, halves, mixer, mixer_sems)
        n_z, own, mine, _ = mixed_ref.shape
        attended = output_bias + jnp.concatenate(
            [
                sum(
                    dot(mixer[s, :, :mine], mixed_ref[lax.rem(info_ref[0] + n_z - s, n_z), b])
                    for s in range(n_z)
                ).T
                for b in range(own)
            ],
            axis=0,
        )
        normed, inv_scale = norm_rows(tokens_ref[...].astype(f32) + attended)
        whole = normed * first_gain + first_shift
        first_normed_ref[...] = normed
        first_scale_ref[...] = inv_scale
        normed_low_ref[...] = whole.astype(bf16)
        second_sum[...] = whole + outer_bias

    inner, outer = split_units(weights)
    inner_pre = contract_cols(normed_low_ref[...], inner) + bias_ref[0]
    normal_cdf, bell = normal_parts(inner_pre)
    hidden = (inner_pre * normal_cdf).astype(bf16)
    hidden_ref[...] = hidden.T
    slope_ref[...] = (normal_cdf + inner_pre * bell * 0.3989422804014327).astype(bf16)
    second_sum[...] += dot(hidden, outer)

    @pl.when(step == pl.num_programs(0) - 1)
    def _():
        normed, inv_scale = norm_rows(second_sum[...])
        blocks = normed.shape[0] // BUCKET
        live = jnp.concatenate(
            [
                (item_places(lengths_ref, info_ref[0] * blocks + b, (BUCKET, 1), 0) < ITEMS)
                for b in range(blocks)
            ],
            axis=0,
        ).astype(f32)
        output_ref[...] = ((normed * second_gain + second_shift) * live).astype(bf16)
        grad_final = cotangent_ref[...].astype(f32) * live
        grad_second = norm_back(grad_final, second_gain, normed, inv_scale)
        grad_outer = grad_second.astype(bf16)
        grad_second_ref[...] = grad_second
        grad_outer_ref[...] = grad_outer
        sums_ref[0:1, :] = column_sum(grad_outer)
        sums_ref[1:2, :] = column_sum(grad_final * normed)
        sums_ref[2:3, :] = column_sum(grad_final)


def feed_forward(info, lengths, mixed, tokens, cotangent, vectors, biases, own, halves):
    n_z, buckets = mixed.shape[:2]
    rows = buckets * BUCKET
    width = tokens.shape[1]
    mine = width // n_z
    feed_rows, twice = own.shape[0] // 8, 2 * width
    chunk = n_z * feed_rows
    whole = fixed((rows, width))
    my_rows = pl.BlockSpec((rows, width), lambda j, info: (info[0], 0))
    columns = pl.BlockSpec((rows, chunk), lambda j, info: (0, j))
    shapes = [
        ((8 * chunk, rows), bf16, pl.BlockSpec((chunk, rows), lambda j, info: (j, 0))),
        ((rows, 8 * chunk), bf16, columns),
        ((rows, width), bf16, whole),
        ((rows, width), bf16, whole),
        ((rows, width), f32, whole),
        ((rows, 1), f32, fixed((rows, 1))),
        ((rows, width), f32, whole),
        ((rows, width), bf16, whole),
        ((8, width), f32, fixed((8, width))),
    ]
    return pl.pallas_call(
        feed_forward_kernel,
        grid_spec=pltpu.PrefetchScalarGridSpec(
            num_scalar_prefetch=1,
            grid=(8,),
            in_specs=[
                pl.BlockSpec(memory_space=pltpu.SMEM),
                fixed((n_z, buckets, mine, BUCKET)),
                my_rows,
                my_rows,
                fixed((8, width)),
                pl.BlockSpec((1, 1, chunk), lambda j, info: (j, 0, 0)),
                ANYWHERE,
            ]
            + [ANYWHERE] * 16,
            out_specs=[spec for _, _, spec in shapes],
            scratch_shapes=[
                pltpu.VMEM((rows, width), f32),
                pltpu.VMEM((2, n_z, feed_rows, twice), bf16),
                pltpu.SemaphoreType.DMA((2, 3)),
                pltpu.VMEM((n_z, width, own.shape[1] - twice), bf16),
                pltpu.SemaphoreType.DMA((17,)),
            ],
        ),
        out_shape=[jax.ShapeDtypeStruct(shape, kind) for shape, kind, _ in shapes],
        compiler_params=params(1),
        name="feed_forward",
        cost_estimate=cost(21),
    )(info, lengths, mixed, tokens, cotangent, vectors, biases, own, *halves)


STAY = ((0, 1), (0, 2))
GO = ((2, 3), (1, 3))


def feed_back_kernel(
    first, count, keeps, info_ref, grad_outer_ref, normed_low_ref, hidden_ref, slope_ref,
    own_ref, start_ref, *rest,
):
    halves = list(zip(rest[: 2 * count : 2], rest[1 : 2 * count : 2]))
    rest = rest[2 * count :]
    if keeps:
        other_ref, norm_refs, rest = rest[0], rest[1:4], rest[4:]
        stay_refs, go_refs, rest = rest[0:2], rest[2:4], rest[4:]
        bias_grad_ref, grad_first_ref, grad_attended_ref, sums_ref, units, sems = rest[:6]
        grad_normed_ref = rest[6]
    else:
        grad_ref, bias_grad_ref, grad_normed_ref, units, sems = rest
    step = pl.program_id(0)
    side = info_ref[2] if keeps else 1 - info_ref[2]
    picks = [(info_ref[1] ^ (first + k)) * 2 + side for k in range(count)]
    weights = fetch_units(step, picks, own_ref, halves, units, sems)

    @pl.when(step == 0)
    def _():
        grad_normed_ref[...] = start_ref[...]

    n_z, feed_rows, twice = weights.shape
    width = twice // 2
    inner, outer = split_units(weights)
    grad_outer = grad_outer_ref[...]
    grad_hidden = contract_cols(grad_outer, outer)
    grad_inner = (grad_hidden * slope_ref[...].astype(f32)).astype(bf16)
    outer_grad = dot(hidden_ref[...], grad_outer).reshape(n_z, feed_rows, width)
    inner_grad = contract_rows(grad_inner, normed_low_ref[...]).reshape(n_z, feed_rows, width)
    bias_grad_ref[0] = column_sum(grad_inner)
    grad_normed_ref[...] += dot(grad_inner, inner)

    if keeps:
        for number in range(4):

            @pl.when(step == number)
            def _(number=number):
                for track, value in enumerate((inner_grad, outer_grad)):
                    at = slice(track * width, (track + 1) * width)
                    value = (value + other_ref[0, :, :, at].astype(f32)).astype(bf16)
                    ref = stay_refs[track] if number in STAY[track] else go_refs[track]
                    ref[0] = value

        @pl.when(step == pl.num_programs(0) - 1)
        def _():
            first_normed_ref, first_scale_ref, vectors_ref = norm_refs
            grad_rows, normed = grad_normed_ref[...], first_normed_ref[...]
            grad_first = norm_back(grad_rows, vectors_ref[1:2, :], normed, first_scale_ref[...])
            grad_attended = grad_first.astype(bf16)
            grad_first_ref[...] = grad_first
            grad_attended_ref[...] = grad_attended
            sums_ref[0:1, :] = column_sum(grad_attended)
            sums_ref[1:2, :] = column_sum(grad_rows * normed)
            sums_ref[2:3, :] = column_sum(grad_rows)

    else:
        grad_ref[0, :, :, :width] = inner_grad.astype(bf16)
        grad_ref[0, :, :, width:] = outer_grad.astype(bf16)


def feed_back(
    first, count, info, grad_outer, normed_low, hidden, slope, own, start, halves,
    other=None, norm=None,
):
    rows, width = grad_outer.shape
    keeps = other is not None
    feed_rows, twice = own.shape[0] // 8, 2 * width
    n_z = halves[0].shape[0] + 1
    chunk = n_z * feed_rows
    flip = 0 if keeps else 1
    columns = pl.BlockSpec((rows, chunk), lambda i, info: (0, 4 * flip + first + i))
    whole = fixed((rows, width))
    part = (n_z, feed_rows, twice)
    track = (2, n_z, feed_rows, width)
    unit_rows = pl.BlockSpec((chunk, rows), lambda i, info: (4 * flip + first + i, 0))
    in_specs = [whole, whole, unit_rows, columns, ANYWHERE, whole] + [ANYWHERE] * (2 * count)
    args = [grad_outer, normed_low, hidden, slope, own, start] + halves
    bias_shape = (
        (count, 1, chunk),
        f32,
        pl.BlockSpec((1, 1, chunk), lambda i, info: (i, 0, 0)),
    )
    scratch = [pltpu.VMEM((2,) + part, bf16), pltpu.SemaphoreType.DMA((2, 3))]

    def one(shape, at):
        return pl.BlockSpec((1,) + shape[1:], lambda i, info: (at(i), 0, 0, 0))

    if keeps:
        early, late = (lambda i: jnp.minimum(i, 1)), (lambda i: jnp.maximum(i - 2, 0))
        in_specs.append(one((4,) + part, lambda i: i))
        in_specs += [whole, fixed((rows, 1)), fixed((8, width))]
        args += [other] + list(norm)
        slow, slower = (lambda i: i // 2), (lambda i: jnp.maximum(i - 1, 0) // 2)
        shapes = [(track, bf16, one(track, at)) for at in (early, slow, late, slower)] + [
            bias_shape,
            ((rows, width), f32, whole),
            ((rows, width), bf16, whole),
            ((8, width), f32, fixed((8, width))),
        ]
        scratch.append(pltpu.VMEM((rows, width), f32))
    else:
        shapes = [
            ((count,) + part, bf16, one((count,) + part, lambda i: i)),
            bias_shape,
            ((rows, width), f32, whole),
        ]
    return pl.pallas_call(
        functools.partial(feed_back_kernel, first, count, keeps),
        grid_spec=pltpu.PrefetchScalarGridSpec(
            num_scalar_prefetch=1,
            grid=(count,),
            in_specs=in_specs,
            out_specs=[spec for _, _, spec in shapes],
            scratch_shapes=scratch,
        ),
        out_shape=[jax.ShapeDtypeStruct(shape, kind) for shape, kind, _ in shapes],
        compiler_params=params(1),
        name="feed_back_own" if keeps else "feed_back",
        cost_estimate=cost(3 * count),
    )(info, *args)


def finish_feed_kernel(core_ref, own_ref, other_ref, inner_ref, outer_ref, inner_rows):
    places, count, twice = own_ref.shape
    width = twice // 2
    for source, side in ((own_ref, core_ref[0]), (other_ref, 1 - core_ref[0])):
        for place in range(places):
            row = pl.multiple_of((2 * place + side) * count, 16)
            inner_rows[pl.ds(row, count), :] = source[place, :, :width].astype(f32)
            outer_ref[pl.ds(row, count), :] = source[place, :, width:].astype(f32)
    inner_ref[...] = inner_rows[...].T


def finish_feed(core, own, other):
    places, count, twice = own.shape
    shape = (2 * places * count, twice // 2)
    inner_shape = (shape[1], shape[0])
    return pl.pallas_call(
        finish_feed_kernel,
        grid_spec=pltpu.PrefetchScalarGridSpec(
            num_scalar_prefetch=1,
            grid=(1,),
            in_specs=[fixed(own.shape), fixed(other.shape)],
            out_specs=[fixed(inner_shape), fixed(shape)],
            scratch_shapes=[pltpu.VMEM(shape, f32)],
        ),
        out_shape=[
            jax.ShapeDtypeStruct(inner_shape, f32),
            jax.ShapeDtypeStruct(shape, f32),
        ],
        compiler_params=params(1),
        name="finish_feed",
        cost_estimate=cost(5),
    )(core, own, other)


def project_kernel(place_ref, tokens_ref, weights_ref, biases_ref, query_ref, key_ref, value_ref):
    rows = tokens_ref[...]
    width = rows.shape[1]
    queries = contract_cols(weights_ref[:, :width], rows) + as_column(biases_ref[0:1, :])
    query_ref[...] = (queries.astype(bf16) * HEAD ** (-0.5)).astype(bf16)
    key_ref[...] = contract_cols(rows, weights_ref[:, width : 2 * width]).astype(bf16)
    values = contract_cols(rows, weights_ref[:, 2 * width :]) + biases_ref[1:2, :]
    value_ref[...] = values.astype(bf16)


def project(place, tokens, weights, biases, buckets):
    width = tokens.shape[1]
    part = width // 3
    shapes = [
        ((buckets, width, BUCKET), pl.BlockSpec((None, part, BUCKET), lambda b, j, _: (b, j, 0))),
        ((buckets * BUCKET, width), pl.BlockSpec((BUCKET, part), lambda b, j, _: (b, j))),
        ((buckets * BUCKET, width), pl.BlockSpec((BUCKET, part), lambda b, j, _: (b, j))),
    ]
    return pl.pallas_call(
        project_kernel,
        grid_spec=pltpu.PrefetchScalarGridSpec(
            num_scalar_prefetch=1,
            grid=(buckets, 3),
            in_specs=[
                pl.BlockSpec((BUCKET, width), lambda b, j, place: (place[0] * buckets + b, 0)),
                pl.BlockSpec((part, 3 * width), lambda b, j, place: (j, 0)),
                pl.BlockSpec((8, part), lambda b, j, place: (0, j)),
            ],
            out_specs=[spec for _, spec in shapes],
        ),
        out_shape=[jax.ShapeDtypeStruct(shape, bf16) for shape, _ in shapes],
        compiler_params=params(2),
        name="project",
        cost_estimate=cost(5),
    )(place, tokens, weights, biases)


def attend_back_kernel(
    place_ref, lengths_ref, grad_attended_ref, grad_first_ref, weights_ref, query_ref, key_ref,
    value_ref, key_mask_ref,
    grads_ref, tokens_grad_ref, sums_ref,
    bias, grad_mixed_t, whole, weights, sem,
):
    pair = pl.program_id(1)
    pairs, width = whole.shape[1], weights.shape[0]
    fetch = pltpu.make_async_copy(weights_ref, weights, sem)

    @pl.when(pair == 0)
    def _():
        fetch.start()
        row = place_ref[0] * pl.num_programs(0) + pl.program_id(0)
        bias[...] = mask_bias(lengths_ref, row, key_mask_ref[0])
        fetch.wait()
        grad_mixed_t[...] = contract_cols(
            weights[:, 3 * width :], grad_attended_ref[...]
        ).astype(bf16)

    queries, keys, values = query_ref[...], key_ref[...], value_ref[...]
    start = pl.multiple_of(pair * keys.shape[1], 128)
    grad_mixed = grad_mixed_t[pl.ds(start, keys.shape[1]), :]
    keys_t = keys.T
    grad_queries, grad_keys, grad_values = [], [], []
    for head in range(keys.shape[1] // HEAD):
        at = slice(head * HEAD, (head + 1) * HEAD)
        scores = dot(keys[:, at], queries[at]) + bias[...]
        exponent = jnp.exp(scores - jnp.max(scores, axis=0, keepdims=True))
        probs = exponent * (1.0 / jnp.sum(exponent, axis=0, keepdims=True))
        grad_probs = dot(values[:, at], grad_mixed[at])
        shift = jnp.sum(probs * grad_probs, axis=0, keepdims=True)
        grad_scores = (probs * (grad_probs - shift)).astype(bf16)
        grad_values.append(contract_cols(probs.astype(bf16), grad_mixed[at]))
        grad_keys.append(contract_cols(grad_scores, queries[at]))
        grad_queries.append(dot(keys_t[at], grad_scores) * HEAD ** (-0.5))
    query_t = jnp.concatenate(grad_queries, axis=0).astype(bf16)
    found = (
        query_t.T,
        jnp.concatenate(grad_keys, axis=1).astype(bf16),
        jnp.concatenate(grad_values, axis=1).astype(bf16),
    )
    for number, grad in enumerate(found):
        grads_ref[number, 0] = query_t if number == 0 else grad.T
        whole[number, pair] = grad
    sums_ref[0, 0:1, :] = column_sum(found[0])
    sums_ref[0, 1:2, :] = column_sum(found[2])

    @pl.when(pair == pl.num_programs(1) - 1)
    def _():
        total = grad_first_ref[...]
        for number in range(3):
            grad = jnp.concatenate([whole[number, i] for i in range(pairs)], axis=1)
            total += dot(grad, weights[:, number * width : (number + 1) * width])
        tokens_grad_ref[...] = total.astype(bf16)


def attend_back(place, lengths, grad_attended, grad_first, weights, queries, keys, values, key_mask):
    rows, width = grad_attended.shape
    blocks = rows // BUCKET
    pair = 2 * HEAD
    by_bucket = pl.BlockSpec((BUCKET, width), lambda b, h, place: (b, 0))
    by_pair = pl.BlockSpec((BUCKET, pair), lambda b, h, place: (b, h))
    return pl.pallas_call(
        attend_back_kernel,
        grid_spec=pltpu.PrefetchScalarGridSpec(
            num_scalar_prefetch=1,
            grid=(blocks, width // pair),
            in_specs=[
                pl.BlockSpec(memory_space=pltpu.SMEM),
                by_bucket,
                by_bucket,
                ANYWHERE,
                pl.BlockSpec((None, pair, BUCKET), lambda b, h, place: (b, h, 0)),
                by_pair,
                by_pair,
                pl.BlockSpec((1, 1, BUCKET), lambda b, h, place: (place[0] * blocks + b, 0, 0)),
            ],
            out_specs=[
                pl.BlockSpec((3, 1, pair, BUCKET), lambda b, h, place: (0, b, h, 0)),
                by_bucket,
                pl.BlockSpec((1, 8, pair), lambda b, h, place: (b, 0, h)),
            ],
            scratch_shapes=[
                pltpu.VMEM((BUCKET, BUCKET), f32),
                pltpu.VMEM((width, BUCKET), bf16),
                pltpu.VMEM((3, width // pair, BUCKET, pair), bf16),
                pltpu.VMEM(weights.shape, bf16),
                pltpu.SemaphoreType.DMA(()),
            ],
        ),
        out_shape=[
            jax.ShapeDtypeStruct((3, blocks, width, BUCKET), bf16),
            jax.ShapeDtypeStruct((rows, width), bf16),
            jax.ShapeDtypeStruct((blocks, 8, width), f32),
        ],
        compiler_params=params(2),
        name="attend_back",
        cost_estimate=cost(20),
    )(place, lengths, grad_attended, grad_first, weights, queries, keys, values, key_mask)


def attention_grads_kernel(
    n_places, adds, info_ref, grads_ref, mixed_ref, tokens_ref, grad_attended_ref, *rest
):
    if adds:
        other_ref, small_ref = rest[:2]
        out_refs, whole = rest[2:-1], rest[-1]
    else:
        (out_ref, whole) = rest
    step = pl.program_id(0)
    which = info_ref[step]
    n_z, buckets, mine, _ = mixed_ref.shape
    count = mine // n_places

    @pl.when(which < 3)
    def _():
        whole[...] = sum(
            dot(grads_ref[0, b], tokens_ref[b * BUCKET : (b + 1) * BUCKET, :])
            for b in range(buckets)
        ).astype(bf16)

    @pl.when(which == 3)
    def _():
        for t in range(n_z):
            whole[t * mine : (t + 1) * mine, :] = sum(
                dot(mixed_ref[t, b], grad_attended_ref[b * BUCKET : (b + 1) * BUCKET, :])
                for b in range(buckets)
            ).astype(bf16)

    for number in range(n_places):
        for s in range(n_z):
            start = lax.rem(info_ref[2] + s, n_z) * mine + (info_ref[3] ^ number) * count
            value = whole[pl.ds(pl.multiple_of(start, 16), count), :]
            if adds:
                value = value.astype(f32) + other_ref[number, s, 0].astype(f32)
                row = (2 * s + step) * count
                out_refs[number][pl.ds(pl.multiple_of(row, 16), count), :] = value.astype(bf16)
            else:
                out_ref[number, s, 0] = value

    if adds:
        for number in range(n_places):
            out_refs[number][2 * n_z * count :, :] = small_ref[...]


def attention_grads(n_places, info, grads, mixed, tokens, grad_attended, other=None, small=None):
    rows, width = grad_attended.shape
    n_z, buckets = mixed.shape[:2]
    mine = width // n_z
    count = mine // n_places
    parts = (n_places, n_z, 1, count, width)
    by_step = pl.BlockSpec(parts, lambda i, info: (0, 0, i, 0, 0))
    in_specs = [
        pl.BlockSpec(
            (1, buckets, width, BUCKET), lambda i, info: (jnp.minimum(info[i], 2), 0, 0, 0)
        ),
        fixed((n_z, buckets, mine, BUCKET)),
        pl.BlockSpec((rows, width), lambda i, info: (info[2], 0)),
        fixed((rows, width)),
    ]
    args = [grads, mixed, tokens, grad_attended]
    if other is None:
        shapes = [((n_places, n_z, 2, count, width), by_step)]
    else:
        in_specs += [by_step, fixed(small.shape)]
        args += [other, small]
        flat = (2 * n_z * count + small.shape[0], width)
        shapes = [(flat, fixed(flat))] * n_places
    return pl.pallas_call(
        functools.partial(attention_grads_kernel, n_places, other is not None),
        grid_spec=pltpu.PrefetchScalarGridSpec(
            num_scalar_prefetch=1,
            grid=(2,),
            in_specs=in_specs,
            out_specs=[spec for _, spec in shapes],
            scratch_shapes=[pltpu.VMEM((width, width), bf16)],
        ),
        out_shape=[jax.ShapeDtypeStruct(shape, bf16) for shape, _ in shapes],
        compiler_params=params(1),
        name="attention_grads",
        cost_estimate=cost(6),
    )(info, *args)


def together(*values):
    return lax.optimization_barrier(values)


def add(first, *others):
    total = first.astype(f32)
    for other in others:
        total = total + other.astype(f32)
    return total.astype(bf16)


class Plane:
    def __init__(self, n_dp, n_z):
        self.n_dp, self.n_z = n_dp, n_z
        self.n_group = min(n_dp, 8)
        self.n_places = self.n_group // 2
        self.dp = lax.axis_index("dp")
        self.z = lax.axis_index("tensor")
        self.index = lax.rem(self.dp, self.n_group)
        self.core = self.index & 1
        self.place = self.index >> 1

    def swap(self, array, bits):
        return lax.ppermute(array, "dp", [(i, i ^ bits) for i in range(self.n_dp)])

    def shift(self, array, by):
        n = self.n_z
        return lax.ppermute(array, "tensor", [(i, (i + by) % n) for i in range(n)])

    def gather(self, piece):
        if self.n_dp == self.n_group:
            whole = lax.all_gather(piece, ("tensor", "dp"))
            return whole.reshape((self.n_z, self.n_group) + piece.shape)
        groups = [
            list(range(i, i + self.n_group)) for i in range(0, self.n_dp, self.n_group)
        ]
        line = lax.all_gather(piece, "tensor")
        return lax.all_gather(line, "dp", axis=1, axis_index_groups=groups)

    def turned(self, array):
        bit = 1
        while bit < self.n_group:
            lead = array.reshape((-1, 2, bit) + array.shape[1:])
            array = jnp.where((self.index & bit) != 0, lead[:, ::-1], lead).reshape(array.shape)
            bit *= 2
        return array

    def to_places(self, parts):
        return [self.swap(parts[number], 2 * number) for number in range(1, self.n_places)]

    def from_places(self, own, arrived):
        found = jnp.stack([own] + arrived)
        bit = 1
        while bit < self.n_places:
            lead = found.reshape((-1, 2, bit) + own.shape)
            flipped = lead[:, ::-1]
            found = jnp.where((self.place & bit) != 0, flipped, lead).reshape(found.shape)
            bit *= 2
        return found

    def by_core(self, own, other):
        return jnp.where(
            self.core == 1, jnp.stack([other, own]), jnp.stack([own, other])
        )

    def over_groups(self, array):
        bit = self.n_group
        while bit < self.n_dp:
            array = add(array, self.swap(array, bit))
            bit *= 2
        return array


def on_device(
    n_dp,
    n_z,
    tokens,
    lengths,
    key_mask,
    query_weight,
    query_bias,
    key_weight,
    value_weight,
    value_bias,
    output_weight,
    output_bias,
    first_gain,
    first_shift,
    inner_weight,
    inner_bias,
    outer_weight,
    outer_bias,
    second_gain,
    second_shift,
    cotangent,
):
    width = tokens.shape[1]
    mine = query_weight.shape[1]
    units = inner_weight.shape[1]
    all_rows = tokens.shape[0]
    all_blocks = all_rows // BUCKET
    rows = all_rows // n_z
    plane = Plane(n_dp, n_z)
    z, core, place, index = plane.z, plane.core, plane.place, plane.index
    n_places = plane.n_places
    others = range(1, n_z)

    mixer_t = jnp.pad(output_weight.T, ((0, 0), (0, -mine % 128)))
    feed_rows = units // plane.n_group
    head_rows = mine // plane.n_group
    piece = jnp.concatenate(
        [
            lax.dynamic_slice_in_dim(inner_weight, index * feed_rows, feed_rows, 1).T,
            lax.dynamic_slice_in_dim(outer_weight, index * feed_rows, feed_rows, 0),
            lax.dynamic_slice_in_dim(mixer_t, index * feed_rows, feed_rows, 0),
        ],
        axis=1,
    )
    line = [plane.shift(piece, s) for s in others]

    query_t, key_t, value_t = query_weight.T, key_weight.T, value_weight.T
    attention_own = jnp.concatenate([query_t, key_t, value_t, output_weight], axis=1)
    attention_weights = plane.gather(
        lax.dynamic_slice_in_dim(attention_own, index * head_rows, head_rows, 0)
    ).reshape(width, 4 * width)

    key_mask_rows = key_mask.reshape(all_blocks, 1, BUCKET)
    bias_row = jnp.concatenate([query_bias, value_bias, inner_bias])
    bias_rows = jnp.pad(bias_row, (0, 16 * BUCKET - bias_row.shape[0])).reshape(16, BUCKET)
    mixed = attend_forward(
        n_z, lengths, tokens, query_t, key_t, value_t, bias_rows, key_mask_rows
    )
    _, line = together(mixed, line)
    mixed = lax.all_to_all(mixed, "tensor", 0, 0)

    cut = feed_rows // 2
    near = [jnp.stack([part[:cut] for part in line]), jnp.stack([part[cut:] for part in line])]
    by_x, by_y = [plane.swap(half, 2) for half in near], [plane.swap(half, 4) for half in near]
    far = [plane.swap(by_x[0], 4), plane.swap(by_y[1], 2)]
    by_x[1], by_y[0], far, mixed = together(by_x[1], by_y[0], far, mixed)
    keep = near + by_x + by_y + far
    send = [plane.swap(half, 1) for half in near + by_x + by_y]
    send = send + [plane.swap(half, 1) for half in far]
    own_units = jnp.concatenate([inner_weight.T, outer_weight, mixer_t], axis=1)

    biases = mixed[:, 0, mine:].reshape(n_z, -1)[:, : bias_row.shape[0]].astype(f32)
    head_biases = jnp.pad(
        jnp.stack([biases[:, :mine].reshape(-1), biases[:, mine : 2 * mine].reshape(-1)]),
        ((0, 6), (0, 0)),
    )
    inner_biases = biases[:, 2 * mine :]
    inner_biases = jnp.concatenate(
        [
            lax.dynamic_slice_in_dim(inner_biases, lax.rem(z + n_z - s, n_z), 1, 0)
            for s in range(n_z)
        ],
        axis=0,
    )
    inner_biases = inner_biases.reshape(n_z, plane.n_group, feed_rows).transpose(1, 0, 2)
    inner_biases = plane.turned(inner_biases).reshape(n_places, 2, 1, n_z * feed_rows)
    inner_biases = inner_biases.transpose(1, 0, 2, 3).reshape(plane.n_group, 1, -1)
    vectors = jnp.stack(
        [output_bias, first_gain, first_shift, outer_bias, second_gain, second_shift]
        + [jnp.zeros_like(output_bias)] * 2
    ).astype(f32)

    place_z = z.reshape(1)
    info = jnp.stack([z, place, core])
    (
        hidden, slope, my_output, normed_low, first_normed, first_scale, grad_second, grad_outer,
        second_sums,
    ) = feed_forward(
        info, lengths, mixed, tokens, cotangent, vectors, inner_biases, own_units, keep + send
    )
    output_early, output_late = (
        lax.all_gather(half, "tensor") for half in jnp.split(my_output, 2, axis=0)
    )

    shared_args = (info, grad_outer, normed_low, hidden, slope, own_units)
    sent, bias_sent, grad_normed = feed_back(0, 4, *shared_args, grad_second, send)
    other = plane.swap(sent, 1)
    grad_normed, head_biases, tokens = together(grad_normed, head_biases, tokens)
    projected = project(place_z, tokens, attention_weights, head_biases, mixed.shape[1])
    projected, other = together(projected, other)
    (
        inner_stay, outer_stay, inner_go, outer_go, bias_kept, grad_first, grad_attended, first_sums
    ) = feed_back(
        0, 4, *shared_args, grad_normed, keep, other,
        (first_normed, first_scale, vectors),
    )
    grad_first, output_early = together(grad_first, output_early)
    inner_came, outer_came = plane.swap(inner_go, 4), plane.swap(outer_go, 2)
    bias_grads = jnp.stack(
        [bias_kept[:, 0], bias_sent[:, 0]], axis=1
    )
    inner_bias_grad = plane.turned(bias_grads.reshape(plane.n_group, n_z, feed_rows))
    inner_bias_grad = inner_bias_grad.transpose(1, 0, 2)
    inner_bias_grad = jnp.concatenate(
        [
            sum(
                jnp.where(lax.rem(z - t + n_z, n_z) == s, inner_bias_grad[s : s + 1], 0.0)
                for s in range(n_z)
            )
            for t in range(n_z)
        ],
        axis=0,
    ).reshape(n_z, units)

    grads, my_tokens_grad, back_sums = attend_back(
        place_z, lengths, grad_attended, grad_first, attention_weights, *projected, key_mask_rows
    )
    grads, inner_came, outer_came = together(grads, inner_came, outer_came)
    inner_on, outer_on = (
        plane.swap(add(inner_stay[1], inner_came[1]), 2),
        plane.swap(add(outer_stay[1], outer_came[1]), 4),
    )
    grad_early, grad_late = (
        lax.all_gather(half, "tensor") for half in jnp.split(my_tokens_grad, 2, axis=0)
    )

    def weight_grads(side, other=None, small=None):
        info = jnp.stack([2 * side, 2 * side + 1, z, place])
        return attention_grads(
            n_places, info, grads, mixed, tokens, grad_attended, other, small
        )

    (sent,) = weight_grads(1 - core)
    sent, back_sums, first_sums, second_sums, inner_bias_grad, output_late = together(
        sent, back_sums, first_sums, second_sums, inner_bias_grad, output_late
    )
    other = plane.swap(sent, 1)

    small = jnp.concatenate(
        [first_sums[:3], second_sums[:3], inner_bias_grad, jnp.sum(back_sums, axis=0)[:2]], axis=0
    )
    small = jnp.pad(small, ((0, -small.shape[0] % 16), (0, 0))).astype(bf16)
    small_rows = small.shape[0]

    small = add(small, plane.swap(small, 1))
    kept = list(weight_grads(core, other, small))
    arrived = plane.to_places(kept)
    output = jnp.concatenate([output_early, output_late], axis=1).reshape(all_rows, width)
    kept[0], inner_on, outer_on, grad_early, output = together(
        kept[0], inner_on, outer_on, grad_early, output
    )
    feed_parts = [
        jnp.concatenate(
            [
                add(inner_stay[0, s], inner_came[0, s], inner_on[s]),
                add(outer_stay[0, s], outer_came[0, s], outer_on[s]),
            ],
            axis=1,
        )
        for s in range(n_z)
    ]
    feed_line = [plane.shift(feed_parts[s], -s) for s in others]
    arrived, feed_line = together(arrived, feed_line)
    small = add(small, *[a[-small_rows:] for a in arrived])
    count = 2 * mine // n_places
    attention_parts = [
        add(*[a[s * count : (s + 1) * count] for a in [kept[0]] + arrived]) for s in range(n_z)
    ]
    attention_line = [
        plane.shift(jnp.concatenate([attention_parts[s], small], axis=0), s) for s in others
    ]
    feed_total = plane.over_groups(add(feed_parts[0], *feed_line))
    feed_arrived = plane.to_places([feed_total] * n_places)
    attention_line, feed_arrived, grad_late = together(attention_line, feed_arrived, grad_late)
    tokens_grad = jnp.concatenate([grad_early, grad_late], axis=1).reshape(all_rows, width)
    attention_total = plane.over_groups(
        add(attention_parts[0], *[a[:count] for a in attention_line])
    )
    small = plane.over_groups(add(small, *[a[count:] for a in attention_line])).astype(f32)
    arrived = plane.to_places([attention_total] * n_places)
    feed_half = plane.from_places(feed_total, feed_arrived)
    feed_other = plane.swap(feed_half, 1)
    inner_grad, outer_grad = finish_feed(core.reshape(1), feed_half, feed_other)
    inner_bias_sum = lax.dynamic_slice_in_dim(small, 6 + z, 1, 0)[0]
    head_sums = lax.dynamic_slice_in_dim(small[6 + n_z : 8 + n_z], z * mine, mine, 1)
    arrived, inner_grad, outer_grad, small, inner_bias_sum, head_sums, tokens_grad = together(
        arrived, inner_grad, outer_grad, small, inner_bias_sum, head_sums, tokens_grad
    )
    attention_half = plane.from_places(attention_total, arrived)
    attention_other = plane.swap(attention_half, 1)
    grad_list = plane.by_core(attention_half, attention_other)
    grad_list = grad_list.reshape(2, n_places, 2, mine // n_places, width)
    grad_list = grad_list.transpose(0, 2, 1, 3, 4).reshape(4, mine, width)

    shared = small[:6]

    return (
        output,
        tokens_grad,
        grad_list[0].T.astype(f32),
        head_sums[0],
        grad_list[1].T.astype(f32),
        grad_list[2].T.astype(f32),
        head_sums[1],
        grad_list[3].astype(f32),
        shared[0],
        shared[1],
        shared[2],
        inner_grad,
        inner_bias_sum,
        outer_grad,
        shared[3],
        shared[4],
        shared[5],
    )


def solution(mesh):
    n_dp, n_z = mesh.shape["dp"], mesh.shape["tensor"]
    in_specs = (
        P("dp", None),
        P("dp", None),
        P("dp"),
        P(None, "tensor"),
        P("tensor"),
        P(None, "tensor"),
        P(None, "tensor"),
        P("tensor"),
        P("tensor", None),
        P(),
        P(),
        P(),
        P(None, "tensor"),
        P("tensor"),
        P("tensor", None),
        P(),
        P(),
        P(),
        P("dp", None),
    )
    out_specs = (
        P("dp", None),
        P("dp", None),
        P(None, "tensor"),
        P("tensor"),
        P(None, "tensor"),
        P(None, "tensor"),
        P("tensor"),
        P("tensor", None),
        P(),
        P(),
        P(),
        P(None, "tensor"),
        P("tensor"),
        P("tensor", None),
        P(),
        P(),
        P(),
    )

    def program(*args):
        return on_device(n_dp, n_z, *args)

    return jax.shard_map(
        program, mesh=mesh, in_specs=in_specs, out_specs=out_specs, check_vma=False
    )
```

```python
import functools

import jax
import jax.numpy as jnp
from jax import lax
from jax.experimental import pallas as pl
from jax.experimental.pallas import tpu as pltpu
from jax.sharding import PartitionSpec as P

HEAD = 64
BUCKET = 512
ITEMS = 8


negative_fill = -1e30
epsilon = 1e-06
f32 = jnp.float32
bf16 = jnp.bfloat16
VMEM_BYTES = 56 * 1024 * 1024


def dot(left, right):
    return jnp.dot(left, right, preferred_element_type=f32)


def contract_rows(left, right):
    return lax.dot_general(left, right, (((0,), (0,)), ((), ())), preferred_element_type=f32)


def contract_cols(left, right):
    return lax.dot_general(left, right, (((1,), (1,)), ((), ())), preferred_element_type=f32)


def norm_rows(values):
    centred = values - jnp.mean(values, axis=1, keepdims=True)
    inv_scale = lax.rsqrt(jnp.mean(centred * centred, axis=1, keepdims=True) + epsilon)
    return centred * inv_scale, inv_scale


def norm_back(grad_rows, norm_gain, normed, inv_scale):
    scaled = grad_rows * norm_gain
    return inv_scale * (
        scaled
        - jnp.mean(scaled, axis=1, keepdims=True)
        - normed * jnp.mean(scaled * normed, axis=1, keepdims=True)
    )


def column_sum(matrix):
    return jnp.sum(matrix.astype(f32), axis=0, keepdims=True)


def fixed(shape):
    return pl.BlockSpec(shape, lambda *_: (0,) * len(shape))


def cost(microseconds):
    return pl.CostEstimate(
        flops=int(microseconds * 6e7),
        bytes_accessed=int(microseconds * 6e4),
        transcendentals=0,
    )


def params(axes):
    return pltpu.CompilerParams(
        dimension_semantics=("arbitrary",) * axes, vmem_limit_bytes=VMEM_BYTES
    )


def item_places(lengths_ref, row, shape, axis):
    places = lax.broadcasted_iota(jnp.int32, shape, axis)
    end = jnp.int32(0)
    items = jnp.zeros(shape, jnp.int32)
    for slot in range(ITEMS):
        end = end + lengths_ref[row, slot]
        items = items + (places >= end).astype(jnp.int32)
    return items


def as_column(row):
    return jnp.broadcast_to(row.astype(f32), (8, row.shape[1])).T[:, :1]


def mask_bias(lengths_ref, row, key_mask):
    shape = (BUCKET, BUCKET)
    diagonal = lax.broadcasted_iota(jnp.int32, shape, 0) == lax.broadcasted_iota(
        jnp.int32, shape, 1
    )
    item_row = item_places(lengths_ref, row, (1, BUCKET), 1)
    item_column = item_places(lengths_ref, row, (BUCKET, 1), 0)
    code_column = jnp.where(as_column(key_mask) == 1.0, item_column, -1)
    return jnp.where((code_column == item_row) | diagonal, 0.0, negative_fill).astype(f32)


def attend_forward_kernel(
    lengths_ref, tokens_ref, query_ref, key_ref, value_ref, biases_ref, key_mask_ref, mixed_ref,
):
    mine = query_ref.shape[0]
    rows = tokens_ref[...]
    queries = contract_cols(query_ref[...], rows) + as_column(biases_ref[0:1, :mine])
    queries = (queries.astype(bf16) * HEAD ** (-0.5)).astype(bf16)
    keys = contract_cols(rows, key_ref[...]).astype(bf16)
    values = contract_cols(value_ref[...], rows) + as_column(biases_ref[0:1, mine : 2 * mine])
    values = values.astype(bf16)
    bias = mask_bias(lengths_ref, pl.program_id(0), key_mask_ref[0])
    for head in range(mine // HEAD):
        at = slice(head * HEAD, (head + 1) * HEAD)
        scores = dot(keys[:, at], queries[at]) + bias
        exponent = jnp.exp(scores - jnp.max(scores, axis=0, keepdims=True))
        total = jnp.sum(exponent, axis=0, keepdims=True)
        mixed_ref[0, 0, at] = (dot(values[at], exponent.astype(bf16)) / total).astype(bf16)
    mixed_ref[0, 0, mine:] = biases_ref[...]


def attend_forward(n_z, lengths, tokens, query, key, value, biases, key_mask):
    blocks = lengths.shape[0]
    own = blocks // n_z
    mine, width = key.shape
    whole = (n_z, own, mine + biases.shape[0], BUCKET)
    return pl.pallas_call(
        attend_forward_kernel,
        grid=(blocks,),
        in_specs=[
            pl.BlockSpec(memory_space=pltpu.SMEM),
            pl.BlockSpec((BUCKET, width), lambda b: (b, 0)),
            fixed((mine, width)),
            fixed((mine, width)),
            fixed((mine, width)),
            fixed(biases.shape),
            pl.BlockSpec((1, 1, BUCKET), lambda b: (b, 0, 0)),
        ],
        out_specs=pl.BlockSpec((1, 1) + whole[2:], lambda b: (b // own, b % own, 0, 0)),
        out_shape=jax.ShapeDtypeStruct(whole, bf16),
        compiler_params=params(1),
        name="attend_forward",
        cost_estimate=cost(12),
    )(lengths, tokens, query, key, value, biases, key_mask)


def fetch_units(step, picks, own_ref, halves, units, sems):
    feed_rows, twice = units.shape[2:]
    cut = feed_rows // 2

    def copies(number):
        slot = number % 2
        row = pl.multiple_of(picks[number] * feed_rows, 16)
        ends = [
            (own_ref.at[pl.ds(row, feed_rows), :twice], units.at[slot, 0]),
            (halves[number][0].at[:, :, :twice], units.at[slot, 1:, :cut]),
            (halves[number][1].at[:, :, :twice], units.at[slot, 1:, cut:]),
        ]
        return [
            pltpu.make_async_copy(source, target, sems.at[slot, i])
            for i, (source, target) in enumerate(ends)
        ]

    for number in range(len(halves)):

        @pl.when(step == number)
        def _(number=number):
            if number == 0:
                for copy in copies(0):
                    copy.start()
            if number + 1 < len(halves):
                for copy in copies(number + 1):
                    copy.start()
            for copy in copies(number):
                copy.wait()

    return units.at[lax.rem(step, 2)]


def fetch_mixer(picks, own_ref, parts, mixer, sems):
    count = mixer.shape[1] // 8
    ends = [(own_ref, mixer.at[0])]
    for pick, part in zip(picks, parts):
        row = pl.multiple_of(pick * count, 16)
        ends.append((part, mixer.at[1:, pl.ds(row, count)]))
    copies = [
        pltpu.make_async_copy(source, target, sems.at[i])
        for i, (source, target) in enumerate(ends)
    ]
    for copy in copies:
        copy.start()
    for copy in copies:
        copy.wait()


def split_units(units):
    width = units.shape[2] // 2
    return units[:, :, :width].reshape(-1, width), units[:, :, width:].reshape(-1, width)


ANYWHERE = pl.BlockSpec(memory_space=pl.ANY)


def feed_forward_kernel(chunks, first, last, info_ref, *rest):
    def take(count):
        nonlocal rest
        taken, rest = rest[:count], rest[count:]
        return taken

    count = len(chunks)
    vectors_ref, bias_ref, own_ref = take(3)
    flat = take(2 * count)
    halves = list(zip(flat[::2], flat[1::2]))
    if first:
        tokens_ref, mixed_ref, mixer_own_ref, *mixer_parts = take(11)
    else:
        normed_low_ref, start_ref, _, _ = take(4)
    if last:
        lengths_ref, cotangent_ref = take(2)
    hidden_ref, slope_ref = take(2)
    if first:
        normed_low_ref, first_normed_ref, first_scale_ref = take(3)
    if last:
        output_ref, grad_second_ref, grad_outer_ref, sums_ref = take(4)
    else:
        (second_sum,) = take(1)
    units, sems = take(2)
    if first:
        mixer, mixer_sems = take(2)
    if last:
        (second_sum,) = take(1)

    step = pl.program_id(0)
    picks = [(info_ref[1] ^ number) * 2 + (info_ref[2] ^ side) for side, number in chunks]
    weights = fetch_units(step, picks, own_ref, halves, units, sems)
    output_bias, first_gain, first_shift, outer_bias, second_gain, second_shift = (
        vectors_ref[i : i + 1, :] for i in range(6)
    )

    @pl.when(step == 0)
    def _():
        if first:
            all_picks = [
                (info_ref[1] ^ number) * 2 + (info_ref[2] ^ side)
                for side in range(2)
                for number in range(4)
            ]
            fetch_mixer(all_picks, mixer_own_ref, mixer_parts, mixer, mixer_sems)
            n_z, own, mine, _ = mixed_ref.shape
            attended = output_bias + jnp.concatenate(
                [
                    sum(
                        dot(mixer[s, :, :mine], mixed_ref[lax.rem(info_ref[0] + n_z - s, n_z), b])
                        for s in range(n_z)
                    ).T
                    for b in range(own)
                ],
                axis=0,
            )
            normed, inv_scale = norm_rows(tokens_ref[...].astype(f32) + attended)
            whole = normed * first_gain + first_shift
            first_normed_ref[...] = normed
            first_scale_ref[...] = inv_scale
            normed_low_ref[...] = whole.astype(bf16)
            second_sum[...] = whole + outer_bias
        else:
            second_sum[...] = start_ref[...]

    inner, outer = split_units(weights)
    inner_pre = contract_cols(normed_low_ref[...], inner) + bias_ref[0]
    normal_cdf = 0.5 + 0.5 * lax.erf(inner_pre * 0.7071067811865476)
    bell = jnp.exp(-0.5 * inner_pre * inner_pre)
    hidden = (inner_pre * normal_cdf).astype(bf16)
    hidden_ref[...] = hidden.T
    slope_ref[...] = (normal_cdf + inner_pre * bell * 0.3989422804014327).astype(bf16)
    second_sum[...] += dot(hidden, outer)

    if last:

        @pl.when(step == pl.num_programs(0) - 1)
        def _():
            normed, inv_scale = norm_rows(second_sum[...])
            blocks = normed.shape[0] // BUCKET
            live = jnp.concatenate(
                [
                    (item_places(lengths_ref, info_ref[0] * blocks + b, (BUCKET, 1), 0) < ITEMS)
                    for b in range(blocks)
                ],
                axis=0,
            ).astype(f32)
            output_ref[...] = ((normed * second_gain + second_shift) * live).astype(bf16)
            grad_final = cotangent_ref[...].astype(f32) * live
            grad_second = norm_back(grad_final, second_gain, normed, inv_scale)
            grad_outer = grad_second.astype(bf16)
            grad_second_ref[...] = grad_second
            grad_outer_ref[...] = grad_outer
            sums_ref[0:1, :] = column_sum(grad_outer)
            sums_ref[1:2, :] = column_sum(grad_final * normed)
            sums_ref[2:3, :] = column_sum(grad_final)


def feed_forward(chunks, info, vectors, biases, own, halves, first=None, going=None, last=None):
    width = vectors.shape[1]
    n_z = halves[0].shape[0] + 1
    feed_rows, twice = own.shape[0] // 8, 2 * width
    rows = first[1].shape[1] * BUCKET if first else going[0].shape[0]
    chunk = n_z * feed_rows
    whole = fixed((rows, width))
    my_rows = pl.BlockSpec((rows, width), lambda j, info: (info[0], 0))
    at = lambda j, info: info[3 + j]
    hidden_spec = pl.BlockSpec((chunk, rows), lambda j, info: (at(j, info), 0))
    slope_spec = pl.BlockSpec((rows, chunk), lambda j, info: (0, at(j, info)))
    in_specs = [
        fixed((8, width)),
        pl.BlockSpec((1, 1, chunk), lambda j, info: (at(j, info), 0, 0)),
        ANYWHERE,
    ] + [ANYWHERE] * len(halves)
    args = [vectors, biases, own] + halves
    shapes = [
        ((8 * chunk, rows), bf16, hidden_spec),
        ((rows, 8 * chunk), bf16, slope_spec),
    ]
    scratch = [
        pltpu.VMEM((2, n_z, feed_rows, twice), bf16),
        pltpu.SemaphoreType.DMA((2, 3)),
    ]
    aliases = {}
    if first:
        tokens, mixed, mixer_own, mixer_parts = first
        mine = width // n_z
        in_specs += [my_rows, fixed((n_z, mixed.shape[1], mine, BUCKET))] + [ANYWHERE] * 9
        args += [tokens, mixed, mixer_own] + mixer_parts
        shapes += [
            ((rows, width), bf16, whole),
            ((rows, width), f32, whole),
            ((rows, 1), f32, fixed((rows, 1))),
        ]
        scratch += [
            pltpu.VMEM((n_z,) + mixer_own.shape, bf16),
            pltpu.SemaphoreType.DMA((9,)),
        ]
    else:
        aliases = {1 + len(args) + 2: 0, 1 + len(args) + 3: 1}
        in_specs += [whole, whole, ANYWHERE, ANYWHERE]
        args += list(going)
    if last:
        in_specs += [pl.BlockSpec(memory_space=pltpu.SMEM), my_rows]
        args += list(last)
        shapes += [
            ((rows, width), bf16, whole),
            ((rows, width), f32, whole),
            ((rows, width), bf16, whole),
            ((8, width), f32, fixed((8, width))),
        ]
        scratch.append(pltpu.VMEM((rows, width), f32))
    else:
        shapes.append(((rows, width), f32, whole))
    info = jnp.concatenate(
        [info, jnp.array([4 * side + number for side, number in chunks], jnp.int32)]
    )
    return pl.pallas_call(
        functools.partial(feed_forward_kernel, chunks, first is not None, last is not None),
        grid_spec=pltpu.PrefetchScalarGridSpec(
            num_scalar_prefetch=1,
            grid=(len(chunks),),
            in_specs=in_specs,
            out_specs=[spec for _, _, spec in shapes],
            scratch_shapes=scratch,
        ),
        out_shape=[jax.ShapeDtypeStruct(shape, kind) for shape, kind, _ in shapes],
        input_output_aliases=aliases,
        compiler_params=params(1),
        name="feed_forward",
        cost_estimate=cost(3 * len(chunks)),
    )(info, *args)


STAY = ((0, 1), (0, 2))
GO = ((2, 3), (1, 3))


def feed_back_kernel(
    first, count, keeps, info_ref, grad_outer_ref, normed_low_ref, hidden_ref, slope_ref,
    own_ref, start_ref, *rest,
):
    halves = list(zip(rest[: 2 * count : 2], rest[1 : 2 * count : 2]))
    rest = rest[2 * count :]
    if keeps:
        other_ref, norm_refs, rest = rest[0], rest[1:4], rest[4:]
        stay_refs, go_refs, rest = rest[0:2], rest[2:4], rest[4:]
        bias_grad_ref, grad_first_ref, grad_attended_ref, sums_ref, units, sems = rest[:6]
        grad_normed_ref = rest[6]
    else:
        grad_ref, bias_grad_ref, grad_normed_ref, units, sems = rest
    step = pl.program_id(0)
    side = info_ref[2] if keeps else 1 - info_ref[2]
    picks = [(info_ref[1] ^ (first + k)) * 2 + side for k in range(count)]
    weights = fetch_units(step, picks, own_ref, halves, units, sems)

    @pl.when(step == 0)
    def _():
        grad_normed_ref[...] = start_ref[...]

    n_z, feed_rows, twice = weights.shape
    width = twice // 2
    inner, outer = split_units(weights)
    grad_outer = grad_outer_ref[...]
    grad_hidden = contract_cols(grad_outer, outer)
    grad_inner = (grad_hidden * slope_ref[...].astype(f32)).astype(bf16)
    outer_grad = dot(hidden_ref[...], grad_outer).reshape(n_z, feed_rows, width)
    inner_grad = contract_rows(grad_inner, normed_low_ref[...]).reshape(n_z, feed_rows, width)
    bias_grad_ref[0] = column_sum(grad_inner)
    grad_normed_ref[...] += dot(grad_inner, inner)

    if keeps:
        for number in range(4):

            @pl.when(step == number)
            def _(number=number):
                for track, value in enumerate((inner_grad, outer_grad)):
                    at = slice(track * width, (track + 1) * width)
                    value = (value + other_ref[0, :, :, at].astype(f32)).astype(bf16)
                    ref = stay_refs[track] if number in STAY[track] else go_refs[track]
                    ref[0] = value

        @pl.when(step == pl.num_programs(0) - 1)
        def _():
            first_normed_ref, first_scale_ref, vectors_ref = norm_refs
            grad_rows, normed = grad_normed_ref[...], first_normed_ref[...]
            grad_first = norm_back(grad_rows, vectors_ref[1:2, :], normed, first_scale_ref[...])
            grad_attended = grad_first.astype(bf16)
            grad_first_ref[...] = grad_first
            grad_attended_ref[...] = grad_attended
            sums_ref[0:1, :] = column_sum(grad_attended)
            sums_ref[1:2, :] = column_sum(grad_rows * normed)
            sums_ref[2:3, :] = column_sum(grad_rows)

    else:
        grad_ref[0, :, :, :width] = inner_grad.astype(bf16)
        grad_ref[0, :, :, width:] = outer_grad.astype(bf16)


def feed_back(
    first, count, info, grad_outer, normed_low, hidden, slope, own, start, halves,
    other=None, norm=None,
):
    rows, width = grad_outer.shape
    keeps = other is not None
    feed_rows, twice = own.shape[0] // 8, 2 * width
    n_z = halves[0].shape[0] + 1
    chunk = n_z * feed_rows
    flip = 0 if keeps else 1
    columns = pl.BlockSpec((rows, chunk), lambda i, info: (0, 4 * flip + first + i))
    whole = fixed((rows, width))
    part = (n_z, feed_rows, twice)
    track = (2, n_z, feed_rows, width)
    unit_rows = pl.BlockSpec((chunk, rows), lambda i, info: (4 * flip + first + i, 0))
    in_specs = [whole, whole, unit_rows, columns, ANYWHERE, whole] + [ANYWHERE] * (2 * count)
    args = [grad_outer, normed_low, hidden, slope, own, start] + halves
    bias_shape = (
        (count, 1, chunk),
        f32,
        pl.BlockSpec((1, 1, chunk), lambda i, info: (i, 0, 0)),
    )
    scratch = [pltpu.VMEM((2,) + part, bf16), pltpu.SemaphoreType.DMA((2, 3))]

    def one(shape, at):
        return pl.BlockSpec((1,) + shape[1:], lambda i, info: (at(i), 0, 0, 0))

    if keeps:
        early, late = (lambda i: jnp.minimum(i, 1)), (lambda i: jnp.maximum(i - 2, 0))
        in_specs.append(one((4,) + part, lambda i: i))
        in_specs += [whole, fixed((rows, 1)), fixed((8, width))]
        args += [other] + list(norm)
        slow, slower = (lambda i: i // 2), (lambda i: jnp.maximum(i - 1, 0) // 2)
        shapes = [(track, bf16, one(track, at)) for at in (early, slow, late, slower)] + [
            bias_shape,
            ((rows, width), f32, whole),
            ((rows, width), bf16, whole),
            ((8, width), f32, fixed((8, width))),
        ]
        scratch.append(pltpu.VMEM((rows, width), f32))
    else:
        shapes = [
            ((count,) + part, bf16, one((count,) + part, lambda i: i)),
            bias_shape,
            ((rows, width), f32, whole),
        ]
    return pl.pallas_call(
        functools.partial(feed_back_kernel, first, count, keeps),
        grid_spec=pltpu.PrefetchScalarGridSpec(
            num_scalar_prefetch=1,
            grid=(count,),
            in_specs=in_specs,
            out_specs=[spec for _, _, spec in shapes],
            scratch_shapes=scratch,
        ),
        out_shape=[jax.ShapeDtypeStruct(shape, kind) for shape, kind, _ in shapes],
        compiler_params=params(1),
        name="feed_back_own" if keeps else "feed_back",
        cost_estimate=cost(3 * count),
    )(info, *args)


def finish_feed_kernel(core_ref, own_ref, other_ref, inner_ref, outer_ref, inner_rows):
    places, count, twice = own_ref.shape
    width = twice // 2
    for source, side in ((own_ref, core_ref[0]), (other_ref, 1 - core_ref[0])):
        for place in range(places):
            row = pl.multiple_of((2 * place + side) * count, 16)
            inner_rows[pl.ds(row, count), :] = source[place, :, :width].astype(f32)
            outer_ref[pl.ds(row, count), :] = source[place, :, width:].astype(f32)
    inner_ref[...] = inner_rows[...].T


def finish_feed(core, own, other):
    places, count, twice = own.shape
    shape = (2 * places * count, twice // 2)
    inner_shape = (shape[1], shape[0])
    return pl.pallas_call(
        finish_feed_kernel,
        grid_spec=pltpu.PrefetchScalarGridSpec(
            num_scalar_prefetch=1,
            grid=(1,),
            in_specs=[fixed(own.shape), fixed(other.shape)],
            out_specs=[fixed(inner_shape), fixed(shape)],
            scratch_shapes=[pltpu.VMEM(shape, f32)],
        ),
        out_shape=[
            jax.ShapeDtypeStruct(inner_shape, f32),
            jax.ShapeDtypeStruct(shape, f32),
        ],
        compiler_params=params(1),
        name="finish_feed",
        cost_estimate=cost(5),
    )(core, own, other)


def project_kernel(place_ref, tokens_ref, weights_ref, biases_ref, query_ref, key_ref, value_ref):
    rows = tokens_ref[...]
    width = rows.shape[1]
    queries = contract_cols(weights_ref[:, :width], rows) + as_column(biases_ref[0:1, :])
    query_ref[...] = (queries.astype(bf16) * HEAD ** (-0.5)).astype(bf16)
    key_ref[...] = contract_cols(rows, weights_ref[:, width : 2 * width]).astype(bf16)
    values = contract_cols(rows, weights_ref[:, 2 * width :]) + biases_ref[1:2, :]
    value_ref[...] = values.astype(bf16)


def project(place, tokens, weights, biases, buckets):
    width = tokens.shape[1]
    part = width // 3
    shapes = [
        ((buckets, width, BUCKET), pl.BlockSpec((None, part, BUCKET), lambda b, j, _: (b, j, 0))),
        ((buckets * BUCKET, width), pl.BlockSpec((BUCKET, part), lambda b, j, _: (b, j))),
        ((buckets * BUCKET, width), pl.BlockSpec((BUCKET, part), lambda b, j, _: (b, j))),
    ]
    return pl.pallas_call(
        project_kernel,
        grid_spec=pltpu.PrefetchScalarGridSpec(
            num_scalar_prefetch=1,
            grid=(buckets, 3),
            in_specs=[
                pl.BlockSpec((BUCKET, width), lambda b, j, place: (place[0] * buckets + b, 0)),
                pl.BlockSpec((part, 3 * width), lambda b, j, place: (j, 0)),
                pl.BlockSpec((8, part), lambda b, j, place: (0, j)),
            ],
            out_specs=[spec for _, spec in shapes],
        ),
        out_shape=[jax.ShapeDtypeStruct(shape, bf16) for shape, _ in shapes],
        compiler_params=params(2),
        name="project",
        cost_estimate=cost(5),
    )(place, tokens, weights, biases)


def attend_back_kernel(
    place_ref, lengths_ref, grad_attended_ref, grad_first_ref, weights_ref, query_ref, key_ref,
    value_ref, key_mask_ref,
    grads_ref, tokens_grad_ref, sums_ref,
    bias, grad_mixed_t, whole, weights, sem,
):
    pair = pl.program_id(1)
    pairs, width = whole.shape[1], weights.shape[0]
    fetch = pltpu.make_async_copy(weights_ref, weights, sem)

    @pl.when(pair == 0)
    def _():
        fetch.start()
        row = place_ref[0] * pl.num_programs(0) + pl.program_id(0)
        bias[...] = mask_bias(lengths_ref, row, key_mask_ref[0])
        fetch.wait()
        grad_mixed_t[...] = contract_cols(
            weights[:, 3 * width :], grad_attended_ref[...]
        ).astype(bf16)

    queries, keys, values = query_ref[...], key_ref[...], value_ref[...]
    start = pl.multiple_of(pair * keys.shape[1], 128)
    grad_mixed = grad_mixed_t[pl.ds(start, keys.shape[1]), :]
    keys_t = keys.T
    grad_queries, grad_keys, grad_values = [], [], []
    for head in range(keys.shape[1] // HEAD):
        at = slice(head * HEAD, (head + 1) * HEAD)
        scores = dot(keys[:, at], queries[at]) + bias[...]
        exponent = jnp.exp(scores - jnp.max(scores, axis=0, keepdims=True))
        probs = exponent * (1.0 / jnp.sum(exponent, axis=0, keepdims=True))
        grad_probs = dot(values[:, at], grad_mixed[at])
        shift = jnp.sum(probs * grad_probs, axis=0, keepdims=True)
        grad_scores = (probs * (grad_probs - shift)).astype(bf16)
        grad_values.append(contract_cols(probs.astype(bf16), grad_mixed[at]))
        grad_keys.append(contract_cols(grad_scores, queries[at]))
        grad_queries.append(dot(keys_t[at], grad_scores) * HEAD ** (-0.5))
    query_t = jnp.concatenate(grad_queries, axis=0).astype(bf16)
    found = (
        query_t.T,
        jnp.concatenate(grad_keys, axis=1).astype(bf16),
        jnp.concatenate(grad_values, axis=1).astype(bf16),
    )
    for number, grad in enumerate(found):
        grads_ref[number, 0] = query_t if number == 0 else grad.T
        whole[number, pair] = grad
    sums_ref[0, 0:1, :] = column_sum(found[0])
    sums_ref[0, 1:2, :] = column_sum(found[2])

    @pl.when(pair == pl.num_programs(1) - 1)
    def _():
        total = grad_first_ref[...]
        for number in range(3):
            grad = jnp.concatenate([whole[number, i] for i in range(pairs)], axis=1)
            total += dot(grad, weights[:, number * width : (number + 1) * width])
        tokens_grad_ref[...] = total.astype(bf16)


def attend_back(place, lengths, grad_attended, grad_first, weights, queries, keys, values, key_mask):
    rows, width = grad_attended.shape
    blocks = rows // BUCKET
    pair = 2 * HEAD
    by_bucket = pl.BlockSpec((BUCKET, width), lambda b, h, place: (b, 0))
    by_pair = pl.BlockSpec((BUCKET, pair), lambda b, h, place: (b, h))
    return pl.pallas_call(
        attend_back_kernel,
        grid_spec=pltpu.PrefetchScalarGridSpec(
            num_scalar_prefetch=1,
            grid=(blocks, width // pair),
            in_specs=[
                pl.BlockSpec(memory_space=pltpu.SMEM),
                by_bucket,
                by_bucket,
                ANYWHERE,
                pl.BlockSpec((None, pair, BUCKET), lambda b, h, place: (b, h, 0)),
                by_pair,
                by_pair,
                pl.BlockSpec((1, 1, BUCKET), lambda b, h, place: (place[0] * blocks + b, 0, 0)),
            ],
            out_specs=[
                pl.BlockSpec((3, 1, pair, BUCKET), lambda b, h, place: (0, b, h, 0)),
                by_bucket,
                pl.BlockSpec((1, 8, pair), lambda b, h, place: (b, 0, h)),
            ],
            scratch_shapes=[
                pltpu.VMEM((BUCKET, BUCKET), f32),
                pltpu.VMEM((width, BUCKET), bf16),
                pltpu.VMEM((3, width // pair, BUCKET, pair), bf16),
                pltpu.VMEM(weights.shape, bf16),
                pltpu.SemaphoreType.DMA(()),
            ],
        ),
        out_shape=[
            jax.ShapeDtypeStruct((3, blocks, width, BUCKET), bf16),
            jax.ShapeDtypeStruct((rows, width), bf16),
            jax.ShapeDtypeStruct((blocks, 8, width), f32),
        ],
        compiler_params=params(2),
        name="attend_back",
        cost_estimate=cost(20),
    )(place, lengths, grad_attended, grad_first, weights, queries, keys, values, key_mask)


def attention_grads_kernel(
    n_places, adds, info_ref, grads_ref, mixed_ref, tokens_ref, grad_attended_ref, *rest
):
    if adds:
        other_ref, small_ref = rest[:2]
        out_refs, whole = rest[2:-1], rest[-1]
    else:
        (out_ref, whole) = rest
    step = pl.program_id(0)
    which = info_ref[step]
    n_z, buckets, mine, _ = mixed_ref.shape
    count = mine // n_places

    @pl.when(which < 3)
    def _():
        whole[...] = sum(
            dot(grads_ref[0, b], tokens_ref[b * BUCKET : (b + 1) * BUCKET, :])
            for b in range(buckets)
        ).astype(bf16)

    @pl.when(which == 3)
    def _():
        for t in range(n_z):
            whole[t * mine : (t + 1) * mine, :] = sum(
                dot(mixed_ref[t, b], grad_attended_ref[b * BUCKET : (b + 1) * BUCKET, :])
                for b in range(buckets)
            ).astype(bf16)

    for number in range(n_places):
        for s in range(n_z):
            start = lax.rem(info_ref[2] + s, n_z) * mine + (info_ref[3] ^ number) * count
            value = whole[pl.ds(pl.multiple_of(start, 16), count), :]
            if adds:
                value = value.astype(f32) + other_ref[number, s, 0].astype(f32)
                row = (2 * s + step) * count
                out_refs[number][pl.ds(pl.multiple_of(row, 16), count), :] = value.astype(bf16)
            else:
                out_ref[number, s, 0] = value

    if adds:
        for number in range(n_places):
            out_refs[number][2 * n_z * count :, :] = small_ref[...]


def attention_grads(n_places, info, grads, mixed, tokens, grad_attended, other=None, small=None):
    rows, width = grad_attended.shape
    n_z, buckets = mixed.shape[:2]
    mine = width // n_z
    count = mine // n_places
    parts = (n_places, n_z, 1, count, width)
    by_step = pl.BlockSpec(parts, lambda i, info: (0, 0, i, 0, 0))
    in_specs = [
        pl.BlockSpec(
            (1, buckets, width, BUCKET), lambda i, info: (jnp.minimum(info[i], 2), 0, 0, 0)
        ),
        fixed((n_z, buckets, mine, BUCKET)),
        pl.BlockSpec((rows, width), lambda i, info: (info[2], 0)),
        fixed((rows, width)),
    ]
    args = [grads, mixed, tokens, grad_attended]
    if other is None:
        shapes = [((n_places, n_z, 2, count, width), by_step)]
    else:
        in_specs += [by_step, fixed(small.shape)]
        args += [other, small]
        flat = (2 * n_z * count + small.shape[0], width)
        shapes = [(flat, fixed(flat))] * n_places
    return pl.pallas_call(
        functools.partial(attention_grads_kernel, n_places, other is not None),
        grid_spec=pltpu.PrefetchScalarGridSpec(
            num_scalar_prefetch=1,
            grid=(2,),
            in_specs=in_specs,
            out_specs=[spec for _, spec in shapes],
            scratch_shapes=[pltpu.VMEM((width, width), bf16)],
        ),
        out_shape=[jax.ShapeDtypeStruct(shape, bf16) for shape, _ in shapes],
        compiler_params=params(1),
        name="attention_grads",
        cost_estimate=cost(6),
    )(info, *args)


def together(*values):
    return lax.optimization_barrier(values)


def add(first, *others):
    total = first.astype(f32)
    for other in others:
        total = total + other.astype(f32)
    return total.astype(bf16)


class Plane:
    def __init__(self, n_dp, n_z):
        self.n_dp, self.n_z = n_dp, n_z
        self.n_group = min(n_dp, 8)
        self.n_places = self.n_group // 2
        self.dp = lax.axis_index("dp")
        self.z = lax.axis_index("tensor")
        self.index = lax.rem(self.dp, self.n_group)
        self.core = self.index & 1
        self.place = self.index >> 1

    def swap(self, array, bits):
        return lax.ppermute(array, "dp", [(i, i ^ bits) for i in range(self.n_dp)])

    def shift(self, array, by):
        n = self.n_z
        return lax.ppermute(array, "tensor", [(i, (i + by) % n) for i in range(n)])

    def gather(self, piece):
        if self.n_dp == self.n_group:
            whole = lax.all_gather(piece, ("tensor", "dp"))
            return whole.reshape((self.n_z, self.n_group) + piece.shape)
        groups = [
            list(range(i, i + self.n_group)) for i in range(0, self.n_dp, self.n_group)
        ]
        line = lax.all_gather(piece, "tensor")
        return lax.all_gather(line, "dp", axis=1, axis_index_groups=groups)

    def turned(self, array):
        bit = 1
        while bit < self.n_group:
            lead = array.reshape((-1, 2, bit) + array.shape[1:])
            array = jnp.where((self.index & bit) != 0, lead[:, ::-1], lead).reshape(array.shape)
            bit *= 2
        return array

    def to_places(self, parts):
        return [self.swap(parts[number], 2 * number) for number in range(1, self.n_places)]

    def from_places(self, own, arrived):
        found = jnp.stack([own] + arrived)
        bit = 1
        while bit < self.n_places:
            lead = found.reshape((-1, 2, bit) + own.shape)
            flipped = lead[:, ::-1]
            found = jnp.where((self.place & bit) != 0, flipped, lead).reshape(found.shape)
            bit *= 2
        return found

    def by_core(self, own, other):
        return jnp.where(
            self.core == 1, jnp.stack([other, own]), jnp.stack([own, other])
        )

    def over_groups(self, array):
        bit = self.n_group
        while bit < self.n_dp:
            array = add(array, self.swap(array, bit))
            bit *= 2
        return array


def on_device(
    n_dp,
    n_z,
    tokens,
    lengths,
    key_mask,
    query_weight,
    query_bias,
    key_weight,
    value_weight,
    value_bias,
    output_weight,
    output_bias,
    first_gain,
    first_shift,
    inner_weight,
    inner_bias,
    outer_weight,
    outer_bias,
    second_gain,
    second_shift,
    cotangent,
):
    width = tokens.shape[1]
    mine = query_weight.shape[1]
    units = inner_weight.shape[1]
    all_rows = tokens.shape[0]
    all_blocks = all_rows // BUCKET
    rows = all_rows // n_z
    plane = Plane(n_dp, n_z)
    z, core, place, index = plane.z, plane.core, plane.place, plane.index
    n_places = plane.n_places
    others = range(1, n_z)

    feed_rows = units // plane.n_group
    head_rows = mine // plane.n_group
    mixer_t = jnp.pad(output_weight.T, ((0, 0), (0, -mine % 128)))
    mixer_count = width // plane.n_group
    mixer_piece = lax.dynamic_slice_in_dim(mixer_t, index * mixer_count, mixer_count, 0)
    mixer_line = [plane.shift(mixer_piece, s) for s in others]
    piece = jnp.concatenate(
        [
            lax.dynamic_slice_in_dim(inner_weight, index * feed_rows, feed_rows, 1).T,
            lax.dynamic_slice_in_dim(outer_weight, index * feed_rows, feed_rows, 0),
        ],
        axis=1,
    )
    line = [plane.shift(piece, s) for s in others]

    query_t, key_t, value_t = query_weight.T, key_weight.T, value_weight.T
    attention_own = jnp.concatenate([query_t, key_t, value_t, output_weight], axis=1)
    attention_weights = plane.gather(
        lax.dynamic_slice_in_dim(attention_own, index * head_rows, head_rows, 0)
    ).reshape(width, 4 * width)

    key_mask_rows = key_mask.reshape(all_blocks, 1, BUCKET)
    bias_row = jnp.concatenate([query_bias, value_bias, inner_bias])
    bias_rows = jnp.pad(bias_row, (0, 16 * BUCKET - bias_row.shape[0])).reshape(16, BUCKET)
    mixed = attend_forward(
        n_z, lengths, tokens, query_t, key_t, value_t, bias_rows, key_mask_rows
    )
    _, line, mixer_line = together(mixed, line, mixer_line)
    mixed = lax.all_to_all(mixed, "tensor", 0, 0)

    mixer_keep = [jnp.stack(mixer_line)]
    mixer_keep += plane.to_places(mixer_keep * n_places)
    mixer_send = [plane.swap(part, 1) for part in mixer_keep]

    cut = feed_rows // 2
    near = [jnp.stack([part[:cut] for part in line]), jnp.stack([part[cut:] for part in line])]
    by_x, by_y = [plane.swap(half, 2) for half in near], [plane.swap(half, 4) for half in near]
    own_units = jnp.concatenate([inner_weight.T, outer_weight], axis=1)

    biases = mixed[:, 0, mine:].reshape(n_z, -1)[:, : bias_row.shape[0]].astype(f32)
    head_biases = jnp.pad(
        jnp.stack([biases[:, :mine].reshape(-1), biases[:, mine : 2 * mine].reshape(-1)]),
        ((0, 6), (0, 0)),
    )
    inner_biases = biases[:, 2 * mine :]
    inner_biases = jnp.concatenate(
        [
            lax.dynamic_slice_in_dim(inner_biases, lax.rem(z + n_z - s, n_z), 1, 0)
            for s in range(n_z)
        ],
        axis=0,
    )
    inner_biases = inner_biases.reshape(n_z, plane.n_group, feed_rows).transpose(1, 0, 2)
    inner_biases = plane.turned(inner_biases).reshape(n_places, 2, 1, n_z * feed_rows)
    inner_biases = inner_biases.transpose(1, 0, 2, 3).reshape(plane.n_group, 1, -1)
    vectors = jnp.stack(
        [output_bias, first_gain, first_shift, outer_bias, second_gain, second_shift]
        + [jnp.zeros_like(output_bias)] * 2
    ).astype(f32)

    place_z = z.reshape(1)
    info = jnp.stack([z, place, core])
    shared_args = (info, vectors, inner_biases, own_units)
    hidden, slope, normed_low, first_normed, first_scale, second_sum = feed_forward(
        ((0, 0),), *shared_args, near, first=(tokens, mixed, mixer_t, mixer_keep + mixer_send)
    )
    second_sum, by_x, by_y = together(second_sum, by_x, by_y)
    far = [plane.swap(by_x[0], 4), plane.swap(by_y[1], 2)]
    send = [plane.swap(half, 1) for half in near + by_x + by_y]
    hidden, slope, second_sum = feed_forward(
        ((0, 1), (0, 2), (1, 0), (1, 1), (1, 2)), *shared_args, by_x + by_y + send,
        going=(normed_low, second_sum, hidden, slope),
    )
    second_sum, far, attention_weights = together(second_sum, far, attention_weights)
    keep = near + by_x + by_y + far
    far_send = [plane.swap(half, 1) for half in far]
    send = send + far_send
    hidden, slope, my_output, grad_second, grad_outer, second_sums = feed_forward(
        ((0, 3), (1, 3)), *shared_args, far + far_send,
        going=(normed_low, second_sum, hidden, slope), last=(lengths, cotangent),
    )
    output = lax.all_gather(my_output, "tensor", axis=0, tiled=True)

    shared_args = (info, grad_outer, normed_low, hidden, slope, own_units)
    sent, bias_sent, grad_normed = feed_back(0, 4, *shared_args, grad_second, send)
    other = plane.swap(sent, 1)
    grad_normed, head_biases, tokens = together(grad_normed, head_biases, tokens)
    projected = project(place_z, tokens, attention_weights, head_biases, mixed.shape[1])
    projected, other = together(projected, other)
    (
        inner_stay, outer_stay, inner_go, outer_go, bias_kept, grad_first, grad_attended, first_sums
    ) = feed_back(
        0, 4, *shared_args, grad_normed, keep, other,
        (first_normed, first_scale, vectors),
    )
    inner_came, outer_came = plane.swap(inner_go, 4), plane.swap(outer_go, 2)
    bias_grads = jnp.stack(
        [bias_kept[:, 0], bias_sent[:, 0]], axis=1
    )
    inner_bias_grad = plane.turned(bias_grads.reshape(plane.n_group, n_z, feed_rows))
    inner_bias_grad = inner_bias_grad.transpose(1, 0, 2)
    inner_bias_grad = jnp.concatenate(
        [
            sum(
                jnp.where(lax.rem(z - t + n_z, n_z) == s, inner_bias_grad[s : s + 1], 0.0)
                for s in range(n_z)
            )
            for t in range(n_z)
        ],
        axis=0,
    ).reshape(n_z, units)

    grads, my_tokens_grad, back_sums = attend_back(
        place_z, lengths, grad_attended, grad_first, attention_weights, *projected, key_mask_rows
    )
    grads, inner_came, outer_came, output = together(grads, inner_came, outer_came, output)
    inner_on, outer_on = (
        plane.swap(add(inner_stay[1], inner_came[1]), 2),
        plane.swap(add(outer_stay[1], outer_came[1]), 4),
    )
    tokens_grad = lax.all_gather(my_tokens_grad, "tensor", axis=0, tiled=True)

    def weight_grads(side, other=None, small=None):
        info = jnp.stack([2 * side, 2 * side + 1, z, place])
        return attention_grads(
            n_places, info, grads, mixed, tokens, grad_attended, other, small
        )

    (sent,) = weight_grads(1 - core)
    sent, back_sums, first_sums, second_sums, inner_bias_grad = together(
        sent, back_sums, first_sums, second_sums, inner_bias_grad
    )
    other = plane.swap(sent, 1)

    small = jnp.concatenate(
        [first_sums[:3], second_sums[:3], inner_bias_grad, jnp.sum(back_sums, axis=0)[:2]], axis=0
    )
    small = jnp.pad(small, ((0, -small.shape[0] % 16), (0, 0))).astype(bf16)
    small_rows = small.shape[0]

    small = add(small, plane.swap(small, 1))
    kept = list(weight_grads(core, other, small))
    arrived = plane.to_places(kept)
    kept[0], inner_on, outer_on = together(kept[0], inner_on, outer_on)
    feed_parts = [
        jnp.concatenate(
            [
                add(inner_stay[0, s], inner_came[0, s], inner_on[s]),
                add(outer_stay[0, s], outer_came[0, s], outer_on[s]),
            ],
            axis=1,
        )
        for s in range(n_z)
    ]
    feed_line = [plane.shift(feed_parts[s], -s) for s in others]
    arrived, feed_line = together(arrived, feed_line)
    small = add(small, *[a[-small_rows:] for a in arrived])
    count = 2 * mine // n_places
    attention_parts = [
        add(*[a[s * count : (s + 1) * count] for a in [kept[0]] + arrived]) for s in range(n_z)
    ]
    attention_line = [
        plane.shift(jnp.concatenate([attention_parts[s], small], axis=0), s) for s in others
    ]
    feed_total = plane.over_groups(add(feed_parts[0], *feed_line))
    feed_arrived = plane.to_places([feed_total] * n_places)
    attention_line, feed_arrived, tokens_grad = together(
        attention_line, feed_arrived, tokens_grad
    )
    attention_total = plane.over_groups(
        add(attention_parts[0], *[a[:count] for a in attention_line])
    )
    small = plane.over_groups(add(small, *[a[count:] for a in attention_line])).astype(f32)
    arrived = plane.to_places([attention_total] * n_places)
    feed_half = plane.from_places(feed_total, feed_arrived)
    feed_other = plane.swap(feed_half, 1)
    inner_grad, outer_grad = finish_feed(core.reshape(1), feed_half, feed_other)
    inner_bias_sum = lax.dynamic_slice_in_dim(small, 6 + z, 1, 0)[0]
    head_sums = lax.dynamic_slice_in_dim(small[6 + n_z : 8 + n_z], z * mine, mine, 1)
    arrived, inner_grad, outer_grad, small, inner_bias_sum, head_sums = together(
        arrived, inner_grad, outer_grad, small, inner_bias_sum, head_sums
    )
    attention_half = plane.from_places(attention_total, arrived)
    attention_other = plane.swap(attention_half, 1)
    grad_list = plane.by_core(attention_half, attention_other)
    grad_list = grad_list.reshape(2, n_places, 2, mine // n_places, width)
    grad_list = grad_list.transpose(0, 2, 1, 3, 4).reshape(4, mine, width)

    shared = small[:6]

    return (
        output,
        tokens_grad,
        grad_list[0].T.astype(f32),
        head_sums[0],
        grad_list[1].T.astype(f32),
        grad_list[2].T.astype(f32),
        head_sums[1],
        grad_list[3].astype(f32),
        shared[0],
        shared[1],
        shared[2],
        inner_grad,
        inner_bias_sum,
        outer_grad,
        shared[3],
        shared[4],
        shared[5],
    )


def solution(mesh):
    n_dp, n_z = mesh.shape["dp"], mesh.shape["tensor"]
    in_specs = (
        P("dp", None),
        P("dp", None),
        P("dp"),
        P(None, "tensor"),
        P("tensor"),
        P(None, "tensor"),
        P(None, "tensor"),
        P("tensor"),
        P("tensor", None),
        P(),
        P(),
        P(),
        P(None, "tensor"),
        P("tensor"),
        P("tensor", None),
        P(),
        P(),
        P(),
        P("dp", None),
    )
    out_specs = (
        P("dp", None),
        P("dp", None),
        P(None, "tensor"),
        P("tensor"),
        P(None, "tensor"),
        P(None, "tensor"),
        P("tensor"),
        P("tensor", None),
        P(),
        P(),
        P(),
        P(None, "tensor"),
        P("tensor"),
        P("tensor", None),
        P(),
        P(),
        P(),
    )

    def program(*args):
        return on_device(n_dp, n_z, *args)

    return jax.shard_map(
        program, mesh=mesh, in_specs=in_specs, out_specs=out_specs, check_vma=False
    )
```

```python
import functools

import jax
import jax.numpy as jnp
from jax import lax
from jax.experimental import pallas as pl
from jax.experimental.pallas import tpu as pltpu
from jax.sharding import PartitionSpec as P

HEAD = 64
BUCKET = 512
ITEMS = 8


negative_fill = -1e30
epsilon = 1e-06
f32 = jnp.float32
bf16 = jnp.bfloat16
VMEM_BYTES = 56 * 1024 * 1024


def dot(left, right):
    return jnp.dot(left, right, preferred_element_type=f32)


def contract_rows(left, right):
    return lax.dot_general(left, right, (((0,), (0,)), ((), ())), preferred_element_type=f32)


def contract_cols(left, right):
    return lax.dot_general(left, right, (((1,), (1,)), ((), ())), preferred_element_type=f32)


def norm_rows(values):
    centred = values - jnp.mean(values, axis=1, keepdims=True)
    inv_scale = lax.rsqrt(jnp.mean(centred * centred, axis=1, keepdims=True) + epsilon)
    return centred * inv_scale, inv_scale


def norm_back(grad_rows, norm_gain, normed, inv_scale):
    scaled = grad_rows * norm_gain
    return inv_scale * (
        scaled
        - jnp.mean(scaled, axis=1, keepdims=True)
        - normed * jnp.mean(scaled * normed, axis=1, keepdims=True)
    )


def column_sum(matrix):
    return jnp.sum(matrix.astype(f32), axis=0, keepdims=True)


def fixed(shape):
    return pl.BlockSpec(shape, lambda *_: (0,) * len(shape))


def cost(microseconds):
    return pl.CostEstimate(
        flops=int(microseconds * 1e9),
        bytes_accessed=int(microseconds * 1e6),
        transcendentals=0,
    )


def params(axes):
    return pltpu.CompilerParams(
        dimension_semantics=("arbitrary",) * axes, vmem_limit_bytes=VMEM_BYTES
    )


def item_places(lengths_ref, row, shape, axis):
    places = lax.broadcasted_iota(jnp.int32, shape, axis)
    end = jnp.int32(0)
    items = jnp.zeros(shape, jnp.int32)
    for slot in range(ITEMS):
        end = end + lengths_ref[row, slot]
        items = items + (places >= end).astype(jnp.int32)
    return items


def as_column(row):
    return jnp.broadcast_to(row.astype(f32), (8, row.shape[1])).T[:, :1]


def mask_bias(lengths_ref, row, key_mask):
    shape = (BUCKET, BUCKET)
    diagonal = lax.broadcasted_iota(jnp.int32, shape, 0) == lax.broadcasted_iota(
        jnp.int32, shape, 1
    )
    item_row = item_places(lengths_ref, row, (1, BUCKET), 1)
    item_column = item_places(lengths_ref, row, (BUCKET, 1), 0)
    code_column = jnp.where(as_column(key_mask) == 1.0, item_column, -1)
    return jnp.where((code_column == item_row) | diagonal, 0.0, negative_fill).astype(f32)


def attend_forward_kernel(
    lengths_ref, tokens_ref, query_ref, key_ref, value_ref, biases_ref, key_mask_ref, mixed_ref,
):
    mine = query_ref.shape[0]
    rows = tokens_ref[...]
    queries = contract_cols(query_ref[...], rows) + as_column(biases_ref[0:1, :mine])
    queries = (queries.astype(bf16) * HEAD ** (-0.5)).astype(bf16)
    keys = contract_cols(rows, key_ref[...]).astype(bf16)
    values = contract_cols(value_ref[...], rows) + as_column(biases_ref[0:1, mine : 2 * mine])
    values = values.astype(bf16)
    bias = mask_bias(lengths_ref, pl.program_id(0), key_mask_ref[0])
    for head in range(mine // HEAD):
        at = slice(head * HEAD, (head + 1) * HEAD)
        scores = dot(keys[:, at], queries[at]) + bias
        exponent = jnp.exp(scores - jnp.max(scores, axis=0, keepdims=True))
        total = jnp.sum(exponent, axis=0, keepdims=True)
        mixed_ref[0, 0, at] = (dot(values[at], exponent.astype(bf16)) / total).astype(bf16)
    mixed_ref[0, 0, mine:] = biases_ref[...]


def attend_forward(n_z, lengths, tokens, query, key, value, biases, key_mask):
    blocks = lengths.shape[0]
    own = blocks // n_z
    mine, width = key.shape
    whole = (n_z, own, mine + biases.shape[0], BUCKET)
    return pl.pallas_call(
        attend_forward_kernel,
        grid=(blocks,),
        in_specs=[
            pl.BlockSpec(memory_space=pltpu.SMEM),
            pl.BlockSpec((BUCKET, width), lambda b: (b, 0)),
            fixed((mine, width)),
            fixed((mine, width)),
            fixed((mine, width)),
            fixed(biases.shape),
            pl.BlockSpec((1, 1, BUCKET), lambda b: (b, 0, 0)),
        ],
        out_specs=pl.BlockSpec((1, 1) + whole[2:], lambda b: (b // own, b % own, 0, 0)),
        out_shape=jax.ShapeDtypeStruct(whole, bf16),
        compiler_params=params(1),
        name="attend_forward",
        cost_estimate=cost(12),
    )(lengths, tokens, query, key, value, biases, key_mask)


def fetch_units(step, picks, own_ref, halves, units, sems):
    feed_rows, twice = units.shape[2:]
    cut = feed_rows // 2

    def copies(number):
        slot = number % 2
        row = pl.multiple_of(picks[number] * feed_rows, 16)
        ends = [
            (own_ref.at[pl.ds(row, feed_rows), :twice], units.at[slot, 0]),
            (halves[number][0].at[:, :, :twice], units.at[slot, 1:, :cut]),
            (halves[number][1].at[:, :, :twice], units.at[slot, 1:, cut:]),
        ]
        return [
            pltpu.make_async_copy(source, target, sems.at[slot, i])
            for i, (source, target) in enumerate(ends)
        ]

    for number in range(len(halves)):

        @pl.when(step == number)
        def _(number=number):
            if number == 0:
                for copy in copies(0):
                    copy.start()
            if number + 1 < len(halves):
                for copy in copies(number + 1):
                    copy.start()
            for copy in copies(number):
                copy.wait()

    return units.at[lax.rem(step, 2)]


def fetch_mixer(picks, own_ref, parts, mixer, sems):
    count = mixer.shape[1] // 8
    ends = [(own_ref, mixer.at[0])]
    for pick, part in zip(picks, parts):
        row = pl.multiple_of(pick * count, 16)
        ends.append((part, mixer.at[1:, pl.ds(row, count)]))
    copies = [
        pltpu.make_async_copy(source, target, sems.at[i])
        for i, (source, target) in enumerate(ends)
    ]
    for copy in copies:
        copy.start()
    for copy in copies:
        copy.wait()


def split_units(units):
    width = units.shape[2] // 2
    return units[:, :, :width].reshape(-1, width), units[:, :, width:].reshape(-1, width)


ANYWHERE = pl.BlockSpec(memory_space=pl.ANY)


def feed_forward_kernel(chunks, first, last, info_ref, *rest):
    def take(count):
        nonlocal rest
        taken, rest = rest[:count], rest[count:]
        return taken

    count = len(chunks)
    vectors_ref, bias_ref, own_ref = take(3)
    flat = take(2 * count)
    halves = list(zip(flat[::2], flat[1::2]))
    if first:
        tokens_ref, mixed_ref, mixer_own_ref, *mixer_parts = take(11)
    else:
        normed_low_ref, start_ref, _, _ = take(4)
    if last:
        lengths_ref, cotangent_ref = take(2)
    hidden_ref, slope_ref = take(2)
    if first:
        normed_low_ref, first_normed_ref, first_scale_ref = take(3)
    if last:
        output_ref, grad_second_ref, grad_outer_ref, sums_ref = take(4)
    else:
        (second_sum,) = take(1)
    units, sems = take(2)
    if first:
        mixer, mixer_sems = take(2)
    if last:
        (second_sum,) = take(1)

    step = pl.program_id(0)
    picks = [(info_ref[1] ^ number) * 2 + (info_ref[2] ^ side) for side, number in chunks]
    weights = fetch_units(step, picks, own_ref, halves, units, sems)
    output_bias, first_gain, first_shift, outer_bias, second_gain, second_shift = (
        vectors_ref[i : i + 1, :] for i in range(6)
    )

    @pl.when(step == 0)
    def _():
        if first:
            all_picks = [
                (info_ref[1] ^ number) * 2 + (info_ref[2] ^ side)
                for side in range(2)
                for number in range(4)
            ]
            fetch_mixer(all_picks, mixer_own_ref, mixer_parts, mixer, mixer_sems)
            n_z, own, mine, _ = mixed_ref.shape
            attended = output_bias + jnp.concatenate(
                [
                    sum(
                        dot(mixer[s, :, :mine], mixed_ref[lax.rem(info_ref[0] + n_z - s, n_z), b])
                        for s in range(n_z)
                    ).T
                    for b in range(own)
                ],
                axis=0,
            )
            normed, inv_scale = norm_rows(tokens_ref[...].astype(f32) + attended)
            whole = normed * first_gain + first_shift
            first_normed_ref[...] = normed
            first_scale_ref[...] = inv_scale
            normed_low_ref[...] = whole.astype(bf16)
            second_sum[...] = whole + outer_bias
        else:
            second_sum[...] = start_ref[...]

    inner, outer = split_units(weights)
    inner_pre = contract_cols(normed_low_ref[...], inner) + bias_ref[0]
    normal_cdf = 0.5 + 0.5 * lax.erf(inner_pre * 0.7071067811865476)
    bell = jnp.exp(-0.5 * inner_pre * inner_pre)
    hidden = (inner_pre * normal_cdf).astype(bf16)
    hidden_ref[...] = hidden.T
    slope_ref[...] = (normal_cdf + inner_pre * bell * 0.3989422804014327).astype(bf16)
    second_sum[...] += dot(hidden, outer)

    if last:

        @pl.when(step == pl.num_programs(0) - 1)
        def _():
            normed, inv_scale = norm_rows(second_sum[...])
            blocks = normed.shape[0] // BUCKET
            live = jnp.concatenate(
                [
                    (item_places(lengths_ref, info_ref[0] * blocks + b, (BUCKET, 1), 0) < ITEMS)
                    for b in range(blocks)
                ],
                axis=0,
            ).astype(f32)
            output_ref[...] = ((normed * second_gain + second_shift) * live).astype(bf16)
            grad_final = cotangent_ref[...].astype(f32) * live
            grad_second = norm_back(grad_final, second_gain, normed, inv_scale)
            grad_outer = grad_second.astype(bf16)
            grad_second_ref[...] = grad_second
            grad_outer_ref[...] = grad_outer
            sums_ref[0:1, :] = column_sum(grad_outer)
            sums_ref[1:2, :] = column_sum(grad_final * normed)
            sums_ref[2:3, :] = column_sum(grad_final)


def feed_forward(chunks, info, vectors, biases, own, halves, first=None, going=None, last=None):
    width = vectors.shape[1]
    n_z = halves[0].shape[0] + 1
    feed_rows, twice = own.shape[0] // 8, 2 * width
    rows = first[1].shape[1] * BUCKET if first else going[0].shape[0]
    chunk = n_z * feed_rows
    whole = fixed((rows, width))
    my_rows = pl.BlockSpec((rows, width), lambda j, info: (info[0], 0))
    at = lambda j, info: info[3 + j]
    hidden_spec = pl.BlockSpec((chunk, rows), lambda j, info: (at(j, info), 0))
    slope_spec = pl.BlockSpec((rows, chunk), lambda j, info: (0, at(j, info)))
    in_specs = [
        fixed((8, width)),
        pl.BlockSpec((1, 1, chunk), lambda j, info: (at(j, info), 0, 0)),
        ANYWHERE,
    ] + [ANYWHERE] * len(halves)
    args = [vectors, biases, own] + halves
    shapes = [
        ((8 * chunk, rows), bf16, hidden_spec),
        ((rows, 8 * chunk), bf16, slope_spec),
    ]
    scratch = [
        pltpu.VMEM((2, n_z, feed_rows, twice), bf16),
        pltpu.SemaphoreType.DMA((2, 3)),
    ]
    aliases = {}
    if first:
        tokens, mixed, mixer_own, mixer_parts = first
        mine = width // n_z
        in_specs += [my_rows, fixed((n_z, mixed.shape[1], mine, BUCKET))] + [ANYWHERE] * 9
        args += [tokens, mixed, mixer_own] + mixer_parts
        shapes += [
            ((rows, width), bf16, whole),
            ((rows, width), f32, whole),
            ((rows, 1), f32, fixed((rows, 1))),
        ]
        scratch += [
            pltpu.VMEM((n_z,) + mixer_own.shape, bf16),
            pltpu.SemaphoreType.DMA((9,)),
        ]
    else:
        aliases = {1 + len(args) + 2: 0, 1 + len(args) + 3: 1}
        in_specs += [whole, whole, ANYWHERE, ANYWHERE]
        args += list(going)
    if last:
        in_specs += [pl.BlockSpec(memory_space=pltpu.SMEM), my_rows]
        args += list(last)
        shapes += [
            ((rows, width), bf16, whole),
            ((rows, width), f32, whole),
            ((rows, width), bf16, whole),
            ((8, width), f32, fixed((8, width))),
        ]
        scratch.append(pltpu.VMEM((rows, width), f32))
    else:
        shapes.append(((rows, width), f32, whole))
    info = jnp.concatenate(
        [info, jnp.array([4 * side + number for side, number in chunks], jnp.int32)]
    )
    return pl.pallas_call(
        functools.partial(feed_forward_kernel, chunks, first is not None, last is not None),
        grid_spec=pltpu.PrefetchScalarGridSpec(
            num_scalar_prefetch=1,
            grid=(len(chunks),),
            in_specs=in_specs,
            out_specs=[spec for _, _, spec in shapes],
            scratch_shapes=scratch,
        ),
        out_shape=[jax.ShapeDtypeStruct(shape, kind) for shape, kind, _ in shapes],
        input_output_aliases=aliases,
        compiler_params=params(1),
        name="feed_forward",
        cost_estimate=cost(3 * len(chunks)),
    )(info, *args)


STAY = ((0, 1), (0, 2))
GO = ((2, 3), (1, 3))


def feed_back_kernel(
    first, count, keeps, info_ref, grad_outer_ref, normed_low_ref, hidden_ref, slope_ref,
    own_ref, start_ref, *rest,
):
    halves = list(zip(rest[: 2 * count : 2], rest[1 : 2 * count : 2]))
    rest = rest[2 * count :]
    if keeps:
        other_ref, norm_refs, rest = rest[0], rest[1:4], rest[4:]
        stay_refs, go_refs, rest = rest[0:2], rest[2:4], rest[4:]
        bias_grad_ref, grad_first_ref, grad_attended_ref, sums_ref, units, sems = rest[:6]
        grad_normed_ref = rest[6]
    else:
        grad_ref, bias_grad_ref, grad_normed_ref, units, sems = rest
    step = pl.program_id(0)
    side = info_ref[2] if keeps else 1 - info_ref[2]
    picks = [(info_ref[1] ^ (first + k)) * 2 + side for k in range(count)]
    weights = fetch_units(step, picks, own_ref, halves, units, sems)

    @pl.when(step == 0)
    def _():
        grad_normed_ref[...] = start_ref[...]

    n_z, feed_rows, twice = weights.shape
    width = twice // 2
    inner, outer = split_units(weights)
    grad_outer = grad_outer_ref[...]
    grad_hidden = contract_cols(grad_outer, outer)
    grad_inner = (grad_hidden * slope_ref[...].astype(f32)).astype(bf16)
    outer_grad = dot(hidden_ref[...], grad_outer).reshape(n_z, feed_rows, width)
    inner_grad = contract_rows(grad_inner, normed_low_ref[...]).reshape(n_z, feed_rows, width)
    bias_grad_ref[0] = column_sum(grad_inner)
    grad_normed_ref[...] += dot(grad_inner, inner)

    if keeps:
        for number in range(4):

            @pl.when(step == number)
            def _(number=number):
                for track, value in enumerate((inner_grad, outer_grad)):
                    at = slice(track * width, (track + 1) * width)
                    value = (value + other_ref[0, :, :, at].astype(f32)).astype(bf16)
                    ref = stay_refs[track] if number in STAY[track] else go_refs[track]
                    ref[0] = value

        @pl.when(step == pl.num_programs(0) - 1)
        def _():
            first_normed_ref, first_scale_ref, vectors_ref = norm_refs
            grad_rows, normed = grad_normed_ref[...], first_normed_ref[...]
            grad_first = norm_back(grad_rows, vectors_ref[1:2, :], normed, first_scale_ref[...])
            grad_attended = grad_first.astype(bf16)
            grad_first_ref[...] = grad_first
            grad_attended_ref[...] = grad_attended
            sums_ref[0:1, :] = column_sum(grad_attended)
            sums_ref[1:2, :] = column_sum(grad_rows * normed)
            sums_ref[2:3, :] = column_sum(grad_rows)

    else:
        grad_ref[0, :, :, :width] = inner_grad.astype(bf16)
        grad_ref[0, :, :, width:] = outer_grad.astype(bf16)


def feed_back(
    first, count, info, grad_outer, normed_low, hidden, slope, own, start, halves,
    other=None, norm=None,
):
    rows, width = grad_outer.shape
    keeps = other is not None
    feed_rows, twice = own.shape[0] // 8, 2 * width
    n_z = halves[0].shape[0] + 1
    chunk = n_z * feed_rows
    flip = 0 if keeps else 1
    columns = pl.BlockSpec((rows, chunk), lambda i, info: (0, 4 * flip + first + i))
    whole = fixed((rows, width))
    part = (n_z, feed_rows, twice)
    track = (2, n_z, feed_rows, width)
    unit_rows = pl.BlockSpec((chunk, rows), lambda i, info: (4 * flip + first + i, 0))
    in_specs = [whole, whole, unit_rows, columns, ANYWHERE, whole] + [ANYWHERE] * (2 * count)
    args = [grad_outer, normed_low, hidden, slope, own, start] + halves
    bias_shape = (
        (count, 1, chunk),
        f32,
        pl.BlockSpec((1, 1, chunk), lambda i, info: (i, 0, 0)),
    )
    scratch = [pltpu.VMEM((2,) + part, bf16), pltpu.SemaphoreType.DMA((2, 3))]

    def one(shape, at):
        return pl.BlockSpec((1,) + shape[1:], lambda i, info: (at(i), 0, 0, 0))

    if keeps:
        early, late = (lambda i: jnp.minimum(i, 1)), (lambda i: jnp.maximum(i - 2, 0))
        in_specs.append(one((4,) + part, lambda i: i))
        in_specs += [whole, fixed((rows, 1)), fixed((8, width))]
        args += [other] + list(norm)
        slow, slower = (lambda i: i // 2), (lambda i: jnp.maximum(i - 1, 0) // 2)
        shapes = [(track, bf16, one(track, at)) for at in (early, slow, late, slower)] + [
            bias_shape,
            ((rows, width), f32, whole),
            ((rows, width), bf16, whole),
            ((8, width), f32, fixed((8, width))),
        ]
        scratch.append(pltpu.VMEM((rows, width), f32))
    else:
        shapes = [
            ((count,) + part, bf16, one((count,) + part, lambda i: i)),
            bias_shape,
            ((rows, width), f32, whole),
        ]
    return pl.pallas_call(
        functools.partial(feed_back_kernel, first, count, keeps),
        grid_spec=pltpu.PrefetchScalarGridSpec(
            num_scalar_prefetch=1,
            grid=(count,),
            in_specs=in_specs,
            out_specs=[spec for _, _, spec in shapes],
            scratch_shapes=scratch,
        ),
        out_shape=[jax.ShapeDtypeStruct(shape, kind) for shape, kind, _ in shapes],
        compiler_params=params(1),
        name="feed_back_own" if keeps else "feed_back",
        cost_estimate=cost(3 * count),
    )(info, *args)


def finish_feed_kernel(core_ref, own_ref, other_ref, inner_ref, outer_ref, inner_rows):
    places, count, twice = own_ref.shape
    width = twice // 2
    for source, side in ((own_ref, core_ref[0]), (other_ref, 1 - core_ref[0])):
        for place in range(places):
            row = pl.multiple_of((2 * place + side) * count, 16)
            inner_rows[pl.ds(row, count), :] = source[place, :, :width].astype(f32)
            outer_ref[pl.ds(row, count), :] = source[place, :, width:].astype(f32)
    inner_ref[...] = inner_rows[...].T


def finish_feed(core, own, other):
    places, count, twice = own.shape
    shape = (2 * places * count, twice // 2)
    inner_shape = (shape[1], shape[0])
    return pl.pallas_call(
        finish_feed_kernel,
        grid_spec=pltpu.PrefetchScalarGridSpec(
            num_scalar_prefetch=1,
            grid=(1,),
            in_specs=[fixed(own.shape), fixed(other.shape)],
            out_specs=[fixed(inner_shape), fixed(shape)],
            scratch_shapes=[pltpu.VMEM(shape, f32)],
        ),
        out_shape=[
            jax.ShapeDtypeStruct(inner_shape, f32),
            jax.ShapeDtypeStruct(shape, f32),
        ],
        compiler_params=params(1),
        name="finish_feed",
        cost_estimate=cost(5),
    )(core, own, other)


def project_kernel(place_ref, tokens_ref, weights_ref, biases_ref, query_ref, key_ref, value_ref):
    rows = tokens_ref[...]
    width = rows.shape[1]
    queries = contract_cols(weights_ref[:, :width], rows) + as_column(biases_ref[0:1, :])
    query_ref[...] = (queries.astype(bf16) * HEAD ** (-0.5)).astype(bf16)
    key_ref[...] = contract_cols(rows, weights_ref[:, width : 2 * width]).astype(bf16)
    values = contract_cols(rows, weights_ref[:, 2 * width :]) + biases_ref[1:2, :]
    value_ref[...] = values.astype(bf16)


def project(place, tokens, weights, biases, buckets):
    width = tokens.shape[1]
    part = width // 3
    shapes = [
        ((buckets, width, BUCKET), pl.BlockSpec((None, part, BUCKET), lambda b, j, _: (b, j, 0))),
        ((buckets * BUCKET, width), pl.BlockSpec((BUCKET, part), lambda b, j, _: (b, j))),
        ((buckets * BUCKET, width), pl.BlockSpec((BUCKET, part), lambda b, j, _: (b, j))),
    ]
    return pl.pallas_call(
        project_kernel,
        grid_spec=pltpu.PrefetchScalarGridSpec(
            num_scalar_prefetch=1,
            grid=(buckets, 3),
            in_specs=[
                pl.BlockSpec((BUCKET, width), lambda b, j, place: (place[0] * buckets + b, 0)),
                pl.BlockSpec((part, 3 * width), lambda b, j, place: (j, 0)),
                pl.BlockSpec((8, part), lambda b, j, place: (0, j)),
            ],
            out_specs=[spec for _, spec in shapes],
        ),
        out_shape=[jax.ShapeDtypeStruct(shape, bf16) for shape, _ in shapes],
        compiler_params=params(2),
        name="project",
        cost_estimate=cost(5),
    )(place, tokens, weights, biases)


def attend_back_kernel(
    place_ref, lengths_ref, grad_attended_ref, grad_first_ref, weights_ref, query_ref, key_ref,
    value_ref, key_mask_ref,
    grads_ref, tokens_grad_ref, sums_ref,
    bias, grad_mixed_t, whole, weights, sem,
):
    pair = pl.program_id(1)
    pairs, width = whole.shape[1], weights.shape[0]
    fetch = pltpu.make_async_copy(weights_ref, weights, sem)

    @pl.when(pair == 0)
    def _():
        fetch.start()
        row = place_ref[0] * pl.num_programs(0) + pl.program_id(0)
        bias[...] = mask_bias(lengths_ref, row, key_mask_ref[0])
        fetch.wait()
        grad_mixed_t[...] = contract_cols(
            weights[:, 3 * width :], grad_attended_ref[...]
        ).astype(bf16)

    queries, keys, values = query_ref[...], key_ref[...], value_ref[...]
    start = pl.multiple_of(pair * keys.shape[1], 128)
    grad_mixed = grad_mixed_t[pl.ds(start, keys.shape[1]), :]
    keys_t = keys.T
    grad_queries, grad_keys, grad_values = [], [], []
    for head in range(keys.shape[1] // HEAD):
        at = slice(head * HEAD, (head + 1) * HEAD)
        scores = dot(keys[:, at], queries[at]) + bias[...]
        exponent = jnp.exp(scores - jnp.max(scores, axis=0, keepdims=True))
        probs = exponent * (1.0 / jnp.sum(exponent, axis=0, keepdims=True))
        grad_probs = dot(values[:, at], grad_mixed[at])
        shift = jnp.sum(probs * grad_probs, axis=0, keepdims=True)
        grad_scores = (probs * (grad_probs - shift)).astype(bf16)
        grad_values.append(contract_cols(probs.astype(bf16), grad_mixed[at]))
        grad_keys.append(contract_cols(grad_scores, queries[at]))
        grad_queries.append(dot(keys_t[at], grad_scores) * HEAD ** (-0.5))
    query_t = jnp.concatenate(grad_queries, axis=0).astype(bf16)
    found = (
        query_t.T,
        jnp.concatenate(grad_keys, axis=1).astype(bf16),
        jnp.concatenate(grad_values, axis=1).astype(bf16),
    )
    for number, grad in enumerate(found):
        grads_ref[number, 0] = query_t if number == 0 else grad.T
        whole[number, pair] = grad
    sums_ref[0, 0:1, :] = column_sum(found[0])
    sums_ref[0, 1:2, :] = column_sum(found[2])

    @pl.when(pair == pl.num_programs(1) - 1)
    def _():
        total = grad_first_ref[...]
        for number in range(3):
            grad = jnp.concatenate([whole[number, i] for i in range(pairs)], axis=1)
            total += dot(grad, weights[:, number * width : (number + 1) * width])
        tokens_grad_ref[...] = total.astype(bf16)


def attend_back(place, lengths, grad_attended, grad_first, weights, queries, keys, values, key_mask):
    rows, width = grad_attended.shape
    blocks = rows // BUCKET
    pair = 2 * HEAD
    by_bucket = pl.BlockSpec((BUCKET, width), lambda b, h, place: (b, 0))
    by_pair = pl.BlockSpec((BUCKET, pair), lambda b, h, place: (b, h))
    return pl.pallas_call(
        attend_back_kernel,
        grid_spec=pltpu.PrefetchScalarGridSpec(
            num_scalar_prefetch=1,
            grid=(blocks, width // pair),
            in_specs=[
                pl.BlockSpec(memory_space=pltpu.SMEM),
                by_bucket,
                by_bucket,
                ANYWHERE,
                pl.BlockSpec((None, pair, BUCKET), lambda b, h, place: (b, h, 0)),
                by_pair,
                by_pair,
                pl.BlockSpec((1, 1, BUCKET), lambda b, h, place: (place[0] * blocks + b, 0, 0)),
            ],
            out_specs=[
                pl.BlockSpec((3, 1, pair, BUCKET), lambda b, h, place: (0, b, h, 0)),
                by_bucket,
                pl.BlockSpec((1, 8, pair), lambda b, h, place: (b, 0, h)),
            ],
            scratch_shapes=[
                pltpu.VMEM((BUCKET, BUCKET), f32),
                pltpu.VMEM((width, BUCKET), bf16),
                pltpu.VMEM((3, width // pair, BUCKET, pair), bf16),
                pltpu.VMEM(weights.shape, bf16),
                pltpu.SemaphoreType.DMA(()),
            ],
        ),
        out_shape=[
            jax.ShapeDtypeStruct((3, blocks, width, BUCKET), bf16),
            jax.ShapeDtypeStruct((rows, width), bf16),
            jax.ShapeDtypeStruct((blocks, 8, width), f32),
        ],
        compiler_params=params(2),
        name="attend_back",
        cost_estimate=cost(20),
    )(place, lengths, grad_attended, grad_first, weights, queries, keys, values, key_mask)


def attention_grads_kernel(
    n_places, adds, info_ref, grads_ref, mixed_ref, tokens_ref, grad_attended_ref, *rest
):
    if adds:
        other_ref, small_ref = rest[:2]
        out_refs, whole = rest[2:-1], rest[-1]
    else:
        (out_ref, whole) = rest
    step = pl.program_id(0)
    which = info_ref[step]
    n_z, buckets, mine, _ = mixed_ref.shape
    count = mine // n_places

    @pl.when(which < 3)
    def _():
        whole[...] = sum(
            dot(grads_ref[0, b], tokens_ref[b * BUCKET : (b + 1) * BUCKET, :])
            for b in range(buckets)
        ).astype(bf16)

    @pl.when(which == 3)
    def _():
        for t in range(n_z):
            whole[t * mine : (t + 1) * mine, :] = sum(
                dot(mixed_ref[t, b], grad_attended_ref[b * BUCKET : (b + 1) * BUCKET, :])
                for b in range(buckets)
            ).astype(bf16)

    for number in range(n_places):
        for s in range(n_z):
            start = lax.rem(info_ref[2] + s, n_z) * mine + (info_ref[3] ^ number) * count
            value = whole[pl.ds(pl.multiple_of(start, 16), count), :]
            if adds:
                value = value.astype(f32) + other_ref[number, s, 0].astype(f32)
                row = (2 * s + step) * count
                out_refs[number][pl.ds(pl.multiple_of(row, 16), count), :] = value.astype(bf16)
            else:
                out_ref[number, s, 0] = value

    if adds:
        for number in range(n_places):
            out_refs[number][2 * n_z * count :, :] = small_ref[...]


def attention_grads(n_places, info, grads, mixed, tokens, grad_attended, other=None, small=None):
    rows, width = grad_attended.shape
    n_z, buckets = mixed.shape[:2]
    mine = width // n_z
    count = mine // n_places
    parts = (n_places, n_z, 1, count, width)
    by_step = pl.BlockSpec(parts, lambda i, info: (0, 0, i, 0, 0))
    in_specs = [
        pl.BlockSpec(
            (1, buckets, width, BUCKET), lambda i, info: (jnp.minimum(info[i], 2), 0, 0, 0)
        ),
        fixed((n_z, buckets, mine, BUCKET)),
        pl.BlockSpec((rows, width), lambda i, info: (info[2], 0)),
        fixed((rows, width)),
    ]
    args = [grads, mixed, tokens, grad_attended]
    if other is None:
        shapes = [((n_places, n_z, 2, count, width), by_step)]
    else:
        in_specs += [by_step, fixed(small.shape)]
        args += [other, small]
        flat = (2 * n_z * count + small.shape[0], width)
        shapes = [(flat, fixed(flat))] * n_places
    return pl.pallas_call(
        functools.partial(attention_grads_kernel, n_places, other is not None),
        grid_spec=pltpu.PrefetchScalarGridSpec(
            num_scalar_prefetch=1,
            grid=(2,),
            in_specs=in_specs,
            out_specs=[spec for _, spec in shapes],
            scratch_shapes=[pltpu.VMEM((width, width), bf16)],
        ),
        out_shape=[jax.ShapeDtypeStruct(shape, bf16) for shape, _ in shapes],
        compiler_params=params(1),
        name="attention_grads",
        cost_estimate=cost(1.5),
    )(info, *args)


def together(*values):
    return lax.optimization_barrier(values)


def add(first, *others):
    total = first.astype(f32)
    for other in others:
        total = total + other.astype(f32)
    return total.astype(bf16)


class Plane:
    def __init__(self, n_dp, n_z):
        self.n_dp, self.n_z = n_dp, n_z
        self.n_group = min(n_dp, 8)
        self.n_places = self.n_group // 2
        self.dp = lax.axis_index("dp")
        self.z = lax.axis_index("tensor")
        self.index = lax.rem(self.dp, self.n_group)
        self.core = self.index & 1
        self.place = self.index >> 1

    def swap(self, array, bits):
        return lax.ppermute(array, "dp", [(i, i ^ bits) for i in range(self.n_dp)])

    def shift(self, array, by):
        n = self.n_z
        return lax.ppermute(array, "tensor", [(i, (i + by) % n) for i in range(n)])

    def step_line(self, right, left):
        n = self.n_z
        return (
            lax.ppermute(right, "tensor", [(i, i + 1) for i in range(n - 1)]),
            lax.ppermute(left, "tensor", [(i + 1, i) for i in range(n - 1)]),
        )

    def gather_steps(self, own, steps):
        n, rows = self.n_z, own.shape[0]
        whole = jnp.zeros((n * rows,) + own.shape[1:], own.dtype)
        whole = lax.dynamic_update_slice_in_dim(whole, own, self.z * rows, 0)
        for s in range(1, n):
            came = jnp.where(self.z >= s, steps[s - 1][0], steps[n - 1 - s][1])
            there = lax.rem(self.z + n - s, n) * rows
            whole = lax.dynamic_update_slice_in_dim(whole, came, there, 0)
        return whole

    def gather(self, piece):
        if self.n_dp == self.n_group:
            whole = lax.all_gather(piece, ("tensor", "dp"))
            return whole.reshape((self.n_z, self.n_group) + piece.shape)
        groups = [
            list(range(i, i + self.n_group)) for i in range(0, self.n_dp, self.n_group)
        ]
        line = lax.all_gather(piece, "tensor")
        return lax.all_gather(line, "dp", axis=1, axis_index_groups=groups)

    def turned(self, array):
        bit = 1
        while bit < self.n_group:
            lead = array.reshape((-1, 2, bit) + array.shape[1:])
            array = jnp.where((self.index & bit) != 0, lead[:, ::-1], lead).reshape(array.shape)
            bit *= 2
        return array

    def to_places(self, parts):
        return [self.swap(parts[number], 2 * number) for number in range(1, self.n_places)]

    def from_places(self, own, arrived):
        found = jnp.stack([own] + arrived)
        bit = 1
        while bit < self.n_places:
            lead = found.reshape((-1, 2, bit) + own.shape)
            flipped = lead[:, ::-1]
            found = jnp.where((self.place & bit) != 0, flipped, lead).reshape(found.shape)
            bit *= 2
        return found

    def by_core(self, own, other):
        return jnp.where(
            self.core == 1, jnp.stack([other, own]), jnp.stack([own, other])
        )

    def over_groups(self, array):
        bit = self.n_group
        while bit < self.n_dp:
            array = add(array, self.swap(array, bit))
            bit *= 2
        return array


def on_device(
    n_dp,
    n_z,
    tokens,
    lengths,
    key_mask,
    query_weight,
    query_bias,
    key_weight,
    value_weight,
    value_bias,
    output_weight,
    output_bias,
    first_gain,
    first_shift,
    inner_weight,
    inner_bias,
    outer_weight,
    outer_bias,
    second_gain,
    second_shift,
    cotangent,
):
    width = tokens.shape[1]
    mine = query_weight.shape[1]
    units = inner_weight.shape[1]
    all_rows = tokens.shape[0]
    all_blocks = all_rows // BUCKET
    rows = all_rows // n_z
    plane = Plane(n_dp, n_z)
    z, core, place, index = plane.z, plane.core, plane.place, plane.index
    n_places = plane.n_places
    others = range(1, n_z)

    feed_rows = units // plane.n_group
    head_rows = mine // plane.n_group
    mixer_t = jnp.pad(output_weight.T, ((0, 0), (0, -mine % 128)))
    mixer_count = width // plane.n_group
    mixer_piece = lax.dynamic_slice_in_dim(mixer_t, index * mixer_count, mixer_count, 0)
    mixer_line = [plane.shift(mixer_piece, s) for s in others]
    piece = jnp.concatenate(
        [
            lax.dynamic_slice_in_dim(inner_weight, index * feed_rows, feed_rows, 1).T,
            lax.dynamic_slice_in_dim(outer_weight, index * feed_rows, feed_rows, 0),
        ],
        axis=1,
    )
    line = [plane.shift(piece, s) for s in others]

    query_t, key_t, value_t = query_weight.T, key_weight.T, value_weight.T
    attention_own = jnp.concatenate([query_t, key_t, value_t, output_weight], axis=1)
    attention_weights = plane.gather(
        lax.dynamic_slice_in_dim(attention_own, index * head_rows, head_rows, 0)
    ).reshape(width, 4 * width)

    key_mask_rows = key_mask.reshape(all_blocks, 1, BUCKET)
    bias_row = jnp.concatenate([query_bias, value_bias, inner_bias])
    bias_rows = jnp.pad(bias_row, (0, 16 * BUCKET - bias_row.shape[0])).reshape(16, BUCKET)
    mixed = attend_forward(
        n_z, lengths, tokens, query_t, key_t, value_t, bias_rows, key_mask_rows
    )
    _, line, mixer_line = together(mixed, line, mixer_line)
    mixed = lax.all_to_all(mixed, "tensor", 0, 0)

    mixer_keep = [jnp.stack(mixer_line)]
    mixer_keep += plane.to_places(mixer_keep * n_places)
    mixer_send = [plane.swap(part, 1) for part in mixer_keep]

    cut = feed_rows // 2
    near = [jnp.stack([part[:cut] for part in line]), jnp.stack([part[cut:] for part in line])]
    by_x, by_y = [plane.swap(half, 2) for half in near], [plane.swap(half, 4) for half in near]
    own_units = jnp.concatenate([inner_weight.T, outer_weight], axis=1)

    biases = mixed[:, 0, mine:].reshape(n_z, -1)[:, : bias_row.shape[0]].astype(f32)
    head_biases = jnp.pad(
        jnp.stack([biases[:, :mine].reshape(-1), biases[:, mine : 2 * mine].reshape(-1)]),
        ((0, 6), (0, 0)),
    )
    inner_biases = biases[:, 2 * mine :]
    inner_biases = jnp.concatenate(
        [
            lax.dynamic_slice_in_dim(inner_biases, lax.rem(z + n_z - s, n_z), 1, 0)
            for s in range(n_z)
        ],
        axis=0,
    )
    inner_biases = inner_biases.reshape(n_z, plane.n_group, feed_rows).transpose(1, 0, 2)
    inner_biases = plane.turned(inner_biases).reshape(n_places, 2, 1, n_z * feed_rows)
    inner_biases = inner_biases.transpose(1, 0, 2, 3).reshape(plane.n_group, 1, -1)
    vectors = jnp.stack(
        [output_bias, first_gain, first_shift, outer_bias, second_gain, second_shift]
        + [jnp.zeros_like(output_bias)] * 2
    ).astype(f32)

    place_z = z.reshape(1)
    info = jnp.stack([z, place, core])
    shared_args = (info, vectors, inner_biases, own_units)
    hidden, slope, normed_low, first_normed, first_scale, second_sum = feed_forward(
        ((0, 0),), *shared_args, near, first=(tokens, mixed, mixer_t, mixer_keep + mixer_send)
    )
    second_sum, by_x, by_y = together(second_sum, by_x, by_y)
    far = [plane.swap(by_x[0], 4), plane.swap(by_y[1], 2)]
    send = [plane.swap(half, 1) for half in near + by_x + by_y]
    hidden, slope, second_sum = feed_forward(
        ((0, 1), (0, 2), (1, 0), (1, 1), (1, 2)), *shared_args, by_x + by_y + send,
        going=(normed_low, second_sum, hidden, slope),
    )
    second_sum, far, attention_weights = together(second_sum, far, attention_weights)
    keep = near + by_x + by_y + far
    far_send = [plane.swap(half, 1) for half in far]
    send = send + far_send
    hidden, slope, my_output, grad_second, grad_outer, second_sums = feed_forward(
        ((0, 3), (1, 3)), *shared_args, far + far_send,
        going=(normed_low, second_sum, hidden, slope), last=(lengths, cotangent),
    )
    steps = [plane.step_line(my_output, my_output)]

    shared_args = (info, grad_outer, normed_low, hidden, slope, own_units)
    sent, bias_sent, grad_normed = feed_back(0, 4, *shared_args, grad_second, send)
    other = plane.swap(sent, 1)
    grad_normed, head_biases, tokens, steps[0] = together(
        grad_normed, head_biases, tokens, steps[0]
    )
    steps.append(plane.step_line(*steps[0]))
    projected = project(place_z, tokens, attention_weights, head_biases, mixed.shape[1])
    projected, other = together(projected, other)
    (
        inner_stay, outer_stay, inner_go, outer_go, bias_kept, grad_first, grad_attended, first_sums
    ) = feed_back(
        0, 4, *shared_args, grad_normed, keep, other,
        (first_normed, first_scale, vectors),
    )
    grad_first, grad_attended, inner_go, outer_go, steps[1] = together(
        grad_first, grad_attended, inner_go, outer_go, steps[1]
    )
    for _ in range(n_z - 3):
        steps.append(plane.step_line(*steps[-1]))
    inner_came, outer_came = plane.swap(inner_go, 4), plane.swap(outer_go, 2)
    bias_grads = jnp.stack(
        [bias_kept[:, 0], bias_sent[:, 0]], axis=1
    )
    inner_bias_grad = plane.turned(bias_grads.reshape(plane.n_group, n_z, feed_rows))
    inner_bias_grad = inner_bias_grad.transpose(1, 0, 2)
    inner_bias_grad = jnp.concatenate(
        [
            sum(
                jnp.where(lax.rem(z - t + n_z, n_z) == s, inner_bias_grad[s : s + 1], 0.0)
                for s in range(n_z)
            )
            for t in range(n_z)
        ],
        axis=0,
    ).reshape(n_z, units)

    grads, my_tokens_grad, back_sums = attend_back(
        place_z, lengths, grad_attended, grad_first, attention_weights, *projected, key_mask_rows
    )
    grads, inner_came, outer_came, steps[2:] = together(grads, inner_came, outer_came, steps[2:])
    inner_on, outer_on = (
        plane.swap(add(inner_stay[1], inner_came[1]), 2),
        plane.swap(add(outer_stay[1], outer_came[1]), 4),
    )
    tokens_grad = lax.all_gather(my_tokens_grad, "tensor", axis=0, tiled=True)

    def weight_grads(side, other=None, small=None):
        info = jnp.stack([2 * side, 2 * side + 1, z, place])
        return attention_grads(
            n_places, info, grads, mixed, tokens, grad_attended, other, small
        )

    (sent,) = weight_grads(1 - core)
    sent, back_sums, first_sums, second_sums, inner_bias_grad = together(
        sent, back_sums, first_sums, second_sums, inner_bias_grad
    )
    other = plane.swap(sent, 1)

    small = jnp.concatenate(
        [first_sums[:3], second_sums[:3], inner_bias_grad, jnp.sum(back_sums, axis=0)[:2]], axis=0
    )
    small = jnp.pad(small, ((0, -small.shape[0] % 16), (0, 0))).astype(bf16)
    small_rows = small.shape[0]

    small = add(small, plane.swap(small, 1))
    kept = list(weight_grads(core, other, small))
    arrived = plane.to_places(kept)
    kept[0], inner_on, outer_on = together(kept[0], inner_on, outer_on)
    feed_parts = [
        jnp.concatenate(
            [
                add(inner_stay[0, s], inner_came[0, s], inner_on[s]),
                add(outer_stay[0, s], outer_came[0, s], outer_on[s]),
            ],
            axis=1,
        )
        for s in range(n_z)
    ]
    feed_line = [plane.shift(feed_parts[s], -s) for s in others]
    arrived, feed_line = together(arrived, feed_line)
    small = add(small, *[a[-small_rows:] for a in arrived])
    count = 2 * mine // n_places
    attention_parts = [
        add(*[a[s * count : (s + 1) * count] for a in [kept[0]] + arrived]) for s in range(n_z)
    ]
    attention_line = [
        plane.shift(jnp.concatenate([attention_parts[s], small], axis=0), s) for s in others
    ]
    feed_total = plane.over_groups(add(feed_parts[0], *feed_line))
    feed_arrived = plane.to_places([feed_total] * n_places)
    output = plane.gather_steps(my_output, steps)
    attention_line, feed_arrived, tokens_grad, output = together(
        attention_line, feed_arrived, tokens_grad, output
    )
    attention_total = plane.over_groups(
        add(attention_parts[0], *[a[:count] for a in attention_line])
    )
    small = plane.over_groups(add(small, *[a[count:] for a in attention_line])).astype(f32)
    arrived = plane.to_places([attention_total] * n_places)
    feed_half = plane.from_places(feed_total, feed_arrived)
    feed_other = plane.swap(feed_half, 1)
    inner_grad, outer_grad = finish_feed(core.reshape(1), feed_half, feed_other)
    inner_bias_sum = lax.dynamic_slice_in_dim(small, 6 + z, 1, 0)[0]
    head_sums = lax.dynamic_slice_in_dim(small[6 + n_z : 8 + n_z], z * mine, mine, 1)
    arrived, inner_grad, outer_grad, small, inner_bias_sum, head_sums = together(
        arrived, inner_grad, outer_grad, small, inner_bias_sum, head_sums
    )
    attention_half = plane.from_places(attention_total, arrived)
    attention_other = plane.swap(attention_half, 1)
    grad_list = plane.by_core(attention_half, attention_other)
    grad_list = grad_list.reshape(2, n_places, 2, mine // n_places, width)
    grad_list = grad_list.transpose(0, 2, 1, 3, 4).reshape(4, mine, width)

    shared = small[:6]

    return (
        output,
        tokens_grad,
        grad_list[0].T.astype(f32),
        head_sums[0],
        grad_list[1].T.astype(f32),
        grad_list[2].T.astype(f32),
        head_sums[1],
        grad_list[3].astype(f32),
        shared[0],
        shared[1],
        shared[2],
        inner_grad,
        inner_bias_sum,
        outer_grad,
        shared[3],
        shared[4],
        shared[5],
    )


def solution(mesh):
    n_dp, n_z = mesh.shape["dp"], mesh.shape["tensor"]
    in_specs = (
        P("dp", None),
        P("dp", None),
        P("dp"),
        P(None, "tensor"),
        P("tensor"),
        P(None, "tensor"),
        P(None, "tensor"),
        P("tensor"),
        P("tensor", None),
        P(),
        P(),
        P(),
        P(None, "tensor"),
        P("tensor"),
        P("tensor", None),
        P(),
        P(),
        P(),
        P("dp", None),
    )
    out_specs = (
        P("dp", None),
        P("dp", None),
        P(None, "tensor"),
        P("tensor"),
        P(None, "tensor"),
        P(None, "tensor"),
        P("tensor"),
        P("tensor", None),
        P(),
        P(),
        P(),
        P(None, "tensor"),
        P("tensor"),
        P("tensor", None),
        P(),
        P(),
        P(),
    )

    def program(*args):
        return on_device(n_dp, n_z, *args)

    return jax.shard_map(
        program, mesh=mesh, in_specs=in_specs, out_specs=out_specs, check_vma=False
    )
```

```python
import functools

import jax
import jax.numpy as jnp
from jax import lax
from jax.experimental import pallas as pl
from jax.experimental.pallas import tpu as pltpu
from jax.sharding import PartitionSpec as P

HEAD = 64
BUCKET = 512
ITEMS = 8


negative_fill = -1e30
epsilon = 1e-06
f32 = jnp.float32
bf16 = jnp.bfloat16
VMEM_BYTES = 56 * 1024 * 1024


def dot(left, right):
    return jnp.dot(left, right, preferred_element_type=f32)


def contract_rows(left, right):
    return lax.dot_general(left, right, (((0,), (0,)), ((), ())), preferred_element_type=f32)


def contract_cols(left, right):
    return lax.dot_general(left, right, (((1,), (1,)), ((), ())), preferred_element_type=f32)


def norm_rows(values):
    centred = values - jnp.mean(values, axis=1, keepdims=True)
    inv_scale = lax.rsqrt(jnp.mean(centred * centred, axis=1, keepdims=True) + epsilon)
    return centred * inv_scale, inv_scale


def norm_back(grad_rows, norm_gain, normed, inv_scale):
    scaled = grad_rows * norm_gain
    return inv_scale * (
        scaled
        - jnp.mean(scaled, axis=1, keepdims=True)
        - normed * jnp.mean(scaled * normed, axis=1, keepdims=True)
    )


def column_sum(matrix):
    return jnp.sum(matrix.astype(f32), axis=0, keepdims=True)


def fixed(shape):
    return pl.BlockSpec(shape, lambda *_: (0,) * len(shape))


def cost(microseconds):
    return pl.CostEstimate(
        flops=int(microseconds * 2.5e8),
        bytes_accessed=int(microseconds * 2.5e5),
        transcendentals=0,
    )


def params(axes):
    return pltpu.CompilerParams(
        dimension_semantics=("arbitrary",) * axes, vmem_limit_bytes=VMEM_BYTES
    )


def item_places(lengths_ref, row, shape, axis):
    places = lax.broadcasted_iota(jnp.int32, shape, axis)
    end = jnp.int32(0)
    items = jnp.zeros(shape, jnp.int32)
    for slot in range(ITEMS):
        end = end + lengths_ref[row, slot]
        items = items + (places >= end).astype(jnp.int32)
    return items


def as_column(row):
    return jnp.broadcast_to(row.astype(f32), (8, row.shape[1])).T[:, :1]


def mask_bias(lengths_ref, row, key_mask):
    shape = (BUCKET, BUCKET)
    diagonal = lax.broadcasted_iota(jnp.int32, shape, 0) == lax.broadcasted_iota(
        jnp.int32, shape, 1
    )
    item_row = item_places(lengths_ref, row, (1, BUCKET), 1)
    item_column = item_places(lengths_ref, row, (BUCKET, 1), 0)
    code_column = jnp.where(as_column(key_mask) == 1.0, item_column, -1)
    return jnp.where((code_column == item_row) | diagonal, 0.0, negative_fill).astype(f32)


def attend_forward_kernel(
    lengths_ref, tokens_ref, query_ref, key_ref, value_ref, biases_ref, key_mask_ref, mixed_ref,
):
    mine = query_ref.shape[0]
    rows = tokens_ref[...]
    queries = contract_cols(query_ref[...], rows) + as_column(biases_ref[0:1, :mine])
    queries = (queries.astype(bf16) * HEAD ** (-0.5)).astype(bf16)
    keys = contract_cols(rows, key_ref[...]).astype(bf16)
    values = contract_cols(value_ref[...], rows) + as_column(biases_ref[0:1, mine : 2 * mine])
    values = values.astype(bf16)
    bias = mask_bias(lengths_ref, pl.program_id(0), key_mask_ref[0])
    for head in range(mine // HEAD):
        at = slice(head * HEAD, (head + 1) * HEAD)
        scores = dot(keys[:, at], queries[at]) + bias
        exponent = jnp.exp(scores - jnp.max(scores, axis=0, keepdims=True))
        total = jnp.sum(exponent, axis=0, keepdims=True)
        mixed_ref[0, 0, at] = (dot(values[at], exponent.astype(bf16)) / total).astype(bf16)
    mixed_ref[0, 0, mine:] = biases_ref[...]


def attend_forward(n_z, lengths, tokens, query, key, value, biases, key_mask):
    blocks = lengths.shape[0]
    own = blocks // n_z
    mine, width = key.shape
    whole = (n_z, own, mine + biases.shape[0], BUCKET)
    return pl.pallas_call(
        attend_forward_kernel,
        grid=(blocks,),
        in_specs=[
            pl.BlockSpec(memory_space=pltpu.SMEM),
            pl.BlockSpec((BUCKET, width), lambda b: (b, 0)),
            fixed((mine, width)),
            fixed((mine, width)),
            fixed((mine, width)),
            fixed(biases.shape),
            pl.BlockSpec((1, 1, BUCKET), lambda b: (b, 0, 0)),
        ],
        out_specs=pl.BlockSpec((1, 1) + whole[2:], lambda b: (b // own, b % own, 0, 0)),
        out_shape=jax.ShapeDtypeStruct(whole, bf16),
        compiler_params=params(1),
        name="attend_forward",
        cost_estimate=cost(12),
    )(lengths, tokens, query, key, value, biases, key_mask)


def fetch_units(step, picks, own_ref, halves, units, sems):
    feed_rows = units.shape[2]
    cut = feed_rows // 2

    def copies(number):
        slot = number % 2
        row = pl.multiple_of(picks[number] * feed_rows, 16)
        ends = [
            (own_ref.at[pl.ds(row, feed_rows)], units.at[slot, 0]),
            (halves[number][0], units.at[slot, 1:, :cut]),
            (halves[number][1], units.at[slot, 1:, cut:]),
        ]
        return [
            pltpu.make_async_copy(source, target, sems.at[slot, i])
            for i, (source, target) in enumerate(ends)
        ]

    for number in range(len(halves)):

        @pl.when(step == number)
        def _(number=number):
            if number == 0:
                for copy in copies(0):
                    copy.start()
            if number + 1 < len(halves):
                for copy in copies(number + 1):
                    copy.start()
            for copy in copies(number):
                copy.wait()

    return units.at[lax.rem(step, 2)]


def fetch_mixer(picks, own_ref, parts, mixer, sems):
    count = mixer.shape[1] // 8
    ends = [(own_ref, mixer.at[0])]
    for pick, part in zip(picks, parts):
        row = pl.multiple_of(pick * count, 16)
        ends.append((part, mixer.at[1:, pl.ds(row, count)]))
    copies = [
        pltpu.make_async_copy(source, target, sems.at[i])
        for i, (source, target) in enumerate(ends)
    ]
    for copy in copies:
        copy.start()
    for copy in copies:
        copy.wait()


def take_halves(numbers, refs):
    halves, refs = [], list(refs)
    for number in numbers:
        if number == 3:
            halves.append((refs.pop(0), refs.pop(0)))
        else:
            ref = refs.pop(0)
            cut = ref.shape[1] // 2
            halves.append((ref.at[:, :cut], ref.at[:, cut:]))
    return halves, refs


def split_units(units):
    width = units.shape[2] // 2
    return units[:, :, :width].reshape(-1, width), units[:, :, width:].reshape(-1, width)


ANYWHERE = pl.BlockSpec(memory_space=pl.ANY)


def feed_forward_kernel(chunks, first, last, info_ref, *rest):
    def take(count):
        nonlocal rest
        taken, rest = rest[:count], rest[count:]
        return taken

    vectors_ref, bias_ref, own_ref = take(3)
    halves, rest = take_halves([number for _, number in chunks], rest)
    if first:
        tokens_ref, mixed_ref, mixer_own_ref, *mixer_parts = take(11)
    else:
        normed_low_ref, start_ref, _, _ = take(4)
    if last:
        lengths_ref, cotangent_ref = take(2)
    hidden_ref, slope_ref = take(2)
    if first:
        normed_low_ref, first_normed_ref, first_scale_ref = take(3)
    if last:
        output_ref, grad_second_ref, grad_outer_ref, sums_ref = take(4)
    else:
        (second_sum,) = take(1)
    units, sems = take(2)
    if first:
        mixer, mixer_sems = take(2)
    if last:
        (second_sum,) = take(1)

    step = pl.program_id(0)
    picks = [(info_ref[1] ^ number) * 2 + (info_ref[2] ^ side) for side, number in chunks]
    weights = fetch_units(step, picks, own_ref, halves, units, sems)
    output_bias, first_gain, first_shift, outer_bias, second_gain, second_shift = (
        vectors_ref[i : i + 1, :] for i in range(6)
    )

    @pl.when(step == 0)
    def _():
        if first:
            all_picks = [
                (info_ref[1] ^ number) * 2 + (info_ref[2] ^ side)
                for side in range(2)
                for number in range(4)
            ]
            fetch_mixer(all_picks, mixer_own_ref, mixer_parts, mixer, mixer_sems)
            n_z, own, mine, _ = mixed_ref.shape
            attended = output_bias + jnp.concatenate(
                [
                    sum(
                        dot(mixer[s, :, :mine], mixed_ref[lax.rem(info_ref[0] + n_z - s, n_z), b])
                        for s in range(n_z)
                    ).T
                    for b in range(own)
                ],
                axis=0,
            )
            normed, inv_scale = norm_rows(tokens_ref[...].astype(f32) + attended)
            whole = normed * first_gain + first_shift
            first_normed_ref[...] = normed
            first_scale_ref[...] = inv_scale
            normed_low_ref[...] = whole.astype(bf16)
            second_sum[...] = whole + outer_bias
        else:
            second_sum[...] = start_ref[...]

    inner, outer = split_units(weights)
    inner_pre = contract_cols(normed_low_ref[...], inner) + bias_ref[0]
    normal_cdf = 0.5 + 0.5 * lax.erf(inner_pre * 0.7071067811865476)
    bell = jnp.exp(-0.5 * inner_pre * inner_pre)
    hidden = (inner_pre * normal_cdf).astype(bf16)
    hidden_ref[...] = hidden.T
    slope_ref[...] = (normal_cdf + inner_pre * bell * 0.3989422804014327).astype(bf16)
    second_sum[...] += dot(hidden, outer)

    if last:

        @pl.when(step == pl.num_programs(0) - 1)
        def _():
            normed, inv_scale = norm_rows(second_sum[...])
            blocks = normed.shape[0] // BUCKET
            live = jnp.concatenate(
                [
                    (item_places(lengths_ref, info_ref[0] * blocks + b, (BUCKET, 1), 0) < ITEMS)
                    for b in range(blocks)
                ],
                axis=0,
            ).astype(f32)
            output_ref[...] = ((normed * second_gain + second_shift) * live).astype(bf16)
            grad_final = cotangent_ref[...].astype(f32) * live
            grad_second = norm_back(grad_final, second_gain, normed, inv_scale)
            grad_outer = grad_second.astype(bf16)
            grad_second_ref[...] = grad_second
            grad_outer_ref[...] = grad_outer
            sums_ref[0:1, :] = column_sum(grad_outer)
            sums_ref[1:2, :] = column_sum(grad_final * normed)
            sums_ref[2:3, :] = column_sum(grad_final)


def feed_forward(chunks, info, vectors, biases, own, halves, first=None, going=None, last=None):
    width = vectors.shape[1]
    n_z = halves[0].shape[0] + 1
    feed_rows, twice = own.shape[0] // 8, 2 * width
    rows = first[1].shape[1] * BUCKET if first else going[0].shape[0]
    chunk = n_z * feed_rows
    whole = fixed((rows, width))
    my_rows = pl.BlockSpec((rows, width), lambda j, info: (info[0], 0))
    at = lambda j, info: info[3 + j]
    hidden_spec = pl.BlockSpec((chunk, rows), lambda j, info: (at(j, info), 0))
    slope_spec = pl.BlockSpec((rows, chunk), lambda j, info: (0, at(j, info)))
    in_specs = [
        fixed((8, width)),
        pl.BlockSpec((1, 1, chunk), lambda j, info: (at(j, info), 0, 0)),
        ANYWHERE,
    ] + [ANYWHERE] * len(halves)
    args = [vectors, biases, own] + halves
    shapes = [
        ((8 * chunk, rows), bf16, hidden_spec),
        ((rows, 8 * chunk), bf16, slope_spec),
    ]
    scratch = [
        pltpu.VMEM((2, n_z, feed_rows, twice), bf16),
        pltpu.SemaphoreType.DMA((2, 3)),
    ]
    aliases = {}
    if first:
        tokens, mixed, mixer_own, mixer_parts = first
        mine = width // n_z
        in_specs += [my_rows, fixed((n_z, mixed.shape[1], mine, BUCKET))] + [ANYWHERE] * 9
        args += [tokens, mixed, mixer_own] + mixer_parts
        shapes += [
            ((rows, width), bf16, whole),
            ((rows, width), f32, whole),
            ((rows, 1), f32, fixed((rows, 1))),
        ]
        scratch += [
            pltpu.VMEM((n_z,) + mixer_own.shape, bf16),
            pltpu.SemaphoreType.DMA((9,)),
        ]
    else:
        aliases = {1 + len(args) + 2: 0, 1 + len(args) + 3: 1}
        in_specs += [whole, whole, ANYWHERE, ANYWHERE]
        args += list(going)
    if last:
        in_specs += [pl.BlockSpec(memory_space=pltpu.SMEM), my_rows]
        args += list(last)
        shapes += [
            ((rows, width), bf16, whole),
            ((rows, width), f32, whole),
            ((rows, width), bf16, whole),
            ((8, width), f32, fixed((8, width))),
        ]
        scratch.append(pltpu.VMEM((rows, width), f32))
    else:
        shapes.append(((rows, width), f32, whole))
    info = jnp.concatenate(
        [info, jnp.array([4 * side + number for side, number in chunks], jnp.int32)]
    )
    return pl.pallas_call(
        functools.partial(feed_forward_kernel, chunks, first is not None, last is not None),
        grid_spec=pltpu.PrefetchScalarGridSpec(
            num_scalar_prefetch=1,
            grid=(len(chunks),),
            in_specs=in_specs,
            out_specs=[spec for _, _, spec in shapes],
            scratch_shapes=scratch,
        ),
        out_shape=[jax.ShapeDtypeStruct(shape, kind) for shape, kind, _ in shapes],
        input_output_aliases=aliases,
        compiler_params=params(1),
        name="feed_forward",
        cost_estimate=cost(3 * len(chunks)),
    )(info, *args)


STAY = ((0, 1), (0, 2))
GO = ((2, 3), (1, 3))


def feed_back_kernel(
    keeps, info_ref, grad_outer_ref, normed_low_ref, hidden_ref, slope_ref,
    own_ref, start_ref, *rest,
):
    halves, rest = take_halves(range(4), rest)
    if keeps:
        other_refs, norm_refs, rest = rest[:2], rest[2:5], rest[5:]
        stay_refs, go_refs, rest = rest[0:2], rest[2:4], rest[4:]
        bias_grad_ref, grad_first_ref, grad_attended_ref, sums_ref, units, sems = rest[:6]
        grad_normed_ref = rest[6]
    else:
        *grad_refs, bias_grad_ref, grad_normed_ref, units, sems = rest
    step = pl.program_id(0)
    side = info_ref[2] if keeps else 1 - info_ref[2]
    picks = [(info_ref[1] ^ number) * 2 + side for number in range(4)]
    weights = fetch_units(step, picks, own_ref, halves, units, sems)

    @pl.when(step == 0)
    def _():
        grad_normed_ref[...] = start_ref[...]

    n_z, feed_rows, twice = weights.shape
    width = twice // 2
    inner, outer = split_units(weights)
    grad_outer = grad_outer_ref[...]
    grad_hidden = contract_cols(grad_outer, outer)
    grad_inner = (grad_hidden * slope_ref[...].astype(f32)).astype(bf16)
    outer_grad = dot(hidden_ref[...], grad_outer).reshape(n_z, feed_rows, width)
    inner_grad = contract_rows(grad_inner, normed_low_ref[...]).reshape(n_z, feed_rows, width)
    bias_grad_ref[0] = column_sum(grad_inner)
    grad_normed_ref[...] += dot(grad_inner, inner)

    blocks = [lax.rem(info_ref[0] + n_z - s, n_z) for s in range(n_z)]
    for number in range(4):

        @pl.when(step == number)
        def _(number=number):
            for track, value in enumerate((inner_grad, outer_grad)):
                at = slice(track * width, (track + 1) * width)
                for s, block in enumerate(blocks):
                    if keeps:
                        found = value[s] + other_refs[number // 2][0, block, :, at].astype(f32)
                        ref = stay_refs[track] if number in STAY[track] else go_refs[track]
                        ref[0, block] = found.astype(bf16)
                    else:
                        grad_refs[number // 2][0, block, :, at] = value[s].astype(bf16)

    if keeps:

        @pl.when(step == pl.num_programs(0) - 1)
        def _():
            first_normed_ref, first_scale_ref, vectors_ref = norm_refs
            grad_rows, normed = grad_normed_ref[...], first_normed_ref[...]
            grad_first = norm_back(grad_rows, vectors_ref[1:2, :], normed, first_scale_ref[...])
            grad_attended = grad_first.astype(bf16)
            grad_first_ref[...] = grad_first
            grad_attended_ref[...] = grad_attended
            sums_ref[0:1, :] = column_sum(grad_attended)
            sums_ref[1:2, :] = column_sum(grad_rows * normed)
            sums_ref[2:3, :] = column_sum(grad_rows)


def feed_back(
    info, grad_outer, normed_low, hidden, slope, own, start, units, others=None, norm=None
):
    rows, width = grad_outer.shape
    keeps = others is not None
    count = 4
    feed_rows, twice = own.shape[0] // 8, 2 * width
    n_z = units[0].shape[0] + 1
    chunk = n_z * feed_rows
    flip = 0 if keeps else 1
    columns = pl.BlockSpec((rows, chunk), lambda i, info: (0, 4 * flip + i))
    whole = fixed((rows, width))
    part = (n_z, feed_rows, twice)
    track = (2, n_z, feed_rows, width)
    unit_rows = pl.BlockSpec((chunk, rows), lambda i, info: (4 * flip + i, 0))
    in_specs = [whole, whole, unit_rows, columns, ANYWHERE, whole] + [ANYWHERE] * len(units)
    args = [grad_outer, normed_low, hidden, slope, own, start] + units
    bias_shape = (
        (count, 1, chunk),
        f32,
        pl.BlockSpec((1, 1, chunk), lambda i, info: (i, 0, 0)),
    )
    scratch = [pltpu.VMEM((2,) + part, bf16), pltpu.SemaphoreType.DMA((2, 3))]

    def one(shape, at):
        return pl.BlockSpec((1,) + shape[1:], lambda i, info: (at(i), 0, 0, 0))

    early, late = (lambda i: jnp.minimum(i, 1)), (lambda i: jnp.maximum(i - 2, 0))
    pair = (2,) + part
    if keeps:
        in_specs += [one(pair, early), one(pair, late)]
        in_specs += [whole, fixed((rows, 1)), fixed((8, width))]
        args += list(others) + list(norm)
        slow, slower = (lambda i: i // 2), (lambda i: jnp.maximum(i - 1, 0) // 2)
        shapes = [(track, bf16, one(track, at)) for at in (early, slow, late, slower)] + [
            bias_shape,
            ((rows, width), f32, whole),
            ((rows, width), bf16, whole),
            ((8, width), f32, fixed((8, width))),
        ]
        scratch.append(pltpu.VMEM((rows, width), f32))
    else:
        shapes = [
            (pair, bf16, one(pair, early)),
            (pair, bf16, one(pair, late)),
            bias_shape,
            ((rows, width), f32, whole),
        ]
    return pl.pallas_call(
        functools.partial(feed_back_kernel, keeps),
        grid_spec=pltpu.PrefetchScalarGridSpec(
            num_scalar_prefetch=1,
            grid=(count,),
            in_specs=in_specs,
            out_specs=[spec for _, _, spec in shapes],
            scratch_shapes=scratch,
        ),
        out_shape=[jax.ShapeDtypeStruct(shape, kind) for shape, kind, _ in shapes],
        compiler_params=params(1),
        name="feed_back_own" if keeps else "feed_back",
        cost_estimate=cost(3 * count),
    )(info, *args)


def finish_feed_kernel(core_ref, own_ref, other_ref, inner_ref, outer_ref, inner_rows):
    places, count, twice = own_ref.shape
    width = twice // 2
    for source, side in ((own_ref, core_ref[0]), (other_ref, 1 - core_ref[0])):
        for place in range(places):
            row = pl.multiple_of((2 * place + side) * count, 16)
            inner_rows[pl.ds(row, count), :] = source[place, :, :width].astype(f32)
            outer_ref[pl.ds(row, count), :] = source[place, :, width:].astype(f32)
    inner_ref[...] = inner_rows[...].T


def finish_feed(core, own, other):
    places, count, twice = own.shape
    shape = (2 * places * count, twice // 2)
    inner_shape = (shape[1], shape[0])
    return pl.pallas_call(
        finish_feed_kernel,
        grid_spec=pltpu.PrefetchScalarGridSpec(
            num_scalar_prefetch=1,
            grid=(1,),
            in_specs=[fixed(own.shape), fixed(other.shape)],
            out_specs=[fixed(inner_shape), fixed(shape)],
            scratch_shapes=[pltpu.VMEM(shape, f32)],
        ),
        out_shape=[
            jax.ShapeDtypeStruct(inner_shape, f32),
            jax.ShapeDtypeStruct(shape, f32),
        ],
        compiler_params=params(1),
        name="finish_feed",
        cost_estimate=cost(5),
    )(core, own, other)


def project_kernel(place_ref, tokens_ref, weights_ref, biases_ref, query_ref, key_ref, value_ref):
    rows = tokens_ref[...]
    width = rows.shape[1]
    queries = contract_cols(weights_ref[:, :width], rows) + as_column(biases_ref[0:1, :])
    query_ref[...] = (queries.astype(bf16) * HEAD ** (-0.5)).astype(bf16)
    key_ref[...] = contract_cols(rows, weights_ref[:, width : 2 * width]).astype(bf16)
    values = contract_cols(rows, weights_ref[:, 2 * width :]) + biases_ref[1:2, :]
    value_ref[...] = values.astype(bf16)


def project(place, tokens, weights, biases, buckets):
    width = tokens.shape[1]
    part = width // 3
    shapes = [
        ((buckets, width, BUCKET), pl.BlockSpec((None, part, BUCKET), lambda b, j, _: (b, j, 0))),
        ((buckets * BUCKET, width), pl.BlockSpec((BUCKET, part), lambda b, j, _: (b, j))),
        ((buckets * BUCKET, width), pl.BlockSpec((BUCKET, part), lambda b, j, _: (b, j))),
    ]
    return pl.pallas_call(
        project_kernel,
        grid_spec=pltpu.PrefetchScalarGridSpec(
            num_scalar_prefetch=1,
            grid=(buckets, 3),
            in_specs=[
                pl.BlockSpec((BUCKET, width), lambda b, j, place: (place[0] * buckets + b, 0)),
                pl.BlockSpec((part, 3 * width), lambda b, j, place: (j, 0)),
                pl.BlockSpec((8, part), lambda b, j, place: (0, j)),
            ],
            out_specs=[spec for _, spec in shapes],
        ),
        out_shape=[jax.ShapeDtypeStruct(shape, bf16) for shape, _ in shapes],
        compiler_params=params(2),
        name="project",
        cost_estimate=cost(5),
    )(place, tokens, weights, biases)


def attend_back_kernel(
    place_ref, lengths_ref, grad_attended_ref, grad_first_ref, weights_ref, query_ref, key_ref,
    value_ref, key_mask_ref,
    grads_ref, tokens_grad_ref, sums_ref,
    bias, grad_mixed_t, whole, weights, sem,
):
    pair = pl.program_id(1)
    pairs, width = whole.shape[1], weights.shape[0]
    fetch = pltpu.make_async_copy(weights_ref, weights, sem)

    @pl.when(pair == 0)
    def _():
        fetch.start()
        row = place_ref[0] * pl.num_programs(0) + pl.program_id(0)
        bias[...] = mask_bias(lengths_ref, row, key_mask_ref[0])
        fetch.wait()
        grad_mixed_t[...] = contract_cols(
            weights[:, 3 * width :], grad_attended_ref[...]
        ).astype(bf16)

    queries, keys, values = query_ref[...], key_ref[...], value_ref[...]
    start = pl.multiple_of(pair * keys.shape[1], 128)
    grad_mixed = grad_mixed_t[pl.ds(start, keys.shape[1]), :]
    keys_t = keys.T
    grad_queries, grad_keys, grad_values = [], [], []
    for head in range(keys.shape[1] // HEAD):
        at = slice(head * HEAD, (head + 1) * HEAD)
        scores = dot(keys[:, at], queries[at]) + bias[...]
        exponent = jnp.exp(scores - jnp.max(scores, axis=0, keepdims=True))
        probs = exponent * (1.0 / jnp.sum(exponent, axis=0, keepdims=True))
        grad_probs = dot(values[:, at], grad_mixed[at])
        shift = jnp.sum(probs * grad_probs, axis=0, keepdims=True)
        grad_scores = (probs * (grad_probs - shift)).astype(bf16)
        grad_values.append(contract_cols(probs.astype(bf16), grad_mixed[at]))
        grad_keys.append(contract_cols(grad_scores, queries[at]))
        grad_queries.append(dot(keys_t[at], grad_scores) * HEAD ** (-0.5))
    query_t = jnp.concatenate(grad_queries, axis=0).astype(bf16)
    found = (
        query_t.T,
        jnp.concatenate(grad_keys, axis=1).astype(bf16),
        jnp.concatenate(grad_values, axis=1).astype(bf16),
    )
    for number, grad in enumerate(found):
        grads_ref[number, 0] = query_t if number == 0 else grad.T
        whole[number, pair] = grad
    sums_ref[0, 0:1, :] = column_sum(found[0])
    sums_ref[0, 1:2, :] = column_sum(found[2])

    @pl.when(pair == pl.num_programs(1) - 1)
    def _():
        total = grad_first_ref[...]
        for number in range(3):
            grad = jnp.concatenate([whole[number, i] for i in range(pairs)], axis=1)
            total += dot(grad, weights[:, number * width : (number + 1) * width])
        tokens_grad_ref[...] = total.astype(bf16)


def attend_back(place, lengths, grad_attended, grad_first, weights, queries, keys, values, key_mask):
    rows, width = grad_attended.shape
    blocks = rows // BUCKET
    pair = 2 * HEAD
    by_bucket = pl.BlockSpec((BUCKET, width), lambda b, h, place: (b, 0))
    by_pair = pl.BlockSpec((BUCKET, pair), lambda b, h, place: (b, h))
    return pl.pallas_call(
        attend_back_kernel,
        grid_spec=pltpu.PrefetchScalarGridSpec(
            num_scalar_prefetch=1,
            grid=(blocks, width // pair),
            in_specs=[
                pl.BlockSpec(memory_space=pltpu.SMEM),
                by_bucket,
                by_bucket,
                ANYWHERE,
                pl.BlockSpec((None, pair, BUCKET), lambda b, h, place: (b, h, 0)),
                by_pair,
                by_pair,
                pl.BlockSpec((1, 1, BUCKET), lambda b, h, place: (place[0] * blocks + b, 0, 0)),
            ],
            out_specs=[
                pl.BlockSpec((3, 1, pair, BUCKET), lambda b, h, place: (0, b, h, 0)),
                by_bucket,
                pl.BlockSpec((1, 8, pair), lambda b, h, place: (b, 0, h)),
            ],
            scratch_shapes=[
                pltpu.VMEM((BUCKET, BUCKET), f32),
                pltpu.VMEM((width, BUCKET), bf16),
                pltpu.VMEM((3, width // pair, BUCKET, pair), bf16),
                pltpu.VMEM(weights.shape, bf16),
                pltpu.SemaphoreType.DMA(()),
            ],
        ),
        out_shape=[
            jax.ShapeDtypeStruct((3, blocks, width, BUCKET), bf16),
            jax.ShapeDtypeStruct((rows, width), bf16),
            jax.ShapeDtypeStruct((blocks, 8, width), f32),
        ],
        compiler_params=params(2),
        name="attend_back",
        cost_estimate=cost(20),
    )(place, lengths, grad_attended, grad_first, weights, queries, keys, values, key_mask)


def attention_grads_kernel(
    n_places, adds, info_ref, grads_ref, mixed_ref, tokens_ref, grad_attended_ref, *rest
):
    if adds:
        other_ref, small_ref = rest[:2]
        out_refs, whole = rest[2:-1], rest[-1]
    else:
        (out_ref, whole) = rest
    step = pl.program_id(0)
    which = info_ref[step]
    n_z, buckets, mine, _ = mixed_ref.shape
    count = mine // n_places

    @pl.when(which < 3)
    def _():
        whole[...] = sum(
            dot(grads_ref[0, b], tokens_ref[b * BUCKET : (b + 1) * BUCKET, :])
            for b in range(buckets)
        ).astype(bf16)

    @pl.when(which == 3)
    def _():
        for t in range(n_z):
            whole[t * mine : (t + 1) * mine, :] = sum(
                dot(mixed_ref[t, b], grad_attended_ref[b * BUCKET : (b + 1) * BUCKET, :])
                for b in range(buckets)
            ).astype(bf16)

    for number in range(n_places):
        for s in range(n_z):
            start = s * mine + (info_ref[3] ^ number) * count
            value = whole[pl.ds(pl.multiple_of(start, 16), count), :]
            if adds:
                value = value.astype(f32) + other_ref[number, s, 0].astype(f32)
                row = (2 * s + step) * count
                out_refs[number][pl.ds(pl.multiple_of(row, 16), count), :] = value.astype(bf16)
            else:
                out_ref[number, s, 0] = value

    if adds:
        for number in range(n_places):
            out_refs[number][2 * n_z * count :, :] = small_ref[...]


def attention_grads(n_places, info, grads, mixed, tokens, grad_attended, other=None, small=None):
    rows, width = grad_attended.shape
    n_z, buckets = mixed.shape[:2]
    mine = width // n_z
    count = mine // n_places
    parts = (n_places, n_z, 1, count, width)
    by_step = pl.BlockSpec(parts, lambda i, info: (0, 0, i, 0, 0))
    in_specs = [
        pl.BlockSpec(
            (1, buckets, width, BUCKET), lambda i, info: (jnp.minimum(info[i], 2), 0, 0, 0)
        ),
        fixed((n_z, buckets, mine, BUCKET)),
        pl.BlockSpec((rows, width), lambda i, info: (info[2], 0)),
        fixed((rows, width)),
    ]
    args = [grads, mixed, tokens, grad_attended]
    if other is None:
        shapes = [((n_places, n_z, 2, count, width), by_step)]
    else:
        in_specs += [by_step, fixed(small.shape)]
        args += [other, small]
        flat = (2 * n_z * count + small.shape[0], width)
        shapes = [(flat, fixed(flat))] * n_places
    return pl.pallas_call(
        functools.partial(attention_grads_kernel, n_places, other is not None),
        grid_spec=pltpu.PrefetchScalarGridSpec(
            num_scalar_prefetch=1,
            grid=(2,),
            in_specs=in_specs,
            out_specs=[spec for _, spec in shapes],
            scratch_shapes=[pltpu.VMEM((width, width), bf16)],
        ),
        out_shape=[jax.ShapeDtypeStruct(shape, bf16) for shape, _ in shapes],
        compiler_params=params(1),
        name="attention_grads",
        cost_estimate=cost(6),
    )(info, *args)


def together(*values):
    return lax.optimization_barrier(values)


def add(first, *others):
    total = first.astype(f32)
    for other in others:
        total = total + other.astype(f32)
    return total.astype(bf16)


class Plane:
    def __init__(self, n_dp, n_z):
        self.n_dp, self.n_z = n_dp, n_z
        self.n_group = min(n_dp, 8)
        self.n_places = self.n_group // 2
        self.dp = lax.axis_index("dp")
        self.z = lax.axis_index("tensor")
        self.index = lax.rem(self.dp, self.n_group)
        self.core = self.index & 1
        self.place = self.index >> 1

    def swap(self, array, bits):
        return lax.ppermute(array, "dp", [(i, i ^ bits) for i in range(self.n_dp)])

    def shift(self, array, by):
        n = self.n_z
        return lax.ppermute(array, "tensor", [(i, (i + by) % n) for i in range(n)])

    def gather(self, piece):
        if self.n_dp == self.n_group:
            whole = lax.all_gather(piece, ("tensor", "dp"))
            return whole.reshape((self.n_z, self.n_group) + piece.shape)
        groups = [
            list(range(i, i + self.n_group)) for i in range(0, self.n_dp, self.n_group)
        ]
        line = lax.all_gather(piece, "tensor")
        return lax.all_gather(line, "dp", axis=1, axis_index_groups=groups)

    def turned(self, array):
        bit = 1
        while bit < self.n_group:
            lead = array.reshape((-1, 2, bit) + array.shape[1:])
            array = jnp.where((self.index & bit) != 0, lead[:, ::-1], lead).reshape(array.shape)
            bit *= 2
        return array

    def to_places(self, parts):
        return [self.swap(parts[number], 2 * number) for number in range(1, self.n_places)]

    def from_places(self, own, arrived):
        found = jnp.stack([own] + arrived)
        bit = 1
        while bit < self.n_places:
            lead = found.reshape((-1, 2, bit) + own.shape)
            flipped = lead[:, ::-1]
            found = jnp.where((self.place & bit) != 0, flipped, lead).reshape(found.shape)
            bit *= 2
        return found

    def by_core(self, own, other):
        return jnp.where(
            self.core == 1, jnp.stack([other, own]), jnp.stack([own, other])
        )

    def over_groups(self, array):
        bit = self.n_group
        while bit < self.n_dp:
            array = add(array, self.swap(array, bit))
            bit *= 2
        return array


def on_device(
    n_dp,
    n_z,
    tokens,
    lengths,
    key_mask,
    query_weight,
    query_bias,
    key_weight,
    value_weight,
    value_bias,
    output_weight,
    output_bias,
    first_gain,
    first_shift,
    inner_weight,
    inner_bias,
    outer_weight,
    outer_bias,
    second_gain,
    second_shift,
    cotangent,
):
    width = tokens.shape[1]
    mine = query_weight.shape[1]
    units = inner_weight.shape[1]
    all_rows = tokens.shape[0]
    all_blocks = all_rows // BUCKET
    rows = all_rows // n_z
    plane = Plane(n_dp, n_z)
    z, core, place, index = plane.z, plane.core, plane.place, plane.index
    n_places = plane.n_places
    others = range(1, n_z)

    feed_rows = units // plane.n_group
    head_rows = mine // plane.n_group
    mixer_t = jnp.pad(output_weight.T, ((0, 0), (0, -mine % 128)))
    mixer_count = width // plane.n_group
    piece = jnp.concatenate(
        [
            lax.dynamic_slice_in_dim(inner_weight, index * feed_rows, feed_rows, 1).T,
            lax.dynamic_slice_in_dim(outer_weight, index * feed_rows, feed_rows, 0),
            lax.dynamic_slice_in_dim(mixer_t, index * feed_rows, feed_rows, 0),
        ],
        axis=1,
    )
    line = [plane.shift(piece, s) for s in others]

    query_t, key_t, value_t = query_weight.T, key_weight.T, value_weight.T
    attention_own = jnp.concatenate([query_t, key_t, value_t, output_weight], axis=1)
    attention_weights = plane.gather(
        lax.dynamic_slice_in_dim(attention_own, index * head_rows, head_rows, 0)
    ).reshape(width, 4 * width)

    key_mask_rows = key_mask.reshape(all_blocks, 1, BUCKET)
    bias_row = jnp.concatenate([query_bias, value_bias, inner_bias])
    bias_rows = jnp.pad(bias_row, (0, 16 * BUCKET - bias_row.shape[0])).reshape(16, BUCKET)
    mixed = attend_forward(
        n_z, lengths, tokens, query_t, key_t, value_t, bias_rows, key_mask_rows
    )
    _, line = together(mixed, line)
    mixed = lax.all_to_all(mixed, "tensor", 0, 0)

    near = jnp.stack([part[:, : 2 * width] for part in line])
    by_x, by_y = plane.swap(near, 2), plane.swap(near, 4)

    mixer_keep = [jnp.stack([part[:, 2 * width :] for part in line])]
    mixer_keep += plane.to_places(mixer_keep * n_places)
    mixer_send = [plane.swap(part, 1) for part in mixer_keep]
    own_units = jnp.concatenate([inner_weight.T, outer_weight], axis=1)

    biases = mixed[:, 0, mine:].reshape(n_z, -1)[:, : bias_row.shape[0]].astype(f32)
    head_biases = jnp.pad(
        jnp.stack([biases[:, :mine].reshape(-1), biases[:, mine : 2 * mine].reshape(-1)]),
        ((0, 6), (0, 0)),
    )
    inner_biases = biases[:, 2 * mine :]
    inner_biases = jnp.concatenate(
        [
            lax.dynamic_slice_in_dim(inner_biases, lax.rem(z + n_z - s, n_z), 1, 0)
            for s in range(n_z)
        ],
        axis=0,
    )
    inner_biases = inner_biases.reshape(n_z, plane.n_group, feed_rows).transpose(1, 0, 2)
    inner_biases = plane.turned(inner_biases).reshape(n_places, 2, 1, n_z * feed_rows)
    inner_biases = inner_biases.transpose(1, 0, 2, 3).reshape(plane.n_group, 1, -1)
    vectors = jnp.stack(
        [output_bias, first_gain, first_shift, outer_bias, second_gain, second_shift]
        + [jnp.zeros_like(output_bias)] * 2
    ).astype(f32)

    place_z = z.reshape(1)
    info = jnp.stack([z, place, core])
    shared_args = (info, vectors, inner_biases, own_units)
    hidden, slope, normed_low, first_normed, first_scale, second_sum = feed_forward(
        ((0, 0),), *shared_args, [near], first=(tokens, mixed, mixer_t, mixer_keep + mixer_send)
    )
    second_sum, by_x, by_y = together(second_sum, by_x, by_y)
    cut = feed_rows // 2
    far = [plane.swap(by_x[:, :cut], 4), plane.swap(by_y[:, cut:], 2)]
    send = [plane.swap(units_of, 1) for units_of in (near, by_x, by_y)]
    hidden, slope, second_sum = feed_forward(
        ((0, 1), (0, 2), (1, 0), (1, 1), (1, 2)), *shared_args, [by_x, by_y] + send,
        going=(normed_low, second_sum, hidden, slope),
    )
    second_sum, far, attention_weights = together(second_sum, far, attention_weights)
    far_send = [plane.swap(half, 1) for half in far]
    keep = [near, by_x, by_y] + far
    send = send + far_send
    hidden, slope, my_output, grad_second, grad_outer, second_sums = feed_forward(
        ((0, 3), (1, 3)), *shared_args, far + far_send,
        going=(normed_low, second_sum, hidden, slope), last=(lengths, cotangent),
    )
    output = lax.all_gather(my_output, "tensor", axis=0, tiled=True)

    shared_args = (info, grad_outer, normed_low, hidden, slope, own_units)
    sent_early, sent_late, bias_sent, grad_normed = feed_back(*shared_args, grad_second, send)
    other = [plane.swap(sent_early, 1), plane.swap(sent_late, 1)]
    grad_normed, head_biases, tokens = together(grad_normed, head_biases, tokens)
    projected = project(place_z, tokens, attention_weights, head_biases, mixed.shape[1])
    projected, other = together(projected, other)
    (
        inner_stay, outer_stay, inner_go, outer_go, bias_kept, grad_first, grad_attended, first_sums
    ) = feed_back(
        *shared_args, grad_normed, keep, other,
        (first_normed, first_scale, vectors),
    )
    inner_came, outer_came = plane.swap(inner_go, 4), plane.swap(outer_go, 2)
    bias_grads = jnp.stack(
        [bias_kept[:, 0], bias_sent[:, 0]], axis=1
    )
    inner_bias_grad = plane.turned(bias_grads.reshape(plane.n_group, n_z, feed_rows))
    inner_bias_grad = inner_bias_grad.transpose(1, 0, 2)
    inner_bias_grad = jnp.concatenate(
        [
            sum(
                jnp.where(lax.rem(z - t + n_z, n_z) == s, inner_bias_grad[s : s + 1], 0.0)
                for s in range(n_z)
            )
            for t in range(n_z)
        ],
        axis=0,
    ).reshape(n_z, units)

    grads, my_tokens_grad, back_sums = attend_back(
        place_z, lengths, grad_attended, grad_first, attention_weights, *projected, key_mask_rows
    )
    grads, inner_came, outer_came, output = together(grads, inner_came, outer_came, output)
    inner_on, outer_on = (
        plane.swap(add(inner_stay[1], inner_came[1]), 2),
        plane.swap(add(outer_stay[1], outer_came[1]), 4),
    )
    tokens_grad = lax.all_gather(my_tokens_grad, "tensor", axis=0, tiled=True)

    def weight_grads(side, other=None, small=None):
        info = jnp.stack([2 * side, 2 * side + 1, z, place])
        return attention_grads(
            n_places, info, grads, mixed, tokens, grad_attended, other, small
        )

    (sent,) = weight_grads(1 - core)
    sent, back_sums, first_sums, second_sums, inner_bias_grad = together(
        sent, back_sums, first_sums, second_sums, inner_bias_grad
    )
    other = plane.swap(sent, 1)

    small = jnp.concatenate(
        [first_sums[:3], second_sums[:3], inner_bias_grad, jnp.sum(back_sums, axis=0)[:2]], axis=0
    )
    small = jnp.pad(small, ((0, -small.shape[0] % 16), (0, 0))).astype(bf16)
    small_rows = small.shape[0]

    small = add(small, plane.swap(small, 1))
    kept = list(weight_grads(core, other, small))
    arrived = plane.to_places(kept)
    kept[0], inner_on, outer_on = together(kept[0], inner_on, outer_on)
    feed_parts = jnp.concatenate(
        [
            add(inner_stay[0], inner_came[0], inner_on),
            add(outer_stay[0], outer_came[0], outer_on),
        ],
        axis=2,
    )
    feed_line = lax.all_to_all(feed_parts, "tensor", 0, 0)
    arrived, feed_line = together(arrived, feed_line)
    small = add(small, *[a[-small_rows:] for a in arrived])
    attention_parts = add(*[a[:-small_rows] for a in [kept[0]] + arrived])
    attention_parts = jnp.concatenate(
        [
            attention_parts.reshape(n_z, -1, width),
            jnp.broadcast_to(small, (n_z,) + small.shape),
        ],
        axis=1,
    )
    attention_line = lax.all_to_all(attention_parts, "tensor", 0, 0)
    feed_total = plane.over_groups(add(*[feed_line[t] for t in range(n_z)]))
    feed_arrived = plane.to_places([feed_total] * n_places)
    attention_line, feed_arrived, tokens_grad = together(
        attention_line, feed_arrived, tokens_grad
    )
    attention_total = plane.over_groups(add(*[attention_line[t] for t in range(n_z)]))
    small = attention_total[-small_rows:].astype(f32)
    attention_total = attention_total[:-small_rows]
    arrived = plane.to_places([attention_total] * n_places)
    feed_half = plane.from_places(feed_total, feed_arrived)
    feed_other = plane.swap(feed_half, 1)
    inner_grad, outer_grad = finish_feed(core.reshape(1), feed_half, feed_other)
    inner_bias_sum = lax.dynamic_slice_in_dim(small, 6 + z, 1, 0)[0]
    head_sums = lax.dynamic_slice_in_dim(small[6 + n_z : 8 + n_z], z * mine, mine, 1)
    arrived, inner_grad, outer_grad, small, inner_bias_sum, head_sums = together(
        arrived, inner_grad, outer_grad, small, inner_bias_sum, head_sums
    )
    attention_half = plane.from_places(attention_total, arrived)
    attention_other = plane.swap(attention_half, 1)
    grad_list = plane.by_core(attention_half, attention_other)
    grad_list = grad_list.reshape(2, n_places, 2, mine // n_places, width)
    grad_list = grad_list.transpose(0, 2, 1, 3, 4).reshape(4, mine, width)

    shared = small[:6]

    return (
        output,
        tokens_grad,
        grad_list[0].T.astype(f32),
        head_sums[0],
        grad_list[1].T.astype(f32),
        grad_list[2].T.astype(f32),
        head_sums[1],
        grad_list[3].astype(f32),
        shared[0],
        shared[1],
        shared[2],
        inner_grad,
        inner_bias_sum,
        outer_grad,
        shared[3],
        shared[4],
        shared[5],
    )


def solution(mesh):
    n_dp, n_z = mesh.shape["dp"], mesh.shape["tensor"]
    in_specs = (
        P("dp", None),
        P("dp", None),
        P("dp"),
        P(None, "tensor"),
        P("tensor"),
        P(None, "tensor"),
        P(None, "tensor"),
        P("tensor"),
        P("tensor", None),
        P(),
        P(),
        P(),
        P(None, "tensor"),
        P("tensor"),
        P("tensor", None),
        P(),
        P(),
        P(),
        P("dp", None),
    )
    out_specs = (
        P("dp", None),
        P("dp", None),
        P(None, "tensor"),
        P("tensor"),
        P(None, "tensor"),
        P(None, "tensor"),
        P("tensor"),
        P("tensor", None),
        P(),
        P(),
        P(),
        P(None, "tensor"),
        P("tensor"),
        P("tensor", None),
        P(),
        P(),
        P(),
    )

    def program(*args):
        return on_device(n_dp, n_z, *args)

    return jax.shard_map(
        program, mesh=mesh, in_specs=in_specs, out_specs=out_specs, check_vma=False
    )
```

```python
import functools

import jax
import jax.numpy as jnp
from jax import lax
from jax.experimental import pallas as pl
from jax.experimental.pallas import tpu as pltpu
from jax.sharding import PartitionSpec as P

HEAD = 64
BUCKET = 512
ITEMS = 8


negative_fill = -1e30
epsilon = 1e-06
f32 = jnp.float32
bf16 = jnp.bfloat16
VMEM_BYTES = 56 * 1024 * 1024


def dot(left, right):
    return jnp.dot(left, right, preferred_element_type=f32)


def contract_rows(left, right):
    return lax.dot_general(left, right, (((0,), (0,)), ((), ())), preferred_element_type=f32)


def contract_cols(left, right):
    return lax.dot_general(left, right, (((1,), (1,)), ((), ())), preferred_element_type=f32)


def norm_rows(values):
    centred = values - jnp.mean(values, axis=1, keepdims=True)
    inv_scale = lax.rsqrt(jnp.mean(centred * centred, axis=1, keepdims=True) + epsilon)
    return centred * inv_scale, inv_scale


def norm_back(grad_rows, norm_gain, normed, inv_scale):
    scaled = grad_rows * norm_gain
    return inv_scale * (
        scaled
        - jnp.mean(scaled, axis=1, keepdims=True)
        - normed * jnp.mean(scaled * normed, axis=1, keepdims=True)
    )


def column_sum(matrix):
    return jnp.sum(matrix.astype(f32), axis=0, keepdims=True)


def fixed(shape):
    return pl.BlockSpec(shape, lambda *_: (0,) * len(shape))


def cost(microseconds):
    return pl.CostEstimate(
        flops=int(microseconds * 2.5e8),
        bytes_accessed=int(microseconds * 2.5e5),
        transcendentals=0,
    )


def params(axes):
    return pltpu.CompilerParams(
        dimension_semantics=("arbitrary",) * axes, vmem_limit_bytes=VMEM_BYTES
    )


def item_places(lengths_ref, row, shape, axis):
    places = lax.broadcasted_iota(jnp.int32, shape, axis)
    end = jnp.int32(0)
    items = jnp.zeros(shape, jnp.int32)
    for slot in range(ITEMS):
        end = end + lengths_ref[row, slot]
        items = items + (places >= end).astype(jnp.int32)
    return items


def as_column(row):
    return jnp.broadcast_to(row.astype(f32), (8, row.shape[1])).T[:, :1]


def mask_bias(lengths_ref, row, key_mask):
    shape = (BUCKET, BUCKET)
    diagonal = lax.broadcasted_iota(jnp.int32, shape, 0) == lax.broadcasted_iota(
        jnp.int32, shape, 1
    )
    item_row = item_places(lengths_ref, row, (1, BUCKET), 1)
    item_column = item_places(lengths_ref, row, (BUCKET, 1), 0)
    code_column = jnp.where(as_column(key_mask) == 1.0, item_column, -1)
    return jnp.where((code_column == item_row) | diagonal, 0.0, negative_fill).astype(f32)


def attend_forward_kernel(
    place_ref, lengths_ref, tokens_ref, query_ref, key_ref, value_ref, biases_ref, key_mask_ref,
    *mixed_refs,
):
    mine = query_ref.shape[0]
    n_z, own = pl.num_programs(0), pl.num_programs(1)
    bucket = lax.rem(place_ref[0] + pl.program_id(0), n_z) * own + pl.program_id(1)
    parts = []
    rows = tokens_ref[...]
    queries = contract_cols(query_ref[...], rows) + as_column(biases_ref[0:1, :mine])
    queries = (queries.astype(bf16) * HEAD ** (-0.5)).astype(bf16)
    keys = contract_cols(rows, key_ref[...]).astype(bf16)
    values = contract_cols(value_ref[...], rows) + as_column(biases_ref[0:1, mine : 2 * mine])
    values = values.astype(bf16)
    bias = mask_bias(lengths_ref, bucket, key_mask_ref[0])
    for head in range(mine // HEAD):
        at = slice(head * HEAD, (head + 1) * HEAD)
        scores = dot(keys[:, at], queries[at]) + bias
        exponent = jnp.exp(scores - jnp.max(scores, axis=0, keepdims=True))
        total = jnp.sum(exponent, axis=0, keepdims=True)
        parts.append((dot(values[at], exponent.astype(bf16)) / total).astype(bf16))
    for s, mixed_ref in enumerate(mixed_refs):

        @pl.when(pl.program_id(0) == s)
        def _(mixed_ref=mixed_ref):
            for head, part in enumerate(parts):
                mixed_ref[0, head * HEAD : (head + 1) * HEAD] = part
            mixed_ref[0, mine:] = biases_ref[...]


def attend_forward(n_z, place, lengths, tokens, query, key, value, biases, key_mask):
    own = lengths.shape[0] // n_z
    mine, width = key.shape
    part = (own, mine + biases.shape[0], BUCKET)
    bucket = lambda s, b, place: lax.rem(place[0] + s, n_z) * own + b

    def out_spec(number):
        def at(s, b, place):
            return (jnp.where(s < number, 0, jnp.where(s > number, own - 1, b)), 0, 0)

        return pl.BlockSpec((1,) + part[1:], at)

    return pl.pallas_call(
        attend_forward_kernel,
        grid_spec=pltpu.PrefetchScalarGridSpec(
            num_scalar_prefetch=1,
            grid=(n_z, own),
            in_specs=[
                pl.BlockSpec(memory_space=pltpu.SMEM),
                pl.BlockSpec((BUCKET, width), lambda s, b, place: (bucket(s, b, place), 0)),
                fixed((mine, width)),
                fixed((mine, width)),
                fixed((mine, width)),
                fixed(biases.shape),
                pl.BlockSpec((1, 1, BUCKET), lambda s, b, place: (bucket(s, b, place), 0, 0)),
            ],
            out_specs=[out_spec(s) for s in range(n_z)],
        ),
        out_shape=[jax.ShapeDtypeStruct(part, bf16)] * n_z,
        compiler_params=params(2),
        name="attend_forward",
        cost_estimate=cost(12),
    )(place, lengths, tokens, query, key, value, biases, key_mask)


def fetch_units(step, picks, own_ref, halves, units, sems):
    feed_rows = units.shape[2]
    cut = feed_rows // 2

    def copies(number):
        slot = number % 2
        row = pl.multiple_of(picks[number] * feed_rows, 16)
        ends = [
            (own_ref.at[pl.ds(row, feed_rows)], units.at[slot, 0]),
            (halves[number][0], units.at[slot, 1:, :cut]),
            (halves[number][1], units.at[slot, 1:, cut:]),
        ]
        return [
            pltpu.make_async_copy(source, target, sems.at[slot, i])
            for i, (source, target) in enumerate(ends)
        ]

    for number in range(len(halves)):

        @pl.when(step == number)
        def _(number=number):
            if number == 0:
                for copy in copies(0):
                    copy.start()
            if number + 1 < len(halves):
                for copy in copies(number + 1):
                    copy.start()
            for copy in copies(number):
                copy.wait()

    return units.at[lax.rem(step, 2)]


def fetch_mixer(picks, own_ref, parts, mixer, sems):
    count = mixer.shape[1] // 8
    ends = [(own_ref, mixer.at[0])]
    for pick, part in zip(picks, parts):
        row = pl.multiple_of(pick * count, 16)
        ends.append((part, mixer.at[1:, pl.ds(row, count)]))
    copies = [
        pltpu.make_async_copy(source, target, sems.at[i])
        for i, (source, target) in enumerate(ends)
    ]
    for copy in copies:
        copy.start()
    for copy in copies:
        copy.wait()


def take_halves(numbers, refs):
    halves, refs = [], list(refs)
    for number in numbers:
        if number == 3:
            halves.append((refs.pop(0), refs.pop(0)))
        else:
            ref = refs.pop(0)
            cut = ref.shape[1] // 2
            halves.append((ref.at[:, :cut], ref.at[:, cut:]))
    return halves, refs


def split_units(units):
    width = units.shape[2] // 2
    return units[:, :, :width].reshape(-1, width), units[:, :, width:].reshape(-1, width)


ANYWHERE = pl.BlockSpec(memory_space=pl.ANY)


def feed_forward_kernel(n_z, chunks, first, last, info_ref, *rest):
    def take(count):
        nonlocal rest
        taken, rest = rest[:count], rest[count:]
        return taken

    vectors_ref, bias_ref, own_ref = take(3)
    halves, rest = take_halves([number for _, number in chunks], rest)
    if first:
        (tokens_ref,) = take(1)
        mixed_refs = take(n_z)
        mixer_own_ref, *mixer_parts = take(9)
    else:
        normed_low_ref, start_ref, _, _ = take(4)
    if last:
        lengths_ref, cotangent_ref = take(2)
    hidden_ref, slope_ref = take(2)
    if first:
        normed_low_ref, first_normed_ref, first_scale_ref = take(3)
    if last:
        output_ref, grad_second_ref, grad_outer_ref, sums_ref = take(4)
    else:
        (second_sum,) = take(1)
    units, sems = take(2)
    if first:
        mixer, mixer_sems = take(2)
    if last:
        (second_sum,) = take(1)

    step = pl.program_id(0)
    picks = [(info_ref[1] ^ number) * 2 + (info_ref[2] ^ side) for side, number in chunks]
    weights = fetch_units(step, picks, own_ref, halves, units, sems)
    output_bias, first_gain, first_shift, outer_bias, second_gain, second_shift = (
        vectors_ref[i : i + 1, :] for i in range(6)
    )

    @pl.when(step == 0)
    def _():
        if first:
            all_picks = [
                (info_ref[1] ^ number) * 2 + (info_ref[2] ^ side)
                for side in range(2)
                for number in range(4)
            ]
            fetch_mixer(all_picks, mixer_own_ref, mixer_parts, mixer, mixer_sems)
            own, mine, _ = mixed_refs[0].shape
            attended = output_bias + jnp.concatenate(
                [
                    sum(dot(mixer[s, :, :mine], mixed_refs[s][b]) for s in range(n_z)).T
                    for b in range(own)
                ],
                axis=0,
            )
            normed, inv_scale = norm_rows(tokens_ref[...].astype(f32) + attended)
            whole = normed * first_gain + first_shift
            first_normed_ref[...] = normed
            first_scale_ref[...] = inv_scale
            normed_low_ref[...] = whole.astype(bf16)
            second_sum[...] = whole + outer_bias
        else:
            second_sum[...] = start_ref[...]

    inner, outer = split_units(weights)
    inner_pre = contract_cols(normed_low_ref[...], inner) + bias_ref[0]
    normal_cdf = 0.5 + 0.5 * lax.erf(inner_pre * 0.7071067811865476)
    bell = jnp.exp(-0.5 * inner_pre * inner_pre)
    hidden = (inner_pre * normal_cdf).astype(bf16)
    hidden_ref[...] = hidden.T
    slope_ref[...] = (normal_cdf + inner_pre * bell * 0.3989422804014327).astype(bf16)
    second_sum[...] += dot(hidden, outer)

    if last:

        @pl.when(step == pl.num_programs(0) - 1)
        def _():
            normed, inv_scale = norm_rows(second_sum[...])
            blocks = normed.shape[0] // BUCKET
            live = jnp.concatenate(
                [
                    (item_places(lengths_ref, info_ref[0] * blocks + b, (BUCKET, 1), 0) < ITEMS)
                    for b in range(blocks)
                ],
                axis=0,
            ).astype(f32)
            output_ref[...] = ((normed * second_gain + second_shift) * live).astype(bf16)
            grad_final = cotangent_ref[...].astype(f32) * live
            grad_second = norm_back(grad_final, second_gain, normed, inv_scale)
            grad_outer = grad_second.astype(bf16)
            grad_second_ref[...] = grad_second
            grad_outer_ref[...] = grad_outer
            sums_ref[0:1, :] = column_sum(grad_outer)
            sums_ref[1:2, :] = column_sum(grad_final * normed)
            sums_ref[2:3, :] = column_sum(grad_final)


def feed_forward(chunks, info, vectors, biases, own, halves, first=None, going=None, last=None):
    width = vectors.shape[1]
    n_z = halves[0].shape[0] + 1
    feed_rows, twice = own.shape[0] // 8, 2 * width
    rows = first[1][0].shape[0] * BUCKET if first else going[0].shape[0]
    chunk = n_z * feed_rows
    whole = fixed((rows, width))
    my_rows = pl.BlockSpec((rows, width), lambda j, info: (info[0], 0))
    at = lambda j, info: info[3 + j]
    hidden_spec = pl.BlockSpec((chunk, rows), lambda j, info: (at(j, info), 0))
    slope_spec = pl.BlockSpec((rows, chunk), lambda j, info: (0, at(j, info)))
    in_specs = [
        fixed((8, width)),
        pl.BlockSpec((1, 1, chunk), lambda j, info: (at(j, info), 0, 0)),
        ANYWHERE,
    ] + [ANYWHERE] * len(halves)
    args = [vectors, biases, own] + halves
    shapes = [
        ((8 * chunk, rows), bf16, hidden_spec),
        ((rows, 8 * chunk), bf16, slope_spec),
    ]
    scratch = [
        pltpu.VMEM((2, n_z, feed_rows, twice), bf16),
        pltpu.SemaphoreType.DMA((2, 3)),
    ]
    aliases = {}
    if first:
        tokens, mixed, mixer_own, mixer_parts = first
        mine = width // n_z
        in_specs += [my_rows] + [fixed((mixed[0].shape[0], mine, BUCKET))] * n_z + [ANYWHERE] * 9
        args += [tokens] + mixed + [mixer_own] + mixer_parts
        shapes += [
            ((rows, width), bf16, whole),
            ((rows, width), f32, whole),
            ((rows, 1), f32, fixed((rows, 1))),
        ]
        scratch += [
            pltpu.VMEM((n_z,) + mixer_own.shape, bf16),
            pltpu.SemaphoreType.DMA((9,)),
        ]
    else:
        aliases = {1 + len(args) + 2: 0, 1 + len(args) + 3: 1}
        in_specs += [whole, whole, ANYWHERE, ANYWHERE]
        args += list(going)
    if last:
        in_specs += [pl.BlockSpec(memory_space=pltpu.SMEM), my_rows]
        args += list(last)
        shapes += [
            ((rows, width), bf16, whole),
            ((rows, width), f32, whole),
            ((rows, width), bf16, whole),
            ((8, width), f32, fixed((8, width))),
        ]
        scratch.append(pltpu.VMEM((rows, width), f32))
    else:
        shapes.append(((rows, width), f32, whole))
    info = jnp.concatenate(
        [info, jnp.array([4 * side + number for side, number in chunks], jnp.int32)]
    )
    return pl.pallas_call(
        functools.partial(feed_forward_kernel, n_z, chunks, first is not None, last is not None),
        grid_spec=pltpu.PrefetchScalarGridSpec(
            num_scalar_prefetch=1,
            grid=(len(chunks),),
            in_specs=in_specs,
            out_specs=[spec for _, _, spec in shapes],
            scratch_shapes=scratch,
        ),
        out_shape=[jax.ShapeDtypeStruct(shape, kind) for shape, kind, _ in shapes],
        input_output_aliases=aliases,
        compiler_params=params(1),
        name="feed_forward",
        cost_estimate=cost(3 * len(chunks)),
    )(info, *args)


STAY = ((0, 1), (0, 2))
GO = ((2, 3), (1, 3))


def feed_back_kernel(
    keeps, info_ref, grad_outer_ref, normed_low_ref, hidden_ref, slope_ref,
    own_ref, start_ref, *rest,
):
    halves, rest = take_halves(range(4), rest)
    if keeps:
        other_refs, norm_refs, rest = rest[:2], rest[2:5], rest[5:]
        stay_refs, go_refs, rest = rest[0:2], rest[2:4], rest[4:]
        bias_grad_ref, grad_first_ref, grad_attended_ref, sums_ref, units, sems = rest[:6]
        grad_normed_ref = rest[6]
    else:
        *grad_refs, bias_grad_ref, grad_normed_ref, units, sems = rest
    step = pl.program_id(0)
    side = info_ref[2] if keeps else 1 - info_ref[2]
    picks = [(info_ref[1] ^ number) * 2 + side for number in range(4)]
    weights = fetch_units(step, picks, own_ref, halves, units, sems)

    @pl.when(step == 0)
    def _():
        grad_normed_ref[...] = start_ref[...]

    n_z, feed_rows, twice = weights.shape
    width = twice // 2
    inner, outer = split_units(weights)
    grad_outer = grad_outer_ref[...]
    grad_hidden = contract_cols(grad_outer, outer)
    grad_inner = (grad_hidden * slope_ref[...].astype(f32)).astype(bf16)
    outer_grad = dot(hidden_ref[...], grad_outer).reshape(n_z, feed_rows, width)
    inner_grad = contract_rows(grad_inner, normed_low_ref[...]).reshape(n_z, feed_rows, width)
    bias_grad_ref[0] = column_sum(grad_inner)
    grad_normed_ref[...] += dot(grad_inner, inner)

    for number in range(4):

        @pl.when(step == number)
        def _(number=number):
            for track, value in enumerate((inner_grad, outer_grad)):
                at = slice(track * width, (track + 1) * width)
                if keeps:
                    found = value + other_refs[number // 2][0, :, :, at].astype(f32)
                    ref = stay_refs[track] if number in STAY[track] else go_refs[track]
                    ref[0] = found.astype(bf16)
                else:
                    grad_refs[number // 2][0, :, :, at] = value.astype(bf16)

    if keeps:

        @pl.when(step == pl.num_programs(0) - 1)
        def _():
            first_normed_ref, first_scale_ref, vectors_ref = norm_refs
            grad_rows, normed = grad_normed_ref[...], first_normed_ref[...]
            grad_first = norm_back(grad_rows, vectors_ref[1:2, :], normed, first_scale_ref[...])
            grad_attended = grad_first.astype(bf16)
            grad_first_ref[...] = grad_first
            grad_attended_ref[...] = grad_attended
            sums_ref[0:1, :] = column_sum(grad_attended)
            sums_ref[1:2, :] = column_sum(grad_rows * normed)
            sums_ref[2:3, :] = column_sum(grad_rows)


def feed_back(
    info, grad_outer, normed_low, hidden, slope, own, start, units, others=None, norm=None
):
    rows, width = grad_outer.shape
    keeps = others is not None
    count = 4
    feed_rows, twice = own.shape[0] // 8, 2 * width
    n_z = units[0].shape[0] + 1
    chunk = n_z * feed_rows
    flip = 0 if keeps else 1
    columns = pl.BlockSpec((rows, chunk), lambda i, info: (0, 4 * flip + i))
    whole = fixed((rows, width))
    part = (n_z, feed_rows, twice)
    track = (2, n_z, feed_rows, width)
    unit_rows = pl.BlockSpec((chunk, rows), lambda i, info: (4 * flip + i, 0))
    in_specs = [whole, whole, unit_rows, columns, ANYWHERE, whole] + [ANYWHERE] * len(units)
    args = [grad_outer, normed_low, hidden, slope, own, start] + units
    bias_shape = (
        (count, 1, chunk),
        f32,
        pl.BlockSpec((1, 1, chunk), lambda i, info: (i, 0, 0)),
    )
    scratch = [pltpu.VMEM((2,) + part, bf16), pltpu.SemaphoreType.DMA((2, 3))]

    def one(shape, at):
        return pl.BlockSpec((1,) + shape[1:], lambda i, info: (at(i), 0, 0, 0))

    early, late = (lambda i: jnp.minimum(i, 1)), (lambda i: jnp.maximum(i - 2, 0))
    pair = (2,) + part
    if keeps:
        in_specs += [one(pair, early), one(pair, late)]
        in_specs += [whole, fixed((rows, 1)), fixed((8, width))]
        args += list(others) + list(norm)
        slow, slower = (lambda i: i // 2), (lambda i: jnp.maximum(i - 1, 0) // 2)
        shapes = [(track, bf16, one(track, at)) for at in (early, slow, late, slower)] + [
            bias_shape,
            ((rows, width), f32, whole),
            ((rows, width), bf16, whole),
            ((8, width), f32, fixed((8, width))),
        ]
        scratch.append(pltpu.VMEM((rows, width), f32))
    else:
        shapes = [
            (pair, bf16, one(pair, early)),
            (pair, bf16, one(pair, late)),
            bias_shape,
            ((rows, width), f32, whole),
        ]
    return pl.pallas_call(
        functools.partial(feed_back_kernel, keeps),
        grid_spec=pltpu.PrefetchScalarGridSpec(
            num_scalar_prefetch=1,
            grid=(count,),
            in_specs=in_specs,
            out_specs=[spec for _, _, spec in shapes],
            scratch_shapes=scratch,
        ),
        out_shape=[jax.ShapeDtypeStruct(shape, kind) for shape, kind, _ in shapes],
        compiler_params=params(1),
        name="feed_back_own" if keeps else "feed_back",
        cost_estimate=cost(3 * count),
    )(info, *args)


def finish_feed_kernel(core_ref, own_ref, other_ref, inner_ref, outer_ref, inner_rows):
    places, count, twice = own_ref.shape
    width = twice // 2
    for source, side in ((own_ref, core_ref[0]), (other_ref, 1 - core_ref[0])):
        for place in range(places):
            row = pl.multiple_of((2 * place + side) * count, 16)
            inner_rows[pl.ds(row, count), :] = source[place, :, :width].astype(f32)
            outer_ref[pl.ds(row, count), :] = source[place, :, width:].astype(f32)
    inner_ref[...] = inner_rows[...].T


def finish_feed(core, own, other):
    places, count, twice = own.shape
    shape = (2 * places * count, twice // 2)
    inner_shape = (shape[1], shape[0])
    return pl.pallas_call(
        finish_feed_kernel,
        grid_spec=pltpu.PrefetchScalarGridSpec(
            num_scalar_prefetch=1,
            grid=(1,),
            in_specs=[fixed(own.shape), fixed(other.shape)],
            out_specs=[fixed(inner_shape), fixed(shape)],
            scratch_shapes=[pltpu.VMEM(shape, f32)],
        ),
        out_shape=[
            jax.ShapeDtypeStruct(inner_shape, f32),
            jax.ShapeDtypeStruct(shape, f32),
        ],
        compiler_params=params(1),
        name="finish_feed",
        cost_estimate=cost(5),
    )(core, own, other)


def copy_kernel(from_ref, to_ref):
    to_ref[...] = from_ref[...]


def copied(array):
    block = pl.BlockSpec((BUCKET, array.shape[1]), lambda i: (i, 0))
    return pl.pallas_call(
        copy_kernel,
        grid=(array.shape[0] // BUCKET,),
        in_specs=[block],
        out_specs=block,
        out_shape=jax.ShapeDtypeStruct(array.shape, array.dtype),
        compiler_params=params(1),
        name="copied",
        cost_estimate=cost(4),
    )(array)


def project_kernel(place_ref, tokens_ref, weights_ref, biases_ref, query_ref, key_ref, value_ref):
    rows = tokens_ref[...]
    width = rows.shape[1]
    queries = contract_cols(weights_ref[:, :width], rows) + as_column(biases_ref[0:1, :])
    query_ref[...] = (queries.astype(bf16) * HEAD ** (-0.5)).astype(bf16)
    key_ref[...] = contract_cols(rows, weights_ref[:, width : 2 * width]).astype(bf16)
    values = contract_cols(rows, weights_ref[:, 2 * width :]) + biases_ref[1:2, :]
    value_ref[...] = values.astype(bf16)


def project(place, tokens, weights, biases, buckets):
    width = tokens.shape[1]
    part = width // 3
    shapes = [
        ((buckets, width, BUCKET), pl.BlockSpec((None, part, BUCKET), lambda b, j, _: (b, j, 0))),
        ((buckets * BUCKET, width), pl.BlockSpec((BUCKET, part), lambda b, j, _: (b, j))),
        ((buckets * BUCKET, width), pl.BlockSpec((BUCKET, part), lambda b, j, _: (b, j))),
    ]
    return pl.pallas_call(
        project_kernel,
        grid_spec=pltpu.PrefetchScalarGridSpec(
            num_scalar_prefetch=1,
            grid=(buckets, 3),
            in_specs=[
                pl.BlockSpec((BUCKET, width), lambda b, j, place: (place[0] * buckets + b, 0)),
                pl.BlockSpec((part, 3 * width), lambda b, j, place: (j, 0)),
                pl.BlockSpec((8, part), lambda b, j, place: (0, j)),
            ],
            out_specs=[spec for _, spec in shapes],
        ),
        out_shape=[jax.ShapeDtypeStruct(shape, bf16) for shape, _ in shapes],
        compiler_params=params(2),
        name="project",
        cost_estimate=cost(5),
    )(place, tokens, weights, biases)


def attend_back_kernel(
    place_ref, lengths_ref, grad_attended_ref, grad_first_ref, weights_ref, query_ref, key_ref,
    value_ref, key_mask_ref,
    grads_ref, tokens_grad_ref, sums_ref,
    bias, grad_mixed_t, whole, weights, sem,
):
    pair = pl.program_id(1)
    pairs, width = whole.shape[1], weights.shape[0]
    fetch = pltpu.make_async_copy(weights_ref, weights, sem)

    @pl.when(pair == 0)
    def _():
        fetch.start()
        row = place_ref[0] * pl.num_programs(0) + pl.program_id(0)
        bias[...] = mask_bias(lengths_ref, row, key_mask_ref[0])
        fetch.wait()
        grad_mixed_t[...] = contract_cols(
            weights[:, 3 * width :], grad_attended_ref[...]
        ).astype(bf16)

    queries, keys, values = query_ref[...], key_ref[...], value_ref[...]
    start = pl.multiple_of(pair * keys.shape[1], 128)
    grad_mixed = grad_mixed_t[pl.ds(start, keys.shape[1]), :]
    keys_t = keys.T
    grad_queries, grad_keys, grad_values = [], [], []
    for head in range(keys.shape[1] // HEAD):
        at = slice(head * HEAD, (head + 1) * HEAD)
        scores = dot(keys[:, at], queries[at]) + bias[...]
        exponent = jnp.exp(scores - jnp.max(scores, axis=0, keepdims=True))
        probs = exponent * (1.0 / jnp.sum(exponent, axis=0, keepdims=True))
        grad_probs = dot(values[:, at], grad_mixed[at])
        shift = jnp.sum(probs * grad_probs, axis=0, keepdims=True)
        grad_scores = (probs * (grad_probs - shift)).astype(bf16)
        grad_values.append(contract_cols(probs.astype(bf16), grad_mixed[at]))
        grad_keys.append(contract_cols(grad_scores, queries[at]))
        grad_queries.append(dot(keys_t[at], grad_scores) * HEAD ** (-0.5))
    query_t = jnp.concatenate(grad_queries, axis=0).astype(bf16)
    found = (
        query_t.T,
        jnp.concatenate(grad_keys, axis=1).astype(bf16),
        jnp.concatenate(grad_values, axis=1).astype(bf16),
    )
    for number, grad in enumerate(found):
        grads_ref[number, 0] = query_t if number == 0 else grad.T
        whole[number, pair] = grad
    sums_ref[0, 0:1, :] = column_sum(found[0])
    sums_ref[0, 1:2, :] = column_sum(found[2])

    @pl.when(pair == pl.num_programs(1) - 1)
    def _():
        total = grad_first_ref[...]
        for number in range(3):
            grad = jnp.concatenate([whole[number, i] for i in range(pairs)], axis=1)
            total += dot(grad, weights[:, number * width : (number + 1) * width])
        tokens_grad_ref[...] = total.astype(bf16)


def attend_back(place, lengths, grad_attended, grad_first, weights, queries, keys, values, key_mask):
    rows, width = grad_attended.shape
    blocks = rows // BUCKET
    pair = 2 * HEAD
    by_bucket = pl.BlockSpec((BUCKET, width), lambda b, h, place: (b, 0))
    by_pair = pl.BlockSpec((BUCKET, pair), lambda b, h, place: (b, h))
    return pl.pallas_call(
        attend_back_kernel,
        grid_spec=pltpu.PrefetchScalarGridSpec(
            num_scalar_prefetch=1,
            grid=(blocks, width // pair),
            in_specs=[
                pl.BlockSpec(memory_space=pltpu.SMEM),
                by_bucket,
                by_bucket,
                ANYWHERE,
                pl.BlockSpec((None, pair, BUCKET), lambda b, h, place: (b, h, 0)),
                by_pair,
                by_pair,
                pl.BlockSpec((1, 1, BUCKET), lambda b, h, place: (place[0] * blocks + b, 0, 0)),
            ],
            out_specs=[
                pl.BlockSpec((3, 1, pair, BUCKET), lambda b, h, place: (0, b, h, 0)),
                by_bucket,
                pl.BlockSpec((1, 8, pair), lambda b, h, place: (b, 0, h)),
            ],
            scratch_shapes=[
                pltpu.VMEM((BUCKET, BUCKET), f32),
                pltpu.VMEM((width, BUCKET), bf16),
                pltpu.VMEM((3, width // pair, BUCKET, pair), bf16),
                pltpu.VMEM(weights.shape, bf16),
                pltpu.SemaphoreType.DMA(()),
            ],
        ),
        out_shape=[
            jax.ShapeDtypeStruct((3, blocks, width, BUCKET), bf16),
            jax.ShapeDtypeStruct((rows, width), bf16),
            jax.ShapeDtypeStruct((blocks, 8, width), f32),
        ],
        compiler_params=params(2),
        name="attend_back",
        cost_estimate=cost(20),
    )(place, lengths, grad_attended, grad_first, weights, queries, keys, values, key_mask)


def attention_grads_kernel(
    n_z, n_places, adds, info_ref, grads_ref, tokens_ref, grad_attended_ref, *rest
):
    mixed_refs, rest = rest[:n_z], rest[n_z:]
    if adds:
        other_ref, small_ref = rest[:2]
        out_refs, whole = rest[2:-1], rest[-1]
    else:
        (out_ref, whole) = rest
    step = pl.program_id(0)
    which = info_ref[step]
    buckets, mine, _ = mixed_refs[0].shape
    count = mine // n_places

    @pl.when(which < 3)
    def _():
        whole[...] = sum(
            dot(grads_ref[0, b], tokens_ref[b * BUCKET : (b + 1) * BUCKET, :])
            for b in range(buckets)
        ).astype(bf16)

    @pl.when(which == 3)
    def _():
        for s in range(n_z):
            row = lax.rem(info_ref[2] + n_z - s, n_z) * mine
            whole[pl.ds(pl.multiple_of(row, 16), mine), :] = sum(
                dot(mixed_refs[s][b], grad_attended_ref[b * BUCKET : (b + 1) * BUCKET, :])
                for b in range(buckets)
            ).astype(bf16)

    for number in range(n_places):
        for s in range(n_z):
            start = lax.rem(info_ref[2] + s, n_z) * mine + (info_ref[3] ^ number) * count
            value = whole[pl.ds(pl.multiple_of(start, 16), count), :]
            if adds:
                value = value.astype(f32) + other_ref[number, s, 0].astype(f32)
                row = (2 * s + step) * count
                out_refs[number][pl.ds(pl.multiple_of(row, 16), count), :] = value.astype(bf16)
            else:
                out_ref[number, s, 0] = value

    if adds:
        for number in range(n_places):
            out_refs[number][2 * n_z * count :, :] = small_ref[...]


def attention_grads(n_places, info, grads, mixed, tokens, grad_attended, other=None, small=None):
    rows, width = grad_attended.shape
    n_z, buckets = len(mixed), mixed[0].shape[0]
    mine = width // n_z
    count = mine // n_places
    parts = (n_places, n_z, 1, count, width)
    by_step = pl.BlockSpec(parts, lambda i, info: (0, 0, i, 0, 0))
    in_specs = [
        pl.BlockSpec(
            (1, buckets, width, BUCKET), lambda i, info: (jnp.minimum(info[i], 2), 0, 0, 0)
        ),
        pl.BlockSpec((rows, width), lambda i, info: (info[2], 0)),
        fixed((rows, width)),
    ] + [fixed((buckets, mine, BUCKET))] * n_z
    args = [grads, tokens, grad_attended] + mixed
    if other is None:
        shapes = [((n_places, n_z, 2, count, width), by_step)]
    else:
        in_specs += [by_step, fixed(small.shape)]
        args += [other, small]
        flat = (2 * n_z * count + small.shape[0], width)
        shapes = [(flat, fixed(flat))] * n_places
    return pl.pallas_call(
        functools.partial(attention_grads_kernel, n_z, n_places, other is not None),
        grid_spec=pltpu.PrefetchScalarGridSpec(
            num_scalar_prefetch=1,
            grid=(2,),
            in_specs=in_specs,
            out_specs=[spec for _, spec in shapes],
            scratch_shapes=[pltpu.VMEM((width, width), bf16)],
        ),
        out_shape=[jax.ShapeDtypeStruct(shape, bf16) for shape, _ in shapes],
        compiler_params=params(1),
        name="attention_grads",
        cost_estimate=cost(6),
    )(info, *args)


def together(*values):
    return lax.optimization_barrier(values)


def add(first, *others):
    total = first.astype(f32)
    for other in others:
        total = total + other.astype(f32)
    return total.astype(bf16)


class Plane:
    def __init__(self, n_dp, n_z):
        self.n_dp, self.n_z = n_dp, n_z
        self.n_group = min(n_dp, 8)
        self.n_places = self.n_group // 2
        self.dp = lax.axis_index("dp")
        self.z = lax.axis_index("tensor")
        self.index = lax.rem(self.dp, self.n_group)
        self.core = self.index & 1
        self.place = self.index >> 1

    def swap(self, array, bits):
        return lax.ppermute(array, "dp", [(i, i ^ bits) for i in range(self.n_dp)])

    def shift(self, array, by):
        n = self.n_z
        return lax.ppermute(array, "tensor", [(i, (i + by) % n) for i in range(n)])

    def gather(self, piece):
        if self.n_dp == self.n_group:
            whole = lax.all_gather(piece, ("tensor", "dp"))
            return whole.reshape((self.n_z, self.n_group) + piece.shape)
        groups = [
            list(range(i, i + self.n_group)) for i in range(0, self.n_dp, self.n_group)
        ]
        line = lax.all_gather(piece, "tensor")
        return lax.all_gather(line, "dp", axis=1, axis_index_groups=groups)

    def turned(self, array):
        bit = 1
        while bit < self.n_group:
            lead = array.reshape((-1, 2, bit) + array.shape[1:])
            array = jnp.where((self.index & bit) != 0, lead[:, ::-1], lead).reshape(array.shape)
            bit *= 2
        return array

    def to_places(self, parts):
        return [self.swap(parts[number], 2 * number) for number in range(1, self.n_places)]

    def from_places(self, own, arrived):
        found = jnp.stack([own] + arrived)
        bit = 1
        while bit < self.n_places:
            lead = found.reshape((-1, 2, bit) + own.shape)
            flipped = lead[:, ::-1]
            found = jnp.where((self.place & bit) != 0, flipped, lead).reshape(found.shape)
            bit *= 2
        return found

    def by_core(self, own, other):
        return jnp.where(
            self.core == 1, jnp.stack([other, own]), jnp.stack([own, other])
        )

    def over_groups(self, array):
        bit = self.n_group
        while bit < self.n_dp:
            array = add(array, self.swap(array, bit))
            bit *= 2
        return array


def on_device(
    n_dp,
    n_z,
    tokens,
    lengths,
    key_mask,
    query_weight,
    query_bias,
    key_weight,
    value_weight,
    value_bias,
    output_weight,
    output_bias,
    first_gain,
    first_shift,
    inner_weight,
    inner_bias,
    outer_weight,
    outer_bias,
    second_gain,
    second_shift,
    cotangent,
):
    width = tokens.shape[1]
    mine = query_weight.shape[1]
    units = inner_weight.shape[1]
    all_rows = tokens.shape[0]
    all_blocks = all_rows // BUCKET
    rows = all_rows // n_z
    plane = Plane(n_dp, n_z)
    z, core, place, index = plane.z, plane.core, plane.place, plane.index
    n_places = plane.n_places
    others = range(1, n_z)

    feed_rows = units // plane.n_group
    head_rows = mine // plane.n_group
    mixer_t = jnp.pad(output_weight.T, ((0, 0), (0, -mine % 128)))
    mixer_count = width // plane.n_group
    piece = jnp.concatenate(
        [
            lax.dynamic_slice_in_dim(inner_weight, index * feed_rows, feed_rows, 1).T,
            lax.dynamic_slice_in_dim(outer_weight, index * feed_rows, feed_rows, 0),
            lax.dynamic_slice_in_dim(mixer_t, index * feed_rows, feed_rows, 0),
        ],
        axis=1,
    )
    line = [plane.shift(piece, s) for s in others]

    query_t, key_t, value_t = query_weight.T, key_weight.T, value_weight.T
    attention_own = jnp.concatenate([query_t, key_t, value_t, output_weight], axis=1)
    attention_weights = plane.gather(
        lax.dynamic_slice_in_dim(attention_own, index * head_rows, head_rows, 0)
    ).reshape(width, 4 * width)

    key_mask_rows = key_mask.reshape(all_blocks, 1, BUCKET)
    bias_row = jnp.concatenate([query_bias, value_bias, inner_bias])
    bias_rows = jnp.pad(bias_row, (0, 16 * BUCKET - bias_row.shape[0])).reshape(16, BUCKET)
    place_z = z.reshape(1)
    mixed = attend_forward(
        n_z, place_z, lengths, tokens, query_t, key_t, value_t, bias_rows, key_mask_rows
    )
    mixed, line = together(mixed, line)
    mixed = [mixed[0]] + [plane.shift(mixed[s], s) for s in others]

    near = jnp.stack([part[:, : 2 * width] for part in line])
    by_x, by_y = plane.swap(near, 2), plane.swap(near, 4)

    mixer_keep = [jnp.stack([part[:, 2 * width :] for part in line])]
    mixer_keep += plane.to_places(mixer_keep * n_places)
    mixer_send = [plane.swap(part, 1) for part in mixer_keep]
    own_units = jnp.concatenate([inner_weight.T, outer_weight], axis=1)

    biases = jnp.stack([part[0, mine:].reshape(-1)[: bias_row.shape[0]] for part in mixed])
    biases = biases.astype(f32)
    inner_biases = biases[:, 2 * mine :]
    biases = jnp.concatenate(
        [
            lax.dynamic_slice_in_dim(biases[:, : 2 * mine], lax.rem(z + n_z - t, n_z), 1, 0)
            for t in range(n_z)
        ],
        axis=0,
    )
    head_biases = jnp.pad(
        jnp.stack([biases[:, :mine].reshape(-1), biases[:, mine:].reshape(-1)]), ((0, 6), (0, 0))
    )
    inner_biases = inner_biases.reshape(n_z, plane.n_group, feed_rows).transpose(1, 0, 2)
    inner_biases = plane.turned(inner_biases).reshape(n_places, 2, 1, n_z * feed_rows)
    inner_biases = inner_biases.transpose(1, 0, 2, 3).reshape(plane.n_group, 1, -1)
    vectors = jnp.stack(
        [output_bias, first_gain, first_shift, outer_bias, second_gain, second_shift]
        + [jnp.zeros_like(output_bias)] * 2
    ).astype(f32)

    info = jnp.stack([z, place, core])
    shared_args = (info, vectors, inner_biases, own_units)
    hidden, slope, normed_low, first_normed, first_scale, second_sum = feed_forward(
        ((0, 0),), *shared_args, [near], first=(tokens, mixed, mixer_t, mixer_keep + mixer_send)
    )
    second_sum, by_x, by_y = together(second_sum, by_x, by_y)
    cut = feed_rows // 2
    far = [plane.swap(by_x[:, :cut], 4), plane.swap(by_y[:, cut:], 2)]
    send = [plane.swap(units_of, 1) for units_of in (near, by_x, by_y)]
    hidden, slope, second_sum = feed_forward(
        ((0, 1), (0, 2), (1, 0), (1, 1), (1, 2)), *shared_args, [by_x, by_y] + send,
        going=(normed_low, second_sum, hidden, slope),
    )
    second_sum, far, attention_weights = together(second_sum, far, attention_weights)
    far_send = [plane.swap(half, 1) for half in far]
    keep = [near, by_x, by_y] + far
    send = send + far_send
    hidden, slope, my_output, grad_second, grad_outer, second_sums = feed_forward(
        ((0, 3), (1, 3)), *shared_args, far + far_send,
        going=(normed_low, second_sum, hidden, slope), last=(lengths, cotangent),
    )
    output = lax.all_gather(my_output, "tensor", axis=0, tiled=True)

    shared_args = (info, grad_outer, normed_low, hidden, slope, own_units)
    sent_early, sent_late, bias_sent, grad_normed = feed_back(*shared_args, grad_second, send)
    other = [plane.swap(sent_early, 1), plane.swap(sent_late, 1)]
    grad_normed, head_biases, tokens = together(grad_normed, head_biases, tokens)
    projected = project(place_z, tokens, attention_weights, head_biases, rows // BUCKET)
    projected, other = together(projected, other)
    (
        inner_stay, outer_stay, inner_go, outer_go, bias_kept, grad_first, grad_attended, first_sums
    ) = feed_back(
        *shared_args, grad_normed, keep, other,
        (first_normed, first_scale, vectors),
    )
    inner_came, outer_came = plane.swap(inner_go, 4), plane.swap(outer_go, 2)
    bias_grads = jnp.stack(
        [bias_kept[:, 0], bias_sent[:, 0]], axis=1
    )
    inner_bias_grad = plane.turned(bias_grads.reshape(plane.n_group, n_z, feed_rows))
    inner_bias_grad = inner_bias_grad.transpose(1, 0, 2)
    inner_bias_grad = jnp.concatenate(
        [
            sum(
                jnp.where(lax.rem(z - t + n_z, n_z) == s, inner_bias_grad[s : s + 1], 0.0)
                for s in range(n_z)
            )
            for t in range(n_z)
        ],
        axis=0,
    ).reshape(n_z, units)

    grads, my_tokens_grad, back_sums = attend_back(
        place_z, lengths, grad_attended, grad_first, attention_weights, *projected, key_mask_rows
    )
    grads, inner_came, outer_came, output = together(grads, inner_came, outer_came, output)
    inner_on, outer_on = (
        plane.swap(add(inner_stay[1], inner_came[1]), 2),
        plane.swap(add(outer_stay[1], outer_came[1]), 4),
    )
    tokens_grad = lax.all_gather(my_tokens_grad, "tensor", axis=0, tiled=True)

    def weight_grads(side, other=None, small=None):
        info = jnp.stack([2 * side, 2 * side + 1, z, place])
        return attention_grads(
            n_places, info, grads, mixed, tokens, grad_attended, other, small
        )

    (sent,) = weight_grads(1 - core)
    sent, back_sums, first_sums, second_sums, inner_bias_grad = together(
        sent, back_sums, first_sums, second_sums, inner_bias_grad
    )
    other = plane.swap(sent, 1)

    small = jnp.concatenate(
        [first_sums[:3], second_sums[:3], inner_bias_grad, jnp.sum(back_sums, axis=0)[:2]], axis=0
    )
    small = jnp.pad(small, ((0, -small.shape[0] % 16), (0, 0))).astype(bf16)
    small_rows = small.shape[0]

    small = add(small, plane.swap(small, 1))
    kept = list(weight_grads(core, other, small))
    arrived = plane.to_places(kept)
    arrived[0], inner_on, outer_on = together(arrived[0], inner_on, outer_on)
    feed_parts = [
        jnp.concatenate(
            [
                add(inner_stay[0, s], inner_came[0, s], inner_on[s]),
                add(outer_stay[0, s], outer_came[0, s], outer_on[s]),
            ],
            axis=1,
        )
        for s in range(n_z)
    ]
    feed_line = [plane.shift(feed_parts[s], -s) for s in others]
    output = copied(output)
    arrived, output = together(arrived, output)
    small = add(small, *[a[-small_rows:] for a in arrived])
    count = 2 * mine // n_places
    attention_parts = [
        add(*[a[s * count : (s + 1) * count] for a in [kept[0]] + arrived]) for s in range(n_z)
    ]
    attention_line = [
        plane.shift(jnp.concatenate([attention_parts[s], small], axis=0), s) for s in others
    ]
    feed_total = plane.over_groups(add(feed_parts[0], *feed_line))
    feed_arrived = plane.to_places([feed_total] * n_places)
    attention_line, feed_arrived, tokens_grad = together(
        attention_line, feed_arrived, tokens_grad
    )
    attention_total = plane.over_groups(
        add(attention_parts[0], *[a[:count] for a in attention_line])
    )
    small = plane.over_groups(add(small, *[a[count:] for a in attention_line])).astype(f32)
    arrived = plane.to_places([attention_total] * n_places)
    feed_half = plane.from_places(feed_total, feed_arrived)
    feed_other = plane.swap(feed_half, 1)
    inner_grad, outer_grad = finish_feed(core.reshape(1), feed_half, feed_other)
    inner_bias_sum = lax.dynamic_slice_in_dim(small, 6 + z, 1, 0)[0]
    head_sums = lax.dynamic_slice_in_dim(small[6 + n_z : 8 + n_z], z * mine, mine, 1)
    arrived, inner_grad, outer_grad, small, inner_bias_sum, head_sums = together(
        arrived, inner_grad, outer_grad, small, inner_bias_sum, head_sums
    )
    attention_half = plane.from_places(attention_total, arrived)
    attention_other = plane.swap(attention_half, 1)
    grad_list = plane.by_core(attention_half, attention_other)
    grad_list = grad_list.reshape(2, n_places, 2, mine // n_places, width)
    grad_list = grad_list.transpose(0, 2, 1, 3, 4).reshape(4, mine, width)

    shared = small[:6]

    return (
        output,
        tokens_grad,
        grad_list[0].T.astype(f32),
        head_sums[0],
        grad_list[1].T.astype(f32),
        grad_list[2].T.astype(f32),
        head_sums[1],
        grad_list[3].astype(f32),
        shared[0],
        shared[1],
        shared[2],
        inner_grad,
        inner_bias_sum,
        outer_grad,
        shared[3],
        shared[4],
        shared[5],
    )


def solution(mesh):
    n_dp, n_z = mesh.shape["dp"], mesh.shape["tensor"]
    in_specs = (
        P("dp", None),
        P("dp", None),
        P("dp"),
        P(None, "tensor"),
        P("tensor"),
        P(None, "tensor"),
        P(None, "tensor"),
        P("tensor"),
        P("tensor", None),
        P(),
        P(),
        P(),
        P(None, "tensor"),
        P("tensor"),
        P("tensor", None),
        P(),
        P(),
        P(),
        P("dp", None),
    )
    out_specs = (
        P("dp", None),
        P("dp", None),
        P(None, "tensor"),
        P("tensor"),
        P(None, "tensor"),
        P(None, "tensor"),
        P("tensor"),
        P("tensor", None),
        P(),
        P(),
        P(),
        P(None, "tensor"),
        P("tensor"),
        P("tensor", None),
        P(),
        P(),
        P(),
    )

    def program(*args):
        return on_device(n_dp, n_z, *args)

    return jax.shard_map(
        program, mesh=mesh, in_specs=in_specs, out_specs=out_specs, check_vma=False
    )
```

```python
import functools

import jax
import jax.numpy as jnp
from jax import lax
from jax.experimental import pallas as pl
from jax.experimental.pallas import tpu as pltpu
from jax.sharding import PartitionSpec as P

HEAD = 64
BUCKET = 512
ITEMS = 8


negative_fill = -1e30
epsilon = 1e-06
f32 = jnp.float32
bf16 = jnp.bfloat16
VMEM_BYTES = 56 * 1024 * 1024


def dot(left, right):
    return jnp.dot(left, right, preferred_element_type=f32)


def contract_rows(left, right):
    return lax.dot_general(left, right, (((0,), (0,)), ((), ())), preferred_element_type=f32)


def contract_cols(left, right):
    return lax.dot_general(left, right, (((1,), (1,)), ((), ())), preferred_element_type=f32)


def norm_rows(values):
    centred = values - jnp.mean(values, axis=1, keepdims=True)
    inv_scale = lax.rsqrt(jnp.mean(centred * centred, axis=1, keepdims=True) + epsilon)
    return centred * inv_scale, inv_scale


def norm_back(grad_rows, norm_gain, normed, inv_scale):
    scaled = grad_rows * norm_gain
    return inv_scale * (
        scaled
        - jnp.mean(scaled, axis=1, keepdims=True)
        - normed * jnp.mean(scaled * normed, axis=1, keepdims=True)
    )


def column_sum(matrix):
    return jnp.sum(matrix.astype(f32), axis=0, keepdims=True)


def fixed(shape):
    return pl.BlockSpec(shape, lambda *_: (0,) * len(shape))


def cost(microseconds):
    return pl.CostEstimate(
        flops=int(microseconds * 2.5e8),
        bytes_accessed=int(microseconds * 2.5e5),
        transcendentals=0,
    )


def params(axes):
    return pltpu.CompilerParams(
        dimension_semantics=("arbitrary",) * axes, vmem_limit_bytes=VMEM_BYTES
    )


def item_places(lengths_ref, row, shape, axis):
    places = lax.broadcasted_iota(jnp.int32, shape, axis)
    end = jnp.int32(0)
    items = jnp.zeros(shape, jnp.int32)
    for slot in range(ITEMS):
        end = end + lengths_ref[row, slot]
        items = items + (places >= end).astype(jnp.int32)
    return items


def as_column(row):
    return jnp.broadcast_to(row.astype(f32), (8, row.shape[1])).T[:, :1]


def mask_bias(lengths_ref, row, key_mask):
    shape = (BUCKET, BUCKET)
    diagonal = lax.broadcasted_iota(jnp.int32, shape, 0) == lax.broadcasted_iota(
        jnp.int32, shape, 1
    )
    item_row = item_places(lengths_ref, row, (1, BUCKET), 1)
    item_column = item_places(lengths_ref, row, (BUCKET, 1), 0)
    code_column = jnp.where(as_column(key_mask) == 1.0, item_column, -1)
    return jnp.where((code_column == item_row) | diagonal, 0.0, negative_fill).astype(f32)


def attend_forward_kernel(
    lengths_ref, tokens_ref, query_ref, key_ref, value_ref, biases_ref, key_mask_ref, mixed_ref,
):
    mine = query_ref.shape[0]
    rows = tokens_ref[...]
    queries = contract_cols(query_ref[...], rows) + as_column(biases_ref[0:1, :mine])
    queries = (queries.astype(bf16) * HEAD ** (-0.5)).astype(bf16)
    keys = contract_cols(rows, key_ref[...]).astype(bf16)
    values = contract_cols(value_ref[...], rows) + as_column(biases_ref[0:1, mine : 2 * mine])
    values = values.astype(bf16)
    bias = mask_bias(lengths_ref, pl.program_id(0), key_mask_ref[0])
    for head in range(mine // HEAD):
        at = slice(head * HEAD, (head + 1) * HEAD)
        scores = dot(keys[:, at], queries[at]) + bias
        exponent = jnp.exp(scores - jnp.max(scores, axis=0, keepdims=True))
        total = jnp.sum(exponent, axis=0, keepdims=True)
        mixed_ref[0, 0, at] = (dot(values[at], exponent.astype(bf16)) / total).astype(bf16)
    mixed_ref[0, 0, mine:] = biases_ref[...]


def attend_forward(n_z, lengths, tokens, query, key, value, biases, key_mask):
    blocks = lengths.shape[0]
    own = blocks // n_z
    mine, width = key.shape
    whole = (n_z, own, mine + biases.shape[0], BUCKET)
    return pl.pallas_call(
        attend_forward_kernel,
        grid=(blocks,),
        in_specs=[
            pl.BlockSpec(memory_space=pltpu.SMEM),
            pl.BlockSpec((BUCKET, width), lambda b: (b, 0)),
            fixed((mine, width)),
            fixed((mine, width)),
            fixed((mine, width)),
            fixed(biases.shape),
            pl.BlockSpec((1, 1, BUCKET), lambda b: (b, 0, 0)),
        ],
        out_specs=pl.BlockSpec((1, 1) + whole[2:], lambda b: (b // own, b % own, 0, 0)),
        out_shape=jax.ShapeDtypeStruct(whole, bf16),
        compiler_params=params(1),
        name="attend_forward",
        cost_estimate=cost(12),
    )(lengths, tokens, query, key, value, biases, key_mask)


def fetch_units(step, picks, own_ref, halves, units, sems):
    feed_rows = units.shape[2]
    cut = feed_rows // 2

    def copies(number):
        slot = number % 2
        row = pl.multiple_of(picks[number] * feed_rows, 16)
        ends = [
            (own_ref.at[pl.ds(row, feed_rows)], units.at[slot, 0]),
            (halves[number][0], units.at[slot, 1:, :cut]),
            (halves[number][1], units.at[slot, 1:, cut:]),
        ]
        return [
            pltpu.make_async_copy(source, target, sems.at[slot, i])
            for i, (source, target) in enumerate(ends)
        ]

    for number in range(len(halves)):

        @pl.when(step == number)
        def _(number=number):
            if number == 0:
                for copy in copies(0):
                    copy.start()
            if number + 1 < len(halves):
                for copy in copies(number + 1):
                    copy.start()
            for copy in copies(number):
                copy.wait()

    return units.at[lax.rem(step, 2)]


def fetch_mixer(picks, own_ref, parts, mixer, sems):
    count = mixer.shape[1] // 8
    ends = [(own_ref, mixer.at[0])]
    for pick, part in zip(picks, parts):
        row = pl.multiple_of(pick * count, 16)
        ends.append((part, mixer.at[1:, pl.ds(row, count)]))
    copies = [
        pltpu.make_async_copy(source, target, sems.at[i])
        for i, (source, target) in enumerate(ends)
    ]
    for copy in copies:
        copy.start()
    for copy in copies:
        copy.wait()


def take_halves(numbers, refs):
    halves, refs = [], list(refs)
    for number in numbers:
        if number == 3:
            halves.append((refs.pop(0), refs.pop(0)))
        else:
            ref = refs.pop(0)
            cut = ref.shape[1] // 2
            halves.append((ref.at[:, :cut], ref.at[:, cut:]))
    return halves, refs


def split_units(units):
    width = units.shape[2] // 2
    return units[:, :, :width].reshape(-1, width), units[:, :, width:].reshape(-1, width)


ANYWHERE = pl.BlockSpec(memory_space=pl.ANY)


def feed_forward_kernel(chunks, first, last, info_ref, *rest):
    def take(count):
        nonlocal rest
        taken, rest = rest[:count], rest[count:]
        return taken

    vectors_ref, bias_ref, own_ref = take(3)
    halves, rest = take_halves([number for _, number in chunks], rest)
    if first:
        tokens_ref, mixed_ref, mixer_own_ref, *mixer_parts = take(11)
    else:
        normed_low_ref, start_ref, _, _ = take(4)
    if last:
        lengths_ref, cotangent_ref = take(2)
    hidden_ref, slope_ref = take(2)
    if first:
        normed_low_ref, first_normed_ref, first_scale_ref = take(3)
    if last:
        output_ref, grad_second_ref, grad_outer_ref, sums_ref = take(4)
    else:
        (second_sum,) = take(1)
    units, sems = take(2)
    if first:
        mixer, mixer_sems = take(2)
    if last:
        (second_sum,) = take(1)

    step = pl.program_id(0)
    picks = [(info_ref[1] ^ number) * 2 + (info_ref[2] ^ side) for side, number in chunks]
    weights = fetch_units(step, picks, own_ref, halves, units, sems)
    output_bias, first_gain, first_shift, outer_bias, second_gain, second_shift = (
        vectors_ref[i : i + 1, :] for i in range(6)
    )

    @pl.when(step == 0)
    def _():
        if first:
            all_picks = [
                (info_ref[1] ^ number) * 2 + (info_ref[2] ^ side)
                for side in range(2)
                for number in range(4)
            ]
            fetch_mixer(all_picks, mixer_own_ref, mixer_parts, mixer, mixer_sems)
            n_z, own, mine, _ = mixed_ref.shape
            attended = output_bias + jnp.concatenate(
                [
                    sum(
                        dot(mixer[s, :, :mine], mixed_ref[lax.rem(info_ref[0] + n_z - s, n_z), b])
                        for s in range(n_z)
                    ).T
                    for b in range(own)
                ],
                axis=0,
            )
            normed, inv_scale = norm_rows(tokens_ref[...].astype(f32) + attended)
            whole = normed * first_gain + first_shift
            first_normed_ref[...] = normed
            first_scale_ref[...] = inv_scale
            normed_low_ref[...] = whole.astype(bf16)
            second_sum[...] = whole + outer_bias
        else:
            second_sum[...] = start_ref[...]

    inner, outer = split_units(weights)
    inner_pre = contract_cols(normed_low_ref[...], inner) + bias_ref[0]
    normal_cdf = 0.5 + 0.5 * lax.erf(inner_pre * 0.7071067811865476)
    bell = jnp.exp(-0.5 * inner_pre * inner_pre)
    hidden = (inner_pre * normal_cdf).astype(bf16)
    hidden_ref[...] = hidden.T
    slope_ref[...] = (normal_cdf + inner_pre * bell * 0.3989422804014327).astype(bf16)
    second_sum[...] += dot(hidden, outer)

    if last:

        @pl.when(step == pl.num_programs(0) - 1)
        def _():
            normed, inv_scale = norm_rows(second_sum[...])
            blocks = normed.shape[0] // BUCKET
            live = jnp.concatenate(
                [
                    (item_places(lengths_ref, info_ref[0] * blocks + b, (BUCKET, 1), 0) < ITEMS)
                    for b in range(blocks)
                ],
                axis=0,
            ).astype(f32)
            output_ref[...] = ((normed * second_gain + second_shift) * live).astype(bf16)
            grad_final = cotangent_ref[...].astype(f32) * live
            grad_second = norm_back(grad_final, second_gain, normed, inv_scale)
            grad_outer = grad_second.astype(bf16)
            grad_second_ref[...] = grad_second
            grad_outer_ref[...] = grad_outer
            sums_ref[0:1, :] = column_sum(grad_outer)
            sums_ref[1:2, :] = column_sum(grad_final * normed)
            sums_ref[2:3, :] = column_sum(grad_final)


def feed_forward(chunks, info, vectors, biases, own, halves, first=None, going=None, last=None):
    width = vectors.shape[1]
    n_z = halves[0].shape[0] + 1
    feed_rows, twice = own.shape[0] // 8, 2 * width
    rows = first[1].shape[1] * BUCKET if first else going[0].shape[0]
    chunk = n_z * feed_rows
    whole = fixed((rows, width))
    my_rows = pl.BlockSpec((rows, width), lambda j, info: (info[0], 0))
    at = lambda j, info: info[3 + j]
    hidden_spec = pl.BlockSpec((chunk, rows), lambda j, info: (at(j, info), 0))
    slope_spec = pl.BlockSpec((rows, chunk), lambda j, info: (0, at(j, info)))
    in_specs = [
        fixed((8, width)),
        pl.BlockSpec((1, 1, chunk), lambda j, info: (at(j, info), 0, 0)),
        ANYWHERE,
    ] + [ANYWHERE] * len(halves)
    args = [vectors, biases, own] + halves
    shapes = [
        ((8 * chunk, rows), bf16, hidden_spec),
        ((rows, 8 * chunk), bf16, slope_spec),
    ]
    scratch = [
        pltpu.VMEM((2, n_z, feed_rows, twice), bf16),
        pltpu.SemaphoreType.DMA((2, 3)),
    ]
    aliases = {}
    if first:
        tokens, mixed, mixer_own, mixer_parts = first
        mine = width // n_z
        in_specs += [my_rows, fixed((n_z, mixed.shape[1], mine, BUCKET))] + [ANYWHERE] * 9
        args += [tokens, mixed, mixer_own] + mixer_parts
        shapes += [
            ((rows, width), bf16, whole),
            ((rows, width), f32, whole),
            ((rows, 1), f32, fixed((rows, 1))),
        ]
        scratch += [
            pltpu.VMEM((n_z,) + mixer_own.shape, bf16),
            pltpu.SemaphoreType.DMA((9,)),
        ]
    else:
        aliases = {1 + len(args) + 2: 0, 1 + len(args) + 3: 1}
        in_specs += [whole, whole, ANYWHERE, ANYWHERE]
        args += list(going)
    if last:
        in_specs += [pl.BlockSpec(memory_space=pltpu.SMEM), my_rows]
        args += list(last)
        shapes += [
            ((rows, width), bf16, whole),
            ((rows, width), f32, whole),
            ((rows, width), bf16, whole),
            ((8, width), f32, fixed((8, width))),
        ]
        scratch.append(pltpu.VMEM((rows, width), f32))
    else:
        shapes.append(((rows, width), f32, whole))
    info = jnp.concatenate(
        [info, jnp.array([4 * side + number for side, number in chunks], jnp.int32)]
    )
    return pl.pallas_call(
        functools.partial(feed_forward_kernel, chunks, first is not None, last is not None),
        grid_spec=pltpu.PrefetchScalarGridSpec(
            num_scalar_prefetch=1,
            grid=(len(chunks),),
            in_specs=in_specs,
            out_specs=[spec for _, _, spec in shapes],
            scratch_shapes=scratch,
        ),
        out_shape=[jax.ShapeDtypeStruct(shape, kind) for shape, kind, _ in shapes],
        input_output_aliases=aliases,
        compiler_params=params(1),
        name="feed_forward",
        cost_estimate=cost(3 * len(chunks)),
    )(info, *args)


STAY = ((0, 1), (0, 2))
GO = ((2, 3), (1, 3))


def feed_back_kernel(
    keeps, info_ref, grad_outer_ref, normed_low_ref, hidden_ref, slope_ref,
    own_ref, start_ref, *rest,
):
    halves, rest = take_halves(range(4), rest)
    if keeps:
        other_refs, norm_refs, rest = rest[:2], rest[2:5], rest[5:]
        stay_refs, go_refs, rest = rest[0:2], rest[2:4], rest[4:]
        bias_grad_ref, grad_first_ref, grad_attended_ref, sums_ref, units, sems = rest[:6]
        grad_normed_ref = rest[6]
    else:
        *grad_refs, bias_grad_ref, grad_normed_ref, units, sems = rest
    step = pl.program_id(0)
    side = info_ref[2] if keeps else 1 - info_ref[2]
    picks = [(info_ref[1] ^ number) * 2 + side for number in range(4)]
    weights = fetch_units(step, picks, own_ref, halves, units, sems)

    @pl.when(step == 0)
    def _():
        grad_normed_ref[...] = start_ref[...]

    n_z, feed_rows, twice = weights.shape
    width = twice // 2
    inner, outer = split_units(weights)
    grad_outer = grad_outer_ref[...]
    grad_hidden = contract_cols(grad_outer, outer)
    grad_inner = (grad_hidden * slope_ref[...].astype(f32)).astype(bf16)
    outer_grad = dot(hidden_ref[...], grad_outer).reshape(n_z, feed_rows, width)
    inner_grad = contract_rows(grad_inner, normed_low_ref[...]).reshape(n_z, feed_rows, width)
    bias_grad_ref[0] = column_sum(grad_inner)
    grad_normed_ref[...] += dot(grad_inner, inner)

    for number in range(4):

        @pl.when(step == number)
        def _(number=number):
            for track, value in enumerate((inner_grad, outer_grad)):
                at = slice(track * width, (track + 1) * width)
                if keeps:
                    found = value + other_refs[number // 2][0, :, :, at].astype(f32)
                    ref = stay_refs[track] if number in STAY[track] else go_refs[track]
                    ref[0] = found.astype(bf16)
                else:
                    grad_refs[number // 2][0, :, :, at] = value.astype(bf16)

    if keeps:

        @pl.when(step == pl.num_programs(0) - 1)
        def _():
            first_normed_ref, first_scale_ref, vectors_ref = norm_refs
            grad_rows, normed = grad_normed_ref[...], first_normed_ref[...]
            grad_first = norm_back(grad_rows, vectors_ref[1:2, :], normed, first_scale_ref[...])
            grad_attended = grad_first.astype(bf16)
            grad_first_ref[...] = grad_first
            grad_attended_ref[...] = grad_attended
            sums_ref[0:1, :] = column_sum(grad_attended)
            sums_ref[1:2, :] = column_sum(grad_rows * normed)
            sums_ref[2:3, :] = column_sum(grad_rows)


def feed_back(
    info, grad_outer, normed_low, hidden, slope, own, start, units, others=None, norm=None
):
    rows, width = grad_outer.shape
    keeps = others is not None
    count = 4
    feed_rows, twice = own.shape[0] // 8, 2 * width
    n_z = units[0].shape[0] + 1
    chunk = n_z * feed_rows
    flip = 0 if keeps else 1
    columns = pl.BlockSpec((rows, chunk), lambda i, info: (0, 4 * flip + i))
    whole = fixed((rows, width))
    part = (n_z, feed_rows, twice)
    track = (2, n_z, feed_rows, width)
    unit_rows = pl.BlockSpec((chunk, rows), lambda i, info: (4 * flip + i, 0))
    in_specs = [whole, whole, unit_rows, columns, ANYWHERE, whole] + [ANYWHERE] * len(units)
    args = [grad_outer, normed_low, hidden, slope, own, start] + units
    bias_shape = (
        (count, 1, chunk),
        f32,
        pl.BlockSpec((1, 1, chunk), lambda i, info: (i, 0, 0)),
    )
    scratch = [pltpu.VMEM((2,) + part, bf16), pltpu.SemaphoreType.DMA((2, 3))]

    def one(shape, at):
        return pl.BlockSpec((1,) + shape[1:], lambda i, info: (at(i), 0, 0, 0))

    early, late = (lambda i: jnp.minimum(i, 1)), (lambda i: jnp.maximum(i - 2, 0))
    pair = (2,) + part
    if keeps:
        in_specs += [one(pair, early), one(pair, late)]
        in_specs += [whole, fixed((rows, 1)), fixed((8, width))]
        args += list(others) + list(norm)
        slow, slower = (lambda i: i // 2), (lambda i: jnp.maximum(i - 1, 0) // 2)
        shapes = [(track, bf16, one(track, at)) for at in (early, slow, late, slower)] + [
            bias_shape,
            ((rows, width), f32, whole),
            ((rows, width), bf16, whole),
            ((8, width), f32, fixed((8, width))),
        ]
        scratch.append(pltpu.VMEM((rows, width), f32))
    else:
        shapes = [
            (pair, bf16, one(pair, early)),
            (pair, bf16, one(pair, late)),
            bias_shape,
            ((rows, width), f32, whole),
        ]
    return pl.pallas_call(
        functools.partial(feed_back_kernel, keeps),
        grid_spec=pltpu.PrefetchScalarGridSpec(
            num_scalar_prefetch=1,
            grid=(count,),
            in_specs=in_specs,
            out_specs=[spec for _, _, spec in shapes],
            scratch_shapes=scratch,
        ),
        out_shape=[jax.ShapeDtypeStruct(shape, kind) for shape, kind, _ in shapes],
        compiler_params=params(1),
        name="feed_back_own" if keeps else "feed_back",
        cost_estimate=cost(3 * count),
    )(info, *args)


def finish_feed_kernel(core_ref, own_ref, other_ref, inner_ref, outer_ref, inner_rows):
    places, count, twice = own_ref.shape
    width = twice // 2
    for source, side in ((own_ref, core_ref[0]), (other_ref, 1 - core_ref[0])):
        for place in range(places):
            row = pl.multiple_of((2 * place + side) * count, 16)
            inner_rows[pl.ds(row, count), :] = source[place, :, :width].astype(f32)
            outer_ref[pl.ds(row, count), :] = source[place, :, width:].astype(f32)
    inner_ref[...] = inner_rows[...].T


def finish_feed(core, own, other):
    places, count, twice = own.shape
    shape = (2 * places * count, twice // 2)
    inner_shape = (shape[1], shape[0])
    return pl.pallas_call(
        finish_feed_kernel,
        grid_spec=pltpu.PrefetchScalarGridSpec(
            num_scalar_prefetch=1,
            grid=(1,),
            in_specs=[fixed(own.shape), fixed(other.shape)],
            out_specs=[fixed(inner_shape), fixed(shape)],
            scratch_shapes=[pltpu.VMEM(shape, f32)],
        ),
        out_shape=[
            jax.ShapeDtypeStruct(inner_shape, f32),
            jax.ShapeDtypeStruct(shape, f32),
        ],
        compiler_params=params(1),
        name="finish_feed",
        cost_estimate=cost(5),
    )(core, own, other)


def copy_kernel(from_ref, to_ref):
    to_ref[...] = from_ref[...]


def copied(array):
    block = pl.BlockSpec((BUCKET, array.shape[1]), lambda i: (i, 0))
    return pl.pallas_call(
        copy_kernel,
        grid=(array.shape[0] // BUCKET,),
        in_specs=[block],
        out_specs=block,
        out_shape=jax.ShapeDtypeStruct(array.shape, array.dtype),
        compiler_params=params(1),
        name="copied",
        cost_estimate=cost(0.5),
    )(array)


def project_kernel(place_ref, tokens_ref, weights_ref, biases_ref, query_ref, key_ref, value_ref):
    rows = tokens_ref[...]
    width = rows.shape[1]
    queries = contract_cols(weights_ref[:, :width], rows) + as_column(biases_ref[0:1, :])
    query_ref[...] = (queries.astype(bf16) * HEAD ** (-0.5)).astype(bf16)
    key_ref[...] = contract_cols(rows, weights_ref[:, width : 2 * width]).astype(bf16)
    values = contract_cols(rows, weights_ref[:, 2 * width :]) + biases_ref[1:2, :]
    value_ref[...] = values.astype(bf16)


def project(place, tokens, weights, biases, buckets):
    width = tokens.shape[1]
    part = width // 3
    shapes = [
        ((buckets, width, BUCKET), pl.BlockSpec((None, part, BUCKET), lambda b, j, _: (b, j, 0))),
        ((buckets * BUCKET, width), pl.BlockSpec((BUCKET, part), lambda b, j, _: (b, j))),
        ((buckets * BUCKET, width), pl.BlockSpec((BUCKET, part), lambda b, j, _: (b, j))),
    ]
    return pl.pallas_call(
        project_kernel,
        grid_spec=pltpu.PrefetchScalarGridSpec(
            num_scalar_prefetch=1,
            grid=(buckets, 3),
            in_specs=[
                pl.BlockSpec((BUCKET, width), lambda b, j, place: (place[0] * buckets + b, 0)),
                pl.BlockSpec((part, 3 * width), lambda b, j, place: (j, 0)),
                pl.BlockSpec((8, part), lambda b, j, place: (0, j)),
            ],
            out_specs=[spec for _, spec in shapes],
        ),
        out_shape=[jax.ShapeDtypeStruct(shape, bf16) for shape, _ in shapes],
        compiler_params=params(2),
        name="project",
        cost_estimate=cost(5),
    )(place, tokens, weights, biases)


def attend_back_kernel(
    place_ref, lengths_ref, grad_attended_ref, grad_first_ref, weights_ref, query_ref, key_ref,
    value_ref, key_mask_ref,
    grads_ref, tokens_grad_ref, sums_ref,
    bias, grad_mixed_t, whole, weights, sem,
):
    pair = pl.program_id(1)
    pairs, width = whole.shape[1], weights.shape[0]
    fetch = pltpu.make_async_copy(weights_ref, weights, sem)

    @pl.when(pair == 0)
    def _():
        fetch.start()
        row = place_ref[0] * pl.num_programs(0) + pl.program_id(0)
        bias[...] = mask_bias(lengths_ref, row, key_mask_ref[0])
        fetch.wait()
        grad_mixed_t[...] = contract_cols(
            weights[:, 3 * width :], grad_attended_ref[...]
        ).astype(bf16)

    queries, keys, values = query_ref[...], key_ref[...], value_ref[...]
    start = pl.multiple_of(pair * keys.shape[1], 128)
    grad_mixed = grad_mixed_t[pl.ds(start, keys.shape[1]), :]
    keys_t = keys.T
    grad_queries, grad_keys, grad_values = [], [], []
    for head in range(keys.shape[1] // HEAD):
        at = slice(head * HEAD, (head + 1) * HEAD)
        scores = dot(keys[:, at], queries[at]) + bias[...]
        exponent = jnp.exp(scores - jnp.max(scores, axis=0, keepdims=True))
        probs = exponent * (1.0 / jnp.sum(exponent, axis=0, keepdims=True))
        grad_probs = dot(values[:, at], grad_mixed[at])
        shift = jnp.sum(probs * grad_probs, axis=0, keepdims=True)
        grad_scores = (probs * (grad_probs - shift)).astype(bf16)
        grad_values.append(contract_cols(probs.astype(bf16), grad_mixed[at]))
        grad_keys.append(contract_cols(grad_scores, queries[at]))
        grad_queries.append(dot(keys_t[at], grad_scores) * HEAD ** (-0.5))
    query_t = jnp.concatenate(grad_queries, axis=0).astype(bf16)
    found = (
        query_t.T,
        jnp.concatenate(grad_keys, axis=1).astype(bf16),
        jnp.concatenate(grad_values, axis=1).astype(bf16),
    )
    for number, grad in enumerate(found):
        grads_ref[number, 0] = query_t if number == 0 else grad.T
        whole[number, pair] = grad
    sums_ref[0, 0:1, :] = column_sum(found[0])
    sums_ref[0, 1:2, :] = column_sum(found[2])

    @pl.when(pair == pl.num_programs(1) - 1)
    def _():
        total = grad_first_ref[...]
        for number in range(3):
            grad = jnp.concatenate([whole[number, i] for i in range(pairs)], axis=1)
            total += dot(grad, weights[:, number * width : (number + 1) * width])
        tokens_grad_ref[...] = total.astype(bf16)


def attend_back(place, lengths, grad_attended, grad_first, weights, queries, keys, values, key_mask):
    rows, width = grad_attended.shape
    blocks = rows // BUCKET
    pair = 2 * HEAD
    by_bucket = pl.BlockSpec((BUCKET, width), lambda b, h, place: (b, 0))
    by_pair = pl.BlockSpec((BUCKET, pair), lambda b, h, place: (b, h))
    return pl.pallas_call(
        attend_back_kernel,
        grid_spec=pltpu.PrefetchScalarGridSpec(
            num_scalar_prefetch=1,
            grid=(blocks, width // pair),
            in_specs=[
                pl.BlockSpec(memory_space=pltpu.SMEM),
                by_bucket,
                by_bucket,
                ANYWHERE,
                pl.BlockSpec((None, pair, BUCKET), lambda b, h, place: (b, h, 0)),
                by_pair,
                by_pair,
                pl.BlockSpec((1, 1, BUCKET), lambda b, h, place: (place[0] * blocks + b, 0, 0)),
            ],
            out_specs=[
                pl.BlockSpec((3, 1, pair, BUCKET), lambda b, h, place: (0, b, h, 0)),
                by_bucket,
                pl.BlockSpec((1, 8, pair), lambda b, h, place: (b, 0, h)),
            ],
            scratch_shapes=[
                pltpu.VMEM((BUCKET, BUCKET), f32),
                pltpu.VMEM((width, BUCKET), bf16),
                pltpu.VMEM((3, width // pair, BUCKET, pair), bf16),
                pltpu.VMEM(weights.shape, bf16),
                pltpu.SemaphoreType.DMA(()),
            ],
        ),
        out_shape=[
            jax.ShapeDtypeStruct((3, blocks, width, BUCKET), bf16),
            jax.ShapeDtypeStruct((rows, width), bf16),
            jax.ShapeDtypeStruct((blocks, 8, width), f32),
        ],
        compiler_params=params(2),
        name="attend_back",
        cost_estimate=cost(20),
    )(place, lengths, grad_attended, grad_first, weights, queries, keys, values, key_mask)


def attention_grads_kernel(
    n_places, adds, info_ref, grads_ref, mixed_ref, tokens_ref, grad_attended_ref, *rest
):
    if adds:
        other_ref, small_ref = rest[:2]
        out_refs, whole = rest[2:-1], rest[-1]
    else:
        (out_ref, whole) = rest
    step = pl.program_id(0)
    which = info_ref[step]
    n_z, buckets, mine, _ = mixed_ref.shape
    count = mine // n_places

    @pl.when(which < 3)
    def _():
        whole[...] = sum(
            dot(grads_ref[0, b], tokens_ref[b * BUCKET : (b + 1) * BUCKET, :])
            for b in range(buckets)
        ).astype(bf16)

    @pl.when(which == 3)
    def _():
        for t in range(n_z):
            whole[t * mine : (t + 1) * mine, :] = sum(
                dot(mixed_ref[t, b], grad_attended_ref[b * BUCKET : (b + 1) * BUCKET, :])
                for b in range(buckets)
            ).astype(bf16)

    for number in range(n_places):
        for s in range(n_z):
            start = lax.rem(info_ref[2] + s, n_z) * mine + (info_ref[3] ^ number) * count
            value = whole[pl.ds(pl.multiple_of(start, 16), count), :]
            if adds:
                value = value.astype(f32) + other_ref[number, s, 0].astype(f32)
                row = (2 * s + step) * count
                out_refs[number][pl.ds(pl.multiple_of(row, 16), count), :] = value.astype(bf16)
            else:
                out_ref[number, s, 0] = value

    if adds:
        for number in range(n_places):
            out_refs[number][2 * n_z * count :, :] = small_ref[...]


def attention_grads(n_places, info, grads, mixed, tokens, grad_attended, other=None, small=None):
    rows, width = grad_attended.shape
    n_z, buckets = mixed.shape[:2]
    mine = width // n_z
    count = mine // n_places
    parts = (n_places, n_z, 1, count, width)
    by_step = pl.BlockSpec(parts, lambda i, info: (0, 0, i, 0, 0))
    in_specs = [
        pl.BlockSpec(
            (1, buckets, width, BUCKET), lambda i, info: (jnp.minimum(info[i], 2), 0, 0, 0)
        ),
        fixed((n_z, buckets, mine, BUCKET)),
        pl.BlockSpec((rows, width), lambda i, info: (info[2], 0)),
        fixed((rows, width)),
    ]
    args = [grads, mixed, tokens, grad_attended]
    if other is None:
        shapes = [((n_places, n_z, 2, count, width), by_step)]
    else:
        in_specs += [by_step, fixed(small.shape)]
        args += [other, small]
        flat = (2 * n_z * count + small.shape[0], width)
        shapes = [(flat, fixed(flat))] * n_places
    return pl.pallas_call(
        functools.partial(attention_grads_kernel, n_places, other is not None),
        grid_spec=pltpu.PrefetchScalarGridSpec(
            num_scalar_prefetch=1,
            grid=(2,),
            in_specs=in_specs,
            out_specs=[spec for _, spec in shapes],
            scratch_shapes=[pltpu.VMEM((width, width), bf16)],
        ),
        out_shape=[jax.ShapeDtypeStruct(shape, bf16) for shape, _ in shapes],
        compiler_params=params(1),
        name="attention_grads",
        cost_estimate=cost(0.5),
    )(info, *args)


def together(*values):
    return lax.optimization_barrier(values)


def add(first, *others):
    total = first.astype(f32)
    for other in others:
        total = total + other.astype(f32)
    return total.astype(bf16)


class Plane:
    def __init__(self, n_dp, n_z):
        self.n_dp, self.n_z = n_dp, n_z
        self.n_group = min(n_dp, 8)
        self.n_places = self.n_group // 2
        self.dp = lax.axis_index("dp")
        self.z = lax.axis_index("tensor")
        self.index = lax.rem(self.dp, self.n_group)
        self.core = self.index & 1
        self.place = self.index >> 1

    def swap(self, array, bits):
        return lax.ppermute(array, "dp", [(i, i ^ bits) for i in range(self.n_dp)])

    def shift(self, array, by):
        n = self.n_z
        return lax.ppermute(array, "tensor", [(i, (i + by) % n) for i in range(n)])

    def gather(self, piece):
        if self.n_dp == self.n_group:
            whole = lax.all_gather(piece, ("tensor", "dp"))
            return whole.reshape((self.n_z, self.n_group) + piece.shape)
        groups = [
            list(range(i, i + self.n_group)) for i in range(0, self.n_dp, self.n_group)
        ]
        line = lax.all_gather(piece, "tensor")
        return lax.all_gather(line, "dp", axis=1, axis_index_groups=groups)

    def turned(self, array):
        bit = 1
        while bit < self.n_group:
            lead = array.reshape((-1, 2, bit) + array.shape[1:])
            array = jnp.where((self.index & bit) != 0, lead[:, ::-1], lead).reshape(array.shape)
            bit *= 2
        return array

    def to_places(self, parts):
        return [self.swap(parts[number], 2 * number) for number in range(1, self.n_places)]

    def from_places(self, own, arrived):
        found = jnp.stack([own] + arrived)
        bit = 1
        while bit < self.n_places:
            lead = found.reshape((-1, 2, bit) + own.shape)
            flipped = lead[:, ::-1]
            found = jnp.where((self.place & bit) != 0, flipped, lead).reshape(found.shape)
            bit *= 2
        return found

    def by_core(self, own, other):
        return jnp.where(
            self.core == 1, jnp.stack([other, own]), jnp.stack([own, other])
        )

    def over_groups(self, array):
        bit = self.n_group
        while bit < self.n_dp:
            array = add(array, self.swap(array, bit))
            bit *= 2
        return array


def on_device(
    n_dp,
    n_z,
    tokens,
    lengths,
    key_mask,
    query_weight,
    query_bias,
    key_weight,
    value_weight,
    value_bias,
    output_weight,
    output_bias,
    first_gain,
    first_shift,
    inner_weight,
    inner_bias,
    outer_weight,
    outer_bias,
    second_gain,
    second_shift,
    cotangent,
):
    width = tokens.shape[1]
    mine = query_weight.shape[1]
    units = inner_weight.shape[1]
    all_rows = tokens.shape[0]
    all_blocks = all_rows // BUCKET
    rows = all_rows // n_z
    plane = Plane(n_dp, n_z)
    z, core, place, index = plane.z, plane.core, plane.place, plane.index
    n_places = plane.n_places
    others = range(1, n_z)

    feed_rows = units // plane.n_group
    head_rows = mine // plane.n_group
    mixer_t = jnp.pad(output_weight.T, ((0, 0), (0, -mine % 128)))
    mixer_count = width // plane.n_group
    piece = jnp.concatenate(
        [
            lax.dynamic_slice_in_dim(inner_weight, index * feed_rows, feed_rows, 1).T,
            lax.dynamic_slice_in_dim(outer_weight, index * feed_rows, feed_rows, 0),
            lax.dynamic_slice_in_dim(mixer_t, index * feed_rows, feed_rows, 0),
        ],
        axis=1,
    )
    line = [plane.shift(piece, s) for s in others]

    query_t, key_t, value_t = query_weight.T, key_weight.T, value_weight.T
    attention_own = jnp.concatenate([query_t, key_t, value_t, output_weight], axis=1)
    attention_weights = plane.gather(
        lax.dynamic_slice_in_dim(attention_own, index * head_rows, head_rows, 0)
    ).reshape(width, 4 * width)

    key_mask_rows = key_mask.reshape(all_blocks, 1, BUCKET)
    bias_row = jnp.concatenate([query_bias, value_bias, inner_bias])
    bias_rows = jnp.pad(bias_row, (0, 16 * BUCKET - bias_row.shape[0])).reshape(16, BUCKET)
    place_z = z.reshape(1)
    mixed = attend_forward(
        n_z, lengths, tokens, query_t, key_t, value_t, bias_rows, key_mask_rows
    )
    _, line = together(mixed, line)
    mixed = lax.all_to_all(mixed, "tensor", 0, 0)

    near = jnp.stack([part[:, : 2 * width] for part in line])
    by_x, by_y = plane.swap(near, 2), plane.swap(near, 4)

    mixer_keep = [jnp.stack([part[:, 2 * width :] for part in line])]
    mixer_keep += plane.to_places(mixer_keep * n_places)
    mixer_send = [plane.swap(part, 1) for part in mixer_keep]
    own_units = jnp.concatenate([inner_weight.T, outer_weight], axis=1)

    biases = mixed[:, 0, mine:].reshape(n_z, -1)[:, : bias_row.shape[0]].astype(f32)
    head_biases = jnp.pad(
        jnp.stack([biases[:, :mine].reshape(-1), biases[:, mine : 2 * mine].reshape(-1)]),
        ((0, 6), (0, 0)),
    )
    inner_biases = biases[:, 2 * mine :]
    inner_biases = jnp.concatenate(
        [
            lax.dynamic_slice_in_dim(inner_biases, lax.rem(z + n_z - s, n_z), 1, 0)
            for s in range(n_z)
        ],
        axis=0,
    )
    inner_biases = inner_biases.reshape(n_z, plane.n_group, feed_rows).transpose(1, 0, 2)
    inner_biases = plane.turned(inner_biases).reshape(n_places, 2, 1, n_z * feed_rows)
    inner_biases = inner_biases.transpose(1, 0, 2, 3).reshape(plane.n_group, 1, -1)
    vectors = jnp.stack(
        [output_bias, first_gain, first_shift, outer_bias, second_gain, second_shift]
        + [jnp.zeros_like(output_bias)] * 2
    ).astype(f32)

    info = jnp.stack([z, place, core])
    shared_args = (info, vectors, inner_biases, own_units)
    cut = feed_rows // 2
    far = [plane.swap(by_x[:, :cut], 4), plane.swap(by_y[:, cut:], 2)]
    send = [plane.swap(units_of, 1) for units_of in (near, by_x, by_y)]
    hidden, slope, normed_low, first_normed, first_scale, second_sum = feed_forward(
        ((0, 0), (0, 1), (0, 2), (1, 0), (1, 1), (1, 2)),
        *shared_args,
        [near, by_x, by_y] + send,
        first=(tokens, mixed, mixer_t, mixer_keep + mixer_send),
    )
    second_sum, far = together(second_sum, far)
    far_send = [plane.swap(half, 1) for half in far]
    keep = [near, by_x, by_y] + far
    send = send + far_send
    hidden, slope, my_output, grad_second, grad_outer, second_sums = feed_forward(
        ((0, 3), (1, 3)), *shared_args, far + far_send,
        going=(normed_low, second_sum, hidden, slope), last=(lengths, cotangent),
    )
    my_output, attention_weights = together(my_output, attention_weights)
    output = lax.all_gather(my_output, "tensor", axis=0, tiled=True)

    shared_args = (info, grad_outer, normed_low, hidden, slope, own_units)
    sent_early, sent_late, bias_sent, grad_normed = feed_back(*shared_args, grad_second, send)
    other = [plane.swap(sent_early, 1), plane.swap(sent_late, 1)]
    grad_normed, head_biases, tokens = together(grad_normed, head_biases, tokens)
    projected = project(place_z, tokens, attention_weights, head_biases, rows // BUCKET)
    projected, other = together(projected, other)
    (
        inner_stay, outer_stay, inner_go, outer_go, bias_kept, grad_first, grad_attended, first_sums
    ) = feed_back(
        *shared_args, grad_normed, keep, other,
        (first_normed, first_scale, vectors),
    )
    inner_came, outer_came = plane.swap(inner_go, 4), plane.swap(outer_go, 2)
    bias_grads = jnp.stack(
        [bias_kept[:, 0], bias_sent[:, 0]], axis=1
    )
    inner_bias_grad = plane.turned(bias_grads.reshape(plane.n_group, n_z, feed_rows))
    inner_bias_grad = inner_bias_grad.transpose(1, 0, 2)
    inner_bias_grad = jnp.concatenate(
        [
            sum(
                jnp.where(lax.rem(z - t + n_z, n_z) == s, inner_bias_grad[s : s + 1], 0.0)
                for s in range(n_z)
            )
            for t in range(n_z)
        ],
        axis=0,
    ).reshape(n_z, units)

    grads, my_tokens_grad, back_sums = attend_back(
        place_z, lengths, grad_attended, grad_first, attention_weights, *projected, key_mask_rows
    )
    grads, inner_came, outer_came, output = together(grads, inner_came, outer_came, output)
    inner_on, outer_on = (
        plane.swap(add(inner_stay[1], inner_came[1]), 2),
        plane.swap(add(outer_stay[1], outer_came[1]), 4),
    )
    tokens_grad = lax.all_gather(my_tokens_grad, "tensor", axis=0, tiled=True)

    def weight_grads(side, other=None, small=None):
        info = jnp.stack([2 * side, 2 * side + 1, z, place])
        return attention_grads(
            n_places, info, grads, mixed, tokens, grad_attended, other, small
        )

    (sent,) = weight_grads(1 - core)
    sent, back_sums, first_sums, second_sums, inner_bias_grad = together(
        sent, back_sums, first_sums, second_sums, inner_bias_grad
    )
    other = plane.swap(sent, 1)

    small = jnp.concatenate(
        [first_sums[:3], second_sums[:3], inner_bias_grad, jnp.sum(back_sums, axis=0)[:2]], axis=0
    )
    small = jnp.pad(small, ((0, -small.shape[0] % 16), (0, 0))).astype(bf16)
    small_rows = small.shape[0]

    small = add(small, plane.swap(small, 1))
    kept = list(weight_grads(core, other, small))
    arrived = plane.to_places(kept)
    kept[0], inner_on, outer_on = together(kept[0], inner_on, outer_on)
    feed_parts = [
        jnp.concatenate(
            [
                add(inner_stay[0, s], inner_came[0, s], inner_on[s]),
                add(outer_stay[0, s], outer_came[0, s], outer_on[s]),
            ],
            axis=1,
        )
        for s in range(n_z)
    ]
    feed_line = [plane.shift(feed_parts[s], -s) for s in others]
    output = copied(output)
    arrived, output = together(arrived, output)
    small = add(small, *[a[-small_rows:] for a in arrived])
    count = 2 * mine // n_places
    attention_parts = [
        add(*[a[s * count : (s + 1) * count] for a in [kept[0]] + arrived]) for s in range(n_z)
    ]
    attention_line = [
        plane.shift(jnp.concatenate([attention_parts[s], small], axis=0), s) for s in others
    ]
    feed_total = plane.over_groups(add(feed_parts[0], *feed_line))
    feed_arrived = plane.to_places([feed_total] * n_places)
    tokens_grad = copied(tokens_grad)
    attention_line, feed_arrived, tokens_grad = together(
        attention_line, feed_arrived, tokens_grad
    )
    attention_total = plane.over_groups(
        add(attention_parts[0], *[a[:count] for a in attention_line])
    )
    small = plane.over_groups(add(small, *[a[count:] for a in attention_line])).astype(f32)
    arrived = plane.to_places([attention_total] * n_places)
    feed_half = plane.from_places(feed_total, feed_arrived)
    feed_other = plane.swap(feed_half, 1)
    inner_grad, outer_grad = finish_feed(core.reshape(1), feed_half, feed_other)
    inner_bias_sum = lax.dynamic_slice_in_dim(small, 6 + z, 1, 0)[0]
    head_sums = lax.dynamic_slice_in_dim(small[6 + n_z : 8 + n_z], z * mine, mine, 1)
    arrived, inner_grad, outer_grad, small, inner_bias_sum, head_sums = together(
        arrived, inner_grad, outer_grad, small, inner_bias_sum, head_sums
    )
    attention_half = plane.from_places(attention_total, arrived)
    attention_other = plane.swap(attention_half, 1)
    grad_list = plane.by_core(attention_half, attention_other)
    grad_list = grad_list.reshape(2, n_places, 2, mine // n_places, width)
    grad_list = grad_list.transpose(0, 2, 1, 3, 4).reshape(4, mine, width)

    shared = small[:6]

    return (
        output,
        tokens_grad,
        grad_list[0].T.astype(f32),
        head_sums[0],
        grad_list[1].T.astype(f32),
        grad_list[2].T.astype(f32),
        head_sums[1],
        grad_list[3].astype(f32),
        shared[0],
        shared[1],
        shared[2],
        inner_grad,
        inner_bias_sum,
        outer_grad,
        shared[3],
        shared[4],
        shared[5],
    )


def solution(mesh):
    n_dp, n_z = mesh.shape["dp"], mesh.shape["tensor"]
    in_specs = (
        P("dp", None),
        P("dp", None),
        P("dp"),
        P(None, "tensor"),
        P("tensor"),
        P(None, "tensor"),
        P(None, "tensor"),
        P("tensor"),
        P("tensor", None),
        P(),
        P(),
        P(),
        P(None, "tensor"),
        P("tensor"),
        P("tensor", None),
        P(),
        P(),
        P(),
        P("dp", None),
    )
    out_specs = (
        P("dp", None),
        P("dp", None),
        P(None, "tensor"),
        P("tensor"),
        P(None, "tensor"),
        P(None, "tensor"),
        P("tensor"),
        P("tensor", None),
        P(),
        P(),
        P(),
        P(None, "tensor"),
        P("tensor"),
        P("tensor", None),
        P(),
        P(),
        P(),
    )

    def program(*args):
        return on_device(n_dp, n_z, *args)

    return jax.shard_map(
        program, mesh=mesh, in_specs=in_specs, out_specs=out_specs, check_vma=False
    )
```

```python
import functools

import jax
import jax.numpy as jnp
from jax import lax
from jax.experimental import pallas as pl
from jax.experimental.pallas import tpu as pltpu
from jax.sharding import PartitionSpec as P

HEAD = 64
BUCKET = 512
ITEMS = 8


negative_fill = -1e30
epsilon = 1e-06
f32 = jnp.float32
bf16 = jnp.bfloat16
VMEM_BYTES = 56 * 1024 * 1024


def dot(left, right):
    return jnp.dot(left, right, preferred_element_type=f32)


def contract_rows(left, right):
    return lax.dot_general(left, right, (((0,), (0,)), ((), ())), preferred_element_type=f32)


def contract_cols(left, right):
    return lax.dot_general(left, right, (((1,), (1,)), ((), ())), preferred_element_type=f32)


def norm_rows(values):
    centred = values - jnp.mean(values, axis=1, keepdims=True)
    inv_scale = lax.rsqrt(jnp.mean(centred * centred, axis=1, keepdims=True) + epsilon)
    return centred * inv_scale, inv_scale


def norm_back(grad_rows, norm_gain, normed, inv_scale):
    scaled = grad_rows * norm_gain
    return inv_scale * (
        scaled
        - jnp.mean(scaled, axis=1, keepdims=True)
        - normed * jnp.mean(scaled * normed, axis=1, keepdims=True)
    )


def column_sum(matrix):
    return jnp.sum(matrix.astype(f32), axis=0, keepdims=True)


def fixed(shape):
    return pl.BlockSpec(shape, lambda *_: (0,) * len(shape))


def cost(microseconds):
    return pl.CostEstimate(
        flops=int(microseconds * 2.5e8),
        bytes_accessed=int(microseconds * 2.5e5),
        transcendentals=0,
    )


def params(axes):
    return pltpu.CompilerParams(
        dimension_semantics=("arbitrary",) * axes, vmem_limit_bytes=VMEM_BYTES
    )


def item_places(lengths_ref, row, shape, axis):
    places = lax.broadcasted_iota(jnp.int32, shape, axis)
    end = jnp.int32(0)
    items = jnp.zeros(shape, jnp.int32)
    for slot in range(ITEMS):
        end = end + lengths_ref[row, slot]
        items = items + (places >= end).astype(jnp.int32)
    return items


def as_column(row):
    return jnp.broadcast_to(row.astype(f32), (8, row.shape[1])).T[:, :1]


def mask_bias(lengths_ref, row, key_mask):
    shape = (BUCKET, BUCKET)
    diagonal = lax.broadcasted_iota(jnp.int32, shape, 0) == lax.broadcasted_iota(
        jnp.int32, shape, 1
    )
    item_row = item_places(lengths_ref, row, (1, BUCKET), 1)
    item_column = item_places(lengths_ref, row, (BUCKET, 1), 0)
    code_column = jnp.where(as_column(key_mask) == 1.0, item_column, -1)
    return jnp.where((code_column == item_row) | diagonal, 0.0, negative_fill).astype(f32)


def attend_forward_kernel(
    lengths_ref, tokens_ref, query_ref, key_ref, value_ref, biases_ref, key_mask_ref, mixed_ref,
):
    mine = query_ref.shape[0]
    rows = tokens_ref[...]
    queries = contract_cols(query_ref[...], rows) + as_column(biases_ref[0:1, :mine])
    queries = (queries.astype(bf16) * HEAD ** (-0.5)).astype(bf16)
    keys = contract_cols(rows, key_ref[...]).astype(bf16)
    values = contract_cols(value_ref[...], rows) + as_column(biases_ref[0:1, mine : 2 * mine])
    values = values.astype(bf16)
    bias = mask_bias(lengths_ref, pl.program_id(0), key_mask_ref[0])
    for head in range(mine // HEAD):
        at = slice(head * HEAD, (head + 1) * HEAD)
        scores = dot(keys[:, at], queries[at]) + bias
        exponent = jnp.exp(scores - jnp.max(scores, axis=0, keepdims=True))
        total = jnp.sum(exponent, axis=0, keepdims=True)
        mixed_ref[0, 0, at] = (dot(values[at], exponent.astype(bf16)) / total).astype(bf16)
    mixed_ref[0, 0, mine:] = biases_ref[...]


def attend_forward(n_z, lengths, tokens, query, key, value, biases, key_mask):
    blocks = lengths.shape[0]
    own = blocks // n_z
    mine, width = key.shape
    whole = (n_z, own, mine + biases.shape[0], BUCKET)
    return pl.pallas_call(
        attend_forward_kernel,
        grid=(blocks,),
        in_specs=[
            pl.BlockSpec(memory_space=pltpu.SMEM),
            pl.BlockSpec((BUCKET, width), lambda b: (b, 0)),
            fixed((mine, width)),
            fixed((mine, width)),
            fixed((mine, width)),
            fixed(biases.shape),
            pl.BlockSpec((1, 1, BUCKET), lambda b: (b, 0, 0)),
        ],
        out_specs=pl.BlockSpec((1, 1) + whole[2:], lambda b: (b // own, b % own, 0, 0)),
        out_shape=jax.ShapeDtypeStruct(whole, bf16),
        compiler_params=params(1),
        name="attend_forward",
        cost_estimate=cost(12),
    )(lengths, tokens, query, key, value, biases, key_mask)


def fetch_units(step, picks, own_ref, halves, units, sems):
    feed_rows = units.shape[2]
    cut = feed_rows // 2

    def copies(number):
        slot = number % 2
        row = pl.multiple_of(picks[number] * feed_rows, 16)
        ends = [
            (own_ref.at[pl.ds(row, feed_rows)], units.at[slot, 0]),
            (halves[number][0], units.at[slot, 1:, :cut]),
            (halves[number][1], units.at[slot, 1:, cut:]),
        ]
        return [
            pltpu.make_async_copy(source, target, sems.at[slot, i])
            for i, (source, target) in enumerate(ends)
        ]

    for number in range(len(halves)):

        @pl.when(step == number)
        def _(number=number):
            if number == 0:
                for copy in copies(0):
                    copy.start()
            if number + 1 < len(halves):
                for copy in copies(number + 1):
                    copy.start()
            for copy in copies(number):
                copy.wait()

    return units.at[lax.rem(step, 2)]


def fetch_mixer(picks, own_ref, parts, mixer, sems):
    count = mixer.shape[1] // 8
    ends = [(own_ref, mixer.at[0])]
    for pick, part in zip(picks, parts):
        row = pl.multiple_of(pick * count, 16)
        ends.append((part, mixer.at[1:, pl.ds(row, count)]))
    copies = [
        pltpu.make_async_copy(source, target, sems.at[i])
        for i, (source, target) in enumerate(ends)
    ]
    for copy in copies:
        copy.start()
    for copy in copies:
        copy.wait()


def take_halves(numbers, refs):
    halves, refs = [], list(refs)
    for number in numbers:
        if number == 3:
            halves.append((refs.pop(0), refs.pop(0)))
        else:
            ref = refs.pop(0)
            cut = ref.shape[1] // 2
            halves.append((ref.at[:, :cut], ref.at[:, cut:]))
    return halves, refs


def split_units(units):
    width = units.shape[2] // 2
    return units[:, :, :width].reshape(-1, width), units[:, :, width:].reshape(-1, width)


ANYWHERE = pl.BlockSpec(memory_space=pl.ANY)


def feed_forward_kernel(chunks, first, last, info_ref, *rest):
    def take(count):
        nonlocal rest
        taken, rest = rest[:count], rest[count:]
        return taken

    vectors_ref, bias_ref, own_ref = take(3)
    halves, rest = take_halves([number for _, number in chunks], rest)
    if first:
        tokens_ref, mixed_ref, mixer_own_ref, *mixer_parts = take(11)
    else:
        normed_low_ref, start_ref, _, _ = take(4)
    if last:
        lengths_ref, cotangent_ref = take(2)
    hidden_ref, slope_ref = take(2)
    if first:
        normed_low_ref, first_normed_ref, first_scale_ref = take(3)
    if last:
        output_ref, grad_second_ref, grad_outer_ref, sums_ref = take(4)
    else:
        (second_sum,) = take(1)
    units, sems = take(2)
    if first:
        mixer, mixer_sems = take(2)
    if last:
        (second_sum,) = take(1)

    step = pl.program_id(0)
    picks = [(info_ref[1] ^ number) * 2 + (info_ref[2] ^ side) for side, number in chunks]
    weights = fetch_units(step, picks, own_ref, halves, units, sems)
    output_bias, first_gain, first_shift, outer_bias, second_gain, second_shift = (
        vectors_ref[i : i + 1, :] for i in range(6)
    )

    @pl.when(step == 0)
    def _():
        if first:
            all_picks = [
                (info_ref[1] ^ number) * 2 + (info_ref[2] ^ side)
                for side in range(2)
                for number in range(4)
            ]
            fetch_mixer(all_picks, mixer_own_ref, mixer_parts, mixer, mixer_sems)
            n_z, own, mine, _ = mixed_ref.shape
            attended = output_bias + jnp.concatenate(
                [
                    sum(
                        dot(mixer[s, :, :mine], mixed_ref[lax.rem(info_ref[0] + n_z - s, n_z), b])
                        for s in range(n_z)
                    ).T
                    for b in range(own)
                ],
                axis=0,
            )
            normed, inv_scale = norm_rows(tokens_ref[...].astype(f32) + attended)
            whole = normed * first_gain + first_shift
            first_normed_ref[...] = normed
            first_scale_ref[...] = inv_scale
            normed_low_ref[...] = whole.astype(bf16)
            second_sum[...] = whole + outer_bias
        else:
            second_sum[...] = start_ref[...]

    inner, outer = split_units(weights)
    inner_pre = contract_cols(normed_low_ref[...], inner) + bias_ref[0]
    normal_cdf = 0.5 + 0.5 * lax.erf(inner_pre * 0.7071067811865476)
    bell = jnp.exp(-0.5 * inner_pre * inner_pre)
    hidden = (inner_pre * normal_cdf).astype(bf16)
    hidden_ref[...] = hidden.T
    slope_ref[...] = (normal_cdf + inner_pre * bell * 0.3989422804014327).astype(bf16)
    second_sum[...] += dot(hidden, outer)

    if last:

        @pl.when(step == pl.num_programs(0) - 1)
        def _():
            normed, inv_scale = norm_rows(second_sum[...])
            blocks = normed.shape[0] // BUCKET
            live = jnp.concatenate(
                [
                    (item_places(lengths_ref, info_ref[0] * blocks + b, (BUCKET, 1), 0) < ITEMS)
                    for b in range(blocks)
                ],
                axis=0,
            ).astype(f32)
            output_ref[...] = ((normed * second_gain + second_shift) * live).astype(bf16)
            grad_final = cotangent_ref[...].astype(f32) * live
            grad_second = norm_back(grad_final, second_gain, normed, inv_scale)
            grad_outer = grad_second.astype(bf16)
            grad_second_ref[...] = grad_second
            grad_outer_ref[...] = grad_outer
            sums_ref[0:1, :] = column_sum(grad_outer)
            sums_ref[1:2, :] = column_sum(grad_final * normed)
            sums_ref[2:3, :] = column_sum(grad_final)


def feed_forward(chunks, info, vectors, biases, own, halves, first=None, going=None, last=None):
    width = vectors.shape[1]
    n_z = halves[0].shape[0] + 1
    feed_rows, twice = own.shape[0] // 8, 2 * width
    rows = first[1].shape[1] * BUCKET if first else going[0].shape[0]
    chunk = n_z * feed_rows
    whole = fixed((rows, width))
    my_rows = pl.BlockSpec((rows, width), lambda j, info: (info[0], 0))
    at = lambda j, info: info[3 + j]
    hidden_spec = pl.BlockSpec((chunk, rows), lambda j, info: (at(j, info), 0))
    slope_spec = pl.BlockSpec((rows, chunk), lambda j, info: (0, at(j, info)))
    in_specs = [
        fixed((8, width)),
        pl.BlockSpec((1, 1, chunk), lambda j, info: (at(j, info), 0, 0)),
        ANYWHERE,
    ] + [ANYWHERE] * len(halves)
    args = [vectors, biases, own] + halves
    shapes = [
        ((8 * chunk, rows), bf16, hidden_spec),
        ((rows, 8 * chunk), bf16, slope_spec),
    ]
    scratch = [
        pltpu.VMEM((2, n_z, feed_rows, twice), bf16),
        pltpu.SemaphoreType.DMA((2, 3)),
    ]
    aliases = {}
    if first:
        tokens, mixed, mixer_own, mixer_parts = first
        mine = width // n_z
        in_specs += [my_rows, fixed((n_z, mixed.shape[1], mine, BUCKET))] + [ANYWHERE] * 9
        args += [tokens, mixed, mixer_own] + mixer_parts
        shapes += [
            ((rows, width), bf16, whole),
            ((rows, width), f32, whole),
            ((rows, 1), f32, fixed((rows, 1))),
        ]
        scratch += [
            pltpu.VMEM((n_z,) + mixer_own.shape, bf16),
            pltpu.SemaphoreType.DMA((9,)),
        ]
    else:
        aliases = {1 + len(args) + 2: 0, 1 + len(args) + 3: 1}
        in_specs += [whole, whole, ANYWHERE, ANYWHERE]
        args += list(going)
    if last:
        in_specs += [pl.BlockSpec(memory_space=pltpu.SMEM), my_rows]
        args += list(last)
        shapes += [
            ((rows, width), bf16, whole),
            ((rows, width), f32, whole),
            ((rows, width), bf16, whole),
            ((8, width), f32, fixed((8, width))),
        ]
        scratch.append(pltpu.VMEM((rows, width), f32))
    else:
        shapes.append(((rows, width), f32, whole))
    info = jnp.concatenate(
        [info, jnp.array([4 * side + number for side, number in chunks], jnp.int32)]
    )
    return pl.pallas_call(
        functools.partial(feed_forward_kernel, chunks, first is not None, last is not None),
        grid_spec=pltpu.PrefetchScalarGridSpec(
            num_scalar_prefetch=1,
            grid=(len(chunks),),
            in_specs=in_specs,
            out_specs=[spec for _, _, spec in shapes],
            scratch_shapes=scratch,
        ),
        out_shape=[jax.ShapeDtypeStruct(shape, kind) for shape, kind, _ in shapes],
        input_output_aliases=aliases,
        compiler_params=params(1),
        name="feed_forward",
        cost_estimate=cost(3 * len(chunks)),
    )(info, *args)


STAY = ((0, 1), (0, 2))
GO = ((2, 3), (1, 3))


def feed_back_kernel(
    keeps, info_ref, grad_outer_ref, normed_low_ref, hidden_ref, slope_ref,
    own_ref, start_ref, *rest,
):
    halves, rest = take_halves(range(4), rest)
    if keeps:
        other_refs, norm_refs, rest = rest[:2], rest[2:5], rest[5:]
        stay_refs, go_refs, rest = rest[0:2], rest[2:4], rest[4:]
        bias_grad_ref, grad_first_ref, grad_attended_ref, sums_ref, units, sems = rest[:6]
        grad_normed_ref = rest[6]
    else:
        *grad_refs, bias_grad_ref, grad_normed_ref, units, sems = rest
    step = pl.program_id(0)
    side = info_ref[2] if keeps else 1 - info_ref[2]
    picks = [(info_ref[1] ^ number) * 2 + side for number in range(4)]
    weights = fetch_units(step, picks, own_ref, halves, units, sems)

    @pl.when(step == 0)
    def _():
        grad_normed_ref[...] = start_ref[...]

    n_z, feed_rows, twice = weights.shape
    width = twice // 2
    inner, outer = split_units(weights)
    grad_outer = grad_outer_ref[...]
    grad_hidden = contract_cols(grad_outer, outer)
    grad_inner = (grad_hidden * slope_ref[...].astype(f32)).astype(bf16)
    outer_grad = dot(hidden_ref[...], grad_outer).reshape(n_z, feed_rows, width)
    inner_grad = contract_rows(grad_inner, normed_low_ref[...]).reshape(n_z, feed_rows, width)
    bias_grad_ref[0] = column_sum(grad_inner)
    grad_normed_ref[...] += dot(grad_inner, inner)

    for number in range(4):

        @pl.when(step == number)
        def _(number=number):
            for track, value in enumerate((inner_grad, outer_grad)):
                at = slice(track * width, (track + 1) * width)
                if keeps:
                    found = value + other_refs[number // 2][0, :, :, at].astype(f32)
                    ref = stay_refs[track] if number in STAY[track] else go_refs[track]
                    ref[0] = found.astype(bf16)
                else:
                    grad_refs[number // 2][0, :, :, at] = value.astype(bf16)

    if keeps:

        @pl.when(step == pl.num_programs(0) - 1)
        def _():
            first_normed_ref, first_scale_ref, vectors_ref = norm_refs
            grad_rows, normed = grad_normed_ref[...], first_normed_ref[...]
            grad_first = norm_back(grad_rows, vectors_ref[1:2, :], normed, first_scale_ref[...])
            grad_attended = grad_first.astype(bf16)
            grad_first_ref[...] = grad_first
            grad_attended_ref[...] = grad_attended
            sums_ref[0:1, :] = column_sum(grad_attended)
            sums_ref[1:2, :] = column_sum(grad_rows * normed)
            sums_ref[2:3, :] = column_sum(grad_rows)


def feed_back(
    info, grad_outer, normed_low, hidden, slope, own, start, units, others=None, norm=None
):
    rows, width = grad_outer.shape
    keeps = others is not None
    count = 4
    feed_rows, twice = own.shape[0] // 8, 2 * width
    n_z = units[0].shape[0] + 1
    chunk = n_z * feed_rows
    flip = 0 if keeps else 1
    columns = pl.BlockSpec((rows, chunk), lambda i, info: (0, 4 * flip + i))
    whole = fixed((rows, width))
    part = (n_z, feed_rows, twice)
    track = (2, n_z, feed_rows, width)
    unit_rows = pl.BlockSpec((chunk, rows), lambda i, info: (4 * flip + i, 0))
    in_specs = [whole, whole, unit_rows, columns, ANYWHERE, whole] + [ANYWHERE] * len(units)
    args = [grad_outer, normed_low, hidden, slope, own, start] + units
    bias_shape = (
        (count, 1, chunk),
        f32,
        pl.BlockSpec((1, 1, chunk), lambda i, info: (i, 0, 0)),
    )
    scratch = [pltpu.VMEM((2,) + part, bf16), pltpu.SemaphoreType.DMA((2, 3))]

    def one(shape, at):
        return pl.BlockSpec((1,) + shape[1:], lambda i, info: (at(i), 0, 0, 0))

    early, late = (lambda i: jnp.minimum(i, 1)), (lambda i: jnp.maximum(i - 2, 0))
    pair = (2,) + part
    if keeps:
        in_specs += [one(pair, early), one(pair, late)]
        in_specs += [whole, fixed((rows, 1)), fixed((8, width))]
        args += list(others) + list(norm)
        slow, slower = (lambda i: i // 2), (lambda i: jnp.maximum(i - 1, 0) // 2)
        shapes = [(track, bf16, one(track, at)) for at in (early, slow, late, slower)] + [
            bias_shape,
            ((rows, width), f32, whole),
            ((rows, width), bf16, whole),
            ((8, width), f32, fixed((8, width))),
        ]
        scratch.append(pltpu.VMEM((rows, width), f32))
    else:
        shapes = [
            (pair, bf16, one(pair, early)),
            (pair, bf16, one(pair, late)),
            bias_shape,
            ((rows, width), f32, whole),
        ]
    return pl.pallas_call(
        functools.partial(feed_back_kernel, keeps),
        grid_spec=pltpu.PrefetchScalarGridSpec(
            num_scalar_prefetch=1,
            grid=(count,),
            in_specs=in_specs,
            out_specs=[spec for _, _, spec in shapes],
            scratch_shapes=scratch,
        ),
        out_shape=[jax.ShapeDtypeStruct(shape, kind) for shape, kind, _ in shapes],
        compiler_params=params(1),
        name="feed_back_own" if keeps else "feed_back",
        cost_estimate=cost(3 * count),
    )(info, *args)


def finish_feed_kernel(core_ref, own_ref, other_ref, inner_ref, outer_ref, inner_rows):
    places, count, twice = own_ref.shape
    width = twice // 2
    for source, side in ((own_ref, core_ref[0]), (other_ref, 1 - core_ref[0])):
        for place in range(places):
            row = pl.multiple_of((2 * place + side) * count, 16)
            inner_rows[pl.ds(row, count), :] = source[place, :, :width].astype(f32)
            outer_ref[pl.ds(row, count), :] = source[place, :, width:].astype(f32)
    inner_ref[...] = inner_rows[...].T


def finish_feed(core, own, other):
    places, count, twice = own.shape
    shape = (2 * places * count, twice // 2)
    inner_shape = (shape[1], shape[0])
    return pl.pallas_call(
        finish_feed_kernel,
        grid_spec=pltpu.PrefetchScalarGridSpec(
            num_scalar_prefetch=1,
            grid=(1,),
            in_specs=[fixed(own.shape), fixed(other.shape)],
            out_specs=[fixed(inner_shape), fixed(shape)],
            scratch_shapes=[pltpu.VMEM(shape, f32)],
        ),
        out_shape=[
            jax.ShapeDtypeStruct(inner_shape, f32),
            jax.ShapeDtypeStruct(shape, f32),
        ],
        compiler_params=params(1),
        name="finish_feed",
        cost_estimate=cost(5),
    )(core, own, other)


def copy_kernel(from_ref, to_ref):
    to_ref[...] = from_ref[...]


def copied(array):
    block = pl.BlockSpec((BUCKET, array.shape[1]), lambda i: (i, 0))
    return pl.pallas_call(
        copy_kernel,
        grid=(array.shape[0] // BUCKET,),
        in_specs=[block],
        out_specs=block,
        out_shape=jax.ShapeDtypeStruct(array.shape, array.dtype),
        compiler_params=params(1),
        name="copied",
        cost_estimate=cost(0.5),
    )(array)


def project_kernel(place_ref, tokens_ref, weights_ref, biases_ref, query_ref, key_ref, value_ref):
    rows = tokens_ref[...]
    width = rows.shape[1]
    queries = contract_cols(weights_ref[:, :width], rows) + as_column(biases_ref[0:1, :])
    query_ref[...] = (queries.astype(bf16) * HEAD ** (-0.5)).astype(bf16)
    key_ref[...] = contract_cols(rows, weights_ref[:, width : 2 * width]).astype(bf16)
    values = contract_cols(rows, weights_ref[:, 2 * width :]) + biases_ref[1:2, :]
    value_ref[...] = values.astype(bf16)


def project(place, tokens, weights, biases, buckets):
    width = tokens.shape[1]
    part = width // 3
    shapes = [
        ((buckets, width, BUCKET), pl.BlockSpec((None, part, BUCKET), lambda b, j, _: (b, j, 0))),
        ((buckets * BUCKET, width), pl.BlockSpec((BUCKET, part), lambda b, j, _: (b, j))),
        ((buckets * BUCKET, width), pl.BlockSpec((BUCKET, part), lambda b, j, _: (b, j))),
    ]
    return pl.pallas_call(
        project_kernel,
        grid_spec=pltpu.PrefetchScalarGridSpec(
            num_scalar_prefetch=1,
            grid=(buckets, 3),
            in_specs=[
                pl.BlockSpec((BUCKET, width), lambda b, j, place: (place[0] * buckets + b, 0)),
                pl.BlockSpec((part, 3 * width), lambda b, j, place: (j, 0)),
                pl.BlockSpec((8, part), lambda b, j, place: (0, j)),
            ],
            out_specs=[spec for _, spec in shapes],
        ),
        out_shape=[jax.ShapeDtypeStruct(shape, bf16) for shape, _ in shapes],
        compiler_params=params(2),
        name="project",
        cost_estimate=cost(5),
    )(place, tokens, weights, biases)


def attend_back_kernel(
    place_ref, lengths_ref, grad_attended_ref, grad_first_ref, weights_ref, query_ref, key_ref,
    value_ref, key_mask_ref,
    grads_ref, tokens_grad_ref, sums_ref,
    bias, grad_mixed_t, whole, weights, sem,
):
    pair = pl.program_id(1)
    pairs, width = whole.shape[1], weights.shape[0]
    fetch = pltpu.make_async_copy(weights_ref, weights, sem)

    @pl.when(pair == 0)
    def _():
        fetch.start()
        row = place_ref[0] * pl.num_programs(0) + pl.program_id(0)
        bias[...] = mask_bias(lengths_ref, row, key_mask_ref[0])
        fetch.wait()
        grad_mixed_t[...] = contract_cols(
            weights[:, 3 * width :], grad_attended_ref[...]
        ).astype(bf16)

    queries, keys, values = query_ref[...], key_ref[...], value_ref[...]
    start = pl.multiple_of(pair * keys.shape[1], 128)
    grad_mixed = grad_mixed_t[pl.ds(start, keys.shape[1]), :]
    keys_t = keys.T
    grad_queries, grad_keys, grad_values = [], [], []
    for head in range(keys.shape[1] // HEAD):
        at = slice(head * HEAD, (head + 1) * HEAD)
        scores = dot(keys[:, at], queries[at]) + bias[...]
        exponent = jnp.exp(scores - jnp.max(scores, axis=0, keepdims=True))
        probs = exponent * (1.0 / jnp.sum(exponent, axis=0, keepdims=True))
        grad_probs = dot(values[:, at], grad_mixed[at])
        shift = jnp.sum(probs * grad_probs, axis=0, keepdims=True)
        grad_scores = (probs * (grad_probs - shift)).astype(bf16)
        grad_values.append(contract_cols(probs.astype(bf16), grad_mixed[at]))
        grad_keys.append(contract_cols(grad_scores, queries[at]))
        grad_queries.append(dot(keys_t[at], grad_scores) * HEAD ** (-0.5))
    query_t = jnp.concatenate(grad_queries, axis=0).astype(bf16)
    found = (
        query_t.T,
        jnp.concatenate(grad_keys, axis=1).astype(bf16),
        jnp.concatenate(grad_values, axis=1).astype(bf16),
    )
    for number, grad in enumerate(found):
        grads_ref[number, 0] = query_t if number == 0 else grad.T
        whole[number, pair] = grad
    sums_ref[0, 0:1, :] = column_sum(found[0])
    sums_ref[0, 1:2, :] = column_sum(found[2])

    @pl.when(pair == pl.num_programs(1) - 1)
    def _():
        total = grad_first_ref[...]
        for number in range(3):
            grad = jnp.concatenate([whole[number, i] for i in range(pairs)], axis=1)
            total += dot(grad, weights[:, number * width : (number + 1) * width])
        tokens_grad_ref[...] = total.astype(bf16)


def attend_back(place, lengths, grad_attended, grad_first, weights, queries, keys, values, key_mask):
    rows, width = grad_attended.shape
    blocks = rows // BUCKET
    pair = 2 * HEAD
    by_bucket = pl.BlockSpec((BUCKET, width), lambda b, h, place: (b, 0))
    by_pair = pl.BlockSpec((BUCKET, pair), lambda b, h, place: (b, h))
    return pl.pallas_call(
        attend_back_kernel,
        grid_spec=pltpu.PrefetchScalarGridSpec(
            num_scalar_prefetch=1,
            grid=(blocks, width // pair),
            in_specs=[
                pl.BlockSpec(memory_space=pltpu.SMEM),
                by_bucket,
                by_bucket,
                ANYWHERE,
                pl.BlockSpec((None, pair, BUCKET), lambda b, h, place: (b, h, 0)),
                by_pair,
                by_pair,
                pl.BlockSpec((1, 1, BUCKET), lambda b, h, place: (place[0] * blocks + b, 0, 0)),
            ],
            out_specs=[
                pl.BlockSpec((3, 1, pair, BUCKET), lambda b, h, place: (0, b, h, 0)),
                by_bucket,
                pl.BlockSpec((1, 8, pair), lambda b, h, place: (b, 0, h)),
            ],
            scratch_shapes=[
                pltpu.VMEM((BUCKET, BUCKET), f32),
                pltpu.VMEM((width, BUCKET), bf16),
                pltpu.VMEM((3, width // pair, BUCKET, pair), bf16),
                pltpu.VMEM(weights.shape, bf16),
                pltpu.SemaphoreType.DMA(()),
            ],
        ),
        out_shape=[
            jax.ShapeDtypeStruct((3, blocks, width, BUCKET), bf16),
            jax.ShapeDtypeStruct((rows, width), bf16),
            jax.ShapeDtypeStruct((blocks, 8, width), f32),
        ],
        compiler_params=params(2),
        name="attend_back",
        cost_estimate=cost(20),
    )(place, lengths, grad_attended, grad_first, weights, queries, keys, values, key_mask)


def attention_grads_kernel(
    n_places, adds, info_ref, grads_ref, mixed_ref, tokens_ref, grad_attended_ref, *rest
):
    if adds:
        other_refs, small_ref, rest = rest[:n_places], rest[n_places], rest[n_places + 1 :]
    out_refs, whole = rest[:-1], rest[-1]
    step = pl.program_id(0)
    which = info_ref[step]
    n_z, buckets, mine, _ = mixed_ref.shape
    count = mine // n_places

    @pl.when(which < 3)
    def _():
        whole[...] = sum(
            dot(grads_ref[0, b], tokens_ref[b * BUCKET : (b + 1) * BUCKET, :])
            for b in range(buckets)
        ).astype(bf16)

    @pl.when(which == 3)
    def _():
        for t in range(n_z):
            whole[t * mine : (t + 1) * mine, :] = sum(
                dot(mixed_ref[t, b], grad_attended_ref[b * BUCKET : (b + 1) * BUCKET, :])
                for b in range(buckets)
            ).astype(bf16)

    for number in range(n_places):
        for s in range(n_z):
            start = lax.rem(info_ref[2] + s, n_z) * mine + (info_ref[3] ^ number) * count
            value = whole[pl.ds(pl.multiple_of(start, 16), count), :]
            if adds:
                value = value.astype(f32) + other_refs[number][s, 0].astype(f32)
                row = (2 * s + step) * count
                out_refs[number][pl.ds(pl.multiple_of(row, 16), count), :] = value.astype(bf16)
            else:
                out_refs[number][s, 0] = value

    if adds:
        for number in range(n_places):
            out_refs[number][2 * n_z * count :, :] = small_ref[...]


def attention_grads(n_places, info, grads, mixed, tokens, grad_attended, other=None, small=None):
    rows, width = grad_attended.shape
    n_z, buckets = mixed.shape[:2]
    mine = width // n_z
    count = mine // n_places
    by_step = pl.BlockSpec((n_z, 1, count, width), lambda i, info: (0, i, 0, 0))
    in_specs = [
        pl.BlockSpec(
            (1, buckets, width, BUCKET), lambda i, info: (jnp.minimum(info[i], 2), 0, 0, 0)
        ),
        fixed((n_z, buckets, mine, BUCKET)),
        pl.BlockSpec((rows, width), lambda i, info: (info[2], 0)),
        fixed((rows, width)),
    ]
    args = [grads, mixed, tokens, grad_attended]
    if other is None:
        shapes = [((n_z, 2, count, width), by_step)] * n_places
    else:
        in_specs += [by_step] * n_places + [fixed(small.shape)]
        args += list(other) + [small]
        flat = (2 * n_z * count + small.shape[0], width)
        shapes = [(flat, fixed(flat))] * n_places
    return pl.pallas_call(
        functools.partial(attention_grads_kernel, n_places, other is not None),
        grid_spec=pltpu.PrefetchScalarGridSpec(
            num_scalar_prefetch=1,
            grid=(2,),
            in_specs=in_specs,
            out_specs=[spec for _, spec in shapes],
            scratch_shapes=[pltpu.VMEM((width, width), bf16)],
        ),
        out_shape=[jax.ShapeDtypeStruct(shape, bf16) for shape, _ in shapes],
        compiler_params=params(1),
        name="attention_grads",
        cost_estimate=cost(0.5),
    )(info, *args)


def together(*values):
    return lax.optimization_barrier(values)


def add(first, *others):
    total = first.astype(f32)
    for other in others:
        total = total + other.astype(f32)
    return total.astype(bf16)


class Plane:
    def __init__(self, n_dp, n_z):
        self.n_dp, self.n_z = n_dp, n_z
        self.n_group = min(n_dp, 8)
        self.n_places = self.n_group // 2
        self.dp = lax.axis_index("dp")
        self.z = lax.axis_index("tensor")
        self.index = lax.rem(self.dp, self.n_group)
        self.core = self.index & 1
        self.place = self.index >> 1

    def swap(self, array, bits):
        return lax.ppermute(array, "dp", [(i, i ^ bits) for i in range(self.n_dp)])

    def shift(self, array, by):
        n = self.n_z
        return lax.ppermute(array, "tensor", [(i, (i + by) % n) for i in range(n)])

    def gather(self, piece):
        if self.n_dp == self.n_group:
            whole = lax.all_gather(piece, ("tensor", "dp"))
            return whole.reshape((self.n_z, self.n_group) + piece.shape)
        groups = [
            list(range(i, i + self.n_group)) for i in range(0, self.n_dp, self.n_group)
        ]
        line = lax.all_gather(piece, "tensor")
        return lax.all_gather(line, "dp", axis=1, axis_index_groups=groups)

    def turned(self, array):
        bit = 1
        while bit < self.n_group:
            lead = array.reshape((-1, 2, bit) + array.shape[1:])
            array = jnp.where((self.index & bit) != 0, lead[:, ::-1], lead).reshape(array.shape)
            bit *= 2
        return array

    def to_places(self, parts):
        return [self.swap(parts[number], 2 * number) for number in range(1, self.n_places)]

    def from_places(self, own, arrived):
        found = jnp.stack([own] + arrived)
        bit = 1
        while bit < self.n_places:
            lead = found.reshape((-1, 2, bit) + own.shape)
            flipped = lead[:, ::-1]
            found = jnp.where((self.place & bit) != 0, flipped, lead).reshape(found.shape)
            bit *= 2
        return found

    def by_core(self, own, other):
        return jnp.where(
            self.core == 1, jnp.stack([other, own]), jnp.stack([own, other])
        )

    def over_groups(self, array):
        bit = self.n_group
        while bit < self.n_dp:
            array = add(array, self.swap(array, bit))
            bit *= 2
        return array


def on_device(
    n_dp,
    n_z,
    tokens,
    lengths,
    key_mask,
    query_weight,
    query_bias,
    key_weight,
    value_weight,
    value_bias,
    output_weight,
    output_bias,
    first_gain,
    first_shift,
    inner_weight,
    inner_bias,
    outer_weight,
    outer_bias,
    second_gain,
    second_shift,
    cotangent,
):
    width = tokens.shape[1]
    mine = query_weight.shape[1]
    units = inner_weight.shape[1]
    all_rows = tokens.shape[0]
    all_blocks = all_rows // BUCKET
    rows = all_rows // n_z
    plane = Plane(n_dp, n_z)
    z, core, place, index = plane.z, plane.core, plane.place, plane.index
    n_places = plane.n_places
    others = range(1, n_z)

    feed_rows = units // plane.n_group
    head_rows = mine // plane.n_group
    mixer_t = jnp.pad(output_weight.T, ((0, 0), (0, -mine % 128)))
    mixer_count = width // plane.n_group
    piece = jnp.concatenate(
        [
            lax.dynamic_slice_in_dim(inner_weight, index * feed_rows, feed_rows, 1).T,
            lax.dynamic_slice_in_dim(outer_weight, index * feed_rows, feed_rows, 0),
            lax.dynamic_slice_in_dim(mixer_t, index * feed_rows, feed_rows, 0),
        ],
        axis=1,
    )
    line = [plane.shift(piece, s) for s in others]

    query_t, key_t, value_t = query_weight.T, key_weight.T, value_weight.T
    attention_piece = jnp.concatenate(
        [
            lax.dynamic_slice_in_dim(weight, index * head_rows, head_rows, 0)
            for weight in (query_t, key_t, value_t, output_weight)
        ],
        axis=1,
    )
    attention_weights = plane.gather(attention_piece).reshape(width, 4 * width)

    key_mask_rows = key_mask.reshape(all_blocks, 1, BUCKET)
    bias_row = jnp.concatenate([query_bias, value_bias, inner_bias])
    bias_rows = jnp.pad(bias_row, (0, 16 * BUCKET - bias_row.shape[0])).reshape(16, BUCKET)
    place_z = z.reshape(1)
    mixed = attend_forward(
        n_z, lengths, tokens, query_t, key_t, value_t, bias_rows, key_mask_rows
    )
    mixed, line = together(mixed, line)

    near = jnp.stack([part[:, : 2 * width] for part in line])
    by_x, by_y = plane.swap(near, 2), plane.swap(near, 4)

    mixer_keep = [jnp.stack([part[:, 2 * width :] for part in line])]
    mixed, mixer_keep[0] = together(mixed, mixer_keep[0])
    mixed = lax.all_to_all(mixed, "tensor", 0, 0)
    mixer_keep += plane.to_places(mixer_keep * n_places)
    mixer_send = [plane.swap(part, 1) for part in mixer_keep]
    own_units = jnp.concatenate([inner_weight.T, outer_weight], axis=1)

    biases = mixed[:, 0, mine:].reshape(n_z, -1)[:, : bias_row.shape[0]].astype(f32)
    head_biases = jnp.pad(
        jnp.stack([biases[:, :mine].reshape(-1), biases[:, mine : 2 * mine].reshape(-1)]),
        ((0, 6), (0, 0)),
    )
    inner_biases = biases[:, 2 * mine :]
    inner_biases = jnp.concatenate(
        [
            lax.dynamic_slice_in_dim(inner_biases, lax.rem(z + n_z - s, n_z), 1, 0)
            for s in range(n_z)
        ],
        axis=0,
    )
    inner_biases = inner_biases.reshape(n_z, plane.n_group, feed_rows).transpose(1, 0, 2)
    inner_biases = plane.turned(inner_biases).reshape(n_places, 2, 1, n_z * feed_rows)
    inner_biases = inner_biases.transpose(1, 0, 2, 3).reshape(plane.n_group, 1, -1)
    vectors = jnp.stack(
        [output_bias, first_gain, first_shift, outer_bias, second_gain, second_shift]
        + [jnp.zeros_like(output_bias)] * 2
    ).astype(f32)

    info = jnp.stack([z, place, core])
    shared_args = (info, vectors, inner_biases, own_units)
    cut = feed_rows // 2
    far = [plane.swap(by_x[:, :cut], 4), plane.swap(by_y[:, cut:], 2)]
    send = [plane.swap(units_of, 1) for units_of in (near, by_x, by_y)]
    hidden, slope, normed_low, first_normed, first_scale, second_sum = feed_forward(
        ((0, 0), (0, 1), (0, 2), (1, 0), (1, 1), (1, 2)),
        *shared_args,
        [near, by_x, by_y] + send,
        first=(tokens, mixed, mixer_t, mixer_keep + mixer_send),
    )
    second_sum, far = together(second_sum, far)
    far_send = [plane.swap(half, 1) for half in far]
    keep = [near, by_x, by_y] + far
    send = send + far_send
    hidden, slope, my_output, grad_second, grad_outer, second_sums = feed_forward(
        ((0, 3), (1, 3)), *shared_args, far + far_send,
        going=(normed_low, second_sum, hidden, slope), last=(lengths, cotangent),
    )
    my_output, attention_weights = together(my_output, attention_weights)
    output = lax.all_gather(my_output, "tensor", axis=0, tiled=True)

    shared_args = (info, grad_outer, normed_low, hidden, slope, own_units)
    sent_early, sent_late, bias_sent, grad_normed = feed_back(*shared_args, grad_second, send)
    other = [plane.swap(sent_early, 1), plane.swap(sent_late, 1)]
    grad_normed, head_biases, tokens = together(grad_normed, head_biases, tokens)
    projected = project(place_z, tokens, attention_weights, head_biases, rows // BUCKET)
    projected, other = together(projected, other)
    (
        inner_stay, outer_stay, inner_go, outer_go, bias_kept, grad_first, grad_attended, first_sums
    ) = feed_back(
        *shared_args, grad_normed, keep, other,
        (first_normed, first_scale, vectors),
    )
    inner_came, outer_came = plane.swap(inner_go, 4), plane.swap(outer_go, 2)
    bias_grads = jnp.stack(
        [bias_kept[:, 0], bias_sent[:, 0]], axis=1
    )
    inner_bias_grad = plane.turned(bias_grads.reshape(plane.n_group, n_z, feed_rows))
    inner_bias_grad = inner_bias_grad.transpose(1, 0, 2)
    inner_bias_grad = jnp.concatenate(
        [
            sum(
                jnp.where(lax.rem(z - t + n_z, n_z) == s, inner_bias_grad[s : s + 1], 0.0)
                for s in range(n_z)
            )
            for t in range(n_z)
        ],
        axis=0,
    ).reshape(n_z, units)

    grads, my_tokens_grad, back_sums = attend_back(
        place_z, lengths, grad_attended, grad_first, attention_weights, *projected, key_mask_rows
    )
    grads, inner_came, outer_came, output = together(grads, inner_came, outer_came, output)
    inner_on, outer_on = (
        plane.swap(add(inner_stay[1], inner_came[1]), 2),
        plane.swap(add(outer_stay[1], outer_came[1]), 4),
    )
    tokens_grad = lax.all_gather(my_tokens_grad, "tensor", axis=0, tiled=True)

    def weight_grads(side, other=None, small=None):
        info = jnp.stack([2 * side, 2 * side + 1, z, place])
        return attention_grads(
            n_places, info, grads, mixed, tokens, grad_attended, other, small
        )

    sent = weight_grads(1 - core)
    sent, back_sums, first_sums, second_sums, inner_bias_grad = together(
        sent, back_sums, first_sums, second_sums, inner_bias_grad
    )
    other = [plane.swap(part, 1) for part in sent]

    small = jnp.concatenate(
        [first_sums[:3], second_sums[:3], inner_bias_grad, jnp.sum(back_sums, axis=0)[:2]], axis=0
    )
    small = jnp.pad(small, ((0, -small.shape[0] % 16), (0, 0))).astype(bf16)
    small_rows = small.shape[0]

    small = add(small, plane.swap(small, 1))
    kept = list(weight_grads(core, other, small))
    arrived = plane.to_places(kept)
    kept[0], inner_on, outer_on = together(kept[0], inner_on, outer_on)
    feed_parts = [
        jnp.concatenate(
            [
                add(inner_stay[0, s], inner_came[0, s], inner_on[s]),
                add(outer_stay[0, s], outer_came[0, s], outer_on[s]),
            ],
            axis=1,
        )
        for s in range(n_z)
    ]
    feed_line = [plane.shift(feed_parts[s], -s) for s in others]
    output = copied(output)
    arrived, output = together(arrived, output)
    small = add(small, *[a[-small_rows:] for a in arrived])
    count = 2 * mine // n_places
    attention_parts = [
        add(*[a[s * count : (s + 1) * count] for a in [kept[0]] + arrived]) for s in range(n_z)
    ]
    attention_line = [
        plane.shift(jnp.concatenate([attention_parts[s], small], axis=0), s) for s in others
    ]
    feed_total = plane.over_groups(add(feed_parts[0], *feed_line))
    feed_arrived = plane.to_places([feed_total] * n_places)
    tokens_grad = copied(tokens_grad)
    attention_line, feed_arrived, tokens_grad = together(
        attention_line, feed_arrived, tokens_grad
    )
    attention_total = plane.over_groups(
        add(attention_parts[0], *[a[:count] for a in attention_line])
    )
    small = plane.over_groups(add(small, *[a[count:] for a in attention_line])).astype(f32)
    arrived = plane.to_places([attention_total] * n_places)
    feed_half = plane.from_places(feed_total, feed_arrived)
    feed_other = plane.swap(feed_half, 1)
    inner_grad, outer_grad = finish_feed(core.reshape(1), feed_half, feed_other)
    inner_bias_sum = lax.dynamic_slice_in_dim(small, 6 + z, 1, 0)[0]
    head_sums = lax.dynamic_slice_in_dim(small[6 + n_z : 8 + n_z], z * mine, mine, 1)
    arrived, inner_grad, outer_grad, small, inner_bias_sum, head_sums = together(
        arrived, inner_grad, outer_grad, small, inner_bias_sum, head_sums
    )
    attention_half = plane.from_places(attention_total, arrived)
    attention_other = plane.swap(attention_half, 1)
    grad_list = plane.by_core(attention_half, attention_other)
    grad_list = grad_list.reshape(2, n_places, 2, mine // n_places, width)
    grad_list = grad_list.transpose(0, 2, 1, 3, 4).reshape(4, mine, width)

    shared = small[:6]

    return (
        output,
        tokens_grad,
        grad_list[0].T.astype(f32),
        head_sums[0],
        grad_list[1].T.astype(f32),
        grad_list[2].T.astype(f32),
        head_sums[1],
        grad_list[3].astype(f32),
        shared[0],
        shared[1],
        shared[2],
        inner_grad,
        inner_bias_sum,
        outer_grad,
        shared[3],
        shared[4],
        shared[5],
    )


def solution(mesh):
    n_dp, n_z = mesh.shape["dp"], mesh.shape["tensor"]
    in_specs = (
        P("dp", None),
        P("dp", None),
        P("dp"),
        P(None, "tensor"),
        P("tensor"),
        P(None, "tensor"),
        P(None, "tensor"),
        P("tensor"),
        P("tensor", None),
        P(),
        P(),
        P(),
        P(None, "tensor"),
        P("tensor"),
        P("tensor", None),
        P(),
        P(),
        P(),
        P("dp", None),
    )
    out_specs = (
        P("dp", None),
        P("dp", None),
        P(None, "tensor"),
        P("tensor"),
        P(None, "tensor"),
        P(None, "tensor"),
        P("tensor"),
        P("tensor", None),
        P(),
        P(),
        P(),
        P(None, "tensor"),
        P("tensor"),
        P("tensor", None),
        P(),
        P(),
        P(),
    )

    def program(*args):
        return on_device(n_dp, n_z, *args)

    return jax.shard_map(
        program, mesh=mesh, in_specs=in_specs, out_specs=out_specs, check_vma=False
    )
```

```python
import functools

import jax
import jax.numpy as jnp
from jax import lax
from jax.experimental import pallas as pl
from jax.experimental.pallas import tpu as pltpu
from jax.sharding import PartitionSpec as P

HEAD = 64
BUCKET = 512
ITEMS = 8


negative_fill = -1e30
epsilon = 1e-06
f32 = jnp.float32
bf16 = jnp.bfloat16
VMEM_BYTES = 56 * 1024 * 1024


def dot(left, right):
    return jnp.dot(left, right, preferred_element_type=f32)


def contract_rows(left, right):
    return lax.dot_general(left, right, (((0,), (0,)), ((), ())), preferred_element_type=f32)


def contract_cols(left, right):
    return lax.dot_general(left, right, (((1,), (1,)), ((), ())), preferred_element_type=f32)


def norm_rows(values):
    centred = values - jnp.mean(values, axis=1, keepdims=True)
    inv_scale = lax.rsqrt(jnp.mean(centred * centred, axis=1, keepdims=True) + epsilon)
    return centred * inv_scale, inv_scale


def norm_back(grad_rows, norm_gain, normed, inv_scale):
    scaled = grad_rows * norm_gain
    return inv_scale * (
        scaled
        - jnp.mean(scaled, axis=1, keepdims=True)
        - normed * jnp.mean(scaled * normed, axis=1, keepdims=True)
    )


def column_sum(matrix):
    return jnp.sum(matrix.astype(f32), axis=0, keepdims=True)


def fixed(shape):
    return pl.BlockSpec(shape, lambda *_: (0,) * len(shape))


def cost(microseconds):
    return pl.CostEstimate(
        flops=int(microseconds * 2.5e8),
        bytes_accessed=int(microseconds * 2.5e5),
        transcendentals=0,
    )


def params(axes):
    return pltpu.CompilerParams(
        dimension_semantics=("arbitrary",) * axes, vmem_limit_bytes=VMEM_BYTES
    )


def item_places(lengths_ref, row, shape, axis):
    places = lax.broadcasted_iota(jnp.int32, shape, axis)
    end = jnp.int32(0)
    items = jnp.zeros(shape, jnp.int32)
    for slot in range(ITEMS):
        end = end + lengths_ref[row, slot]
        items = items + (places >= end).astype(jnp.int32)
    return items


def as_column(row):
    return jnp.broadcast_to(row.astype(f32), (8, row.shape[1])).T[:, :1]


def mask_bias(lengths_ref, row, key_mask):
    shape = (BUCKET, BUCKET)
    diagonal = lax.broadcasted_iota(jnp.int32, shape, 0) == lax.broadcasted_iota(
        jnp.int32, shape, 1
    )
    item_row = item_places(lengths_ref, row, (1, BUCKET), 1)
    item_column = item_places(lengths_ref, row, (BUCKET, 1), 0)
    code_column = jnp.where(as_column(key_mask) == 1.0, item_column, -1)
    return jnp.where((code_column == item_row) | diagonal, 0.0, negative_fill).astype(f32)


def attend_forward_kernel(
    lengths_ref, tokens_ref, query_ref, key_ref, value_ref, biases_ref, key_mask_ref, mixed_ref,
):
    mine = query_ref.shape[0]
    rows = tokens_ref[...]
    queries = contract_cols(query_ref[...], rows) + as_column(biases_ref[0:1, :mine])
    queries = (queries.astype(bf16) * HEAD ** (-0.5)).astype(bf16)
    keys = contract_cols(rows, key_ref[...]).astype(bf16)
    values = contract_cols(value_ref[...], rows) + as_column(biases_ref[0:1, mine : 2 * mine])
    values = values.astype(bf16)
    bias = mask_bias(lengths_ref, pl.program_id(0), key_mask_ref[0])
    for head in range(mine // HEAD):
        at = slice(head * HEAD, (head + 1) * HEAD)
        scores = dot(keys[:, at], queries[at]) + bias
        exponent = jnp.exp(scores - jnp.max(scores, axis=0, keepdims=True))
        total = jnp.sum(exponent, axis=0, keepdims=True)
        mixed_ref[0, 0, at] = (dot(values[at], exponent.astype(bf16)) / total).astype(bf16)
    mixed_ref[0, 0, mine:] = biases_ref[...]


def attend_forward(n_z, lengths, tokens, query, key, value, biases, key_mask):
    blocks = lengths.shape[0]
    own = blocks // n_z
    mine, width = key.shape
    whole = (n_z, own, mine + biases.shape[0], BUCKET)
    return pl.pallas_call(
        attend_forward_kernel,
        grid=(blocks,),
        in_specs=[
            pl.BlockSpec(memory_space=pltpu.SMEM),
            pl.BlockSpec((BUCKET, width), lambda b: (b, 0)),
            fixed((mine, width)),
            fixed((mine, width)),
            fixed((mine, width)),
            fixed(biases.shape),
            pl.BlockSpec((1, 1, BUCKET), lambda b: (b, 0, 0)),
        ],
        out_specs=pl.BlockSpec((1, 1) + whole[2:], lambda b: (b // own, b % own, 0, 0)),
        out_shape=jax.ShapeDtypeStruct(whole, bf16),
        compiler_params=params(1),
        name="attend_forward",
        cost_estimate=cost(12),
    )(lengths, tokens, query, key, value, biases, key_mask)


def fetch_units(step, picks, own_ref, halves, units, sems):
    feed_rows = units.shape[2]
    cut = feed_rows // 2

    def copies(number):
        slot = number % 2
        row = pl.multiple_of(picks[number] * feed_rows, 16)
        ends = [
            (own_ref.at[pl.ds(row, feed_rows)], units.at[slot, 0]),
            (halves[number][0], units.at[slot, 1:, :cut]),
            (halves[number][1], units.at[slot, 1:, cut:]),
        ]
        return [
            pltpu.make_async_copy(source, target, sems.at[slot, i])
            for i, (source, target) in enumerate(ends)
        ]

    for number in range(len(halves)):

        @pl.when(step == number)
        def _(number=number):
            if number == 0:
                for copy in copies(0):
                    copy.start()
            if number + 1 < len(halves):
                for copy in copies(number + 1):
                    copy.start()
            for copy in copies(number):
                copy.wait()

    return units.at[lax.rem(step, 2)]


def take_halves(numbers, refs):
    halves, refs = [], list(refs)
    for number in numbers:
        if number == 3:
            halves.append((refs.pop(0), refs.pop(0)))
        else:
            ref = refs.pop(0)
            cut = ref.shape[1] // 2
            halves.append((ref.at[:, :cut], ref.at[:, cut:]))
    return halves, refs


def split_units(units):
    width = units.shape[2] // 2
    return units[:, :, :width].reshape(-1, width), units[:, :, width:].reshape(-1, width)


ANYWHERE = pl.BlockSpec(memory_space=pl.ANY)


def feed_forward_kernel(chunks, first, last, info_ref, *rest):
    def take(count):
        nonlocal rest
        taken, rest = rest[:count], rest[count:]
        return taken

    vectors_ref, bias_ref, own_ref = take(3)
    halves, rest = take_halves([number for _, number in chunks], rest)
    if first:
        tokens_ref, mixed_ref, mixer_ref = take(3)
    else:
        normed_low_ref, start_ref, _, _ = take(4)
    if last:
        lengths_ref, cotangent_ref = take(2)
    hidden_ref, slope_ref = take(2)
    if first:
        normed_low_ref, first_normed_ref, first_scale_ref = take(3)
    if last:
        output_ref, grad_second_ref, grad_outer_ref, sums_ref = take(4)
    else:
        (second_sum,) = take(1)
    units, sems = take(2)
    if last:
        (second_sum,) = take(1)

    step = pl.program_id(0)
    picks = [(info_ref[1] ^ number) * 2 + (info_ref[2] ^ side) for side, number in chunks]
    weights = fetch_units(step, picks, own_ref, halves, units, sems)
    output_bias, first_gain, first_shift, outer_bias, second_gain, second_shift = (
        vectors_ref[i : i + 1, :] for i in range(6)
    )

    @pl.when(step == 0)
    def _():
        if first:
            n_z, own, mine, _ = mixed_ref.shape
            attended = output_bias + jnp.concatenate(
                [
                    sum(
                        contract_rows(mixed_ref[t, b], mixer_ref[t * mine : (t + 1) * mine, :])
                        for t in range(n_z)
                    )
                    for b in range(own)
                ],
                axis=0,
            )
            normed, inv_scale = norm_rows(tokens_ref[...].astype(f32) + attended)
            whole = normed * first_gain + first_shift
            first_normed_ref[...] = normed
            first_scale_ref[...] = inv_scale
            normed_low_ref[...] = whole.astype(bf16)
            second_sum[...] = whole + outer_bias
        else:
            second_sum[...] = start_ref[...]

    inner, outer = split_units(weights)
    inner_pre = contract_cols(normed_low_ref[...], inner) + bias_ref[0]
    normal_cdf = 0.5 + 0.5 * lax.erf(inner_pre * 0.7071067811865476)
    bell = jnp.exp(-0.5 * inner_pre * inner_pre)
    hidden = (inner_pre * normal_cdf).astype(bf16)
    hidden_ref[...] = hidden.T
    slope_ref[...] = (normal_cdf + inner_pre * bell * 0.3989422804014327).astype(bf16)
    second_sum[...] += dot(hidden, outer)

    if last:

        @pl.when(step == pl.num_programs(0) - 1)
        def _():
            normed, inv_scale = norm_rows(second_sum[...])
            blocks = normed.shape[0] // BUCKET
            live = jnp.concatenate(
                [
                    (item_places(lengths_ref, info_ref[0] * blocks + b, (BUCKET, 1), 0) < ITEMS)
                    for b in range(blocks)
                ],
                axis=0,
            ).astype(f32)
            output_ref[...] = ((normed * second_gain + second_shift) * live).astype(bf16)
            grad_final = cotangent_ref[...].astype(f32) * live
            grad_second = norm_back(grad_final, second_gain, normed, inv_scale)
            grad_outer = grad_second.astype(bf16)
            grad_second_ref[...] = grad_second
            grad_outer_ref[...] = grad_outer
            sums_ref[0:1, :] = column_sum(grad_outer)
            sums_ref[1:2, :] = column_sum(grad_final * normed)
            sums_ref[2:3, :] = column_sum(grad_final)


def feed_forward(chunks, info, vectors, biases, own, halves, first=None, going=None, last=None):
    width = vectors.shape[1]
    n_z = halves[0].shape[0] + 1
    feed_rows, twice = own.shape[0] // 8, 2 * width
    rows = first[1].shape[1] * BUCKET if first else going[0].shape[0]
    chunk = n_z * feed_rows
    whole = fixed((rows, width))
    my_rows = pl.BlockSpec((rows, width), lambda j, info: (info[0], 0))
    at = lambda j, info: info[3 + j]
    hidden_spec = pl.BlockSpec((chunk, rows), lambda j, info: (at(j, info), 0))
    slope_spec = pl.BlockSpec((rows, chunk), lambda j, info: (0, at(j, info)))
    in_specs = [
        fixed((8, width)),
        pl.BlockSpec((1, 1, chunk), lambda j, info: (at(j, info), 0, 0)),
        ANYWHERE,
    ] + [ANYWHERE] * len(halves)
    args = [vectors, biases, own] + halves
    shapes = [
        ((8 * chunk, rows), bf16, hidden_spec),
        ((rows, 8 * chunk), bf16, slope_spec),
    ]
    scratch = [
        pltpu.VMEM((2, n_z, feed_rows, twice), bf16),
        pltpu.SemaphoreType.DMA((2, 3)),
    ]
    aliases = {}
    if first:
        tokens, mixed, mixer = first
        mine = width // n_z
        in_specs += [my_rows, fixed((n_z, mixed.shape[1], mine, BUCKET)), fixed(mixer.shape)]
        args += [tokens, mixed, mixer]
        shapes += [
            ((rows, width), bf16, whole),
            ((rows, width), f32, whole),
            ((rows, 1), f32, fixed((rows, 1))),
        ]
    else:
        aliases = {1 + len(args) + 2: 0, 1 + len(args) + 3: 1}
        in_specs += [whole, whole, ANYWHERE, ANYWHERE]
        args += list(going)
    if last:
        in_specs += [pl.BlockSpec(memory_space=pltpu.SMEM), my_rows]
        args += list(last)
        shapes += [
            ((rows, width), bf16, whole),
            ((rows, width), f32, whole),
            ((rows, width), bf16, whole),
            ((8, width), f32, fixed((8, width))),
        ]
        scratch.append(pltpu.VMEM((rows, width), f32))
    else:
        shapes.append(((rows, width), f32, whole))
    info = jnp.concatenate(
        [info, jnp.array([4 * side + number for side, number in chunks], jnp.int32)]
    )
    return pl.pallas_call(
        functools.partial(feed_forward_kernel, chunks, first is not None, last is not None),
        grid_spec=pltpu.PrefetchScalarGridSpec(
            num_scalar_prefetch=1,
            grid=(len(chunks),),
            in_specs=in_specs,
            out_specs=[spec for _, _, spec in shapes],
            scratch_shapes=scratch,
        ),
        out_shape=[jax.ShapeDtypeStruct(shape, kind) for shape, kind, _ in shapes],
        input_output_aliases=aliases,
        compiler_params=params(1),
        name="feed_forward",
        cost_estimate=cost(3 * len(chunks)),
    )(info, *args)


STAY = ((0, 1), (0, 2))
GO = ((2, 3), (1, 3))


def feed_back_kernel(
    keeps, info_ref, grad_outer_ref, normed_low_ref, hidden_ref, slope_ref,
    own_ref, start_ref, *rest,
):
    halves, rest = take_halves(range(4), rest)
    if keeps:
        other_refs, norm_refs, rest = rest[:2], rest[2:5], rest[5:]
        stay_refs, go_refs, rest = rest[0:2], rest[2:4], rest[4:]
        bias_grad_ref, grad_first_ref, grad_attended_ref, sums_ref, units, sems = rest[:6]
        grad_normed_ref = rest[6]
    else:
        *grad_refs, bias_grad_ref, grad_normed_ref, units, sems = rest
    step = pl.program_id(0)
    side = info_ref[2] if keeps else 1 - info_ref[2]
    picks = [(info_ref[1] ^ number) * 2 + side for number in range(4)]
    weights = fetch_units(step, picks, own_ref, halves, units, sems)

    @pl.when(step == 0)
    def _():
        grad_normed_ref[...] = start_ref[...]

    n_z, feed_rows, twice = weights.shape
    width = twice // 2
    inner, outer = split_units(weights)
    grad_outer = grad_outer_ref[...]
    grad_hidden = contract_cols(grad_outer, outer)
    grad_inner = (grad_hidden * slope_ref[...].astype(f32)).astype(bf16)
    outer_grad = dot(hidden_ref[...], grad_outer).reshape(n_z, feed_rows, width)
    inner_grad = contract_rows(grad_inner, normed_low_ref[...]).reshape(n_z, feed_rows, width)
    bias_grad_ref[0] = column_sum(grad_inner)
    grad_normed_ref[...] += dot(grad_inner, inner)

    for number in range(4):

        @pl.when(step == number)
        def _(number=number):
            for track, value in enumerate((inner_grad, outer_grad)):
                at = slice(track * width, (track + 1) * width)
                if keeps:
                    found = value + other_refs[number // 2][0, :, :, at].astype(f32)
                    ref = stay_refs[track] if number in STAY[track] else go_refs[track]
                    ref[0] = found.astype(bf16)
                else:
                    grad_refs[number // 2][0, :, :, at] = value.astype(bf16)

    if keeps:

        @pl.when(step == pl.num_programs(0) - 1)
        def _():
            first_normed_ref, first_scale_ref, vectors_ref = norm_refs
            grad_rows, normed = grad_normed_ref[...], first_normed_ref[...]
            grad_first = norm_back(grad_rows, vectors_ref[1:2, :], normed, first_scale_ref[...])
            grad_attended = grad_first.astype(bf16)
            grad_first_ref[...] = grad_first
            grad_attended_ref[...] = grad_attended
            sums_ref[0:1, :] = column_sum(grad_attended)
            sums_ref[1:2, :] = column_sum(grad_rows * normed)
            sums_ref[2:3, :] = column_sum(grad_rows)


def feed_back(
    info, grad_outer, normed_low, hidden, slope, own, start, units, others=None, norm=None
):
    rows, width = grad_outer.shape
    keeps = others is not None
    count = 4
    feed_rows, twice = own.shape[0] // 8, 2 * width
    n_z = units[0].shape[0] + 1
    chunk = n_z * feed_rows
    flip = 0 if keeps else 1
    columns = pl.BlockSpec((rows, chunk), lambda i, info: (0, 4 * flip + i))
    whole = fixed((rows, width))
    part = (n_z, feed_rows, twice)
    track = (2, n_z, feed_rows, width)
    unit_rows = pl.BlockSpec((chunk, rows), lambda i, info: (4 * flip + i, 0))
    in_specs = [whole, whole, unit_rows, columns, ANYWHERE, whole] + [ANYWHERE] * len(units)
    args = [grad_outer, normed_low, hidden, slope, own, start] + units
    bias_shape = (
        (count, 1, chunk),
        f32,
        pl.BlockSpec((1, 1, chunk), lambda i, info: (i, 0, 0)),
    )
    scratch = [pltpu.VMEM((2,) + part, bf16), pltpu.SemaphoreType.DMA((2, 3))]

    def one(shape, at):
        return pl.BlockSpec((1,) + shape[1:], lambda i, info: (at(i), 0, 0, 0))

    early, late = (lambda i: jnp.minimum(i, 1)), (lambda i: jnp.maximum(i - 2, 0))
    pair = (2,) + part
    if keeps:
        in_specs += [one(pair, early), one(pair, late)]
        in_specs += [whole, fixed((rows, 1)), fixed((8, width))]
        args += list(others) + list(norm)
        slow, slower = (lambda i: i // 2), (lambda i: jnp.maximum(i - 1, 0) // 2)
        shapes = [(track, bf16, one(track, at)) for at in (early, slow, late, slower)] + [
            bias_shape,
            ((rows, width), f32, whole),
            ((rows, width), bf16, whole),
            ((8, width), f32, fixed((8, width))),
        ]
        scratch.append(pltpu.VMEM((rows, width), f32))
    else:
        shapes = [
            (pair, bf16, one(pair, early)),
            (pair, bf16, one(pair, late)),
            bias_shape,
            ((rows, width), f32, whole),
        ]
    return pl.pallas_call(
        functools.partial(feed_back_kernel, keeps),
        grid_spec=pltpu.PrefetchScalarGridSpec(
            num_scalar_prefetch=1,
            grid=(count,),
            in_specs=in_specs,
            out_specs=[spec for _, _, spec in shapes],
            scratch_shapes=scratch,
        ),
        out_shape=[jax.ShapeDtypeStruct(shape, kind) for shape, kind, _ in shapes],
        compiler_params=params(1),
        name="feed_back_own" if keeps else "feed_back",
        cost_estimate=cost(3 * count),
    )(info, *args)


def finish_feed_kernel(core_ref, own_ref, other_ref, inner_ref, outer_ref, inner_rows):
    places, count, twice = own_ref.shape
    width = twice // 2
    for source, side in ((own_ref, core_ref[0]), (other_ref, 1 - core_ref[0])):
        for place in range(places):
            row = pl.multiple_of((2 * place + side) * count, 16)
            inner_rows[pl.ds(row, count), :] = source[place, :, :width].astype(f32)
            outer_ref[pl.ds(row, count), :] = source[place, :, width:].astype(f32)
    inner_ref[...] = inner_rows[...].T


def finish_feed(core, own, other):
    places, count, twice = own.shape
    shape = (2 * places * count, twice // 2)
    inner_shape = (shape[1], shape[0])
    return pl.pallas_call(
        finish_feed_kernel,
        grid_spec=pltpu.PrefetchScalarGridSpec(
            num_scalar_prefetch=1,
            grid=(1,),
            in_specs=[fixed(own.shape), fixed(other.shape)],
            out_specs=[fixed(inner_shape), fixed(shape)],
            scratch_shapes=[pltpu.VMEM(shape, f32)],
        ),
        out_shape=[
            jax.ShapeDtypeStruct(inner_shape, f32),
            jax.ShapeDtypeStruct(shape, f32),
        ],
        compiler_params=params(1),
        name="finish_feed",
        cost_estimate=cost(5),
    )(core, own, other)


def copy_kernel(from_ref, to_ref):
    to_ref[...] = from_ref[...]


def copied(array):
    block = pl.BlockSpec((BUCKET, array.shape[1]), lambda i: (i, 0))
    return pl.pallas_call(
        copy_kernel,
        grid=(array.shape[0] // BUCKET,),
        in_specs=[block],
        out_specs=block,
        out_shape=jax.ShapeDtypeStruct(array.shape, array.dtype),
        compiler_params=params(1),
        name="copied",
        cost_estimate=cost(0.5),
    )(array)


def project_kernel(
    place_ref, tokens_ref, own_ref, remote_ref, biases_ref, query_ref, key_ref, value_ref
):
    rows = tokens_ref[...]
    width = rows.shape[1]
    weights = jnp.where(pl.program_id(1) == 0, own_ref[...], remote_ref[0])
    queries = contract_cols(weights[:, :width], rows) + as_column(biases_ref[0, 0:1, :])
    query_ref[...] = (queries.astype(bf16) * HEAD ** (-0.5)).astype(bf16)
    key_ref[...] = contract_cols(weights[:, width : 2 * width], rows).astype(bf16)
    values = contract_cols(weights[:, 2 * width :], rows) + as_column(biases_ref[0, 1:2, :])
    value_ref[...] = values.astype(bf16)


def project(place, tokens, own, remote, biases, buckets):
    width = tokens.shape[1]
    mine = own.shape[0]
    n_z = width // mine
    there = lambda s, place: lax.rem(place[0] + n_z - s, n_z)
    out = pl.BlockSpec((None, mine, BUCKET), lambda b, s, place: (b, there(s, place), 0))
    return pl.pallas_call(
        project_kernel,
        grid_spec=pltpu.PrefetchScalarGridSpec(
            num_scalar_prefetch=1,
            grid=(buckets, n_z),
            in_specs=[
                pl.BlockSpec((BUCKET, width), lambda b, s, place: (place[0] * buckets + b, 0)),
                fixed(own.shape),
                pl.BlockSpec(
                    (1, mine, 3 * width), lambda b, s, place: (jnp.maximum(s - 1, 0), 0, 0)
                ),
                pl.BlockSpec((1, 8, mine), lambda b, s, place: (there(s, place), 0, 0)),
            ],
            out_specs=[out] * 3,
        ),
        out_shape=[jax.ShapeDtypeStruct((buckets, width, BUCKET), bf16)] * 3,
        compiler_params=params(2),
        name="project",
        cost_estimate=cost(5),
    )(place, tokens, own, remote, biases)


def attend_back_kernel(
    place_ref, lengths_ref, grad_attended_ref, grad_first_ref, own_ref, remote_ref, mixer_ref,
    query_ref, key_ref, value_ref, key_mask_ref,
    grads_ref, tokens_grad_ref, sums_ref,
    bias, grad_mixed_t, whole, weights, mixer, sems,
):
    pair = pl.program_id(1)
    pairs, width = whole.shape[1], weights.shape[0]
    mine = own_ref.shape[0]
    n_z = width // mine

    def fetches():
        ends = [(mixer_ref, mixer)]
        for s in range(n_z):
            row = pl.multiple_of(lax.rem(place_ref[0] + n_z - s, n_z) * mine, 16)
            source = own_ref if s == 0 else remote_ref.at[s - 1]
            ends.append((source, weights.at[pl.ds(row, mine)]))
        return [
            pltpu.make_async_copy(source, target, sems.at[i])
            for i, (source, target) in enumerate(ends)
        ]

    @pl.when(pair == 0)
    def _():
        for fetch in fetches():
            fetch.start()
        row = place_ref[0] * pl.num_programs(0) + pl.program_id(0)
        bias[...] = mask_bias(lengths_ref, row, key_mask_ref[0])
        for fetch in fetches():
            fetch.wait()
        grad_mixed_t[...] = contract_cols(mixer[...], grad_attended_ref[...]).astype(bf16)

    queries, keys_t = query_ref[...], key_ref[...]
    keys, values = keys_t.T, value_ref[...].T
    start = pl.multiple_of(pair * keys.shape[1], 128)
    grad_mixed = grad_mixed_t[pl.ds(start, keys.shape[1]), :]
    grad_queries, grad_keys, grad_values = [], [], []
    for head in range(keys.shape[1] // HEAD):
        at = slice(head * HEAD, (head + 1) * HEAD)
        scores = dot(keys[:, at], queries[at]) + bias[...]
        exponent = jnp.exp(scores - jnp.max(scores, axis=0, keepdims=True))
        probs = exponent * (1.0 / jnp.sum(exponent, axis=0, keepdims=True))
        grad_probs = dot(values[:, at], grad_mixed[at])
        shift = jnp.sum(probs * grad_probs, axis=0, keepdims=True)
        grad_scores = (probs * (grad_probs - shift)).astype(bf16)
        grad_values.append(contract_cols(probs.astype(bf16), grad_mixed[at]))
        grad_keys.append(contract_cols(grad_scores, queries[at]))
        grad_queries.append(dot(keys_t[at], grad_scores) * HEAD ** (-0.5))
    query_t = jnp.concatenate(grad_queries, axis=0).astype(bf16)
    found = (
        query_t.T,
        jnp.concatenate(grad_keys, axis=1).astype(bf16),
        jnp.concatenate(grad_values, axis=1).astype(bf16),
    )
    for number, grad in enumerate(found):
        grads_ref[number, 0] = query_t if number == 0 else grad.T
        whole[number, pair] = grad
    sums_ref[0, 0:1, :] = column_sum(found[0])
    sums_ref[0, 1:2, :] = column_sum(found[2])

    @pl.when(pair == pl.num_programs(1) - 1)
    def _():
        total = grad_first_ref[...]
        for number in range(3):
            grad = jnp.concatenate([whole[number, i] for i in range(pairs)], axis=1)
            total += dot(grad, weights[:, number * width : (number + 1) * width])
        tokens_grad_ref[...] = total.astype(bf16)


def attend_back(
    place, lengths, grad_attended, grad_first, own, remote, mixer, queries, keys, values, key_mask
):
    rows, width = grad_attended.shape
    blocks = rows // BUCKET
    pair = 2 * HEAD
    by_bucket = pl.BlockSpec((BUCKET, width), lambda b, h, place: (b, 0))
    by_pair = pl.BlockSpec((None, pair, BUCKET), lambda b, h, place: (b, h, 0))
    return pl.pallas_call(
        attend_back_kernel,
        grid_spec=pltpu.PrefetchScalarGridSpec(
            num_scalar_prefetch=1,
            grid=(blocks, width // pair),
            in_specs=[
                pl.BlockSpec(memory_space=pltpu.SMEM),
                by_bucket,
                by_bucket,
                ANYWHERE,
                ANYWHERE,
                ANYWHERE,
                by_pair,
                by_pair,
                by_pair,
                pl.BlockSpec((1, 1, BUCKET), lambda b, h, place: (place[0] * blocks + b, 0, 0)),
            ],
            out_specs=[
                pl.BlockSpec((3, 1, pair, BUCKET), lambda b, h, place: (0, b, h, 0)),
                by_bucket,
                pl.BlockSpec((1, 8, pair), lambda b, h, place: (b, 0, h)),
            ],
            scratch_shapes=[
                pltpu.VMEM((BUCKET, BUCKET), f32),
                pltpu.VMEM((width, BUCKET), bf16),
                pltpu.VMEM((3, width // pair, BUCKET, pair), bf16),
                pltpu.VMEM((width, own.shape[1]), bf16),
                pltpu.VMEM(mixer.shape, bf16),
                pltpu.SemaphoreType.DMA((1 + width // own.shape[0],)),
            ],
        ),
        out_shape=[
            jax.ShapeDtypeStruct((3, blocks, width, BUCKET), bf16),
            jax.ShapeDtypeStruct((rows, width), bf16),
            jax.ShapeDtypeStruct((blocks, 8, width), f32),
        ],
        compiler_params=params(2),
        name="attend_back",
        cost_estimate=cost(20),
    )(
        place, lengths, grad_attended, grad_first, own, remote, mixer, queries, keys, values, key_mask
    )


def attention_grads_kernel(
    n_places, adds, info_ref, grads_ref, mixed_ref, tokens_ref, grad_attended_ref, *rest
):
    if adds:
        other_refs, small_ref, rest = rest[:n_places], rest[n_places], rest[n_places + 1 :]
    out_refs, whole = rest[:-1], rest[-1]
    step = pl.program_id(0)
    which = info_ref[step]
    n_z, buckets, mine, _ = mixed_ref.shape
    count = mine // n_places

    @pl.when(which < 3)
    def _():
        whole[...] = sum(
            dot(grads_ref[0, b], tokens_ref[b * BUCKET : (b + 1) * BUCKET, :])
            for b in range(buckets)
        ).astype(bf16)

    @pl.when(which == 3)
    def _():
        for t in range(n_z):
            whole[t * mine : (t + 1) * mine, :] = sum(
                dot(mixed_ref[t, b], grad_attended_ref[b * BUCKET : (b + 1) * BUCKET, :])
                for b in range(buckets)
            ).astype(bf16)

    for number in range(n_places):
        for s in range(n_z):
            start = lax.rem(info_ref[2] + s, n_z) * mine + (info_ref[3] ^ number) * count
            value = whole[pl.ds(pl.multiple_of(start, 16), count), :]
            if adds:
                value = value.astype(f32) + other_refs[number][s, 0].astype(f32)
                row = (2 * s + step) * count
                out_refs[number][pl.ds(pl.multiple_of(row, 16), count), :] = value.astype(bf16)
            else:
                out_refs[number][s, 0] = value

    if adds:
        for number in range(n_places):
            out_refs[number][2 * n_z * count :, :] = small_ref[...]


def attention_grads(n_places, info, grads, mixed, tokens, grad_attended, other=None, small=None):
    rows, width = grad_attended.shape
    n_z, buckets = mixed.shape[:2]
    mine = width // n_z
    count = mine // n_places
    by_step = pl.BlockSpec((n_z, 1, count, width), lambda i, info: (0, i, 0, 0))
    in_specs = [
        pl.BlockSpec(
            (1, buckets, width, BUCKET), lambda i, info: (jnp.minimum(info[i], 2), 0, 0, 0)
        ),
        fixed((n_z, buckets, mine, BUCKET)),
        pl.BlockSpec((rows, width), lambda i, info: (info[2], 0)),
        fixed((rows, width)),
    ]
    args = [grads, mixed, tokens, grad_attended]
    if other is None:
        shapes = [((n_z, 2, count, width), by_step)] * n_places
    else:
        in_specs += [by_step] * n_places + [fixed(small.shape)]
        args += list(other) + [small]
        flat = (2 * n_z * count + small.shape[0], width)
        shapes = [(flat, fixed(flat))] * n_places
    return pl.pallas_call(
        functools.partial(attention_grads_kernel, n_places, other is not None),
        grid_spec=pltpu.PrefetchScalarGridSpec(
            num_scalar_prefetch=1,
            grid=(2,),
            in_specs=in_specs,
            out_specs=[spec for _, spec in shapes],
            scratch_shapes=[pltpu.VMEM((width, width), bf16)],
        ),
        out_shape=[jax.ShapeDtypeStruct(shape, bf16) for shape, _ in shapes],
        compiler_params=params(1),
        name="attention_grads",
        cost_estimate=cost(0.5),
    )(info, *args)


def together(*values):
    return lax.optimization_barrier(values)


def add(first, *others):
    total = first.astype(f32)
    for other in others:
        total = total + other.astype(f32)
    return total.astype(bf16)


class Plane:
    def __init__(self, n_dp, n_z):
        self.n_dp, self.n_z = n_dp, n_z
        self.n_group = min(n_dp, 8)
        self.n_places = self.n_group // 2
        self.dp = lax.axis_index("dp")
        self.z = lax.axis_index("tensor")
        self.index = lax.rem(self.dp, self.n_group)
        self.core = self.index & 1
        self.place = self.index >> 1

    def swap(self, array, bits):
        return lax.ppermute(array, "dp", [(i, i ^ bits) for i in range(self.n_dp)])

    def shift(self, array, by):
        n = self.n_z
        return lax.ppermute(array, "tensor", [(i, (i + by) % n) for i in range(n)])

    def gather(self, piece):
        if self.n_dp == self.n_group:
            whole = lax.all_gather(piece, ("tensor", "dp"))
            return whole.reshape((self.n_z, self.n_group) + piece.shape)
        groups = [
            list(range(i, i + self.n_group)) for i in range(0, self.n_dp, self.n_group)
        ]
        line = lax.all_gather(piece, "tensor")
        return lax.all_gather(line, "dp", axis=1, axis_index_groups=groups)

    def turned(self, array):
        bit = 1
        while bit < self.n_group:
            lead = array.reshape((-1, 2, bit) + array.shape[1:])
            array = jnp.where((self.index & bit) != 0, lead[:, ::-1], lead).reshape(array.shape)
            bit *= 2
        return array

    def to_places(self, parts):
        return [self.swap(parts[number], 2 * number) for number in range(1, self.n_places)]

    def from_places(self, own, arrived):
        found = jnp.stack([own] + arrived)
        bit = 1
        while bit < self.n_places:
            lead = found.reshape((-1, 2, bit) + own.shape)
            flipped = lead[:, ::-1]
            found = jnp.where((self.place & bit) != 0, flipped, lead).reshape(found.shape)
            bit *= 2
        return found

    def by_core(self, own, other):
        return jnp.where(
            self.core == 1, jnp.stack([other, own]), jnp.stack([own, other])
        )

    def over_groups(self, array):
        bit = self.n_group
        while bit < self.n_dp:
            array = add(array, self.swap(array, bit))
            bit *= 2
        return array


def on_device(
    n_dp,
    n_z,
    tokens,
    lengths,
    key_mask,
    query_weight,
    query_bias,
    key_weight,
    value_weight,
    value_bias,
    output_weight,
    output_bias,
    first_gain,
    first_shift,
    inner_weight,
    inner_bias,
    outer_weight,
    outer_bias,
    second_gain,
    second_shift,
    cotangent,
):
    width = tokens.shape[1]
    mine = query_weight.shape[1]
    units = inner_weight.shape[1]
    all_rows = tokens.shape[0]
    all_blocks = all_rows // BUCKET
    rows = all_rows // n_z
    plane = Plane(n_dp, n_z)
    z, core, place, index = plane.z, plane.core, plane.place, plane.index
    n_places = plane.n_places
    others = range(1, n_z)

    feed_rows = units // plane.n_group
    head_rows = mine // plane.n_group
    mixer_count = width // plane.n_group
    piece = jnp.concatenate(
        [
            lax.dynamic_slice_in_dim(inner_weight, index * feed_rows, feed_rows, 1).T,
            lax.dynamic_slice_in_dim(outer_weight, index * feed_rows, feed_rows, 0),
        ],
        axis=1,
    )
    line = [plane.shift(piece, s) for s in others]

    mixer = plane.gather(
        lax.dynamic_slice_in_dim(output_weight, index * head_rows, head_rows, 0)
    ).reshape(width, width)
    query_t, key_t, value_t = query_weight.T, key_weight.T, value_weight.T

    key_mask_rows = key_mask.reshape(all_blocks, 1, BUCKET)
    bias_row = jnp.concatenate([query_bias, value_bias, inner_bias])
    bias_rows = jnp.pad(bias_row, (0, 16 * BUCKET - bias_row.shape[0])).reshape(16, BUCKET)
    place_z = z.reshape(1)
    mixed = attend_forward(
        n_z, lengths, tokens, query_t, key_t, value_t, bias_rows, key_mask_rows
    )
    mixed, line = together(mixed, line)

    near = jnp.stack(line)
    by_x, by_y = plane.swap(near, 2), plane.swap(near, 4)
    mixed, near = together(mixed, near)
    mixed = lax.all_to_all(mixed, "tensor", 0, 0)
    own_units = jnp.concatenate([inner_weight.T, outer_weight], axis=1)

    attention_own = jnp.concatenate([query_t, key_t, value_t], axis=1)
    attention_piece = lax.dynamic_slice_in_dim(attention_own, index * head_rows, head_rows, 0)
    attention_line = [plane.shift(attention_piece, s) for s in others]
    by_x, by_y, attention_line = together(by_x, by_y, attention_line)
    attention_line = jnp.stack(attention_line)
    attention_swaps = plane.to_places([attention_line] * n_places)

    biases = mixed[:, 0, mine:].reshape(n_z, -1)[:, : bias_row.shape[0]].astype(f32)
    head_biases = jnp.pad(
        jnp.stack([biases[:, :mine], biases[:, mine : 2 * mine]], axis=1), ((0, 0), (0, 6), (0, 0))
    )
    inner_biases = biases[:, 2 * mine :]
    inner_biases = jnp.concatenate(
        [
            lax.dynamic_slice_in_dim(inner_biases, lax.rem(z + n_z - s, n_z), 1, 0)
            for s in range(n_z)
        ],
        axis=0,
    )
    inner_biases = inner_biases.reshape(n_z, plane.n_group, feed_rows).transpose(1, 0, 2)
    inner_biases = plane.turned(inner_biases).reshape(n_places, 2, 1, n_z * feed_rows)
    inner_biases = inner_biases.transpose(1, 0, 2, 3).reshape(plane.n_group, 1, -1)
    vectors = jnp.stack(
        [output_bias, first_gain, first_shift, outer_bias, second_gain, second_shift]
        + [jnp.zeros_like(output_bias)] * 2
    ).astype(f32)

    info = jnp.stack([z, place, core])
    shared_args = (info, vectors, inner_biases, own_units)
    cut = feed_rows // 2
    far = [plane.swap(by_x[:, :cut], 4), plane.swap(by_y[:, cut:], 2)]
    send = [plane.swap(units_of, 1) for units_of in (near, by_x, by_y)]
    hidden, slope, normed_low, first_normed, first_scale, second_sum = feed_forward(
        ((0, 0), (0, 1), (0, 2), (1, 0), (1, 1), (1, 2)),
        *shared_args,
        [near, by_x, by_y] + send,
        first=(tokens, mixed, mixer),
    )
    second_sum, far, attention_swaps = together(second_sum, far, attention_swaps)
    attention_half = plane.from_places(attention_line, attention_swaps)
    attention_other = plane.swap(attention_half, 1)
    far_send = [plane.swap(half, 1) for half in far]
    keep = [near, by_x, by_y] + far
    send = send + far_send
    hidden, slope, my_output, grad_second, grad_outer, second_sums = feed_forward(
        ((0, 3), (1, 3)), *shared_args, far + far_send,
        going=(normed_low, second_sum, hidden, slope), last=(lengths, cotangent),
    )
    output = lax.all_gather(my_output, "tensor", axis=0, tiled=True)

    shared_args = (info, grad_outer, normed_low, hidden, slope, own_units)
    sent_early, sent_late, bias_sent, grad_normed = feed_back(*shared_args, grad_second, send)
    other = [plane.swap(sent_early, 1), plane.swap(sent_late, 1)]
    grad_normed, attention_other = together(grad_normed, attention_other)
    attention_remote = plane.by_core(attention_half, attention_other)
    attention_remote = attention_remote.transpose(2, 1, 0, 3, 4).reshape(n_z - 1, mine, 3 * width)
    projected = project(
        place_z, tokens, attention_own, attention_remote, head_biases, rows // BUCKET
    )
    projected, other = together(projected, other)
    (
        inner_stay, outer_stay, inner_go, outer_go, bias_kept, grad_first, grad_attended, first_sums
    ) = feed_back(
        *shared_args, grad_normed, keep, other,
        (first_normed, first_scale, vectors),
    )
    inner_came, outer_came = plane.swap(inner_go, 4), plane.swap(outer_go, 2)
    bias_grads = jnp.stack(
        [bias_kept[:, 0], bias_sent[:, 0]], axis=1
    )
    inner_bias_grad = plane.turned(bias_grads.reshape(plane.n_group, n_z, feed_rows))
    inner_bias_grad = inner_bias_grad.transpose(1, 0, 2)
    inner_bias_grad = jnp.concatenate(
        [
            sum(
                jnp.where(lax.rem(z - t + n_z, n_z) == s, inner_bias_grad[s : s + 1], 0.0)
                for s in range(n_z)
            )
            for t in range(n_z)
        ],
        axis=0,
    ).reshape(n_z, units)

    grads, my_tokens_grad, back_sums = attend_back(
        place_z, lengths, grad_attended, grad_first, attention_own, attention_remote, mixer,
        *projected, key_mask_rows,
    )
    grads, inner_came, outer_came, output = together(grads, inner_came, outer_came, output)
    inner_on, outer_on = (
        plane.swap(add(inner_stay[1], inner_came[1]), 2),
        plane.swap(add(outer_stay[1], outer_came[1]), 4),
    )
    tokens_grad = lax.all_gather(my_tokens_grad, "tensor", axis=0, tiled=True)

    def weight_grads(side, other=None, small=None):
        info = jnp.stack([2 * side, 2 * side + 1, z, place])
        return attention_grads(
            n_places, info, grads, mixed, tokens, grad_attended, other, small
        )

    sent = weight_grads(1 - core)
    sent, back_sums, first_sums, second_sums, inner_bias_grad = together(
        sent, back_sums, first_sums, second_sums, inner_bias_grad
    )
    other = [plane.swap(part, 1) for part in sent]

    small = jnp.concatenate(
        [first_sums[:3], second_sums[:3], inner_bias_grad, jnp.sum(back_sums, axis=0)[:2]], axis=0
    )
    small = jnp.pad(small, ((0, -small.shape[0] % 16), (0, 0))).astype(bf16)
    small_rows = small.shape[0]

    small = add(small, plane.swap(small, 1))
    kept = list(weight_grads(core, other, small))
    arrived = plane.to_places(kept)
    kept[0], inner_on, outer_on = together(kept[0], inner_on, outer_on)
    feed_parts = [
        jnp.concatenate(
            [
                add(inner_stay[0, s], inner_came[0, s], inner_on[s]),
                add(outer_stay[0, s], outer_came[0, s], outer_on[s]),
            ],
            axis=1,
        )
        for s in range(n_z)
    ]
    feed_line = [plane.shift(feed_parts[s], -s) for s in others]
    output = copied(output)
    arrived, output = together(arrived, output)
    small = add(small, *[a[-small_rows:] for a in arrived])
    count = 2 * mine // n_places
    attention_parts = [
        add(*[a[s * count : (s + 1) * count] for a in [kept[0]] + arrived]) for s in range(n_z)
    ]
    attention_line = [
        plane.shift(jnp.concatenate([attention_parts[s], small], axis=0), s) for s in others
    ]
    feed_total = plane.over_groups(add(feed_parts[0], *feed_line))
    feed_arrived = plane.to_places([feed_total] * n_places)
    tokens_grad = copied(tokens_grad)
    attention_line, feed_arrived, tokens_grad = together(
        attention_line, feed_arrived, tokens_grad
    )
    attention_total = plane.over_groups(
        add(attention_parts[0], *[a[:count] for a in attention_line])
    )
    small = plane.over_groups(add(small, *[a[count:] for a in attention_line])).astype(f32)
    arrived = plane.to_places([attention_total] * n_places)
    feed_half = plane.from_places(feed_total, feed_arrived)
    feed_other = plane.swap(feed_half, 1)
    inner_grad, outer_grad = finish_feed(core.reshape(1), feed_half, feed_other)
    inner_bias_sum = lax.dynamic_slice_in_dim(small, 6 + z, 1, 0)[0]
    head_sums = lax.dynamic_slice_in_dim(small[6 + n_z : 8 + n_z], z * mine, mine, 1)
    arrived, inner_grad, outer_grad, small, inner_bias_sum, head_sums = together(
        arrived, inner_grad, outer_grad, small, inner_bias_sum, head_sums
    )
    attention_half = plane.from_places(attention_total, arrived)
    attention_other = plane.swap(attention_half, 1)
    grad_list = plane.by_core(attention_half, attention_other)
    grad_list = grad_list.reshape(2, n_places, 2, mine // n_places, width)
    grad_list = grad_list.transpose(0, 2, 1, 3, 4).reshape(4, mine, width)

    shared = small[:6]

    return (
        output,
        tokens_grad,
        grad_list[0].T.astype(f32),
        head_sums[0],
        grad_list[1].T.astype(f32),
        grad_list[2].T.astype(f32),
        head_sums[1],
        grad_list[3].astype(f32),
        shared[0],
        shared[1],
        shared[2],
        inner_grad,
        inner_bias_sum,
        outer_grad,
        shared[3],
        shared[4],
        shared[5],
    )


def solution(mesh):
    n_dp, n_z = mesh.shape["dp"], mesh.shape["tensor"]
    in_specs = (
        P("dp", None),
        P("dp", None),
        P("dp"),
        P(None, "tensor"),
        P("tensor"),
        P(None, "tensor"),
        P(None, "tensor"),
        P("tensor"),
        P("tensor", None),
        P(),
        P(),
        P(),
        P(None, "tensor"),
        P("tensor"),
        P("tensor", None),
        P(),
        P(),
        P(),
        P("dp", None),
    )
    out_specs = (
        P("dp", None),
        P("dp", None),
        P(None, "tensor"),
        P("tensor"),
        P(None, "tensor"),
        P(None, "tensor"),
        P("tensor"),
        P("tensor", None),
        P(),
        P(),
        P(),
        P(None, "tensor"),
        P("tensor"),
        P("tensor", None),
        P(),
        P(),
        P(),
    )

    def program(*args):
        return on_device(n_dp, n_z, *args)

    return jax.shard_map(
        program, mesh=mesh, in_specs=in_specs, out_specs=out_specs, check_vma=False
    )
```

```python
import functools

import jax
import jax.numpy as jnp
from jax import lax
from jax.experimental import pallas as pl
from jax.experimental.pallas import tpu as pltpu
from jax.sharding import PartitionSpec as P

HEAD = 64
BUCKET = 512
ITEMS = 8


negative_fill = -1e30
epsilon = 1e-06
f32 = jnp.float32
bf16 = jnp.bfloat16
VMEM_BYTES = 56 * 1024 * 1024


def dot(left, right):
    return jnp.dot(left, right, preferred_element_type=f32)


def contract_rows(left, right):
    return lax.dot_general(left, right, (((0,), (0,)), ((), ())), preferred_element_type=f32)


def contract_cols(left, right):
    return lax.dot_general(left, right, (((1,), (1,)), ((), ())), preferred_element_type=f32)


def norm_rows(values):
    centred = values - jnp.mean(values, axis=1, keepdims=True)
    inv_scale = lax.rsqrt(jnp.mean(centred * centred, axis=1, keepdims=True) + epsilon)
    return centred * inv_scale, inv_scale


def norm_back(grad_rows, norm_gain, normed, inv_scale):
    scaled = grad_rows * norm_gain
    return inv_scale * (
        scaled
        - jnp.mean(scaled, axis=1, keepdims=True)
        - normed * jnp.mean(scaled * normed, axis=1, keepdims=True)
    )


def column_sum(matrix):
    return jnp.sum(matrix.astype(f32), axis=0, keepdims=True)


def fixed(shape):
    return pl.BlockSpec(shape, lambda *_: (0,) * len(shape))


def cost(microseconds):
    return pl.CostEstimate(
        flops=int(microseconds * 2.5e8),
        bytes_accessed=int(microseconds * 2.5e5),
        transcendentals=0,
    )


def params(axes):
    return pltpu.CompilerParams(
        dimension_semantics=("arbitrary",) * axes, vmem_limit_bytes=VMEM_BYTES
    )


def item_places(lengths_ref, row, shape, axis):
    places = lax.broadcasted_iota(jnp.int32, shape, axis)
    end = jnp.int32(0)
    items = jnp.zeros(shape, jnp.int32)
    for slot in range(ITEMS):
        end = end + lengths_ref[row, slot]
        items = items + (places >= end).astype(jnp.int32)
    return items


def as_column(row):
    return jnp.broadcast_to(row.astype(f32), (8, row.shape[1])).T[:, :1]


def mask_bias(lengths_ref, row, key_mask):
    shape = (BUCKET, BUCKET)
    diagonal = lax.broadcasted_iota(jnp.int32, shape, 0) == lax.broadcasted_iota(
        jnp.int32, shape, 1
    )
    item_row = item_places(lengths_ref, row, (1, BUCKET), 1)
    item_column = item_places(lengths_ref, row, (BUCKET, 1), 0)
    code_column = jnp.where(as_column(key_mask) == 1.0, item_column, -1)
    return jnp.where((code_column == item_row) | diagonal, 0.0, negative_fill).astype(f32)


def attend_forward_kernel(
    lengths_ref, tokens_ref, query_ref, key_ref, value_ref, biases_ref, key_mask_ref, mixed_ref,
):
    mine = query_ref.shape[0]
    rows = tokens_ref[...]
    queries = contract_cols(query_ref[...], rows) + as_column(biases_ref[0:1, :mine])
    queries = (queries.astype(bf16) * HEAD ** (-0.5)).astype(bf16)
    keys = contract_cols(rows, key_ref[...]).astype(bf16)
    values = contract_cols(value_ref[...], rows) + as_column(biases_ref[0:1, mine : 2 * mine])
    values = values.astype(bf16)
    bias = mask_bias(lengths_ref, pl.program_id(0), key_mask_ref[0])
    for head in range(mine // HEAD):
        at = slice(head * HEAD, (head + 1) * HEAD)
        scores = dot(keys[:, at], queries[at]) + bias
        exponent = jnp.exp(scores - jnp.max(scores, axis=0, keepdims=True))
        total = jnp.sum(exponent, axis=0, keepdims=True)
        mixed_ref[0, 0, at] = (dot(values[at], exponent.astype(bf16)) / total).astype(bf16)
    mixed_ref[0, 0, mine:] = biases_ref[...]


def attend_forward(n_z, lengths, tokens, query, key, value, biases, key_mask):
    blocks = lengths.shape[0]
    own = blocks // n_z
    mine, width = key.shape
    whole = (n_z, own, mine + biases.shape[0], BUCKET)
    return pl.pallas_call(
        attend_forward_kernel,
        grid=(blocks,),
        in_specs=[
            pl.BlockSpec(memory_space=pltpu.SMEM),
            pl.BlockSpec((BUCKET, width), lambda b: (b, 0)),
            fixed((mine, width)),
            fixed((mine, width)),
            fixed((mine, width)),
            fixed(biases.shape),
            pl.BlockSpec((1, 1, BUCKET), lambda b: (b, 0, 0)),
        ],
        out_specs=pl.BlockSpec((1, 1) + whole[2:], lambda b: (b // own, b % own, 0, 0)),
        out_shape=jax.ShapeDtypeStruct(whole, bf16),
        compiler_params=params(1),
        name="attend_forward",
        cost_estimate=cost(12),
    )(lengths, tokens, query, key, value, biases, key_mask)


def fetch_units(step, picks, own_ref, halves, units, sems):
    feed_rows = units.shape[2]
    cut = feed_rows // 2

    def copies(number):
        slot = number % 2
        row = pl.multiple_of(picks[number] * feed_rows, 16)
        ends = [
            (own_ref.at[pl.ds(row, feed_rows)], units.at[slot, 0]),
            (halves[number][0], units.at[slot, 1:, :cut]),
            (halves[number][1], units.at[slot, 1:, cut:]),
        ]
        return [
            pltpu.make_async_copy(source, target, sems.at[slot, i])
            for i, (source, target) in enumerate(ends)
        ]

    for number in range(len(halves)):

        @pl.when(step == number)
        def _(number=number):
            if number == 0:
                for copy in copies(0):
                    copy.start()
            if number + 1 < len(halves):
                for copy in copies(number + 1):
                    copy.start()
            for copy in copies(number):
                copy.wait()

    return units.at[lax.rem(step, 2)]


def take_halves(numbers, refs):
    halves, refs = [], list(refs)
    for number in numbers:
        if number == 3:
            halves.append((refs.pop(0), refs.pop(0)))
        else:
            ref = refs.pop(0)
            cut = ref.shape[1] // 2
            halves.append((ref.at[:, :cut], ref.at[:, cut:]))
    return halves, refs


def split_units(units):
    width = units.shape[2] // 2
    return units[:, :, :width].reshape(-1, width), units[:, :, width:].reshape(-1, width)


ANYWHERE = pl.BlockSpec(memory_space=pl.ANY)


def feed_forward_kernel(chunks, first, last, info_ref, *rest):
    def take(count):
        nonlocal rest
        taken, rest = rest[:count], rest[count:]
        return taken

    vectors_ref, bias_ref, own_ref = take(3)
    halves, rest = take_halves([number for _, number in chunks], rest)
    if first:
        tokens_ref, mixed_ref, mixer_ref = take(3)
    else:
        normed_low_ref, start_ref, _, _ = take(4)
    if last:
        lengths_ref, cotangent_ref = take(2)
    hidden_ref, slope_ref = take(2)
    if first:
        normed_low_ref, first_normed_ref, first_scale_ref = take(3)
    if last:
        output_ref, grad_second_ref, grad_outer_ref, sums_ref = take(4)
    else:
        (second_sum,) = take(1)
    units, sems = take(2)
    if last:
        (second_sum,) = take(1)

    step = pl.program_id(0)
    picks = [(info_ref[1] ^ number) * 2 + (info_ref[2] ^ side) for side, number in chunks]
    weights = fetch_units(step, picks, own_ref, halves, units, sems)
    output_bias, first_gain, first_shift, outer_bias, second_gain, second_shift = (
        vectors_ref[i : i + 1, :] for i in range(6)
    )

    @pl.when(step == 0)
    def _():
        if first:
            n_z, own, mine, _ = mixed_ref.shape
            attended = output_bias + jnp.concatenate(
                [
                    sum(
                        contract_rows(mixed_ref[t, b], mixer_ref[t * mine : (t + 1) * mine, :])
                        for t in range(n_z)
                    )
                    for b in range(own)
                ],
                axis=0,
            )
            normed, inv_scale = norm_rows(tokens_ref[...].astype(f32) + attended)
            whole = normed * first_gain + first_shift
            first_normed_ref[...] = normed
            first_scale_ref[...] = inv_scale
            normed_low_ref[...] = whole.astype(bf16)
            second_sum[...] = whole + outer_bias
        else:
            second_sum[...] = start_ref[...]

    inner, outer = split_units(weights)
    inner_pre = contract_cols(normed_low_ref[...], inner) + bias_ref[0]
    normal_cdf = 0.5 + 0.5 * lax.erf(inner_pre * 0.7071067811865476)
    bell = jnp.exp(-0.5 * inner_pre * inner_pre)
    hidden = (inner_pre * normal_cdf).astype(bf16)
    hidden_ref[...] = hidden.T
    slope_ref[...] = (normal_cdf + inner_pre * bell * 0.3989422804014327).astype(bf16)
    second_sum[...] += dot(hidden, outer)

    if last:

        @pl.when(step == pl.num_programs(0) - 1)
        def _():
            normed, inv_scale = norm_rows(second_sum[...])
            blocks = normed.shape[0] // BUCKET
            live = jnp.concatenate(
                [
                    (item_places(lengths_ref, info_ref[0] * blocks + b, (BUCKET, 1), 0) < ITEMS)
                    for b in range(blocks)
                ],
                axis=0,
            ).astype(f32)
            output_ref[...] = ((normed * second_gain + second_shift) * live).astype(bf16)
            grad_final = cotangent_ref[...].astype(f32) * live
            grad_second = norm_back(grad_final, second_gain, normed, inv_scale)
            grad_outer = grad_second.astype(bf16)
            grad_second_ref[...] = grad_second
            grad_outer_ref[...] = grad_outer
            sums_ref[0:1, :] = column_sum(grad_outer)
            sums_ref[1:2, :] = column_sum(grad_final * normed)
            sums_ref[2:3, :] = column_sum(grad_final)


def feed_forward(chunks, info, vectors, biases, own, halves, first=None, going=None, last=None):
    width = vectors.shape[1]
    n_z = halves[0].shape[0] + 1
    feed_rows, twice = own.shape[0] // 8, 2 * width
    rows = first[1].shape[1] * BUCKET if first else going[0].shape[0]
    chunk = n_z * feed_rows
    whole = fixed((rows, width))
    my_rows = pl.BlockSpec((rows, width), lambda j, info: (info[0], 0))
    at = lambda j, info: info[3 + j]
    hidden_spec = pl.BlockSpec((chunk, rows), lambda j, info: (at(j, info), 0))
    slope_spec = pl.BlockSpec((rows, chunk), lambda j, info: (0, at(j, info)))
    in_specs = [
        fixed((8, width)),
        pl.BlockSpec((1, 1, chunk), lambda j, info: (at(j, info), 0, 0)),
        ANYWHERE,
    ] + [ANYWHERE] * len(halves)
    args = [vectors, biases, own] + halves
    shapes = [
        ((8 * chunk, rows), bf16, hidden_spec),
        ((rows, 8 * chunk), bf16, slope_spec),
    ]
    scratch = [
        pltpu.VMEM((2, n_z, feed_rows, twice), bf16),
        pltpu.SemaphoreType.DMA((2, 3)),
    ]
    aliases = {}
    if first:
        tokens, mixed, mixer = first
        mine = width // n_z
        in_specs += [my_rows, fixed((n_z, mixed.shape[1], mine, BUCKET)), fixed(mixer.shape)]
        args += [tokens, mixed, mixer]
        shapes += [
            ((rows, width), bf16, whole),
            ((rows, width), f32, whole),
            ((rows, 1), f32, fixed((rows, 1))),
        ]
    else:
        aliases = {1 + len(args) + 2: 0, 1 + len(args) + 3: 1}
        in_specs += [whole, whole, ANYWHERE, ANYWHERE]
        args += list(going)
    if last:
        in_specs += [pl.BlockSpec(memory_space=pltpu.SMEM), my_rows]
        args += list(last)
        shapes += [
            ((rows, width), bf16, whole),
            ((rows, width), f32, whole),
            ((rows, width), bf16, whole),
            ((8, width), f32, fixed((8, width))),
        ]
        scratch.append(pltpu.VMEM((rows, width), f32))
    else:
        shapes.append(((rows, width), f32, whole))
    info = jnp.concatenate(
        [info, jnp.array([4 * side + number for side, number in chunks], jnp.int32)]
    )
    return pl.pallas_call(
        functools.partial(feed_forward_kernel, chunks, first is not None, last is not None),
        grid_spec=pltpu.PrefetchScalarGridSpec(
            num_scalar_prefetch=1,
            grid=(len(chunks),),
            in_specs=in_specs,
            out_specs=[spec for _, _, spec in shapes],
            scratch_shapes=scratch,
        ),
        out_shape=[jax.ShapeDtypeStruct(shape, kind) for shape, kind, _ in shapes],
        input_output_aliases=aliases,
        compiler_params=params(1),
        name="feed_forward",
        cost_estimate=cost(3 * len(chunks)),
    )(info, *args)


STAY = ((0, 1), (0, 2))
GO = ((2, 3), (1, 3))


def feed_back_kernel(
    keeps, info_ref, grad_outer_ref, normed_low_ref, hidden_ref, slope_ref,
    own_ref, start_ref, *rest,
):
    halves, rest = take_halves(range(4), rest)
    if keeps:
        other_refs, norm_refs, rest = rest[:2], rest[2:5], rest[5:]
        stay_refs, go_refs, rest = rest[0:2], rest[2:4], rest[4:]
        bias_grad_ref, grad_first_ref, grad_attended_ref, sums_ref, units, sems = rest[:6]
        grad_normed_ref = rest[6]
    else:
        *grad_refs, bias_grad_ref, grad_normed_ref, units, sems = rest
    step = pl.program_id(0)
    side = info_ref[2] if keeps else 1 - info_ref[2]
    picks = [(info_ref[1] ^ number) * 2 + side for number in range(4)]
    weights = fetch_units(step, picks, own_ref, halves, units, sems)

    @pl.when(step == 0)
    def _():
        grad_normed_ref[...] = start_ref[...]

    n_z, feed_rows, twice = weights.shape
    width = twice // 2
    inner, outer = split_units(weights)
    grad_outer = grad_outer_ref[...]
    grad_hidden = contract_cols(grad_outer, outer)
    grad_inner = (grad_hidden * slope_ref[...].astype(f32)).astype(bf16)
    outer_grad = dot(hidden_ref[...], grad_outer).reshape(n_z, feed_rows, width)
    inner_grad = contract_rows(grad_inner, normed_low_ref[...]).reshape(n_z, feed_rows, width)
    bias_grad_ref[0] = column_sum(grad_inner)
    grad_normed_ref[...] += dot(grad_inner, inner)

    for number in range(4):

        @pl.when(step == number)
        def _(number=number):
            for track, value in enumerate((inner_grad, outer_grad)):
                at = slice(track * width, (track + 1) * width)
                if keeps:
                    found = value + other_refs[number // 2][0, :, :, at].astype(f32)
                    ref = stay_refs[track] if number in STAY[track] else go_refs[track]
                    ref[0] = found.astype(bf16)
                else:
                    grad_refs[number // 2][0, :, :, at] = value.astype(bf16)

    if keeps:

        @pl.when(step == pl.num_programs(0) - 1)
        def _():
            first_normed_ref, first_scale_ref, vectors_ref = norm_refs
            grad_rows, normed = grad_normed_ref[...], first_normed_ref[...]
            grad_first = norm_back(grad_rows, vectors_ref[1:2, :], normed, first_scale_ref[...])
            grad_attended = grad_first.astype(bf16)
            grad_first_ref[...] = grad_first
            grad_attended_ref[...] = grad_attended
            sums_ref[0:1, :] = column_sum(grad_attended)
            sums_ref[1:2, :] = column_sum(grad_rows * normed)
            sums_ref[2:3, :] = column_sum(grad_rows)


def feed_back(
    info, grad_outer, normed_low, hidden, slope, own, start, units, others=None, norm=None
):
    rows, width = grad_outer.shape
    keeps = others is not None
    count = 4
    feed_rows, twice = own.shape[0] // 8, 2 * width
    n_z = units[0].shape[0] + 1
    chunk = n_z * feed_rows
    flip = 0 if keeps else 1
    columns = pl.BlockSpec((rows, chunk), lambda i, info: (0, 4 * flip + i))
    whole = fixed((rows, width))
    part = (n_z, feed_rows, twice)
    track = (2, n_z, feed_rows, width)
    unit_rows = pl.BlockSpec((chunk, rows), lambda i, info: (4 * flip + i, 0))
    in_specs = [whole, whole, unit_rows, columns, ANYWHERE, whole] + [ANYWHERE] * len(units)
    args = [grad_outer, normed_low, hidden, slope, own, start] + units
    bias_shape = (
        (count, 1, chunk),
        f32,
        pl.BlockSpec((1, 1, chunk), lambda i, info: (i, 0, 0)),
    )
    scratch = [pltpu.VMEM((2,) + part, bf16), pltpu.SemaphoreType.DMA((2, 3))]

    def one(shape, at):
        return pl.BlockSpec((1,) + shape[1:], lambda i, info: (at(i), 0, 0, 0))

    early, late = (lambda i: jnp.minimum(i, 1)), (lambda i: jnp.maximum(i - 2, 0))
    pair = (2,) + part
    if keeps:
        in_specs += [one(pair, early), one(pair, late)]
        in_specs += [whole, fixed((rows, 1)), fixed((8, width))]
        args += list(others) + list(norm)
        slow, slower = (lambda i: i // 2), (lambda i: jnp.maximum(i - 1, 0) // 2)
        shapes = [(track, bf16, one(track, at)) for at in (early, slow, late, slower)] + [
            bias_shape,
            ((rows, width), f32, whole),
            ((rows, width), bf16, whole),
            ((8, width), f32, fixed((8, width))),
        ]
        scratch.append(pltpu.VMEM((rows, width), f32))
    else:
        shapes = [
            (pair, bf16, one(pair, early)),
            (pair, bf16, one(pair, late)),
            bias_shape,
            ((rows, width), f32, whole),
        ]
    return pl.pallas_call(
        functools.partial(feed_back_kernel, keeps),
        grid_spec=pltpu.PrefetchScalarGridSpec(
            num_scalar_prefetch=1,
            grid=(count,),
            in_specs=in_specs,
            out_specs=[spec for _, _, spec in shapes],
            scratch_shapes=scratch,
        ),
        out_shape=[jax.ShapeDtypeStruct(shape, kind) for shape, kind, _ in shapes],
        compiler_params=params(1),
        name="feed_back_own" if keeps else "feed_back",
        cost_estimate=cost(3 * count),
    )(info, *args)


def finish_feed_kernel(core_ref, own_ref, other_ref, inner_ref, outer_ref, inner_rows):
    places, count, twice = own_ref.shape
    width = twice // 2
    for source, side in ((own_ref, core_ref[0]), (other_ref, 1 - core_ref[0])):
        for place in range(places):
            row = pl.multiple_of((2 * place + side) * count, 16)
            inner_rows[pl.ds(row, count), :] = source[place, :, :width].astype(f32)
            outer_ref[pl.ds(row, count), :] = source[place, :, width:].astype(f32)
    inner_ref[...] = inner_rows[...].T


def finish_feed(core, own, other):
    places, count, twice = own.shape
    shape = (2 * places * count, twice // 2)
    inner_shape = (shape[1], shape[0])
    return pl.pallas_call(
        finish_feed_kernel,
        grid_spec=pltpu.PrefetchScalarGridSpec(
            num_scalar_prefetch=1,
            grid=(1,),
            in_specs=[fixed(own.shape), fixed(other.shape)],
            out_specs=[fixed(inner_shape), fixed(shape)],
            scratch_shapes=[pltpu.VMEM(shape, f32)],
        ),
        out_shape=[
            jax.ShapeDtypeStruct(inner_shape, f32),
            jax.ShapeDtypeStruct(shape, f32),
        ],
        compiler_params=params(1),
        name="finish_feed",
        cost_estimate=cost(5),
    )(core, own, other)


def copy_kernel(from_ref, to_ref):
    to_ref[...] = from_ref[...]


def copied(array):
    block = pl.BlockSpec((BUCKET, array.shape[1]), lambda i: (i, 0))
    return pl.pallas_call(
        copy_kernel,
        grid=(array.shape[0] // BUCKET,),
        in_specs=[block],
        out_specs=block,
        out_shape=jax.ShapeDtypeStruct(array.shape, array.dtype),
        compiler_params=params(1),
        name="copied",
        cost_estimate=cost(0.5),
    )(array)


def project_kernel(
    place_ref, tokens_ref, own_ref, remote_ref, biases_ref, query_ref, key_ref, value_ref
):
    rows = tokens_ref[...]
    width = rows.shape[1]
    weights = jnp.where(pl.program_id(1) == 0, own_ref[...], remote_ref[0])
    queries = contract_cols(weights[:, :width], rows) + as_column(biases_ref[0, 0:1, :])
    query_ref[...] = (queries.astype(bf16) * HEAD ** (-0.5)).astype(bf16)
    key_ref[...] = contract_cols(weights[:, width : 2 * width], rows).astype(bf16)
    values = contract_cols(weights[:, 2 * width :], rows) + as_column(biases_ref[0, 1:2, :])
    value_ref[...] = values.astype(bf16)


def project(place, tokens, own, remote, biases, buckets):
    width = tokens.shape[1]
    mine = own.shape[0]
    n_z = width // mine
    there = lambda s, place: lax.rem(place[0] + n_z - s, n_z)
    out = pl.BlockSpec((None, mine, BUCKET), lambda b, s, place: (b, there(s, place), 0))
    return pl.pallas_call(
        project_kernel,
        grid_spec=pltpu.PrefetchScalarGridSpec(
            num_scalar_prefetch=1,
            grid=(buckets, n_z),
            in_specs=[
                pl.BlockSpec((BUCKET, width), lambda b, s, place: (place[0] * buckets + b, 0)),
                fixed(own.shape),
                pl.BlockSpec(
                    (1, mine, 3 * width), lambda b, s, place: (jnp.maximum(s - 1, 0), 0, 0)
                ),
                pl.BlockSpec((1, 8, mine), lambda b, s, place: (there(s, place), 0, 0)),
            ],
            out_specs=[out] * 3,
        ),
        out_shape=[jax.ShapeDtypeStruct((buckets, width, BUCKET), bf16)] * 3,
        compiler_params=params(2),
        name="project",
        cost_estimate=cost(5),
    )(place, tokens, own, remote, biases)


def attend_back_kernel(
    place_ref, lengths_ref, grad_attended_ref, grad_first_ref, own_ref, remote_ref, mixer_ref,
    query_ref, key_ref, value_ref, key_mask_ref,
    grads_ref, tokens_grad_ref, sums_ref,
    bias, grad_mixed_t, whole, weights, mixer, sems,
):
    pair = pl.program_id(1)
    pairs, width = whole.shape[1], weights.shape[0]
    mine = own_ref.shape[0]
    n_z = width // mine

    def fetches():
        ends = [(mixer_ref, mixer)]
        for s in range(n_z):
            row = pl.multiple_of(lax.rem(place_ref[0] + n_z - s, n_z) * mine, 16)
            source = own_ref if s == 0 else remote_ref.at[s - 1]
            ends.append((source, weights.at[pl.ds(row, mine)]))
        return [
            pltpu.make_async_copy(source, target, sems.at[i])
            for i, (source, target) in enumerate(ends)
        ]

    @pl.when(pair == 0)
    def _():
        for fetch in fetches():
            fetch.start()
        row = place_ref[0] * pl.num_programs(0) + pl.program_id(0)
        bias[...] = mask_bias(lengths_ref, row, key_mask_ref[0])
        for fetch in fetches():
            fetch.wait()
        grad_mixed_t[...] = contract_cols(mixer[...], grad_attended_ref[...]).astype(bf16)

    queries, keys_t = query_ref[...], key_ref[...]
    keys, values = keys_t.T, value_ref[...].T
    start = pl.multiple_of(pair * keys.shape[1], 128)
    grad_mixed = grad_mixed_t[pl.ds(start, keys.shape[1]), :]
    grad_queries, grad_keys, grad_values = [], [], []
    for head in range(keys.shape[1] // HEAD):
        at = slice(head * HEAD, (head + 1) * HEAD)
        scores = dot(keys[:, at], queries[at]) + bias[...]
        exponent = jnp.exp(scores - jnp.max(scores, axis=0, keepdims=True))
        probs = exponent * (1.0 / jnp.sum(exponent, axis=0, keepdims=True))
        grad_probs = dot(values[:, at], grad_mixed[at])
        shift = jnp.sum(probs * grad_probs, axis=0, keepdims=True)
        grad_scores = (probs * (grad_probs - shift)).astype(bf16)
        grad_values.append(contract_cols(probs.astype(bf16), grad_mixed[at]))
        grad_keys.append(contract_cols(grad_scores, queries[at]))
        grad_queries.append(dot(keys_t[at], grad_scores) * HEAD ** (-0.5))
    query_t = jnp.concatenate(grad_queries, axis=0).astype(bf16)
    found = (
        query_t.T,
        jnp.concatenate(grad_keys, axis=1).astype(bf16),
        jnp.concatenate(grad_values, axis=1).astype(bf16),
    )
    for number, grad in enumerate(found):
        grads_ref[number, 0] = query_t if number == 0 else grad.T
        whole[number, pair] = grad
    sums_ref[0, 0:1, :] = column_sum(found[0])
    sums_ref[0, 1:2, :] = column_sum(found[2])

    @pl.when(pair == pl.num_programs(1) - 1)
    def _():
        total = grad_first_ref[...]
        for number in range(3):
            grad = jnp.concatenate([whole[number, i] for i in range(pairs)], axis=1)
            total += dot(grad, weights[:, number * width : (number + 1) * width])
        tokens_grad_ref[...] = total.astype(bf16)


def attend_back(
    place, lengths, grad_attended, grad_first, own, remote, mixer, queries, keys, values, key_mask
):
    rows, width = grad_attended.shape
    blocks = rows // BUCKET
    pair = 2 * HEAD
    by_bucket = pl.BlockSpec((BUCKET, width), lambda b, h, place: (b, 0))
    by_pair = pl.BlockSpec((None, pair, BUCKET), lambda b, h, place: (b, h, 0))
    return pl.pallas_call(
        attend_back_kernel,
        grid_spec=pltpu.PrefetchScalarGridSpec(
            num_scalar_prefetch=1,
            grid=(blocks, width // pair),
            in_specs=[
                pl.BlockSpec(memory_space=pltpu.SMEM),
                by_bucket,
                by_bucket,
                ANYWHERE,
                ANYWHERE,
                ANYWHERE,
                by_pair,
                by_pair,
                by_pair,
                pl.BlockSpec((1, 1, BUCKET), lambda b, h, place: (place[0] * blocks + b, 0, 0)),
            ],
            out_specs=[
                pl.BlockSpec((3, 1, pair, BUCKET), lambda b, h, place: (0, b, h, 0)),
                by_bucket,
                pl.BlockSpec((1, 8, pair), lambda b, h, place: (b, 0, h)),
            ],
            scratch_shapes=[
                pltpu.VMEM((BUCKET, BUCKET), f32),
                pltpu.VMEM((width, BUCKET), bf16),
                pltpu.VMEM((3, width // pair, BUCKET, pair), bf16),
                pltpu.VMEM((width, own.shape[1]), bf16),
                pltpu.VMEM(mixer.shape, bf16),
                pltpu.SemaphoreType.DMA((1 + width // own.shape[0],)),
            ],
        ),
        out_shape=[
            jax.ShapeDtypeStruct((3, blocks, width, BUCKET), bf16),
            jax.ShapeDtypeStruct((rows, width), bf16),
            jax.ShapeDtypeStruct((blocks, 8, width), f32),
        ],
        compiler_params=params(2),
        name="attend_back",
        cost_estimate=cost(20),
    )(
        place, lengths, grad_attended, grad_first, own, remote, mixer, queries, keys, values, key_mask
    )


def attention_grads_kernel(
    n_places, adds, info_ref, grads_ref, mixed_ref, tokens_ref, grad_attended_ref, *rest
):
    if adds:
        other_refs, small_ref, rest = rest[:n_places], rest[n_places], rest[n_places + 1 :]
    out_refs, whole = rest[:-1], rest[-1]
    step = pl.program_id(0)
    which = info_ref[step]
    n_z, buckets, mine, _ = mixed_ref.shape
    count = mine // n_places

    @pl.when(which < 3)
    def _():
        whole[...] = sum(
            dot(grads_ref[0, b], tokens_ref[b * BUCKET : (b + 1) * BUCKET, :])
            for b in range(buckets)
        ).astype(bf16)

    @pl.when(which == 3)
    def _():
        for t in range(n_z):
            whole[t * mine : (t + 1) * mine, :] = sum(
                dot(mixed_ref[t, b], grad_attended_ref[b * BUCKET : (b + 1) * BUCKET, :])
                for b in range(buckets)
            ).astype(bf16)

    for number in range(n_places):
        for s in range(n_z):
            start = lax.rem(info_ref[2] + s, n_z) * mine + (info_ref[3] ^ number) * count
            value = whole[pl.ds(pl.multiple_of(start, 16), count), :]
            if adds:
                value = value.astype(f32) + other_refs[number][s, 0].astype(f32)
                row = (2 * s + step) * count
                out_refs[number][pl.ds(pl.multiple_of(row, 16), count), :] = value.astype(bf16)
            else:
                out_refs[number][s, 0] = value

    if adds:
        for number in range(n_places):
            out_refs[number][2 * n_z * count :, :] = small_ref[...]


def attention_grads(n_places, info, grads, mixed, tokens, grad_attended, other=None, small=None):
    rows, width = grad_attended.shape
    n_z, buckets = mixed.shape[:2]
    mine = width // n_z
    count = mine // n_places
    by_step = pl.BlockSpec((n_z, 1, count, width), lambda i, info: (0, i, 0, 0))
    in_specs = [
        pl.BlockSpec(
            (1, buckets, width, BUCKET), lambda i, info: (jnp.minimum(info[i], 2), 0, 0, 0)
        ),
        fixed((n_z, buckets, mine, BUCKET)),
        pl.BlockSpec((rows, width), lambda i, info: (info[2], 0)),
        fixed((rows, width)),
    ]
    args = [grads, mixed, tokens, grad_attended]
    if other is None:
        shapes = [((n_z, 2, count, width), by_step)] * n_places
    else:
        in_specs += [by_step] * n_places + [fixed(small.shape)]
        args += list(other) + [small]
        flat = (2 * n_z * count + small.shape[0], width)
        shapes = [(flat, fixed(flat))] * n_places
    return pl.pallas_call(
        functools.partial(attention_grads_kernel, n_places, other is not None),
        grid_spec=pltpu.PrefetchScalarGridSpec(
            num_scalar_prefetch=1,
            grid=(2,),
            in_specs=in_specs,
            out_specs=[spec for _, spec in shapes],
            scratch_shapes=[pltpu.VMEM((width, width), bf16)],
        ),
        out_shape=[jax.ShapeDtypeStruct(shape, bf16) for shape, _ in shapes],
        compiler_params=params(1),
        name="attention_grads",
        cost_estimate=cost(0.5),
    )(info, *args)


def together(*values):
    return lax.optimization_barrier(values)


def add(first, *others):
    total = first.astype(f32)
    for other in others:
        total = total + other.astype(f32)
    return total.astype(bf16)


class Plane:
    def __init__(self, n_dp, n_z):
        self.n_dp, self.n_z = n_dp, n_z
        self.n_group = min(n_dp, 8)
        self.n_places = self.n_group // 2
        self.dp = lax.axis_index("dp")
        self.z = lax.axis_index("tensor")
        self.index = lax.rem(self.dp, self.n_group)
        self.core = self.index & 1
        self.place = self.index >> 1

    def swap(self, array, bits):
        return lax.ppermute(array, "dp", [(i, i ^ bits) for i in range(self.n_dp)])

    def shift(self, array, by):
        n = self.n_z
        return lax.ppermute(array, "tensor", [(i, (i + by) % n) for i in range(n)])

    def gather(self, piece):
        if self.n_dp == self.n_group:
            whole = lax.all_gather(piece, ("tensor", "dp"))
            return whole.reshape((self.n_z, self.n_group) + piece.shape)
        groups = [
            list(range(i, i + self.n_group)) for i in range(0, self.n_dp, self.n_group)
        ]
        line = lax.all_gather(piece, "tensor")
        return lax.all_gather(line, "dp", axis=1, axis_index_groups=groups)

    def turned(self, array):
        bit = 1
        while bit < self.n_group:
            lead = array.reshape((-1, 2, bit) + array.shape[1:])
            array = jnp.where((self.index & bit) != 0, lead[:, ::-1], lead).reshape(array.shape)
            bit *= 2
        return array

    def to_places(self, parts):
        return [self.swap(parts[number], 2 * number) for number in range(1, self.n_places)]

    def from_places(self, own, arrived):
        found = jnp.stack([own] + arrived)
        bit = 1
        while bit < self.n_places:
            lead = found.reshape((-1, 2, bit) + own.shape)
            flipped = lead[:, ::-1]
            found = jnp.where((self.place & bit) != 0, flipped, lead).reshape(found.shape)
            bit *= 2
        return found

    def by_core(self, own, other):
        return jnp.where(
            self.core == 1, jnp.stack([other, own]), jnp.stack([own, other])
        )

    def over_groups(self, array):
        bit = self.n_group
        while bit < self.n_dp:
            array = add(array, self.swap(array, bit))
            bit *= 2
        return array


def on_device(
    n_dp,
    n_z,
    tokens,
    lengths,
    key_mask,
    query_weight,
    query_bias,
    key_weight,
    value_weight,
    value_bias,
    output_weight,
    output_bias,
    first_gain,
    first_shift,
    inner_weight,
    inner_bias,
    outer_weight,
    outer_bias,
    second_gain,
    second_shift,
    cotangent,
):
    width = tokens.shape[1]
    mine = query_weight.shape[1]
    units = inner_weight.shape[1]
    all_rows = tokens.shape[0]
    all_blocks = all_rows // BUCKET
    rows = all_rows // n_z
    plane = Plane(n_dp, n_z)
    z, core, place, index = plane.z, plane.core, plane.place, plane.index
    n_places = plane.n_places
    others = range(1, n_z)

    feed_rows = units // plane.n_group
    head_rows = mine // plane.n_group
    mixer_count = width // plane.n_group
    piece = jnp.concatenate(
        [
            lax.dynamic_slice_in_dim(inner_weight, index * feed_rows, feed_rows, 1).T,
            lax.dynamic_slice_in_dim(outer_weight, index * feed_rows, feed_rows, 0),
        ],
        axis=1,
    )
    line = [plane.shift(piece, s) for s in others]

    mixer = plane.gather(
        lax.dynamic_slice_in_dim(output_weight, index * head_rows, head_rows, 0)
    ).reshape(width, width)
    query_t, key_t, value_t = query_weight.T, key_weight.T, value_weight.T

    key_mask_rows = key_mask.reshape(all_blocks, 1, BUCKET)
    bias_row = jnp.concatenate([query_bias, value_bias, inner_bias])
    bias_rows = jnp.pad(bias_row, (0, 16 * BUCKET - bias_row.shape[0])).reshape(16, BUCKET)
    place_z = z.reshape(1)
    mixed = attend_forward(
        n_z, lengths, tokens, query_t, key_t, value_t, bias_rows, key_mask_rows
    )
    mixed, line = together(mixed, line)

    near = jnp.stack(line)
    by_x, by_y = plane.swap(near, 2), plane.swap(near, 4)
    mixed, near = together(mixed, near)
    mixed = lax.all_to_all(mixed, "tensor", 0, 0)
    own_units = jnp.concatenate([inner_weight.T, outer_weight], axis=1)

    attention_own = jnp.concatenate([query_t, key_t, value_t], axis=1)
    attention_piece = lax.dynamic_slice_in_dim(attention_own, index * head_rows, head_rows, 0)
    attention_line = [plane.shift(attention_piece, s) for s in others]
    by_x, by_y, mixer = together(by_x, by_y, mixer)

    biases = mixed[:, 0, mine:].reshape(n_z, -1)[:, : bias_row.shape[0]].astype(f32)
    head_biases = jnp.pad(
        jnp.stack([biases[:, :mine], biases[:, mine : 2 * mine]], axis=1), ((0, 0), (0, 6), (0, 0))
    )
    inner_biases = biases[:, 2 * mine :]
    inner_biases = jnp.concatenate(
        [
            lax.dynamic_slice_in_dim(inner_biases, lax.rem(z + n_z - s, n_z), 1, 0)
            for s in range(n_z)
        ],
        axis=0,
    )
    inner_biases = inner_biases.reshape(n_z, plane.n_group, feed_rows).transpose(1, 0, 2)
    inner_biases = plane.turned(inner_biases).reshape(n_places, 2, 1, n_z * feed_rows)
    inner_biases = inner_biases.transpose(1, 0, 2, 3).reshape(plane.n_group, 1, -1)
    vectors = jnp.stack(
        [output_bias, first_gain, first_shift, outer_bias, second_gain, second_shift]
        + [jnp.zeros_like(output_bias)] * 2
    ).astype(f32)

    info = jnp.stack([z, place, core])
    shared_args = (info, vectors, inner_biases, own_units)
    cut = feed_rows // 2
    far = [plane.swap(by_x[:, :cut], 4), plane.swap(by_y[:, cut:], 2)]
    send = [plane.swap(units_of, 1) for units_of in (near, by_x, by_y)]
    hidden, slope, normed_low, first_normed, first_scale, second_sum = feed_forward(
        ((0, 0), (0, 1), (0, 2), (1, 0), (1, 1), (1, 2)),
        *shared_args,
        [near, by_x, by_y] + send,
        first=(tokens, mixed, mixer),
    )
    second_sum, far, attention_line = together(second_sum, far, attention_line)
    attention_line = jnp.stack(attention_line)
    attention_swaps = plane.to_places([attention_line] * n_places)
    far_send = [plane.swap(half, 1) for half in far]
    keep = [near, by_x, by_y] + far
    send = send + far_send
    hidden, slope, my_output, grad_second, grad_outer, second_sums = feed_forward(
        ((0, 3), (1, 3)), *shared_args, far + far_send,
        going=(normed_low, second_sum, hidden, slope), last=(lengths, cotangent),
    )
    output = lax.all_gather(my_output, "tensor", axis=0, tiled=True)

    grad_outer, attention_swaps = together(grad_outer, attention_swaps)
    attention_half = plane.from_places(attention_line, attention_swaps)
    attention_other = plane.swap(attention_half, 1)

    shared_args = (info, grad_outer, normed_low, hidden, slope, own_units)
    sent_early, sent_late, bias_sent, grad_normed = feed_back(*shared_args, grad_second, send)
    other = [plane.swap(sent_early, 1), plane.swap(sent_late, 1)]
    grad_normed, attention_other = together(grad_normed, attention_other)
    attention_remote = plane.by_core(attention_half, attention_other)
    attention_remote = attention_remote.transpose(2, 1, 0, 3, 4).reshape(n_z - 1, mine, 3 * width)
    projected = project(
        place_z, tokens, attention_own, attention_remote, head_biases, rows // BUCKET
    )
    projected, other = together(projected, other)
    (
        inner_stay, outer_stay, inner_go, outer_go, bias_kept, grad_first, grad_attended, first_sums
    ) = feed_back(
        *shared_args, grad_normed, keep, other,
        (first_normed, first_scale, vectors),
    )
    inner_came, outer_came = plane.swap(inner_go, 4), plane.swap(outer_go, 2)
    bias_grads = jnp.stack(
        [bias_kept[:, 0], bias_sent[:, 0]], axis=1
    )
    inner_bias_grad = plane.turned(bias_grads.reshape(plane.n_group, n_z, feed_rows))
    inner_bias_grad = inner_bias_grad.transpose(1, 0, 2)
    inner_bias_grad = jnp.concatenate(
        [
            sum(
                jnp.where(lax.rem(z - t + n_z, n_z) == s, inner_bias_grad[s : s + 1], 0.0)
                for s in range(n_z)
            )
            for t in range(n_z)
        ],
        axis=0,
    ).reshape(n_z, units)

    grads, my_tokens_grad, back_sums = attend_back(
        place_z, lengths, grad_attended, grad_first, attention_own, attention_remote, mixer,
        *projected, key_mask_rows,
    )
    grads, inner_came, outer_came, output = together(grads, inner_came, outer_came, output)
    inner_on, outer_on = (
        plane.swap(add(inner_stay[1], inner_came[1]), 2),
        plane.swap(add(outer_stay[1], outer_came[1]), 4),
    )
    tokens_grad = lax.all_gather(my_tokens_grad, "tensor", axis=0, tiled=True)

    def weight_grads(side, other=None, small=None):
        info = jnp.stack([2 * side, 2 * side + 1, z, place])
        return attention_grads(
            n_places, info, grads, mixed, tokens, grad_attended, other, small
        )

    sent = weight_grads(1 - core)
    sent, back_sums, first_sums, second_sums, inner_bias_grad = together(
        sent, back_sums, first_sums, second_sums, inner_bias_grad
    )
    other = [plane.swap(part, 1) for part in sent]

    small = jnp.concatenate(
        [first_sums[:3], second_sums[:3], inner_bias_grad, jnp.sum(back_sums, axis=0)[:2]], axis=0
    )
    small = jnp.pad(small, ((0, -small.shape[0] % 16), (0, 0))).astype(bf16)
    small_rows = small.shape[0]

    small = add(small, plane.swap(small, 1))
    kept = list(weight_grads(core, other, small))
    arrived = plane.to_places(kept)
    kept[0], inner_on, outer_on = together(kept[0], inner_on, outer_on)
    feed_parts = [
        jnp.concatenate(
            [
                add(inner_stay[0, s], inner_came[0, s], inner_on[s]),
                add(outer_stay[0, s], outer_came[0, s], outer_on[s]),
            ],
            axis=1,
        )
        for s in range(n_z)
    ]
    feed_line = [plane.shift(feed_parts[s], -s) for s in others]
    output = copied(output)
    arrived, output = together(arrived, output)
    small = add(small, *[a[-small_rows:] for a in arrived])
    count = 2 * mine // n_places
    attention_parts = [
        add(*[a[s * count : (s + 1) * count] for a in [kept[0]] + arrived]) for s in range(n_z)
    ]
    attention_line = [
        plane.shift(jnp.concatenate([attention_parts[s], small], axis=0), s) for s in others
    ]
    feed_total = plane.over_groups(add(feed_parts[0], *feed_line))
    feed_arrived = plane.to_places([feed_total] * n_places)
    tokens_grad = copied(tokens_grad)
    attention_line, feed_arrived, tokens_grad = together(
        attention_line, feed_arrived, tokens_grad
    )
    attention_total = plane.over_groups(
        add(attention_parts[0], *[a[:count] for a in attention_line])
    )
    small = plane.over_groups(add(small, *[a[count:] for a in attention_line])).astype(f32)
    arrived = plane.to_places([attention_total] * n_places)
    feed_half = plane.from_places(feed_total, feed_arrived)
    feed_other = plane.swap(feed_half, 1)
    inner_grad, outer_grad = finish_feed(core.reshape(1), feed_half, feed_other)
    inner_bias_sum = lax.dynamic_slice_in_dim(small, 6 + z, 1, 0)[0]
    head_sums = lax.dynamic_slice_in_dim(small[6 + n_z : 8 + n_z], z * mine, mine, 1)
    arrived, inner_grad, outer_grad, small, inner_bias_sum, head_sums = together(
        arrived, inner_grad, outer_grad, small, inner_bias_sum, head_sums
    )
    attention_half = plane.from_places(attention_total, arrived)
    attention_other = plane.swap(attention_half, 1)
    grad_list = plane.by_core(attention_half, attention_other)
    grad_list = grad_list.reshape(2, n_places, 2, mine // n_places, width)
    grad_list = grad_list.transpose(0, 2, 1, 3, 4).reshape(4, mine, width)

    shared = small[:6]

    return (
        output,
        tokens_grad,
        grad_list[0].T.astype(f32),
        head_sums[0],
        grad_list[1].T.astype(f32),
        grad_list[2].T.astype(f32),
        head_sums[1],
        grad_list[3].astype(f32),
        shared[0],
        shared[1],
        shared[2],
        inner_grad,
        inner_bias_sum,
        outer_grad,
        shared[3],
        shared[4],
        shared[5],
    )


def solution(mesh):
    n_dp, n_z = mesh.shape["dp"], mesh.shape["tensor"]
    in_specs = (
        P("dp", None),
        P("dp", None),
        P("dp"),
        P(None, "tensor"),
        P("tensor"),
        P(None, "tensor"),
        P(None, "tensor"),
        P("tensor"),
        P("tensor", None),
        P(),
        P(),
        P(),
        P(None, "tensor"),
        P("tensor"),
        P("tensor", None),
        P(),
        P(),
        P(),
        P("dp", None),
    )
    out_specs = (
        P("dp", None),
        P("dp", None),
        P(None, "tensor"),
        P("tensor"),
        P(None, "tensor"),
        P(None, "tensor"),
        P("tensor"),
        P("tensor", None),
        P(),
        P(),
        P(),
        P(None, "tensor"),
        P("tensor"),
        P("tensor", None),
        P(),
        P(),
        P(),
    )

    def program(*args):
        return on_device(n_dp, n_z, *args)

    return jax.shard_map(
        program, mesh=mesh, in_specs=in_specs, out_specs=out_specs, check_vma=False
    )
```

```python
import functools

import jax
import jax.numpy as jnp
from jax import lax
from jax.experimental import pallas as pl
from jax.experimental.pallas import tpu as pltpu
from jax.sharding import PartitionSpec as P

HEAD = 64
BUCKET = 512
ITEMS = 8


negative_fill = -1e30
epsilon = 1e-06
f32 = jnp.float32
bf16 = jnp.bfloat16
VMEM_BYTES = 56 * 1024 * 1024


def dot(left, right):
    return jnp.dot(left, right, preferred_element_type=f32)


def contract_rows(left, right):
    return lax.dot_general(left, right, (((0,), (0,)), ((), ())), preferred_element_type=f32)


def contract_cols(left, right):
    return lax.dot_general(left, right, (((1,), (1,)), ((), ())), preferred_element_type=f32)


def norm_rows(values):
    centred = values - jnp.mean(values, axis=1, keepdims=True)
    inv_scale = lax.rsqrt(jnp.mean(centred * centred, axis=1, keepdims=True) + epsilon)
    return centred * inv_scale, inv_scale


def norm_back(grad_rows, norm_gain, normed, inv_scale):
    scaled = grad_rows * norm_gain
    return inv_scale * (
        scaled
        - jnp.mean(scaled, axis=1, keepdims=True)
        - normed * jnp.mean(scaled * normed, axis=1, keepdims=True)
    )


def column_sum(matrix):
    return jnp.sum(matrix.astype(f32), axis=0, keepdims=True)


def fixed(shape):
    return pl.BlockSpec(shape, lambda *_: (0,) * len(shape))


def cost(microseconds):
    return pl.CostEstimate(
        flops=int(microseconds * 2.5e8),
        bytes_accessed=int(microseconds * 2.5e5),
        transcendentals=0,
    )


def params(axes):
    return pltpu.CompilerParams(
        dimension_semantics=("arbitrary",) * axes, vmem_limit_bytes=VMEM_BYTES
    )


def item_places(lengths_ref, row, shape, axis):
    places = lax.broadcasted_iota(jnp.int32, shape, axis)
    end = jnp.int32(0)
    items = jnp.zeros(shape, jnp.int32)
    for slot in range(ITEMS):
        end = end + lengths_ref[row, slot]
        items = items + (places >= end).astype(jnp.int32)
    return items


def as_column(row):
    return jnp.broadcast_to(row.astype(f32), (8, row.shape[1])).T[:, :1]


def mask_bias(lengths_ref, row, key_mask):
    shape = (BUCKET, BUCKET)
    diagonal = lax.broadcasted_iota(jnp.int32, shape, 0) == lax.broadcasted_iota(
        jnp.int32, shape, 1
    )
    item_row = item_places(lengths_ref, row, (1, BUCKET), 1)
    item_column = item_places(lengths_ref, row, (BUCKET, 1), 0)
    code_column = jnp.where(as_column(key_mask) == 1.0, item_column, -1)
    return jnp.where((code_column == item_row) | diagonal, 0.0, negative_fill).astype(f32)


def attend_forward_kernel(
    lengths_ref, tokens_ref, query_ref, key_ref, value_ref, biases_ref, key_mask_ref, mixed_ref,
):
    mine = query_ref.shape[0]
    rows = tokens_ref[...]
    queries = contract_cols(query_ref[...], rows) + as_column(biases_ref[0:1, :mine])
    queries = (queries.astype(bf16) * HEAD ** (-0.5)).astype(bf16)
    keys = contract_cols(rows, key_ref[...]).astype(bf16)
    values = contract_cols(value_ref[...], rows) + as_column(biases_ref[0:1, mine : 2 * mine])
    values = values.astype(bf16)
    bias = mask_bias(lengths_ref, pl.program_id(0), key_mask_ref[0])
    for head in range(mine // HEAD):
        at = slice(head * HEAD, (head + 1) * HEAD)
        scores = dot(keys[:, at], queries[at]) + bias
        exponent = jnp.exp(scores - jnp.max(scores, axis=0, keepdims=True))
        total = jnp.sum(exponent, axis=0, keepdims=True)
        mixed_ref[0, 0, at] = (dot(values[at], exponent.astype(bf16)) / total).astype(bf16)
    mixed_ref[0, 0, mine:] = biases_ref[...]


def attend_forward(n_z, lengths, tokens, query, key, value, biases, key_mask):
    blocks = lengths.shape[0]
    own = blocks // n_z
    mine, width = key.shape
    whole = (n_z, own, mine + biases.shape[0], BUCKET)
    return pl.pallas_call(
        attend_forward_kernel,
        grid=(blocks,),
        in_specs=[
            pl.BlockSpec(memory_space=pltpu.SMEM),
            pl.BlockSpec((BUCKET, width), lambda b: (b, 0)),
            fixed((mine, width)),
            fixed((mine, width)),
            fixed((mine, width)),
            fixed(biases.shape),
            pl.BlockSpec((1, 1, BUCKET), lambda b: (b, 0, 0)),
        ],
        out_specs=pl.BlockSpec((1, 1) + whole[2:], lambda b: (b // own, b % own, 0, 0)),
        out_shape=jax.ShapeDtypeStruct(whole, bf16),
        compiler_params=params(1),
        name="attend_forward",
        cost_estimate=cost(12),
    )(lengths, tokens, query, key, value, biases, key_mask)


def fetch_units(step, picks, own_ref, halves, units, sems):
    feed_rows = units.shape[2]
    cut = feed_rows // 2

    def copies(number):
        slot = number % 2
        row = pl.multiple_of(picks[number] * feed_rows, 16)
        ends = [
            (own_ref.at[pl.ds(row, feed_rows)], units.at[slot, 0]),
            (halves[number][0], units.at[slot, 1:, :cut]),
            (halves[number][1], units.at[slot, 1:, cut:]),
        ]
        return [
            pltpu.make_async_copy(source, target, sems.at[slot, i])
            for i, (source, target) in enumerate(ends)
        ]

    for number in range(len(halves)):

        @pl.when(step == number)
        def _(number=number):
            if number == 0:
                for copy in copies(0):
                    copy.start()
            if number + 1 < len(halves):
                for copy in copies(number + 1):
                    copy.start()
            for copy in copies(number):
                copy.wait()

    return units.at[lax.rem(step, 2)]


def take_halves(numbers, refs):
    halves, refs = [], list(refs)
    for number in numbers:
        if number == 3:
            halves.append((refs.pop(0), refs.pop(0)))
        else:
            ref = refs.pop(0)
            cut = ref.shape[1] // 2
            halves.append((ref.at[:, :cut], ref.at[:, cut:]))
    return halves, refs


def split_units(units):
    width = units.shape[2] // 2
    return units[:, :, :width].reshape(-1, width), units[:, :, width:].reshape(-1, width)


ANYWHERE = pl.BlockSpec(memory_space=pl.ANY)


def feed_forward_kernel(chunks, first, last, info_ref, *rest):
    def take(count):
        nonlocal rest
        taken, rest = rest[:count], rest[count:]
        return taken

    vectors_ref, bias_ref, own_ref = take(3)
    halves, rest = take_halves([number for _, number in chunks], rest)
    if first:
        tokens_ref, mixed_ref, mixer_ref = take(3)
    else:
        normed_low_ref, start_ref, _, _ = take(4)
    if last:
        lengths_ref, cotangent_ref = take(2)
    hidden_ref, slope_ref = take(2)
    if first:
        normed_low_ref, first_normed_ref, first_scale_ref = take(3)
    if last:
        output_ref, grad_second_ref, grad_outer_ref, sums_ref = take(4)
    else:
        (second_sum,) = take(1)
    units, sems = take(2)
    if last:
        (second_sum,) = take(1)

    step = pl.program_id(0)
    picks = [(info_ref[1] ^ number) * 2 + (info_ref[2] ^ side) for side, number in chunks]
    weights = fetch_units(step, picks, own_ref, halves, units, sems)
    output_bias, first_gain, first_shift, outer_bias, second_gain, second_shift = (
        vectors_ref[i : i + 1, :] for i in range(6)
    )

    @pl.when(step == 0)
    def _():
        if first:
            n_z, own, mine, _ = mixed_ref.shape
            attended = output_bias + jnp.concatenate(
                [
                    sum(
                        contract_rows(mixed_ref[t, b], mixer_ref[t * mine : (t + 1) * mine, :])
                        for t in range(n_z)
                    )
                    for b in range(own)
                ],
                axis=0,
            )
            normed, inv_scale = norm_rows(tokens_ref[...].astype(f32) + attended)
            whole = normed * first_gain + first_shift
            first_normed_ref[...] = normed
            first_scale_ref[...] = inv_scale
            normed_low_ref[...] = whole.astype(bf16)
            second_sum[...] = whole + outer_bias
        else:
            second_sum[...] = start_ref[...]

    inner, outer = split_units(weights)
    inner_pre = contract_cols(normed_low_ref[...], inner) + bias_ref[0]
    normal_cdf = 0.5 + 0.5 * lax.erf(inner_pre * 0.7071067811865476)
    bell = jnp.exp(-0.5 * inner_pre * inner_pre)
    hidden = (inner_pre * normal_cdf).astype(bf16)
    hidden_ref[...] = hidden.T
    slope_ref[...] = (normal_cdf + inner_pre * bell * 0.3989422804014327).astype(bf16)
    second_sum[...] += dot(hidden, outer)

    if last:

        @pl.when(step == pl.num_programs(0) - 1)
        def _():
            normed, inv_scale = norm_rows(second_sum[...])
            blocks = normed.shape[0] // BUCKET
            live = jnp.concatenate(
                [
                    (item_places(lengths_ref, info_ref[0] * blocks + b, (BUCKET, 1), 0) < ITEMS)
                    for b in range(blocks)
                ],
                axis=0,
            ).astype(f32)
            output_ref[...] = ((normed * second_gain + second_shift) * live).astype(bf16)
            grad_final = cotangent_ref[...].astype(f32) * live
            grad_second = norm_back(grad_final, second_gain, normed, inv_scale)
            grad_outer = grad_second.astype(bf16)
            grad_second_ref[...] = grad_second
            grad_outer_ref[...] = grad_outer
            sums_ref[0:1, :] = column_sum(grad_outer)
            sums_ref[1:2, :] = column_sum(grad_final * normed)
            sums_ref[2:3, :] = column_sum(grad_final)


def feed_forward(chunks, info, vectors, biases, own, halves, first=None, going=None, last=None):
    width = vectors.shape[1]
    n_z = halves[0].shape[0] + 1
    feed_rows, twice = own.shape[0] // 8, 2 * width
    rows = first[1].shape[1] * BUCKET if first else going[0].shape[0]
    chunk = n_z * feed_rows
    whole = fixed((rows, width))
    my_rows = pl.BlockSpec((rows, width), lambda j, info: (info[0], 0))
    at = lambda j, info: info[3 + j]
    hidden_spec = pl.BlockSpec((chunk, rows), lambda j, info: (at(j, info), 0))
    slope_spec = pl.BlockSpec((rows, chunk), lambda j, info: (0, at(j, info)))
    in_specs = [
        fixed((8, width)),
        pl.BlockSpec((1, 1, chunk), lambda j, info: (at(j, info), 0, 0)),
        ANYWHERE,
    ] + [ANYWHERE] * len(halves)
    args = [vectors, biases, own] + halves
    shapes = [
        ((8 * chunk, rows), bf16, hidden_spec),
        ((rows, 8 * chunk), bf16, slope_spec),
    ]
    scratch = [
        pltpu.VMEM((2, n_z, feed_rows, twice), bf16),
        pltpu.SemaphoreType.DMA((2, 3)),
    ]
    aliases = {}
    if first:
        tokens, mixed, mixer = first
        mine = width // n_z
        in_specs += [my_rows, fixed((n_z, mixed.shape[1], mine, BUCKET)), fixed(mixer.shape)]
        args += [tokens, mixed, mixer]
        shapes += [
            ((rows, width), bf16, whole),
            ((rows, width), f32, whole),
            ((rows, 1), f32, fixed((rows, 1))),
        ]
    else:
        aliases = {1 + len(args) + 2: 0, 1 + len(args) + 3: 1}
        in_specs += [whole, whole, ANYWHERE, ANYWHERE]
        args += list(going)
    if last:
        in_specs += [pl.BlockSpec(memory_space=pltpu.SMEM), my_rows]
        args += list(last)
        shapes += [
            ((rows, width), bf16, whole),
            ((rows, width), f32, whole),
            ((rows, width), bf16, whole),
            ((8, width), f32, fixed((8, width))),
        ]
        scratch.append(pltpu.VMEM((rows, width), f32))
    else:
        shapes.append(((rows, width), f32, whole))
    info = jnp.concatenate(
        [info, jnp.array([4 * side + number for side, number in chunks], jnp.int32)]
    )
    return pl.pallas_call(
        functools.partial(feed_forward_kernel, chunks, first is not None, last is not None),
        grid_spec=pltpu.PrefetchScalarGridSpec(
            num_scalar_prefetch=1,
            grid=(len(chunks),),
            in_specs=in_specs,
            out_specs=[spec for _, _, spec in shapes],
            scratch_shapes=scratch,
        ),
        out_shape=[jax.ShapeDtypeStruct(shape, kind) for shape, kind, _ in shapes],
        input_output_aliases=aliases,
        compiler_params=params(1),
        name="feed_forward",
        cost_estimate=cost(3 * len(chunks)),
    )(info, *args)


STAY = ((0, 1), (0, 2))
GO = ((2, 3), (1, 3))


def feed_back_kernel(
    keeps, info_ref, grad_outer_ref, normed_low_ref, hidden_ref, slope_ref,
    own_ref, start_ref, *rest,
):
    halves, rest = take_halves(range(4), rest)
    if keeps:
        other_refs, norm_refs, rest = rest[:2], rest[2:5], rest[5:]
        stay_refs, go_refs, rest = rest[0:2], rest[2:4], rest[4:]
        bias_grad_ref, grad_first_ref, grad_attended_ref, sums_ref, units, sems = rest[:6]
        grad_normed_ref = rest[6]
    else:
        *grad_refs, bias_grad_ref, grad_normed_ref, units, sems = rest
    step = pl.program_id(0)
    side = info_ref[2] if keeps else 1 - info_ref[2]
    picks = [(info_ref[1] ^ number) * 2 + side for number in range(4)]
    weights = fetch_units(step, picks, own_ref, halves, units, sems)

    @pl.when(step == 0)
    def _():
        grad_normed_ref[...] = start_ref[...]

    n_z, feed_rows, twice = weights.shape
    width = twice // 2
    inner, outer = split_units(weights)
    grad_outer = grad_outer_ref[...]
    grad_hidden = contract_cols(grad_outer, outer)
    grad_inner = (grad_hidden * slope_ref[...].astype(f32)).astype(bf16)
    outer_grad = dot(hidden_ref[...], grad_outer).reshape(n_z, feed_rows, width)
    inner_grad = contract_rows(grad_inner, normed_low_ref[...]).reshape(n_z, feed_rows, width)
    bias_grad_ref[0] = column_sum(grad_inner)
    grad_normed_ref[...] += dot(grad_inner, inner)

    for number in range(4):

        @pl.when(step == number)
        def _(number=number):
            for track, value in enumerate((inner_grad, outer_grad)):
                at = slice(track * width, (track + 1) * width)
                if keeps:
                    found = value + other_refs[number // 2][0, :, :, at].astype(f32)
                    ref = stay_refs[track] if number in STAY[track] else go_refs[track]
                    ref[0] = found.astype(bf16)
                else:
                    grad_refs[number // 2][0, :, :, at] = value.astype(bf16)

    if keeps:

        @pl.when(step == pl.num_programs(0) - 1)
        def _():
            first_normed_ref, first_scale_ref, vectors_ref = norm_refs
            grad_rows, normed = grad_normed_ref[...], first_normed_ref[...]
            grad_first = norm_back(grad_rows, vectors_ref[1:2, :], normed, first_scale_ref[...])
            grad_attended = grad_first.astype(bf16)
            grad_first_ref[...] = grad_first
            grad_attended_ref[...] = grad_attended
            sums_ref[0:1, :] = column_sum(grad_attended)
            sums_ref[1:2, :] = column_sum(grad_rows * normed)
            sums_ref[2:3, :] = column_sum(grad_rows)


def feed_back(
    info, grad_outer, normed_low, hidden, slope, own, start, units, others=None, norm=None
):
    rows, width = grad_outer.shape
    keeps = others is not None
    count = 4
    feed_rows, twice = own.shape[0] // 8, 2 * width
    n_z = units[0].shape[0] + 1
    chunk = n_z * feed_rows
    flip = 0 if keeps else 1
    columns = pl.BlockSpec((rows, chunk), lambda i, info: (0, 4 * flip + i))
    whole = fixed((rows, width))
    part = (n_z, feed_rows, twice)
    track = (2, n_z, feed_rows, width)
    unit_rows = pl.BlockSpec((chunk, rows), lambda i, info: (4 * flip + i, 0))
    in_specs = [whole, whole, unit_rows, columns, ANYWHERE, whole] + [ANYWHERE] * len(units)
    args = [grad_outer, normed_low, hidden, slope, own, start] + units
    bias_shape = (
        (count, 1, chunk),
        f32,
        pl.BlockSpec((1, 1, chunk), lambda i, info: (i, 0, 0)),
    )
    scratch = [pltpu.VMEM((2,) + part, bf16), pltpu.SemaphoreType.DMA((2, 3))]

    def one(shape, at):
        return pl.BlockSpec((1,) + shape[1:], lambda i, info: (at(i), 0, 0, 0))

    early, late = (lambda i: jnp.minimum(i, 1)), (lambda i: jnp.maximum(i - 2, 0))
    pair = (2,) + part
    if keeps:
        in_specs += [one(pair, early), one(pair, late)]
        in_specs += [whole, fixed((rows, 1)), fixed((8, width))]
        args += list(others) + list(norm)
        slow, slower = (lambda i: i // 2), (lambda i: jnp.maximum(i - 1, 0) // 2)
        shapes = [(track, bf16, one(track, at)) for at in (early, slow, late, slower)] + [
            bias_shape,
            ((rows, width), f32, whole),
            ((rows, width), bf16, whole),
            ((8, width), f32, fixed((8, width))),
        ]
        scratch.append(pltpu.VMEM((rows, width), f32))
    else:
        shapes = [
            (pair, bf16, one(pair, early)),
            (pair, bf16, one(pair, late)),
            bias_shape,
            ((rows, width), f32, whole),
        ]
    return pl.pallas_call(
        functools.partial(feed_back_kernel, keeps),
        grid_spec=pltpu.PrefetchScalarGridSpec(
            num_scalar_prefetch=1,
            grid=(count,),
            in_specs=in_specs,
            out_specs=[spec for _, _, spec in shapes],
            scratch_shapes=scratch,
        ),
        out_shape=[jax.ShapeDtypeStruct(shape, kind) for shape, kind, _ in shapes],
        compiler_params=params(1),
        name="feed_back_own" if keeps else "feed_back",
        cost_estimate=cost(3 * count),
    )(info, *args)


def finish_feed_kernel(core_ref, own_ref, other_ref, inner_ref, outer_ref, inner_rows):
    places, count, twice = own_ref.shape
    width = twice // 2
    for source, side in ((own_ref, core_ref[0]), (other_ref, 1 - core_ref[0])):
        for place in range(places):
            row = pl.multiple_of((2 * place + side) * count, 16)
            inner_rows[pl.ds(row, count), :] = source[place, :, :width].astype(f32)
            outer_ref[pl.ds(row, count), :] = source[place, :, width:].astype(f32)
    inner_ref[...] = inner_rows[...].T


def finish_feed(core, own, other):
    places, count, twice = own.shape
    shape = (2 * places * count, twice // 2)
    inner_shape = (shape[1], shape[0])
    return pl.pallas_call(
        finish_feed_kernel,
        grid_spec=pltpu.PrefetchScalarGridSpec(
            num_scalar_prefetch=1,
            grid=(1,),
            in_specs=[fixed(own.shape), fixed(other.shape)],
            out_specs=[fixed(inner_shape), fixed(shape)],
            scratch_shapes=[pltpu.VMEM(shape, f32)],
        ),
        out_shape=[
            jax.ShapeDtypeStruct(inner_shape, f32),
            jax.ShapeDtypeStruct(shape, f32),
        ],
        compiler_params=params(1),
        name="finish_feed",
        cost_estimate=cost(5),
    )(core, own, other)


def copy_kernel(from_ref, to_ref):
    to_ref[...] = from_ref[...]


def copied(array):
    block = pl.BlockSpec((BUCKET, array.shape[1]), lambda i: (i, 0))
    return pl.pallas_call(
        copy_kernel,
        grid=(array.shape[0] // BUCKET,),
        in_specs=[block],
        out_specs=block,
        out_shape=jax.ShapeDtypeStruct(array.shape, array.dtype),
        compiler_params=params(1),
        name="copied",
        cost_estimate=cost(0.5),
    )(array)


def project_kernel(
    place_ref, tokens_ref, own_ref, remote_ref, biases_ref, query_ref, key_ref, value_ref
):
    rows = tokens_ref[...]
    width = rows.shape[1]
    weights = jnp.where(pl.program_id(1) == 0, own_ref[...], remote_ref[0])
    queries = contract_cols(weights[:, :width], rows) + as_column(biases_ref[0, 0:1, :])
    query_ref[...] = (queries.astype(bf16) * HEAD ** (-0.5)).astype(bf16)
    key_ref[...] = contract_cols(weights[:, width : 2 * width], rows).astype(bf16)
    values = contract_cols(weights[:, 2 * width :], rows) + as_column(biases_ref[0, 1:2, :])
    value_ref[...] = values.astype(bf16)


def project(place, tokens, own, remote, biases, buckets):
    width = tokens.shape[1]
    mine = own.shape[0]
    n_z = width // mine
    there = lambda s, place: lax.rem(place[0] + n_z - s, n_z)
    out = pl.BlockSpec((None, mine, BUCKET), lambda b, s, place: (b, there(s, place), 0))
    return pl.pallas_call(
        project_kernel,
        grid_spec=pltpu.PrefetchScalarGridSpec(
            num_scalar_prefetch=1,
            grid=(buckets, n_z),
            in_specs=[
                pl.BlockSpec((BUCKET, width), lambda b, s, place: (place[0] * buckets + b, 0)),
                fixed(own.shape),
                pl.BlockSpec(
                    (1, mine, 3 * width), lambda b, s, place: (jnp.maximum(s - 1, 0), 0, 0)
                ),
                pl.BlockSpec((1, 8, mine), lambda b, s, place: (there(s, place), 0, 0)),
            ],
            out_specs=[out] * 3,
        ),
        out_shape=[jax.ShapeDtypeStruct((buckets, width, BUCKET), bf16)] * 3,
        compiler_params=params(2),
        name="project",
        cost_estimate=cost(5),
    )(place, tokens, own, remote, biases)


def attend_back_kernel(
    place_ref, lengths_ref, grad_attended_ref, grad_first_ref, own_ref, remote_ref, mixer_ref,
    query_ref, key_ref, value_ref, key_mask_ref,
    grads_ref, tokens_grad_ref, sums_ref,
    bias, grad_mixed_t, whole, weights, mixer, sems,
):
    pair = pl.program_id(1)
    pairs, width = whole.shape[1], weights.shape[0]
    mine = own_ref.shape[0]
    n_z = width // mine

    def fetches():
        ends = [(mixer_ref, mixer)]
        for s in range(n_z):
            row = pl.multiple_of(lax.rem(place_ref[0] + n_z - s, n_z) * mine, 16)
            source = own_ref if s == 0 else remote_ref.at[s - 1]
            ends.append((source, weights.at[pl.ds(row, mine)]))
        return [
            pltpu.make_async_copy(source, target, sems.at[i])
            for i, (source, target) in enumerate(ends)
        ]

    @pl.when(pair == 0)
    def _():
        for fetch in fetches():
            fetch.start()
        row = place_ref[0] * pl.num_programs(0) + pl.program_id(0)
        bias[...] = mask_bias(lengths_ref, row, key_mask_ref[0])
        for fetch in fetches():
            fetch.wait()
        grad_mixed_t[...] = contract_cols(mixer[...], grad_attended_ref[...]).astype(bf16)

    queries, keys_t = query_ref[...], key_ref[...]
    keys, values = keys_t.T, value_ref[...].T
    start = pl.multiple_of(pair * keys.shape[1], 128)
    grad_mixed = grad_mixed_t[pl.ds(start, keys.shape[1]), :]
    grad_queries, grad_keys, grad_values = [], [], []
    for head in range(keys.shape[1] // HEAD):
        at = slice(head * HEAD, (head + 1) * HEAD)
        scores = dot(keys[:, at], queries[at]) + bias[...]
        exponent = jnp.exp(scores - jnp.max(scores, axis=0, keepdims=True))
        probs = exponent * (1.0 / jnp.sum(exponent, axis=0, keepdims=True))
        grad_probs = dot(values[:, at], grad_mixed[at])
        shift = jnp.sum(probs * grad_probs, axis=0, keepdims=True)
        grad_scores = (probs * (grad_probs - shift)).astype(bf16)
        grad_values.append(contract_cols(probs.astype(bf16), grad_mixed[at]))
        grad_keys.append(contract_cols(grad_scores, queries[at]))
        grad_queries.append(dot(keys_t[at], grad_scores) * HEAD ** (-0.5))
    query_t = jnp.concatenate(grad_queries, axis=0).astype(bf16)
    found = (
        query_t.T,
        jnp.concatenate(grad_keys, axis=1).astype(bf16),
        jnp.concatenate(grad_values, axis=1).astype(bf16),
    )
    for number, grad in enumerate(found):
        grads_ref[number, 0] = query_t if number == 0 else grad.T
        whole[number, pair] = grad
    sums_ref[0, 0:1, :] = column_sum(found[0])
    sums_ref[0, 1:2, :] = column_sum(found[2])

    @pl.when(pair == pl.num_programs(1) - 1)
    def _():
        total = grad_first_ref[...]
        for number in range(3):
            grad = jnp.concatenate([whole[number, i] for i in range(pairs)], axis=1)
            total += dot(grad, weights[:, number * width : (number + 1) * width])
        tokens_grad_ref[...] = total.astype(bf16)


def attend_back(
    place, lengths, grad_attended, grad_first, own, remote, mixer, queries, keys, values, key_mask
):
    rows, width = grad_attended.shape
    blocks = rows // BUCKET
    pair = 2 * HEAD
    by_bucket = pl.BlockSpec((BUCKET, width), lambda b, h, place: (b, 0))
    by_pair = pl.BlockSpec((None, pair, BUCKET), lambda b, h, place: (b, h, 0))
    return pl.pallas_call(
        attend_back_kernel,
        grid_spec=pltpu.PrefetchScalarGridSpec(
            num_scalar_prefetch=1,
            grid=(blocks, width // pair),
            in_specs=[
                pl.BlockSpec(memory_space=pltpu.SMEM),
                by_bucket,
                by_bucket,
                ANYWHERE,
                ANYWHERE,
                ANYWHERE,
                by_pair,
                by_pair,
                by_pair,
                pl.BlockSpec((1, 1, BUCKET), lambda b, h, place: (place[0] * blocks + b, 0, 0)),
            ],
            out_specs=[
                pl.BlockSpec((3, 1, pair, BUCKET), lambda b, h, place: (0, b, h, 0)),
                by_bucket,
                pl.BlockSpec((1, 8, pair), lambda b, h, place: (b, 0, h)),
            ],
            scratch_shapes=[
                pltpu.VMEM((BUCKET, BUCKET), f32),
                pltpu.VMEM((width, BUCKET), bf16),
                pltpu.VMEM((3, width // pair, BUCKET, pair), bf16),
                pltpu.VMEM((width, own.shape[1]), bf16),
                pltpu.VMEM(mixer.shape, bf16),
                pltpu.SemaphoreType.DMA((1 + width // own.shape[0],)),
            ],
        ),
        out_shape=[
            jax.ShapeDtypeStruct((3, blocks, width, BUCKET), bf16),
            jax.ShapeDtypeStruct((rows, width), bf16),
            jax.ShapeDtypeStruct((blocks, 8, width), f32),
        ],
        compiler_params=params(2),
        name="attend_back",
        cost_estimate=cost(20),
    )(
        place, lengths, grad_attended, grad_first, own, remote, mixer, queries, keys, values, key_mask
    )


def attention_grads_kernel(
    n_places, adds, info_ref, grads_ref, mixed_ref, tokens_ref, grad_attended_ref, *rest
):
    if adds:
        other_refs, small_ref, rest = rest[:n_places], rest[n_places], rest[n_places + 1 :]
    out_refs, whole = rest[:-1], rest[-1]
    step = pl.program_id(0)
    which = info_ref[step]
    n_z, buckets, mine, _ = mixed_ref.shape
    count = mine // n_places

    @pl.when(which < 3)
    def _():
        whole[...] = sum(
            dot(grads_ref[0, b], tokens_ref[b * BUCKET : (b + 1) * BUCKET, :])
            for b in range(buckets)
        ).astype(bf16)

    @pl.when(which == 3)
    def _():
        for t in range(n_z):
            whole[t * mine : (t + 1) * mine, :] = sum(
                dot(mixed_ref[t, b], grad_attended_ref[b * BUCKET : (b + 1) * BUCKET, :])
                for b in range(buckets)
            ).astype(bf16)

    for number in range(n_places):
        for s in range(n_z):
            start = lax.rem(info_ref[2] + s, n_z) * mine + (info_ref[3] ^ number) * count
            value = whole[pl.ds(pl.multiple_of(start, 16), count), :]
            if adds:
                value = value.astype(f32) + other_refs[number][s, 0].astype(f32)
                row = (2 * s + step) * count
                out_refs[number][pl.ds(pl.multiple_of(row, 16), count), :] = value.astype(bf16)
            else:
                out_refs[number][s, 0] = value

    if adds:
        for number in range(n_places):
            out_refs[number][2 * n_z * count :, :] = small_ref[...]


def attention_grads(n_places, info, grads, mixed, tokens, grad_attended, other=None, small=None):
    rows, width = grad_attended.shape
    n_z, buckets = mixed.shape[:2]
    mine = width // n_z
    count = mine // n_places
    by_step = pl.BlockSpec((n_z, 1, count, width), lambda i, info: (0, i, 0, 0))
    in_specs = [
        pl.BlockSpec(
            (1, buckets, width, BUCKET), lambda i, info: (jnp.minimum(info[i], 2), 0, 0, 0)
        ),
        fixed((n_z, buckets, mine, BUCKET)),
        pl.BlockSpec((rows, width), lambda i, info: (info[2], 0)),
        fixed((rows, width)),
    ]
    args = [grads, mixed, tokens, grad_attended]
    if other is None:
        shapes = [((n_z, 2, count, width), by_step)] * n_places
    else:
        in_specs += [by_step] * n_places + [fixed(small.shape)]
        args += list(other) + [small]
        flat = (2 * n_z * count + small.shape[0], width)
        shapes = [(flat, fixed(flat))] * n_places
    return pl.pallas_call(
        functools.partial(attention_grads_kernel, n_places, other is not None),
        grid_spec=pltpu.PrefetchScalarGridSpec(
            num_scalar_prefetch=1,
            grid=(2,),
            in_specs=in_specs,
            out_specs=[spec for _, spec in shapes],
            scratch_shapes=[pltpu.VMEM((width, width), bf16)],
        ),
        out_shape=[jax.ShapeDtypeStruct(shape, bf16) for shape, _ in shapes],
        compiler_params=params(1),
        name="attention_grads",
        cost_estimate=cost(0.5),
    )(info, *args)


def together(*values):
    return lax.optimization_barrier(values)


def add(first, *others):
    total = first.astype(f32)
    for other in others:
        total = total + other.astype(f32)
    return total.astype(bf16)


class Plane:
    def __init__(self, n_dp, n_z):
        self.n_dp, self.n_z = n_dp, n_z
        self.n_group = min(n_dp, 8)
        self.n_places = self.n_group // 2
        self.dp = lax.axis_index("dp")
        self.z = lax.axis_index("tensor")
        self.index = lax.rem(self.dp, self.n_group)
        self.core = self.index & 1
        self.place = self.index >> 1

    def swap(self, array, bits):
        return lax.ppermute(array, "dp", [(i, i ^ bits) for i in range(self.n_dp)])

    def shift(self, array, by):
        n = self.n_z
        return lax.ppermute(array, "tensor", [(i, (i + by) % n) for i in range(n)])

    def gather(self, piece):
        if self.n_dp == self.n_group:
            whole = lax.all_gather(piece, ("tensor", "dp"))
            return whole.reshape((self.n_z, self.n_group) + piece.shape)
        groups = [
            list(range(i, i + self.n_group)) for i in range(0, self.n_dp, self.n_group)
        ]
        line = lax.all_gather(piece, "tensor")
        return lax.all_gather(line, "dp", axis=1, axis_index_groups=groups)

    def turned(self, array):
        bit = 1
        while bit < self.n_group:
            lead = array.reshape((-1, 2, bit) + array.shape[1:])
            array = jnp.where((self.index & bit) != 0, lead[:, ::-1], lead).reshape(array.shape)
            bit *= 2
        return array

    def to_places(self, parts):
        return [self.swap(parts[number], 2 * number) for number in range(1, self.n_places)]

    def from_places(self, own, arrived):
        found = jnp.stack([own] + arrived)
        bit = 1
        while bit < self.n_places:
            lead = found.reshape((-1, 2, bit) + own.shape)
            flipped = lead[:, ::-1]
            found = jnp.where((self.place & bit) != 0, flipped, lead).reshape(found.shape)
            bit *= 2
        return found

    def by_core(self, own, other):
        return jnp.where(
            self.core == 1, jnp.stack([other, own]), jnp.stack([own, other])
        )

    def over_groups(self, array):
        bit = self.n_group
        while bit < self.n_dp:
            array = add(array, self.swap(array, bit))
            bit *= 2
        return array


def on_device(
    n_dp,
    n_z,
    tokens,
    lengths,
    key_mask,
    query_weight,
    query_bias,
    key_weight,
    value_weight,
    value_bias,
    output_weight,
    output_bias,
    first_gain,
    first_shift,
    inner_weight,
    inner_bias,
    outer_weight,
    outer_bias,
    second_gain,
    second_shift,
    cotangent,
):
    width = tokens.shape[1]
    mine = query_weight.shape[1]
    units = inner_weight.shape[1]
    all_rows = tokens.shape[0]
    all_blocks = all_rows // BUCKET
    rows = all_rows // n_z
    plane = Plane(n_dp, n_z)
    z, core, place, index = plane.z, plane.core, plane.place, plane.index
    n_places = plane.n_places
    others = range(1, n_z)

    feed_rows = units // plane.n_group
    head_rows = mine // plane.n_group
    mixer_count = width // plane.n_group
    piece = jnp.concatenate(
        [
            lax.dynamic_slice_in_dim(inner_weight, index * feed_rows, feed_rows, 1).T,
            lax.dynamic_slice_in_dim(outer_weight, index * feed_rows, feed_rows, 0),
        ],
        axis=1,
    )
    line = [plane.shift(piece, s) for s in others]

    mixer = plane.gather(
        lax.dynamic_slice_in_dim(output_weight, index * head_rows, head_rows, 0)
    ).reshape(width, width)
    query_t, key_t, value_t = query_weight.T, key_weight.T, value_weight.T

    key_mask_rows = key_mask.reshape(all_blocks, 1, BUCKET)
    bias_row = jnp.concatenate([query_bias, value_bias, inner_bias])
    bias_rows = jnp.pad(bias_row, (0, 16 * BUCKET - bias_row.shape[0])).reshape(16, BUCKET)
    place_z = z.reshape(1)
    mixed = attend_forward(
        n_z, lengths, tokens, query_t, key_t, value_t, bias_rows, key_mask_rows
    )
    mixed, line = together(mixed, line)

    near = jnp.stack(line)
    by_x, by_y = plane.swap(near, 2), plane.swap(near, 4)
    mixed, near = together(mixed, near)
    mixed = lax.all_to_all(mixed, "tensor", 0, 0)
    own_units = jnp.concatenate([inner_weight.T, outer_weight], axis=1)

    attention_own = jnp.concatenate([query_t, key_t, value_t], axis=1)
    attention_piece = lax.dynamic_slice_in_dim(attention_own, index * head_rows, head_rows, 0)
    attention_line = [plane.shift(attention_piece, s) for s in others]
    biases = mixed[:, 0, mine:].reshape(n_z, -1)[:, : bias_row.shape[0]].astype(f32)
    head_biases = jnp.pad(
        jnp.stack([biases[:, :mine], biases[:, mine : 2 * mine]], axis=1), ((0, 0), (0, 6), (0, 0))
    )
    inner_biases = biases[:, 2 * mine :]
    inner_biases = jnp.concatenate(
        [
            lax.dynamic_slice_in_dim(inner_biases, lax.rem(z + n_z - s, n_z), 1, 0)
            for s in range(n_z)
        ],
        axis=0,
    )
    inner_biases = inner_biases.reshape(n_z, plane.n_group, feed_rows).transpose(1, 0, 2)
    inner_biases = plane.turned(inner_biases).reshape(n_places, 2, 1, n_z * feed_rows)
    inner_biases = inner_biases.transpose(1, 0, 2, 3).reshape(plane.n_group, 1, -1)
    vectors = jnp.stack(
        [output_bias, first_gain, first_shift, outer_bias, second_gain, second_shift]
        + [jnp.zeros_like(output_bias)] * 2
    ).astype(f32)

    info = jnp.stack([z, place, core])
    shared_args = (info, vectors, inner_biases, own_units)
    cut = feed_rows // 2
    far = [plane.swap(by_x[:, :cut], 4), plane.swap(by_y[:, cut:], 2)]
    near_there, x_there, y_there, mixer, attention_line = together(
        near, by_x, by_y, mixer, attention_line
    )
    send = [plane.swap(units_of, 1) for units_of in (near_there, x_there, y_there)]
    attention_line = jnp.stack(attention_line)
    attention_swaps = plane.to_places([attention_line] * n_places)
    hidden, slope, normed_low, first_normed, first_scale, second_sum = feed_forward(
        ((0, 0), (0, 1), (0, 2), (1, 0), (1, 1), (1, 2)),
        *shared_args,
        [near, by_x, by_y] + send,
        first=(tokens, mixed, mixer),
    )
    second_sum, far, attention_swaps = together(second_sum, far, attention_swaps)
    attention_half = plane.from_places(attention_line, attention_swaps)
    attention_other = plane.swap(attention_half, 1)
    far_send = [plane.swap(half, 1) for half in far]
    keep = [near, by_x, by_y] + far
    send = send + far_send
    hidden, slope, my_output, grad_second, grad_outer, second_sums = feed_forward(
        ((0, 3), (1, 3)), *shared_args, far + far_send,
        going=(normed_low, second_sum, hidden, slope), last=(lengths, cotangent),
    )
    output = lax.all_gather(my_output, "tensor", axis=0, tiled=True)

    grad_outer, attention_other = together(grad_outer, attention_other)

    shared_args = (info, grad_outer, normed_low, hidden, slope, own_units)
    sent_early, sent_late, bias_sent, grad_normed = feed_back(*shared_args, grad_second, send)
    other = [plane.swap(sent_early, 1), plane.swap(sent_late, 1)]
    attention_remote = plane.by_core(attention_half, attention_other)
    attention_remote = attention_remote.transpose(2, 1, 0, 3, 4).reshape(n_z - 1, mine, 3 * width)
    projected = project(
        place_z, tokens, attention_own, attention_remote, head_biases, rows // BUCKET
    )
    projected, other = together(projected, other)
    (
        inner_stay, outer_stay, inner_go, outer_go, bias_kept, grad_first, grad_attended, first_sums
    ) = feed_back(
        *shared_args, grad_normed, keep, other,
        (first_normed, first_scale, vectors),
    )
    inner_came, outer_came = plane.swap(inner_go, 4), plane.swap(outer_go, 2)
    bias_grads = jnp.stack(
        [bias_kept[:, 0], bias_sent[:, 0]], axis=1
    )
    inner_bias_grad = plane.turned(bias_grads.reshape(plane.n_group, n_z, feed_rows))
    inner_bias_grad = inner_bias_grad.transpose(1, 0, 2)
    inner_bias_grad = jnp.concatenate(
        [
            sum(
                jnp.where(lax.rem(z - t + n_z, n_z) == s, inner_bias_grad[s : s + 1], 0.0)
                for s in range(n_z)
            )
            for t in range(n_z)
        ],
        axis=0,
    ).reshape(n_z, units)

    grads, my_tokens_grad, back_sums = attend_back(
        place_z, lengths, grad_attended, grad_first, attention_own, attention_remote, mixer,
        *projected, key_mask_rows,
    )
    grads, inner_came, outer_came, output = together(grads, inner_came, outer_came, output)
    inner_on, outer_on = (
        plane.swap(add(inner_stay[1], inner_came[1]), 2),
        plane.swap(add(outer_stay[1], outer_came[1]), 4),
    )
    tokens_grad = lax.all_gather(my_tokens_grad, "tensor", axis=0, tiled=True)

    def weight_grads(side, other=None, small=None):
        info = jnp.stack([2 * side, 2 * side + 1, z, place])
        return attention_grads(
            n_places, info, grads, mixed, tokens, grad_attended, other, small
        )

    sent = weight_grads(1 - core)
    sent, inner_on, outer_on, back_sums, first_sums, second_sums, inner_bias_grad = together(
        sent, inner_on, outer_on, back_sums, first_sums, second_sums, inner_bias_grad
    )
    other = [plane.swap(part, 1) for part in sent]

    small = jnp.concatenate(
        [first_sums[:3], second_sums[:3], inner_bias_grad, jnp.sum(back_sums, axis=0)[:2]], axis=0
    )
    small = jnp.pad(small, ((0, -small.shape[0] % 16), (0, 0))).astype(bf16)
    small_rows = small.shape[0]

    small = add(small, plane.swap(small, 1))
    kept = list(weight_grads(core, other, small))
    arrived = plane.to_places(kept)
    feed_parts = [
        jnp.concatenate(
            [
                add(inner_stay[0, s], inner_came[0, s], inner_on[s]),
                add(outer_stay[0, s], outer_came[0, s], outer_on[s]),
            ],
            axis=1,
        )
        for s in range(n_z)
    ]
    feed_line = [plane.shift(feed_parts[s], -s) for s in others]
    output = copied(output)
    arrived, output = together(arrived, output)
    small = add(small, *[a[-small_rows:] for a in arrived])
    count = 2 * mine // n_places
    attention_parts = [
        add(*[a[s * count : (s + 1) * count] for a in [kept[0]] + arrived]) for s in range(n_z)
    ]
    attention_line = [
        plane.shift(jnp.concatenate([attention_parts[s], small], axis=0), s) for s in others
    ]
    feed_total = plane.over_groups(add(feed_parts[0], *feed_line))
    feed_arrived = plane.to_places([feed_total] * n_places)
    tokens_grad = copied(tokens_grad)
    attention_line, feed_arrived, tokens_grad = together(
        attention_line, feed_arrived, tokens_grad
    )
    attention_total = plane.over_groups(
        add(attention_parts[0], *[a[:count] for a in attention_line])
    )
    small = plane.over_groups(add(small, *[a[count:] for a in attention_line])).astype(f32)
    arrived = plane.to_places([attention_total] * n_places)
    feed_half = plane.from_places(feed_total, feed_arrived)
    feed_other = plane.swap(feed_half, 1)
    inner_grad, outer_grad = finish_feed(core.reshape(1), feed_half, feed_other)
    inner_bias_sum = lax.dynamic_slice_in_dim(small, 6 + z, 1, 0)[0]
    head_sums = lax.dynamic_slice_in_dim(small[6 + n_z : 8 + n_z], z * mine, mine, 1)
    arrived, inner_grad, outer_grad, small, inner_bias_sum, head_sums = together(
        arrived, inner_grad, outer_grad, small, inner_bias_sum, head_sums
    )
    attention_half = plane.from_places(attention_total, arrived)
    attention_other = plane.swap(attention_half, 1)
    grad_list = plane.by_core(attention_half, attention_other)
    grad_list = grad_list.reshape(2, n_places, 2, mine // n_places, width)
    grad_list = grad_list.transpose(0, 2, 1, 3, 4).reshape(4, mine, width)

    shared = small[:6]

    return (
        output,
        tokens_grad,
        grad_list[0].T.astype(f32),
        head_sums[0],
        grad_list[1].T.astype(f32),
        grad_list[2].T.astype(f32),
        head_sums[1],
        grad_list[3].astype(f32),
        shared[0],
        shared[1],
        shared[2],
        inner_grad,
        inner_bias_sum,
        outer_grad,
        shared[3],
        shared[4],
        shared[5],
    )


def solution(mesh):
    n_dp, n_z = mesh.shape["dp"], mesh.shape["tensor"]
    in_specs = (
        P("dp", None),
        P("dp", None),
        P("dp"),
        P(None, "tensor"),
        P("tensor"),
        P(None, "tensor"),
        P(None, "tensor"),
        P("tensor"),
        P("tensor", None),
        P(),
        P(),
        P(),
        P(None, "tensor"),
        P("tensor"),
        P("tensor", None),
        P(),
        P(),
        P(),
        P("dp", None),
    )
    out_specs = (
        P("dp", None),
        P("dp", None),
        P(None, "tensor"),
        P("tensor"),
        P(None, "tensor"),
        P(None, "tensor"),
        P("tensor"),
        P("tensor", None),
        P(),
        P(),
        P(),
        P(None, "tensor"),
        P("tensor"),
        P("tensor", None),
        P(),
        P(),
        P(),
    )

    def program(*args):
        return on_device(n_dp, n_z, *args)

    return jax.shard_map(
        program, mesh=mesh, in_specs=in_specs, out_specs=out_specs, check_vma=False
    )
```

```python
import functools

import jax
import jax.numpy as jnp
from jax import lax
from jax.experimental import pallas as pl
from jax.experimental.pallas import tpu as pltpu
from jax.sharding import PartitionSpec as P

HEAD = 64
BUCKET = 512
ITEMS = 8


negative_fill = -1e30
epsilon = 1e-06
f32 = jnp.float32
bf16 = jnp.bfloat16
VMEM_BYTES = 56 * 1024 * 1024


def dot(left, right):
    return jnp.dot(left, right, preferred_element_type=f32)


def contract_rows(left, right):
    return lax.dot_general(left, right, (((0,), (0,)), ((), ())), preferred_element_type=f32)


def contract_cols(left, right):
    return lax.dot_general(left, right, (((1,), (1,)), ((), ())), preferred_element_type=f32)


def norm_rows(values):
    centred = values - jnp.mean(values, axis=1, keepdims=True)
    inv_scale = lax.rsqrt(jnp.mean(centred * centred, axis=1, keepdims=True) + epsilon)
    return centred * inv_scale, inv_scale


def norm_back(grad_rows, norm_gain, normed, inv_scale):
    scaled = grad_rows * norm_gain
    return inv_scale * (
        scaled
        - jnp.mean(scaled, axis=1, keepdims=True)
        - normed * jnp.mean(scaled * normed, axis=1, keepdims=True)
    )


def column_sum(matrix):
    return jnp.sum(matrix.astype(f32), axis=0, keepdims=True)


def fixed(shape):
    return pl.BlockSpec(shape, lambda *_: (0,) * len(shape))


def cost(microseconds):
    return pl.CostEstimate(
        flops=int(microseconds * 2.5e8),
        bytes_accessed=int(microseconds * 2.5e5),
        transcendentals=0,
    )


def params(axes):
    return pltpu.CompilerParams(
        dimension_semantics=("arbitrary",) * axes, vmem_limit_bytes=VMEM_BYTES
    )


def item_places(lengths_ref, row, shape, axis):
    places = lax.broadcasted_iota(jnp.int32, shape, axis)
    end = jnp.int32(0)
    items = jnp.zeros(shape, jnp.int32)
    for slot in range(ITEMS):
        end = end + lengths_ref[row, slot]
        items = items + (places >= end).astype(jnp.int32)
    return items


def as_column(row):
    return jnp.broadcast_to(row.astype(f32), (8, row.shape[1])).T[:, :1]


def mask_bias(lengths_ref, row, key_mask):
    shape = (BUCKET, BUCKET)
    diagonal = lax.broadcasted_iota(jnp.int32, shape, 0) == lax.broadcasted_iota(
        jnp.int32, shape, 1
    )
    item_row = item_places(lengths_ref, row, (1, BUCKET), 1)
    item_column = item_places(lengths_ref, row, (BUCKET, 1), 0)
    code_column = jnp.where(as_column(key_mask) == 1.0, item_column, -1)
    return jnp.where((code_column == item_row) | diagonal, 0.0, negative_fill).astype(f32)


def attend_forward_kernel(
    lengths_ref, tokens_ref, query_ref, key_ref, value_ref, biases_ref, key_mask_ref, mixed_ref,
):
    mine = query_ref.shape[0]
    rows = tokens_ref[...]
    queries = contract_cols(query_ref[...], rows) + as_column(biases_ref[0:1, :mine])
    queries = (queries.astype(bf16) * HEAD ** (-0.5)).astype(bf16)
    keys = contract_cols(rows, key_ref[...]).astype(bf16)
    values = contract_cols(value_ref[...], rows) + as_column(biases_ref[0:1, mine : 2 * mine])
    values = values.astype(bf16)
    bias = mask_bias(lengths_ref, pl.program_id(0), key_mask_ref[0])
    for head in range(mine // HEAD):
        at = slice(head * HEAD, (head + 1) * HEAD)
        scores = dot(keys[:, at], queries[at]) + bias
        exponent = jnp.exp(scores - jnp.max(scores, axis=0, keepdims=True))
        total = jnp.sum(exponent, axis=0, keepdims=True)
        mixed_ref[0, 0, at] = (dot(values[at], exponent.astype(bf16)) / total).astype(bf16)
    mixed_ref[0, 0, mine:] = biases_ref[...]


def attend_forward(n_z, lengths, tokens, query, key, value, biases, key_mask):
    blocks = lengths.shape[0]
    own = blocks // n_z
    mine, width = key.shape
    whole = (n_z, own, mine + biases.shape[0], BUCKET)
    return pl.pallas_call(
        attend_forward_kernel,
        grid=(blocks,),
        in_specs=[
            pl.BlockSpec(memory_space=pltpu.SMEM),
            pl.BlockSpec((BUCKET, width), lambda b: (b, 0)),
            fixed((mine, width)),
            fixed((mine, width)),
            fixed((mine, width)),
            fixed(biases.shape),
            pl.BlockSpec((1, 1, BUCKET), lambda b: (b, 0, 0)),
        ],
        out_specs=pl.BlockSpec((1, 1) + whole[2:], lambda b: (b // own, b % own, 0, 0)),
        out_shape=jax.ShapeDtypeStruct(whole, bf16),
        compiler_params=params(1),
        name="attend_forward",
        cost_estimate=cost(12),
    )(lengths, tokens, query, key, value, biases, key_mask)


def fetch_units(step, picks, own_ref, halves, units, sems):
    feed_rows = units.shape[2]
    cut = feed_rows // 2

    def copies(number):
        slot = number % 2
        row = pl.multiple_of(picks[number] * feed_rows, 16)
        ends = [
            (own_ref.at[pl.ds(row, feed_rows)], units.at[slot, 0]),
            (halves[number][0], units.at[slot, 1:, :cut]),
            (halves[number][1], units.at[slot, 1:, cut:]),
        ]
        return [
            pltpu.make_async_copy(source, target, sems.at[slot, i])
            for i, (source, target) in enumerate(ends)
        ]

    for number in range(len(halves)):

        @pl.when(step == number)
        def _(number=number):
            if number == 0:
                for copy in copies(0):
                    copy.start()
            if number + 1 < len(halves):
                for copy in copies(number + 1):
                    copy.start()
            for copy in copies(number):
                copy.wait()

    return units.at[lax.rem(step, 2)]


def take_halves(numbers, refs):
    halves, refs = [], list(refs)
    for number in numbers:
        if number == 3:
            halves.append((refs.pop(0), refs.pop(0)))
        else:
            ref = refs.pop(0)
            cut = ref.shape[1] // 2
            halves.append((ref.at[:, :cut], ref.at[:, cut:]))
    return halves, refs


def split_units(units):
    width = units.shape[2] // 2
    return units[:, :, :width].reshape(-1, width), units[:, :, width:].reshape(-1, width)


ANYWHERE = pl.BlockSpec(memory_space=pl.ANY)


def feed_forward_kernel(chunks, first, last, info_ref, *rest):
    def take(count):
        nonlocal rest
        taken, rest = rest[:count], rest[count:]
        return taken

    vectors_ref, bias_ref, own_ref = take(3)
    halves, rest = take_halves([number for _, number in chunks], rest)
    if first:
        tokens_ref, mixed_ref, mixer_ref = take(3)
    else:
        normed_low_ref, start_ref, _, _ = take(4)
    if last:
        lengths_ref, cotangent_ref = take(2)
    hidden_ref, slope_ref = take(2)
    if first:
        normed_low_ref, first_normed_ref, first_scale_ref = take(3)
    if last:
        output_ref, grad_second_ref, grad_outer_ref, sums_ref = take(4)
    else:
        (second_sum,) = take(1)
    units, sems = take(2)
    if last:
        (second_sum,) = take(1)

    step = pl.program_id(0)
    picks = [(info_ref[1] ^ number) * 2 + (info_ref[2] ^ side) for side, number in chunks]
    weights = fetch_units(step, picks, own_ref, halves, units, sems)
    output_bias, first_gain, first_shift, outer_bias, second_gain, second_shift = (
        vectors_ref[i : i + 1, :] for i in range(6)
    )

    @pl.when(step == 0)
    def _():
        if first:
            n_z, own, mine, _ = mixed_ref.shape
            attended = output_bias + jnp.concatenate(
                [
                    sum(
                        contract_rows(mixed_ref[t, b], mixer_ref[t * mine : (t + 1) * mine, :])
                        for t in range(n_z)
                    )
                    for b in range(own)
                ],
                axis=0,
            )
            normed, inv_scale = norm_rows(tokens_ref[...].astype(f32) + attended)
            whole = normed * first_gain + first_shift
            first_normed_ref[...] = normed
            first_scale_ref[...] = inv_scale
            normed_low_ref[...] = whole.astype(bf16)
            second_sum[...] = whole + outer_bias
        else:
            second_sum[...] = start_ref[...]

    inner, outer = split_units(weights)
    inner_pre = contract_cols(normed_low_ref[...], inner) + bias_ref[0]
    normal_cdf = 0.5 + 0.5 * lax.erf(inner_pre * 0.7071067811865476)
    bell = jnp.exp(-0.5 * inner_pre * inner_pre)
    hidden = (inner_pre * normal_cdf).astype(bf16)
    hidden_ref[...] = hidden.T
    slope_ref[...] = (normal_cdf + inner_pre * bell * 0.3989422804014327).astype(bf16)
    second_sum[...] += dot(hidden, outer)

    if last:

        @pl.when(step == pl.num_programs(0) - 1)
        def _():
            normed, inv_scale = norm_rows(second_sum[...])
            blocks = normed.shape[0] // BUCKET
            live = jnp.concatenate(
                [
                    (item_places(lengths_ref, info_ref[0] * blocks + b, (BUCKET, 1), 0) < ITEMS)
                    for b in range(blocks)
                ],
                axis=0,
            ).astype(f32)
            output_ref[...] = ((normed * second_gain + second_shift) * live).astype(bf16)
            grad_final = cotangent_ref[...].astype(f32) * live
            grad_second = norm_back(grad_final, second_gain, normed, inv_scale)
            grad_outer = grad_second.astype(bf16)
            grad_second_ref[...] = grad_second
            grad_outer_ref[...] = grad_outer
            sums_ref[0:1, :] = column_sum(grad_outer)
            sums_ref[1:2, :] = column_sum(grad_final * normed)
            sums_ref[2:3, :] = column_sum(grad_final)


def feed_forward(chunks, info, vectors, biases, own, halves, first=None, going=None, last=None):
    width = vectors.shape[1]
    n_z = halves[0].shape[0] + 1
    feed_rows, twice = own.shape[0] // 8, 2 * width
    rows = first[1].shape[1] * BUCKET if first else going[0].shape[0]
    chunk = n_z * feed_rows
    whole = fixed((rows, width))
    my_rows = pl.BlockSpec((rows, width), lambda j, info: (info[0], 0))
    at = lambda j, info: info[3 + j]
    hidden_spec = pl.BlockSpec((chunk, rows), lambda j, info: (at(j, info), 0))
    slope_spec = pl.BlockSpec((rows, chunk), lambda j, info: (0, at(j, info)))
    in_specs = [
        fixed((8, width)),
        pl.BlockSpec((1, 1, chunk), lambda j, info: (at(j, info), 0, 0)),
        ANYWHERE,
    ] + [ANYWHERE] * len(halves)
    args = [vectors, biases, own] + halves
    shapes = [
        ((8 * chunk, rows), bf16, hidden_spec),
        ((rows, 8 * chunk), bf16, slope_spec),
    ]
    scratch = [
        pltpu.VMEM((2, n_z, feed_rows, twice), bf16),
        pltpu.SemaphoreType.DMA((2, 3)),
    ]
    aliases = {}
    if first:
        tokens, mixed, mixer = first
        mine = width // n_z
        in_specs += [my_rows, fixed((n_z, mixed.shape[1], mine, BUCKET)), fixed(mixer.shape)]
        args += [tokens, mixed, mixer]
        shapes += [
            ((rows, width), bf16, whole),
            ((rows, width), f32, whole),
            ((rows, 1), f32, fixed((rows, 1))),
        ]
    else:
        aliases = {1 + len(args) + 2: 0, 1 + len(args) + 3: 1}
        in_specs += [whole, whole, ANYWHERE, ANYWHERE]
        args += list(going)
    if last:
        in_specs += [pl.BlockSpec(memory_space=pltpu.SMEM), my_rows]
        args += list(last)
        shapes += [
            ((rows, width), bf16, whole),
            ((rows, width), f32, whole),
            ((rows, width), bf16, whole),
            ((8, width), f32, fixed((8, width))),
        ]
        scratch.append(pltpu.VMEM((rows, width), f32))
    else:
        shapes.append(((rows, width), f32, whole))
    info = jnp.concatenate(
        [info, jnp.array([4 * side + number for side, number in chunks], jnp.int32)]
    )
    return pl.pallas_call(
        functools.partial(feed_forward_kernel, chunks, first is not None, last is not None),
        grid_spec=pltpu.PrefetchScalarGridSpec(
            num_scalar_prefetch=1,
            grid=(len(chunks),),
            in_specs=in_specs,
            out_specs=[spec for _, _, spec in shapes],
            scratch_shapes=scratch,
        ),
        out_shape=[jax.ShapeDtypeStruct(shape, kind) for shape, kind, _ in shapes],
        input_output_aliases=aliases,
        compiler_params=params(1),
        name="feed_forward",
        cost_estimate=cost(3 * len(chunks)),
    )(info, *args)


STAY = ((0, 1), (0, 2))
GO = ((2, 3), (1, 3))


def feed_back_kernel(
    keeps, info_ref, grad_outer_ref, normed_low_ref, hidden_ref, slope_ref,
    own_ref, start_ref, *rest,
):
    halves, rest = take_halves(range(4), rest)
    if keeps:
        other_refs, norm_refs, rest = rest[:2], rest[2:5], rest[5:]
        stay_refs, go_refs, rest = rest[0:2], rest[2:4], rest[4:]
        bias_grad_ref, grad_first_ref, grad_attended_ref, sums_ref, units, sems = rest[:6]
        grad_normed_ref = rest[6]
    else:
        *grad_refs, bias_grad_ref, grad_normed_ref, units, sems = rest
    step = pl.program_id(0)
    side = info_ref[2] if keeps else 1 - info_ref[2]
    picks = [(info_ref[1] ^ number) * 2 + side for number in range(4)]
    weights = fetch_units(step, picks, own_ref, halves, units, sems)

    @pl.when(step == 0)
    def _():
        grad_normed_ref[...] = start_ref[...]

    n_z, feed_rows, twice = weights.shape
    width = twice // 2
    inner, outer = split_units(weights)
    grad_outer = grad_outer_ref[...]
    grad_hidden = contract_cols(grad_outer, outer)
    grad_inner = (grad_hidden * slope_ref[...].astype(f32)).astype(bf16)
    outer_grad = dot(hidden_ref[...], grad_outer).reshape(n_z, feed_rows, width)
    inner_grad = contract_rows(grad_inner, normed_low_ref[...]).reshape(n_z, feed_rows, width)
    bias_grad_ref[0] = column_sum(grad_inner)
    grad_normed_ref[...] += dot(grad_inner, inner)

    for number in range(4):

        @pl.when(step == number)
        def _(number=number):
            for track, value in enumerate((inner_grad, outer_grad)):
                at = slice(track * width, (track + 1) * width)
                if keeps:
                    found = value + other_refs[number // 2][0, :, :, at].astype(f32)
                    ref = stay_refs[track] if number in STAY[track] else go_refs[track]
                    ref[0] = found.astype(bf16)
                else:
                    grad_refs[number // 2][0, :, :, at] = value.astype(bf16)

    if keeps:

        @pl.when(step == pl.num_programs(0) - 1)
        def _():
            first_normed_ref, first_scale_ref, vectors_ref = norm_refs
            grad_rows, normed = grad_normed_ref[...], first_normed_ref[...]
            grad_first = norm_back(grad_rows, vectors_ref[1:2, :], normed, first_scale_ref[...])
            grad_attended = grad_first.astype(bf16)
            grad_first_ref[...] = grad_first
            grad_attended_ref[...] = grad_attended
            sums_ref[0:1, :] = column_sum(grad_attended)
            sums_ref[1:2, :] = column_sum(grad_rows * normed)
            sums_ref[2:3, :] = column_sum(grad_rows)


def feed_back(
    info, grad_outer, normed_low, hidden, slope, own, start, units, others=None, norm=None
):
    rows, width = grad_outer.shape
    keeps = others is not None
    count = 4
    feed_rows, twice = own.shape[0] // 8, 2 * width
    n_z = units[0].shape[0] + 1
    chunk = n_z * feed_rows
    flip = 0 if keeps else 1
    columns = pl.BlockSpec((rows, chunk), lambda i, info: (0, 4 * flip + i))
    whole = fixed((rows, width))
    part = (n_z, feed_rows, twice)
    track = (2, n_z, feed_rows, width)
    unit_rows = pl.BlockSpec((chunk, rows), lambda i, info: (4 * flip + i, 0))
    in_specs = [whole, whole, unit_rows, columns, ANYWHERE, whole] + [ANYWHERE] * len(units)
    args = [grad_outer, normed_low, hidden, slope, own, start] + units
    bias_shape = (
        (count, 1, chunk),
        f32,
        pl.BlockSpec((1, 1, chunk), lambda i, info: (i, 0, 0)),
    )
    scratch = [pltpu.VMEM((2,) + part, bf16), pltpu.SemaphoreType.DMA((2, 3))]

    def one(shape, at):
        return pl.BlockSpec((1,) + shape[1:], lambda i, info: (at(i), 0, 0, 0))

    early, late = (lambda i: jnp.minimum(i, 1)), (lambda i: jnp.maximum(i - 2, 0))
    pair = (2,) + part
    if keeps:
        in_specs += [one(pair, early), one(pair, late)]
        in_specs += [whole, fixed((rows, 1)), fixed((8, width))]
        args += list(others) + list(norm)
        slow, slower = (lambda i: i // 2), (lambda i: jnp.maximum(i - 1, 0) // 2)
        shapes = [(track, bf16, one(track, at)) for at in (early, slow, late, slower)] + [
            bias_shape,
            ((rows, width), f32, whole),
            ((rows, width), bf16, whole),
            ((8, width), f32, fixed((8, width))),
        ]
        scratch.append(pltpu.VMEM((rows, width), f32))
    else:
        shapes = [
            (pair, bf16, one(pair, early)),
            (pair, bf16, one(pair, late)),
            bias_shape,
            ((rows, width), f32, whole),
        ]
    return pl.pallas_call(
        functools.partial(feed_back_kernel, keeps),
        grid_spec=pltpu.PrefetchScalarGridSpec(
            num_scalar_prefetch=1,
            grid=(count,),
            in_specs=in_specs,
            out_specs=[spec for _, _, spec in shapes],
            scratch_shapes=scratch,
        ),
        out_shape=[jax.ShapeDtypeStruct(shape, kind) for shape, kind, _ in shapes],
        compiler_params=params(1),
        name="feed_back_own" if keeps else "feed_back",
        cost_estimate=cost(3 * count),
    )(info, *args)


def finish_feed_kernel(core_ref, own_ref, other_ref, inner_ref, outer_ref, inner_rows):
    places, count, twice = own_ref.shape
    width = twice // 2
    for source, side in ((own_ref, core_ref[0]), (other_ref, 1 - core_ref[0])):
        for place in range(places):
            row = pl.multiple_of((2 * place + side) * count, 16)
            inner_rows[pl.ds(row, count), :] = source[place, :, :width].astype(f32)
            outer_ref[pl.ds(row, count), :] = source[place, :, width:].astype(f32)
    inner_ref[...] = inner_rows[...].T


def finish_feed(core, own, other):
    places, count, twice = own.shape
    shape = (2 * places * count, twice // 2)
    inner_shape = (shape[1], shape[0])
    return pl.pallas_call(
        finish_feed_kernel,
        grid_spec=pltpu.PrefetchScalarGridSpec(
            num_scalar_prefetch=1,
            grid=(1,),
            in_specs=[fixed(own.shape), fixed(other.shape)],
            out_specs=[fixed(inner_shape), fixed(shape)],
            scratch_shapes=[pltpu.VMEM(shape, f32)],
        ),
        out_shape=[
            jax.ShapeDtypeStruct(inner_shape, f32),
            jax.ShapeDtypeStruct(shape, f32),
        ],
        compiler_params=params(1),
        name="finish_feed",
        cost_estimate=cost(5),
    )(core, own, other)


def copy_kernel(from_ref, to_ref):
    to_ref[...] = from_ref[...]


def copied(array):
    block = pl.BlockSpec((BUCKET, array.shape[1]), lambda i: (i, 0))
    return pl.pallas_call(
        copy_kernel,
        grid=(array.shape[0] // BUCKET,),
        in_specs=[block],
        out_specs=block,
        out_shape=jax.ShapeDtypeStruct(array.shape, array.dtype),
        compiler_params=params(1),
        name="copied",
        cost_estimate=cost(0.5),
    )(array)


def project_kernel(
    place_ref, tokens_ref, own_ref, remote_ref, biases_ref, query_ref, key_ref, value_ref
):
    rows = tokens_ref[...]
    width = rows.shape[1]
    weights = jnp.where(pl.program_id(1) == 0, own_ref[...], remote_ref[0])
    queries = contract_cols(weights[:, :width], rows) + as_column(biases_ref[0, 0:1, :])
    query_ref[...] = (queries.astype(bf16) * HEAD ** (-0.5)).astype(bf16)
    key_ref[...] = contract_cols(weights[:, width : 2 * width], rows).astype(bf16)
    values = contract_cols(weights[:, 2 * width :], rows) + as_column(biases_ref[0, 1:2, :])
    value_ref[...] = values.astype(bf16)


def project(place, tokens, own, remote, biases, buckets):
    width = tokens.shape[1]
    mine = own.shape[0]
    n_z = width // mine
    there = lambda s, place: lax.rem(place[0] + n_z - s, n_z)
    out = pl.BlockSpec((None, mine, BUCKET), lambda b, s, place: (b, there(s, place), 0))
    return pl.pallas_call(
        project_kernel,
        grid_spec=pltpu.PrefetchScalarGridSpec(
            num_scalar_prefetch=1,
            grid=(buckets, n_z),
            in_specs=[
                pl.BlockSpec((BUCKET, width), lambda b, s, place: (place[0] * buckets + b, 0)),
                fixed(own.shape),
                pl.BlockSpec(
                    (1, mine, 3 * width), lambda b, s, place: (jnp.maximum(s - 1, 0), 0, 0)
                ),
                pl.BlockSpec((1, 8, mine), lambda b, s, place: (there(s, place), 0, 0)),
            ],
            out_specs=[out] * 3,
        ),
        out_shape=[jax.ShapeDtypeStruct((buckets, width, BUCKET), bf16)] * 3,
        compiler_params=params(2),
        name="project",
        cost_estimate=cost(5),
    )(place, tokens, own, remote, biases)


def attend_back_kernel(
    place_ref, lengths_ref, grad_attended_ref, grad_first_ref, own_ref, remote_ref, mixer_ref,
    query_ref, key_ref, value_ref, key_mask_ref,
    grads_ref, tokens_grad_ref, sums_ref,
    bias, grad_mixed_t, whole, weights, mixer, sems,
):
    pair = pl.program_id(1)
    pairs, width = whole.shape[1], weights.shape[0]
    mine = own_ref.shape[0]
    n_z = width // mine

    def fetches():
        ends = [(mixer_ref, mixer)]
        for s in range(n_z):
            row = pl.multiple_of(lax.rem(place_ref[0] + n_z - s, n_z) * mine, 16)
            source = own_ref if s == 0 else remote_ref.at[s - 1]
            ends.append((source, weights.at[pl.ds(row, mine)]))
        return [
            pltpu.make_async_copy(source, target, sems.at[i])
            for i, (source, target) in enumerate(ends)
        ]

    @pl.when(pair == 0)
    def _():
        for fetch in fetches():
            fetch.start()
        row = place_ref[0] * pl.num_programs(0) + pl.program_id(0)
        bias[...] = mask_bias(lengths_ref, row, key_mask_ref[0])
        for fetch in fetches():
            fetch.wait()
        grad_mixed_t[...] = contract_cols(mixer[...], grad_attended_ref[...]).astype(bf16)

    queries, keys_t = query_ref[...], key_ref[...]
    keys, values = keys_t.T, value_ref[...].T
    start = pl.multiple_of(pair * keys.shape[1], 128)
    grad_mixed = grad_mixed_t[pl.ds(start, keys.shape[1]), :]
    grad_queries, grad_keys, grad_values = [], [], []
    for head in range(keys.shape[1] // HEAD):
        at = slice(head * HEAD, (head + 1) * HEAD)
        scores = dot(keys[:, at], queries[at]) + bias[...]
        exponent = jnp.exp(scores - jnp.max(scores, axis=0, keepdims=True))
        probs = exponent * (1.0 / jnp.sum(exponent, axis=0, keepdims=True))
        grad_probs = dot(values[:, at], grad_mixed[at])
        shift = jnp.sum(probs * grad_probs, axis=0, keepdims=True)
        grad_scores = (probs * (grad_probs - shift)).astype(bf16)
        grad_values.append(contract_cols(probs.astype(bf16), grad_mixed[at]))
        grad_keys.append(contract_cols(grad_scores, queries[at]))
        grad_queries.append(dot(keys_t[at], grad_scores) * HEAD ** (-0.5))
    query_t = jnp.concatenate(grad_queries, axis=0).astype(bf16)
    found = (
        query_t.T,
        jnp.concatenate(grad_keys, axis=1).astype(bf16),
        jnp.concatenate(grad_values, axis=1).astype(bf16),
    )
    for number, grad in enumerate(found):
        grads_ref[number, 0] = query_t if number == 0 else grad.T
        whole[number, pair] = grad
    sums_ref[0, 0:1, :] = column_sum(found[0])
    sums_ref[0, 1:2, :] = column_sum(found[2])

    @pl.when(pair == pl.num_programs(1) - 1)
    def _():
        total = grad_first_ref[...]
        for number in range(3):
            grad = jnp.concatenate([whole[number, i] for i in range(pairs)], axis=1)
            total += dot(grad, weights[:, number * width : (number + 1) * width])
        tokens_grad_ref[...] = total.astype(bf16)


def attend_back(
    place, lengths, grad_attended, grad_first, own, remote, mixer, queries, keys, values, key_mask
):
    rows, width = grad_attended.shape
    blocks = rows // BUCKET
    pair = 2 * HEAD
    by_bucket = pl.BlockSpec((BUCKET, width), lambda b, h, place: (b, 0))
    by_pair = pl.BlockSpec((None, pair, BUCKET), lambda b, h, place: (b, h, 0))
    return pl.pallas_call(
        attend_back_kernel,
        grid_spec=pltpu.PrefetchScalarGridSpec(
            num_scalar_prefetch=1,
            grid=(blocks, width // pair),
            in_specs=[
                pl.BlockSpec(memory_space=pltpu.SMEM),
                by_bucket,
                by_bucket,
                ANYWHERE,
                ANYWHERE,
                ANYWHERE,
                by_pair,
                by_pair,
                by_pair,
                pl.BlockSpec((1, 1, BUCKET), lambda b, h, place: (place[0] * blocks + b, 0, 0)),
            ],
            out_specs=[
                pl.BlockSpec((3, 1, pair, BUCKET), lambda b, h, place: (0, b, h, 0)),
                by_bucket,
                pl.BlockSpec((1, 8, pair), lambda b, h, place: (b, 0, h)),
            ],
            scratch_shapes=[
                pltpu.VMEM((BUCKET, BUCKET), f32),
                pltpu.VMEM((width, BUCKET), bf16),
                pltpu.VMEM((3, width // pair, BUCKET, pair), bf16),
                pltpu.VMEM((width, own.shape[1]), bf16),
                pltpu.VMEM(mixer.shape, bf16),
                pltpu.SemaphoreType.DMA((1 + width // own.shape[0],)),
            ],
        ),
        out_shape=[
            jax.ShapeDtypeStruct((3, blocks, width, BUCKET), bf16),
            jax.ShapeDtypeStruct((rows, width), bf16),
            jax.ShapeDtypeStruct((blocks, 8, width), f32),
        ],
        compiler_params=params(2),
        name="attend_back",
        cost_estimate=cost(20),
    )(
        place, lengths, grad_attended, grad_first, own, remote, mixer, queries, keys, values, key_mask
    )


def attention_grads_kernel(
    n_places, adds, info_ref, grads_ref, mixed_ref, tokens_ref, grad_attended_ref, *rest
):
    if adds:
        other_refs, small_ref, rest = rest[:n_places], rest[n_places], rest[n_places + 1 :]
    out_refs, whole = rest[:-1], rest[-1]
    step = pl.program_id(0)
    which = info_ref[step]
    n_z, buckets, mine, _ = mixed_ref.shape
    count = mine // n_places

    @pl.when(which < 3)
    def _():
        whole[...] = sum(
            dot(grads_ref[0, b], tokens_ref[b * BUCKET : (b + 1) * BUCKET, :])
            for b in range(buckets)
        ).astype(bf16)

    @pl.when(which == 3)
    def _():
        for t in range(n_z):
            whole[t * mine : (t + 1) * mine, :] = sum(
                dot(mixed_ref[t, b], grad_attended_ref[b * BUCKET : (b + 1) * BUCKET, :])
                for b in range(buckets)
            ).astype(bf16)

    for number in range(n_places):
        for s in range(n_z):
            start = lax.rem(info_ref[2] + s, n_z) * mine + (info_ref[3] ^ number) * count
            value = whole[pl.ds(pl.multiple_of(start, 16), count), :]
            if adds:
                value = value.astype(f32) + other_refs[number][s, 0].astype(f32)
                row = (2 * s + step) * count
                out_refs[number][pl.ds(pl.multiple_of(row, 16), count), :] = value.astype(bf16)
            else:
                out_refs[number][s, 0] = value

    if adds:
        for number in range(n_places):
            out_refs[number][2 * n_z * count :, :] = small_ref[...]


def attention_grads(n_places, info, grads, mixed, tokens, grad_attended, other=None, small=None):
    rows, width = grad_attended.shape
    n_z, buckets = mixed.shape[:2]
    mine = width // n_z
    count = mine // n_places
    by_step = pl.BlockSpec((n_z, 1, count, width), lambda i, info: (0, i, 0, 0))
    in_specs = [
        pl.BlockSpec(
            (1, buckets, width, BUCKET), lambda i, info: (jnp.minimum(info[i], 2), 0, 0, 0)
        ),
        fixed((n_z, buckets, mine, BUCKET)),
        pl.BlockSpec((rows, width), lambda i, info: (info[2], 0)),
        fixed((rows, width)),
    ]
    args = [grads, mixed, tokens, grad_attended]
    if other is None:
        shapes = [((n_z, 2, count, width), by_step)] * n_places
    else:
        in_specs += [by_step] * n_places + [fixed(small.shape)]
        args += list(other) + [small]
        flat = (2 * n_z * count + small.shape[0], width)
        shapes = [(flat, fixed(flat))] * n_places
    return pl.pallas_call(
        functools.partial(attention_grads_kernel, n_places, other is not None),
        grid_spec=pltpu.PrefetchScalarGridSpec(
            num_scalar_prefetch=1,
            grid=(2,),
            in_specs=in_specs,
            out_specs=[spec for _, spec in shapes],
            scratch_shapes=[pltpu.VMEM((width, width), bf16)],
        ),
        out_shape=[jax.ShapeDtypeStruct(shape, bf16) for shape, _ in shapes],
        compiler_params=params(1),
        name="attention_grads",
        cost_estimate=cost(0.5),
    )(info, *args)


def together(*values):
    return lax.optimization_barrier(values)


def add(first, *others):
    total = first.astype(f32)
    for other in others:
        total = total + other.astype(f32)
    return total.astype(bf16)


class Plane:
    def __init__(self, n_dp, n_z):
        self.n_dp, self.n_z = n_dp, n_z
        self.n_group = min(n_dp, 8)
        self.n_places = self.n_group // 2
        self.dp = lax.axis_index("dp")
        self.z = lax.axis_index("tensor")
        self.index = lax.rem(self.dp, self.n_group)
        self.core = self.index & 1
        self.place = self.index >> 1

    def swap(self, array, bits):
        return lax.ppermute(array, "dp", [(i, i ^ bits) for i in range(self.n_dp)])

    def shift(self, array, by):
        n = self.n_z
        return lax.ppermute(array, "tensor", [(i, (i + by) % n) for i in range(n)])

    def gather(self, piece):
        if self.n_dp == self.n_group:
            whole = lax.all_gather(piece, ("tensor", "dp"))
            return whole.reshape((self.n_z, self.n_group) + piece.shape)
        groups = [
            list(range(i, i + self.n_group)) for i in range(0, self.n_dp, self.n_group)
        ]
        line = lax.all_gather(piece, "tensor")
        return lax.all_gather(line, "dp", axis=1, axis_index_groups=groups)

    def turned(self, array):
        bit = 1
        while bit < self.n_group:
            lead = array.reshape((-1, 2, bit) + array.shape[1:])
            array = jnp.where((self.index & bit) != 0, lead[:, ::-1], lead).reshape(array.shape)
            bit *= 2
        return array

    def to_places(self, parts):
        return [self.swap(parts[number], 2 * number) for number in range(1, self.n_places)]

    def from_places(self, own, arrived):
        found = jnp.stack([own] + arrived)
        bit = 1
        while bit < self.n_places:
            lead = found.reshape((-1, 2, bit) + own.shape)
            flipped = lead[:, ::-1]
            found = jnp.where((self.place & bit) != 0, flipped, lead).reshape(found.shape)
            bit *= 2
        return found

    def by_core(self, own, other):
        return jnp.where(
            self.core == 1, jnp.stack([other, own]), jnp.stack([own, other])
        )

    def over_groups(self, array):
        bit = self.n_group
        while bit < self.n_dp:
            array = add(array, self.swap(array, bit))
            bit *= 2
        return array


def on_device(
    n_dp,
    n_z,
    tokens,
    lengths,
    key_mask,
    query_weight,
    query_bias,
    key_weight,
    value_weight,
    value_bias,
    output_weight,
    output_bias,
    first_gain,
    first_shift,
    inner_weight,
    inner_bias,
    outer_weight,
    outer_bias,
    second_gain,
    second_shift,
    cotangent,
):
    width = tokens.shape[1]
    mine = query_weight.shape[1]
    units = inner_weight.shape[1]
    all_rows = tokens.shape[0]
    all_blocks = all_rows // BUCKET
    rows = all_rows // n_z
    plane = Plane(n_dp, n_z)
    z, core, place, index = plane.z, plane.core, plane.place, plane.index
    n_places = plane.n_places
    others = range(1, n_z)

    feed_rows = units // plane.n_group
    head_rows = mine // plane.n_group
    mixer_count = width // plane.n_group
    piece = jnp.concatenate(
        [
            lax.dynamic_slice_in_dim(inner_weight, index * feed_rows, feed_rows, 1).T,
            lax.dynamic_slice_in_dim(outer_weight, index * feed_rows, feed_rows, 0),
        ],
        axis=1,
    )
    mixer_piece = lax.dynamic_slice_in_dim(output_weight, index * head_rows, head_rows, 0)
    piece, mixer_piece = together(piece, mixer_piece)
    line = [plane.shift(piece, s) for s in others]

    mixer = plane.gather(mixer_piece).reshape(width, width)
    query_t, key_t, value_t = query_weight.T, key_weight.T, value_weight.T

    key_mask_rows = key_mask.reshape(all_blocks, 1, BUCKET)
    bias_row = jnp.concatenate([query_bias, value_bias, inner_bias])
    bias_rows = jnp.pad(bias_row, (0, 16 * BUCKET - bias_row.shape[0])).reshape(16, BUCKET)
    place_z = z.reshape(1)
    mixed = attend_forward(
        n_z, lengths, tokens, query_t, key_t, value_t, bias_rows, key_mask_rows
    )
    mixed, line = together(mixed, line)

    near = jnp.stack(line)
    by_x, by_y = plane.swap(near, 2), plane.swap(near, 4)
    mixed, near = together(mixed, near)
    mixed = lax.all_to_all(mixed, "tensor", 0, 0)
    own_units = jnp.concatenate([inner_weight.T, outer_weight], axis=1)

    attention_own = jnp.concatenate([query_t, key_t, value_t], axis=1)
    attention_piece = lax.dynamic_slice_in_dim(attention_own, index * head_rows, head_rows, 0)
    attention_line = [plane.shift(attention_piece, s) for s in others]
    biases = mixed[:, 0, mine:].reshape(n_z, -1)[:, : bias_row.shape[0]].astype(f32)
    head_biases = jnp.pad(
        jnp.stack([biases[:, :mine], biases[:, mine : 2 * mine]], axis=1), ((0, 0), (0, 6), (0, 0))
    )
    inner_biases = biases[:, 2 * mine :]
    inner_biases = jnp.concatenate(
        [
            lax.dynamic_slice_in_dim(inner_biases, lax.rem(z + n_z - s, n_z), 1, 0)
            for s in range(n_z)
        ],
        axis=0,
    )
    inner_biases = inner_biases.reshape(n_z, plane.n_group, feed_rows).transpose(1, 0, 2)
    inner_biases = plane.turned(inner_biases).reshape(n_places, 2, 1, n_z * feed_rows)
    inner_biases = inner_biases.transpose(1, 0, 2, 3).reshape(plane.n_group, 1, -1)
    vectors = jnp.stack(
        [output_bias, first_gain, first_shift, outer_bias, second_gain, second_shift]
        + [jnp.zeros_like(output_bias)] * 2
    ).astype(f32)

    info = jnp.stack([z, place, core])
    shared_args = (info, vectors, inner_biases, own_units)
    cut = feed_rows // 2
    far = [plane.swap(by_x[:, :cut], 4), plane.swap(by_y[:, cut:], 2)]
    near_there, x_there, y_there, mixer, attention_line = together(
        near, by_x, by_y, mixer, attention_line
    )
    send = [plane.swap(units_of, 1) for units_of in (near_there, x_there, y_there)]
    attention_line = jnp.stack(attention_line)
    attention_swaps = plane.to_places([attention_line] * n_places)
    hidden, slope, normed_low, first_normed, first_scale, second_sum = feed_forward(
        ((0, 0), (0, 1), (0, 2), (1, 0), (1, 1), (1, 2)),
        *shared_args,
        [near, by_x, by_y] + send,
        first=(tokens, mixed, mixer),
    )
    second_sum, far, attention_swaps = together(second_sum, far, attention_swaps)
    attention_half = plane.from_places(attention_line, attention_swaps)
    attention_other = plane.swap(attention_half, 1)
    far_send = [plane.swap(half, 1) for half in far]
    keep = [near, by_x, by_y] + far
    send = send + far_send
    hidden, slope, my_output, grad_second, grad_outer, second_sums = feed_forward(
        ((0, 3), (1, 3)), *shared_args, far + far_send,
        going=(normed_low, second_sum, hidden, slope), last=(lengths, cotangent),
    )
    output = lax.all_gather(my_output, "tensor", axis=0, tiled=True)

    grad_outer, attention_other = together(grad_outer, attention_other)

    shared_args = (info, grad_outer, normed_low, hidden, slope, own_units)
    sent_early, sent_late, bias_sent, grad_normed = feed_back(*shared_args, grad_second, send)
    other = [plane.swap(sent_early, 1), plane.swap(sent_late, 1)]
    attention_remote = plane.by_core(attention_half, attention_other)
    attention_remote = attention_remote.transpose(2, 1, 0, 3, 4).reshape(n_z - 1, mine, 3 * width)
    projected = project(
        place_z, tokens, attention_own, attention_remote, head_biases, rows // BUCKET
    )
    projected, other = together(projected, other)
    (
        inner_stay, outer_stay, inner_go, outer_go, bias_kept, grad_first, grad_attended, first_sums
    ) = feed_back(
        *shared_args, grad_normed, keep, other,
        (first_normed, first_scale, vectors),
    )
    inner_came, outer_came = plane.swap(inner_go, 4), plane.swap(outer_go, 2)
    bias_grads = jnp.stack(
        [bias_kept[:, 0], bias_sent[:, 0]], axis=1
    )
    inner_bias_grad = plane.turned(bias_grads.reshape(plane.n_group, n_z, feed_rows))
    inner_bias_grad = inner_bias_grad.transpose(1, 0, 2)
    inner_bias_grad = jnp.concatenate(
        [
            sum(
                jnp.where(lax.rem(z - t + n_z, n_z) == s, inner_bias_grad[s : s + 1], 0.0)
                for s in range(n_z)
            )
            for t in range(n_z)
        ],
        axis=0,
    ).reshape(n_z, units)

    grads, my_tokens_grad, back_sums = attend_back(
        place_z, lengths, grad_attended, grad_first, attention_own, attention_remote, mixer,
        *projected, key_mask_rows,
    )
    grads, inner_came, outer_came, output = together(grads, inner_came, outer_came, output)
    inner_on, outer_on = (
        plane.swap(add(inner_stay[1], inner_came[1]), 2),
        plane.swap(add(outer_stay[1], outer_came[1]), 4),
    )
    tokens_grad = lax.all_gather(my_tokens_grad, "tensor", axis=0, tiled=True)

    def weight_grads(side, other=None, small=None):
        info = jnp.stack([2 * side, 2 * side + 1, z, place])
        return attention_grads(
            n_places, info, grads, mixed, tokens, grad_attended, other, small
        )

    sent = weight_grads(1 - core)
    sent, inner_on, outer_on, back_sums, first_sums, second_sums, inner_bias_grad = together(
        sent, inner_on, outer_on, back_sums, first_sums, second_sums, inner_bias_grad
    )
    other = [plane.swap(part, 1) for part in sent]

    small = jnp.concatenate(
        [first_sums[:3], second_sums[:3], inner_bias_grad, jnp.sum(back_sums, axis=0)[:2]], axis=0
    )
    small = jnp.pad(small, ((0, -small.shape[0] % 16), (0, 0))).astype(bf16)
    small_rows = small.shape[0]

    small = add(small, plane.swap(small, 1))
    kept = list(weight_grads(core, other, small))
    arrived = plane.to_places(kept)
    feed_parts = [
        jnp.concatenate(
            [
                add(inner_stay[0, s], inner_came[0, s], inner_on[s]),
                add(outer_stay[0, s], outer_came[0, s], outer_on[s]),
            ],
            axis=1,
        )
        for s in range(n_z)
    ]
    feed_line = [plane.shift(feed_parts[s], -s) for s in others]
    output = copied(output)
    arrived, output = together(arrived, output)
    small = add(small, *[a[-small_rows:] for a in arrived])
    count = 2 * mine // n_places
    attention_parts = [
        add(*[a[s * count : (s + 1) * count] for a in [kept[0]] + arrived]) for s in range(n_z)
    ]
    attention_line = [
        plane.shift(jnp.concatenate([attention_parts[s], small], axis=0), s) for s in others
    ]
    feed_total = plane.over_groups(add(feed_parts[0], *feed_line))
    feed_arrived = plane.to_places([feed_total] * n_places)
    tokens_grad = copied(tokens_grad)
    attention_line, feed_arrived, tokens_grad = together(
        attention_line, feed_arrived, tokens_grad
    )
    attention_total = plane.over_groups(
        add(attention_parts[0], *[a[:count] for a in attention_line])
    )
    small = plane.over_groups(add(small, *[a[count:] for a in attention_line])).astype(f32)
    arrived = plane.to_places([attention_total] * n_places)
    feed_half = plane.from_places(feed_total, feed_arrived)
    feed_other = plane.swap(feed_half, 1)
    inner_grad, outer_grad = finish_feed(core.reshape(1), feed_half, feed_other)
    inner_bias_sum = lax.dynamic_slice_in_dim(small, 6 + z, 1, 0)[0]
    head_sums = lax.dynamic_slice_in_dim(small[6 + n_z : 8 + n_z], z * mine, mine, 1)
    arrived, inner_grad, outer_grad, small, inner_bias_sum, head_sums = together(
        arrived, inner_grad, outer_grad, small, inner_bias_sum, head_sums
    )
    attention_half = plane.from_places(attention_total, arrived)
    attention_other = plane.swap(attention_half, 1)
    grad_list = plane.by_core(attention_half, attention_other)
    grad_list = grad_list.reshape(2, n_places, 2, mine // n_places, width)
    grad_list = grad_list.transpose(0, 2, 1, 3, 4).reshape(4, mine, width)

    shared = small[:6]

    return (
        output,
        tokens_grad,
        grad_list[0].T.astype(f32),
        head_sums[0],
        grad_list[1].T.astype(f32),
        grad_list[2].T.astype(f32),
        head_sums[1],
        grad_list[3].astype(f32),
        shared[0],
        shared[1],
        shared[2],
        inner_grad,
        inner_bias_sum,
        outer_grad,
        shared[3],
        shared[4],
        shared[5],
    )


def solution(mesh):
    n_dp, n_z = mesh.shape["dp"], mesh.shape["tensor"]
    in_specs = (
        P("dp", None),
        P("dp", None),
        P("dp"),
        P(None, "tensor"),
        P("tensor"),
        P(None, "tensor"),
        P(None, "tensor"),
        P("tensor"),
        P("tensor", None),
        P(),
        P(),
        P(),
        P(None, "tensor"),
        P("tensor"),
        P("tensor", None),
        P(),
        P(),
        P(),
        P("dp", None),
    )
    out_specs = (
        P("dp", None),
        P("dp", None),
        P(None, "tensor"),
        P("tensor"),
        P(None, "tensor"),
        P(None, "tensor"),
        P("tensor"),
        P("tensor", None),
        P(),
        P(),
        P(),
        P(None, "tensor"),
        P("tensor"),
        P("tensor", None),
        P(),
        P(),
        P(),
    )

    def program(*args):
        return on_device(n_dp, n_z, *args)

    return jax.shard_map(
        program, mesh=mesh, in_specs=in_specs, out_specs=out_specs, check_vma=False
    )
```

```python
import functools

import jax
import jax.numpy as jnp
from jax import lax
from jax.experimental import pallas as pl
from jax.experimental.pallas import tpu as pltpu
from jax.sharding import PartitionSpec as P

HEAD = 64
BUCKET = 512
ITEMS = 8


negative_fill = -1e30
epsilon = 1e-06
f32 = jnp.float32
bf16 = jnp.bfloat16
VMEM_BYTES = 56 * 1024 * 1024


def dot(left, right):
    return jnp.dot(left, right, preferred_element_type=f32)


def contract_rows(left, right):
    return lax.dot_general(left, right, (((0,), (0,)), ((), ())), preferred_element_type=f32)


def contract_cols(left, right):
    return lax.dot_general(left, right, (((1,), (1,)), ((), ())), preferred_element_type=f32)


def norm_rows(values):
    centred = values - jnp.mean(values, axis=1, keepdims=True)
    inv_scale = lax.rsqrt(jnp.mean(centred * centred, axis=1, keepdims=True) + epsilon)
    return centred * inv_scale, inv_scale


def norm_back(grad_rows, norm_gain, normed, inv_scale):
    scaled = grad_rows * norm_gain
    return inv_scale * (
        scaled
        - jnp.mean(scaled, axis=1, keepdims=True)
        - normed * jnp.mean(scaled * normed, axis=1, keepdims=True)
    )


def column_sum(matrix):
    return jnp.sum(matrix.astype(f32), axis=0, keepdims=True)


def fixed(shape):
    return pl.BlockSpec(shape, lambda *_: (0,) * len(shape))


def cost(microseconds):
    return pl.CostEstimate(
        flops=int(microseconds * 2.5e8),
        bytes_accessed=int(microseconds * 2.5e5),
        transcendentals=0,
    )


def params(axes):
    return pltpu.CompilerParams(
        dimension_semantics=("arbitrary",) * axes, vmem_limit_bytes=VMEM_BYTES
    )


def item_places(lengths_ref, row, shape, axis):
    places = lax.broadcasted_iota(jnp.int32, shape, axis)
    end = jnp.int32(0)
    items = jnp.zeros(shape, jnp.int32)
    for slot in range(ITEMS):
        end = end + lengths_ref[row, slot]
        items = items + (places >= end).astype(jnp.int32)
    return items


def as_column(row):
    return jnp.broadcast_to(row.astype(f32), (8, row.shape[1])).T[:, :1]


def mask_bias(lengths_ref, row, key_mask):
    shape = (BUCKET, BUCKET)
    diagonal = lax.broadcasted_iota(jnp.int32, shape, 0) == lax.broadcasted_iota(
        jnp.int32, shape, 1
    )
    item_row = item_places(lengths_ref, row, (1, BUCKET), 1)
    item_column = item_places(lengths_ref, row, (BUCKET, 1), 0)
    code_column = jnp.where(as_column(key_mask) == 1.0, item_column, -1)
    return jnp.where((code_column == item_row) | diagonal, 0.0, negative_fill).astype(f32)


def attend_forward_kernel(
    lengths_ref, tokens_ref, query_ref, key_ref, value_ref, biases_ref, key_mask_ref, mixed_ref,
):
    mine = query_ref.shape[0]
    rows = tokens_ref[...]
    queries = contract_cols(query_ref[...], rows) + as_column(biases_ref[0:1, :mine])
    queries = (queries.astype(bf16) * HEAD ** (-0.5)).astype(bf16)
    keys = contract_cols(rows, key_ref[...]).astype(bf16)
    values = contract_cols(value_ref[...], rows) + as_column(biases_ref[0:1, mine : 2 * mine])
    values = values.astype(bf16)
    bias = mask_bias(lengths_ref, pl.program_id(0), key_mask_ref[0])
    for head in range(mine // HEAD):
        at = slice(head * HEAD, (head + 1) * HEAD)
        scores = dot(keys[:, at], queries[at]) + bias
        exponent = jnp.exp(scores - jnp.max(scores, axis=0, keepdims=True))
        total = jnp.sum(exponent, axis=0, keepdims=True)
        mixed_ref[0, 0, at] = (dot(values[at], exponent.astype(bf16)) / total).astype(bf16)
    mixed_ref[0, 0, mine:] = biases_ref[...]


def attend_forward(n_z, lengths, tokens, query, key, value, biases, key_mask):
    blocks = lengths.shape[0]
    own = blocks // n_z
    mine, width = key.shape
    whole = (n_z, own, mine + biases.shape[0], BUCKET)
    return pl.pallas_call(
        attend_forward_kernel,
        grid=(blocks,),
        in_specs=[
            pl.BlockSpec(memory_space=pltpu.SMEM),
            pl.BlockSpec((BUCKET, width), lambda b: (b, 0)),
            fixed((mine, width)),
            fixed((mine, width)),
            fixed((mine, width)),
            fixed(biases.shape),
            pl.BlockSpec((1, 1, BUCKET), lambda b: (b, 0, 0)),
        ],
        out_specs=pl.BlockSpec((1, 1) + whole[2:], lambda b: (b // own, b % own, 0, 0)),
        out_shape=jax.ShapeDtypeStruct(whole, bf16),
        compiler_params=params(1),
        name="attend_forward",
        cost_estimate=cost(12),
    )(lengths, tokens, query, key, value, biases, key_mask)


def fetch_units(step, picks, own_ref, halves, units, sems):
    feed_rows = units.shape[2]
    cut = feed_rows // 2

    def copies(number):
        slot = number % 2
        row = pl.multiple_of(picks[number] * feed_rows, 16)
        ends = [
            (own_ref.at[pl.ds(row, feed_rows)], units.at[slot, 0]),
            (halves[number][0], units.at[slot, 1:, :cut]),
            (halves[number][1], units.at[slot, 1:, cut:]),
        ]
        return [
            pltpu.make_async_copy(source, target, sems.at[slot, i])
            for i, (source, target) in enumerate(ends)
        ]

    for number in range(len(halves)):

        @pl.when(step == number)
        def _(number=number):
            if number == 0:
                for copy in copies(0):
                    copy.start()
            if number + 1 < len(halves):
                for copy in copies(number + 1):
                    copy.start()
            for copy in copies(number):
                copy.wait()

    return units.at[lax.rem(step, 2)]


def take_halves(numbers, refs):
    halves, refs = [], list(refs)
    for number in numbers:
        if number == 3:
            halves.append((refs.pop(0), refs.pop(0)))
        else:
            ref = refs.pop(0)
            cut = ref.shape[1] // 2
            halves.append((ref.at[:, :cut], ref.at[:, cut:]))
    return halves, refs


def split_units(units):
    width = units.shape[2] // 2
    return units[:, :, :width].reshape(-1, width), units[:, :, width:].reshape(-1, width)


ANYWHERE = pl.BlockSpec(memory_space=pl.ANY)


def feed_forward_kernel(chunks, first, last, info_ref, *rest):
    def take(count):
        nonlocal rest
        taken, rest = rest[:count], rest[count:]
        return taken

    vectors_ref, bias_ref, own_ref = take(3)
    halves, rest = take_halves([number for _, number in chunks], rest)
    if first:
        tokens_ref, mixed_ref, mixer_ref = take(3)
    else:
        normed_low_ref, start_ref, _, _ = take(4)
    if last:
        lengths_ref, cotangent_ref = take(2)
    hidden_ref, slope_ref = take(2)
    if first:
        normed_low_ref, first_normed_ref, first_scale_ref = take(3)
    if last:
        output_ref, grad_second_ref, grad_outer_ref, sums_ref = take(4)
    else:
        (second_sum,) = take(1)
    units, sems = take(2)
    if last:
        (second_sum,) = take(1)

    step = pl.program_id(0)
    picks = [(info_ref[1] ^ number) * 2 + (info_ref[2] ^ side) for side, number in chunks]
    weights = fetch_units(step, picks, own_ref, halves, units, sems)
    output_bias, first_gain, first_shift, outer_bias, second_gain, second_shift = (
        vectors_ref[i : i + 1, :] for i in range(6)
    )

    @pl.when(step == 0)
    def _():
        if first:
            n_z, own, mine, _ = mixed_ref.shape
            attended = output_bias + jnp.concatenate(
                [
                    sum(
                        contract_rows(mixed_ref[t, b], mixer_ref[t * mine : (t + 1) * mine, :])
                        for t in range(n_z)
                    )
                    for b in range(own)
                ],
                axis=0,
            )
            normed, inv_scale = norm_rows(tokens_ref[...].astype(f32) + attended)
            whole = normed * first_gain + first_shift
            first_normed_ref[...] = normed
            first_scale_ref[...] = inv_scale
            normed_low_ref[...] = whole.astype(bf16)
            second_sum[...] = whole + outer_bias
        else:
            second_sum[...] = start_ref[...]

    inner, outer = split_units(weights)
    inner_pre = contract_cols(normed_low_ref[...], inner) + bias_ref[0]
    normal_cdf = 0.5 + 0.5 * lax.erf(inner_pre * 0.7071067811865476)
    bell = jnp.exp(-0.5 * inner_pre * inner_pre)
    hidden = (inner_pre * normal_cdf).astype(bf16)
    hidden_ref[...] = hidden.T
    slope_ref[...] = (normal_cdf + inner_pre * bell * 0.3989422804014327).astype(bf16)
    second_sum[...] += dot(hidden, outer)

    if last:

        @pl.when(step == pl.num_programs(0) - 1)
        def _():
            normed, inv_scale = norm_rows(second_sum[...])
            blocks = normed.shape[0] // BUCKET
            live = jnp.concatenate(
                [
                    (item_places(lengths_ref, info_ref[0] * blocks + b, (BUCKET, 1), 0) < ITEMS)
                    for b in range(blocks)
                ],
                axis=0,
            ).astype(f32)
            output_ref[...] = ((normed * second_gain + second_shift) * live).astype(bf16)
            grad_final = cotangent_ref[...].astype(f32) * live
            grad_second = norm_back(grad_final, second_gain, normed, inv_scale)
            grad_outer = grad_second.astype(bf16)
            grad_second_ref[...] = grad_second
            grad_outer_ref[...] = grad_outer
            sums_ref[0:1, :] = column_sum(grad_outer)
            sums_ref[1:2, :] = column_sum(grad_final * normed)
            sums_ref[2:3, :] = column_sum(grad_final)


def feed_forward(chunks, info, vectors, biases, own, halves, first=None, going=None, last=None):
    width = vectors.shape[1]
    n_z = halves[0].shape[0] + 1
    feed_rows, twice = own.shape[0] // 8, 2 * width
    rows = first[1].shape[1] * BUCKET if first else going[0].shape[0]
    chunk = n_z * feed_rows
    whole = fixed((rows, width))
    my_rows = pl.BlockSpec((rows, width), lambda j, info: (info[0], 0))
    numbers = [4 * side + number for side, number in chunks]

    def at(j, info):
        found = numbers[0]
        for step, number in enumerate(numbers[1:], 1):
            found = jnp.where(j >= step, number, found)
        return found

    hidden_spec = pl.BlockSpec((chunk, rows), lambda j, info: (at(j, info), 0))
    slope_spec = pl.BlockSpec((rows, chunk), lambda j, info: (0, at(j, info)))
    in_specs = [
        fixed((8, width)),
        pl.BlockSpec((1, 1, chunk), lambda j, info: (at(j, info), 0, 0)),
        ANYWHERE,
    ] + [ANYWHERE] * len(halves)
    args = [vectors, biases, own] + halves
    shapes = [
        ((8 * chunk, rows), bf16, hidden_spec),
        ((rows, 8 * chunk), bf16, slope_spec),
    ]
    scratch = [
        pltpu.VMEM((2, n_z, feed_rows, twice), bf16),
        pltpu.SemaphoreType.DMA((2, 3)),
    ]
    aliases = {}
    if first:
        tokens, mixed, mixer = first
        mine = width // n_z
        in_specs += [my_rows, fixed((n_z, mixed.shape[1], mine, BUCKET)), fixed(mixer.shape)]
        args += [tokens, mixed, mixer]
        shapes += [
            ((rows, width), bf16, whole),
            ((rows, width), f32, whole),
            ((rows, 1), f32, fixed((rows, 1))),
        ]
    else:
        aliases = {1 + len(args) + 2: 0, 1 + len(args) + 3: 1}
        in_specs += [whole, whole, ANYWHERE, ANYWHERE]
        args += list(going)
    if last:
        in_specs += [pl.BlockSpec(memory_space=pltpu.SMEM), my_rows]
        args += list(last)
        shapes += [
            ((rows, width), bf16, whole),
            ((rows, width), f32, whole),
            ((rows, width), bf16, whole),
            ((8, width), f32, fixed((8, width))),
        ]
        scratch.append(pltpu.VMEM((rows, width), f32))
    else:
        shapes.append(((rows, width), f32, whole))
    return pl.pallas_call(
        functools.partial(feed_forward_kernel, chunks, first is not None, last is not None),
        grid_spec=pltpu.PrefetchScalarGridSpec(
            num_scalar_prefetch=1,
            grid=(len(chunks),),
            in_specs=in_specs,
            out_specs=[spec for _, _, spec in shapes],
            scratch_shapes=scratch,
        ),
        out_shape=[jax.ShapeDtypeStruct(shape, kind) for shape, kind, _ in shapes],
        input_output_aliases=aliases,
        compiler_params=params(1),
        name="feed_forward",
        cost_estimate=cost(3 * len(chunks)),
    )(info, *args)


STAY = ((0, 1), (0, 2))
GO = ((2, 3), (1, 3))


def feed_back_kernel(
    keeps, info_ref, grad_outer_ref, normed_low_ref, hidden_ref, slope_ref,
    own_ref, start_ref, *rest,
):
    halves, rest = take_halves(range(4), rest)
    if keeps:
        other_refs, norm_refs, rest = rest[:2], rest[2:5], rest[5:]
        stay_refs, go_refs, rest = rest[0:2], rest[2:4], rest[4:]
        bias_grad_ref, grad_first_ref, grad_attended_ref, sums_ref, units, sems = rest[:6]
        grad_normed_ref = rest[6]
    else:
        *grad_refs, bias_grad_ref, grad_normed_ref, units, sems = rest
    step = pl.program_id(0)
    side = info_ref[2] if keeps else 1 - info_ref[2]
    picks = [(info_ref[1] ^ number) * 2 + side for number in range(4)]
    weights = fetch_units(step, picks, own_ref, halves, units, sems)

    @pl.when(step == 0)
    def _():
        grad_normed_ref[...] = start_ref[...]

    n_z, feed_rows, twice = weights.shape
    width = twice // 2
    inner, outer = split_units(weights)
    grad_outer = grad_outer_ref[...]
    grad_hidden = contract_cols(grad_outer, outer)
    grad_inner = (grad_hidden * slope_ref[...].astype(f32)).astype(bf16)
    outer_grad = dot(hidden_ref[...], grad_outer).reshape(n_z, feed_rows, width)
    inner_grad = contract_rows(grad_inner, normed_low_ref[...]).reshape(n_z, feed_rows, width)
    bias_grad_ref[0] = column_sum(grad_inner)
    grad_normed_ref[...] += dot(grad_inner, inner)

    for number in range(4):

        @pl.when(step == number)
        def _(number=number):
            for track, value in enumerate((inner_grad, outer_grad)):
                at = slice(track * width, (track + 1) * width)
                if keeps:
                    found = value + other_refs[number // 2][0, :, :, at].astype(f32)
                    ref = stay_refs[track] if number in STAY[track] else go_refs[track]
                    ref[0] = found.astype(bf16)
                else:
                    grad_refs[number // 2][0, :, :, at] = value.astype(bf16)

    if keeps:

        @pl.when(step == pl.num_programs(0) - 1)
        def _():
            first_normed_ref, first_scale_ref, vectors_ref = norm_refs
            grad_rows, normed = grad_normed_ref[...], first_normed_ref[...]
            grad_first = norm_back(grad_rows, vectors_ref[1:2, :], normed, first_scale_ref[...])
            grad_attended = grad_first.astype(bf16)
            grad_first_ref[...] = grad_first
            grad_attended_ref[...] = grad_attended
            sums_ref[0:1, :] = column_sum(grad_attended)
            sums_ref[1:2, :] = column_sum(grad_rows * normed)
            sums_ref[2:3, :] = column_sum(grad_rows)


def feed_back(
    info, grad_outer, normed_low, hidden, slope, own, start, units, others=None, norm=None
):
    rows, width = grad_outer.shape
    keeps = others is not None
    count = 4
    feed_rows, twice = own.shape[0] // 8, 2 * width
    n_z = units[0].shape[0] + 1
    chunk = n_z * feed_rows
    flip = 0 if keeps else 1
    columns = pl.BlockSpec((rows, chunk), lambda i, info: (0, 4 * flip + i))
    whole = fixed((rows, width))
    part = (n_z, feed_rows, twice)
    track = (2, n_z, feed_rows, width)
    unit_rows = pl.BlockSpec((chunk, rows), lambda i, info: (4 * flip + i, 0))
    in_specs = [whole, whole, unit_rows, columns, ANYWHERE, whole] + [ANYWHERE] * len(units)
    args = [grad_outer, normed_low, hidden, slope, own, start] + units
    bias_shape = (
        (count, 1, chunk),
        f32,
        pl.BlockSpec((1, 1, chunk), lambda i, info: (i, 0, 0)),
    )
    scratch = [pltpu.VMEM((2,) + part, bf16), pltpu.SemaphoreType.DMA((2, 3))]

    def one(shape, at):
        return pl.BlockSpec((1,) + shape[1:], lambda i, info: (at(i), 0, 0, 0))

    early, late = (lambda i: jnp.minimum(i, 1)), (lambda i: jnp.maximum(i - 2, 0))
    pair = (2,) + part
    if keeps:
        in_specs += [one(pair, early), one(pair, late)]
        in_specs += [whole, fixed((rows, 1)), fixed((8, width))]
        args += list(others) + list(norm)
        slow, slower = (lambda i: i // 2), (lambda i: jnp.maximum(i - 1, 0) // 2)
        shapes = [(track, bf16, one(track, at)) for at in (early, slow, late, slower)] + [
            bias_shape,
            ((rows, width), f32, whole),
            ((rows, width), bf16, whole),
            ((8, width), f32, fixed((8, width))),
        ]
        scratch.append(pltpu.VMEM((rows, width), f32))
    else:
        shapes = [
            (pair, bf16, one(pair, early)),
            (pair, bf16, one(pair, late)),
            bias_shape,
            ((rows, width), f32, whole),
        ]
    return pl.pallas_call(
        functools.partial(feed_back_kernel, keeps),
        grid_spec=pltpu.PrefetchScalarGridSpec(
            num_scalar_prefetch=1,
            grid=(count,),
            in_specs=in_specs,
            out_specs=[spec for _, _, spec in shapes],
            scratch_shapes=scratch,
        ),
        out_shape=[jax.ShapeDtypeStruct(shape, kind) for shape, kind, _ in shapes],
        compiler_params=params(1),
        name="feed_back_own" if keeps else "feed_back",
        cost_estimate=cost(3 * count),
    )(info, *args)


def finish_feed_kernel(core_ref, own_ref, other_ref, inner_ref, outer_ref, inner_rows):
    places, count, twice = own_ref.shape
    width = twice // 2
    for source, side in ((own_ref, core_ref[0]), (other_ref, 1 - core_ref[0])):
        for place in range(places):
            row = pl.multiple_of((2 * place + side) * count, 16)
            inner_rows[pl.ds(row, count), :] = source[place, :, :width].astype(f32)
            outer_ref[pl.ds(row, count), :] = source[place, :, width:].astype(f32)
    inner_ref[...] = inner_rows[...].T


def finish_feed(core, own, other):
    places, count, twice = own.shape
    shape = (2 * places * count, twice // 2)
    inner_shape = (shape[1], shape[0])
    return pl.pallas_call(
        finish_feed_kernel,
        grid_spec=pltpu.PrefetchScalarGridSpec(
            num_scalar_prefetch=1,
            grid=(1,),
            in_specs=[fixed(own.shape), fixed(other.shape)],
            out_specs=[fixed(inner_shape), fixed(shape)],
            scratch_shapes=[pltpu.VMEM(shape, f32)],
        ),
        out_shape=[
            jax.ShapeDtypeStruct(inner_shape, f32),
            jax.ShapeDtypeStruct(shape, f32),
        ],
        compiler_params=params(1),
        name="finish_feed",
        cost_estimate=cost(5),
    )(core, own, other)


def copy_kernel(from_ref, to_ref):
    to_ref[...] = from_ref[...]


def copied(array):
    block = pl.BlockSpec((BUCKET, array.shape[1]), lambda i: (i, 0))
    return pl.pallas_call(
        copy_kernel,
        grid=(array.shape[0] // BUCKET,),
        in_specs=[block],
        out_specs=block,
        out_shape=jax.ShapeDtypeStruct(array.shape, array.dtype),
        compiler_params=params(1),
        name="copied",
        cost_estimate=cost(0.5),
    )(array)


def project_kernel(
    place_ref, tokens_ref, own_ref, remote_ref, biases_ref, query_ref, key_ref, value_ref
):
    rows = tokens_ref[...]
    width = rows.shape[1]
    weights = jnp.where(pl.program_id(1) == 0, own_ref[...], remote_ref[0])
    queries = contract_cols(weights[:, :width], rows) + as_column(biases_ref[0, 0:1, :])
    query_ref[...] = (queries.astype(bf16) * HEAD ** (-0.5)).astype(bf16)
    key_ref[...] = contract_cols(weights[:, width : 2 * width], rows).astype(bf16)
    values = contract_cols(weights[:, 2 * width :], rows) + as_column(biases_ref[0, 1:2, :])
    value_ref[...] = values.astype(bf16)


def project(place, tokens, own, remote, biases, buckets):
    width = tokens.shape[1]
    mine = own.shape[0]
    n_z = width // mine
    there = lambda s, place: lax.rem(place[0] + n_z - s, n_z)
    out = pl.BlockSpec((None, mine, BUCKET), lambda b, s, place: (b, there(s, place), 0))
    return pl.pallas_call(
        project_kernel,
        grid_spec=pltpu.PrefetchScalarGridSpec(
            num_scalar_prefetch=1,
            grid=(buckets, n_z),
            in_specs=[
                pl.BlockSpec((BUCKET, width), lambda b, s, place: (place[0] * buckets + b, 0)),
                fixed(own.shape),
                pl.BlockSpec(
                    (1, mine, 3 * width), lambda b, s, place: (jnp.maximum(s - 1, 0), 0, 0)
                ),
                pl.BlockSpec((1, 8, mine), lambda b, s, place: (there(s, place), 0, 0)),
            ],
            out_specs=[out] * 3,
        ),
        out_shape=[jax.ShapeDtypeStruct((buckets, width, BUCKET), bf16)] * 3,
        compiler_params=params(2),
        name="project",
        cost_estimate=cost(5),
    )(place, tokens, own, remote, biases)


def attend_back_kernel(
    place_ref, lengths_ref, grad_attended_ref, grad_first_ref, own_ref, remote_ref, mixer_ref,
    query_ref, key_ref, value_ref, key_mask_ref,
    grads_ref, tokens_grad_ref, sums_ref,
    bias, grad_mixed_t, whole, weights, mixer, sems,
):
    pair = pl.program_id(1)
    pairs, width = whole.shape[1], weights.shape[0]
    mine = own_ref.shape[0]
    n_z = width // mine

    def fetches():
        ends = [(mixer_ref, mixer)]
        for s in range(n_z):
            row = pl.multiple_of(lax.rem(place_ref[0] + n_z - s, n_z) * mine, 16)
            source = own_ref if s == 0 else remote_ref.at[s - 1]
            ends.append((source, weights.at[pl.ds(row, mine)]))
        return [
            pltpu.make_async_copy(source, target, sems.at[i])
            for i, (source, target) in enumerate(ends)
        ]

    @pl.when(pair == 0)
    def _():
        for fetch in fetches():
            fetch.start()
        row = place_ref[0] * pl.num_programs(0) + pl.program_id(0)
        bias[...] = mask_bias(lengths_ref, row, key_mask_ref[0])
        for fetch in fetches():
            fetch.wait()
        grad_mixed_t[...] = contract_cols(mixer[...], grad_attended_ref[...]).astype(bf16)

    queries, keys_t = query_ref[...], key_ref[...]
    keys, values = keys_t.T, value_ref[...].T
    start = pl.multiple_of(pair * keys.shape[1], 128)
    grad_mixed = grad_mixed_t[pl.ds(start, keys.shape[1]), :]
    grad_queries, grad_keys, grad_values = [], [], []
    for head in range(keys.shape[1] // HEAD):
        at = slice(head * HEAD, (head + 1) * HEAD)
        scores = dot(keys[:, at], queries[at]) + bias[...]
        exponent = jnp.exp(scores - jnp.max(scores, axis=0, keepdims=True))
        probs = exponent * (1.0 / jnp.sum(exponent, axis=0, keepdims=True))
        grad_probs = dot(values[:, at], grad_mixed[at])
        shift = jnp.sum(probs * grad_probs, axis=0, keepdims=True)
        grad_scores = (probs * (grad_probs - shift)).astype(bf16)
        grad_values.append(contract_cols(probs.astype(bf16), grad_mixed[at]))
        grad_keys.append(contract_cols(grad_scores, queries[at]))
        grad_queries.append(dot(keys_t[at], grad_scores) * HEAD ** (-0.5))
    query_t = jnp.concatenate(grad_queries, axis=0).astype(bf16)
    found = (
        query_t.T,
        jnp.concatenate(grad_keys, axis=1).astype(bf16),
        jnp.concatenate(grad_values, axis=1).astype(bf16),
    )
    for number, grad in enumerate(found):
        grads_ref[number, 0] = query_t if number == 0 else grad.T
        whole[number, pair] = grad
    sums_ref[0, 0:1, :] = column_sum(found[0])
    sums_ref[0, 1:2, :] = column_sum(found[2])

    @pl.when(pair == pl.num_programs(1) - 1)
    def _():
        total = grad_first_ref[...]
        for number in range(3):
            grad = jnp.concatenate([whole[number, i] for i in range(pairs)], axis=1)
            total += dot(grad, weights[:, number * width : (number + 1) * width])
        tokens_grad_ref[...] = total.astype(bf16)


def attend_back(
    place, lengths, grad_attended, grad_first, own, remote, mixer, queries, keys, values, key_mask
):
    rows, width = grad_attended.shape
    blocks = rows // BUCKET
    pair = 2 * HEAD
    by_bucket = pl.BlockSpec((BUCKET, width), lambda b, h, place: (b, 0))
    by_pair = pl.BlockSpec((None, pair, BUCKET), lambda b, h, place: (b, h, 0))
    return pl.pallas_call(
        attend_back_kernel,
        grid_spec=pltpu.PrefetchScalarGridSpec(
            num_scalar_prefetch=1,
            grid=(blocks, width // pair),
            in_specs=[
                pl.BlockSpec(memory_space=pltpu.SMEM),
                by_bucket,
                by_bucket,
                ANYWHERE,
                ANYWHERE,
                ANYWHERE,
                by_pair,
                by_pair,
                by_pair,
                pl.BlockSpec((1, 1, BUCKET), lambda b, h, place: (place[0] * blocks + b, 0, 0)),
            ],
            out_specs=[
                pl.BlockSpec((3, 1, pair, BUCKET), lambda b, h, place: (0, b, h, 0)),
                by_bucket,
                pl.BlockSpec((1, 8, pair), lambda b, h, place: (b, 0, h)),
            ],
            scratch_shapes=[
                pltpu.VMEM((BUCKET, BUCKET), f32),
                pltpu.VMEM((width, BUCKET), bf16),
                pltpu.VMEM((3, width // pair, BUCKET, pair), bf16),
                pltpu.VMEM((width, own.shape[1]), bf16),
                pltpu.VMEM(mixer.shape, bf16),
                pltpu.SemaphoreType.DMA((1 + width // own.shape[0],)),
            ],
        ),
        out_shape=[
            jax.ShapeDtypeStruct((3, blocks, width, BUCKET), bf16),
            jax.ShapeDtypeStruct((rows, width), bf16),
            jax.ShapeDtypeStruct((blocks, 8, width), f32),
        ],
        compiler_params=params(2),
        name="attend_back",
        cost_estimate=cost(20),
    )(
        place, lengths, grad_attended, grad_first, own, remote, mixer, queries, keys, values, key_mask
    )


def attention_grads_kernel(
    n_places, adds, info_ref, grads_ref, mixed_ref, tokens_ref, grad_attended_ref, *rest
):
    if adds:
        other_refs, small_ref, rest = rest[:n_places], rest[n_places], rest[n_places + 1 :]
    out_refs, whole = rest[:-1], rest[-1]
    step = pl.program_id(0)
    which = 2 * (info_ref[2] if adds else 1 - info_ref[2]) + step
    n_z, buckets, mine, _ = mixed_ref.shape
    count = mine // n_places

    @pl.when(which < 3)
    def _():
        whole[...] = sum(
            dot(grads_ref[0, b], tokens_ref[b * BUCKET : (b + 1) * BUCKET, :])
            for b in range(buckets)
        ).astype(bf16)

    @pl.when(which == 3)
    def _():
        for t in range(n_z):
            whole[t * mine : (t + 1) * mine, :] = sum(
                dot(mixed_ref[t, b], grad_attended_ref[b * BUCKET : (b + 1) * BUCKET, :])
                for b in range(buckets)
            ).astype(bf16)

    for number in range(n_places):
        for s in range(n_z):
            start = lax.rem(info_ref[0] + s, n_z) * mine + (info_ref[1] ^ number) * count
            value = whole[pl.ds(pl.multiple_of(start, 16), count), :]
            if adds:
                value = value.astype(f32) + other_refs[number][s, 0].astype(f32)
                row = (2 * s + step) * count
                out_refs[number][pl.ds(pl.multiple_of(row, 16), count), :] = value.astype(bf16)
            else:
                out_refs[number][s, 0] = value

    if adds:
        for number in range(n_places):
            out_refs[number][2 * n_z * count :, :] = small_ref[...]


def attention_grads(n_places, info, grads, mixed, tokens, grad_attended, other=None, small=None):
    rows, width = grad_attended.shape
    n_z, buckets = mixed.shape[:2]
    mine = width // n_z
    count = mine // n_places
    side = lambda info: 1 - info[2] if other is None else info[2]
    by_step = pl.BlockSpec((n_z, 1, count, width), lambda i, info: (0, i, 0, 0))
    in_specs = [
        pl.BlockSpec(
            (1, buckets, width, BUCKET), lambda i, info: (jnp.minimum(2 * side(info) + i, 2), 0, 0, 0)
        ),
        fixed((n_z, buckets, mine, BUCKET)),
        pl.BlockSpec((rows, width), lambda i, info: (info[0], 0)),
        fixed((rows, width)),
    ]
    args = [grads, mixed, tokens, grad_attended]
    if other is None:
        shapes = [((n_z, 2, count, width), by_step)] * n_places
    else:
        in_specs += [by_step] * n_places + [fixed(small.shape)]
        args += list(other) + [small]
        flat = (2 * n_z * count + small.shape[0], width)
        shapes = [(flat, fixed(flat))] * n_places
    return pl.pallas_call(
        functools.partial(attention_grads_kernel, n_places, other is not None),
        grid_spec=pltpu.PrefetchScalarGridSpec(
            num_scalar_prefetch=1,
            grid=(2,),
            in_specs=in_specs,
            out_specs=[spec for _, spec in shapes],
            scratch_shapes=[pltpu.VMEM((width, width), bf16)],
        ),
        out_shape=[jax.ShapeDtypeStruct(shape, bf16) for shape, _ in shapes],
        compiler_params=params(1),
        name="attention_grads",
        cost_estimate=cost(0.5),
    )(info, *args)


def together(*values):
    return lax.optimization_barrier(values)


def add(first, *others):
    total = first.astype(f32)
    for other in others:
        total = total + other.astype(f32)
    return total.astype(bf16)


class Plane:
    def __init__(self, n_dp, n_z):
        self.n_dp, self.n_z = n_dp, n_z
        self.n_group = min(n_dp, 8)
        self.n_places = self.n_group // 2
        self.dp = lax.axis_index("dp")
        self.z = lax.axis_index("tensor")
        self.index = lax.rem(self.dp, self.n_group)
        self.core = self.index & 1
        self.place = self.index >> 1

    def swap(self, array, bits):
        return lax.ppermute(array, "dp", [(i, i ^ bits) for i in range(self.n_dp)])

    def shift(self, array, by):
        n = self.n_z
        return lax.ppermute(array, "tensor", [(i, (i + by) % n) for i in range(n)])

    def gather(self, piece):
        if self.n_dp == self.n_group:
            whole = lax.all_gather(piece, ("tensor", "dp"))
            return whole.reshape((self.n_z, self.n_group) + piece.shape)
        groups = [
            list(range(i, i + self.n_group)) for i in range(0, self.n_dp, self.n_group)
        ]
        line = lax.all_gather(piece, "tensor")
        return lax.all_gather(line, "dp", axis=1, axis_index_groups=groups)

    def turned(self, array):
        bit = 1
        while bit < self.n_group:
            lead = array.reshape((-1, 2, bit) + array.shape[1:])
            array = jnp.where((self.index & bit) != 0, lead[:, ::-1], lead).reshape(array.shape)
            bit *= 2
        return array

    def to_places(self, parts):
        return [self.swap(parts[number], 2 * number) for number in range(1, self.n_places)]

    def from_places(self, own, arrived):
        found = jnp.stack([own] + arrived)
        bit = 1
        while bit < self.n_places:
            lead = found.reshape((-1, 2, bit) + own.shape)
            flipped = lead[:, ::-1]
            found = jnp.where((self.place & bit) != 0, flipped, lead).reshape(found.shape)
            bit *= 2
        return found

    def by_core(self, own, other):
        return jnp.where(
            self.core == 1, jnp.stack([other, own]), jnp.stack([own, other])
        )

    def over_groups(self, array):
        bit = self.n_group
        while bit < self.n_dp:
            array = add(array, self.swap(array, bit))
            bit *= 2
        return array


def on_device(
    n_dp,
    n_z,
    tokens,
    lengths,
    key_mask,
    query_weight,
    query_bias,
    key_weight,
    value_weight,
    value_bias,
    output_weight,
    output_bias,
    first_gain,
    first_shift,
    inner_weight,
    inner_bias,
    outer_weight,
    outer_bias,
    second_gain,
    second_shift,
    cotangent,
):
    width = tokens.shape[1]
    mine = query_weight.shape[1]
    units = inner_weight.shape[1]
    all_rows = tokens.shape[0]
    all_blocks = all_rows // BUCKET
    rows = all_rows // n_z
    plane = Plane(n_dp, n_z)
    z, core, place, index = plane.z, plane.core, plane.place, plane.index
    n_places = plane.n_places
    others = range(1, n_z)

    feed_rows = units // plane.n_group
    head_rows = mine // plane.n_group
    mixer_count = width // plane.n_group
    piece = jnp.concatenate(
        [
            lax.dynamic_slice_in_dim(inner_weight, index * feed_rows, feed_rows, 1).T,
            lax.dynamic_slice_in_dim(outer_weight, index * feed_rows, feed_rows, 0),
        ],
        axis=1,
    )
    mixer_piece = lax.dynamic_slice_in_dim(output_weight, index * head_rows, head_rows, 0)
    piece, mixer_piece = together(piece, mixer_piece)
    line = [plane.shift(piece, s) for s in others]

    mixer = plane.gather(mixer_piece).reshape(width, width)
    query_t, key_t, value_t = query_weight.T, key_weight.T, value_weight.T

    key_mask_rows = key_mask.reshape(all_blocks, 1, BUCKET)
    bias_row = jnp.concatenate([query_bias, value_bias, inner_bias])
    bias_rows = jnp.pad(bias_row, (0, 16 * BUCKET - bias_row.shape[0])).reshape(16, BUCKET)
    place_z = z.reshape(1)
    mixed = attend_forward(
        n_z, lengths, tokens, query_t, key_t, value_t, bias_rows, key_mask_rows
    )
    mixed, line = together(mixed, line)

    near = jnp.stack(line)
    by_x, by_y = plane.swap(near, 2), plane.swap(near, 4)
    mixed, near = together(mixed, near)
    mixed = lax.all_to_all(mixed, "tensor", 0, 0)
    own_units = jnp.concatenate([inner_weight.T, outer_weight], axis=1)

    attention_own = jnp.concatenate([query_t, key_t, value_t], axis=1)
    attention_piece = lax.dynamic_slice_in_dim(attention_own, index * head_rows, head_rows, 0)
    attention_line = [plane.shift(attention_piece, s) for s in others]
    biases = mixed[:, 0, mine:].reshape(n_z, -1)[:, : bias_row.shape[0]].astype(f32)
    head_biases = jnp.pad(
        jnp.stack([biases[:, :mine], biases[:, mine : 2 * mine]], axis=1), ((0, 0), (0, 6), (0, 0))
    )
    inner_biases = biases[:, 2 * mine :]
    inner_biases = jnp.concatenate(
        [
            lax.dynamic_slice_in_dim(inner_biases, lax.rem(z + n_z - s, n_z), 1, 0)
            for s in range(n_z)
        ],
        axis=0,
    )
    inner_biases = inner_biases.reshape(n_z, plane.n_group, feed_rows).transpose(1, 0, 2)
    inner_biases = plane.turned(inner_biases).reshape(n_places, 2, 1, n_z * feed_rows)
    inner_biases = inner_biases.transpose(1, 0, 2, 3).reshape(plane.n_group, 1, -1)
    vectors = jnp.stack(
        [output_bias, first_gain, first_shift, outer_bias, second_gain, second_shift]
        + [jnp.zeros_like(output_bias)] * 2
    ).astype(f32)

    info = jnp.stack([z, place, core])
    shared_args = (info, vectors, inner_biases, own_units)
    cut = feed_rows // 2
    far = [plane.swap(by_x[:, :cut], 4), plane.swap(by_y[:, cut:], 2)]
    near_there, x_there, y_there, mixer, attention_line = together(
        near, by_x, by_y, mixer, attention_line
    )
    send = [plane.swap(units_of, 1) for units_of in (near_there, x_there, y_there)]
    attention_line = jnp.stack(attention_line)
    attention_swaps = plane.to_places([attention_line] * n_places)
    hidden, slope, normed_low, first_normed, first_scale, second_sum = feed_forward(
        ((0, 0), (0, 1), (0, 2), (1, 0), (1, 1), (1, 2)),
        *shared_args,
        [near, by_x, by_y] + send,
        first=(tokens, mixed, mixer),
    )
    second_sum, far, attention_swaps = together(second_sum, far, attention_swaps)
    attention_half = plane.from_places(attention_line, attention_swaps)
    attention_other = plane.swap(attention_half, 1)
    far_send = [plane.swap(half, 1) for half in far]
    keep = [near, by_x, by_y] + far
    send = send + far_send
    hidden, slope, my_output, grad_second, grad_outer, second_sums = feed_forward(
        ((0, 3), (1, 3)), *shared_args, far + far_send,
        going=(normed_low, second_sum, hidden, slope), last=(lengths, cotangent),
    )
    output = lax.all_gather(my_output, "tensor", axis=0, tiled=True)

    grad_outer, attention_other = together(grad_outer, attention_other)

    shared_args = (info, grad_outer, normed_low, hidden, slope, own_units)
    sent_early, sent_late, bias_sent, grad_normed = feed_back(*shared_args, grad_second, send)
    other = [plane.swap(sent_early, 1), plane.swap(sent_late, 1)]
    attention_remote = plane.by_core(attention_half, attention_other)
    attention_remote = attention_remote.transpose(2, 1, 0, 3, 4).reshape(n_z - 1, mine, 3 * width)
    projected = project(
        place_z, tokens, attention_own, attention_remote, head_biases, rows // BUCKET
    )
    projected, other = together(projected, other)
    (
        inner_stay, outer_stay, inner_go, outer_go, bias_kept, grad_first, grad_attended, first_sums
    ) = feed_back(
        *shared_args, grad_normed, keep, other,
        (first_normed, first_scale, vectors),
    )
    inner_came, outer_came = plane.swap(inner_go, 4), plane.swap(outer_go, 2)
    grads, my_tokens_grad, back_sums = attend_back(
        place_z, lengths, grad_attended, grad_first, attention_own, attention_remote, mixer,
        *projected, key_mask_rows,
    )
    grads, inner_came, outer_came, output = together(grads, inner_came, outer_came, output)
    inner_on, outer_on = (
        plane.swap(add(inner_stay[1], inner_came[1]), 2),
        plane.swap(add(outer_stay[1], outer_came[1]), 4),
    )
    tokens_grad = lax.all_gather(my_tokens_grad, "tensor", axis=0, tiled=True)

    def weight_grads(other=None, small=None):
        return attention_grads(n_places, info, grads, mixed, tokens, grad_attended, other, small)

    sent = weight_grads()
    sent, inner_on, outer_on, back_sums, first_sums, second_sums, bias_kept, bias_sent = together(
        sent, inner_on, outer_on, back_sums, first_sums, second_sums, bias_kept, bias_sent
    )
    other = [plane.swap(part, 1) for part in sent]

    bias_grads = jnp.stack(
        [bias_kept[:, 0], bias_sent[:, 0]], axis=1
    )
    inner_bias_grad = plane.turned(bias_grads.reshape(plane.n_group, n_z, feed_rows))
    inner_bias_grad = inner_bias_grad.transpose(1, 0, 2)
    inner_bias_grad = jnp.concatenate(
        [
            sum(
                jnp.where(lax.rem(z - t + n_z, n_z) == s, inner_bias_grad[s : s + 1], 0.0)
                for s in range(n_z)
            )
            for t in range(n_z)
        ],
        axis=0,
    ).reshape(n_z, units)

    small = jnp.concatenate(
        [first_sums[:3], second_sums[:3], inner_bias_grad, jnp.sum(back_sums, axis=0)[:2]], axis=0
    )
    small = jnp.pad(small, ((0, -small.shape[0] % 16), (0, 0))).astype(bf16)
    small_rows = small.shape[0]

    small = add(small, plane.swap(small, 1))
    kept = list(weight_grads(other, small))
    arrived = plane.to_places(kept)
    feed_parts = [
        jnp.concatenate(
            [
                add(inner_stay[0, s], inner_came[0, s], inner_on[s]),
                add(outer_stay[0, s], outer_came[0, s], outer_on[s]),
            ],
            axis=1,
        )
        for s in range(n_z)
    ]
    feed_line = [plane.shift(feed_parts[s], -s) for s in others]
    output = copied(output)
    arrived, output = together(arrived, output)
    small = add(small, *[a[-small_rows:] for a in arrived])
    count = 2 * mine // n_places
    attention_parts = [
        add(*[a[s * count : (s + 1) * count] for a in [kept[0]] + arrived]) for s in range(n_z)
    ]
    attention_line = [
        plane.shift(jnp.concatenate([attention_parts[s], small], axis=0), s) for s in others
    ]
    feed_total = plane.over_groups(add(feed_parts[0], *feed_line))
    feed_arrived = plane.to_places([feed_total] * n_places)
    tokens_grad = copied(tokens_grad)
    attention_line, feed_arrived, tokens_grad = together(
        attention_line, feed_arrived, tokens_grad
    )
    attention_total = plane.over_groups(
        add(attention_parts[0], *[a[:count] for a in attention_line])
    )
    small = plane.over_groups(add(small, *[a[count:] for a in attention_line])).astype(f32)
    arrived = plane.to_places([attention_total] * n_places)
    feed_half = plane.from_places(feed_total, feed_arrived)
    feed_other = plane.swap(feed_half, 1)
    inner_grad, outer_grad = finish_feed(core.reshape(1), feed_half, feed_other)
    inner_bias_sum = lax.dynamic_slice_in_dim(small, 6 + z, 1, 0)[0]
    head_sums = lax.dynamic_slice_in_dim(small[6 + n_z : 8 + n_z], z * mine, mine, 1)
    arrived, inner_grad, outer_grad, small, inner_bias_sum, head_sums = together(
        arrived, inner_grad, outer_grad, small, inner_bias_sum, head_sums
    )
    attention_half = plane.from_places(attention_total, arrived)
    attention_other = plane.swap(attention_half, 1)
    grad_list = plane.by_core(attention_half, attention_other)
    grad_list = grad_list.reshape(2, n_places, 2, mine // n_places, width)
    grad_list = grad_list.transpose(0, 2, 1, 3, 4).reshape(4, mine, width)

    shared = small[:6]

    return (
        output,
        tokens_grad,
        grad_list[0].T.astype(f32),
        head_sums[0],
        grad_list[1].T.astype(f32),
        grad_list[2].T.astype(f32),
        head_sums[1],
        grad_list[3].astype(f32),
        shared[0],
        shared[1],
        shared[2],
        inner_grad,
        inner_bias_sum,
        outer_grad,
        shared[3],
        shared[4],
        shared[5],
    )


def solution(mesh):
    n_dp, n_z = mesh.shape["dp"], mesh.shape["tensor"]
    in_specs = (
        P("dp", None),
        P("dp", None),
        P("dp"),
        P(None, "tensor"),
        P("tensor"),
        P(None, "tensor"),
        P(None, "tensor"),
        P("tensor"),
        P("tensor", None),
        P(),
        P(),
        P(),
        P(None, "tensor"),
        P("tensor"),
        P("tensor", None),
        P(),
        P(),
        P(),
        P("dp", None),
    )
    out_specs = (
        P("dp", None),
        P("dp", None),
        P(None, "tensor"),
        P("tensor"),
        P(None, "tensor"),
        P(None, "tensor"),
        P("tensor"),
        P("tensor", None),
        P(),
        P(),
        P(),
        P(None, "tensor"),
        P("tensor"),
        P("tensor", None),
        P(),
        P(),
        P(),
    )

    def program(*args):
        return on_device(n_dp, n_z, *args)

    return jax.shard_map(
        program, mesh=mesh, in_specs=in_specs, out_specs=out_specs, check_vma=False
    )
```
